32 devices in a mesh: fsdp: 8 (over y, x, core), seq: 4 (over z).
Axes of the slice: x: 2, y: 2, z: 4, core: 2. Of those that a mesh axis runs over, the one named last changes fastest.
Arguments:
- tokens: bfloat16 [8192, 1536], P(('fsdp', 'seq')), may hold values from -6 to 6
- cotangent: bfloat16 [8192, 1536], P(('fsdp', 'seq')), may hold values from -6 to 6
- lengths: int32 [8, 3], P('fsdp'), may hold values from 1 to 768, as said below
- balance: int32 [8192], P(('fsdp', 'seq')), may hold values from 0 to 8191, as said below
- norm1_gain: bfloat16 [1536], P('fsdp'), may hold values from 0.5 to 1.5
- w_query: bfloat16 [1536, 1536], P('fsdp'), may hold values from -0.15625 to 0.15625
- b_query: bfloat16 [1536], P('fsdp'), may hold values from -3 to 3
- w_key: bfloat16 [1536, 256], P('fsdp'), may hold values from -0.15625 to 0.15625
- b_key: bfloat16 [256], P('fsdp'), may hold values from -3 to 3
- w_value: bfloat16 [1536, 256], P('fsdp'), may hold values from -0.15625 to 0.15625
- b_value: bfloat16 [256], P('fsdp'), may hold values from -3 to 3
- w_out: bfloat16 [1536, 1536], P('fsdp'), may hold values from -0.625 to 0.625
- norm2_gain: bfloat16 [1536], P('fsdp'), may hold values from 0.5 to 1.5
- w_gate: bfloat16 [1536, 8960], P('fsdp'), may hold values from -0.15625 to 0.15625
- w_up: bfloat16 [1536, 8960], P('fsdp'), may hold values from -0.15625 to 0.15625
- w_down: bfloat16 [8960, 1536], P('fsdp'), may hold values from -0.109375 to 0.109375
Outputs:
- layer_out: bfloat16 [8192, 1536], P(('fsdp', 'seq'))
- input_grad: bfloat16 [8192, 1536], P(('fsdp', 'seq'))
- grad_norm1: float32 [1536], P(('fsdp', 'seq'))
- grad_w_query: float32 [1536, 1536], P(('fsdp', 'seq'))
- grad_b_query: float32 [1536], P(('fsdp', 'seq'))
- grad_w_key: float32 [1536, 256], P(('fsdp', 'seq'))
- grad_b_key: float32 [256], replicated
- grad_w_value: float32 [1536, 256], P(('fsdp', 'seq'))
- grad_b_value: float32 [256], replicated
- grad_w_out: float32 [1536, 1536], P(('fsdp', 'seq'))
- grad_norm2: float32 [1536], P(('fsdp', 'seq'))
- grad_w_gate: float32 [1536, 8960], P(('fsdp', 'seq'))
- grad_w_up: float32 [1536, 8960], P(('fsdp', 'seq'))
- grad_w_down: float32 [8960, 1536], P(('fsdp', 'seq'))
The draws below stay inside these ranges and needn't reach their ends.
Inputs may be any that keep to these rules, and one draw needn't show every extreme that they name: Row g gives, in order, the lengths of the three sequences that fill balanced rows g * 1024 to (g + 1) * 1024 - 1; each row sums to 1024 and its middle entry is 768. balance is a permutation that keeps every row within its block of 1024 rows. Of the rows of one device, at most 96 go to any one device of the block, and in every block some device sends exactly 96 rows to some device.
All inputs are finite; a program needn't handle non-finite values.
Results may differ from the reference program's by a relative error of at most 0.025.
Values may be sent and summed in bfloat16 or wider, within the bound.
A program may use at most 512 MiB of HBM per device.

```python
import jax
import jax.numpy as jnp
from jax import lax

D = 1536
HEADS = 12
KV_HEADS = 2
HEAD_DIM = 128
FF = 8960
TOK_DEV = 256
TOKENS = 8192
GROUP_TOKENS = 1024
KV_WIDTH = 256
N_FSDP = 8
N_SEQ = 4


def draw_lengths(key, part):
    key = jax.random.fold_in(key, 3)
    leading = jax.random.randint(key, (N_FSDP,), 1, TOK_DEV)
    longest = jnp.full((N_FSDP,), (N_SEQ - 1) * TOK_DEV, jnp.int32)
    return jnp.stack([leading, longest, TOK_DEV - leading], 1).astype(jnp.int32)


def draw_balance(key, part):
    key = jax.random.fold_in(key, 7)
    seq_count = N_SEQ
    per_device = TOK_DEV
    middle = per_device // seq_count
    swing = per_device // (2 * seq_count)

    def shuffled(chosen_key):
        return jax.random.permutation(chosen_key, per_device)

    def one_group(group_key):
        four_keys = jax.random.split(group_key, 4)
        leading = jax.random.permutation(four_keys[0], seq_count)
        offset = jax.random.randint(four_keys[1], (), 1, seq_count)
        trailing = leading[(jnp.arange(seq_count) + offset) % seq_count]
        targets = jnp.arange(seq_count)
        raised = (targets[None, :] == leading[:, None]).astype(jnp.int32)
        lowered = (targets[None, :] == trailing[:, None]).astype(jnp.int32)
        counts = middle + swing * (raised - lowered)
        ends = jnp.cumsum(counts, 1)
        row_start = ends - counts
        column_start = jnp.cumsum(counts, 0) - counts
        ranks = jax.vmap(shuffled)(jax.random.split(four_keys[2], seq_count))
        target = jnp.sum((ranks[:, :, None] >= ends[:, None, :]).astype(jnp.int32), -1)
        sources = jnp.arange(seq_count)[:, None]
        within = ranks - row_start[sources, target]
        arrival = column_start[sources, target] + within
        places = jax.vmap(shuffled)(jax.random.split(four_keys[3], seq_count))
        landing = places[target, arrival]
        return target * per_device + landing
    every = jax.vmap(one_group)(jax.random.split(key, N_FSDP))
    offsets = jnp.arange(N_FSDP) * seq_count * per_device
    return (every + offsets[:, None, None]).reshape(-1).astype(jnp.int32)


def with_spikes(values, rng, source, target, shards_of, factor):
    def block_of(dim):
        return (jnp.arange(values.shape[dim]) // (values.shape[dim] // shards_of)).reshape((-1,) + (1,) * (values.ndim - 1 - dim))

    one_side = jax.random.permutation(rng, shards_of)[block_of(target)]
    far = (block_of(target) + shards_of // 2) % shards_of
    return jnp.where((block_of(source) == one_side) | (block_of(source) == far), factor * values, values)


def level_of(rng, shape, cuts, low, high):
    level, own = 1.0, jax.random.fold_in(rng, 6)
    for dim, shards_of in cuts:
        draws = jnp.exp(jax.random.uniform(jax.random.fold_in(own, dim), (shards_of,), jnp.float32, low / len(cuts), high / len(cuts)))
        level = level * jnp.repeat(draws, shape[dim] // shards_of).reshape([-1 if axis == dim else 1 for axis in range(len(shape))])
    return level


def gaussian(own_key, dims, scale, reach, shards=(), kind=jnp.bfloat16):
    values = scale * jax.random.normal(own_key, dims, jnp.float32)
    if shards:
        values = values * level_of(own_key, dims, shards, -0.22, 0.18)
    return jnp.clip(values, -reach, reach).astype(kind)


def gaussian_with(key, shape, spread, reach, shards, heavy, kind=jnp.bfloat16):
    array = spread * jax.random.normal(key, shape, jnp.float32)
    if shards:
        array = array * level_of(key, shape, shards, -0.22, 0.18)
    return jnp.clip(with_spikes(array, jax.random.fold_in(key, 3), *heavy), -reach, reach).astype(kind)


def setup_inputs(seed: int = 0) -> dict:
    arg_keys = jax.random.split(jax.random.key(seed), 17)
    return {
        "tokens": gaussian_with(arg_keys[0], (TOKENS, D), 1.0, 6.0, ((0, 32),), (0, 1, 32, 2.75)),
        "cotangent": gaussian(arg_keys[1], (TOKENS, D), 1.0, 6.0, ((0, 32),)),
        "lengths": draw_lengths(jax.random.fold_in(arg_keys[16], 71), 0),
        "balance": draw_balance(jax.random.fold_in(arg_keys[16], 71), 0),
        "norm1_gain": jnp.clip(1.0 + 0.1 * jax.random.normal(arg_keys[4], (D,), jnp.float32), 0.5, 1.5).astype(jnp.bfloat16),
        "w_query": gaussian(arg_keys[5], (D, D), D ** -0.5, 0.15625, ((0, 8),)),
        "b_query": gaussian(arg_keys[6], (D,), 0.5, 3.0, ((0, 8),)),
        "w_key": gaussian(arg_keys[7], (D, KV_WIDTH), D ** -0.5, 0.15625, ((0, 8),)),
        "b_key": gaussian(arg_keys[8], (KV_WIDTH,), 0.5, 3.0, ((0, 8),)),
        "w_value": gaussian(arg_keys[9], (D, KV_WIDTH), D ** -0.5, 0.15625, ((0, 8),)),
        "b_value": gaussian(arg_keys[10], (KV_WIDTH,), 0.5, 3.0, ((0, 8),)),
        "w_out": gaussian(arg_keys[11], (D, D), (D // 16) ** -0.5, 0.625, ((0, 8),)),
        "norm2_gain": jnp.clip(1.0 + 0.1 * jax.random.normal(arg_keys[12], (D,), jnp.float32), 0.5, 1.5).astype(jnp.bfloat16),
        "w_gate": gaussian(arg_keys[13], (D, FF), D ** -0.5, 0.15625, ((0, 8),)),
        "w_up": gaussian(arg_keys[14], (D, FF), D ** -0.5, 0.15625, ((0, 8),)),
        "w_down": gaussian(arg_keys[15], (FF, D), (FF // 3) ** -0.5, 0.109375, ((0, 8),)),
    }


epsilon = 1e-06
rope_base = 1000000.0

@jax.custom_vjp
def low(v):
    return lax.optimization_barrier(v.astype(jnp.bfloat16)).astype(jnp.float32)

@jax.custom_vjp
def low_back(v):
    return v

def low_keep(v):
    return (low(v), None)

def low_pass(kept, grad):
    return (grad,)

def back_keep(v):
    return (v, None)

def back_low(kept, grad):
    return (low(grad),)
low.defvjp(low_keep, low_pass)
low_back.defvjp(back_keep, back_low)

def matmul(left, right):
    return jnp.dot(left, right, precision=lax.Precision.HIGHEST, preferred_element_type=jnp.float32)

def norm_piece(values, gain):
    return values * lax.rsqrt(lax.optimization_barrier(jnp.mean(values * values, -1, keepdims=True)) + epsilon) * gain

def rope_tables(position):
    half = HEAD_DIM // 2
    inverse = rope_base ** (-(jnp.arange(half, dtype=jnp.float32) * 2.0 / HEAD_DIM))
    angle = position.astype(jnp.float32)[:, None] * inverse[None, :]
    cosine = jnp.concatenate([jnp.cos(angle), jnp.cos(angle)], -1)
    sine = jnp.concatenate([jnp.sin(angle), jnp.sin(angle)], -1)
    return (cosine, sine)

def turn_half(values):
    half = values.shape[-1] // 2
    return jnp.concatenate([-values[..., half:], values[..., :half]], -1)

def rotate(values, cosine, sine):
    return values * cosine[:, None, :] + turn_half(values) * sine[:, None, :]

def group_attention(queries, keys, values, segment):
    repeat = HEADS // KV_HEADS
    keys_all = jnp.repeat(keys, repeat, axis=1)
    values_all = jnp.repeat(values, repeat, axis=1)
    slots = jnp.arange(GROUP_TOKENS, dtype=jnp.int32)
    allowed = (segment[:, None] == segment[None, :]) & (slots[None, :] <= slots[:, None])
    raw = jnp.einsum('qhd,khd->hqk', queries, keys_all, precision=lax.Precision.HIGHEST)
    raw = low_back(raw * HEAD_DIM ** (-0.5))
    scores = jnp.where(allowed[None], raw, -jnp.inf)
    top_score = lax.optimization_barrier(jnp.max(scores, -1, keepdims=True))
    expo = jnp.exp(scores - top_score)
    probs = low(expo / lax.optimization_barrier(jnp.sum(expo, -1, keepdims=True)))
    return jnp.einsum('hqk,khd->qhd', probs, values_all, precision=lax.Precision.HIGHEST)

def attend_packed(packed):
    return jax.checkpoint(group_attention)(packed[0], packed[1], packed[2], packed[3])

def layer(inputs, weights, segment, position):
    gain_one, weight_query, bias_query, weight_key, bias_key, weight_value, bias_value, weight_out, gain_two, weight_gate, weight_up, weight_down = weights
    count_rows = inputs.shape[0]
    groups = count_rows // GROUP_TOKENS
    normed_one = low(norm_piece(inputs, gain_one))
    query_pre = low_back(matmul(normed_one, weight_query) + bias_query)
    key_pre = low_back(matmul(normed_one, weight_key) + bias_key)
    value_pre = low_back(matmul(normed_one, weight_value) + bias_value)
    cosine, sine = rope_tables(position)
    queries = low(rotate(query_pre.reshape(count_rows, HEADS, HEAD_DIM), cosine, sine))
    keys = low(rotate(key_pre.reshape(count_rows, KV_HEADS, HEAD_DIM), cosine, sine))
    values = low(value_pre.reshape(count_rows, KV_HEADS, HEAD_DIM))
    attended = lax.map(attend_packed, (queries.reshape(groups, GROUP_TOKENS, HEADS, HEAD_DIM), keys.reshape(groups, GROUP_TOKENS, KV_HEADS, HEAD_DIM), values.reshape(groups, GROUP_TOKENS, KV_HEADS, HEAD_DIM), segment))
    attended = low(low_back(attended.reshape(count_rows, D)))
    resid = inputs + low_back(matmul(attended, weight_out))
    normed_two = low(norm_piece(resid, gain_two))
    gate = low_back(matmul(normed_two, weight_gate))
    up = low_back(matmul(normed_two, weight_up))
    hidden = low(gate * jax.nn.sigmoid(gate) * up)
    return resid + low_back(matmul(hidden, weight_down))

def reference(tokens, cotangent, lengths, balance, norm1_gain, w_query, b_query, w_key, b_key, w_value, b_value, w_out, norm2_gain, w_gate, w_up, w_down):
    balanced = jnp.zeros((TOKENS, D), jnp.float32).at[balance].set(tokens.astype(jnp.float32))
    upstream = jnp.zeros((TOKENS, D), jnp.float32).at[balance].set(cotangent.astype(jnp.float32))
    starts = (jnp.cumsum(lengths, 1) - lengths).astype(jnp.int32)
    slots = jnp.arange(GROUP_TOKENS, dtype=jnp.int32)
    segment = (slots[None, :] >= starts[:, 1:2]).astype(jnp.int32) + (slots[None, :] >= starts[:, 2:3]).astype(jnp.int32)
    first_row = jnp.where(segment == 0, starts[:, 0:1], jnp.where(segment == 1, starts[:, 1:2], starts[:, 2:3]))
    position = (slots[None, :] - first_row).astype(jnp.int32).reshape(TOKENS)
    params = (norm1_gain.astype(jnp.float32), w_query.astype(jnp.float32), b_query.astype(jnp.float32), w_key.astype(jnp.float32), b_key.astype(jnp.float32), w_value.astype(jnp.float32), b_value.astype(jnp.float32), w_out.astype(jnp.float32), norm2_gain.astype(jnp.float32), w_gate.astype(jnp.float32), w_up.astype(jnp.float32), w_down.astype(jnp.float32))

    def forward(inputs, weights):
        return layer(inputs, weights, segment, position)
    result, pull = jax.vjp(forward, balanced, params)
    input_part, grads = pull(upstream)
    layer_out = result[balance].astype(jnp.bfloat16)
    input_grad = input_part[balance].astype(jnp.bfloat16)
    return (layer_out, input_grad, grads[0], grads[1], grads[2], grads[3], grads[4], grads[5], grads[6], grads[7], grads[8], grads[9], grads[10], grads[11])
```

```python
import jax
import jax.numpy as jnp
from jax import lax
from jax.sharding import PartitionSpec as P

HEADS = 12
KV_HEADS = 2
HEAD_DIM = 128

epsilon = 1e-06
rope_base = 1000000.0


def norm_piece(values, gain):
    return values * lax.rsqrt(jnp.mean(values * values, -1, keepdims=True) + epsilon) * gain


def rope_tables(position):
    half = HEAD_DIM // 2
    inverse = rope_base ** (-(jnp.arange(half, dtype=jnp.float32) * 2.0 / HEAD_DIM))
    angle = position.astype(jnp.float32)[:, None] * inverse[None, :]
    cosine = jnp.concatenate([jnp.cos(angle), jnp.cos(angle)], -1)
    sine = jnp.concatenate([jnp.sin(angle), jnp.sin(angle)], -1)
    return (cosine, sine)


def turn_half(values):
    half = values.shape[-1] // 2
    return jnp.concatenate([-values[..., half:], values[..., :half]], -1)


def rotate(values, cosine, sine):
    return values * cosine[:, None, :] + turn_half(values) * sine[:, None, :]


def rotate_back(grads, cosine, sine):
    return grads * cosine[:, None, :] - turn_half(grads * sine[:, None, :])


def segment_of(slots, starts):
    return (slots >= starts[1]).astype(jnp.int32) + (slots >= starts[2]).astype(jnp.int32)


def contract_rows(left, right):
    return lax.dot_general(
        left, right, (((0,), (0,)), ((), ())), preferred_element_type=jnp.float32
    )


def contract_columns(left, right):
    return lax.dot_general(
        left, right, (((1,), (1,)), ((), ())), preferred_element_type=jnp.float32
    )


def per_device(
    tokens, cotangent, lengths, balance, norm1_gain, w_query, b_query, w_key, b_key,
    w_value, b_value, w_out, norm2_gain, w_gate, w_up, w_down,
):
    seq_count = lax.axis_size("seq")
    fsdp_count = lax.axis_size("fsdp")
    seq_rank = lax.axis_index("seq")
    rows_here, width = tokens.shape
    group = seq_count * rows_here
    kv_width = KV_HEADS * HEAD_DIM
    qkv_width = width + 2 * kv_width
    hidden_width = w_gate.shape[1]
    unit = hidden_width // (fsdp_count * seq_count)
    own_units = hidden_width // seq_count
    weight_rows = w_gate.shape[0]
    score_scale = HEAD_DIM ** (-0.5)
    repeat = HEADS // KV_HEADS

    slot = balance % group
    slots_all = lax.all_gather(slot, "seq", axis=0, tiled=True)
    seq_lengths = lengths[0]
    starts = jnp.cumsum(seq_lengths) - seq_lengths
    segment = segment_of(slot, starts)
    segments_all = segment_of(slots_all, starts)
    first_row = jnp.where(segment == 0, starts[0], jnp.where(segment == 1, starts[1], starts[2]))
    cosine, sine = rope_tables(slot - first_row)
    allowed = (segment[:, None] == segments_all[None, :]) & (slots_all[None, :] <= slot[:, None])

    small = jnp.concatenate([norm1_gain, norm2_gain, b_query, b_key, b_value], 0)[None]
    small = lax.all_gather(small, "fsdp", axis=0, tiled=True)
    piece = norm1_gain.shape[0]
    bias_piece = b_key.shape[0]
    gain_one = small[:, :piece].reshape(-1).astype(jnp.float32)
    gain_two = small[:, piece : 2 * piece].reshape(-1).astype(jnp.float32)
    bias_qkv = jnp.concatenate(
        [
            small[:, 2 * piece : 3 * piece].reshape(-1),
            small[:, 3 * piece : 3 * piece + bias_piece].reshape(-1),
            small[:, 3 * piece + bias_piece :].reshape(-1),
        ],
        0,
    ).astype(jnp.float32)
    weight_qkv = lax.all_gather(
        jnp.concatenate([w_query, w_key, w_value], 1), "fsdp", axis=0, tiled=True
    )
    weight_out = lax.all_gather(w_out, "fsdp", axis=0, tiled=True)
    upstream_all = lax.all_gather(cotangent, "seq", axis=0, tiled=True)

    def own_columns(weight):
        cut = weight.reshape(weight_rows, fsdp_count, seq_count, unit)
        return lax.dynamic_index_in_dim(cut, seq_rank, 2, False).reshape(weight_rows, own_units)

    weight_gu = lax.all_gather(
        jnp.concatenate([own_columns(w_gate), own_columns(w_up)], 1), "fsdp", axis=0, tiled=True
    )
    weight_down = lax.all_gather(
        lax.dynamic_slice_in_dim(w_down, seq_rank * unit, unit, 0), "fsdp", axis=0, tiled=True
    )

    inputs = tokens.astype(jnp.float32)
    normed_one = norm_piece(inputs, gain_one).astype(jnp.bfloat16)
    projected = jnp.dot(normed_one, weight_qkv, preferred_element_type=jnp.float32) + bias_qkv
    query_pre = projected[:, :width].reshape(rows_here, HEADS, HEAD_DIM)
    key_pre = projected[:, width : width + kv_width].reshape(rows_here, KV_HEADS, HEAD_DIM)
    value_pre = projected[:, width + kv_width :]
    queries = rotate(query_pre, cosine, sine).astype(jnp.bfloat16)
    keys = rotate(key_pre, cosine, sine).astype(jnp.bfloat16).reshape(rows_here, kv_width)
    values = value_pre.astype(jnp.bfloat16)
    paired = lax.all_gather(jnp.concatenate([keys, values], 1), "seq", axis=0, tiled=True)
    keys_all = paired[:, :kv_width].reshape(group, KV_HEADS, HEAD_DIM)
    values_all = paired[:, kv_width:].reshape(group, KV_HEADS, HEAD_DIM)
    grouped = queries.reshape(rows_here, KV_HEADS, repeat, HEAD_DIM)
    raw = (
        jnp.einsum("qgrd,kgd->grqk", grouped, keys_all, preferred_element_type=jnp.float32)
        * score_scale
    )
    scores = jnp.where(allowed, raw, -jnp.inf)
    expo = jnp.exp(scores - jnp.max(scores, -1, keepdims=True))
    probs = expo / jnp.sum(expo, -1, keepdims=True)
    probs_low = probs.astype(jnp.bfloat16)
    attended = jnp.einsum(
        "grqk,kgd->qgrd", probs_low, values_all, preferred_element_type=jnp.float32
    )
    attended = attended.astype(jnp.bfloat16).reshape(rows_here, width)
    resid = inputs + jnp.dot(attended, weight_out, preferred_element_type=jnp.float32)
    normed_two = norm_piece(resid, gain_two).astype(jnp.bfloat16)

    normed_all = lax.all_gather(normed_two, "seq", axis=0, tiled=True)
    both = jnp.dot(normed_all, weight_gu, preferred_element_type=jnp.float32)
    gate = both[:, :own_units]
    up = both[:, own_units:]
    sigma = jax.nn.sigmoid(gate)
    activated = gate * sigma
    hidden = (activated * up).astype(jnp.bfloat16)
    d_hidden = contract_columns(upstream_all, weight_down)
    d_gate = (d_hidden * up * sigma * (1.0 + gate * (1.0 - sigma))).astype(jnp.bfloat16)
    d_up = (d_hidden * activated).astype(jnp.bfloat16)
    d_both = jnp.concatenate([d_gate, d_up], 1)
    columns = lax.psum_scatter(
        contract_columns(d_both, weight_gu).astype(jnp.bfloat16),
        "seq", scatter_dimension=0, tiled=True,
    ).astype(jnp.float32)
    branch = lax.psum_scatter(
        jnp.dot(hidden, weight_down, preferred_element_type=jnp.float32).astype(jnp.bfloat16),
        "seq", scatter_dimension=0, tiled=True,
    ).astype(jnp.float32)
    layer_out = (resid + branch).astype(jnp.bfloat16)
    grad_down = lax.psum_scatter(
        contract_rows(hidden, upstream_all).astype(jnp.bfloat16),
        "fsdp", scatter_dimension=0, tiled=True,
    ).astype(jnp.float32)
    grad_pair = lax.psum_scatter(
        contract_rows(normed_all, d_both).astype(jnp.bfloat16),
        "fsdp", scatter_dimension=0, tiled=True,
    )
    grad_pair = lax.all_to_all(grad_pair, "seq", split_axis=0, concat_axis=0, tiled=True)
    grad_pair = grad_pair.reshape(seq_count, weight_rows // seq_count, 2, fsdp_count, unit)
    grad_pair = grad_pair.transpose(2, 1, 3, 0, 4).astype(jnp.float32)
    grad_pair = grad_pair.reshape(2, weight_rows // seq_count, hidden_width)

    _, pull_two = jax.vjp(norm_piece, resid, gain_two)
    d_resid_norm, grad_gain_two = pull_two(columns)
    d_resid = cotangent.astype(jnp.float32) + d_resid_norm
    d_branch = d_resid.astype(jnp.bfloat16)
    grad_out = contract_rows(attended, d_branch).astype(jnp.bfloat16)
    d_attended = contract_columns(d_branch, weight_out).astype(jnp.bfloat16)
    d_attended = d_attended.reshape(rows_here, KV_HEADS, repeat, HEAD_DIM)
    d_probs = jnp.einsum(
        "qgrd,kgd->grqk", d_attended, values_all, preferred_element_type=jnp.float32
    )
    delta = jnp.sum(probs * d_probs, -1, keepdims=True)
    d_score = (probs * (d_probs - delta)).astype(jnp.bfloat16)
    d_queries = (
        jnp.einsum("grqk,kgd->qgrd", d_score, keys_all, preferred_element_type=jnp.float32)
        * score_scale
    )
    d_keys = (
        jnp.einsum("grqk,qgrd->kgd", d_score, grouped, preferred_element_type=jnp.float32)
        * score_scale
    )
    d_values = jnp.einsum(
        "grqk,qgrd->kgd", probs_low, d_attended, preferred_element_type=jnp.float32
    )
    d_paired = jnp.concatenate([d_keys.reshape(group, kv_width), d_values.reshape(group, kv_width)], 1)
    d_paired = lax.psum_scatter(
        d_paired.astype(jnp.bfloat16), "seq", scatter_dimension=0, tiled=True
    ).astype(jnp.float32)
    d_query_pre = rotate_back(
        d_queries.reshape(rows_here, HEADS, HEAD_DIM), cosine, sine
    ).astype(jnp.bfloat16)
    d_key_pre = rotate_back(
        d_paired[:, :kv_width].reshape(rows_here, KV_HEADS, HEAD_DIM), cosine, sine
    ).astype(jnp.bfloat16)
    d_value_pre = d_paired[:, kv_width:].astype(jnp.bfloat16)
    d_qkv = jnp.concatenate(
        [
            d_query_pre.reshape(rows_here, width),
            d_key_pre.reshape(rows_here, kv_width),
            d_value_pre,
        ],
        1,
    )
    grad_qkv = contract_rows(normed_one, d_qkv).astype(jnp.bfloat16)
    grad_bias = jnp.sum(d_qkv.astype(jnp.float32), 0)
    d_normed_one = contract_columns(d_qkv, weight_qkv)
    _, pull_one = jax.vjp(norm_piece, inputs, gain_one)
    d_input_norm, grad_gain_one = pull_one(d_normed_one)
    input_grad = (d_resid + d_input_norm).astype(jnp.bfloat16)

    def summed(value):
        value = lax.psum_scatter(value, "fsdp", scatter_dimension=0, tiled=True)
        return lax.psum_scatter(value, "seq", scatter_dimension=0, tiled=True).astype(jnp.float32)

    grad_out = summed(grad_out)
    grad_qkv = summed(grad_qkv)
    vectors = lax.psum(
        jnp.concatenate([grad_gain_one, grad_gain_two, grad_bias], 0), ("fsdp", "seq")
    )
    own = width // (fsdp_count * seq_count)
    first = (lax.axis_index("fsdp") * seq_count + seq_rank) * own

    def own_part(offset):
        return lax.dynamic_slice_in_dim(vectors, offset + first, own, 0)

    biases = 2 * width
    return (
        layer_out,
        input_grad,
        own_part(0),
        grad_qkv[:, :width],
        own_part(biases),
        grad_qkv[:, width : width + kv_width],
        vectors[biases + width : biases + width + kv_width],
        grad_qkv[:, width + kv_width :],
        vectors[biases + width + kv_width :],
        grad_out,
        own_part(width),
        grad_pair[0],
        grad_pair[1],
        grad_down,
    )


def solution(mesh):
    both = P(("fsdp", "seq"), None)
    both_one = P(("fsdp", "seq"))
    placed = (
        both, both, P("fsdp", None), both_one, P("fsdp"), P("fsdp", None), P("fsdp"),
        P("fsdp", None), P("fsdp"), P("fsdp", None), P("fsdp"), P("fsdp", None), P("fsdp"),
        P("fsdp", None), P("fsdp", None), P("fsdp", None),
    )
    return jax.shard_map(
        per_device,
        mesh=mesh,
        in_specs=placed,
        out_specs=(
            both, both, both_one, both, both_one, both, P(), both, P(), both, both_one,
            both, both, both,
        ),
        check_vma=False,
    )
```

```python
import jax
import jax.numpy as jnp
from jax import lax
from jax.experimental import pallas as pl
from jax.experimental.pallas import tpu as pltpu
from jax.sharding import PartitionSpec as P

HEADS = 12
KV_HEADS = 2
HEAD_DIM = 128

epsilon = 1e-06
rope_base = 1000000.0


def norm_piece(values, gain):
    return values * lax.rsqrt(jnp.mean(values * values, -1, keepdims=True) + epsilon) * gain


def rope_tables(position):
    half = HEAD_DIM // 2
    inverse = rope_base ** (-(jnp.arange(half, dtype=jnp.float32) * 2.0 / HEAD_DIM))
    angle = position.astype(jnp.float32)[:, None] * inverse[None, :]
    cosine = jnp.concatenate([jnp.cos(angle), jnp.cos(angle)], -1)
    sine = jnp.concatenate([jnp.sin(angle), jnp.sin(angle)], -1)
    return (cosine, sine)


def turn_half(values):
    half = values.shape[-1] // 2
    return jnp.concatenate([-values[..., half:], values[..., :half]], -1)


def rotate(values, cosine, sine):
    return values * cosine[:, None, :] + turn_half(values) * sine[:, None, :]


def rotate_back(grads, cosine, sine):
    return grads * cosine[:, None, :] - turn_half(grads * sine[:, None, :])


def segment_of(slots, starts):
    return (slots >= starts[1]).astype(jnp.int32) + (slots >= starts[2]).astype(jnp.int32)


def contract_rows(left, right):
    return lax.dot_general(
        left, right, (((0,), (0,)), ((), ())), preferred_element_type=jnp.float32
    )


def contract_columns(left, right):
    return lax.dot_general(
        left, right, (((1,), (1,)), ((), ())), preferred_element_type=jnp.float32
    )


def after(value, *earlier):
    return lax.optimization_barrier((value, *earlier))[0]


def add_low(*values):
    return sum(value.astype(jnp.float32) for value in values).astype(jnp.bfloat16)


def cross(value, bits):
    count = lax.axis_size("fsdp")
    return lax.ppermute(value, "fsdp", [(i, i ^ bits) for i in range(count)])


def shift(value, step):
    count = lax.axis_size("seq")
    return lax.ppermute(value, "seq", [(i, (i + step) % count) for i in range(count)])


def place(parts, rank):
    rows = parts[0].shape[0]
    whole = jnp.zeros((len(parts) * rows,) + parts[0].shape[1:], parts[0].dtype)
    for k, part in enumerate(parts):
        whole = lax.dynamic_update_slice_in_dim(whole, part, (rank ^ k) * rows, 0)
    return whole


def gather_plane(block, earlier=()):
    if lax.axis_size("fsdp") != 8:
        whole = lax.all_gather(block, "fsdp", axis=0, tiled=True)
        return whole, ()
    rank = lax.axis_index("fsdp")
    half = block.shape[0] // 2
    if earlier:
        block = after(block, *earlier)
    from_x = cross(block, 2)
    from_y = cross(block, 4)
    diagonal = (cross(from_x[:half], 4), cross(from_y[half:], 2))
    from_core = cross(block, 1)
    both = cross(jnp.concatenate([from_x, from_y], 0), 1)
    diagonal = jnp.concatenate(diagonal, 0)
    rows = block.shape[0]
    parts = [
        block, from_core, from_x, both[:rows], from_y, both[rows:], diagonal, cross(diagonal, 1),
    ]
    return place(parts, rank), (from_x, from_y)


def scatter_plane(whole, earlier=()):
    count = lax.axis_size("fsdp")
    if count != 8:
        return lax.psum_scatter(whole, "fsdp", scatter_dimension=0, tiled=True)
    rank = lax.axis_index("fsdp")
    rows = whole.shape[0] // count
    half = whole.shape[1] // 2
    if earlier:
        whole = after(whole, *earlier)

    def part(k):
        return lax.dynamic_slice_in_dim(whole, (rank ^ k) * rows, rows, 0)

    arrived = cross(jnp.concatenate([part(1), part(3), part(5), part(7)], 0), 1)
    own, to_x, to_y, to_both = [
        add_low(part(2 * i), arrived[i * rows : (i + 1) * rows]) for i in range(4)
    ]
    got_x = cross(jnp.concatenate([to_x[:, :half], to_both[:, :half]], 0), 2)
    got_y = cross(jnp.concatenate([to_y[:, half:], to_both[:, half:]], 0), 4)
    last_y = cross(add_low(to_y[:, :half], got_x[rows:]), 4)
    last_x = cross(add_low(to_x[:, half:], got_y[rows:]), 2)
    return jnp.concatenate(
        [
            add_low(own[:, :half], got_x[:rows], last_y),
            add_low(own[:, half:], got_y[:rows], last_x),
        ],
        1,
    )


def chain_step(up, down, step):
    count = lax.axis_size("seq")
    up = lax.ppermute(up, "seq", [(i, i + 1) for i in range(step - 1, count - 1)])
    down = lax.ppermute(down, "seq", [(i, i - 1) for i in range(1, count - step + 1)])
    return up, down


def gather_seq(block, pause=None):
    count = lax.axis_size("seq")
    rank = lax.axis_index("seq")
    up, down = block, block
    ups, downs = [], []
    for step in range(1, count):
        if pause is not None and step == count - 1:
            up, down = pause(up), pause(down)
        up, down = chain_step(up, down, step)
        ups.append(up)
        downs.append(down)
    rest = [jnp.where(rank >= j, ups[j - 1], downs[count - j - 1]) for j in range(1, count)]
    return [block] + rest


def scatter_seq(parts, earlier=()):
    count = lax.axis_size("seq")
    up, down = None, None
    for step in range(1, count):
        send_up = parts[step] if up is None else add_low(parts[step], up)
        send_down = parts[count - step] if down is None else add_low(parts[count - step], down)
        if up is None and earlier:
            send_up = after(send_up, *earlier)
            send_down = after(send_down, *earlier)
        up = lax.ppermute(send_up, "seq", [(i, i + 1) for i in range(min(step, count - 1))])
        down = lax.ppermute(
            send_down, "seq", [(i, i - 1) for i in range(count - 1, max(count - 1 - step, 0), -1)]
        )
    return parts[0].astype(jnp.float32) + up.astype(jnp.float32) + down.astype(jnp.float32)


def exchange_seq(whole):
    count = lax.axis_size("seq")
    rank = lax.axis_index("seq")
    rows = whole.shape[0] // count

    def part(step):
        return lax.dynamic_slice_in_dim(whole, ((rank + step) % count) * rows, rows, 0)

    return [part(0)] + [shift(part(step), step) for step in range(1, count)]


def attend_kernel(query, key, value, bias, out, logsum):
    scale = HEAD_DIM ** (-0.5)
    raw = lax.dot_general(
        key[...], query[...], (((1,), (1,)), ((), ())), preferred_element_type=jnp.float32
    )
    scores = raw * scale + bias[...]
    top = jnp.max(scores, 0, keepdims=True)
    expo = jnp.exp(scores - top)
    total = jnp.sum(expo, 0, keepdims=True)
    probs = (expo * (1.0 / total)).astype(jnp.bfloat16)
    turned = lax.dot_general(
        value[...], probs, (((0,), (0,)), ((), ())), preferred_element_type=jnp.float32
    )
    out[...] = turned.T.astype(jnp.bfloat16)
    logsum[...] = jnp.broadcast_to(top + jnp.log(total), logsum.shape)


def attend(queries, paired, bias):
    rows, width = queries.shape
    group = paired.shape[0]
    repeat = HEADS // KV_HEADS
    return pl.pallas_call(
        attend_kernel,
        grid=(HEADS,),
        in_specs=[
            pl.BlockSpec((rows, HEAD_DIM), lambda h: (0, h)),
            pl.BlockSpec((group, HEAD_DIM), lambda h: (0, h // repeat)),
            pl.BlockSpec((group, HEAD_DIM), lambda h: (0, KV_HEADS + h // repeat)),
            pl.BlockSpec((group, rows), lambda h: (0, 0)),
        ],
        out_specs=[
            pl.BlockSpec((rows, HEAD_DIM), lambda h: (0, h)),
            pl.BlockSpec((8, rows), lambda h: (h, 0)),
        ],
        out_shape=[
            jax.ShapeDtypeStruct((rows, width), jnp.bfloat16),
            jax.ShapeDtypeStruct((8 * HEADS, rows), jnp.float32),
        ],
        compiler_params=pltpu.CompilerParams(vmem_limit_bytes=48 * 2**20),
        cost_estimate=pl.CostEstimate(
            flops=4 * HEADS * rows * group * HEAD_DIM * 3, bytes_accessed=4 * 2**20, transcendentals=HEADS * rows * group
        ),
        name="attend",
    )(queries, paired, paired, bias)


def attend_back_kernel(query, key, value, bias, logsum, grad, d_query, d_key, d_value):
    scale = HEAD_DIM ** (-0.5)
    repeat = HEADS // KV_HEADS
    raw = lax.dot_general(
        key[...], query[...], (((1,), (1,)), ((), ())), preferred_element_type=jnp.float32
    )
    probs = jnp.exp(raw * scale + bias[...] - logsum[0:1])
    d_probs = lax.dot_general(
        value[...], grad[...], (((1,), (1,)), ((), ())), preferred_element_type=jnp.float32
    )
    delta = jnp.sum(probs * d_probs, 0, keepdims=True)
    d_score = (probs * (d_probs - delta)).astype(jnp.bfloat16)
    turned = lax.dot_general(
        key[...], d_score, (((0,), (0,)), ((), ())), preferred_element_type=jnp.float32
    )
    d_query[...] = (turned * scale).T.astype(jnp.bfloat16)
    key_part = jnp.dot(d_score, query[...], preferred_element_type=jnp.float32) * scale
    value_part = jnp.dot(
        probs.astype(jnp.bfloat16), grad[...], preferred_element_type=jnp.float32
    )

    @pl.when(pl.program_id(0) % repeat == 0)
    def _():
        d_key[...] = key_part
        d_value[...] = value_part

    @pl.when(pl.program_id(0) % repeat != 0)
    def _():
        d_key[...] += key_part
        d_value[...] += value_part


def attend_back(queries, paired, bias, logsum, grads):
    rows, width = queries.shape
    group = paired.shape[0]
    repeat = HEADS // KV_HEADS
    return pl.pallas_call(
        attend_back_kernel,
        grid=(HEADS,),
        in_specs=[
            pl.BlockSpec((rows, HEAD_DIM), lambda h: (0, h)),
            pl.BlockSpec((group, HEAD_DIM), lambda h: (0, h // repeat)),
            pl.BlockSpec((group, HEAD_DIM), lambda h: (0, KV_HEADS + h // repeat)),
            pl.BlockSpec((group, rows), lambda h: (0, 0)),
            pl.BlockSpec((8, rows), lambda h: (h, 0)),
            pl.BlockSpec((rows, HEAD_DIM), lambda h: (0, h)),
        ],
        out_specs=[
            pl.BlockSpec((rows, HEAD_DIM), lambda h: (0, h)),
            pl.BlockSpec((group, HEAD_DIM), lambda h: (0, h // repeat)),
            pl.BlockSpec((group, HEAD_DIM), lambda h: (0, h // repeat)),
        ],
        out_shape=[
            jax.ShapeDtypeStruct((rows, width), jnp.bfloat16),
            jax.ShapeDtypeStruct((group, KV_HEADS * HEAD_DIM), jnp.float32),
            jax.ShapeDtypeStruct((group, KV_HEADS * HEAD_DIM), jnp.float32),
        ],
        compiler_params=pltpu.CompilerParams(vmem_limit_bytes=48 * 2**20),
        cost_estimate=pl.CostEstimate(
            flops=10 * HEADS * rows * group * HEAD_DIM * 3, bytes_accessed=8 * 2**20, transcendentals=HEADS * rows * group
        ),
        name="attend_back",
    )(queries, paired, paired, bias, logsum, grads)


def pick_kernel(starts, gate, up, out, *, unit, stride, pieces, window):
    rank = lax.axis_index("seq")
    units = unit * pieces
    padded = out.shape[1] // 2
    tile = 128
    for first in range(0, 2 * padded, tile):
        source = gate if first < padded else up
        local = first % padded
        total = jnp.zeros((out.shape[0], tile), jnp.float32)
        for f in range(pieces):
            low, high = max(local, f * unit), min(local + tile, (f + 1) * unit)
            if low >= high:
                continue
            begin = f * stride + rank * unit
            base = jnp.minimum(begin // 128, (source.shape[1] - window) // 128) * 128
            base = pl.multiple_of(base, 128)
            rows = lax.broadcasted_iota(jnp.int32, (window, tile), 0)
            columns = lax.broadcasted_iota(jnp.int32, (window, tile), 1)
            wanted = columns + (local - f * unit + begin - base)
            inside = (columns >= low - local) & (columns < high - local)
            chosen = jnp.where((rows == wanted) & inside, 1.0, 0.0).astype(jnp.bfloat16)
            total += jnp.dot(
                source[:, pl.ds(base, window)], chosen, preferred_element_type=jnp.float32
            )
        out[:, first : first + tile] = total.astype(jnp.bfloat16)


def pick_columns(w_gate, w_up, unit, stride, pieces, padded):
    rows, width = w_gate.shape
    window = 512
    return pl.pallas_call(
        lambda gate, up, out: pick_kernel(
            None, gate, up, out, unit=unit, stride=stride, pieces=pieces, window=window
        ),
        in_specs=[pl.BlockSpec(memory_space=pltpu.VMEM)] * 2,
        out_specs=pl.BlockSpec(memory_space=pltpu.VMEM),
        out_shape=jax.ShapeDtypeStruct((rows, 2 * padded), jnp.bfloat16),
        compiler_params=pltpu.CompilerParams(vmem_limit_bytes=48 * 2**20),
        cost_estimate=pl.CostEstimate(
            flops=2 * 2 * rows * 2 * padded * window, bytes_accessed=12 * 2**20, transcendentals=0
        ),
        name="pick_columns",
    )(w_gate, w_up)


def per_device(
    tokens, cotangent, lengths, balance, norm1_gain, w_query, b_query, w_key, b_key,
    w_value, b_value, w_out, norm2_gain, w_gate, w_up, w_down,
):
    seq_count = lax.axis_size("seq")
    fsdp_count = lax.axis_size("fsdp")
    seq_rank = lax.axis_index("seq")
    fsdp_rank = lax.axis_index("fsdp")
    rows_here, width = tokens.shape
    group = seq_count * rows_here
    kv_width = KV_HEADS * HEAD_DIM
    qkv_width = width + 2 * kv_width
    hidden_width = w_gate.shape[1]
    unit = hidden_width // (fsdp_count * seq_count)
    own_units = hidden_width // seq_count
    padded = -(-own_units // 256) * 256
    weight_rows = w_gate.shape[0]

    weight_qkv, first_got = gather_plane(jnp.concatenate([w_query, w_key, w_value], 1))
    small = jnp.concatenate([norm1_gain, norm2_gain, b_query, b_key, b_value], 0)[None]
    if fsdp_count == 8:
        small = place([small] + [cross(small, k) for k in range(1, 8)], fsdp_rank)
    else:
        small = lax.all_gather(small, "fsdp", axis=0, tiled=True)
    piece = norm1_gain.shape[0]
    bias_piece = b_key.shape[0]
    gain_one = small[:, :piece].reshape(-1).astype(jnp.float32)
    gain_two = small[:, piece : 2 * piece].reshape(-1).astype(jnp.float32)
    bias_qkv = jnp.concatenate(
        [
            small[:, 2 * piece : 3 * piece].reshape(-1),
            small[:, 3 * piece : 3 * piece + bias_piece].reshape(-1),
            small[:, 3 * piece + bias_piece :].reshape(-1),
        ],
        0,
    ).astype(jnp.float32)
    weight_out, second_got = gather_plane(w_out, first_got)
    picked = pick_columns(
        w_gate, w_up, unit, hidden_width // fsdp_count, fsdp_count, padded
    )
    weight_gu, third_got = gather_plane(picked, second_got)
    weight_down, _ = gather_plane(
        lax.dynamic_slice_in_dim(w_down, seq_rank * unit, unit, 0), third_got
    )
    weight_down = jnp.pad(weight_down, ((0, padded - own_units), (0, 0)))

    slot = (balance % group)[None]
    slots_all = jnp.concatenate([slot] + [shift(slot, j) for j in range(1, seq_count)], 1)[0]
    slot = slot[0]
    seq_lengths = lengths[0]
    starts = jnp.cumsum(seq_lengths) - seq_lengths
    segment = segment_of(slot, starts)
    first_row = jnp.where(segment == 0, starts[0], jnp.where(segment == 1, starts[1], starts[2]))
    cosine, sine = rope_tables(slot - first_row)
    allowed = (slots_all[:, None] <= slot[None, :]) & (slots_all[:, None] >= first_row[None, :])
    bias = jnp.where(allowed, 0.0, -1e30).astype(jnp.float32)

    inputs = tokens.astype(jnp.float32)
    normed_one = norm_piece(inputs, gain_one).astype(jnp.bfloat16)
    projected = jnp.dot(normed_one, weight_qkv, preferred_element_type=jnp.float32) + bias_qkv
    query_pre = projected[:, :width].reshape(rows_here, HEADS, HEAD_DIM)
    key_pre = projected[:, width : width + kv_width].reshape(rows_here, KV_HEADS, HEAD_DIM)
    value_pre = projected[:, width + kv_width :]
    queries = rotate(query_pre, cosine, sine).astype(jnp.bfloat16).reshape(rows_here, width)
    keys = rotate(key_pre, cosine, sine).astype(jnp.bfloat16).reshape(rows_here, kv_width)
    values = value_pre.astype(jnp.bfloat16)
    paired = jnp.concatenate([keys, values], 1)
    paired = [paired] + [shift(paired, j) for j in range(1, seq_count)]
    upstream_all = gather_seq(cotangent, lambda value: after(value, *paired[1:]))
    upstream_all = jnp.concatenate(upstream_all, 0)
    paired = jnp.concatenate(paired, 0)
    attended, logsum = attend(queries, paired, bias)
    resid = inputs + jnp.dot(attended, weight_out, preferred_element_type=jnp.float32)
    normed_two = norm_piece(resid, gain_two).astype(jnp.bfloat16)

    normed_all = jnp.concatenate(gather_seq(normed_two), 0)
    both = jnp.dot(normed_all, weight_gu, preferred_element_type=jnp.float32)
    gate = both[:, :padded]
    up = both[:, padded:]
    sigma = jax.nn.sigmoid(gate)
    activated = gate * sigma
    hidden = (activated * up).astype(jnp.bfloat16)
    d_hidden = contract_columns(upstream_all, weight_down)
    d_gate = (d_hidden * up * sigma * (1.0 + gate * (1.0 - sigma))).astype(jnp.bfloat16)
    d_up = (d_hidden * activated).astype(jnp.bfloat16)
    d_both = jnp.concatenate([d_gate, d_up], 1)
    columns = contract_columns(d_both, weight_gu).astype(jnp.bfloat16)
    columns = scatter_seq([columns[j * rows_here : (j + 1) * rows_here] for j in range(seq_count)])

    grad_down = contract_rows(hidden, upstream_all).astype(jnp.bfloat16)
    grad_down = scatter_plane(grad_down[:own_units]).astype(jnp.float32)
    grad_pair = scatter_plane(contract_rows(normed_all, d_both).astype(jnp.bfloat16))
    branch = jnp.dot(hidden, weight_down, preferred_element_type=jnp.float32).astype(jnp.bfloat16)
    branch = scatter_seq(
        [branch[j * rows_here : (j + 1) * rows_here] for j in range(seq_count)], (columns,)
    )
    layer_out = (resid + branch).astype(jnp.bfloat16)
    grad_pair = exchange_seq(grad_pair)
    own_rows = weight_rows // seq_count
    grad_pair = jnp.stack(grad_pair, 0).reshape(seq_count, own_rows, 2, padded)[..., :own_units]
    order = (seq_rank - jnp.arange(seq_count)) % seq_count
    grad_pair = grad_pair[order]
    grad_pair = grad_pair.reshape(seq_count, own_rows, 2, fsdp_count, unit)
    grad_pair = grad_pair.transpose(2, 1, 3, 0, 4).astype(jnp.float32)
    grad_pair = grad_pair.reshape(2, own_rows, hidden_width)

    _, pull_two = jax.vjp(norm_piece, resid, gain_two)
    d_resid_norm, grad_gain_two = pull_two(columns)
    d_resid = cotangent.astype(jnp.float32) + d_resid_norm
    d_branch = d_resid.astype(jnp.bfloat16)
    d_attended = contract_columns(d_branch, weight_out).astype(jnp.bfloat16)
    d_queries, d_keys, d_values = attend_back(queries, paired, bias, logsum, d_attended)
    d_paired = jnp.concatenate([d_keys, d_values], 1).astype(jnp.bfloat16)
    d_paired = [d_paired[j * rows_here : (j + 1) * rows_here] for j in range(seq_count)]
    d_paired = sum(
        part.astype(jnp.float32)
        for part in [d_paired[0]] + [shift(d_paired[j], -j) for j in range(1, seq_count)]
    )
    d_query_pre = rotate_back(
        d_queries.astype(jnp.float32).reshape(rows_here, HEADS, HEAD_DIM), cosine, sine
    ).astype(jnp.bfloat16)
    d_key_pre = rotate_back(
        d_paired[:, :kv_width].reshape(rows_here, KV_HEADS, HEAD_DIM), cosine, sine
    ).astype(jnp.bfloat16)
    d_value_pre = d_paired[:, kv_width:].astype(jnp.bfloat16)
    d_qkv = jnp.concatenate(
        [
            d_query_pre.reshape(rows_here, width),
            d_key_pre.reshape(rows_here, kv_width),
            d_value_pre,
        ],
        1,
    )
    grad_out = contract_rows(attended, d_branch).astype(jnp.bfloat16)
    grad_qkv = contract_rows(normed_one, d_qkv).astype(jnp.bfloat16)
    grad_bias = jnp.sum(d_qkv.astype(jnp.float32), 0)
    d_normed_one = contract_columns(d_qkv, weight_qkv)
    _, pull_one = jax.vjp(norm_piece, inputs, gain_one)
    d_input_norm, grad_gain_one = pull_one(d_normed_one)
    input_grad = (d_resid + d_input_norm).astype(jnp.bfloat16)

    def summed(value):
        return sum(part.astype(jnp.float32) for part in exchange_seq(scatter_plane(value)))

    grad_out = summed(grad_out)
    grad_qkv = summed(grad_qkv)
    vectors = jnp.concatenate([grad_gain_one, grad_gain_two, grad_bias], 0)
    if fsdp_count == 8:
        for bits in (1, 2, 4):
            vectors = vectors + cross(vectors, bits)
        vectors = vectors + sum(shift(vectors, j) for j in range(1, seq_count))
    else:
        vectors = lax.psum(vectors, ("fsdp", "seq"))
    own = width // (fsdp_count * seq_count)
    first = (fsdp_rank * seq_count + seq_rank) * own

    def own_part(offset):
        return lax.dynamic_slice_in_dim(vectors, offset + first, own, 0)

    biases = 2 * width
    return (
        layer_out,
        input_grad,
        own_part(0),
        grad_qkv[:, :width],
        own_part(biases),
        grad_qkv[:, width : width + kv_width],
        vectors[biases + width : biases + width + kv_width],
        grad_qkv[:, width + kv_width :],
        vectors[biases + width + kv_width :],
        grad_out,
        own_part(width),
        grad_pair[0],
        grad_pair[1],
        grad_down,
    )


def solution(mesh):
    both = P(("fsdp", "seq"), None)
    both_one = P(("fsdp", "seq"))
    placed = (
        both, both, P("fsdp", None), both_one, P("fsdp"), P("fsdp", None), P("fsdp"),
        P("fsdp", None), P("fsdp"), P("fsdp", None), P("fsdp"), P("fsdp", None), P("fsdp"),
        P("fsdp", None), P("fsdp", None), P("fsdp", None),
    )
    return jax.shard_map(
        per_device,
        mesh=mesh,
        in_specs=placed,
        out_specs=(
            both, both, both_one, both, both_one, both, P(), both, P(), both, both_one,
            both, both, both,
        ),
        check_vma=False,
    )
```

```python
import jax
import jax.numpy as jnp
import numpy as np
from jax import lax
from jax.experimental import pallas as pl
from jax.experimental.pallas import tpu as pltpu
from jax.sharding import PartitionSpec as P

HEADS = 12
KV_HEADS = 2
HEAD_DIM = 128

MESH = pl.DeviceIdType.MESH

epsilon = 1e-06
rope_base = 1000000.0


def norm_piece(values, gain):
    return values * lax.rsqrt(jnp.mean(values * values, -1, keepdims=True) + epsilon) * gain


def rope_tables(position):
    half = HEAD_DIM // 2
    inverse = rope_base ** (-(jnp.arange(half, dtype=jnp.float32) * 2.0 / HEAD_DIM))
    angle = position.astype(jnp.float32)[:, None] * inverse[None, :]
    cosine = jnp.concatenate([jnp.cos(angle), jnp.cos(angle)], -1)
    sine = jnp.concatenate([jnp.sin(angle), jnp.sin(angle)], -1)
    return (cosine, sine)


def turn_half(values):
    half = values.shape[-1] // 2
    return jnp.concatenate([-values[..., half:], values[..., :half]], -1)


def rotate(values, cosine, sine):
    return values * cosine[:, None, :] + turn_half(values) * sine[:, None, :]


def rotate_back(grads, cosine, sine):
    return grads * cosine[:, None, :] - turn_half(grads * sine[:, None, :])


def segment_of(slots, starts):
    return (slots >= starts[1]).astype(jnp.int32) + (slots >= starts[2]).astype(jnp.int32)


def contract_rows(left, right):
    return lax.dot_general(
        left, right, (((0,), (0,)), ((), ())), preferred_element_type=jnp.float32
    )


def contract_columns(left, right):
    return lax.dot_general(
        left, right, (((1,), (1,)), ((), ())), preferred_element_type=jnp.float32
    )


def after(value, *earlier):
    return lax.optimization_barrier((value, *earlier))[0]


def add_low(*values):
    return sum(value.astype(jnp.float32) for value in values).astype(jnp.bfloat16)


def cross(value, bits):
    count = lax.axis_size("fsdp")
    return lax.ppermute(value, "fsdp", [(i, i ^ bits) for i in range(count)])


def shift(value, step):
    count = lax.axis_size("seq")
    return lax.ppermute(value, "seq", [(i, (i + step) % count) for i in range(count)])


def place(parts, rank):
    rows = parts[0].shape[0]
    whole = jnp.zeros((len(parts) * rows,) + parts[0].shape[1:], parts[0].dtype)
    for k, part in enumerate(parts):
        whole = lax.dynamic_update_slice_in_dim(whole, part, (rank ^ k) * rows, 0)
    return whole


def gather_plane(block, earlier=()):
    if lax.axis_size("fsdp") != 8:
        whole = lax.all_gather(block, "fsdp", axis=0, tiled=True)
        return whole, ()
    rank = lax.axis_index("fsdp")
    half = block.shape[0] // 2
    if earlier:
        block = after(block, *earlier)
    from_x = cross(block, 2)
    from_y = cross(block, 4)
    diagonal = (cross(from_x[:half], 4), cross(from_y[half:], 2))
    from_core = cross(block, 1)
    both = cross(jnp.concatenate([from_x, from_y], 0), 1)
    diagonal = jnp.concatenate(diagonal, 0)
    rows = block.shape[0]
    parts = [
        block, from_core, from_x, both[:rows], from_y, both[rows:], diagonal, cross(diagonal, 1),
    ]
    return place(parts, rank), (from_x, from_y)


def scatter_plane(whole, earlier=()):
    count = lax.axis_size("fsdp")
    if count != 8:
        return lax.psum_scatter(whole, "fsdp", scatter_dimension=0, tiled=True)
    rank = lax.axis_index("fsdp")
    rows = whole.shape[0] // count
    half = whole.shape[1] // 2
    if earlier:
        whole = after(whole, *earlier)

    def part(k):
        return lax.dynamic_slice_in_dim(whole, (rank ^ k) * rows, rows, 0)

    arrived = cross(jnp.concatenate([part(1), part(3), part(5), part(7)], 0), 1)
    own, to_x, to_y, to_both = [
        add_low(part(2 * i), arrived[i * rows : (i + 1) * rows]) for i in range(4)
    ]
    got_x = cross(jnp.concatenate([to_x[:, :half], to_both[:, :half]], 0), 2)
    got_y = cross(jnp.concatenate([to_y[:, half:], to_both[:, half:]], 0), 4)
    last_y = cross(add_low(to_y[:, :half], got_x[rows:]), 4)
    last_x = cross(add_low(to_x[:, half:], got_y[rows:]), 2)
    return jnp.concatenate(
        [
            add_low(own[:, :half], got_x[:rows], last_y),
            add_low(own[:, half:], got_y[:rows], last_x),
        ],
        1,
    )


def chain_step(up, down, step):
    count = lax.axis_size("seq")
    up = lax.ppermute(up, "seq", [(i, i + 1) for i in range(step - 1, count - 1)])
    down = lax.ppermute(down, "seq", [(i, i - 1) for i in range(1, count - step + 1)])
    return up, down


def gather_seq(block, pause=None):
    count = lax.axis_size("seq")
    rank = lax.axis_index("seq")
    up, down = block, block
    ups, downs = [], []
    for step in range(1, count):
        if pause is not None and step == count - 1:
            up, down = pause(up), pause(down)
        up, down = chain_step(up, down, step)
        ups.append(up)
        downs.append(down)
    rest = [jnp.where(rank >= j, ups[j - 1], downs[count - j - 1]) for j in range(1, count)]
    return [block] + rest


def scatter_seq(parts, earlier=()):
    count = lax.axis_size("seq")
    up, down = None, None
    for step in range(1, count):
        send_up = parts[step] if up is None else add_low(parts[step], up)
        send_down = parts[count - step] if down is None else add_low(parts[count - step], down)
        if up is None and earlier:
            send_up = after(send_up, *earlier)
            send_down = after(send_down, *earlier)
        up = lax.ppermute(send_up, "seq", [(i, i + 1) for i in range(min(step, count - 1))])
        down = lax.ppermute(
            send_down, "seq", [(i, i - 1) for i in range(count - 1, max(count - 1 - step, 0), -1)]
        )
    return parts[0].astype(jnp.float32) + up.astype(jnp.float32) + down.astype(jnp.float32)


def exchange_seq(whole):
    count = lax.axis_size("seq")
    rank = lax.axis_index("seq")
    rows = whole.shape[0] // count

    def part(step):
        return lax.dynamic_slice_in_dim(whole, ((rank + step) % count) * rows, rows, 0)

    return [part(0)] + [shift(part(step), step) for step in range(1, count)]


def attend_back_kernel(query, key, value, bias, logsum, grad, d_query, d_key, d_value):
    scale = HEAD_DIM ** (-0.5)
    repeat = HEADS // KV_HEADS
    raw = lax.dot_general(
        key[...], query[...], (((1,), (1,)), ((), ())), preferred_element_type=jnp.float32
    )
    probs = jnp.exp(raw * scale + bias[...] - logsum[0:1])
    d_probs = lax.dot_general(
        value[...], grad[...], (((1,), (1,)), ((), ())), preferred_element_type=jnp.float32
    )
    delta = jnp.sum(probs * d_probs, 0, keepdims=True)
    d_score = (probs * (d_probs - delta)).astype(jnp.bfloat16)
    turned = lax.dot_general(
        key[...], d_score, (((0,), (0,)), ((), ())), preferred_element_type=jnp.float32
    )
    d_query[...] = (turned * scale).T.astype(jnp.bfloat16)
    key_part = jnp.dot(d_score, query[...], preferred_element_type=jnp.float32) * scale
    value_part = jnp.dot(
        probs.astype(jnp.bfloat16), grad[...], preferred_element_type=jnp.float32
    )

    @pl.when(pl.program_id(0) % repeat == 0)
    def _():
        d_key[...] = key_part
        d_value[...] = value_part

    @pl.when(pl.program_id(0) % repeat != 0)
    def _():
        d_key[...] += key_part
        d_value[...] += value_part


def attend_back(queries, paired, bias, logsum, grads):
    rows, width = queries.shape
    group = paired.shape[0]
    repeat = HEADS // KV_HEADS
    return pl.pallas_call(
        attend_back_kernel,
        grid=(HEADS,),
        in_specs=[
            pl.BlockSpec((rows, HEAD_DIM), lambda h: (0, h)),
            pl.BlockSpec((group, HEAD_DIM), lambda h: (0, h // repeat)),
            pl.BlockSpec((group, HEAD_DIM), lambda h: (0, KV_HEADS + h // repeat)),
            pl.BlockSpec((group, rows), lambda h: (0, 0)),
            pl.BlockSpec((8, rows), lambda h: (h, 0)),
            pl.BlockSpec((rows, HEAD_DIM), lambda h: (0, h)),
        ],
        out_specs=[
            pl.BlockSpec((rows, HEAD_DIM), lambda h: (0, h)),
            pl.BlockSpec((group, HEAD_DIM), lambda h: (0, h // repeat)),
            pl.BlockSpec((group, HEAD_DIM), lambda h: (0, h // repeat)),
        ],
        out_shape=[
            jax.ShapeDtypeStruct((rows, width), jnp.bfloat16),
            jax.ShapeDtypeStruct((group, KV_HEADS * HEAD_DIM), jnp.float32),
            jax.ShapeDtypeStruct((group, KV_HEADS * HEAD_DIM), jnp.float32),
        ],
        compiler_params=pltpu.CompilerParams(vmem_limit_bytes=48 * 2**20),
        cost_estimate=pl.CostEstimate(
            flops=10 * HEADS * rows * group * HEAD_DIM * 3, bytes_accessed=8 * 2**20, transcendentals=HEADS * rows * group
        ),
        name="attend_back",
    )(queries, paired, paired, bias, logsum, grads)


def plain_device(
    tokens, cotangent, lengths, balance, norm1_gain, w_query, b_query, w_key, b_key,
    w_value, b_value, w_out, norm2_gain, w_gate, w_up, w_down,
):
    seq_count = lax.axis_size("seq")
    fsdp_count = lax.axis_size("fsdp")
    seq_rank = lax.axis_index("seq")
    rows_here, width = tokens.shape
    group = seq_count * rows_here
    kv_width = KV_HEADS * HEAD_DIM
    qkv_width = width + 2 * kv_width
    hidden_width = w_gate.shape[1]
    unit = hidden_width // (fsdp_count * seq_count)
    own_units = hidden_width // seq_count
    weight_rows = w_gate.shape[0]
    score_scale = HEAD_DIM ** (-0.5)
    repeat = HEADS // KV_HEADS

    slot = balance % group
    slots_all = lax.all_gather(slot, "seq", axis=0, tiled=True)
    seq_lengths = lengths[0]
    starts = jnp.cumsum(seq_lengths) - seq_lengths
    segment = segment_of(slot, starts)
    segments_all = segment_of(slots_all, starts)
    first_row = jnp.where(segment == 0, starts[0], jnp.where(segment == 1, starts[1], starts[2]))
    cosine, sine = rope_tables(slot - first_row)
    allowed = (segment[:, None] == segments_all[None, :]) & (slots_all[None, :] <= slot[:, None])

    small = jnp.concatenate([norm1_gain, norm2_gain, b_query, b_key, b_value], 0)[None]
    small = lax.all_gather(small, "fsdp", axis=0, tiled=True)
    piece = norm1_gain.shape[0]
    bias_piece = b_key.shape[0]
    gain_one = small[:, :piece].reshape(-1).astype(jnp.float32)
    gain_two = small[:, piece : 2 * piece].reshape(-1).astype(jnp.float32)
    bias_qkv = jnp.concatenate(
        [
            small[:, 2 * piece : 3 * piece].reshape(-1),
            small[:, 3 * piece : 3 * piece + bias_piece].reshape(-1),
            small[:, 3 * piece + bias_piece :].reshape(-1),
        ],
        0,
    ).astype(jnp.float32)
    weight_qkv = lax.all_gather(
        jnp.concatenate([w_query, w_key, w_value], 1), "fsdp", axis=0, tiled=True
    )
    weight_out = lax.all_gather(w_out, "fsdp", axis=0, tiled=True)
    upstream_all = lax.all_gather(cotangent, "seq", axis=0, tiled=True)

    def own_columns(weight):
        cut = weight.reshape(weight_rows, fsdp_count, seq_count, unit)
        return lax.dynamic_index_in_dim(cut, seq_rank, 2, False).reshape(weight_rows, own_units)

    weight_gu = lax.all_gather(
        jnp.concatenate([own_columns(w_gate), own_columns(w_up)], 1), "fsdp", axis=0, tiled=True
    )
    weight_down = lax.all_gather(
        lax.dynamic_slice_in_dim(w_down, seq_rank * unit, unit, 0), "fsdp", axis=0, tiled=True
    )

    inputs = tokens.astype(jnp.float32)
    normed_one = norm_piece(inputs, gain_one).astype(jnp.bfloat16)
    projected = jnp.dot(normed_one, weight_qkv, preferred_element_type=jnp.float32) + bias_qkv
    query_pre = projected[:, :width].reshape(rows_here, HEADS, HEAD_DIM)
    key_pre = projected[:, width : width + kv_width].reshape(rows_here, KV_HEADS, HEAD_DIM)
    value_pre = projected[:, width + kv_width :]
    queries = rotate(query_pre, cosine, sine).astype(jnp.bfloat16)
    keys = rotate(key_pre, cosine, sine).astype(jnp.bfloat16).reshape(rows_here, kv_width)
    values = value_pre.astype(jnp.bfloat16)
    paired = lax.all_gather(jnp.concatenate([keys, values], 1), "seq", axis=0, tiled=True)
    keys_all = paired[:, :kv_width].reshape(group, KV_HEADS, HEAD_DIM)
    values_all = paired[:, kv_width:].reshape(group, KV_HEADS, HEAD_DIM)
    grouped = queries.reshape(rows_here, KV_HEADS, repeat, HEAD_DIM)
    raw = (
        jnp.einsum("qgrd,kgd->grqk", grouped, keys_all, preferred_element_type=jnp.float32)
        * score_scale
    )
    scores = jnp.where(allowed, raw, -jnp.inf)
    expo = jnp.exp(scores - jnp.max(scores, -1, keepdims=True))
    probs = expo / jnp.sum(expo, -1, keepdims=True)
    probs_low = probs.astype(jnp.bfloat16)
    attended = jnp.einsum(
        "grqk,kgd->qgrd", probs_low, values_all, preferred_element_type=jnp.float32
    )
    attended = attended.astype(jnp.bfloat16).reshape(rows_here, width)
    resid = inputs + jnp.dot(attended, weight_out, preferred_element_type=jnp.float32)
    normed_two = norm_piece(resid, gain_two).astype(jnp.bfloat16)

    normed_all = lax.all_gather(normed_two, "seq", axis=0, tiled=True)
    both = jnp.dot(normed_all, weight_gu, preferred_element_type=jnp.float32)
    gate = both[:, :own_units]
    up = both[:, own_units:]
    sigma = jax.nn.sigmoid(gate)
    activated = gate * sigma
    hidden = (activated * up).astype(jnp.bfloat16)
    d_hidden = contract_columns(upstream_all, weight_down)
    d_gate = (d_hidden * up * sigma * (1.0 + gate * (1.0 - sigma))).astype(jnp.bfloat16)
    d_up = (d_hidden * activated).astype(jnp.bfloat16)
    d_both = jnp.concatenate([d_gate, d_up], 1)
    columns = lax.psum_scatter(
        contract_columns(d_both, weight_gu).astype(jnp.bfloat16),
        "seq", scatter_dimension=0, tiled=True,
    ).astype(jnp.float32)
    branch = lax.psum_scatter(
        jnp.dot(hidden, weight_down, preferred_element_type=jnp.float32).astype(jnp.bfloat16),
        "seq", scatter_dimension=0, tiled=True,
    ).astype(jnp.float32)
    layer_out = (resid + branch).astype(jnp.bfloat16)
    grad_down = lax.psum_scatter(
        contract_rows(hidden, upstream_all).astype(jnp.bfloat16),
        "fsdp", scatter_dimension=0, tiled=True,
    ).astype(jnp.float32)
    grad_pair = lax.psum_scatter(
        contract_rows(normed_all, d_both).astype(jnp.bfloat16),
        "fsdp", scatter_dimension=0, tiled=True,
    )
    grad_pair = lax.all_to_all(grad_pair, "seq", split_axis=0, concat_axis=0, tiled=True)
    grad_pair = grad_pair.reshape(seq_count, weight_rows // seq_count, 2, fsdp_count, unit)
    grad_pair = grad_pair.transpose(2, 1, 3, 0, 4).astype(jnp.float32)
    grad_pair = grad_pair.reshape(2, weight_rows // seq_count, hidden_width)

    _, pull_two = jax.vjp(norm_piece, resid, gain_two)
    d_resid_norm, grad_gain_two = pull_two(columns)
    d_resid = cotangent.astype(jnp.float32) + d_resid_norm
    d_branch = d_resid.astype(jnp.bfloat16)
    grad_out = contract_rows(attended, d_branch).astype(jnp.bfloat16)
    d_attended = contract_columns(d_branch, weight_out).astype(jnp.bfloat16)
    d_attended = d_attended.reshape(rows_here, KV_HEADS, repeat, HEAD_DIM)
    d_probs = jnp.einsum(
        "qgrd,kgd->grqk", d_attended, values_all, preferred_element_type=jnp.float32
    )
    delta = jnp.sum(probs * d_probs, -1, keepdims=True)
    d_score = (probs * (d_probs - delta)).astype(jnp.bfloat16)
    d_queries = (
        jnp.einsum("grqk,kgd->qgrd", d_score, keys_all, preferred_element_type=jnp.float32)
        * score_scale
    )
    d_keys = (
        jnp.einsum("grqk,qgrd->kgd", d_score, grouped, preferred_element_type=jnp.float32)
        * score_scale
    )
    d_values = jnp.einsum(
        "grqk,qgrd->kgd", probs_low, d_attended, preferred_element_type=jnp.float32
    )
    d_paired = jnp.concatenate([d_keys.reshape(group, kv_width), d_values.reshape(group, kv_width)], 1)
    d_paired = lax.psum_scatter(
        d_paired.astype(jnp.bfloat16), "seq", scatter_dimension=0, tiled=True
    ).astype(jnp.float32)
    d_query_pre = rotate_back(
        d_queries.reshape(rows_here, HEADS, HEAD_DIM), cosine, sine
    ).astype(jnp.bfloat16)
    d_key_pre = rotate_back(
        d_paired[:, :kv_width].reshape(rows_here, KV_HEADS, HEAD_DIM), cosine, sine
    ).astype(jnp.bfloat16)
    d_value_pre = d_paired[:, kv_width:].astype(jnp.bfloat16)
    d_qkv = jnp.concatenate(
        [
            d_query_pre.reshape(rows_here, width),
            d_key_pre.reshape(rows_here, kv_width),
            d_value_pre,
        ],
        1,
    )
    grad_qkv = contract_rows(normed_one, d_qkv).astype(jnp.bfloat16)
    grad_bias = jnp.sum(d_qkv.astype(jnp.float32), 0)
    d_normed_one = contract_columns(d_qkv, weight_qkv)
    _, pull_one = jax.vjp(norm_piece, inputs, gain_one)
    d_input_norm, grad_gain_one = pull_one(d_normed_one)
    input_grad = (d_resid + d_input_norm).astype(jnp.bfloat16)

    def summed(value):
        value = lax.psum_scatter(value, "fsdp", scatter_dimension=0, tiled=True)
        return lax.psum_scatter(value, "seq", scatter_dimension=0, tiled=True).astype(jnp.float32)

    grad_out = summed(grad_out)
    grad_qkv = summed(grad_qkv)
    vectors = lax.psum(
        jnp.concatenate([grad_gain_one, grad_gain_two, grad_bias], 0), ("fsdp", "seq")
    )
    own = width // (fsdp_count * seq_count)
    first = (lax.axis_index("fsdp") * seq_count + seq_rank) * own

    def own_part(offset):
        return lax.dynamic_slice_in_dim(vectors, offset + first, own, 0)

    biases = 2 * width
    return (
        layer_out,
        input_grad,
        own_part(0),
        grad_qkv[:, :width],
        own_part(biases),
        grad_qkv[:, width : width + kv_width],
        vectors[biases + width : biases + width + kv_width],
        grad_qkv[:, width + kv_width :],
        vectors[biases + width + kv_width :],
        grad_out,
        own_part(width),
        grad_pair[0],
        grad_pair[1],
        grad_down,
    )


def front_kernel(
    tokens, cotangent, small, slot_keys, slot_row, first_row, cosine, sine,
    w_query, w_key, w_value, w_out, w_gate, w_up, w_down,
    gu_all, down_all, upstream_all, normed_all, qkv_out, out_out,
    queries, paired_out, slots_out, logsum, attended, resid, normed_one, gain_one, gain_two,
    qkv, out_w, gate_v, up_v, gu_own, kv, small_all, slots_all, bias, normed_own,
    local, ssem, rsem, zsend, zrecv,
):
    f = lax.axis_index("fsdp")
    s = lax.axis_index("seq")
    rows, width = tokens.shape
    n_f, n_s = 8, slots_all.shape[0]
    block = w_query.shape[0]
    unit = w_down.shape[0]
    kv_width = KV_HEADS * HEAD_DIM
    qkv_width = width + 2 * kv_width
    scale = HEAD_DIM ** (-0.5)
    repeat = HEADS // KV_HEADS
    plane = [f ^ k for k in range(n_f)]

    entry = pltpu.get_barrier_semaphore()
    for k in range(1, n_f):
        pl.semaphore_signal(entry, inc=1, device_id={"fsdp": plane[k]}, device_id_type=MESH)
    for j in range(1, n_s):
        pl.semaphore_signal(
            entry, inc=1, device_id={"seq": lax.rem(s + j, n_s)}, device_id_type=MESH
        )

    def here(source, target, index):
        return pltpu.make_async_copy(source, target, local.at[index])

    def there(source, target, index, **device):
        return pltpu.make_async_remote_copy(
            src_ref=source, dst_ref=target, send_sem=ssem.at[index], recv_sem=rsem.at[index],
            device_id=device, device_id_type=MESH,
        )

    def own_rows(ref, owner, size, start=0, count=None):
        first = pl.multiple_of(owner * size + start, 16)
        return ref.at[pl.ds(first, size if count is None else count)]

    class Gather:
        def __init__(self, source, target, size, index):
            half = size // 2
            x, y, c = plane[2], plane[4], plane[1]
            self.own = here(source, own_rows(target, f, size), index // 8) if source is not None else None
            if source is None:
                source = own_rows(target, f, size)
            mine = own_rows(target, f, size)
            self.first = [
                there(source, mine, index, fsdp=x),
                there(source, mine, index + 1, fsdp=y),
                there(source, mine, index + 2, fsdp=c),
            ]
            from_x, from_y = own_rows(target, x, size), own_rows(target, y, size)
            part_x = own_rows(target, x, size, 0, half)
            part_y = own_rows(target, y, size, half, half)
            self.second = [
                there(part_x, part_x, index + 3, fsdp=y),
                there(part_y, part_y, index + 4, fsdp=x),
                there(from_x, from_x, index + 5, fsdp=c),
                there(from_y, from_y, index + 6, fsdp=c),
            ]
            diagonal = own_rows(target, plane[6], size)
            self.third = there(diagonal, diagonal, index + 7, fsdp=c)

        def start(self):
            if self.own is not None:
                self.own.start()
            for copy in self.first:
                copy.start()

        def forward(self):
            self.first[0].wait_recv()
            self.second[0].start()
            self.second[2].start()
            self.first[1].wait_recv()
            self.second[1].start()
            self.second[3].start()

        def last(self):
            self.second[0].wait_recv()
            self.second[1].wait_recv()
            self.third.start()

        def finish(self):
            if self.own is not None:
                self.own.wait()
            self.first[2].wait_recv()
            self.second[2].wait_recv()
            self.second[3].wait_recv()
            self.third.wait_recv()

        def sent(self):
            for copy in self.first + self.second + [self.third]:
                copy.wait_send()

    class Chain:
        def __init__(self, target, index):
            self.steps = []
            for step in range(1, n_s):
                up = own_rows(target, s - (step - 1), rows)
                down = own_rows(target, s + (step - 1), rows)
                i = index + 2 * (step - 1)
                self.steps.append((
                    pltpu.make_async_remote_copy(
                        src_ref=up, dst_ref=up, send_sem=zsend.at[i], recv_sem=zrecv.at[i],
                        device_id={"seq": s + 1}, device_id_type=MESH,
                    ),
                    pltpu.make_async_remote_copy(
                        src_ref=down, dst_ref=down, send_sem=zsend.at[i + 1], recv_sem=zrecv.at[i + 1],
                        device_id={"seq": s - 1}, device_id_type=MESH,
                    ),
                    (s >= step - 1) & (s < n_s - 1),
                    (s >= 1) & (s <= n_s - step),
                    s >= step,
                    s <= n_s - 1 - step,
                ))

        def send(self, step):
            up, down, can_up, can_down, _, _ = self.steps[step - 1]
            pl.when(can_up)(up.start)
            pl.when(can_down)(down.start)

        def receive(self, step):
            up, down, _, _, from_below, from_above = self.steps[step - 1]
            pl.when(from_below)(up.wait_recv)
            pl.when(from_above)(down.wait_recv)

        def sent(self):
            for up, down, can_up, can_down, _, _ in self.steps:
                pl.when(can_up)(up.wait_send)
                pl.when(can_down)(down.wait_send)

    pieces = [
        here(w_query, qkv.at[pl.ds(pl.multiple_of(f * block, 16), block), pl.ds(0, width)], 5),
        here(w_key, qkv.at[pl.ds(pl.multiple_of(f * block, 16), block), pl.ds(width, kv_width)], 6),
        here(w_value, qkv.at[pl.ds(pl.multiple_of(f * block, 16), block), pl.ds(width + kv_width, kv_width)], 7),
        here(cotangent, own_rows(upstream_all, s, rows), 8),
    ]
    load_gate = here(w_gate, gate_v, 9)
    load_up = here(w_up, up_v, 10)
    for copy in pieces:
        copy.start()
    load_gate.start()
    load_up.start()
    small_all[f] = small[...]
    slots_all[s] = slot_keys[...]

    gather_qkv = Gather(None, qkv, block, 0)
    gather_out = Gather(w_out, out_w, block, 8)
    gather_gu = Gather(gu_own, gu_all, block, 16)
    gather_down = Gather(w_down, down_all, unit, 24)
    chain_up = Chain(upstream_all, 0)
    chain_normed = Chain(normed_all, 6)
    send_small = [
        there(small, small_all.at[f], 32 + k, fsdp=plane[k]) for k in range(1, n_f)
    ]
    send_slots = [
        there(slot_keys, slots_all.at[s], 40 + j, seq=lax.rem(s + j, n_s)) for j in range(1, n_s)
    ]
    send_kv = [
        there(kv.at[s], kv.at[s], 44 + j, seq=lax.rem(s + j, n_s)) for j in range(1, n_s)
    ]
    for copy in pieces[:3]:
        copy.wait()
    pl.semaphore_wait(entry, n_f - 1 + n_s - 1)
    gather_qkv.start()
    for copy in send_small + send_slots:
        copy.start()
    pieces[3].wait()
    chain_up.send(1)

    load_gate.wait()
    load_up.wait()
    pick_units(gate_v, up_v, gu_own, w_gate.shape[1] // n_f, w_gate.shape[1] // (n_f * n_s), unit)

    for copy in send_small + send_slots:
        copy.wait_recv()
    third = 2 * block
    for i in range(n_f // 2):
        columns = slice(i * third, (i + 1) * third)
        gain_one[:, columns] = (
            small_all[2 * i, 0:1, :third].astype(jnp.float32)
            + small_all[2 * i + 1, 0:1, :third].astype(jnp.float32)
        )
        gain_two[:, columns] = (
            small_all[2 * i, 0:1, third : 2 * third].astype(jnp.float32)
            + small_all[2 * i + 1, 0:1, third : 2 * third].astype(jnp.float32)
        )
    bias_query = [
        small_all[2 * i, 0:1, 2 * third : 3 * third].astype(jnp.float32)
        + small_all[2 * i + 1, 0:1, 2 * third : 3 * third].astype(jnp.float32)
        for i in range(n_f // 2)
    ]
    bias_query = jnp.concatenate(bias_query, 1)
    bias_pair = sum(small_all[i, 0:1, 3 * third :].astype(jnp.float32) for i in range(n_f))

    inputs = tokens[...].astype(jnp.float32)
    root = lax.rsqrt(jnp.mean(inputs * inputs, -1, keepdims=True) + epsilon)
    normed_one[...] = (inputs * root * gain_one[...]).astype(jnp.bfloat16)
    for j in range(n_s):
        keys_slot = slots_all[j]
        keys_slot = jnp.concatenate([keys_slot] * (rows // 128), 1)
        ok = (keys_slot <= slot_row[0:1]) & (keys_slot >= first_row[0:1])
        bias[j * rows : (j + 1) * rows] = jnp.where(ok, 0.0, -1e30)

    gather_qkv.forward()
    gather_out.start()
    chain_up.receive(1)
    chain_up.send(2)
    gather_qkv.last()
    gather_qkv.finish()
    save_qkv = here(qkv, qkv_out, 11)
    save_qkv.start()

    def turned(value):
        return value * cosine[...] + pltpu.roll(value, HEAD_DIM // 2, 1) * sine[...]

    normed = normed_one[...]
    pair = jnp.dot(normed, qkv[:, width : width + kv_width], preferred_element_type=jnp.float32)
    pair = pair + bias_pair[:, :kv_width]
    for g in range(KV_HEADS):
        columns = slice(g * HEAD_DIM, (g + 1) * HEAD_DIM)
        kv[s, :, columns] = turned(pair[:, columns]).astype(jnp.bfloat16)
    pair = jnp.dot(normed, qkv[:, width + kv_width :], preferred_element_type=jnp.float32)
    kv[s, :, kv_width:] = (pair + bias_pair[:, kv_width:]).astype(jnp.bfloat16)
    for copy in send_kv:
        copy.start()
    for g in range(HEADS // 2):
        columns = slice(g * 2 * HEAD_DIM, (g + 1) * 2 * HEAD_DIM)
        pair = jnp.dot(normed, qkv[:, columns], preferred_element_type=jnp.float32)
        pair = pair + bias_query[:, columns]
        for h in range(2):
            part = turned(pair[:, h * HEAD_DIM : (h + 1) * HEAD_DIM]).astype(jnp.bfloat16)
            queries[:, (2 * g + h) * HEAD_DIM : (2 * g + h + 1) * HEAD_DIM] = part

    gather_out.forward()
    gather_gu.start()
    chain_up.receive(2)
    gather_out.last()
    for copy in send_kv:
        copy.wait_recv()
    chain_up.send(3)
    save_kv = here(kv, paired_out, 12)
    save_kv.start()
    slots_out[...] = slots_all[...]

    for g in range(KV_HEADS):
        keys = kv[:, :, g * HEAD_DIM : (g + 1) * HEAD_DIM].reshape(n_s * rows, HEAD_DIM)
        values = kv[:, :, kv_width + g * HEAD_DIM : kv_width + (g + 1) * HEAD_DIM]
        values = values.reshape(n_s * rows, HEAD_DIM)

        def head(i, carry, g=g, keys=keys, values=values):
            h = g * repeat + i
            columns = pl.ds(pl.multiple_of(h * HEAD_DIM, HEAD_DIM), HEAD_DIM)
            raw = lax.dot_general(
                keys, queries[:, columns], (((1,), (1,)), ((), ())),
                preferred_element_type=jnp.float32,
            )
            scores = raw * scale + bias[...]
            top = jnp.max(scores, 0, keepdims=True)
            expo = jnp.exp(scores - top)
            total = jnp.sum(expo, 0, keepdims=True)
            probs = (expo * (1.0 / total)).astype(jnp.bfloat16)
            mixed = lax.dot_general(
                values, probs, (((0,), (0,)), ((), ())), preferred_element_type=jnp.float32
            )
            attended[:, columns] = mixed.T.astype(jnp.bfloat16)
            logsum[pl.ds(pl.multiple_of(h * 8, 8), 8)] = jnp.broadcast_to(
                top + jnp.log(total), (8, rows)
            )
            return carry

        lax.fori_loop(0, repeat, head, 0)

    gather_out.finish()
    save_out = here(out_w, out_out, 13)
    save_out.start()
    mixed = attended[...]
    for g in range(width // 256):
        columns = slice(g * 256, (g + 1) * 256)
        part = jnp.dot(mixed, out_w[:, columns], preferred_element_type=jnp.float32)
        resid[:, columns] = tokens[:, columns].astype(jnp.float32) + part
    value = resid[...]
    root = lax.rsqrt(jnp.mean(value * value, -1, keepdims=True) + epsilon)
    normed_own[...] = (value * root * gain_two[...]).astype(jnp.bfloat16)
    place_normed = here(normed_own, own_rows(normed_all, s, rows), 14)
    place_normed.start()
    place_normed.wait()
    chain_normed.send(1)

    gather_gu.forward()
    gather_down.start()
    chain_normed.receive(1)
    chain_normed.send(2)
    gather_gu.last()
    chain_normed.receive(2)
    chain_normed.send(3)
    chain_up.receive(3)
    gather_down.forward()
    gather_gu.finish()
    gather_down.last()
    chain_normed.receive(3)
    gather_down.finish()
    save_qkv.wait()
    save_kv.wait()
    save_out.wait()
    for part in (gather_qkv, gather_out, gather_gu, gather_down, chain_up, chain_normed):
        part.sent()
    for copy in send_small + send_slots + send_kv:
        copy.wait_send()


def pick_units(gate, up, out, stride, unit, padded):
    rank = lax.axis_index("seq")
    pieces = gate.shape[1] // stride
    half = out.shape[1] // 2
    window, tile = 512, 128
    rows = lax.broadcasted_iota(jnp.int32, (window, tile), 0)
    columns = lax.broadcasted_iota(jnp.int32, (window, tile), 1)
    for first in range(0, 2 * half, tile):
        source = gate if first < half else up
        local = first % half
        total = jnp.zeros((out.shape[0], tile), jnp.float32)
        for f in range(pieces):
            low = max(local, f * padded)
            high = min(local + tile, f * padded + unit)
            if low >= high:
                continue
            begin = f * stride + rank * unit
            base = jnp.minimum(begin // 128, (source.shape[1] - window) // 128) * 128
            base = pl.multiple_of(base, 128)
            wanted = columns + (local - f * padded + begin - base)
            inside = (columns >= low - local) & (columns < high - local)
            chosen = jnp.where((rows == wanted) & inside, 1.0, 0.0).astype(jnp.bfloat16)
            total += jnp.dot(
                source[:, pl.ds(base, window)], chosen, preferred_element_type=jnp.float32
            )
        out[:, first : first + tile] = total.astype(jnp.bfloat16)


def front(tokens, cotangent, small, slot, first_row, cosine, sine, weights, w_down_own):
    rows, width = tokens.shape
    n_s = lax.axis_size("seq")
    w_query, w_key, w_value, w_out, w_gate, w_up = weights
    block = w_query.shape[0]
    unit = w_down_own.shape[0]
    kv_width = KV_HEADS * HEAD_DIM
    qkv_width = width + 2 * kv_width
    units = 8 * unit
    group = n_s * rows
    low, full = jnp.bfloat16, jnp.float32
    slot_f = slot.astype(full)
    slot_keys = jnp.broadcast_to(slot_f[:, None], (rows, 128))
    slot_row = jnp.broadcast_to(slot_f[None], (8, rows))
    first_f = jnp.broadcast_to(first_row.astype(full)[None], (8, rows))
    half = HEAD_DIM // 2
    sine = jnp.concatenate([-sine[:, :half], sine[:, half:]], 1)
    vmem = pl.BlockSpec(memory_space=pltpu.VMEM)
    hbm = pl.BlockSpec(memory_space=pl.ANY)
    shape = jax.ShapeDtypeStruct
    return pl.pallas_call(
        front_kernel,
        in_specs=[vmem, hbm] + [vmem] * 6 + [hbm] * 7,
        out_specs=[hbm] * 6 + [vmem, hbm] + [vmem] * 7,
        out_shape=[
            shape((8 * block, 2 * units), low),
            shape((units, width), low),
            shape((group, width), low),
            shape((group, width), low),
            shape((width, qkv_width), low),
            shape((width, width), low),
            shape((rows, width), low),
            shape((n_s, rows, 2 * kv_width), low),
            shape((n_s, rows, 128), full),
            shape((8 * HEADS, rows), full),
            shape((rows, width), low),
            shape((rows, width), full),
            shape((rows, width), low),
            shape((1, width), full),
            shape((1, width), full),
        ],
        scratch_shapes=[
            pltpu.VMEM((width, qkv_width), low),
            pltpu.VMEM((width, width), low),
            pltpu.VMEM(w_gate.shape, low),
            pltpu.VMEM(w_up.shape, low),
            pltpu.VMEM((block, 2 * units), low),
            pltpu.VMEM((n_s, rows, 2 * kv_width), low),
            pltpu.VMEM((8,) + small.shape, low),
            pltpu.VMEM((n_s, rows, 128), full),
            pltpu.VMEM((group, rows), full),
            pltpu.VMEM((rows, width), low),
            pltpu.SemaphoreType.DMA((16,)),
            pltpu.SemaphoreType.DMA((48,)),
            pltpu.SemaphoreType.DMA((48,)),
            pltpu.SemaphoreType.DMA((12,)),
            pltpu.SemaphoreType.DMA((12,)),
        ],
        compiler_params=pltpu.CompilerParams(
            collective_id=0, has_side_effects=True, vmem_limit_bytes=56 * 2**20
        ),
        name="front",
    )(
        tokens, cotangent, small, slot_keys, slot_row, first_f, cosine, sine,
        w_query, w_key, w_value, w_out, w_gate, w_up, w_down_own,
    )


def per_device(
    tokens, cotangent, lengths, balance, norm1_gain, w_query, b_query, w_key, b_key,
    w_value, b_value, w_out, norm2_gain, w_gate, w_up, w_down,
):
    seq_count = lax.axis_size("seq")
    fsdp_count = lax.axis_size("fsdp")
    seq_rank = lax.axis_index("seq")
    fsdp_rank = lax.axis_index("fsdp")
    rows_here, width = tokens.shape
    group = seq_count * rows_here
    kv_width = KV_HEADS * HEAD_DIM
    qkv_width = width + 2 * kv_width
    hidden_width = w_gate.shape[1]
    unit = hidden_width // (fsdp_count * seq_count)
    own_units = hidden_width // seq_count
    padded = fsdp_count * (-(-unit // 16) * 16)
    weight_rows = w_gate.shape[0]

    unit_pad = -(-unit // 16) * 16
    pair_bias = jnp.concatenate([jnp.tile(b_key, fsdp_count), jnp.tile(b_value, fsdp_count)])
    small = jnp.concatenate([norm1_gain] * 2 + [norm2_gain] * 2 + [b_query] * 2 + [pair_bias])
    place_of = np.concatenate(
        [np.repeat([0, 1], weight_rows)] * 3 + [8 + np.repeat(np.arange(8), b_key.shape[0])] * 2
    )
    place_of = jnp.asarray(place_of, jnp.int32)
    mine = (place_of == fsdp_rank % 2) | (place_of == 8 + fsdp_rank)
    small = jnp.broadcast_to(jnp.where(mine, small, 0)[None], (16, small.shape[0]))

    slot = balance % group
    seq_lengths = lengths[0]
    starts = jnp.cumsum(seq_lengths) - seq_lengths
    segment = segment_of(slot, starts)
    first_row = jnp.where(segment == 0, starts[0], jnp.where(segment == 1, starts[1], starts[2]))
    cosine, sine = rope_tables(slot - first_row)
    down_own = lax.dynamic_slice_in_dim(w_down, seq_rank * unit, unit, 0)
    down_own = jnp.pad(down_own, ((0, unit_pad - unit), (0, 0)))
    (
        weight_gu, weight_down, upstream_all, normed_all, weight_qkv, weight_out,
        queries, paired, slots_all, logsum, attended, resid, normed_one, gain_one, gain_two,
    ) = front(
        tokens, cotangent, small, slot, first_row, cosine, sine,
        (w_query, w_key, w_value, w_out, w_gate, w_up), down_own,
    )
    gain_one, gain_two = gain_one[0], gain_two[0]
    paired = paired.reshape(group, 2 * kv_width)
    slots_all = slots_all[:, :, 0].reshape(group)
    slot = slot.astype(jnp.float32)
    allowed = (slots_all[:, None] <= slot[None, :]) & (
        slots_all[:, None] >= first_row.astype(jnp.float32)[None, :]
    )
    bias = jnp.where(allowed, 0.0, -1e30).astype(jnp.float32)
    inputs = tokens.astype(jnp.float32)

    def blocks_back(value):
        return [
            lax.dynamic_slice_in_dim(value, ((seq_rank - j) % seq_count) * rows_here, rows_here, 0)
            for j in range(seq_count)
        ]

    both = jnp.dot(normed_all, weight_gu, preferred_element_type=jnp.float32)
    gate = both[:, :padded]
    up = both[:, padded:]
    sigma = jax.nn.sigmoid(gate)
    activated = gate * sigma
    hidden = (activated * up).astype(jnp.bfloat16)
    d_hidden = contract_columns(upstream_all, weight_down)
    d_gate = (d_hidden * up * sigma * (1.0 + gate * (1.0 - sigma))).astype(jnp.bfloat16)
    d_up = (d_hidden * activated).astype(jnp.bfloat16)
    d_both = jnp.concatenate([d_gate, d_up], 1)
    columns = contract_columns(d_both, weight_gu).astype(jnp.bfloat16)
    columns = scatter_seq(blocks_back(columns))

    grad_down = contract_rows(hidden, upstream_all).astype(jnp.bfloat16)
    grad_down = scatter_plane(grad_down)[:unit].astype(jnp.float32)
    grad_pair = scatter_plane(contract_rows(normed_all, d_both).astype(jnp.bfloat16))
    branch = jnp.dot(hidden, weight_down, preferred_element_type=jnp.float32).astype(jnp.bfloat16)
    branch = scatter_seq(blocks_back(branch), (columns,))
    layer_out = (resid + branch).astype(jnp.bfloat16)
    grad_pair = exchange_seq(grad_pair)
    own_rows = weight_rows // seq_count
    grad_pair = jnp.stack(grad_pair, 0).reshape(seq_count, own_rows, 2, padded)
    order = (seq_rank - jnp.arange(seq_count)) % seq_count
    grad_pair = grad_pair[order]
    grad_pair = grad_pair.reshape(seq_count, own_rows, 2, fsdp_count, unit_pad)[..., :unit]
    grad_pair = grad_pair.transpose(2, 1, 3, 0, 4).astype(jnp.float32)
    grad_pair = grad_pair.reshape(2, own_rows, hidden_width)

    _, pull_two = jax.vjp(norm_piece, resid, gain_two)
    d_resid_norm, grad_gain_two = pull_two(columns)
    d_resid = cotangent.astype(jnp.float32) + d_resid_norm
    d_branch = d_resid.astype(jnp.bfloat16)
    d_attended = contract_columns(d_branch, weight_out).astype(jnp.bfloat16)
    d_queries, d_keys, d_values = attend_back(queries, paired, bias, logsum, d_attended)
    d_paired = jnp.concatenate([d_keys, d_values], 1).astype(jnp.bfloat16)
    d_paired = blocks_back(d_paired)
    d_paired = sum(
        part.astype(jnp.float32)
        for part in [d_paired[0]] + [shift(d_paired[j], -j) for j in range(1, seq_count)]
    )
    d_query_pre = rotate_back(
        d_queries.astype(jnp.float32).reshape(rows_here, HEADS, HEAD_DIM), cosine, sine
    ).astype(jnp.bfloat16)
    d_key_pre = rotate_back(
        d_paired[:, :kv_width].reshape(rows_here, KV_HEADS, HEAD_DIM), cosine, sine
    ).astype(jnp.bfloat16)
    d_value_pre = d_paired[:, kv_width:].astype(jnp.bfloat16)
    d_qkv = jnp.concatenate(
        [
            d_query_pre.reshape(rows_here, width),
            d_key_pre.reshape(rows_here, kv_width),
            d_value_pre,
        ],
        1,
    )
    grad_out = contract_rows(attended, d_branch).astype(jnp.bfloat16)
    grad_qkv = contract_rows(normed_one, d_qkv).astype(jnp.bfloat16)
    grad_bias = jnp.sum(d_qkv.astype(jnp.float32), 0)
    d_normed_one = contract_columns(d_qkv, weight_qkv)
    _, pull_one = jax.vjp(norm_piece, inputs, gain_one)
    d_input_norm, grad_gain_one = pull_one(d_normed_one)
    input_grad = (d_resid + d_input_norm).astype(jnp.bfloat16)

    def summed(value):
        return sum(part.astype(jnp.float32) for part in exchange_seq(scatter_plane(value)))

    grad_out = summed(grad_out)
    grad_qkv = summed(grad_qkv)
    vectors = jnp.concatenate([grad_gain_one, grad_gain_two, grad_bias], 0)
    if fsdp_count == 8:
        for bits in (1, 2, 4):
            vectors = vectors + cross(vectors, bits)
        vectors = vectors + sum(shift(vectors, j) for j in range(1, seq_count))
    else:
        vectors = lax.psum(vectors, ("fsdp", "seq"))
    own = width // (fsdp_count * seq_count)
    first = (fsdp_rank * seq_count + seq_rank) * own

    def own_part(offset):
        return lax.dynamic_slice_in_dim(vectors, offset + first, own, 0)

    biases = 2 * width
    return (
        layer_out,
        input_grad,
        own_part(0),
        grad_qkv[:, :width],
        own_part(biases),
        grad_qkv[:, width : width + kv_width],
        vectors[biases + width : biases + width + kv_width],
        grad_qkv[:, width + kv_width :],
        vectors[biases + width + kv_width :],
        grad_out,
        own_part(width),
        grad_pair[0],
        grad_pair[1],
        grad_down,
    )


def solution(mesh):
    both = P(("fsdp", "seq"), None)
    both_one = P(("fsdp", "seq"))
    placed = (
        both, both, P("fsdp", None), both_one, P("fsdp"), P("fsdp", None), P("fsdp"),
        P("fsdp", None), P("fsdp"), P("fsdp", None), P("fsdp"), P("fsdp", None), P("fsdp"),
        P("fsdp", None), P("fsdp", None), P("fsdp", None),
    )
    return jax.shard_map(
        per_device if mesh.shape["fsdp"] == 8 else plain_device,
        mesh=mesh,
        in_specs=placed,
        out_specs=(
            both, both, both_one, both, both_one, both, P(), both, P(), both, both_one,
            both, both, both,
        ),
        check_vma=False,
    )
```

```python
import jax
import jax.numpy as jnp
import numpy as np
from jax import lax
from jax.experimental import pallas as pl
from jax.experimental.pallas import tpu as pltpu
from jax.sharding import PartitionSpec as P

HEADS = 12
KV_HEADS = 2
HEAD_DIM = 128

MESH = pl.DeviceIdType.MESH

epsilon = 1e-06
rope_base = 1000000.0


def norm_piece(values, gain):
    return values * lax.rsqrt(jnp.mean(values * values, -1, keepdims=True) + epsilon) * gain


def rope_tables(position):
    half = HEAD_DIM // 2
    inverse = rope_base ** (-(jnp.arange(half, dtype=jnp.float32) * 2.0 / HEAD_DIM))
    angle = position.astype(jnp.float32)[:, None] * inverse[None, :]
    cosine = jnp.concatenate([jnp.cos(angle), jnp.cos(angle)], -1)
    sine = jnp.concatenate([jnp.sin(angle), jnp.sin(angle)], -1)
    return (cosine, sine)


def turn_half(values):
    half = values.shape[-1] // 2
    return jnp.concatenate([-values[..., half:], values[..., :half]], -1)


def rotate(values, cosine, sine):
    return values * cosine[:, None, :] + turn_half(values) * sine[:, None, :]


def rotate_back(grads, cosine, sine):
    return grads * cosine[:, None, :] - turn_half(grads * sine[:, None, :])


def segment_of(slots, starts):
    return (slots >= starts[1]).astype(jnp.int32) + (slots >= starts[2]).astype(jnp.int32)


def contract_rows(left, right):
    return lax.dot_general(
        left, right, (((0,), (0,)), ((), ())), preferred_element_type=jnp.float32
    )


def contract_columns(left, right):
    return lax.dot_general(
        left, right, (((1,), (1,)), ((), ())), preferred_element_type=jnp.float32
    )


def after(value, *earlier):
    return lax.optimization_barrier((value, *earlier))[0]


def add_low(*values):
    return sum(value.astype(jnp.float32) for value in values).astype(jnp.bfloat16)


def cross(value, bits):
    count = lax.axis_size("fsdp")
    return lax.ppermute(value, "fsdp", [(i, i ^ bits) for i in range(count)])


def shift(value, step):
    count = lax.axis_size("seq")
    return lax.ppermute(value, "seq", [(i, (i + step) % count) for i in range(count)])


def place(parts, rank):
    rows = parts[0].shape[0]
    whole = jnp.zeros((len(parts) * rows,) + parts[0].shape[1:], parts[0].dtype)
    for k, part in enumerate(parts):
        whole = lax.dynamic_update_slice_in_dim(whole, part, (rank ^ k) * rows, 0)
    return whole


def gather_plane(block, earlier=()):
    if lax.axis_size("fsdp") != 8:
        whole = lax.all_gather(block, "fsdp", axis=0, tiled=True)
        return whole, ()
    rank = lax.axis_index("fsdp")
    half = block.shape[0] // 2
    if earlier:
        block = after(block, *earlier)
    from_x = cross(block, 2)
    from_y = cross(block, 4)
    diagonal = (cross(from_x[:half], 4), cross(from_y[half:], 2))
    from_core = cross(block, 1)
    both = cross(jnp.concatenate([from_x, from_y], 0), 1)
    diagonal = jnp.concatenate(diagonal, 0)
    rows = block.shape[0]
    parts = [
        block, from_core, from_x, both[:rows], from_y, both[rows:], diagonal, cross(diagonal, 1),
    ]
    return place(parts, rank), (from_x, from_y)


def scatter_plane(whole, earlier=()):
    count = lax.axis_size("fsdp")
    if count != 8:
        return lax.psum_scatter(whole, "fsdp", scatter_dimension=0, tiled=True)
    rank = lax.axis_index("fsdp")
    rows = whole.shape[0] // count
    if earlier:
        whole = after(whole, *earlier)

    def part(k):
        return lax.dynamic_slice_in_dim(whole, (rank ^ k) * rows, rows, 0)

    arrived = cross(jnp.concatenate([part(1), part(3), part(5), part(7)], 0), 1)
    return scatter_chips(
        [add_low(part(2 * i), arrived[i * rows : (i + 1) * rows]) for i in range(4)]
    )


def scatter_chips(parts):
    own, to_x, to_y, to_both = parts
    rows = own.shape[0]
    half = own.shape[1] // 2
    got_x = cross(jnp.concatenate([to_x[:, :half], to_both[:, :half]], 0), 2)
    got_y = cross(jnp.concatenate([to_y[:, half:], to_both[:, half:]], 0), 4)
    last_y = cross(add_low(to_y[:, :half], got_x[rows:]), 4)
    last_x = cross(add_low(to_x[:, half:], got_y[rows:]), 2)
    return jnp.concatenate(
        [
            add_low(own[:, :half], got_x[:rows], last_y),
            add_low(own[:, half:], got_y[:rows], last_x),
        ],
        1,
    )


def chain_step(up, down, step):
    count = lax.axis_size("seq")
    up = lax.ppermute(up, "seq", [(i, i + 1) for i in range(step - 1, count - 1)])
    down = lax.ppermute(down, "seq", [(i, i - 1) for i in range(1, count - step + 1)])
    return up, down


def gather_seq(block, pause=None):
    count = lax.axis_size("seq")
    rank = lax.axis_index("seq")
    up, down = block, block
    ups, downs = [], []
    for step in range(1, count):
        if pause is not None and step == count - 1:
            up, down = pause(up), pause(down)
        up, down = chain_step(up, down, step)
        ups.append(up)
        downs.append(down)
    rest = [jnp.where(rank >= j, ups[j - 1], downs[count - j - 1]) for j in range(1, count)]
    return [block] + rest


def scatter_seq(parts, earlier=()):
    count = lax.axis_size("seq")
    up, down = None, None
    for step in range(1, count):
        send_up = parts[step] if up is None else add_low(parts[step], up)
        send_down = parts[count - step] if down is None else add_low(parts[count - step], down)
        if up is None and earlier:
            send_up = after(send_up, *earlier)
            send_down = after(send_down, *earlier)
        up = lax.ppermute(send_up, "seq", [(i, i + 1) for i in range(min(step, count - 1))])
        down = lax.ppermute(
            send_down, "seq", [(i, i - 1) for i in range(count - 1, max(count - 1 - step, 0), -1)]
        )
    return parts[0].astype(jnp.float32) + up.astype(jnp.float32) + down.astype(jnp.float32)


def exchange_seq(whole):
    count = lax.axis_size("seq")
    rank = lax.axis_index("seq")
    rows = whole.shape[0] // count

    def part(step):
        return lax.dynamic_slice_in_dim(whole, ((rank + step) % count) * rows, rows, 0)

    return [part(0)] + [shift(part(step), step) for step in range(1, count)]


def attend_back_kernel(query, key, value, bias, logsum, grad, d_query, d_key, d_value):
    scale = HEAD_DIM ** (-0.5)
    repeat = HEADS // KV_HEADS
    raw = lax.dot_general(
        key[...], query[...], (((1,), (1,)), ((), ())), preferred_element_type=jnp.float32
    )
    probs = jnp.exp(raw * scale + bias[...] - logsum[0:1])
    d_probs = lax.dot_general(
        value[...], grad[...], (((1,), (1,)), ((), ())), preferred_element_type=jnp.float32
    )
    delta = jnp.sum(probs * d_probs, 0, keepdims=True)
    d_score = (probs * (d_probs - delta)).astype(jnp.bfloat16)
    turned = lax.dot_general(
        key[...], d_score, (((0,), (0,)), ((), ())), preferred_element_type=jnp.float32
    )
    d_query[...] = (turned * scale).T.astype(jnp.bfloat16)
    key_part = jnp.dot(d_score, query[...], preferred_element_type=jnp.float32) * scale
    value_part = jnp.dot(
        probs.astype(jnp.bfloat16), grad[...], preferred_element_type=jnp.float32
    )

    @pl.when(pl.program_id(0) % repeat == 0)
    def _():
        d_key[...] = key_part
        d_value[...] = value_part

    @pl.when(pl.program_id(0) % repeat != 0)
    def _():
        d_key[...] += key_part
        d_value[...] += value_part


def attend_back(queries, paired, bias, logsum, grads):
    rows, width = queries.shape
    group = paired.shape[0]
    repeat = HEADS // KV_HEADS
    return pl.pallas_call(
        attend_back_kernel,
        grid=(HEADS,),
        in_specs=[
            pl.BlockSpec((rows, HEAD_DIM), lambda h: (0, h)),
            pl.BlockSpec((group, HEAD_DIM), lambda h: (0, h // repeat)),
            pl.BlockSpec((group, HEAD_DIM), lambda h: (0, KV_HEADS + h // repeat)),
            pl.BlockSpec((group, rows), lambda h: (0, 0)),
            pl.BlockSpec((8, rows), lambda h: (h, 0)),
            pl.BlockSpec((rows, HEAD_DIM), lambda h: (0, h)),
        ],
        out_specs=[
            pl.BlockSpec((rows, HEAD_DIM), lambda h: (0, h)),
            pl.BlockSpec((group, HEAD_DIM), lambda h: (0, h // repeat)),
            pl.BlockSpec((group, HEAD_DIM), lambda h: (0, h // repeat)),
        ],
        out_shape=[
            jax.ShapeDtypeStruct((rows, width), jnp.bfloat16),
            jax.ShapeDtypeStruct((group, KV_HEADS * HEAD_DIM), jnp.float32),
            jax.ShapeDtypeStruct((group, KV_HEADS * HEAD_DIM), jnp.float32),
        ],
        compiler_params=pltpu.CompilerParams(vmem_limit_bytes=48 * 2**20),
        cost_estimate=pl.CostEstimate(
            flops=10 * HEADS * rows * group * HEAD_DIM * 3, bytes_accessed=8 * 2**20, transcendentals=HEADS * rows * group
        ),
        name="attend_back",
    )(queries, paired, paired, bias, logsum, grads)


def plain_device(
    tokens, cotangent, lengths, balance, norm1_gain, w_query, b_query, w_key, b_key,
    w_value, b_value, w_out, norm2_gain, w_gate, w_up, w_down,
):
    seq_count = lax.axis_size("seq")
    fsdp_count = lax.axis_size("fsdp")
    seq_rank = lax.axis_index("seq")
    rows_here, width = tokens.shape
    group = seq_count * rows_here
    kv_width = KV_HEADS * HEAD_DIM
    qkv_width = width + 2 * kv_width
    hidden_width = w_gate.shape[1]
    unit = hidden_width // (fsdp_count * seq_count)
    own_units = hidden_width // seq_count
    weight_rows = w_gate.shape[0]
    score_scale = HEAD_DIM ** (-0.5)
    repeat = HEADS // KV_HEADS

    slot = balance % group
    slots_all = lax.all_gather(slot, "seq", axis=0, tiled=True)
    seq_lengths = lengths[0]
    starts = jnp.cumsum(seq_lengths) - seq_lengths
    segment = segment_of(slot, starts)
    segments_all = segment_of(slots_all, starts)
    first_row = jnp.where(segment == 0, starts[0], jnp.where(segment == 1, starts[1], starts[2]))
    cosine, sine = rope_tables(slot - first_row)
    allowed = (segment[:, None] == segments_all[None, :]) & (slots_all[None, :] <= slot[:, None])

    small = jnp.concatenate([norm1_gain, norm2_gain, b_query, b_key, b_value], 0)[None]
    small = lax.all_gather(small, "fsdp", axis=0, tiled=True)
    piece = norm1_gain.shape[0]
    bias_piece = b_key.shape[0]
    gain_one = small[:, :piece].reshape(-1).astype(jnp.float32)
    gain_two = small[:, piece : 2 * piece].reshape(-1).astype(jnp.float32)
    bias_qkv = jnp.concatenate(
        [
            small[:, 2 * piece : 3 * piece].reshape(-1),
            small[:, 3 * piece : 3 * piece + bias_piece].reshape(-1),
            small[:, 3 * piece + bias_piece :].reshape(-1),
        ],
        0,
    ).astype(jnp.float32)
    weight_qkv = lax.all_gather(
        jnp.concatenate([w_query, w_key, w_value], 1), "fsdp", axis=0, tiled=True
    )
    weight_out = lax.all_gather(w_out, "fsdp", axis=0, tiled=True)
    upstream_all = lax.all_gather(cotangent, "seq", axis=0, tiled=True)

    def own_columns(weight):
        cut = weight.reshape(weight_rows, fsdp_count, seq_count, unit)
        return lax.dynamic_index_in_dim(cut, seq_rank, 2, False).reshape(weight_rows, own_units)

    weight_gu = lax.all_gather(
        jnp.concatenate([own_columns(w_gate), own_columns(w_up)], 1), "fsdp", axis=0, tiled=True
    )
    weight_down = lax.all_gather(
        lax.dynamic_slice_in_dim(w_down, seq_rank * unit, unit, 0), "fsdp", axis=0, tiled=True
    )

    inputs = tokens.astype(jnp.float32)
    normed_one = norm_piece(inputs, gain_one).astype(jnp.bfloat16)
    projected = jnp.dot(normed_one, weight_qkv, preferred_element_type=jnp.float32) + bias_qkv
    query_pre = projected[:, :width].reshape(rows_here, HEADS, HEAD_DIM)
    key_pre = projected[:, width : width + kv_width].reshape(rows_here, KV_HEADS, HEAD_DIM)
    value_pre = projected[:, width + kv_width :]
    queries = rotate(query_pre, cosine, sine).astype(jnp.bfloat16)
    keys = rotate(key_pre, cosine, sine).astype(jnp.bfloat16).reshape(rows_here, kv_width)
    values = value_pre.astype(jnp.bfloat16)
    paired = lax.all_gather(jnp.concatenate([keys, values], 1), "seq", axis=0, tiled=True)
    keys_all = paired[:, :kv_width].reshape(group, KV_HEADS, HEAD_DIM)
    values_all = paired[:, kv_width:].reshape(group, KV_HEADS, HEAD_DIM)
    grouped = queries.reshape(rows_here, KV_HEADS, repeat, HEAD_DIM)
    raw = (
        jnp.einsum("qgrd,kgd->grqk", grouped, keys_all, preferred_element_type=jnp.float32)
        * score_scale
    )
    scores = jnp.where(allowed, raw, -jnp.inf)
    expo = jnp.exp(scores - jnp.max(scores, -1, keepdims=True))
    probs = expo / jnp.sum(expo, -1, keepdims=True)
    probs_low = probs.astype(jnp.bfloat16)
    attended = jnp.einsum(
        "grqk,kgd->qgrd", probs_low, values_all, preferred_element_type=jnp.float32
    )
    attended = attended.astype(jnp.bfloat16).reshape(rows_here, width)
    resid = inputs + jnp.dot(attended, weight_out, preferred_element_type=jnp.float32)
    normed_two = norm_piece(resid, gain_two).astype(jnp.bfloat16)

    normed_all = lax.all_gather(normed_two, "seq", axis=0, tiled=True)
    both = jnp.dot(normed_all, weight_gu, preferred_element_type=jnp.float32)
    gate = both[:, :own_units]
    up = both[:, own_units:]
    sigma = jax.nn.sigmoid(gate)
    activated = gate * sigma
    hidden = (activated * up).astype(jnp.bfloat16)
    d_hidden = contract_columns(upstream_all, weight_down)
    d_gate = (d_hidden * up * sigma * (1.0 + gate * (1.0 - sigma))).astype(jnp.bfloat16)
    d_up = (d_hidden * activated).astype(jnp.bfloat16)
    d_both = jnp.concatenate([d_gate, d_up], 1)
    columns = lax.psum_scatter(
        contract_columns(d_both, weight_gu).astype(jnp.bfloat16),
        "seq", scatter_dimension=0, tiled=True,
    ).astype(jnp.float32)
    branch = lax.psum_scatter(
        jnp.dot(hidden, weight_down, preferred_element_type=jnp.float32).astype(jnp.bfloat16),
        "seq", scatter_dimension=0, tiled=True,
    ).astype(jnp.float32)
    layer_out = (resid + branch).astype(jnp.bfloat16)
    grad_down = lax.psum_scatter(
        contract_rows(hidden, upstream_all).astype(jnp.bfloat16),
        "fsdp", scatter_dimension=0, tiled=True,
    ).astype(jnp.float32)
    grad_pair = lax.psum_scatter(
        contract_rows(normed_all, d_both).astype(jnp.bfloat16),
        "fsdp", scatter_dimension=0, tiled=True,
    )
    grad_pair = lax.all_to_all(grad_pair, "seq", split_axis=0, concat_axis=0, tiled=True)
    grad_pair = grad_pair.reshape(seq_count, weight_rows // seq_count, 2, fsdp_count, unit)
    grad_pair = grad_pair.transpose(2, 1, 3, 0, 4).astype(jnp.float32)
    grad_pair = grad_pair.reshape(2, weight_rows // seq_count, hidden_width)

    _, pull_two = jax.vjp(norm_piece, resid, gain_two)
    d_resid_norm, grad_gain_two = pull_two(columns)
    d_resid = cotangent.astype(jnp.float32) + d_resid_norm
    d_branch = d_resid.astype(jnp.bfloat16)
    grad_out = contract_rows(attended, d_branch).astype(jnp.bfloat16)
    d_attended = contract_columns(d_branch, weight_out).astype(jnp.bfloat16)
    d_attended = d_attended.reshape(rows_here, KV_HEADS, repeat, HEAD_DIM)
    d_probs = jnp.einsum(
        "qgrd,kgd->grqk", d_attended, values_all, preferred_element_type=jnp.float32
    )
    delta = jnp.sum(probs * d_probs, -1, keepdims=True)
    d_score = (probs * (d_probs - delta)).astype(jnp.bfloat16)
    d_queries = (
        jnp.einsum("grqk,kgd->qgrd", d_score, keys_all, preferred_element_type=jnp.float32)
        * score_scale
    )
    d_keys = (
        jnp.einsum("grqk,qgrd->kgd", d_score, grouped, preferred_element_type=jnp.float32)
        * score_scale
    )
    d_values = jnp.einsum(
        "grqk,qgrd->kgd", probs_low, d_attended, preferred_element_type=jnp.float32
    )
    d_paired = jnp.concatenate([d_keys.reshape(group, kv_width), d_values.reshape(group, kv_width)], 1)
    d_paired = lax.psum_scatter(
        d_paired.astype(jnp.bfloat16), "seq", scatter_dimension=0, tiled=True
    ).astype(jnp.float32)
    d_query_pre = rotate_back(
        d_queries.reshape(rows_here, HEADS, HEAD_DIM), cosine, sine
    ).astype(jnp.bfloat16)
    d_key_pre = rotate_back(
        d_paired[:, :kv_width].reshape(rows_here, KV_HEADS, HEAD_DIM), cosine, sine
    ).astype(jnp.bfloat16)
    d_value_pre = d_paired[:, kv_width:].astype(jnp.bfloat16)
    d_qkv = jnp.concatenate(
        [
            d_query_pre.reshape(rows_here, width),
            d_key_pre.reshape(rows_here, kv_width),
            d_value_pre,
        ],
        1,
    )
    grad_qkv = contract_rows(normed_one, d_qkv).astype(jnp.bfloat16)
    grad_bias = jnp.sum(d_qkv.astype(jnp.float32), 0)
    d_normed_one = contract_columns(d_qkv, weight_qkv)
    _, pull_one = jax.vjp(norm_piece, inputs, gain_one)
    d_input_norm, grad_gain_one = pull_one(d_normed_one)
    input_grad = (d_resid + d_input_norm).astype(jnp.bfloat16)

    def summed(value):
        value = lax.psum_scatter(value, "fsdp", scatter_dimension=0, tiled=True)
        return lax.psum_scatter(value, "seq", scatter_dimension=0, tiled=True).astype(jnp.float32)

    grad_out = summed(grad_out)
    grad_qkv = summed(grad_qkv)
    vectors = lax.psum(
        jnp.concatenate([grad_gain_one, grad_gain_two, grad_bias], 0), ("fsdp", "seq")
    )
    own = width // (fsdp_count * seq_count)
    first = (lax.axis_index("fsdp") * seq_count + seq_rank) * own

    def own_part(offset):
        return lax.dynamic_slice_in_dim(vectors, offset + first, own, 0)

    biases = 2 * width
    return (
        layer_out,
        input_grad,
        own_part(0),
        grad_qkv[:, :width],
        own_part(biases),
        grad_qkv[:, width : width + kv_width],
        vectors[biases + width : biases + width + kv_width],
        grad_qkv[:, width + kv_width :],
        vectors[biases + width + kv_width :],
        grad_out,
        own_part(width),
        grad_pair[0],
        grad_pair[1],
        grad_down,
    )


def front_kernel(
    tokens, cotangent, small, slot_keys, slot_row, first_row, cosine, sine,
    w_query, w_key, w_value, w_out, w_gate, w_up, w_down,
    gu_all, down_all, upstream_all, normed_all, qkv_out, out_out,
    queries, paired_out, slots_out, logsum, attended, resid, normed_one, gain_one, gain_two,
    qkv, out_w, gate_v, up_v, gu_own, kv, small_all, slots_all, bias, normed_own,
    local, ssem, rsem, zsend, zrecv,
):
    f = lax.axis_index("fsdp")
    s = lax.axis_index("seq")
    rows, width = tokens.shape
    n_f, n_s = 8, slots_all.shape[0]
    block = w_query.shape[0]
    unit = w_down.shape[0]
    kv_width = KV_HEADS * HEAD_DIM
    qkv_width = width + 2 * kv_width
    scale = HEAD_DIM ** (-0.5)
    repeat = HEADS // KV_HEADS
    plane = [f ^ k for k in range(n_f)]

    entry = pltpu.get_barrier_semaphore()
    for k in range(1, n_f):
        pl.semaphore_signal(entry, inc=1, device_id={"fsdp": plane[k]}, device_id_type=MESH)
    for j in range(1, n_s):
        pl.semaphore_signal(
            entry, inc=1, device_id={"seq": lax.rem(s + j, n_s)}, device_id_type=MESH
        )

    def here(source, target, index):
        return pltpu.make_async_copy(source, target, local.at[index])

    def there(source, target, index, **device):
        return pltpu.make_async_remote_copy(
            src_ref=source, dst_ref=target, send_sem=ssem.at[index], recv_sem=rsem.at[index],
            device_id=device, device_id_type=MESH,
        )

    def own_rows(ref, owner, size, start=0, count=None):
        first = pl.multiple_of(owner * size + start, 16)
        return ref.at[pl.ds(first, size if count is None else count)]

    class Gather:
        def __init__(self, source, target, size, index):
            half = size // 2
            x, y, c = plane[2], plane[4], plane[1]
            self.own = here(source, own_rows(target, f, size), index // 8) if source is not None else None
            if source is None:
                source = own_rows(target, f, size)
            mine = own_rows(target, f, size)
            self.first = [
                there(source, mine, index, fsdp=x),
                there(source, mine, index + 1, fsdp=y),
                there(source, mine, index + 2, fsdp=c),
            ]
            from_x, from_y = own_rows(target, x, size), own_rows(target, y, size)
            part_x = own_rows(target, x, size, 0, half)
            part_y = own_rows(target, y, size, half, half)
            self.second = [
                there(part_x, part_x, index + 3, fsdp=y),
                there(part_y, part_y, index + 4, fsdp=x),
                there(from_x, from_x, index + 5, fsdp=c),
                there(from_y, from_y, index + 6, fsdp=c),
            ]
            diagonal = own_rows(target, plane[6], size)
            self.third = there(diagonal, diagonal, index + 7, fsdp=c)

        def start(self):
            if self.own is not None:
                self.own.start()
            for copy in self.first:
                copy.start()

        def forward(self):
            self.first[0].wait_recv()
            self.second[0].start()
            self.second[2].start()
            self.first[1].wait_recv()
            self.second[1].start()
            self.second[3].start()

        def last(self):
            self.second[0].wait_recv()
            self.second[1].wait_recv()
            self.third.start()

        def finish(self):
            if self.own is not None:
                self.own.wait()
            self.first[2].wait_recv()
            self.second[2].wait_recv()
            self.second[3].wait_recv()
            self.third.wait_recv()

        def sent(self):
            for copy in self.first + self.second + [self.third]:
                copy.wait_send()

    class Chain:
        def __init__(self, target, index):
            self.steps = []
            for step in range(1, n_s):
                up = own_rows(target, s - (step - 1), rows)
                down = own_rows(target, s + (step - 1), rows)
                i = index + 2 * (step - 1)
                self.steps.append((
                    pltpu.make_async_remote_copy(
                        src_ref=up, dst_ref=up, send_sem=zsend.at[i], recv_sem=zrecv.at[i],
                        device_id={"seq": s + 1}, device_id_type=MESH,
                    ),
                    pltpu.make_async_remote_copy(
                        src_ref=down, dst_ref=down, send_sem=zsend.at[i + 1], recv_sem=zrecv.at[i + 1],
                        device_id={"seq": s - 1}, device_id_type=MESH,
                    ),
                    (s >= step - 1) & (s < n_s - 1),
                    (s >= 1) & (s <= n_s - step),
                    s >= step,
                    s <= n_s - 1 - step,
                ))

        def send(self, step):
            up, down, can_up, can_down, _, _ = self.steps[step - 1]
            pl.when(can_up)(up.start)
            pl.when(can_down)(down.start)

        def receive(self, step):
            up, down, _, _, from_below, from_above = self.steps[step - 1]
            pl.when(from_below)(up.wait_recv)
            pl.when(from_above)(down.wait_recv)

        def sent(self):
            for up, down, can_up, can_down, _, _ in self.steps:
                pl.when(can_up)(up.wait_send)
                pl.when(can_down)(down.wait_send)

    pieces = [
        here(w_query, qkv.at[pl.ds(pl.multiple_of(f * block, 16), block), pl.ds(0, width)], 5),
        here(w_key, qkv.at[pl.ds(pl.multiple_of(f * block, 16), block), pl.ds(width, kv_width)], 6),
        here(w_value, qkv.at[pl.ds(pl.multiple_of(f * block, 16), block), pl.ds(width + kv_width, kv_width)], 7),
        here(cotangent, own_rows(upstream_all, s, rows), 8),
    ]
    load_gate = here(w_gate, gate_v, 9)
    load_up = here(w_up, up_v, 10)
    for copy in pieces:
        copy.start()
    load_gate.start()
    load_up.start()
    small_all[f] = small[...]
    slots_all[s] = slot_keys[...]

    gather_qkv = Gather(None, qkv, block, 0)
    gather_out = Gather(w_out, out_w, block, 8)
    gather_gu = Gather(gu_own, gu_all, block, 16)
    gather_down = Gather(w_down, down_all, unit, 24)
    chain_up = Chain(upstream_all, 0)
    chain_normed = Chain(normed_all, 6)
    send_small = [
        there(small, small_all.at[f], 32 + k, fsdp=plane[k]) for k in range(1, n_f)
    ]
    send_slots = [
        there(slot_keys, slots_all.at[s], 40 + j, seq=lax.rem(s + j, n_s)) for j in range(1, n_s)
    ]
    send_kv = [
        there(kv.at[s], kv.at[s], 44 + j, seq=lax.rem(s + j, n_s)) for j in range(1, n_s)
    ]
    for copy in pieces[:3]:
        copy.wait()
    pl.semaphore_wait(entry, n_f - 1 + n_s - 1)
    gather_qkv.start()
    for copy in send_small + send_slots:
        copy.start()
    pieces[3].wait()
    chain_up.send(1)

    load_gate.wait()
    load_up.wait()
    pick_units(gate_v, up_v, gu_own, w_gate.shape[1] // n_f, w_gate.shape[1] // (n_f * n_s), unit)

    for copy in send_small + send_slots:
        copy.wait_recv()
    third = 2 * block
    for i in range(n_f // 2):
        columns = slice(i * third, (i + 1) * third)
        gain_one[:, columns] = (
            small_all[2 * i, 0:1, :third].astype(jnp.float32)
            + small_all[2 * i + 1, 0:1, :third].astype(jnp.float32)
        )
        gain_two[:, columns] = (
            small_all[2 * i, 0:1, third : 2 * third].astype(jnp.float32)
            + small_all[2 * i + 1, 0:1, third : 2 * third].astype(jnp.float32)
        )
    bias_query = [
        small_all[2 * i, 0:1, 2 * third : 3 * third].astype(jnp.float32)
        + small_all[2 * i + 1, 0:1, 2 * third : 3 * third].astype(jnp.float32)
        for i in range(n_f // 2)
    ]
    bias_query = jnp.concatenate(bias_query, 1)
    bias_pair = sum(small_all[i, 0:1, 3 * third :].astype(jnp.float32) for i in range(n_f))

    inputs = tokens[...].astype(jnp.float32)
    root = lax.rsqrt(jnp.mean(inputs * inputs, -1, keepdims=True) + epsilon)
    normed_one[...] = (inputs * root * gain_one[...]).astype(jnp.bfloat16)
    for j in range(n_s):
        keys_slot = slots_all[j]
        keys_slot = jnp.concatenate([keys_slot] * (rows // 128), 1)
        ok = (keys_slot <= slot_row[0:1]) & (keys_slot >= first_row[0:1])
        bias[j * rows : (j + 1) * rows] = jnp.where(ok, 0.0, -1e30)

    gather_qkv.forward()
    gather_out.start()
    chain_up.receive(1)
    chain_up.send(2)
    gather_qkv.last()
    gather_qkv.finish()
    save_qkv = here(qkv, qkv_out, 11)
    save_qkv.start()

    def turned(value):
        return value * cosine[...] + pltpu.roll(value, HEAD_DIM // 2, 1) * sine[...]

    normed = normed_one[...]
    pair = jnp.dot(normed, qkv[:, width : width + kv_width], preferred_element_type=jnp.float32)
    pair = pair + bias_pair[:, :kv_width]
    for g in range(KV_HEADS):
        columns = slice(g * HEAD_DIM, (g + 1) * HEAD_DIM)
        kv[s, :, columns] = turned(pair[:, columns]).astype(jnp.bfloat16)
    pair = jnp.dot(normed, qkv[:, width + kv_width :], preferred_element_type=jnp.float32)
    kv[s, :, kv_width:] = (pair + bias_pair[:, kv_width:]).astype(jnp.bfloat16)
    for copy in send_kv:
        copy.start()
    for g in range(HEADS // 2):
        columns = slice(g * 2 * HEAD_DIM, (g + 1) * 2 * HEAD_DIM)
        pair = jnp.dot(normed, qkv[:, columns], preferred_element_type=jnp.float32)
        pair = pair + bias_query[:, columns]
        for h in range(2):
            part = turned(pair[:, h * HEAD_DIM : (h + 1) * HEAD_DIM]).astype(jnp.bfloat16)
            queries[:, (2 * g + h) * HEAD_DIM : (2 * g + h + 1) * HEAD_DIM] = part

    gather_out.forward()
    gather_gu.start()
    chain_up.receive(2)
    gather_out.last()
    for copy in send_kv:
        copy.wait_recv()
    chain_up.send(3)
    save_kv = here(kv, paired_out, 12)
    save_kv.start()
    slots_out[...] = slots_all[...]

    for g in range(KV_HEADS):
        keys = kv[:, :, g * HEAD_DIM : (g + 1) * HEAD_DIM].reshape(n_s * rows, HEAD_DIM)
        values = kv[:, :, kv_width + g * HEAD_DIM : kv_width + (g + 1) * HEAD_DIM]
        values = values.reshape(n_s * rows, HEAD_DIM)

        def head(i, carry, g=g, keys=keys, values=values):
            h = g * repeat + i
            columns = pl.ds(pl.multiple_of(h * HEAD_DIM, HEAD_DIM), HEAD_DIM)
            raw = lax.dot_general(
                keys, queries[:, columns], (((1,), (1,)), ((), ())),
                preferred_element_type=jnp.float32,
            )
            scores = raw * scale + bias[...]
            top = jnp.max(scores, 0, keepdims=True)
            expo = jnp.exp(scores - top)
            total = jnp.sum(expo, 0, keepdims=True)
            probs = (expo * (1.0 / total)).astype(jnp.bfloat16)
            mixed = lax.dot_general(
                values, probs, (((0,), (0,)), ((), ())), preferred_element_type=jnp.float32
            )
            attended[:, columns] = mixed.T.astype(jnp.bfloat16)
            logsum[pl.ds(pl.multiple_of(h * 8, 8), 8)] = jnp.broadcast_to(
                top + jnp.log(total), (8, rows)
            )
            return carry

        lax.fori_loop(0, repeat, head, 0)

    gather_out.finish()
    save_out = here(out_w, out_out, 13)
    save_out.start()
    mixed = attended[...]
    for g in range(width // 256):
        columns = slice(g * 256, (g + 1) * 256)
        part = jnp.dot(mixed, out_w[:, columns], preferred_element_type=jnp.float32)
        resid[:, columns] = tokens[:, columns].astype(jnp.float32) + part
    value = resid[...]
    root = lax.rsqrt(jnp.mean(value * value, -1, keepdims=True) + epsilon)
    normed_own[...] = (value * root * gain_two[...]).astype(jnp.bfloat16)
    place_normed = here(normed_own, own_rows(normed_all, s, rows), 14)
    place_normed.start()
    place_normed.wait()
    chain_normed.send(1)

    gather_gu.forward()
    gather_down.start()
    chain_normed.receive(1)
    chain_normed.send(2)
    gather_gu.last()
    chain_normed.receive(2)
    chain_normed.send(3)
    chain_up.receive(3)
    gather_down.forward()
    gather_gu.finish()
    gather_down.last()
    chain_normed.receive(3)
    gather_down.finish()
    save_qkv.wait()
    save_kv.wait()
    save_out.wait()
    for part in (gather_qkv, gather_out, gather_gu, gather_down, chain_up, chain_normed):
        part.sent()
    for copy in send_small + send_slots + send_kv:
        copy.wait_send()


def pick_units(gate, up, out, stride, unit, padded):
    rank = lax.axis_index("seq")
    pieces = gate.shape[1] // stride
    half = out.shape[1] // 2
    window, tile = 512, 128
    rows = lax.broadcasted_iota(jnp.int32, (window, tile), 0)
    columns = lax.broadcasted_iota(jnp.int32, (window, tile), 1)
    for first in range(0, 2 * half, tile):
        source = gate if first < half else up
        local = first % half
        total = jnp.zeros((out.shape[0], tile), jnp.float32)
        for f in range(pieces):
            low = max(local, f * padded)
            high = min(local + tile, f * padded + unit)
            if low >= high:
                continue
            begin = f * stride + rank * unit
            base = jnp.minimum(begin // 128, (source.shape[1] - window) // 128) * 128
            base = pl.multiple_of(base, 128)
            wanted = columns + (local - f * padded + begin - base)
            inside = (columns >= low - local) & (columns < high - local)
            chosen = jnp.where((rows == wanted) & inside, 1.0, 0.0).astype(jnp.bfloat16)
            total += jnp.dot(
                source[:, pl.ds(base, window)], chosen, preferred_element_type=jnp.float32
            )
        out[:, first : first + tile] = total.astype(jnp.bfloat16)


def front(tokens, cotangent, small, slot, first_row, cosine, sine, weights, w_down_own):
    rows, width = tokens.shape
    n_s = lax.axis_size("seq")
    w_query, w_key, w_value, w_out, w_gate, w_up = weights
    block = w_query.shape[0]
    unit = w_down_own.shape[0]
    kv_width = KV_HEADS * HEAD_DIM
    qkv_width = width + 2 * kv_width
    units = 8 * unit
    group = n_s * rows
    low, full = jnp.bfloat16, jnp.float32
    slot_f = slot.astype(full)
    slot_keys = jnp.broadcast_to(slot_f[:, None], (rows, 128))
    slot_row = jnp.broadcast_to(slot_f[None], (8, rows))
    first_f = jnp.broadcast_to(first_row.astype(full)[None], (8, rows))
    half = HEAD_DIM // 2
    sine = jnp.concatenate([-sine[:, :half], sine[:, half:]], 1)
    vmem = pl.BlockSpec(memory_space=pltpu.VMEM)
    hbm = pl.BlockSpec(memory_space=pl.ANY)
    shape = jax.ShapeDtypeStruct
    return pl.pallas_call(
        front_kernel,
        in_specs=[vmem, hbm] + [vmem] * 6 + [hbm] * 7,
        out_specs=[hbm] * 6 + [vmem, hbm] + [vmem] * 7,
        out_shape=[
            shape((8 * block, 2 * units), low),
            shape((units, width), low),
            shape((group, width), low),
            shape((group, width), low),
            shape((width, qkv_width), low),
            shape((width, width), low),
            shape((rows, width), low),
            shape((n_s, rows, 2 * kv_width), low),
            shape((n_s, rows, 128), full),
            shape((8 * HEADS, rows), full),
            shape((rows, width), low),
            shape((rows, width), full),
            shape((rows, width), low),
            shape((1, width), full),
            shape((1, width), full),
        ],
        scratch_shapes=[
            pltpu.VMEM((width, qkv_width), low),
            pltpu.VMEM((width, width), low),
            pltpu.VMEM(w_gate.shape, low),
            pltpu.VMEM(w_up.shape, low),
            pltpu.VMEM((block, 2 * units), low),
            pltpu.VMEM((n_s, rows, 2 * kv_width), low),
            pltpu.VMEM((8,) + small.shape, low),
            pltpu.VMEM((n_s, rows, 128), full),
            pltpu.VMEM((group, rows), full),
            pltpu.VMEM((rows, width), low),
            pltpu.SemaphoreType.DMA((16,)),
            pltpu.SemaphoreType.DMA((48,)),
            pltpu.SemaphoreType.DMA((48,)),
            pltpu.SemaphoreType.DMA((12,)),
            pltpu.SemaphoreType.DMA((12,)),
        ],
        compiler_params=pltpu.CompilerParams(
            collective_id=0, has_side_effects=True, vmem_limit_bytes=56 * 2**20
        ),
        name="front",
    )(
        tokens, cotangent, small, slot_keys, slot_row, first_f, cosine, sine,
        w_query, w_key, w_value, w_out, w_gate, w_up, w_down_own,
    )


ORDER = (1, 3, 2, 0)


def ffn_kernel(
    normed_all, upstream_all, w_gu, w_down,
    columns, grad_down, gu_sum, branch, down_arrived, gu_arrived,
    normed, upstream, gu, down, hidden, d_both, partial, z_one, z_two, z_three,
    down_x, down_y, down_last, branch_piece,
    load, ssem, rsem,
):
    f = lax.axis_index("fsdp")
    s = lax.axis_index("seq")
    n_s = len(ORDER)
    group, width = normed.shape
    rows = group // n_s
    half_rows = group // 2
    units = down.shape[0]
    tile = 256
    tiles = units // tile
    block = gu.shape[0] // 8
    unit = units // 8
    half = width // 2
    plane = [f ^ k for k in range(8)]
    full = jnp.float32

    entry = pltpu.get_barrier_semaphore()
    for k in (1, 2, 4):
        pl.semaphore_signal(entry, inc=1, device_id={"fsdp": plane[k]}, device_id_type=MESH)
    for j in (1, n_s - 1):
        pl.semaphore_signal(
            entry, inc=1, device_id={"seq": lax.rem(s + j, n_s)}, device_id_type=MESH
        )

    def here(source, target, index):
        return pltpu.make_async_copy(source, target, load.at[index])

    def there(source, target, index, **device):
        return pltpu.make_async_remote_copy(
            src_ref=source, dst_ref=target, send_sem=ssem.at[index], recv_sem=rsem.at[index],
            device_id=device, device_id_type=MESH,
        )

    def part(ref, owner, size):
        return ref.at[pl.ds(pl.multiple_of(owner * size, 16), size)]

    first_loads = []
    for p, j in enumerate(ORDER):
        owner = lax.rem(s + n_s - j, n_s)
        first_loads.append(here(part(normed_all, owner, rows), part(normed, p, rows), p))
        first_loads.append(here(part(upstream_all, owner, rows), part(upstream, p, rows), 4 + p))

    def tile_loads(t):
        gate_columns = pl.ds(pl.multiple_of(t * tile, tile), tile)
        up_columns = pl.ds(pl.multiple_of(units + t * tile, tile), tile)
        return [
            here(w_gu.at[:, gate_columns], gu.at[:, gate_columns], 8 + 3 * t),
            here(w_gu.at[:, up_columns], gu.at[:, up_columns], 9 + 3 * t),
            here(w_down.at[gate_columns], down.at[gate_columns], 10 + 3 * t),
        ]

    for copy in first_loads:
        copy.start()
    for t in range(tiles):
        for copy in tile_loads(t):
            copy.start()
    for copy in first_loads:
        copy.wait()

    def forward(part_rows, wait):
        def body(t, carry):
            if wait:
                for copy in tile_loads(t):
                    copy.wait()
            gate_columns = pl.ds(pl.multiple_of(t * tile, tile), tile)
            up_columns = pl.ds(pl.multiple_of(units + t * tile, tile), tile)
            mine = normed[part_rows]
            gate = jnp.dot(mine, gu[:, gate_columns], preferred_element_type=full)
            up = jnp.dot(mine, gu[:, up_columns], preferred_element_type=full)
            d_hidden = lax.dot_general(
                upstream[part_rows], down[gate_columns], (((1,), (1,)), ((), ())),
                preferred_element_type=full,
            )
            sigma = jax.nn.sigmoid(gate)
            activated = gate * sigma
            hidden[part_rows, gate_columns] = (activated * up).astype(jnp.bfloat16)
            d_both[part_rows, gate_columns] = (
                d_hidden * up * sigma * (1.0 + gate * (1.0 - sigma))
            ).astype(jnp.bfloat16)
            d_both[part_rows, up_columns] = (d_hidden * activated).astype(jnp.bfloat16)
            return carry

        lax.fori_loop(0, tiles, body, 0)

    def backward(part_rows):
        def body(n, carry):
            out_columns = pl.ds(pl.multiple_of(n * tile, tile), tile)
            value = lax.dot_general(
                d_both[part_rows], gu[out_columns], (((1,), (1,)), ((), ())),
                preferred_element_type=full,
            )
            partial[part_rows, out_columns] = value.astype(jnp.bfloat16)
            return carry

        lax.fori_loop(0, width // tile, body, 0)

    def held(j):
        return partial.at[ORDER.index(j) * rows : (ORDER.index(j) + 1) * rows]

    up_one = there(held(1), z_one, 0, seq=s + 1)
    down_one = there(held(3), z_one, 1, seq=s - 1)
    up_two = there(held(2), z_two.at[0], 2, seq=s + 1)
    down_two = there(held(2), z_two.at[1], 3, seq=s - 1)
    up_three = there(held(3), z_three.at[0], 4, seq=s + 1)
    down_three = there(held(1), z_three.at[1], 5, seq=s - 1)

    def add_to(j, arrived):
        ref = held(j)
        ref[...] = (ref[...].astype(full) + arrived[...].astype(full)).astype(jnp.bfloat16)

    def chain_one():
        pl.when(s == 0)(up_one.start)
        pl.when(s == 3)(down_one.start)

    def chain_two():
        @pl.when(s == 1)
        def _():
            up_one.wait_recv()
            add_to(2, z_one)

        @pl.when(s == 2)
        def _():
            down_one.wait_recv()
            add_to(2, z_one)

        pl.when(s <= 1)(up_two.start)
        pl.when(s >= 2)(down_two.start)

    def chain_three():
        @pl.when((s == 1) | (s == 2))
        def _():
            up_two.wait_recv()
            add_to(3, z_two.at[0])
            down_two.wait_recv()
            add_to(1, z_two.at[1])

        pl.when(s <= 2)(up_three.start)
        pl.when(s >= 1)(down_three.start)

    def chain_last():
        columns[...] = held(0)[...].astype(full)

        @pl.when(s >= 1)
        def _():
            up_three.wait_recv()
            columns[...] += z_three[0].astype(full)

        @pl.when(s <= 2)
        def _():
            down_three.wait_recv()
            columns[...] += z_three[1].astype(full)

    def chain_sent():
        pl.when(s == 0)(up_one.wait_send)
        pl.when(s == 3)(down_one.wait_send)
        pl.when(s <= 1)(up_two.wait_send)
        pl.when(s >= 2)(down_two.wait_send)
        pl.when(s <= 2)(up_three.wait_send)
        pl.when(s >= 1)(down_three.wait_send)

    early, late = slice(0, half_rows), slice(half_rows, group)
    forward(early, True)
    backward(early)
    pl.semaphore_wait(entry, 5)
    chain_one()
    forward(late, False)
    backward(late)
    chain_two()

    def branch_store(n):
        out_columns = pl.ds(pl.multiple_of(n * tile, tile), tile)
        return here(branch_piece.at[lax.rem(n, 2)], branch.at[:, out_columns], 8 + n)

    def branch_body(n, carry):
        out_columns = pl.ds(pl.multiple_of(n * tile, tile), tile)
        value = jnp.dot(hidden[...], down[:, out_columns], preferred_element_type=full)

        @pl.when(n >= 2)
        def _():
            branch_store(n - 2).wait()

        branch_piece[lax.rem(n, 2)] = value.astype(jnp.bfloat16)
        branch_store(n).start()
        return carry

    lax.fori_loop(0, width // tile, branch_body, 0)
    for n in (width // tile - 2, width // tile - 1):
        branch_store(n).wait()

    def down_body(t, carry):
        unit_rows = pl.ds(pl.multiple_of(t * tile, tile), tile)
        value = lax.dot_general(
            hidden[:, unit_rows], upstream[...], (((0,), (0,)), ((), ())),
            preferred_element_type=full,
        )
        down[unit_rows] = value.astype(jnp.bfloat16)
        return carry

    lax.fori_loop(0, tiles, down_body, 0)
    down_core = [
        there(part(down, plane[2 * i + 1], unit), down_arrived.at[i], 6 + i, fsdp=plane[1])
        for i in range(4)
    ]
    for copy in down_core:
        copy.start()

    def gu_body(m, carry):
        in_columns = pl.ds(pl.multiple_of(m * tile, tile), tile)
        turned = normed[:, in_columns].T
        for first in range(0, 2 * units, units // 3):
            value = jnp.dot(turned, d_both[:, first : first + units // 3], preferred_element_type=full)
            gu[in_columns, first : first + units // 3] = value.astype(jnp.bfloat16)
        return carry

    lax.fori_loop(0, width // tile // 2, gu_body, 0)

    def add_arrived(ref, size, arrived, pieces, copies, index):
        for i in range(4):
            copies[i].wait_recv()
            fetch = [
                here(arrived.at[i, :, columns], piece, index + k)
                for k, (columns, piece) in enumerate(pieces)
            ]
            for copy in fetch:
                copy.start()
            target = part(ref, plane[2 * i], size)
            for copy, (columns, piece) in zip(fetch, pieces):
                copy.wait()
                target[:, columns] = (
                    target[:, columns].astype(full) + piece[...].astype(full)
                ).astype(jnp.bfloat16)

    add_arrived(down, unit, down_arrived, [(pl.ds(0, width), hidden.at[:unit, :width])], down_core, 14)
    to_x, to_y, to_both = [part(down, plane[k], unit) for k in (2, 4, 6)]
    low_half, high_half = pl.ds(0, half), pl.ds(half, half)
    down_first = [
        there(to_x.at[:, low_half], down_x.at[0], 10, fsdp=plane[2]),
        there(to_both.at[:, low_half], down_x.at[1], 11, fsdp=plane[2]),
        there(to_y.at[:, high_half], down_y.at[0], 12, fsdp=plane[4]),
        there(to_both.at[:, high_half], down_y.at[1], 13, fsdp=plane[4]),
    ]
    for copy in down_first:
        copy.start()
    chain_three()
    lax.fori_loop(width // tile // 2, width // tile, gu_body, 0)
    gu_core = [
        there(part(gu, plane[2 * i + 1], block), gu_arrived.at[i], 16 + i, fsdp=plane[1])
        for i in range(4)
    ]
    for copy in gu_core:
        copy.start()
    chain_last()
    down_second = [
        there(to_y.at[:, low_half], down_last.at[0], 14, fsdp=plane[4]),
        there(to_x.at[:, high_half], down_last.at[1], 15, fsdp=plane[2]),
    ]
    down_first[1].wait_recv()
    to_y[:, :half] = (to_y[:, :half].astype(full) + down_x[1].astype(full)).astype(jnp.bfloat16)
    down_second[0].start()
    down_first[3].wait_recv()
    to_x[:, half:] = (to_x[:, half:].astype(full) + down_y[1].astype(full)).astype(jnp.bfloat16)
    down_second[1].start()
    gu_pieces = [
        (pl.ds(0, units), hidden.at[:block]),
        (pl.ds(units, units), hidden.at[block : 2 * block]),
    ]
    add_arrived(gu, block, gu_arrived, gu_pieces, gu_core, 20)
    store = [here(part(gu, plane[2 * i], block), gu_sum.at[i], 16 + i) for i in range(4)]
    for copy in store:
        copy.start()
    down_first[0].wait_recv()
    down_first[2].wait_recv()
    own = part(down, f, unit)
    down_second[0].wait_recv()
    grad_down[:, :half] = (
        own[:, :half].astype(full) + down_x[0].astype(full) + down_last[0].astype(full)
    )
    down_second[1].wait_recv()
    grad_down[:, half:] = (
        own[:, half:].astype(full) + down_y[0].astype(full) + down_last[1].astype(full)
    )
    for copy in store:
        copy.wait()
    chain_sent()
    for copy in down_core + down_first + down_second + gu_core:
        copy.wait_send()


def ffn(normed_all, upstream_all, w_gu, w_down):
    group, width = normed_all.shape
    units = w_down.shape[0]
    rows = group // len(ORDER)
    unit, block, half = units // 8, width // 8, width // 2
    low, full = jnp.bfloat16, jnp.float32
    vmem = pl.BlockSpec(memory_space=pltpu.VMEM)
    hbm = pl.BlockSpec(memory_space=pl.ANY)
    shape = jax.ShapeDtypeStruct
    return pl.pallas_call(
        ffn_kernel,
        in_specs=[hbm] * 4,
        out_specs=[vmem] * 2 + [hbm] * 4,
        out_shape=[
            shape((rows, width), full),
            shape((unit, width), full),
            shape((4, block, 2 * units), low),
            shape((group, width), low),
            shape((4, unit, width), low),
            shape((4, block, 2 * units), low),
        ],
        scratch_shapes=[
            pltpu.VMEM((group, width), low),
            pltpu.VMEM((group, width), low),
            pltpu.VMEM((width, 2 * units), low),
            pltpu.VMEM((units, width), low),
            pltpu.VMEM((group, units), low),
            pltpu.VMEM((group, 2 * units), low),
            pltpu.VMEM((group, width), low),
            pltpu.VMEM((rows, width), low),
            pltpu.VMEM((2, rows, width), low),
            pltpu.VMEM((2, rows, width), low),
            pltpu.VMEM((2, unit, half), low),
            pltpu.VMEM((2, unit, half), low),
            pltpu.VMEM((2, unit, half), low),
            pltpu.VMEM((2, group, 256), low),
            pltpu.SemaphoreType.DMA((36,)),
            pltpu.SemaphoreType.DMA((20,)),
            pltpu.SemaphoreType.DMA((20,)),
        ],
        compiler_params=pltpu.CompilerParams(
            collective_id=1, has_side_effects=True, vmem_limit_bytes=63 * 2**20
        ),
        name="ffn",
    )(normed_all, upstream_all, w_gu, w_down)[:4]


def per_device(
    tokens, cotangent, lengths, balance, norm1_gain, w_query, b_query, w_key, b_key,
    w_value, b_value, w_out, norm2_gain, w_gate, w_up, w_down,
):
    seq_count = lax.axis_size("seq")
    fsdp_count = lax.axis_size("fsdp")
    seq_rank = lax.axis_index("seq")
    fsdp_rank = lax.axis_index("fsdp")
    rows_here, width = tokens.shape
    group = seq_count * rows_here
    kv_width = KV_HEADS * HEAD_DIM
    qkv_width = width + 2 * kv_width
    hidden_width = w_gate.shape[1]
    unit = hidden_width // (fsdp_count * seq_count)
    own_units = hidden_width // seq_count
    padded = fsdp_count * (-(-unit // 16) * 16)
    weight_rows = w_gate.shape[0]

    unit_pad = -(-unit // 16) * 16
    pair_bias = jnp.concatenate([jnp.tile(b_key, fsdp_count), jnp.tile(b_value, fsdp_count)])
    small = jnp.concatenate([norm1_gain] * 2 + [norm2_gain] * 2 + [b_query] * 2 + [pair_bias])
    place_of = np.concatenate(
        [np.repeat([0, 1], weight_rows)] * 3 + [8 + np.repeat(np.arange(8), b_key.shape[0])] * 2
    )
    place_of = jnp.asarray(place_of, jnp.int32)
    mine = (place_of == fsdp_rank % 2) | (place_of == 8 + fsdp_rank)
    small = jnp.broadcast_to(jnp.where(mine, small, 0)[None], (16, small.shape[0]))

    slot = balance % group
    seq_lengths = lengths[0]
    starts = jnp.cumsum(seq_lengths) - seq_lengths
    segment = segment_of(slot, starts)
    first_row = jnp.where(segment == 0, starts[0], jnp.where(segment == 1, starts[1], starts[2]))
    cosine, sine = rope_tables(slot - first_row)
    down_own = lax.dynamic_slice_in_dim(w_down, seq_rank * unit, unit, 0)
    down_own = jnp.pad(down_own, ((0, unit_pad - unit), (0, 0)))
    (
        weight_gu, weight_down, upstream_all, normed_all, weight_qkv, weight_out,
        queries, paired, slots_all, logsum, attended, resid, normed_one, gain_one, gain_two,
    ) = front(
        tokens, cotangent, small, slot, first_row, cosine, sine,
        (w_query, w_key, w_value, w_out, w_gate, w_up), down_own,
    )
    gain_one, gain_two = gain_one[0], gain_two[0]
    paired = paired.reshape(group, 2 * kv_width)
    slots_all = slots_all[:, :, 0].reshape(group)
    slot = slot.astype(jnp.float32)
    allowed = (slots_all[:, None] <= slot[None, :]) & (
        slots_all[:, None] >= first_row.astype(jnp.float32)[None, :]
    )
    bias = jnp.where(allowed, 0.0, -1e30).astype(jnp.float32)
    inputs = tokens.astype(jnp.float32)

    def blocks_back(value):
        return [
            lax.dynamic_slice_in_dim(value, ((seq_rank - j) % seq_count) * rows_here, rows_here, 0)
            for j in range(seq_count)
        ]

    columns, grad_down, gu_sum, branch = ffn(normed_all, upstream_all, weight_gu, weight_down)
    grad_down = grad_down[:unit]
    grad_pair = scatter_chips(gu_sum)
    branch = [branch[ORDER.index(j) * rows_here : (ORDER.index(j) + 1) * rows_here] for j in range(seq_count)]
    branch = scatter_seq(branch)
    layer_out = (resid + branch).astype(jnp.bfloat16)
    grad_pair = exchange_seq(grad_pair)
    own_rows = weight_rows // seq_count
    grad_pair = jnp.stack(grad_pair, 0).reshape(seq_count, own_rows, 2, padded)
    order = (seq_rank - jnp.arange(seq_count)) % seq_count
    grad_pair = grad_pair[order]
    grad_pair = grad_pair.reshape(seq_count, own_rows, 2, fsdp_count, unit_pad)[..., :unit]
    grad_pair = grad_pair.transpose(2, 1, 3, 0, 4).astype(jnp.float32)
    grad_pair = grad_pair.reshape(2, own_rows, hidden_width)

    _, pull_two = jax.vjp(norm_piece, resid, gain_two)
    d_resid_norm, grad_gain_two = pull_two(columns)
    d_resid = cotangent.astype(jnp.float32) + d_resid_norm
    d_branch = d_resid.astype(jnp.bfloat16)
    d_attended = contract_columns(d_branch, weight_out).astype(jnp.bfloat16)
    d_queries, d_keys, d_values = attend_back(queries, paired, bias, logsum, d_attended)
    d_paired = jnp.concatenate([d_keys, d_values], 1).astype(jnp.bfloat16)
    d_paired = blocks_back(d_paired)
    d_paired = sum(
        part.astype(jnp.float32)
        for part in [d_paired[0]] + [shift(d_paired[j], -j) for j in range(1, seq_count)]
    )
    d_query_pre = rotate_back(
        d_queries.astype(jnp.float32).reshape(rows_here, HEADS, HEAD_DIM), cosine, sine
    ).astype(jnp.bfloat16)
    d_key_pre = rotate_back(
        d_paired[:, :kv_width].reshape(rows_here, KV_HEADS, HEAD_DIM), cosine, sine
    ).astype(jnp.bfloat16)
    d_value_pre = d_paired[:, kv_width:].astype(jnp.bfloat16)
    d_qkv = jnp.concatenate(
        [
            d_query_pre.reshape(rows_here, width),
            d_key_pre.reshape(rows_here, kv_width),
            d_value_pre,
        ],
        1,
    )
    grad_out = contract_rows(attended, d_branch).astype(jnp.bfloat16)
    grad_qkv = contract_rows(normed_one, d_qkv).astype(jnp.bfloat16)
    grad_bias = jnp.sum(d_qkv.astype(jnp.float32), 0)
    d_normed_one = contract_columns(d_qkv, weight_qkv)
    _, pull_one = jax.vjp(norm_piece, inputs, gain_one)
    d_input_norm, grad_gain_one = pull_one(d_normed_one)
    input_grad = (d_resid + d_input_norm).astype(jnp.bfloat16)

    def summed(value):
        return sum(part.astype(jnp.float32) for part in exchange_seq(scatter_plane(value)))

    grad_out = summed(grad_out)
    grad_qkv = summed(grad_qkv)
    vectors = jnp.concatenate([grad_gain_one, grad_gain_two, grad_bias], 0)
    if fsdp_count == 8:
        for bits in (1, 2, 4):
            vectors = vectors + cross(vectors, bits)
        vectors = vectors + sum(shift(vectors, j) for j in range(1, seq_count))
    else:
        vectors = lax.psum(vectors, ("fsdp", "seq"))
    own = width // (fsdp_count * seq_count)
    first = (fsdp_rank * seq_count + seq_rank) * own

    def own_part(offset):
        return lax.dynamic_slice_in_dim(vectors, offset + first, own, 0)

    biases = 2 * width
    return (
        layer_out,
        input_grad,
        own_part(0),
        grad_qkv[:, :width],
        own_part(biases),
        grad_qkv[:, width : width + kv_width],
        vectors[biases + width : biases + width + kv_width],
        grad_qkv[:, width + kv_width :],
        vectors[biases + width + kv_width :],
        grad_out,
        own_part(width),
        grad_pair[0],
        grad_pair[1],
        grad_down,
    )


def solution(mesh):
    both = P(("fsdp", "seq"), None)
    both_one = P(("fsdp", "seq"))
    placed = (
        both, both, P("fsdp", None), both_one, P("fsdp"), P("fsdp", None), P("fsdp"),
        P("fsdp", None), P("fsdp"), P("fsdp", None), P("fsdp"), P("fsdp", None), P("fsdp"),
        P("fsdp", None), P("fsdp", None), P("fsdp", None),
    )
    return jax.shard_map(
        per_device if mesh.shape["fsdp"] == 8 else plain_device,
        mesh=mesh,
        in_specs=placed,
        out_specs=(
            both, both, both_one, both, both_one, both, P(), both, P(), both, both_one,
            both, both, both,
        ),
        check_vma=False,
    )
```

```python
import jax
import jax.numpy as jnp
import numpy as np
from jax import lax
from jax.experimental import pallas as pl
from jax.experimental.pallas import tpu as pltpu
from jax.sharding import PartitionSpec as P

HEADS = 12
KV_HEADS = 2
HEAD_DIM = 128

MESH = pl.DeviceIdType.MESH

epsilon = 1e-06
rope_base = 1000000.0


def norm_piece(values, gain):
    return values * lax.rsqrt(jnp.mean(values * values, -1, keepdims=True) + epsilon) * gain


def rope_tables(position):
    half = HEAD_DIM // 2
    inverse = rope_base ** (-(jnp.arange(half, dtype=jnp.float32) * 2.0 / HEAD_DIM))
    angle = position.astype(jnp.float32)[:, None] * inverse[None, :]
    cosine = jnp.concatenate([jnp.cos(angle), jnp.cos(angle)], -1)
    sine = jnp.concatenate([jnp.sin(angle), jnp.sin(angle)], -1)
    return (cosine, sine)


def turn_half(values):
    half = values.shape[-1] // 2
    return jnp.concatenate([-values[..., half:], values[..., :half]], -1)


def rotate(values, cosine, sine):
    return values * cosine[:, None, :] + turn_half(values) * sine[:, None, :]


def rotate_back(grads, cosine, sine):
    return grads * cosine[:, None, :] - turn_half(grads * sine[:, None, :])


def segment_of(slots, starts):
    return (slots >= starts[1]).astype(jnp.int32) + (slots >= starts[2]).astype(jnp.int32)


def contract_rows(left, right):
    return lax.dot_general(
        left, right, (((0,), (0,)), ((), ())), preferred_element_type=jnp.float32
    )


def contract_columns(left, right):
    return lax.dot_general(
        left, right, (((1,), (1,)), ((), ())), preferred_element_type=jnp.float32
    )


def plain_device(
    tokens, cotangent, lengths, balance, norm1_gain, w_query, b_query, w_key, b_key,
    w_value, b_value, w_out, norm2_gain, w_gate, w_up, w_down,
):
    seq_count = lax.axis_size("seq")
    fsdp_count = lax.axis_size("fsdp")
    seq_rank = lax.axis_index("seq")
    rows_here, width = tokens.shape
    group = seq_count * rows_here
    kv_width = KV_HEADS * HEAD_DIM
    qkv_width = width + 2 * kv_width
    hidden_width = w_gate.shape[1]
    unit = hidden_width // (fsdp_count * seq_count)
    own_units = hidden_width // seq_count
    weight_rows = w_gate.shape[0]
    score_scale = HEAD_DIM ** (-0.5)
    repeat = HEADS // KV_HEADS

    slot = balance % group
    slots_all = lax.all_gather(slot, "seq", axis=0, tiled=True)
    seq_lengths = lengths[0]
    starts = jnp.cumsum(seq_lengths) - seq_lengths
    segment = segment_of(slot, starts)
    segments_all = segment_of(slots_all, starts)
    first_row = jnp.where(segment == 0, starts[0], jnp.where(segment == 1, starts[1], starts[2]))
    cosine, sine = rope_tables(slot - first_row)
    allowed = (segment[:, None] == segments_all[None, :]) & (slots_all[None, :] <= slot[:, None])

    small = jnp.concatenate([norm1_gain, norm2_gain, b_query, b_key, b_value], 0)[None]
    small = lax.all_gather(small, "fsdp", axis=0, tiled=True)
    piece = norm1_gain.shape[0]
    bias_piece = b_key.shape[0]
    gain_one = small[:, :piece].reshape(-1).astype(jnp.float32)
    gain_two = small[:, piece : 2 * piece].reshape(-1).astype(jnp.float32)
    bias_qkv = jnp.concatenate(
        [
            small[:, 2 * piece : 3 * piece].reshape(-1),
            small[:, 3 * piece : 3 * piece + bias_piece].reshape(-1),
            small[:, 3 * piece + bias_piece :].reshape(-1),
        ],
        0,
    ).astype(jnp.float32)
    weight_qkv = lax.all_gather(
        jnp.concatenate([w_query, w_key, w_value], 1), "fsdp", axis=0, tiled=True
    )
    weight_out = lax.all_gather(w_out, "fsdp", axis=0, tiled=True)
    upstream_all = lax.all_gather(cotangent, "seq", axis=0, tiled=True)

    def own_columns(weight):
        cut = weight.reshape(weight_rows, fsdp_count, seq_count, unit)
        return lax.dynamic_index_in_dim(cut, seq_rank, 2, False).reshape(weight_rows, own_units)

    weight_gu = lax.all_gather(
        jnp.concatenate([own_columns(w_gate), own_columns(w_up)], 1), "fsdp", axis=0, tiled=True
    )
    weight_down = lax.all_gather(
        lax.dynamic_slice_in_dim(w_down, seq_rank * unit, unit, 0), "fsdp", axis=0, tiled=True
    )

    inputs = tokens.astype(jnp.float32)
    normed_one = norm_piece(inputs, gain_one).astype(jnp.bfloat16)
    projected = jnp.dot(normed_one, weight_qkv, preferred_element_type=jnp.float32) + bias_qkv
    query_pre = projected[:, :width].reshape(rows_here, HEADS, HEAD_DIM)
    key_pre = projected[:, width : width + kv_width].reshape(rows_here, KV_HEADS, HEAD_DIM)
    value_pre = projected[:, width + kv_width :]
    queries = rotate(query_pre, cosine, sine).astype(jnp.bfloat16)
    keys = rotate(key_pre, cosine, sine).astype(jnp.bfloat16).reshape(rows_here, kv_width)
    values = value_pre.astype(jnp.bfloat16)
    paired = lax.all_gather(jnp.concatenate([keys, values], 1), "seq", axis=0, tiled=True)
    keys_all = paired[:, :kv_width].reshape(group, KV_HEADS, HEAD_DIM)
    values_all = paired[:, kv_width:].reshape(group, KV_HEADS, HEAD_DIM)
    grouped = queries.reshape(rows_here, KV_HEADS, repeat, HEAD_DIM)
    raw = (
        jnp.einsum("qgrd,kgd->grqk", grouped, keys_all, preferred_element_type=jnp.float32)
        * score_scale
    )
    scores = jnp.where(allowed, raw, -jnp.inf)
    expo = jnp.exp(scores - jnp.max(scores, -1, keepdims=True))
    probs = expo / jnp.sum(expo, -1, keepdims=True)
    probs_low = probs.astype(jnp.bfloat16)
    attended = jnp.einsum(
        "grqk,kgd->qgrd", probs_low, values_all, preferred_element_type=jnp.float32
    )
    attended = attended.astype(jnp.bfloat16).reshape(rows_here, width)
    resid = inputs + jnp.dot(attended, weight_out, preferred_element_type=jnp.float32)
    normed_two = norm_piece(resid, gain_two).astype(jnp.bfloat16)

    normed_all = lax.all_gather(normed_two, "seq", axis=0, tiled=True)
    both = jnp.dot(normed_all, weight_gu, preferred_element_type=jnp.float32)
    gate = both[:, :own_units]
    up = both[:, own_units:]
    sigma = jax.nn.sigmoid(gate)
    activated = gate * sigma
    hidden = (activated * up).astype(jnp.bfloat16)
    d_hidden = contract_columns(upstream_all, weight_down)
    d_gate = (d_hidden * up * sigma * (1.0 + gate * (1.0 - sigma))).astype(jnp.bfloat16)
    d_up = (d_hidden * activated).astype(jnp.bfloat16)
    d_both = jnp.concatenate([d_gate, d_up], 1)
    columns = lax.psum_scatter(
        contract_columns(d_both, weight_gu).astype(jnp.bfloat16),
        "seq", scatter_dimension=0, tiled=True,
    ).astype(jnp.float32)
    branch = lax.psum_scatter(
        jnp.dot(hidden, weight_down, preferred_element_type=jnp.float32).astype(jnp.bfloat16),
        "seq", scatter_dimension=0, tiled=True,
    ).astype(jnp.float32)
    layer_out = (resid + branch).astype(jnp.bfloat16)
    grad_down = lax.psum_scatter(
        contract_rows(hidden, upstream_all).astype(jnp.bfloat16),
        "fsdp", scatter_dimension=0, tiled=True,
    ).astype(jnp.float32)
    grad_pair = lax.psum_scatter(
        contract_rows(normed_all, d_both).astype(jnp.bfloat16),
        "fsdp", scatter_dimension=0, tiled=True,
    )
    grad_pair = lax.all_to_all(grad_pair, "seq", split_axis=0, concat_axis=0, tiled=True)
    grad_pair = grad_pair.reshape(seq_count, weight_rows // seq_count, 2, fsdp_count, unit)
    grad_pair = grad_pair.transpose(2, 1, 3, 0, 4).astype(jnp.float32)
    grad_pair = grad_pair.reshape(2, weight_rows // seq_count, hidden_width)

    _, pull_two = jax.vjp(norm_piece, resid, gain_two)
    d_resid_norm, grad_gain_two = pull_two(columns)
    d_resid = cotangent.astype(jnp.float32) + d_resid_norm
    d_branch = d_resid.astype(jnp.bfloat16)
    grad_out = contract_rows(attended, d_branch).astype(jnp.bfloat16)
    d_attended = contract_columns(d_branch, weight_out).astype(jnp.bfloat16)
    d_attended = d_attended.reshape(rows_here, KV_HEADS, repeat, HEAD_DIM)
    d_probs = jnp.einsum(
        "qgrd,kgd->grqk", d_attended, values_all, preferred_element_type=jnp.float32
    )
    delta = jnp.sum(probs * d_probs, -1, keepdims=True)
    d_score = (probs * (d_probs - delta)).astype(jnp.bfloat16)
    d_queries = (
        jnp.einsum("grqk,kgd->qgrd", d_score, keys_all, preferred_element_type=jnp.float32)
        * score_scale
    )
    d_keys = (
        jnp.einsum("grqk,qgrd->kgd", d_score, grouped, preferred_element_type=jnp.float32)
        * score_scale
    )
    d_values = jnp.einsum(
        "grqk,qgrd->kgd", probs_low, d_attended, preferred_element_type=jnp.float32
    )
    d_paired = jnp.concatenate([d_keys.reshape(group, kv_width), d_values.reshape(group, kv_width)], 1)
    d_paired = lax.psum_scatter(
        d_paired.astype(jnp.bfloat16), "seq", scatter_dimension=0, tiled=True
    ).astype(jnp.float32)
    d_query_pre = rotate_back(
        d_queries.reshape(rows_here, HEADS, HEAD_DIM), cosine, sine
    ).astype(jnp.bfloat16)
    d_key_pre = rotate_back(
        d_paired[:, :kv_width].reshape(rows_here, KV_HEADS, HEAD_DIM), cosine, sine
    ).astype(jnp.bfloat16)
    d_value_pre = d_paired[:, kv_width:].astype(jnp.bfloat16)
    d_qkv = jnp.concatenate(
        [
            d_query_pre.reshape(rows_here, width),
            d_key_pre.reshape(rows_here, kv_width),
            d_value_pre,
        ],
        1,
    )
    grad_qkv = contract_rows(normed_one, d_qkv).astype(jnp.bfloat16)
    grad_bias = jnp.sum(d_qkv.astype(jnp.float32), 0)
    d_normed_one = contract_columns(d_qkv, weight_qkv)
    _, pull_one = jax.vjp(norm_piece, inputs, gain_one)
    d_input_norm, grad_gain_one = pull_one(d_normed_one)
    input_grad = (d_resid + d_input_norm).astype(jnp.bfloat16)

    def summed(value):
        value = lax.psum_scatter(value, "fsdp", scatter_dimension=0, tiled=True)
        return lax.psum_scatter(value, "seq", scatter_dimension=0, tiled=True).astype(jnp.float32)

    grad_out = summed(grad_out)
    grad_qkv = summed(grad_qkv)
    vectors = lax.psum(
        jnp.concatenate([grad_gain_one, grad_gain_two, grad_bias], 0), ("fsdp", "seq")
    )
    own = width // (fsdp_count * seq_count)
    first = (lax.axis_index("fsdp") * seq_count + seq_rank) * own

    def own_part(offset):
        return lax.dynamic_slice_in_dim(vectors, offset + first, own, 0)

    biases = 2 * width
    return (
        layer_out,
        input_grad,
        own_part(0),
        grad_qkv[:, :width],
        own_part(biases),
        grad_qkv[:, width : width + kv_width],
        vectors[biases + width : biases + width + kv_width],
        grad_qkv[:, width + kv_width :],
        vectors[biases + width + kv_width :],
        grad_out,
        own_part(width),
        grad_pair[0],
        grad_pair[1],
        grad_down,
    )


ORDER = (1, 3, 2, 0)


class SumChain:
    def __init__(self, partial, rows, z_one, z_two, z_three, there, index):
        self.rank = lax.axis_index("seq")
        s = self.rank

        def held(j):
            return partial.at[ORDER.index(j) * rows : (ORDER.index(j) + 1) * rows]

        self.held, self.arrived = held, (z_one, z_two, z_three)
        self.up = [
            there(held(1), z_one, index, seq=s + 1),
            there(held(2), z_two.at[0], index + 2, seq=s + 1),
            there(held(3), z_three.at[0], index + 4, seq=s + 1),
        ]
        self.down = [
            there(held(3), z_one, index + 1, seq=s - 1),
            there(held(2), z_two.at[1], index + 3, seq=s - 1),
            there(held(1), z_three.at[1], index + 5, seq=s - 1),
        ]

    def add(self, j, arrived):
        ref = self.held(j)
        total = ref[...].astype(jnp.float32) + arrived[...].astype(jnp.float32)
        ref[...] = total.astype(jnp.bfloat16)

    def one(self):
        pl.when(self.rank == 0)(self.up[0].start)
        pl.when(self.rank == 3)(self.down[0].start)

    def two(self):
        @pl.when(self.rank == 1)
        def _():
            self.up[0].wait_recv()
            self.add(2, self.arrived[0])

        @pl.when(self.rank == 2)
        def _():
            self.down[0].wait_recv()
            self.add(2, self.arrived[0])

        pl.when(self.rank <= 1)(self.up[1].start)
        pl.when(self.rank >= 2)(self.down[1].start)

    def three(self):
        @pl.when((self.rank == 1) | (self.rank == 2))
        def _():
            self.up[1].wait_recv()
            self.add(3, self.arrived[1].at[0])
            self.down[1].wait_recv()
            self.add(1, self.arrived[1].at[1])

        pl.when(self.rank <= 2)(self.up[2].start)
        pl.when(self.rank >= 1)(self.down[2].start)

    def last(self, out):
        out[...] = self.held(0)[...].astype(jnp.float32)

        @pl.when(self.rank >= 1)
        def _():
            self.up[2].wait_recv()
            out[...] += self.arrived[2][0].astype(jnp.float32)

        @pl.when(self.rank <= 2)
        def _():
            self.down[2].wait_recv()
            out[...] += self.arrived[2][1].astype(jnp.float32)

    def sent(self):
        pl.when(self.rank == 0)(self.up[0].wait_send)
        pl.when(self.rank == 3)(self.down[0].wait_send)
        pl.when(self.rank <= 1)(self.up[1].wait_send)
        pl.when(self.rank >= 2)(self.down[1].wait_send)
        pl.when(self.rank <= 2)(self.up[2].wait_send)
        pl.when(self.rank >= 1)(self.down[2].wait_send)


class SumPlane:
    def __init__(self, buffer, block, plane, arrived, by_x, by_y, ended, there, index):
        half = buffer.shape[1] // 2
        low, high = pl.ds(0, half), pl.ds(half, half)

        def part(k):
            return buffer.at[pl.ds(pl.multiple_of(plane[k] * block, 16), block)]

        self.parts = own, to_x, to_y, to_both = [part(k) for k in (0, 2, 4, 6)]
        self.arrived, self.by_x, self.by_y, self.ended, self.half = arrived, by_x, by_y, ended, half
        self.core = [
            there(part(2 * i + 1), arrived.at[i], index + i, fsdp=plane[1]) for i in range(4)
        ]
        self.first = [
            there(to_both.at[:, low], by_x.at[1], index + 5, fsdp=plane[2]),
            there(to_both.at[:, high], by_y.at[1], index + 7, fsdp=plane[4]),
            there(to_x.at[:, low], by_x.at[0], index + 4, fsdp=plane[2]),
            there(to_y.at[:, high], by_y.at[0], index + 6, fsdp=plane[4]),
        ]
        self.second = [
            there(to_y.at[:, low], ended.at[0], index + 8, fsdp=plane[4]),
            there(to_x.at[:, high], ended.at[1], index + 9, fsdp=plane[2]),
        ]

    def start_core(self):
        for copy in self.core:
            copy.start()

    def start_first(self):
        for i in (3, 1, 2, 0):
            self.core[i].wait_recv()
            part = self.parts[i]
            total = part[...].astype(jnp.float32) + self.arrived[i].astype(jnp.float32)
            part[...] = total.astype(jnp.bfloat16)
        for copy in self.first:
            copy.start()

    def start_second(self):
        half = self.half
        _, to_x, to_y, _ = self.parts
        self.first[0].wait_recv()
        total = to_y[:, :half].astype(jnp.float32) + self.by_x[1].astype(jnp.float32)
        to_y[:, :half] = total.astype(jnp.bfloat16)
        self.second[0].start()
        self.first[1].wait_recv()
        total = to_x[:, half:].astype(jnp.float32) + self.by_y[1].astype(jnp.float32)
        to_x[:, half:] = total.astype(jnp.bfloat16)
        self.second[1].start()

    def finish(self):
        half = self.half
        own = self.parts[0]
        self.first[2].wait_recv()
        self.second[0].wait_recv()
        total = own[:, :half].astype(jnp.float32) + self.by_x[0].astype(jnp.float32)
        own[:, :half] = (total + self.ended[0].astype(jnp.float32)).astype(jnp.bfloat16)
        self.first[3].wait_recv()
        self.second[1].wait_recv()
        total = own[:, half:].astype(jnp.float32) + self.by_y[0].astype(jnp.float32)
        own[:, half:] = (total + self.ended[1].astype(jnp.float32)).astype(jnp.bfloat16)

    def sent(self):
        for copy in self.core + self.first + self.second:
            copy.wait_send()


def front_kernel(
    tokens, cotangent, small, slot_keys, slot_row, first_row, cosine, sine,
    w_query, w_key, w_value, w_out, w_gate, w_up, w_down,
    gu_all, down_all, upstream_all, normed_all, qkv_out, out_out,
    queries, paired_out, slots_out, logsum, attended, resid, normed_one, gain_one, gain_two,
    qkv, out_w, gate_v, up_v, gu_own, kv, small_all, slots_all, bias, normed_own,
    local, ssem, rsem, zsend, zrecv,
):
    f = lax.axis_index("fsdp")
    s = lax.axis_index("seq")
    rows, width = tokens.shape
    n_f, n_s = 8, slots_all.shape[0]
    block = w_query.shape[0]
    unit = w_down.shape[0]
    kv_width = KV_HEADS * HEAD_DIM
    qkv_width = width + 2 * kv_width
    scale = HEAD_DIM ** (-0.5)
    repeat = HEADS // KV_HEADS
    plane = [f ^ k for k in range(n_f)]

    entry = pltpu.get_barrier_semaphore()
    for k in range(1, n_f):
        pl.semaphore_signal(entry, inc=1, device_id={"fsdp": plane[k]}, device_id_type=MESH)
    for j in range(1, n_s):
        pl.semaphore_signal(
            entry, inc=1, device_id={"seq": lax.rem(s + j, n_s)}, device_id_type=MESH
        )

    def here(source, target, index):
        return pltpu.make_async_copy(source, target, local.at[index])

    def there(source, target, index, **device):
        return pltpu.make_async_remote_copy(
            src_ref=source, dst_ref=target, send_sem=ssem.at[index], recv_sem=rsem.at[index],
            device_id=device, device_id_type=MESH,
        )

    def own_rows(ref, owner, size, start=0, count=None):
        first = pl.multiple_of(owner * size + start, 16)
        return ref.at[pl.ds(first, size if count is None else count)]

    class Gather:
        def __init__(self, source, target, size, index):
            half = size // 2
            x, y, c = plane[2], plane[4], plane[1]
            self.own = here(source, own_rows(target, f, size), index // 8) if source is not None else None
            if source is None:
                source = own_rows(target, f, size)
            mine = own_rows(target, f, size)
            self.first = [
                there(source, mine, index, fsdp=x),
                there(source, mine, index + 1, fsdp=y),
                there(source, mine, index + 2, fsdp=c),
            ]
            from_x, from_y = own_rows(target, x, size), own_rows(target, y, size)
            part_x = own_rows(target, x, size, 0, half)
            part_y = own_rows(target, y, size, half, half)
            self.second = [
                there(part_x, part_x, index + 3, fsdp=y),
                there(part_y, part_y, index + 4, fsdp=x),
                there(from_x, from_x, index + 5, fsdp=c),
                there(from_y, from_y, index + 6, fsdp=c),
            ]
            diagonal = own_rows(target, plane[6], size)
            self.third = there(diagonal, diagonal, index + 7, fsdp=c)

        def start(self):
            if self.own is not None:
                self.own.start()
            for copy in self.first:
                copy.start()

        def forward(self):
            self.first[0].wait_recv()
            self.second[0].start()
            self.second[2].start()
            self.first[1].wait_recv()
            self.second[1].start()
            self.second[3].start()

        def last(self):
            self.second[0].wait_recv()
            self.second[1].wait_recv()
            self.third.start()

        def finish(self):
            if self.own is not None:
                self.own.wait()
            self.first[2].wait_recv()
            self.second[2].wait_recv()
            self.second[3].wait_recv()
            self.third.wait_recv()

        def sent(self):
            for copy in self.first + self.second + [self.third]:
                copy.wait_send()

    class Chain:
        def __init__(self, target, index):
            self.steps = []
            for step in range(1, n_s):
                up = own_rows(target, s - (step - 1), rows)
                down = own_rows(target, s + (step - 1), rows)
                i = index + 2 * (step - 1)
                self.steps.append((
                    pltpu.make_async_remote_copy(
                        src_ref=up, dst_ref=up, send_sem=zsend.at[i], recv_sem=zrecv.at[i],
                        device_id={"seq": s + 1}, device_id_type=MESH,
                    ),
                    pltpu.make_async_remote_copy(
                        src_ref=down, dst_ref=down, send_sem=zsend.at[i + 1], recv_sem=zrecv.at[i + 1],
                        device_id={"seq": s - 1}, device_id_type=MESH,
                    ),
                    (s >= step - 1) & (s < n_s - 1),
                    (s >= 1) & (s <= n_s - step),
                    s >= step,
                    s <= n_s - 1 - step,
                ))

        def send(self, step):
            up, down, can_up, can_down, _, _ = self.steps[step - 1]
            pl.when(can_up)(up.start)
            pl.when(can_down)(down.start)

        def receive(self, step):
            up, down, _, _, from_below, from_above = self.steps[step - 1]
            pl.when(from_below)(up.wait_recv)
            pl.when(from_above)(down.wait_recv)

        def sent(self):
            for up, down, can_up, can_down, _, _ in self.steps:
                pl.when(can_up)(up.wait_send)
                pl.when(can_down)(down.wait_send)

    pieces = [
        here(w_query, qkv.at[pl.ds(pl.multiple_of(f * block, 16), block), pl.ds(0, width)], 5),
        here(w_key, qkv.at[pl.ds(pl.multiple_of(f * block, 16), block), pl.ds(width, kv_width)], 6),
        here(w_value, qkv.at[pl.ds(pl.multiple_of(f * block, 16), block), pl.ds(width + kv_width, kv_width)], 7),
        here(cotangent, own_rows(upstream_all, s, rows), 8),
    ]
    load_gate = here(w_gate, gate_v, 9)
    load_up = here(w_up, up_v, 10)
    for copy in pieces:
        copy.start()
    load_gate.start()
    load_up.start()
    small_all[f] = small[...]
    slots_all[s] = slot_keys[...]

    gather_qkv = Gather(None, qkv, block, 0)
    gather_out = Gather(w_out, out_w, block, 8)
    gather_gu = Gather(gu_own, gu_all, block, 16)
    gather_down = Gather(w_down, down_all, unit, 24)
    chain_up = Chain(upstream_all, 0)
    chain_normed = Chain(normed_all, 6)
    send_small = [
        there(small, small_all.at[f], 32 + k, fsdp=plane[k]) for k in range(1, n_f)
    ]
    send_slots = [
        there(slot_keys, slots_all.at[s], 40 + j, seq=lax.rem(s + j, n_s)) for j in range(1, n_s)
    ]
    send_kv = [
        there(kv.at[s], kv.at[s], 44 + j, seq=lax.rem(s + j, n_s)) for j in range(1, n_s)
    ]
    for copy in pieces[:3]:
        copy.wait()
    pl.semaphore_wait(entry, n_f - 1 + n_s - 1)
    gather_qkv.start()
    for copy in send_small + send_slots:
        copy.start()
    pieces[3].wait()
    chain_up.send(1)

    load_gate.wait()
    load_up.wait()
    pick_units(gate_v, up_v, gu_own, w_gate.shape[1] // n_f, w_gate.shape[1] // (n_f * n_s), unit)

    for copy in send_small + send_slots:
        copy.wait_recv()
    third = 2 * block
    for i in range(n_f // 2):
        columns = slice(i * third, (i + 1) * third)
        gain_one[:, columns] = (
            small_all[2 * i, 0:1, :third].astype(jnp.float32)
            + small_all[2 * i + 1, 0:1, :third].astype(jnp.float32)
        )
        gain_two[:, columns] = (
            small_all[2 * i, 0:1, third : 2 * third].astype(jnp.float32)
            + small_all[2 * i + 1, 0:1, third : 2 * third].astype(jnp.float32)
        )
    bias_query = [
        small_all[2 * i, 0:1, 2 * third : 3 * third].astype(jnp.float32)
        + small_all[2 * i + 1, 0:1, 2 * third : 3 * third].astype(jnp.float32)
        for i in range(n_f // 2)
    ]
    bias_query = jnp.concatenate(bias_query, 1)
    bias_pair = sum(small_all[i, 0:1, 3 * third :].astype(jnp.float32) for i in range(n_f))

    inputs = tokens[...].astype(jnp.float32)
    root = lax.rsqrt(jnp.mean(inputs * inputs, -1, keepdims=True) + epsilon)
    normed_one[...] = (inputs * root * gain_one[...]).astype(jnp.bfloat16)
    for j in range(n_s):
        keys_slot = slots_all[j]
        keys_slot = jnp.concatenate([keys_slot] * (rows // 128), 1)
        ok = (keys_slot <= slot_row[0:1]) & (keys_slot >= first_row[0:1])
        bias[j * rows : (j + 1) * rows] = jnp.where(ok, 0.0, -1e30)

    gather_qkv.forward()
    gather_out.start()
    chain_up.receive(1)
    chain_up.send(2)
    gather_qkv.last()
    gather_qkv.finish()
    save_qkv = here(qkv, qkv_out, 11)
    save_qkv.start()

    def turned(value):
        return value * cosine[...] + pltpu.roll(value, HEAD_DIM // 2, 1) * sine[...]

    normed = normed_one[...]
    pair = jnp.dot(normed, qkv[:, width : width + kv_width], preferred_element_type=jnp.float32)
    pair = pair + bias_pair[:, :kv_width]
    for g in range(KV_HEADS):
        columns = slice(g * HEAD_DIM, (g + 1) * HEAD_DIM)
        kv[s, :, columns] = turned(pair[:, columns]).astype(jnp.bfloat16)
    pair = jnp.dot(normed, qkv[:, width + kv_width :], preferred_element_type=jnp.float32)
    kv[s, :, kv_width:] = (pair + bias_pair[:, kv_width:]).astype(jnp.bfloat16)
    for copy in send_kv:
        copy.start()
    for g in range(HEADS // 2):
        columns = slice(g * 2 * HEAD_DIM, (g + 1) * 2 * HEAD_DIM)
        pair = jnp.dot(normed, qkv[:, columns], preferred_element_type=jnp.float32)
        pair = pair + bias_query[:, columns]
        for h in range(2):
            part = turned(pair[:, h * HEAD_DIM : (h + 1) * HEAD_DIM]).astype(jnp.bfloat16)
            queries[:, (2 * g + h) * HEAD_DIM : (2 * g + h + 1) * HEAD_DIM] = part

    gather_out.forward()
    gather_gu.start()
    chain_up.receive(2)
    gather_out.last()
    for copy in send_kv:
        copy.wait_recv()
    chain_up.send(3)
    save_kv = here(kv, paired_out, 12)
    save_kv.start()
    slots_out[...] = slots_all[...]

    for g in range(KV_HEADS):
        keys = kv[:, :, g * HEAD_DIM : (g + 1) * HEAD_DIM].reshape(n_s * rows, HEAD_DIM)
        values = kv[:, :, kv_width + g * HEAD_DIM : kv_width + (g + 1) * HEAD_DIM]
        values = values.reshape(n_s * rows, HEAD_DIM)

        def head(i, carry, g=g, keys=keys, values=values):
            h = g * repeat + i
            columns = pl.ds(pl.multiple_of(h * HEAD_DIM, HEAD_DIM), HEAD_DIM)
            raw = lax.dot_general(
                keys, queries[:, columns], (((1,), (1,)), ((), ())),
                preferred_element_type=jnp.float32,
            )
            scores = raw * scale + bias[...]
            top = jnp.max(scores, 0, keepdims=True)
            expo = jnp.exp(scores - top)
            total = jnp.sum(expo, 0, keepdims=True)
            probs = (expo * (1.0 / total)).astype(jnp.bfloat16)
            mixed = lax.dot_general(
                values, probs, (((0,), (0,)), ((), ())), preferred_element_type=jnp.float32
            )
            attended[:, columns] = mixed.T.astype(jnp.bfloat16)
            logsum[pl.ds(pl.multiple_of(h * 8, 8), 8)] = jnp.broadcast_to(
                top + jnp.log(total), (8, rows)
            )
            return carry

        lax.fori_loop(0, repeat, head, 0)

    gather_out.finish()
    save_out = here(out_w, out_out, 13)
    save_out.start()
    mixed = attended[...]
    for g in range(width // 256):
        columns = slice(g * 256, (g + 1) * 256)
        part = jnp.dot(mixed, out_w[:, columns], preferred_element_type=jnp.float32)
        resid[:, columns] = tokens[:, columns].astype(jnp.float32) + part
    value = resid[...]
    root = lax.rsqrt(jnp.mean(value * value, -1, keepdims=True) + epsilon)
    normed_own[...] = (value * root * gain_two[...]).astype(jnp.bfloat16)
    place_normed = here(normed_own, own_rows(normed_all, s, rows), 14)
    place_normed.start()
    place_normed.wait()
    chain_normed.send(1)

    gather_gu.forward()
    gather_down.start()
    chain_normed.receive(1)
    chain_normed.send(2)
    gather_gu.last()
    chain_normed.receive(2)
    chain_normed.send(3)
    chain_up.receive(3)
    gather_down.forward()
    gather_gu.finish()
    gather_down.last()
    chain_normed.receive(3)
    gather_down.finish()
    save_qkv.wait()
    save_kv.wait()
    save_out.wait()
    for part in (gather_qkv, gather_out, gather_gu, gather_down, chain_up, chain_normed):
        part.sent()
    for copy in send_small + send_slots + send_kv:
        copy.wait_send()


def pick_units(gate, up, out, stride, unit, padded):
    rank = lax.axis_index("seq")
    pieces = gate.shape[1] // stride
    half = out.shape[1] // 2
    window, tile = 512, 128
    rows = lax.broadcasted_iota(jnp.int32, (window, tile), 0)
    columns = lax.broadcasted_iota(jnp.int32, (window, tile), 1)
    for first in range(0, 2 * half, tile):
        source = gate if first < half else up
        local = first % half
        total = jnp.zeros((out.shape[0], tile), jnp.float32)
        for f in range(pieces):
            low = max(local, f * padded)
            high = min(local + tile, f * padded + unit)
            if low >= high:
                continue
            begin = f * stride + rank * unit
            base = jnp.minimum(begin // 128, (source.shape[1] - window) // 128) * 128
            base = pl.multiple_of(base, 128)
            wanted = columns + (local - f * padded + begin - base)
            inside = (columns >= low - local) & (columns < high - local)
            chosen = jnp.where((rows == wanted) & inside, 1.0, 0.0).astype(jnp.bfloat16)
            total += jnp.dot(
                source[:, pl.ds(base, window)], chosen, preferred_element_type=jnp.float32
            )
        out[:, first : first + tile] = total.astype(jnp.bfloat16)


def front(tokens, cotangent, small, slot, first_row, cosine, sine, weights, w_down_own):
    rows, width = tokens.shape
    n_s = lax.axis_size("seq")
    w_query, w_key, w_value, w_out, w_gate, w_up = weights
    block = w_query.shape[0]
    unit = w_down_own.shape[0]
    kv_width = KV_HEADS * HEAD_DIM
    qkv_width = width + 2 * kv_width
    units = 8 * unit
    group = n_s * rows
    low, full = jnp.bfloat16, jnp.float32
    slot_f = slot.astype(full)
    slot_keys = jnp.broadcast_to(slot_f[:, None], (rows, 128))
    slot_row = jnp.broadcast_to(slot_f[None], (8, rows))
    first_f = jnp.broadcast_to(first_row.astype(full)[None], (8, rows))
    half = HEAD_DIM // 2
    sine = jnp.concatenate([-sine[:, :half], sine[:, half:]], 1)
    vmem = pl.BlockSpec(memory_space=pltpu.VMEM)
    hbm = pl.BlockSpec(memory_space=pl.ANY)
    shape = jax.ShapeDtypeStruct
    return pl.pallas_call(
        front_kernel,
        in_specs=[vmem, hbm] + [vmem] * 6 + [hbm] * 7,
        out_specs=[hbm] * 6 + [vmem, hbm] + [vmem] * 7,
        out_shape=[
            shape((8 * block, 2 * units), low),
            shape((units, width), low),
            shape((group, width), low),
            shape((group, width), low),
            shape((width, qkv_width), low),
            shape((width, width), low),
            shape((rows, width), low),
            shape((n_s, rows, 2 * kv_width), low),
            shape((n_s, rows, 128), full),
            shape((8 * HEADS, rows), full),
            shape((rows, width), low),
            shape((rows, width), full),
            shape((rows, width), low),
            shape((1, width), full),
            shape((1, width), full),
        ],
        scratch_shapes=[
            pltpu.VMEM((width, qkv_width), low),
            pltpu.VMEM((width, width), low),
            pltpu.VMEM(w_gate.shape, low),
            pltpu.VMEM(w_up.shape, low),
            pltpu.VMEM((block, 2 * units), low),
            pltpu.VMEM((n_s, rows, 2 * kv_width), low),
            pltpu.VMEM((8,) + small.shape, low),
            pltpu.VMEM((n_s, rows, 128), full),
            pltpu.VMEM((group, rows), full),
            pltpu.VMEM((rows, width), low),
            pltpu.SemaphoreType.DMA((16,)),
            pltpu.SemaphoreType.DMA((48,)),
            pltpu.SemaphoreType.DMA((48,)),
            pltpu.SemaphoreType.DMA((12,)),
            pltpu.SemaphoreType.DMA((12,)),
        ],
        compiler_params=pltpu.CompilerParams(
            collective_id=0, has_side_effects=True, vmem_limit_bytes=56 * 2**20
        ),
        name="front",
    )(
        tokens, cotangent, small, slot_keys, slot_row, first_f, cosine, sine,
        w_query, w_key, w_value, w_out, w_gate, w_up, w_down_own,
    )


def ffn_kernel(
    normed_all, upstream_all, w_gu, w_down,
    columns, grad_down, gu_sum, branch, down_arrived, gu_arrived,
    normed, upstream, gu, down, hidden, d_both, partial, z_one, z_two, z_three,
    down_x, down_y, down_last, branch_piece,
    load, ssem, rsem,
):
    f = lax.axis_index("fsdp")
    s = lax.axis_index("seq")
    n_s = len(ORDER)
    group, width = normed.shape
    rows = group // n_s
    half_rows = group // 2
    units = down.shape[0]
    tile = 256
    tiles = units // tile
    block = gu.shape[0] // 8
    unit = units // 8
    half = width // 2
    plane = [f ^ k for k in range(8)]
    full = jnp.float32

    entry = pltpu.get_barrier_semaphore()
    for k in (1, 2, 4):
        pl.semaphore_signal(entry, inc=1, device_id={"fsdp": plane[k]}, device_id_type=MESH)
    for j in (1, n_s - 1):
        pl.semaphore_signal(
            entry, inc=1, device_id={"seq": lax.rem(s + j, n_s)}, device_id_type=MESH
        )

    def here(source, target, index):
        return pltpu.make_async_copy(source, target, load.at[index])

    def there(source, target, index, **device):
        return pltpu.make_async_remote_copy(
            src_ref=source, dst_ref=target, send_sem=ssem.at[index], recv_sem=rsem.at[index],
            device_id=device, device_id_type=MESH,
        )

    def part(ref, owner, size):
        return ref.at[pl.ds(pl.multiple_of(owner * size, 16), size)]

    first_loads = []
    for p, j in enumerate(ORDER):
        owner = lax.rem(s + n_s - j, n_s)
        first_loads.append(here(part(normed_all, owner, rows), part(normed, p, rows), p))
        first_loads.append(here(part(upstream_all, owner, rows), part(upstream, p, rows), 4 + p))

    def tile_loads(t):
        gate_columns = pl.ds(pl.multiple_of(t * tile, tile), tile)
        up_columns = pl.ds(pl.multiple_of(units + t * tile, tile), tile)
        return [
            here(w_gu.at[:, gate_columns], gu.at[:, gate_columns], 8 + 3 * t),
            here(w_gu.at[:, up_columns], gu.at[:, up_columns], 9 + 3 * t),
            here(w_down.at[gate_columns], down.at[gate_columns], 10 + 3 * t),
        ]

    for copy in first_loads:
        copy.start()
    for t in range(tiles):
        for copy in tile_loads(t):
            copy.start()
    for copy in first_loads:
        copy.wait()

    def forward(part_rows, wait):
        def body(t, carry):
            if wait:
                for copy in tile_loads(t):
                    copy.wait()
            gate_columns = pl.ds(pl.multiple_of(t * tile, tile), tile)
            up_columns = pl.ds(pl.multiple_of(units + t * tile, tile), tile)
            mine = normed[part_rows]
            gate = jnp.dot(mine, gu[:, gate_columns], preferred_element_type=full)
            up = jnp.dot(mine, gu[:, up_columns], preferred_element_type=full)
            d_hidden = lax.dot_general(
                upstream[part_rows], down[gate_columns], (((1,), (1,)), ((), ())),
                preferred_element_type=full,
            )
            sigma = jax.nn.sigmoid(gate)
            activated = gate * sigma
            hidden[part_rows, gate_columns] = (activated * up).astype(jnp.bfloat16)
            d_both[part_rows, gate_columns] = (
                d_hidden * up * sigma * (1.0 + gate * (1.0 - sigma))
            ).astype(jnp.bfloat16)
            d_both[part_rows, up_columns] = (d_hidden * activated).astype(jnp.bfloat16)
            return carry

        lax.fori_loop(0, tiles, body, 0)

    def backward(part_rows):
        def body(n, carry):
            out_columns = pl.ds(pl.multiple_of(n * tile, tile), tile)
            value = lax.dot_general(
                d_both[part_rows], gu[out_columns], (((1,), (1,)), ((), ())),
                preferred_element_type=full,
            )
            partial[part_rows, out_columns] = value.astype(jnp.bfloat16)
            return carry

        lax.fori_loop(0, width // tile, body, 0)

    chain = SumChain(partial, rows, z_one, z_two, z_three, there, 0)
    early, late = slice(0, half_rows), slice(half_rows, group)
    forward(early, True)
    backward(early)
    pl.semaphore_wait(entry, 5)
    chain.one()
    forward(late, False)
    backward(late)
    chain.two()

    def branch_store(n):
        out_columns = pl.ds(pl.multiple_of(n * tile, tile), tile)
        return here(branch_piece.at[lax.rem(n, 2)], branch.at[:, out_columns], 8 + n)

    def branch_body(n, carry):
        out_columns = pl.ds(pl.multiple_of(n * tile, tile), tile)
        value = jnp.dot(hidden[...], down[:, out_columns], preferred_element_type=full)

        @pl.when(n >= 2)
        def _():
            branch_store(n - 2).wait()

        branch_piece[lax.rem(n, 2)] = value.astype(jnp.bfloat16)
        branch_store(n).start()
        return carry

    lax.fori_loop(0, width // tile, branch_body, 0)
    for n in (width // tile - 2, width // tile - 1):
        branch_store(n).wait()

    def down_body(t, carry):
        unit_rows = pl.ds(pl.multiple_of(t * tile, tile), tile)
        value = lax.dot_general(
            hidden[:, unit_rows], upstream[...], (((0,), (0,)), ((), ())),
            preferred_element_type=full,
        )
        down[unit_rows] = value.astype(jnp.bfloat16)
        return carry

    lax.fori_loop(0, tiles, down_body, 0)
    down_core = [
        there(part(down, plane[2 * i + 1], unit), down_arrived.at[i], 6 + i, fsdp=plane[1])
        for i in range(4)
    ]
    for copy in down_core:
        copy.start()

    def gu_body(m, carry):
        in_columns = pl.ds(pl.multiple_of(m * tile, tile), tile)
        turned = normed[:, in_columns].T
        for first in range(0, 2 * units, units // 3):
            value = jnp.dot(turned, d_both[:, first : first + units // 3], preferred_element_type=full)
            gu[in_columns, first : first + units // 3] = value.astype(jnp.bfloat16)
        return carry

    lax.fori_loop(0, width // tile // 2, gu_body, 0)

    def add_arrived(ref, size, arrived, pieces, copies, index):
        for i in range(4):
            copies[i].wait_recv()
            fetch = [
                here(arrived.at[i, :, columns], piece, index + k)
                for k, (columns, piece) in enumerate(pieces)
            ]
            for copy in fetch:
                copy.start()
            target = part(ref, plane[2 * i], size)
            for copy, (columns, piece) in zip(fetch, pieces):
                copy.wait()
                target[:, columns] = (
                    target[:, columns].astype(full) + piece[...].astype(full)
                ).astype(jnp.bfloat16)

    add_arrived(down, unit, down_arrived, [(pl.ds(0, width), hidden.at[:unit, :width])], down_core, 14)
    to_x, to_y, to_both = [part(down, plane[k], unit) for k in (2, 4, 6)]
    low_half, high_half = pl.ds(0, half), pl.ds(half, half)
    down_first = [
        there(to_x.at[:, low_half], down_x.at[0], 10, fsdp=plane[2]),
        there(to_both.at[:, low_half], down_x.at[1], 11, fsdp=plane[2]),
        there(to_y.at[:, high_half], down_y.at[0], 12, fsdp=plane[4]),
        there(to_both.at[:, high_half], down_y.at[1], 13, fsdp=plane[4]),
    ]
    for copy in down_first:
        copy.start()
    chain.three()
    lax.fori_loop(width // tile // 2, width // tile, gu_body, 0)
    gu_core = [
        there(part(gu, plane[2 * i + 1], block), gu_arrived.at[i], 16 + i, fsdp=plane[1])
        for i in range(4)
    ]
    for copy in gu_core:
        copy.start()
    chain.last(columns)
    down_second = [
        there(to_y.at[:, low_half], down_last.at[0], 14, fsdp=plane[4]),
        there(to_x.at[:, high_half], down_last.at[1], 15, fsdp=plane[2]),
    ]
    down_first[1].wait_recv()
    to_y[:, :half] = (to_y[:, :half].astype(full) + down_x[1].astype(full)).astype(jnp.bfloat16)
    down_second[0].start()
    down_first[3].wait_recv()
    to_x[:, half:] = (to_x[:, half:].astype(full) + down_y[1].astype(full)).astype(jnp.bfloat16)
    down_second[1].start()
    gu_pieces = [
        (pl.ds(0, units), hidden.at[:block]),
        (pl.ds(units, units), hidden.at[block : 2 * block]),
    ]
    add_arrived(gu, block, gu_arrived, gu_pieces, gu_core, 20)
    store = [here(part(gu, plane[2 * i], block), gu_sum.at[i], 16 + i) for i in range(4)]
    for copy in store:
        copy.start()
    down_first[0].wait_recv()
    down_first[2].wait_recv()
    own = part(down, f, unit)
    down_second[0].wait_recv()
    grad_down[:, :half] = (
        own[:, :half].astype(full) + down_x[0].astype(full) + down_last[0].astype(full)
    )
    down_second[1].wait_recv()
    grad_down[:, half:] = (
        own[:, half:].astype(full) + down_y[0].astype(full) + down_last[1].astype(full)
    )
    for copy in store:
        copy.wait()
    chain.sent()
    for copy in down_core + down_first + down_second + gu_core:
        copy.wait_send()


def ffn(normed_all, upstream_all, w_gu, w_down):
    group, width = normed_all.shape
    units = w_down.shape[0]
    rows = group // len(ORDER)
    unit, block, half = units // 8, width // 8, width // 2
    low, full = jnp.bfloat16, jnp.float32
    vmem = pl.BlockSpec(memory_space=pltpu.VMEM)
    hbm = pl.BlockSpec(memory_space=pl.ANY)
    shape = jax.ShapeDtypeStruct
    return pl.pallas_call(
        ffn_kernel,
        in_specs=[hbm] * 4,
        out_specs=[vmem] * 2 + [hbm] * 4,
        out_shape=[
            shape((rows, width), full),
            shape((unit, width), full),
            shape((4, block, 2 * units), low),
            shape((group, width), low),
            shape((4, unit, width), low),
            shape((4, block, 2 * units), low),
        ],
        scratch_shapes=[
            pltpu.VMEM((group, width), low),
            pltpu.VMEM((group, width), low),
            pltpu.VMEM((width, 2 * units), low),
            pltpu.VMEM((units, width), low),
            pltpu.VMEM((group, units), low),
            pltpu.VMEM((group, 2 * units), low),
            pltpu.VMEM((group, width), low),
            pltpu.VMEM((rows, width), low),
            pltpu.VMEM((2, rows, width), low),
            pltpu.VMEM((2, rows, width), low),
            pltpu.VMEM((2, unit, half), low),
            pltpu.VMEM((2, unit, half), low),
            pltpu.VMEM((2, unit, half), low),
            pltpu.VMEM((2, group, 256), low),
            pltpu.SemaphoreType.DMA((36,)),
            pltpu.SemaphoreType.DMA((20,)),
            pltpu.SemaphoreType.DMA((20,)),
        ],
        compiler_params=pltpu.CompilerParams(
            collective_id=1, has_side_effects=True, vmem_limit_bytes=63 * 2**20
        ),
        name="ffn",
    )(normed_all, upstream_all, w_gu, w_down)[:4]


def back_kernel(
    columns, resid, gain_two, cotangent, attended, queries, paired, slots, slot_row, first_row,
    logsum, normeworking, tokens, gain_one, cosine, sine, w_out, w_qkv, gu_sum, branch,
    layer, input_rows, vector, grad_out, grad_qkv, gu_rows,
    out_w, qkv, gu_own, gu_to_y, gu_to_x, gu_x, gu_y, gu_ended,
    branch_v, z_one, z_two, z_three, working, bias, d_branch, d_attended, d_qkv, d_resid,
    keys_grad, values_grad, dkv, dkv_in,
    out_arrived, out_x, out_y, out_ended, qkv_arrived, qkv_x, qkv_y, qkv_ended,
    out_in, qkv_in, vector_in,
    load, ssem, rsem,
):
    f = lax.axis_index("fsdp")
    s = lax.axis_index("seq")
    rows, width = tokens.shape
    n_s = paired.shape[0]
    kv_width = KV_HEADS * HEAD_DIM
    repeat = HEADS // KV_HEADS
    scale = HEAD_DIM ** (-0.5)
    block = width // 8
    piece = block // n_s
    units = gu_sum.shape[2] // 2
    tile = 256
    full, low = jnp.float32, jnp.bfloat16
    plane = [f ^ k for k in range(8)]

    entry = pltpu.get_barrier_semaphore()
    for k in (1, 2, 4):
        pl.semaphore_signal(entry, inc=1, device_id={"fsdp": plane[k]}, device_id_type=MESH)
    for j in range(1, n_s):
        pl.semaphore_signal(
            entry, inc=1, device_id={"seq": lax.rem(s + j, n_s)}, device_id_type=MESH
        )

    def here(source, target, index):
        return pltpu.make_async_copy(source, target, load.at[index])

    def there(source, target, index, **device):
        return pltpu.make_async_remote_copy(
            src_ref=source, dst_ref=target, send_sem=ssem.at[index], recv_sem=rsem.at[index],
            device_id=device, device_id_type=MESH,
        )

    low_units, high_units = pl.ds(0, units), pl.ds(units, units)
    load_branch = here(branch, branch_v, 0)
    load_out = here(w_out, out_w, 1)
    load_gu = [
        here(gu_sum.at[0], gu_own, 2),
        here(gu_sum.at[2, :, low_units], gu_to_y, 3),
        here(gu_sum.at[1, :, high_units], gu_to_x, 4),
    ]
    load_qkv = here(w_qkv, qkv, 5)
    load_columns = here(columns, working, 7)
    for copy in [load_columns, load_branch, load_out] + load_gu + [load_qkv]:
        copy.start()

    gu_first = [
        there(gu_sum.at[3, :, low_units], gu_x.at[1], 0, fsdp=plane[2]),
        there(gu_sum.at[3, :, high_units], gu_y.at[1], 1, fsdp=plane[4]),
        there(gu_sum.at[1, :, low_units], gu_x.at[0], 2, fsdp=plane[2]),
        there(gu_sum.at[2, :, high_units], gu_y.at[0], 3, fsdp=plane[4]),
    ]
    gu_second = [
        there(gu_to_y, gu_ended.at[0], 4, fsdp=plane[4]),
        there(gu_to_x, gu_ended.at[1], 5, fsdp=plane[2]),
    ]

    def around(j):
        return {"seq": lax.rem(s + j, n_s)}

    def rows_for(ref, first, j):
        owner = lax.rem(s + j, n_s)
        return ref.at[pl.ds(pl.multiple_of(first + owner * piece, 16), piece)]

    gu_send = [there(rows_for(gu_own, 0, j), gu_rows.at[j], 5 + j, **around(j)) for j in range(1, n_s)]
    dkv_send = [
        [
            there(dkv.at[g, lax.rem(s + j, n_s)], dkv_in.at[g, j], 8 + 3 * g + j, **around(j))
            for j in range(1, n_s)
        ]
        for g in range(KV_HEADS)
    ]
    chain = SumChain(branch_v, rows, z_one, z_two, z_three, there, 16)
    sum_out = SumPlane(out_w, block, plane, out_arrived, out_x, out_y, out_ended, there, 24)
    sum_qkv = SumPlane(qkv, block, plane, qkv_arrived, qkv_x, qkv_y, qkv_ended, there, 36)
    out_send = [there(rows_for(out_w, f * block, j), out_in.at[j], 47 + j, **around(j)) for j in range(1, n_s)]
    qkv_send = [there(rows_for(qkv, f * block, j), qkv_in.at[j], 51 + j, **around(j)) for j in range(1, n_s)]
    vector_send = [
        there(vector_in.at[0], vector_in.at[1], 56, fsdp=plane[1]),
        there(vector_in.at[2], vector_in.at[3], 57, fsdp=plane[2]),
        there(vector_in.at[4], vector_in.at[5], 58, fsdp=plane[4]),
    ] + [there(vector_in.at[6], vector_in.at[6 + j], 58 + j, **around(j)) for j in range(1, n_s)]

    pl.semaphore_wait(entry, 3 + n_s - 1)
    for copy in gu_first:
        copy.start()
    load_branch.wait()
    chain.one()

    def norm_back(value, gain, grad):
        root = lax.rsqrt(jnp.mean(value * value, -1, keepdims=True) + epsilon)
        scaled = gain * grad
        inner = jnp.mean(scaled * value, -1, keepdims=True)
        gain_grad = jnp.sum(grad * (value * root), 0, keepdims=True)
        return root * scaled - value * (root * root * root * inner), gain_grad

    load_columns.wait()
    d_norm, gain_two_grad = norm_back(resid[...], gain_two[...], working[...])
    d_total = cotangent[...].astype(full) + d_norm
    d_branch[...] = d_total.astype(low)
    d_resid[...] = d_total
    for j in range(n_s):
        keys_slot = slots[j]
        keys_slot = jnp.concatenate([keys_slot] * (rows // 128), 1)
        ok = (keys_slot <= slot_row[0:1]) & (keys_slot >= first_row[0:1])
        bias[j * rows : (j + 1) * rows] = jnp.where(ok, 0.0, -1e30)
    load_out.wait()
    for n in range(width // tile):
        value = lax.dot_general(
            d_branch[...], out_w[n * tile : (n + 1) * tile], (((1,), (1,)), ((), ())),
            preferred_element_type=full,
        )
        d_attended[:, n * tile : (n + 1) * tile] = value.astype(low)

    def turned_back(value):
        return value * cosine[...] + pltpu.roll(value * sine[...], HEAD_DIM // 2, 1)

    for g in range(KV_HEADS):
        keys = paired[:, :, g * HEAD_DIM : (g + 1) * HEAD_DIM].reshape(n_s * rows, HEAD_DIM)
        values = paired[:, :, kv_width + g * HEAD_DIM : kv_width + (g + 1) * HEAD_DIM]
        values = values.reshape(n_s * rows, HEAD_DIM)
        keys_grad[...] = jnp.zeros_like(keys_grad)
        values_grad[...] = jnp.zeros_like(values_grad)

        def head(i, carry, g=g, keys=keys, values=values):
            h = g * repeat + i
            head_columns = pl.ds(pl.multiple_of(h * HEAD_DIM, HEAD_DIM), HEAD_DIM)
            query = queries[:, head_columns]
            grad = d_attended[:, head_columns]
            raw = lax.dot_general(
                keys, query, (((1,), (1,)), ((), ())), preferred_element_type=full
            )
            logs = logsum[pl.ds(pl.multiple_of(h * 8, 8), 8)][0:1]
            probs = jnp.exp(raw * scale + bias[...] - logs)
            d_probs = lax.dot_general(
                values, grad, (((1,), (1,)), ((), ())), preferred_element_type=full
            )
            delta = jnp.sum(probs * d_probs, 0, keepdims=True)
            d_score = (probs * (d_probs - delta)).astype(low)
            turned = lax.dot_general(
                keys, d_score, (((0,), (0,)), ((), ())), preferred_element_type=full
            )
            d_qkv[:, head_columns] = turned_back((turned * scale).T).astype(low)
            keys_grad[...] += jnp.dot(d_score, query, preferred_element_type=full) * scale
            values_grad[...] += jnp.dot(probs.astype(low), grad, preferred_element_type=full)
            return carry

        lax.fori_loop(0, repeat, head, 0)
        dkv[g, :, :, :HEAD_DIM] = keys_grad[...].astype(low).reshape(n_s, rows, HEAD_DIM)
        dkv[g, :, :, HEAD_DIM:] = values_grad[...].astype(low).reshape(n_s, rows, HEAD_DIM)
        for copy in dkv_send[g]:
            copy.start()

    turned = attended[...].T
    for n in range(width // tile):
        n_columns = slice(n * tile, (n + 1) * tile)
        value = jnp.dot(turned, d_branch[:, n_columns], preferred_element_type=full)
        out_w[:, n_columns] = value.astype(low)
    sum_out.start_core()
    load_qkv.wait()

    def back_one(first, count, start):
        for n in range(width // tile):
            n_rows = slice(n * tile, (n + 1) * tile)
            value = lax.dot_general(
                d_qkv[:, first : first + count], qkv[n_rows, first : first + count],
                (((1,), (1,)), ((), ())), preferred_element_type=full,
            )
            working[:, n_rows] = value if start else working[:, n_rows] + value

    back_one(0, width, True)
    normed_turned = normeworking[...].T
    for n in range(width // tile):
        n_columns = slice(n * tile, (n + 1) * tile)
        value = jnp.dot(normed_turned, d_qkv[:, n_columns], preferred_element_type=full)
        qkv[:, n_columns] = value.astype(low)
    sum_out.start_first()

    for g in range(KV_HEADS):
        for copy in dkv_send[g]:
            copy.wait_recv()
        total = dkv[g, s].astype(full)
        for j in range(1, n_s):
            total = total + dkv_in[g, j].astype(full)
        key_columns = slice(width + g * HEAD_DIM, width + (g + 1) * HEAD_DIM)
        value_columns = slice(width + kv_width + g * HEAD_DIM, width + kv_width + (g + 1) * HEAD_DIM)
        d_qkv[:, key_columns] = turned_back(total[:, :HEAD_DIM]).astype(low)
        d_qkv[:, value_columns] = total[:, HEAD_DIM:].astype(low)
    chain.two()
    back_one(width, 2 * kv_width, False)
    value = jnp.dot(normed_turned, d_qkv[:, width:], preferred_element_type=full)
    qkv[:, width:] = value.astype(low)
    sum_qkv.start_core()

    for copy in load_gu:
        copy.wait()
    gu_first[0].wait_recv()
    gu_to_y[...] = (gu_to_y[...].astype(full) + gu_x[1].astype(full)).astype(low)
    gu_second[0].start()
    gu_first[1].wait_recv()
    gu_to_x[...] = (gu_to_x[...].astype(full) + gu_y[1].astype(full)).astype(low)
    gu_second[1].start()

    d_norm, gain_one_grad = norm_back(tokens[...].astype(full), gain_one[...], working[...])
    input_rows[...] = (d_resid[...] + d_norm).astype(low)
    bias_grad = jnp.sum(d_qkv[...].astype(full), 0, keepdims=True)
    vectors = jnp.concatenate([gain_one_grad, gain_two_grad, bias_grad], 1)
    part = vectors.shape[1] // 8
    for r in range(8):
        vector_in[0, r : r + 1] = vectors[:, r * part : (r + 1) * part]
    vector_send[0].start()
    sum_qkv.start_first()
    vector_send[0].wait_recv()
    vector_in[2] = vector_in[0] + vector_in[1]
    vector_send[1].start()
    chain.three()
    sum_out.start_second()

    gu_first[2].wait_recv()
    gu_second[0].wait_recv()
    total = gu_own[:, :units].astype(full) + gu_x[0].astype(full) + gu_ended[0].astype(full)
    gu_own[:, :units] = total.astype(low)
    gu_first[3].wait_recv()
    gu_second[1].wait_recv()
    total = gu_own[:, units:].astype(full) + gu_y[0].astype(full) + gu_ended[1].astype(full)
    gu_own[:, units:] = total.astype(low)
    for copy in gu_send:
        copy.start()
    keep_rows = here(rows_for(gu_own, 0, 0), gu_rows.at[0], 6)
    keep_rows.start()
    vector_send[1].wait_recv()
    vector_in[4] = vector_in[2] + vector_in[3]
    vector_send[2].start()

    sum_out.finish()
    for copy in out_send:
        copy.start()
    sum_qkv.start_second()
    vector_send[2].wait_recv()
    vector_in[6] = vector_in[4] + vector_in[5]
    for copy in vector_send[3:]:
        copy.start()
    chain.last(working)
    layer[...] = (resid[...] + working[...]).astype(low)
    sum_qkv.finish()
    for copy in qkv_send:
        copy.start()

    def gathered(own, copies, arrived, out):
        total = own[...].astype(full)
        for copy in copies:
            copy.wait_recv()
        for j in range(1, n_s):
            total = total + arrived[j].astype(full)
        out[...] = total

    gathered(rows_for(out_w, f * block, 0), out_send, out_in, grad_out)
    for copy in vector_send[3:]:
        copy.wait_recv()
    vector[...] = vector_in[6] + vector_in[7] + vector_in[8] + vector_in[9]
    gathered(rows_for(qkv, f * block, 0), qkv_send, qkv_in, grad_qkv)
    for copy in gu_send:
        copy.wait_recv()
    keep_rows.wait()
    chain.sent()
    sum_out.sent()
    sum_qkv.sent()
    for copy in gu_first + gu_second + gu_send + out_send + qkv_send + vector_send:
        copy.wait_send()
    for g in range(KV_HEADS):
        for copy in dkv_send[g]:
            copy.wait_send()


def back(
    columns, resid, gain_two, cotangent, attended, queries, paired, slots, slot, first_row,
    logsum, normeworking, tokens, gain_one, cosine, sine, w_out, w_qkv, gu_sum, branch,
):
    rows, width = tokens.shape
    n_s = paired.shape[0]
    group = n_s * rows
    kv_width = KV_HEADS * HEAD_DIM
    qkv_width = width + 2 * kv_width
    block = width // 8
    piece = block // n_s
    units = gu_sum.shape[2] // 2
    low, full = jnp.bfloat16, jnp.float32
    slot_row = jnp.broadcast_to(slot.astype(full)[None], (8, rows))
    first_f = jnp.broadcast_to(first_row.astype(full)[None], (8, rows))
    half = HEAD_DIM // 2
    sine = jnp.concatenate([-sine[:, :half], sine[:, half:]], 1)
    vmem = pl.BlockSpec(memory_space=pltpu.VMEM)
    hbm = pl.BlockSpec(memory_space=pl.ANY)
    shape = jax.ShapeDtypeStruct
    vectors = (2 * width + qkv_width) // 8
    return pl.pallas_call(
        back_kernel,
        in_specs=[hbm] + [vmem] * 15 + [hbm] * 4,
        out_specs=[vmem] * 5 + [hbm],
        out_shape=[
            shape((rows, width), low),
            shape((rows, width), low),
            shape((8, vectors), full),
            shape((piece, width), full),
            shape((piece, qkv_width), full),
            shape((n_s, piece, 2 * units), low),
        ],
        scratch_shapes=[
            pltpu.VMEM((width, width), low),
            pltpu.VMEM((width, qkv_width), low),
            pltpu.VMEM((block, 2 * units), low),
            pltpu.VMEM((block, units), low),
            pltpu.VMEM((block, units), low),
            pltpu.VMEM((2, block, units), low),
            pltpu.VMEM((2, block, units), low),
            pltpu.VMEM((2, block, units), low),
            pltpu.VMEM((group, width), low),
            pltpu.VMEM((rows, width), low),
            pltpu.VMEM((2, rows, width), low),
            pltpu.VMEM((2, rows, width), low),
            pltpu.VMEM((rows, width), full),
            pltpu.VMEM((group, rows), full),
            pltpu.VMEM((rows, width), low),
            pltpu.VMEM((rows, width), low),
            pltpu.VMEM((rows, qkv_width), low),
            pltpu.VMEM((rows, width), full),
            pltpu.VMEM((group, HEAD_DIM), full),
            pltpu.VMEM((group, HEAD_DIM), full),
            pltpu.VMEM((KV_HEADS, n_s, rows, 2 * HEAD_DIM), low),
            pltpu.VMEM((KV_HEADS, n_s, rows, 2 * HEAD_DIM), low),
            pltpu.VMEM((4, block, width), low),
            pltpu.VMEM((2, block, width // 2), low),
            pltpu.VMEM((2, block, width // 2), low),
            pltpu.VMEM((2, block, width // 2), low),
            pltpu.VMEM((4, block, qkv_width), low),
            pltpu.VMEM((2, block, qkv_width // 2), low),
            pltpu.VMEM((2, block, qkv_width // 2), low),
            pltpu.VMEM((2, block, qkv_width // 2), low),
            pltpu.VMEM((n_s, piece, width), low),
            pltpu.VMEM((n_s, piece, qkv_width), low),
            pltpu.VMEM((10, 8, vectors), full),
            pltpu.SemaphoreType.DMA((8,)),
            pltpu.SemaphoreType.DMA((64,)),
            pltpu.SemaphoreType.DMA((64,)),
        ],
        compiler_params=pltpu.CompilerParams(
            collective_id=2, has_side_effects=True, vmem_limit_bytes=63 * 2**20
        ),
        name="back",
    )(
        columns, resid, gain_two, cotangent, attended, queries, paired, slots, slot_row, first_f,
        logsum, normeworking, tokens, gain_one, cosine, sine, w_out, w_qkv, gu_sum, branch,
    )


def finish_kernel(
    layer, input_rows, grad_out, grad_qkv, grad_down, gu_rows,
    layer_out, input_grad, out_out, query_out, key_out, value_out, down_out, gate_out, up_out,
):
    s = lax.axis_index("seq")
    n_s = gu_rows.shape[0]
    width = grad_out.shape[1]
    kv_width = KV_HEADS * HEAD_DIM
    unit_pad = grad_down.shape[0]
    unit = down_out.shape[0]
    units = gu_rows.shape[2] // 2
    layer_out[...] = layer[...]
    input_grad[...] = input_rows[...]
    out_out[...] = grad_out[...]
    query_out[...] = grad_qkv[:, :width]
    key_out[...] = grad_qkv[:, width : width + kv_width]
    value_out[...] = grad_qkv[:, width + kv_width :]
    down_out[...] = grad_down[:unit]
    window = 512
    lanes = lax.broadcasted_iota(jnp.int32, (gu_rows.shape[1], 128), 1)
    for base, out in ((0, gate_out), (units, up_out)):
        for f in range(units // unit_pad):
            for owner in range(n_s):
                source = base + f * unit_pad
                begin = min(source // 128 * 128, 2 * units - window)
                target = (f * n_s + owner) * unit
                first = target // 128 * 128
                slot = lax.rem(s + n_s - owner, n_s)
                value = gu_rows[slot, :, begin : begin + window].astype(jnp.float32)
                turn = ((target - first) - (source - begin)) % window
                if turn:
                    value = pltpu.roll(value, turn, 1)
                for t in range(first, min(target + unit, out.shape[1]), 128):
                    part = value[:, t - first : t - first + 128]
                    if t < target:
                        part = jnp.where(lanes >= target - t, part, out[:, t : t + 128])
                    out[:, t : t + 128] = part


def finish(layer, input_rows, grad_out, grad_qkv, grad_down, gu_rows, unit, hidden_width):
    piece, width = grad_out.shape
    kv_width = KV_HEADS * HEAD_DIM
    low, full = jnp.bfloat16, jnp.float32
    shape = jax.ShapeDtypeStruct
    vmem = pl.BlockSpec(memory_space=pltpu.VMEM)
    return pl.pallas_call(
        finish_kernel,
        in_specs=[vmem] * 6,
        out_specs=[vmem] * 9,
        out_shape=[
            shape(layer.shape, low),
            shape(layer.shape, low),
            shape((piece, width), full),
            shape((piece, width), full),
            shape((piece, kv_width), full),
            shape((piece, kv_width), full),
            shape((unit, width), full),
            shape((piece, hidden_width), full),
            shape((piece, hidden_width), full),
        ],
        compiler_params=pltpu.CompilerParams(vmem_limit_bytes=48 * 2**20),
        name="finish",
    )(layer, input_rows, grad_out, grad_qkv, grad_down, gu_rows)


def per_device(
    tokens, cotangent, lengths, balance, norm1_gain, w_query, b_query, w_key, b_key,
    w_value, b_value, w_out, norm2_gain, w_gate, w_up, w_down,
):
    seq_count = lax.axis_size("seq")
    fsdp_count = lax.axis_size("fsdp")
    seq_rank = lax.axis_index("seq")
    fsdp_rank = lax.axis_index("fsdp")
    rows_here, width = tokens.shape
    group = seq_count * rows_here
    kv_width = KV_HEADS * HEAD_DIM
    hidden_width = w_gate.shape[1]
    unit = hidden_width // (fsdp_count * seq_count)
    unit_pad = -(-unit // 16) * 16
    weight_rows = w_gate.shape[0]

    pair_bias = jnp.concatenate([jnp.tile(b_key, fsdp_count), jnp.tile(b_value, fsdp_count)])
    small = jnp.concatenate([norm1_gain] * 2 + [norm2_gain] * 2 + [b_query] * 2 + [pair_bias])
    place_of = np.concatenate(
        [np.repeat([0, 1], weight_rows)] * 3 + [8 + np.repeat(np.arange(8), b_key.shape[0])] * 2
    )
    place_of = jnp.asarray(place_of, jnp.int32)
    mine = (place_of == fsdp_rank % 2) | (place_of == 8 + fsdp_rank)
    small = jnp.broadcast_to(jnp.where(mine, small, 0)[None], (16, small.shape[0]))

    slot = balance % group
    seq_lengths = lengths[0]
    starts = jnp.cumsum(seq_lengths) - seq_lengths
    segment = segment_of(slot, starts)
    first_row = jnp.where(segment == 0, starts[0], jnp.where(segment == 1, starts[1], starts[2]))
    cosine, sine = rope_tables(slot - first_row)
    down_own = lax.dynamic_slice_in_dim(w_down, seq_rank * unit, unit, 0)
    down_own = jnp.pad(down_own, ((0, unit_pad - unit), (0, 0)))
    (
        weight_gu, weight_down, upstream_all, normed_all, weight_qkv, weight_out,
        queries, paired, slots_all, logsum, attended, resid, normed_one, gain_one, gain_two,
    ) = front(
        tokens, cotangent, small, slot, first_row, cosine, sine,
        (w_query, w_key, w_value, w_out, w_gate, w_up), down_own,
    )
    columns, grad_down, gu_sum, branch = ffn(normed_all, upstream_all, weight_gu, weight_down)
    layer, input_rows, vectors, grad_out, grad_qkv, gu_rows = back(
        columns, resid, gain_two, cotangent, attended, queries, paired, slots_all, slot, first_row,
        logsum, normed_one, tokens, gain_one, cosine, sine, weight_out, weight_qkv, gu_sum, branch,
    )
    (
        layer_out, input_grad, grad_out, grad_query, grad_key, grad_value, grad_down, grad_gate,
        grad_up,
    ) = finish(layer, input_rows, grad_out, grad_qkv, grad_down, gu_rows, unit, hidden_width)
    vectors = vectors.reshape(-1)
    own = width // (fsdp_count * seq_count)
    first = (fsdp_rank * seq_count + seq_rank) * own

    def own_part(offset):
        return lax.dynamic_slice_in_dim(vectors, offset + first, own, 0)

    biases = 2 * width
    return (
        layer_out,
        input_grad,
        own_part(0),
        grad_query,
        own_part(biases),
        grad_key,
        vectors[biases + width : biases + width + kv_width],
        grad_value,
        vectors[biases + width + kv_width :],
        grad_out,
        own_part(width),
        grad_gate,
        grad_up,
        grad_down,
    )


def solution(mesh):
    both = P(("fsdp", "seq"), None)
    both_one = P(("fsdp", "seq"))
    placed = (
        both, both, P("fsdp", None), both_one, P("fsdp"), P("fsdp", None), P("fsdp"),
        P("fsdp", None), P("fsdp"), P("fsdp", None), P("fsdp"), P("fsdp", None), P("fsdp"),
        P("fsdp", None), P("fsdp", None), P("fsdp", None),
    )
    return jax.shard_map(
        per_device if mesh.shape["fsdp"] == 8 else plain_device,
        mesh=mesh,
        in_specs=placed,
        out_specs=(
            both, both, both_one, both, both_one, both, P(), both, P(), both, both_one,
            both, both, both,
        ),
        check_vma=False,
    )
```

```python
import jax
import jax.numpy as jnp
import numpy as np
from jax import lax
from jax.experimental import pallas as pl
from jax.experimental.pallas import tpu as pltpu
from jax.sharding import PartitionSpec as P

HEADS = 12
KV_HEADS = 2
HEAD_DIM = 128

MESH = pl.DeviceIdType.MESH

epsilon = 1e-06
rope_base = 1000000.0


def norm_piece(values, gain):
    return values * lax.rsqrt(jnp.mean(values * values, -1, keepdims=True) + epsilon) * gain


def rope_tables(position):
    half = HEAD_DIM // 2
    inverse = rope_base ** (-(jnp.arange(half, dtype=jnp.float32) * 2.0 / HEAD_DIM))
    angle = position.astype(jnp.float32)[:, None] * inverse[None, :]
    cosine = jnp.concatenate([jnp.cos(angle), jnp.cos(angle)], -1)
    sine = jnp.concatenate([jnp.sin(angle), jnp.sin(angle)], -1)
    return (cosine, sine)


def turn_half(values):
    half = values.shape[-1] // 2
    return jnp.concatenate([-values[..., half:], values[..., :half]], -1)


def rotate(values, cosine, sine):
    return values * cosine[:, None, :] + turn_half(values) * sine[:, None, :]


def rotate_back(grads, cosine, sine):
    return grads * cosine[:, None, :] - turn_half(grads * sine[:, None, :])


def segment_of(slots, starts):
    return (slots >= starts[1]).astype(jnp.int32) + (slots >= starts[2]).astype(jnp.int32)


def contract_rows(left, right):
    return lax.dot_general(
        left, right, (((0,), (0,)), ((), ())), preferred_element_type=jnp.float32
    )


def contract_columns(left, right):
    return lax.dot_general(
        left, right, (((1,), (1,)), ((), ())), preferred_element_type=jnp.float32
    )


def plain_device(
    tokens, cotangent, lengths, balance, norm1_gain, w_query, b_query, w_key, b_key,
    w_value, b_value, w_out, norm2_gain, w_gate, w_up, w_down,
):
    seq_count = lax.axis_size("seq")
    fsdp_count = lax.axis_size("fsdp")
    seq_rank = lax.axis_index("seq")
    rows_here, width = tokens.shape
    group = seq_count * rows_here
    kv_width = KV_HEADS * HEAD_DIM
    qkv_width = width + 2 * kv_width
    hidden_width = w_gate.shape[1]
    unit = hidden_width // (fsdp_count * seq_count)
    own_units = hidden_width // seq_count
    weight_rows = w_gate.shape[0]
    score_scale = HEAD_DIM ** (-0.5)
    repeat = HEADS // KV_HEADS

    slot = balance % group
    slots_all = lax.all_gather(slot, "seq", axis=0, tiled=True)
    seq_lengths = lengths[0]
    starts = jnp.cumsum(seq_lengths) - seq_lengths
    segment = segment_of(slot, starts)
    segments_all = segment_of(slots_all, starts)
    first_row = jnp.where(segment == 0, starts[0], jnp.where(segment == 1, starts[1], starts[2]))
    cosine, sine = rope_tables(slot - first_row)
    allowed = (segment[:, None] == segments_all[None, :]) & (slots_all[None, :] <= slot[:, None])

    small = jnp.concatenate([norm1_gain, norm2_gain, b_query, b_key, b_value], 0)[None]
    small = lax.all_gather(small, "fsdp", axis=0, tiled=True)
    piece = norm1_gain.shape[0]
    bias_piece = b_key.shape[0]
    gain_one = small[:, :piece].reshape(-1).astype(jnp.float32)
    gain_two = small[:, piece : 2 * piece].reshape(-1).astype(jnp.float32)
    bias_qkv = jnp.concatenate(
        [
            small[:, 2 * piece : 3 * piece].reshape(-1),
            small[:, 3 * piece : 3 * piece + bias_piece].reshape(-1),
            small[:, 3 * piece + bias_piece :].reshape(-1),
        ],
        0,
    ).astype(jnp.float32)
    weight_qkv = lax.all_gather(
        jnp.concatenate([w_query, w_key, w_value], 1), "fsdp", axis=0, tiled=True
    )
    weight_out = lax.all_gather(w_out, "fsdp", axis=0, tiled=True)
    upstream_all = lax.all_gather(cotangent, "seq", axis=0, tiled=True)

    def own_columns(weight):
        cut = weight.reshape(weight_rows, fsdp_count, seq_count, unit)
        return lax.dynamic_index_in_dim(cut, seq_rank, 2, False).reshape(weight_rows, own_units)

    weight_gu = lax.all_gather(
        jnp.concatenate([own_columns(w_gate), own_columns(w_up)], 1), "fsdp", axis=0, tiled=True
    )
    weight_down = lax.all_gather(
        lax.dynamic_slice_in_dim(w_down, seq_rank * unit, unit, 0), "fsdp", axis=0, tiled=True
    )

    inputs = tokens.astype(jnp.float32)
    normed_one = norm_piece(inputs, gain_one).astype(jnp.bfloat16)
    projected = jnp.dot(normed_one, weight_qkv, preferred_element_type=jnp.float32) + bias_qkv
    query_pre = projected[:, :width].reshape(rows_here, HEADS, HEAD_DIM)
    key_pre = projected[:, width : width + kv_width].reshape(rows_here, KV_HEADS, HEAD_DIM)
    value_pre = projected[:, width + kv_width :]
    queries = rotate(query_pre, cosine, sine).astype(jnp.bfloat16)
    keys = rotate(key_pre, cosine, sine).astype(jnp.bfloat16).reshape(rows_here, kv_width)
    values = value_pre.astype(jnp.bfloat16)
    paired = lax.all_gather(jnp.concatenate([keys, values], 1), "seq", axis=0, tiled=True)
    keys_all = paired[:, :kv_width].reshape(group, KV_HEADS, HEAD_DIM)
    values_all = paired[:, kv_width:].reshape(group, KV_HEADS, HEAD_DIM)
    grouped = queries.reshape(rows_here, KV_HEADS, repeat, HEAD_DIM)
    raw = (
        jnp.einsum("qgrd,kgd->grqk", grouped, keys_all, preferred_element_type=jnp.float32)
        * score_scale
    )
    scores = jnp.where(allowed, raw, -jnp.inf)
    expo = jnp.exp(scores - jnp.max(scores, -1, keepdims=True))
    probs = expo / jnp.sum(expo, -1, keepdims=True)
    probs_low = probs.astype(jnp.bfloat16)
    attended = jnp.einsum(
        "grqk,kgd->qgrd", probs_low, values_all, preferred_element_type=jnp.float32
    )
    attended = attended.astype(jnp.bfloat16).reshape(rows_here, width)
    resid = inputs + jnp.dot(attended, weight_out, preferred_element_type=jnp.float32)
    normed_two = norm_piece(resid, gain_two).astype(jnp.bfloat16)

    normed_all = lax.all_gather(normed_two, "seq", axis=0, tiled=True)
    both = jnp.dot(normed_all, weight_gu, preferred_element_type=jnp.float32)
    gate = both[:, :own_units]
    up = both[:, own_units:]
    sigma = jax.nn.sigmoid(gate)
    activated = gate * sigma
    hidden = (activated * up).astype(jnp.bfloat16)
    d_hidden = contract_columns(upstream_all, weight_down)
    d_gate = (d_hidden * up * sigma * (1.0 + gate * (1.0 - sigma))).astype(jnp.bfloat16)
    d_up = (d_hidden * activated).astype(jnp.bfloat16)
    d_both = jnp.concatenate([d_gate, d_up], 1)
    columns = lax.psum_scatter(
        contract_columns(d_both, weight_gu).astype(jnp.bfloat16),
        "seq", scatter_dimension=0, tiled=True,
    ).astype(jnp.float32)
    branch = lax.psum_scatter(
        jnp.dot(hidden, weight_down, preferred_element_type=jnp.float32).astype(jnp.bfloat16),
        "seq", scatter_dimension=0, tiled=True,
    ).astype(jnp.float32)
    layer_out = (resid + branch).astype(jnp.bfloat16)
    grad_down = lax.psum_scatter(
        contract_rows(hidden, upstream_all).astype(jnp.bfloat16),
        "fsdp", scatter_dimension=0, tiled=True,
    ).astype(jnp.float32)
    grad_pair = lax.psum_scatter(
        contract_rows(normed_all, d_both).astype(jnp.bfloat16),
        "fsdp", scatter_dimension=0, tiled=True,
    )
    grad_pair = lax.all_to_all(grad_pair, "seq", split_axis=0, concat_axis=0, tiled=True)
    grad_pair = grad_pair.reshape(seq_count, weight_rows // seq_count, 2, fsdp_count, unit)
    grad_pair = grad_pair.transpose(2, 1, 3, 0, 4).astype(jnp.float32)
    grad_pair = grad_pair.reshape(2, weight_rows // seq_count, hidden_width)

    _, pull_two = jax.vjp(norm_piece, resid, gain_two)
    d_resid_norm, grad_gain_two = pull_two(columns)
    d_resid = cotangent.astype(jnp.float32) + d_resid_norm
    d_branch = d_resid.astype(jnp.bfloat16)
    grad_out = contract_rows(attended, d_branch).astype(jnp.bfloat16)
    d_attended = contract_columns(d_branch, weight_out).astype(jnp.bfloat16)
    d_attended = d_attended.reshape(rows_here, KV_HEADS, repeat, HEAD_DIM)
    d_probs = jnp.einsum(
        "qgrd,kgd->grqk", d_attended, values_all, preferred_element_type=jnp.float32
    )
    delta = jnp.sum(probs * d_probs, -1, keepdims=True)
    d_score = (probs * (d_probs - delta)).astype(jnp.bfloat16)
    d_queries = (
        jnp.einsum("grqk,kgd->qgrd", d_score, keys_all, preferred_element_type=jnp.float32)
        * score_scale
    )
    d_keys = (
        jnp.einsum("grqk,qgrd->kgd", d_score, grouped, preferred_element_type=jnp.float32)
        * score_scale
    )
    d_values = jnp.einsum(
        "grqk,qgrd->kgd", probs_low, d_attended, preferred_element_type=jnp.float32
    )
    d_paired = jnp.concatenate([d_keys.reshape(group, kv_width), d_values.reshape(group, kv_width)], 1)
    d_paired = lax.psum_scatter(
        d_paired.astype(jnp.bfloat16), "seq", scatter_dimension=0, tiled=True
    ).astype(jnp.float32)
    d_query_pre = rotate_back(
        d_queries.reshape(rows_here, HEADS, HEAD_DIM), cosine, sine
    ).astype(jnp.bfloat16)
    d_key_pre = rotate_back(
        d_paired[:, :kv_width].reshape(rows_here, KV_HEADS, HEAD_DIM), cosine, sine
    ).astype(jnp.bfloat16)
    d_value_pre = d_paired[:, kv_width:].astype(jnp.bfloat16)
    d_qkv = jnp.concatenate(
        [
            d_query_pre.reshape(rows_here, width),
            d_key_pre.reshape(rows_here, kv_width),
            d_value_pre,
        ],
        1,
    )
    grad_qkv = contract_rows(normed_one, d_qkv).astype(jnp.bfloat16)
    grad_bias = jnp.sum(d_qkv.astype(jnp.float32), 0)
    d_normed_one = contract_columns(d_qkv, weight_qkv)
    _, pull_one = jax.vjp(norm_piece, inputs, gain_one)
    d_input_norm, grad_gain_one = pull_one(d_normed_one)
    input_grad = (d_resid + d_input_norm).astype(jnp.bfloat16)

    def summed(value):
        value = lax.psum_scatter(value, "fsdp", scatter_dimension=0, tiled=True)
        return lax.psum_scatter(value, "seq", scatter_dimension=0, tiled=True).astype(jnp.float32)

    grad_out = summed(grad_out)
    grad_qkv = summed(grad_qkv)
    vectors = lax.psum(
        jnp.concatenate([grad_gain_one, grad_gain_two, grad_bias], 0), ("fsdp", "seq")
    )
    own = width // (fsdp_count * seq_count)
    first = (lax.axis_index("fsdp") * seq_count + seq_rank) * own

    def own_part(offset):
        return lax.dynamic_slice_in_dim(vectors, offset + first, own, 0)

    biases = 2 * width
    return (
        layer_out,
        input_grad,
        own_part(0),
        grad_qkv[:, :width],
        own_part(biases),
        grad_qkv[:, width : width + kv_width],
        vectors[biases + width : biases + width + kv_width],
        grad_qkv[:, width + kv_width :],
        vectors[biases + width + kv_width :],
        grad_out,
        own_part(width),
        grad_pair[0],
        grad_pair[1],
        grad_down,
    )


ORDER = (1, 3, 2, 0)


class SumChain:
    def __init__(self, partial, rows, z_one, z_two, z_three, there, index):
        self.rank = lax.axis_index("seq")
        s = self.rank

        def held(j):
            return partial.at[ORDER.index(j) * rows : (ORDER.index(j) + 1) * rows]

        self.held, self.arrived = held, (z_one, z_two, z_three)
        self.up = [
            there(held(1), z_one, index, seq=s + 1),
            there(held(2), z_two.at[0], index + 2, seq=s + 1),
            there(held(3), z_three.at[0], index + 4, seq=s + 1),
        ]
        self.down = [
            there(held(3), z_one, index + 1, seq=s - 1),
            there(held(2), z_two.at[1], index + 3, seq=s - 1),
            there(held(1), z_three.at[1], index + 5, seq=s - 1),
        ]

    def add(self, j, arrived):
        ref = self.held(j)
        total = ref[...].astype(jnp.float32) + arrived[...].astype(jnp.float32)
        ref[...] = total.astype(jnp.bfloat16)

    def one(self):
        pl.when(self.rank == 0)(self.up[0].start)
        pl.when(self.rank == 3)(self.down[0].start)

    def add_one(self):
        @pl.when(self.rank == 1)
        def _():
            self.up[0].wait_recv()
            self.add(2, self.arrived[0])

        @pl.when(self.rank == 2)
        def _():
            self.down[0].wait_recv()
            self.add(2, self.arrived[0])

    def two(self):
        pl.when(self.rank <= 1)(self.up[1].start)
        pl.when(self.rank >= 2)(self.down[1].start)

    def three(self):
        @pl.when((self.rank == 1) | (self.rank == 2))
        def _():
            self.up[1].wait_recv()
            self.add(3, self.arrived[1].at[0])
            self.down[1].wait_recv()
            self.add(1, self.arrived[1].at[1])

        pl.when(self.rank <= 2)(self.up[2].start)
        pl.when(self.rank >= 1)(self.down[2].start)

    def last(self, out):
        out[...] = self.held(0)[...].astype(jnp.float32)

        @pl.when(self.rank >= 1)
        def _():
            self.up[2].wait_recv()
            out[...] += self.arrived[2][0].astype(jnp.float32)

        @pl.when(self.rank <= 2)
        def _():
            self.down[2].wait_recv()
            out[...] += self.arrived[2][1].astype(jnp.float32)

    def one_sent(self):
        pl.when(self.rank == 0)(self.up[0].wait_send)
        pl.when(self.rank == 3)(self.down[0].wait_send)

    def sent(self):
        pl.when(self.rank <= 1)(self.up[1].wait_send)
        pl.when(self.rank >= 2)(self.down[1].wait_send)
        pl.when(self.rank <= 2)(self.up[2].wait_send)
        pl.when(self.rank >= 1)(self.down[2].wait_send)


class SumPlane:
    def __init__(self, buffer, block, plane, arrived, by_x, by_y, ended, there, index):
        half = buffer.shape[1] // 2
        low, high = pl.ds(0, half), pl.ds(half, half)

        def part(k):
            return buffer.at[pl.ds(pl.multiple_of(plane[k] * block, 16), block)]

        self.parts = own, to_x, to_y, to_both = [part(k) for k in (0, 2, 4, 6)]
        self.arrived, self.by_x, self.by_y, self.ended, self.half = arrived, by_x, by_y, ended, half
        self.core = [
            there(part(2 * i + 1), arrived.at[i], index + i, fsdp=plane[1]) for i in range(4)
        ]
        self.first = [
            there(to_both.at[:, low], by_x.at[1], index + 5, fsdp=plane[2]),
            there(to_both.at[:, high], by_y.at[1], index + 7, fsdp=plane[4]),
            there(to_x.at[:, low], by_x.at[0], index + 4, fsdp=plane[2]),
            there(to_y.at[:, high], by_y.at[0], index + 6, fsdp=plane[4]),
        ]
        self.second = [
            there(to_y.at[:, low], ended.at[0], index + 8, fsdp=plane[4]),
            there(to_x.at[:, high], ended.at[1], index + 9, fsdp=plane[2]),
        ]

    def start_core(self):
        for copy in self.core:
            copy.start()

    def start_first(self):
        for i in (3, 1, 2, 0):
            self.core[i].wait_recv()
            part = self.parts[i]
            total = part[...].astype(jnp.float32) + self.arrived[i].astype(jnp.float32)
            part[...] = total.astype(jnp.bfloat16)
        for copy in self.first:
            copy.start()

    def start_second(self):
        half = self.half
        _, to_x, to_y, _ = self.parts
        self.first[0].wait_recv()
        total = to_y[:, :half].astype(jnp.float32) + self.by_x[1].astype(jnp.float32)
        to_y[:, :half] = total.astype(jnp.bfloat16)
        self.second[0].start()
        self.first[1].wait_recv()
        total = to_x[:, half:].astype(jnp.float32) + self.by_y[1].astype(jnp.float32)
        to_x[:, half:] = total.astype(jnp.bfloat16)
        self.second[1].start()

    def finish(self):
        half = self.half
        own = self.parts[0]
        self.first[2].wait_recv()
        self.second[0].wait_recv()
        total = own[:, :half].astype(jnp.float32) + self.by_x[0].astype(jnp.float32)
        own[:, :half] = (total + self.ended[0].astype(jnp.float32)).astype(jnp.bfloat16)
        self.first[3].wait_recv()
        self.second[1].wait_recv()
        total = own[:, half:].astype(jnp.float32) + self.by_y[0].astype(jnp.float32)
        own[:, half:] = (total + self.ended[1].astype(jnp.float32)).astype(jnp.bfloat16)

    def sent(self):
        for copy in self.core + self.first + self.second:
            copy.wait_send()


def front_kernel(
    tokens, cotangent, small, slot_keys, slot_row, first_row, cosine, sine,
    w_query, w_key, w_value, w_out, w_gate, w_up, w_down,
    gu_all, down_all, upstream_all, normed_all, qkv_out, out_out,
    queries, paired_out, slots_out, logsum, attended, resid, normed_one, gain_one, gain_two,
    qkv, out_w, gate_v, up_v, gu_own, kv, small_all, slots_all, bias, normed_own,
    local, ssem, rsem, zsend, zrecv,
):
    f = lax.axis_index("fsdp")
    s = lax.axis_index("seq")
    rows, width = tokens.shape
    n_f, n_s = 8, slots_all.shape[0]
    block = w_query.shape[0]
    unit = w_down.shape[0]
    kv_width = KV_HEADS * HEAD_DIM
    qkv_width = width + 2 * kv_width
    scale = HEAD_DIM ** (-0.5)
    repeat = HEADS // KV_HEADS
    plane = [f ^ k for k in range(n_f)]

    entry = pltpu.get_barrier_semaphore()
    for k in range(1, n_f):
        pl.semaphore_signal(entry, inc=1, device_id={"fsdp": plane[k]}, device_id_type=MESH)
    for j in range(1, n_s):
        pl.semaphore_signal(
            entry, inc=1, device_id={"seq": lax.rem(s + j, n_s)}, device_id_type=MESH
        )

    def here(source, target, index):
        return pltpu.make_async_copy(source, target, local.at[index])

    def there(source, target, index, **device):
        return pltpu.make_async_remote_copy(
            src_ref=source, dst_ref=target, send_sem=ssem.at[index], recv_sem=rsem.at[index],
            device_id=device, device_id_type=MESH,
        )

    def own_rows(ref, owner, size, start=0, count=None):
        first = pl.multiple_of(owner * size + start, 16)
        return ref.at[pl.ds(first, size if count is None else count)]

    class Gather:
        def __init__(self, source, target, size, index):
            half = size // 2
            x, y, c = plane[2], plane[4], plane[1]
            self.own = here(source, own_rows(target, f, size), index // 8) if source is not None else None
            if source is None:
                source = own_rows(target, f, size)
            mine = own_rows(target, f, size)
            self.first = [
                there(source, mine, index, fsdp=x),
                there(source, mine, index + 1, fsdp=y),
                there(source, mine, index + 2, fsdp=c),
            ]
            from_x, from_y = own_rows(target, x, size), own_rows(target, y, size)
            part_x = own_rows(target, x, size, 0, half)
            part_y = own_rows(target, y, size, half, half)
            self.second = [
                there(part_x, part_x, index + 3, fsdp=y),
                there(part_y, part_y, index + 4, fsdp=x),
                there(from_x, from_x, index + 5, fsdp=c),
                there(from_y, from_y, index + 6, fsdp=c),
            ]
            diagonal = own_rows(target, plane[6], size)
            self.third = there(diagonal, diagonal, index + 7, fsdp=c)

        def start(self):
            if self.own is not None:
                self.own.start()
            for copy in self.first:
                copy.start()

        def forward(self):
            self.first[0].wait_recv()
            self.second[0].start()
            self.second[2].start()
            self.first[1].wait_recv()
            self.second[1].start()
            self.second[3].start()

        def last(self):
            self.second[0].wait_recv()
            self.second[1].wait_recv()
            self.third.start()

        def finish(self):
            if self.own is not None:
                self.own.wait()
            self.first[2].wait_recv()
            self.second[2].wait_recv()
            self.second[3].wait_recv()
            self.third.wait_recv()

        def sent(self):
            for copy in self.first + self.second + [self.third]:
                copy.wait_send()

    class Chain:
        def __init__(self, target, index):
            self.steps = []
            for step in range(1, n_s):
                up = own_rows(target, s - (step - 1), rows)
                down = own_rows(target, s + (step - 1), rows)
                i = index + 2 * (step - 1)
                self.steps.append((
                    pltpu.make_async_remote_copy(
                        src_ref=up, dst_ref=up, send_sem=zsend.at[i], recv_sem=zrecv.at[i],
                        device_id={"seq": s + 1}, device_id_type=MESH,
                    ),
                    pltpu.make_async_remote_copy(
                        src_ref=down, dst_ref=down, send_sem=zsend.at[i + 1], recv_sem=zrecv.at[i + 1],
                        device_id={"seq": s - 1}, device_id_type=MESH,
                    ),
                    (s >= step - 1) & (s < n_s - 1),
                    (s >= 1) & (s <= n_s - step),
                    s >= step,
                    s <= n_s - 1 - step,
                ))

        def send(self, step):
            up, down, can_up, can_down, _, _ = self.steps[step - 1]
            pl.when(can_up)(up.start)
            pl.when(can_down)(down.start)

        def receive(self, step):
            up, down, _, _, from_below, from_above = self.steps[step - 1]
            pl.when(from_below)(up.wait_recv)
            pl.when(from_above)(down.wait_recv)

        def sent(self):
            for up, down, can_up, can_down, _, _ in self.steps:
                pl.when(can_up)(up.wait_send)
                pl.when(can_down)(down.wait_send)

    pieces = [
        here(w_query, qkv.at[pl.ds(pl.multiple_of(f * block, 16), block), pl.ds(0, width)], 5),
        here(w_key, qkv.at[pl.ds(pl.multiple_of(f * block, 16), block), pl.ds(width, kv_width)], 6),
        here(w_value, qkv.at[pl.ds(pl.multiple_of(f * block, 16), block), pl.ds(width + kv_width, kv_width)], 7),
        here(cotangent, own_rows(upstream_all, s, rows), 8),
    ]
    load_gate = here(w_gate, gate_v, 9)
    load_up = here(w_up, up_v, 10)
    for copy in pieces:
        copy.start()
    load_gate.start()
    load_up.start()
    small_all[f] = small[...]
    slots_all[s] = slot_keys[...]

    gather_qkv = Gather(None, qkv, block, 0)
    gather_out = Gather(w_out, out_w, block, 8)
    gather_gu = Gather(gu_own, gu_all, block, 16)
    gather_down = Gather(w_down, down_all, unit, 24)
    chain_up = Chain(upstream_all, 0)
    chain_normed = Chain(normed_all, 6)
    send_small = [
        there(small, small_all.at[f], 32 + k, fsdp=plane[k]) for k in range(1, n_f)
    ]
    send_slots = [
        there(slot_keys, slots_all.at[s], 40 + j, seq=lax.rem(s + j, n_s)) for j in range(1, n_s)
    ]
    send_kv = [
        there(kv.at[s], kv.at[s], 44 + j, seq=lax.rem(s + j, n_s)) for j in range(1, n_s)
    ]
    for copy in pieces[:3]:
        copy.wait()
    pl.semaphore_wait(entry, n_f - 1 + n_s - 1)
    gather_qkv.start()
    for copy in send_small + send_slots:
        copy.start()
    pieces[3].wait()
    chain_up.send(1)

    load_gate.wait()
    load_up.wait()
    pick_units(gate_v, up_v, gu_own, w_gate.shape[1] // n_f, w_gate.shape[1] // (n_f * n_s), unit)

    for copy in send_small + send_slots:
        copy.wait_recv()
    third = 2 * block
    for i in range(n_f // 2):
        columns = slice(i * third, (i + 1) * third)
        gain_one[:, columns] = (
            small_all[2 * i, 0:1, :third].astype(jnp.float32)
            + small_all[2 * i + 1, 0:1, :third].astype(jnp.float32)
        )
        gain_two[:, columns] = (
            small_all[2 * i, 0:1, third : 2 * third].astype(jnp.float32)
            + small_all[2 * i + 1, 0:1, third : 2 * third].astype(jnp.float32)
        )
    bias_query = [
        small_all[2 * i, 0:1, 2 * third : 3 * third].astype(jnp.float32)
        + small_all[2 * i + 1, 0:1, 2 * third : 3 * third].astype(jnp.float32)
        for i in range(n_f // 2)
    ]
    bias_query = jnp.concatenate(bias_query, 1)
    bias_pair = sum(small_all[i, 0:1, 3 * third :].astype(jnp.float32) for i in range(n_f))

    inputs = tokens[...].astype(jnp.float32)
    root = lax.rsqrt(jnp.mean(inputs * inputs, -1, keepdims=True) + epsilon)
    normed_one[...] = (inputs * root * gain_one[...]).astype(jnp.bfloat16)
    for j in range(n_s):
        keys_slot = slots_all[j]
        keys_slot = jnp.concatenate([keys_slot] * (rows // 128), 1)
        ok = (keys_slot <= slot_row[0:1]) & (keys_slot >= first_row[0:1])
        bias[j * rows : (j + 1) * rows] = jnp.where(ok, 0.0, -1e30)

    gather_qkv.forward()
    gather_out.start()
    chain_up.receive(1)
    chain_up.send(2)
    gather_qkv.last()
    gather_qkv.finish()
    save_qkv = here(qkv, qkv_out, 11)
    save_qkv.start()

    def turned(value):
        return value * cosine[...] + pltpu.roll(value, HEAD_DIM // 2, 1) * sine[...]

    normed = normed_one[...]
    pair = jnp.dot(normed, qkv[:, width : width + kv_width], preferred_element_type=jnp.float32)
    pair = pair + bias_pair[:, :kv_width]
    for g in range(KV_HEADS):
        columns = slice(g * HEAD_DIM, (g + 1) * HEAD_DIM)
        kv[s, :, columns] = turned(pair[:, columns]).astype(jnp.bfloat16)
    pair = jnp.dot(normed, qkv[:, width + kv_width :], preferred_element_type=jnp.float32)
    kv[s, :, kv_width:] = (pair + bias_pair[:, kv_width:]).astype(jnp.bfloat16)
    for copy in send_kv:
        copy.start()
    for g in range(HEADS // 2):
        columns = slice(g * 2 * HEAD_DIM, (g + 1) * 2 * HEAD_DIM)
        pair = jnp.dot(normed, qkv[:, columns], preferred_element_type=jnp.float32)
        pair = pair + bias_query[:, columns]
        for h in range(2):
            part = turned(pair[:, h * HEAD_DIM : (h + 1) * HEAD_DIM]).astype(jnp.bfloat16)
            queries[:, (2 * g + h) * HEAD_DIM : (2 * g + h + 1) * HEAD_DIM] = part

    gather_out.forward()
    gather_gu.start()
    chain_up.receive(2)
    gather_out.last()
    for copy in send_kv:
        copy.wait_recv()
    chain_up.send(3)
    save_kv = here(kv, paired_out, 12)
    save_kv.start()
    slots_out[...] = slots_all[...]

    for g in range(KV_HEADS):
        keys = kv[:, :, g * HEAD_DIM : (g + 1) * HEAD_DIM].reshape(n_s * rows, HEAD_DIM)
        values = kv[:, :, kv_width + g * HEAD_DIM : kv_width + (g + 1) * HEAD_DIM]
        values = values.reshape(n_s * rows, HEAD_DIM)

        def head(i, carry, g=g, keys=keys, values=values):
            h = g * repeat + i
            columns = pl.ds(pl.multiple_of(h * HEAD_DIM, HEAD_DIM), HEAD_DIM)
            raw = lax.dot_general(
                keys, queries[:, columns], (((1,), (1,)), ((), ())),
                preferred_element_type=jnp.float32,
            )
            scores = raw * scale + bias[...]
            top = jnp.max(scores, 0, keepdims=True)
            expo = jnp.exp(scores - top)
            total = jnp.sum(expo, 0, keepdims=True)
            probs = (expo * (1.0 / total)).astype(jnp.bfloat16)
            mixed = lax.dot_general(
                values, probs, (((0,), (0,)), ((), ())), preferred_element_type=jnp.float32
            )
            attended[:, columns] = mixed.T.astype(jnp.bfloat16)
            logsum[pl.ds(pl.multiple_of(h * 8, 8), 8)] = jnp.broadcast_to(
                top + jnp.log(total), (8, rows)
            )
            return carry

        lax.fori_loop(0, repeat, head, 0)

    gather_out.finish()
    save_out = here(out_w, out_out, 13)
    save_out.start()
    mixed = attended[...]
    for g in range(width // 256):
        columns = slice(g * 256, (g + 1) * 256)
        part = jnp.dot(mixed, out_w[:, columns], preferred_element_type=jnp.float32)
        resid[:, columns] = tokens[:, columns].astype(jnp.float32) + part
    value = resid[...]
    root = lax.rsqrt(jnp.mean(value * value, -1, keepdims=True) + epsilon)
    normed_own[...] = (value * root * gain_two[...]).astype(jnp.bfloat16)
    place_normed = here(normed_own, own_rows(normed_all, s, rows), 14)
    place_normed.start()
    place_normed.wait()
    chain_normed.send(1)

    gather_gu.forward()
    gather_down.start()
    chain_normed.receive(1)
    chain_normed.send(2)
    gather_gu.last()
    chain_normed.receive(2)
    chain_normed.send(3)
    chain_up.receive(3)
    gather_down.forward()
    gather_gu.finish()
    gather_down.last()
    chain_normed.receive(3)
    gather_down.finish()
    save_qkv.wait()
    save_kv.wait()
    save_out.wait()
    for part in (gather_qkv, gather_out, gather_gu, gather_down, chain_up, chain_normed):
        part.sent()
    for copy in send_small + send_slots + send_kv:
        copy.wait_send()


def pick_units(gate, up, out, stride, unit, padded):
    rank = lax.axis_index("seq")
    pieces = gate.shape[1] // stride
    half = out.shape[1] // 2
    window, tile = 512, 128
    rows = lax.broadcasted_iota(jnp.int32, (window, tile), 0)
    columns = lax.broadcasted_iota(jnp.int32, (window, tile), 1)
    for first in range(0, 2 * half, tile):
        source = gate if first < half else up
        local = first % half
        total = jnp.zeros((out.shape[0], tile), jnp.float32)
        for f in range(pieces):
            low = max(local, f * padded)
            high = min(local + tile, f * padded + unit)
            if low >= high:
                continue
            begin = f * stride + rank * unit
            base = jnp.minimum(begin // 128, (source.shape[1] - window) // 128) * 128
            base = pl.multiple_of(base, 128)
            wanted = columns + (local - f * padded + begin - base)
            inside = (columns >= low - local) & (columns < high - local)
            chosen = jnp.where((rows == wanted) & inside, 1.0, 0.0).astype(jnp.bfloat16)
            total += jnp.dot(
                source[:, pl.ds(base, window)], chosen, preferred_element_type=jnp.float32
            )
        out[:, first : first + tile] = total.astype(jnp.bfloat16)


def front(tokens, cotangent, small, slot, first_row, cosine, sine, weights, w_down_own):
    rows, width = tokens.shape
    n_s = lax.axis_size("seq")
    w_query, w_key, w_value, w_out, w_gate, w_up = weights
    block = w_query.shape[0]
    unit = w_down_own.shape[0]
    kv_width = KV_HEADS * HEAD_DIM
    qkv_width = width + 2 * kv_width
    units = 8 * unit
    group = n_s * rows
    low, full = jnp.bfloat16, jnp.float32
    slot_f = slot.astype(full)
    slot_keys = jnp.broadcast_to(slot_f[:, None], (rows, 128))
    slot_row = jnp.broadcast_to(slot_f[None], (8, rows))
    first_f = jnp.broadcast_to(first_row.astype(full)[None], (8, rows))
    half = HEAD_DIM // 2
    sine = jnp.concatenate([-sine[:, :half], sine[:, half:]], 1)
    vmem = pl.BlockSpec(memory_space=pltpu.VMEM)
    hbm = pl.BlockSpec(memory_space=pl.ANY)
    shape = jax.ShapeDtypeStruct
    return pl.pallas_call(
        front_kernel,
        in_specs=[vmem, hbm] + [vmem] * 6 + [hbm] * 7,
        out_specs=[hbm] * 6 + [vmem, hbm] + [vmem] * 7,
        out_shape=[
            shape((8 * block, 2 * units), low),
            shape((units, width), low),
            shape((group, width), low),
            shape((group, width), low),
            shape((width, qkv_width), low),
            shape((width, width), low),
            shape((rows, width), low),
            shape((n_s, rows, 2 * kv_width), low),
            shape((n_s, rows, 128), full),
            shape((8 * HEADS, rows), full),
            shape((rows, width), low),
            shape((rows, width), full),
            shape((rows, width), low),
            shape((1, width), full),
            shape((1, width), full),
        ],
        scratch_shapes=[
            pltpu.VMEM((width, qkv_width), low),
            pltpu.VMEM((width, width), low),
            pltpu.VMEM(w_gate.shape, low),
            pltpu.VMEM(w_up.shape, low),
            pltpu.VMEM((block, 2 * units), low),
            pltpu.VMEM((n_s, rows, 2 * kv_width), low),
            pltpu.VMEM((8,) + small.shape, low),
            pltpu.VMEM((n_s, rows, 128), full),
            pltpu.VMEM((group, rows), full),
            pltpu.VMEM((rows, width), low),
            pltpu.SemaphoreType.DMA((16,)),
            pltpu.SemaphoreType.DMA((48,)),
            pltpu.SemaphoreType.DMA((48,)),
            pltpu.SemaphoreType.DMA((12,)),
            pltpu.SemaphoreType.DMA((12,)),
        ],
        compiler_params=pltpu.CompilerParams(
            collective_id=0, has_side_effects=True, vmem_limit_bytes=56 * 2**20
        ),
        name="front",
    )(
        tokens, cotangent, small, slot_keys, slot_row, first_f, cosine, sine,
        w_query, w_key, w_value, w_out, w_gate, w_up, w_down_own,
    )


def ffn_kernel(
    normed_all, upstream_all, w_gu, w_down,
    columns, grad_down, gu_sum, gu_far, branch, down_arrived, gu_arrived,
    normed, upstream, gu, down, hidden, d_both, partial, z_one, z_two, z_three,
    down_x, down_y, down_last, down_piece,
    load, ssem, rsem,
):
    f = lax.axis_index("fsdp")
    s = lax.axis_index("seq")
    n_s = len(ORDER)
    group, width = normed.shape
    rows = group // n_s
    half_rows = group // 2
    units = down.shape[0]
    tile = 256
    tiles = units // tile
    wide = 768
    block = gu.shape[0] // 8
    unit = units // 8
    half = width // 2
    plane = [f ^ k for k in range(8)]
    full = jnp.float32

    entry = pltpu.get_barrier_semaphore()
    for k in (1, 2, 4):
        pl.semaphore_signal(entry, inc=1, device_id={"fsdp": plane[k]}, device_id_type=MESH)
    for j in (1, n_s - 1):
        pl.semaphore_signal(
            entry, inc=1, device_id={"seq": lax.rem(s + j, n_s)}, device_id_type=MESH
        )

    def here(source, target, index):
        return pltpu.make_async_copy(source, target, load.at[index])

    def there(source, target, index, **device):
        return pltpu.make_async_remote_copy(
            src_ref=source, dst_ref=target, send_sem=ssem.at[index], recv_sem=rsem.at[index],
            device_id=device, device_id_type=MESH,
        )

    def part(ref, owner, size):
        return ref.at[pl.ds(pl.multiple_of(owner * size, 16), size)]

    first_loads = []
    for p, j in enumerate(ORDER):
        owner = lax.rem(s + n_s - j, n_s)
        first_loads.append(here(part(normed_all, owner, rows), part(normed, p, rows), p))
        first_loads.append(here(part(upstream_all, owner, rows), part(upstream, p, rows), 4 + p))

    def tile_loads(t):
        gate_columns = pl.ds(pl.multiple_of(t * wide, wide), wide)
        up_columns = pl.ds(pl.multiple_of(units + t * wide, wide), wide)
        return [
            here(w_gu.at[:, gate_columns], gu.at[:, gate_columns], 8 + 3 * t),
            here(w_gu.at[:, up_columns], gu.at[:, up_columns], 9 + 3 * t),
            here(w_down.at[gate_columns], down.at[gate_columns], 10 + 3 * t),
        ]

    for copy in first_loads:
        copy.start()
    for t in range(units // wide):
        for copy in tile_loads(t):
            copy.start()
    for copy in first_loads:
        copy.wait()

    def forward(part_rows, wait):
        def body(t, carry):
            if wait:
                for copy in tile_loads(t):
                    copy.wait()
            gate_columns = pl.ds(pl.multiple_of(t * wide, wide), wide)
            up_columns = pl.ds(pl.multiple_of(units + t * wide, wide), wide)
            mine = normed[part_rows]
            gate = jnp.dot(mine, gu[:, gate_columns], preferred_element_type=full)
            up = jnp.dot(mine, gu[:, up_columns], preferred_element_type=full)
            d_hidden = lax.dot_general(
                upstream[part_rows], down[gate_columns], (((1,), (1,)), ((), ())),
                preferred_element_type=full,
            )
            sigma = jax.nn.sigmoid(gate)
            activated = gate * sigma
            hidden[part_rows, gate_columns] = (activated * up).astype(jnp.bfloat16)
            d_both[part_rows, gate_columns] = (
                d_hidden * up * sigma * (1.0 + gate * (1.0 - sigma))
            ).astype(jnp.bfloat16)
            d_both[part_rows, up_columns] = (d_hidden * activated).astype(jnp.bfloat16)
            return carry

        lax.fori_loop(0, units // wide, body, 0)

    def backward(part_rows):
        def body(n, carry):
            out_columns = pl.ds(pl.multiple_of(n * 512, 512), 512)
            value = lax.dot_general(
                d_both[part_rows], gu[out_columns], (((1,), (1,)), ((), ())),
                preferred_element_type=full,
            )
            partial[part_rows, out_columns] = value.astype(jnp.bfloat16)
            return carry

        lax.fori_loop(0, width // 512, body, 0)

    chain = SumChain(partial, rows, z_one, z_two, z_three, there, 0)
    early, late = slice(0, half_rows), slice(half_rows, group)
    pieces = [(first, min(group, units - first)) for first in range(0, units, group)]
    forward(early, True)
    backward(early)
    pl.semaphore_wait(entry, 5)
    chain.one()
    forward(late, False)
    backward(late)
    chain.add_one()
    chain.two()

    def down_body(t, carry):
        unit_rows = pl.ds(pl.multiple_of(t * tile, tile), tile)
        value = lax.dot_general(
            hidden[:, unit_rows], upstream[...], (((0,), (0,)), ((), ())),
            preferred_element_type=full,
        )
        down[unit_rows] = value.astype(jnp.bfloat16)
        return carry

    lax.fori_loop(0, tiles, down_body, 0)
    down_core = [
        there(part(down, plane[2 * i + 1], unit), down_arrived.at[i], 6 + i, fsdp=plane[1])
        for i in range(4)
    ]
    for copy in down_core:
        copy.start()

    def gu_body(m, carry):
        in_columns = pl.ds(pl.multiple_of(m * tile, tile), tile)
        turned = normed[:, in_columns].T
        for first in range(0, 2 * units, units // 3):
            value = jnp.dot(turned, d_both[:, first : first + units // 3], preferred_element_type=full)
            gu[in_columns, first : first + units // 3] = value.astype(jnp.bfloat16)
        return carry

    lax.fori_loop(0, 2, gu_body, 0)

    def add_arrived(i, ref, size, arrived, pieces, copies, index):
        copies[i].wait_recv()
        fetch = [
            here(arrived.at[i, :, columns], piece, index + k)
            for k, (columns, piece) in enumerate(pieces)
        ]
        for copy in fetch:
            copy.start()
        target = part(ref, plane[2 * i], size)
        for copy, (columns, piece) in zip(fetch, pieces):
            copy.wait()
            target[:, columns] = (
                target[:, columns].astype(full) + piece[...].astype(full)
            ).astype(jnp.bfloat16)

    down_pieces = [(pl.ds(0, width), down_piece)]
    for i in (3, 1, 2, 0):
        add_arrived(i, down, unit, down_arrived, down_pieces, down_core, 14)
    to_x, to_y, to_both = [part(down, plane[k], unit) for k in (2, 4, 6)]
    low_half, high_half = pl.ds(0, half), pl.ds(half, half)
    down_first = [
        there(to_x.at[:, low_half], down_x.at[0], 10, fsdp=plane[2]),
        there(to_both.at[:, low_half], down_x.at[1], 11, fsdp=plane[2]),
        there(to_y.at[:, high_half], down_y.at[0], 12, fsdp=plane[4]),
        there(to_both.at[:, high_half], down_y.at[1], 13, fsdp=plane[4]),
    ]
    for copy in down_first:
        copy.start()
    chain.three()
    lax.fori_loop(2, width // tile, gu_body, 0)
    gu_core = [
        there(part(gu, plane[2 * i + 1], block), gu_arrived.at[i], 16 + i, fsdp=plane[1])
        for i in range(4)
    ]
    for copy in gu_core:
        copy.start()

    again = [
        here(
            w_down.at[first : first + count],
            d_both.at[:count, i * width : (i + 1) * width], 24 + i,
        )
        for i, (first, count) in enumerate(pieces)
    ]
    for copy in again:
        copy.start()
    for copy in again:
        copy.wait()

    def branch_body(n, carry):
        out_columns = pl.ds(pl.multiple_of(n * wide, wide), wide)
        for m in range(2):
            mine = slice(m * half_rows, (m + 1) * half_rows)
            value = jnp.zeros((half_rows, wide), full)
            for i, (first, count) in enumerate(pieces):
                columns_here = pl.ds(pl.multiple_of(i * width + n * wide, wide), wide)
                value += jnp.dot(
                    hidden[mine, first : first + count], d_both[:count, columns_here],
                    preferred_element_type=full,
                )
            upstream[mine, out_columns] = value.astype(jnp.bfloat16)
        return carry

    lax.fori_loop(0, width // wide, branch_body, 0)
    chain.last(columns)
    chain_branch = SumChain(upstream, rows, z_one, z_two, z_three, there, 22)
    chain_branch.one()
    down_second = [
        there(to_y.at[:, low_half], down_last.at[0], 14, fsdp=plane[4]),
        there(to_x.at[:, high_half], down_last.at[1], 15, fsdp=plane[2]),
    ]
    down_first[1].wait_recv()
    to_y[:, :half] = (to_y[:, :half].astype(full) + down_x[1].astype(full)).astype(jnp.bfloat16)
    down_second[0].start()
    down_first[3].wait_recv()
    to_x[:, half:] = (to_x[:, half:].astype(full) + down_y[1].astype(full)).astype(jnp.bfloat16)
    down_second[1].start()
    gu_pieces = [
        (pl.ds(0, units), hidden.at[:block]),
        (pl.ds(units, units), hidden.at[block : 2 * block]),
    ]
    add_arrived(3, gu, block, gu_arrived, gu_pieces, gu_core, 20)
    far = part(gu, plane[6], block)
    gu_first = [
        there(far.at[:, pl.ds(0, units)], gu_far.at[0], 20, fsdp=plane[2]),
        there(far.at[:, pl.ds(units, units)], gu_far.at[1], 21, fsdp=plane[4]),
    ]
    for copy in gu_first:
        copy.start()
    for i in (1, 2, 0):
        add_arrived(i, gu, block, gu_arrived, gu_pieces, gu_core, 20)
    store = [here(part(gu, plane[2 * i], block), gu_sum.at[i], 16 + i) for i in range(3)]
    for copy in store:
        copy.start()
    down_first[0].wait_recv()
    down_first[2].wait_recv()
    own = part(down, f, unit)
    down_second[0].wait_recv()
    grad_down[:, :half] = (
        own[:, :half].astype(full) + down_x[0].astype(full) + down_last[0].astype(full)
    )
    down_second[1].wait_recv()
    grad_down[:, half:] = (
        own[:, half:].astype(full) + down_y[0].astype(full) + down_last[1].astype(full)
    )
    chain_branch.add_one()
    chain_branch.one_sent()
    store_branch = here(upstream, branch, 27)
    store_branch.start()
    chain.one_sent()
    chain.sent()
    for copy in down_core + down_first + down_second + gu_core + gu_first:
        copy.wait_send()
    for copy in gu_first:
        copy.wait_recv()
    for copy in store + [store_branch]:
        copy.wait()


def ffn(normed_all, upstream_all, w_gu, w_down):
    group, width = normed_all.shape
    units = w_down.shape[0]
    rows = group // len(ORDER)
    unit, block, half = units // 8, width // 8, width // 2
    low, full = jnp.bfloat16, jnp.float32
    vmem = pl.BlockSpec(memory_space=pltpu.VMEM)
    hbm = pl.BlockSpec(memory_space=pl.ANY)
    shape = jax.ShapeDtypeStruct
    return pl.pallas_call(
        ffn_kernel,
        in_specs=[hbm] * 4,
        out_specs=[vmem] * 2 + [hbm] * 5,
        out_shape=[
            shape((rows, width), full),
            shape((unit, width), full),
            shape((3, block, 2 * units), low),
            shape((2, block, units), low),
            shape((group, width), low),
            shape((4, unit, width), low),
            shape((4, block, 2 * units), low),
        ],
        scratch_shapes=[
            pltpu.VMEM((group, width), low),
            pltpu.VMEM((group, width), low),
            pltpu.VMEM((width, 2 * units), low),
            pltpu.VMEM((units, width), low),
            pltpu.VMEM((group, units), low),
            pltpu.VMEM((group, 2 * units), low),
            pltpu.VMEM((group, width), low),
            pltpu.VMEM((rows, width), low),
            pltpu.VMEM((2, rows, width), low),
            pltpu.VMEM((2, rows, width), low),
            pltpu.VMEM((2, unit, half), low),
            pltpu.VMEM((2, unit, half), low),
            pltpu.VMEM((2, unit, half), low),
            pltpu.VMEM((unit, width), low),
            pltpu.SemaphoreType.DMA((36,)),
            pltpu.SemaphoreType.DMA((28,)),
            pltpu.SemaphoreType.DMA((28,)),
        ],
        compiler_params=pltpu.CompilerParams(
            collective_id=1, has_side_effects=True, vmem_limit_bytes=63 * 2**20
        ),
        name="ffn",
    )(normed_all, upstream_all, w_gu, w_down)[:5]


def back_kernel(
    columns, resid, gain_two, cotangent, attended, queries, paired, slots, slot_row, first_row,
    logsum, normed_one, tokens, gain_one, cosine, sine, w_out, w_qkv, gu_sum, gu_far, branch,
    layer, input_rows, vector, grad_out, grad_qkv, gu_rows,
    out_w, qkv, gu_own, gu_to_y, gu_to_x, gu_x, gu_y, gu_ended,
    branch_v, z_one, z_two, z_three, working, bias, d_branch, d_attended, d_qkv, d_resid,
    keys_grad, values_grad, dkv, dkv_in,
    out_arrived, out_x, out_y, out_ended, qkv_arrived, qkv_x, qkv_y, qkv_ended,
    out_in, qkv_in, vector_in,
    load, ssem, rsem,
):
    f = lax.axis_index("fsdp")
    s = lax.axis_index("seq")
    rows, width = tokens.shape
    n_s = paired.shape[0]
    kv_width = KV_HEADS * HEAD_DIM
    repeat = HEADS // KV_HEADS
    scale = HEAD_DIM ** (-0.5)
    block = width // 8
    piece = block // n_s
    units = gu_sum.shape[2] // 2
    tile = 256
    full, low = jnp.float32, jnp.bfloat16
    plane = [f ^ k for k in range(8)]

    entry = pltpu.get_barrier_semaphore()
    for k in (1, 2, 4):
        pl.semaphore_signal(entry, inc=1, device_id={"fsdp": plane[k]}, device_id_type=MESH)
    for j in range(1, n_s):
        pl.semaphore_signal(
            entry, inc=1, device_id={"seq": lax.rem(s + j, n_s)}, device_id_type=MESH
        )

    def here(source, target, index):
        return pltpu.make_async_copy(source, target, load.at[index])

    def there(source, target, index, **device):
        return pltpu.make_async_remote_copy(
            src_ref=source, dst_ref=target, send_sem=ssem.at[index], recv_sem=rsem.at[index],
            device_id=device, device_id_type=MESH,
        )

    low_units, high_units = pl.ds(0, units), pl.ds(units, units)
    load_branch = here(branch, branch_v, 0)
    load_out = here(w_out, out_w, 1)
    load_gu = [
        here(gu_sum.at[0], gu_own, 2),
        here(gu_sum.at[2, :, low_units], gu_to_y, 3),
        here(gu_sum.at[1, :, high_units], gu_to_x, 4),
        here(gu_far.at[0], gu_x.at[1], 8),
        here(gu_far.at[1], gu_y.at[1], 9),
    ]
    load_qkv = here(w_qkv, qkv, 5)
    load_columns = here(columns, working, 7)
    for copy in [load_columns, load_branch, load_out] + load_gu + [load_qkv]:
        copy.start()

    gu_first = [
        there(gu_sum.at[1, :, low_units], gu_x.at[0], 2, fsdp=plane[2]),
        there(gu_sum.at[2, :, high_units], gu_y.at[0], 3, fsdp=plane[4]),
    ]
    gu_second = [
        there(gu_to_y, gu_ended.at[0], 4, fsdp=plane[4]),
        there(gu_to_x, gu_ended.at[1], 5, fsdp=plane[2]),
    ]

    def around(j):
        return {"seq": lax.rem(s + j, n_s)}

    def rows_for(ref, first, j):
        owner = lax.rem(s + j, n_s)
        return ref.at[pl.ds(pl.multiple_of(first + owner * piece, 16), piece)]

    gu_send = [there(rows_for(gu_own, 0, j), gu_rows.at[j], 5 + j, **around(j)) for j in range(1, n_s)]
    dkv_send = [
        [
            there(dkv.at[g, lax.rem(s + j, n_s)], dkv_in.at[g, j], 8 + 3 * g + j, **around(j))
            for j in range(1, n_s)
        ]
        for g in range(KV_HEADS)
    ]
    chain = SumChain(branch_v, rows, z_one, z_two, z_three, there, 16)
    sum_out = SumPlane(out_w, block, plane, out_arrived, out_x, out_y, out_ended, there, 24)
    sum_qkv = SumPlane(qkv, block, plane, qkv_arrived, qkv_x, qkv_y, qkv_ended, there, 36)
    out_send = [there(rows_for(out_w, f * block, j), out_in.at[j], 47 + j, **around(j)) for j in range(1, n_s)]
    qkv_send = [there(rows_for(qkv, f * block, j), qkv_in.at[j], 51 + j, **around(j)) for j in range(1, n_s)]
    vector_send = [
        there(vector_in.at[0], vector_in.at[1], 56, fsdp=plane[1]),
        there(vector_in.at[2], vector_in.at[3], 57, fsdp=plane[2]),
        there(vector_in.at[4], vector_in.at[5], 58, fsdp=plane[4]),
    ] + [there(vector_in.at[6], vector_in.at[6 + j], 58 + j, **around(j)) for j in range(1, n_s)]

    pl.semaphore_wait(entry, 3 + n_s - 1)
    for copy in gu_first:
        copy.start()
    load_branch.wait()
    chain.two()
    for copy in load_gu:
        copy.wait()
    gu_to_y[...] = (gu_to_y[...].astype(full) + gu_x[1].astype(full)).astype(low)
    gu_second[0].start()
    gu_to_x[...] = (gu_to_x[...].astype(full) + gu_y[1].astype(full)).astype(low)
    gu_second[1].start()

    def norm_back(value, gain, grad):
        root = lax.rsqrt(jnp.mean(value * value, -1, keepdims=True) + epsilon)
        scaled = gain * grad
        inner = jnp.mean(scaled * value, -1, keepdims=True)
        gain_grad = jnp.sum(grad * (value * root), 0, keepdims=True)
        return root * scaled - value * (root * root * root * inner), gain_grad

    load_columns.wait()
    d_norm, gain_two_grad = norm_back(resid[...], gain_two[...], working[...])
    d_total = cotangent[...].astype(full) + d_norm
    d_branch[...] = d_total.astype(low)
    d_resid[...] = d_total
    for j in range(n_s):
        keys_slot = slots[j]
        keys_slot = jnp.concatenate([keys_slot] * (rows // 128), 1)
        ok = (keys_slot <= slot_row[0:1]) & (keys_slot >= first_row[0:1])
        bias[j * rows : (j + 1) * rows] = jnp.where(ok, 0.0, -1e30)
    load_out.wait()
    for n in range(width // tile):
        value = lax.dot_general(
            d_branch[...], out_w[n * tile : (n + 1) * tile], (((1,), (1,)), ((), ())),
            preferred_element_type=full,
        )
        d_attended[:, n * tile : (n + 1) * tile] = value.astype(low)

    def turned_back(value):
        return value * cosine[...] + pltpu.roll(value * sine[...], HEAD_DIM // 2, 1)

    for g in range(KV_HEADS):
        keys = paired[:, :, g * HEAD_DIM : (g + 1) * HEAD_DIM].reshape(n_s * rows, HEAD_DIM)
        values = paired[:, :, kv_width + g * HEAD_DIM : kv_width + (g + 1) * HEAD_DIM]
        values = values.reshape(n_s * rows, HEAD_DIM)
        keys_grad[...] = jnp.zeros_like(keys_grad)
        values_grad[...] = jnp.zeros_like(values_grad)

        def head(i, carry, g=g, keys=keys, values=values):
            h = g * repeat + i
            head_columns = pl.ds(pl.multiple_of(h * HEAD_DIM, HEAD_DIM), HEAD_DIM)
            query = queries[:, head_columns]
            grad = d_attended[:, head_columns]
            raw = lax.dot_general(
                keys, query, (((1,), (1,)), ((), ())), preferred_element_type=full
            )
            logs = logsum[pl.ds(pl.multiple_of(h * 8, 8), 8)][0:1]
            probs = jnp.exp(raw * scale + bias[...] - logs)
            d_probs = lax.dot_general(
                values, grad, (((1,), (1,)), ((), ())), preferred_element_type=full
            )
            delta = jnp.sum(probs * d_probs, 0, keepdims=True)
            d_score = (probs * (d_probs - delta)).astype(low)
            turned = lax.dot_general(
                keys, d_score, (((0,), (0,)), ((), ())), preferred_element_type=full
            )
            d_qkv[:, head_columns] = turned_back((turned * scale).T).astype(low)
            keys_grad[...] += jnp.dot(d_score, query, preferred_element_type=full) * scale
            values_grad[...] += jnp.dot(probs.astype(low), grad, preferred_element_type=full)
            return carry

        lax.fori_loop(0, repeat, head, 0)
        dkv[g, :, :, :HEAD_DIM] = keys_grad[...].astype(low).reshape(n_s, rows, HEAD_DIM)
        dkv[g, :, :, HEAD_DIM:] = values_grad[...].astype(low).reshape(n_s, rows, HEAD_DIM)
        for copy in dkv_send[g]:
            copy.start()

    turned = attended[...].T
    for n in range(width // tile):
        n_columns = slice(n * tile, (n + 1) * tile)
        value = jnp.dot(turned, d_branch[:, n_columns], preferred_element_type=full)
        out_w[:, n_columns] = value.astype(low)
    sum_out.start_core()
    load_qkv.wait()

    def back_one(first, count, start):
        for n in range(width // tile):
            n_rows = slice(n * tile, (n + 1) * tile)
            value = lax.dot_general(
                d_qkv[:, first : first + count], qkv[n_rows, first : first + count],
                (((1,), (1,)), ((), ())), preferred_element_type=full,
            )
            working[:, n_rows] = value if start else working[:, n_rows] + value

    back_one(0, width, True)
    normed_turned = normed_one[...].T
    for n in range(width // tile):
        n_columns = slice(n * tile, (n + 1) * tile)
        value = jnp.dot(normed_turned, d_qkv[:, n_columns], preferred_element_type=full)
        qkv[:, n_columns] = value.astype(low)
    sum_out.start_first()

    for g in range(KV_HEADS):
        for copy in dkv_send[g]:
            copy.wait_recv()
        total = dkv[g, s].astype(full)
        for j in range(1, n_s):
            total = total + dkv_in[g, j].astype(full)
        key_columns = slice(width + g * HEAD_DIM, width + (g + 1) * HEAD_DIM)
        value_columns = slice(width + kv_width + g * HEAD_DIM, width + kv_width + (g + 1) * HEAD_DIM)
        d_qkv[:, key_columns] = turned_back(total[:, :HEAD_DIM]).astype(low)
        d_qkv[:, value_columns] = total[:, HEAD_DIM:].astype(low)
    back_one(width, 2 * kv_width, False)
    value = jnp.dot(normed_turned, d_qkv[:, width:], preferred_element_type=full)
    qkv[:, width:] = value.astype(low)
    sum_qkv.start_core()
    chain.three()

    d_norm, gain_one_grad = norm_back(tokens[...].astype(full), gain_one[...], working[...])
    input_rows[...] = (d_resid[...] + d_norm).astype(low)
    bias_grad = jnp.sum(d_qkv[...].astype(full), 0, keepdims=True)
    vectors = jnp.concatenate([gain_one_grad, gain_two_grad, bias_grad], 1)
    part = vectors.shape[1] // 8
    for r in range(8):
        vector_in[0, r : r + 1] = vectors[:, r * part : (r + 1) * part]
    vector_send[0].start()
    sum_qkv.start_first()
    vector_send[0].wait_recv()
    vector_in[2] = vector_in[0] + vector_in[1]
    vector_send[1].start()

    gu_first[0].wait_recv()
    gu_second[0].wait_recv()
    total = gu_own[:, :units].astype(full) + gu_x[0].astype(full) + gu_ended[0].astype(full)
    gu_own[:, :units] = total.astype(low)
    gu_first[1].wait_recv()
    gu_second[1].wait_recv()
    total = gu_own[:, units:].astype(full) + gu_y[0].astype(full) + gu_ended[1].astype(full)
    gu_own[:, units:] = total.astype(low)
    for copy in gu_send:
        copy.start()
    keep_rows = here(rows_for(gu_own, 0, 0), gu_rows.at[0], 6)
    keep_rows.start()
    sum_out.start_second()
    vector_send[1].wait_recv()
    vector_in[4] = vector_in[2] + vector_in[3]
    vector_send[2].start()

    sum_qkv.start_second()
    sum_out.finish()
    for copy in out_send:
        copy.start()
    vector_send[2].wait_recv()
    vector_in[6] = vector_in[4] + vector_in[5]
    for copy in vector_send[3:]:
        copy.start()
    chain.last(working)
    layer[...] = (resid[...] + working[...]).astype(low)
    sum_qkv.finish()
    for copy in qkv_send:
        copy.start()

    def gathered(own, copies, arrived, out):
        total = own[...].astype(full)
        for copy in copies:
            copy.wait_recv()
        for j in range(1, n_s):
            total = total + arrived[j].astype(full)
        out[...] = total

    gathered(rows_for(out_w, f * block, 0), out_send, out_in, grad_out)
    for copy in vector_send[3:]:
        copy.wait_recv()
    vector[...] = vector_in[6] + vector_in[7] + vector_in[8] + vector_in[9]
    gathered(rows_for(qkv, f * block, 0), qkv_send, qkv_in, grad_qkv)
    for copy in gu_send:
        copy.wait_recv()
    keep_rows.wait()
    chain.sent()
    sum_out.sent()
    sum_qkv.sent()
    for copy in gu_first + gu_second + gu_send + out_send + qkv_send + vector_send:
        copy.wait_send()
    for g in range(KV_HEADS):
        for copy in dkv_send[g]:
            copy.wait_send()


def back(
    columns, resid, gain_two, cotangent, attended, queries, paired, slots, slot, first_row,
    logsum, normed_one, tokens, gain_one, cosine, sine, w_out, w_qkv, gu_sum, gu_far, branch,
):
    rows, width = tokens.shape
    n_s = paired.shape[0]
    group = n_s * rows
    kv_width = KV_HEADS * HEAD_DIM
    qkv_width = width + 2 * kv_width
    block = width // 8
    piece = block // n_s
    units = gu_sum.shape[2] // 2
    low, full = jnp.bfloat16, jnp.float32
    slot_row = jnp.broadcast_to(slot.astype(full)[None], (8, rows))
    first_f = jnp.broadcast_to(first_row.astype(full)[None], (8, rows))
    half = HEAD_DIM // 2
    sine = jnp.concatenate([-sine[:, :half], sine[:, half:]], 1)
    vmem = pl.BlockSpec(memory_space=pltpu.VMEM)
    hbm = pl.BlockSpec(memory_space=pl.ANY)
    shape = jax.ShapeDtypeStruct
    vectors = (2 * width + qkv_width) // 8
    return pl.pallas_call(
        back_kernel,
        in_specs=[hbm] + [vmem] * 15 + [hbm] * 5,
        out_specs=[vmem] * 5 + [hbm],
        out_shape=[
            shape((rows, width), low),
            shape((rows, width), low),
            shape((8, vectors), full),
            shape((piece, width), full),
            shape((piece, qkv_width), full),
            shape((n_s, piece, 2 * units), low),
        ],
        scratch_shapes=[
            pltpu.VMEM((width, width), low),
            pltpu.VMEM((width, qkv_width), low),
            pltpu.VMEM((block, 2 * units), low),
            pltpu.VMEM((block, units), low),
            pltpu.VMEM((block, units), low),
            pltpu.VMEM((2, block, units), low),
            pltpu.VMEM((2, block, units), low),
            pltpu.VMEM((2, block, units), low),
            pltpu.VMEM((group, width), low),
            pltpu.VMEM((rows, width), low),
            pltpu.VMEM((2, rows, width), low),
            pltpu.VMEM((2, rows, width), low),
            pltpu.VMEM((rows, width), full),
            pltpu.VMEM((group, rows), full),
            pltpu.VMEM((rows, width), low),
            pltpu.VMEM((rows, width), low),
            pltpu.VMEM((rows, qkv_width), low),
            pltpu.VMEM((rows, width), full),
            pltpu.VMEM((group, HEAD_DIM), full),
            pltpu.VMEM((group, HEAD_DIM), full),
            pltpu.VMEM((KV_HEADS, n_s, rows, 2 * HEAD_DIM), low),
            pltpu.VMEM((KV_HEADS, n_s, rows, 2 * HEAD_DIM), low),
            pltpu.VMEM((4, block, width), low),
            pltpu.VMEM((2, block, width // 2), low),
            pltpu.VMEM((2, block, width // 2), low),
            pltpu.VMEM((2, block, width // 2), low),
            pltpu.VMEM((4, block, qkv_width), low),
            pltpu.VMEM((2, block, qkv_width // 2), low),
            pltpu.VMEM((2, block, qkv_width // 2), low),
            pltpu.VMEM((2, block, qkv_width // 2), low),
            pltpu.VMEM((n_s, piece, width), low),
            pltpu.VMEM((n_s, piece, qkv_width), low),
            pltpu.VMEM((10, 8, vectors), full),
            pltpu.SemaphoreType.DMA((10,)),
            pltpu.SemaphoreType.DMA((64,)),
            pltpu.SemaphoreType.DMA((64,)),
        ],
        compiler_params=pltpu.CompilerParams(
            collective_id=2, has_side_effects=True, vmem_limit_bytes=63 * 2**20
        ),
        name="back",
    )(
        columns, resid, gain_two, cotangent, attended, queries, paired, slots, slot_row, first_f,
        logsum, normed_one, tokens, gain_one, cosine, sine, w_out, w_qkv, gu_sum, gu_far, branch,
    )


def finish_kernel(
    layer, input_rows, grad_out, grad_qkv, grad_down, gu_rows,
    layer_out, input_grad, out_out, query_out, key_out, value_out, down_out, gate_out, up_out,
):
    s = lax.axis_index("seq")
    n_s = gu_rows.shape[0]
    width = grad_out.shape[1]
    kv_width = KV_HEADS * HEAD_DIM
    unit_pad = grad_down.shape[0]
    unit = down_out.shape[0]
    units = gu_rows.shape[2] // 2
    layer_out[...] = layer[...]
    input_grad[...] = input_rows[...]
    out_out[...] = grad_out[...]
    query_out[...] = grad_qkv[:, :width]
    key_out[...] = grad_qkv[:, width : width + kv_width]
    value_out[...] = grad_qkv[:, width + kv_width :]
    down_out[...] = grad_down[:unit]
    window = 512
    lanes = lax.broadcasted_iota(jnp.int32, (gu_rows.shape[1], 128), 1)
    for base, out in ((0, gate_out), (units, up_out)):
        for f in range(units // unit_pad):
            for owner in range(n_s):
                source = base + f * unit_pad
                begin = min(source // 128 * 128, 2 * units - window)
                target = (f * n_s + owner) * unit
                first = target // 128 * 128
                slot = lax.rem(s + n_s - owner, n_s)
                value = gu_rows[slot, :, begin : begin + window].astype(jnp.float32)
                turn = ((target - first) - (source - begin)) % window
                if turn:
                    value = pltpu.roll(value, turn, 1)
                for t in range(first, min(target + unit, out.shape[1]), 128):
                    part = value[:, t - first : t - first + 128]
                    if t < target:
                        part = jnp.where(lanes >= target - t, part, out[:, t : t + 128])
                    out[:, t : t + 128] = part


def finish(layer, input_rows, grad_out, grad_qkv, grad_down, gu_rows, unit, hidden_width):
    piece, width = grad_out.shape
    kv_width = KV_HEADS * HEAD_DIM
    low, full = jnp.bfloat16, jnp.float32
    shape = jax.ShapeDtypeStruct
    vmem = pl.BlockSpec(memory_space=pltpu.VMEM)
    return pl.pallas_call(
        finish_kernel,
        in_specs=[vmem] * 6,
        out_specs=[vmem] * 9,
        out_shape=[
            shape(layer.shape, low),
            shape(layer.shape, low),
            shape((piece, width), full),
            shape((piece, width), full),
            shape((piece, kv_width), full),
            shape((piece, kv_width), full),
            shape((unit, width), full),
            shape((piece, hidden_width), full),
            shape((piece, hidden_width), full),
        ],
        compiler_params=pltpu.CompilerParams(vmem_limit_bytes=63 * 2**20),
        name="finish",
    )(layer, input_rows, grad_out, grad_qkv, grad_down, gu_rows)


def per_device(
    tokens, cotangent, lengths, balance, norm1_gain, w_query, b_query, w_key, b_key,
    w_value, b_value, w_out, norm2_gain, w_gate, w_up, w_down,
):
    seq_count = lax.axis_size("seq")
    fsdp_count = lax.axis_size("fsdp")
    seq_rank = lax.axis_index("seq")
    fsdp_rank = lax.axis_index("fsdp")
    rows_here, width = tokens.shape
    group = seq_count * rows_here
    kv_width = KV_HEADS * HEAD_DIM
    hidden_width = w_gate.shape[1]
    unit = hidden_width // (fsdp_count * seq_count)
    unit_pad = -(-unit // 16) * 16
    weight_rows = w_gate.shape[0]

    pair_bias = jnp.concatenate([jnp.tile(b_key, fsdp_count), jnp.tile(b_value, fsdp_count)])
    small = jnp.concatenate([norm1_gain] * 2 + [norm2_gain] * 2 + [b_query] * 2 + [pair_bias])
    place_of = np.concatenate(
        [np.repeat([0, 1], weight_rows)] * 3 + [8 + np.repeat(np.arange(8), b_key.shape[0])] * 2
    )
    place_of = jnp.asarray(place_of, jnp.int32)
    mine = (place_of == fsdp_rank % 2) | (place_of == 8 + fsdp_rank)
    small = jnp.broadcast_to(jnp.where(mine, small, 0)[None], (16, small.shape[0]))

    slot = balance % group
    seq_lengths = lengths[0]
    starts = jnp.cumsum(seq_lengths) - seq_lengths
    segment = segment_of(slot, starts)
    first_row = jnp.where(segment == 0, starts[0], jnp.where(segment == 1, starts[1], starts[2]))
    cosine, sine = rope_tables(slot - first_row)
    down_own = lax.dynamic_slice_in_dim(w_down, seq_rank * unit, unit, 0)
    down_own = jnp.pad(down_own, ((0, unit_pad - unit), (0, 0)))
    (
        weight_gu, weight_down, upstream_all, normed_all, weight_qkv, weight_out,
        queries, paired, slots_all, logsum, attended, resid, normed_one, gain_one, gain_two,
    ) = front(
        tokens, cotangent, small, slot, first_row, cosine, sine,
        (w_query, w_key, w_value, w_out, w_gate, w_up), down_own,
    )
    columns, grad_down, gu_sum, gu_far, branch = ffn(normed_all, upstream_all, weight_gu, weight_down)
    layer, input_rows, vectors, grad_out, grad_qkv, gu_rows = back(
        columns, resid, gain_two, cotangent, attended, queries, paired, slots_all, slot, first_row,
        logsum, normed_one, tokens, gain_one, cosine, sine, weight_out, weight_qkv, gu_sum, gu_far,
        branch,
    )
    (
        layer_out, input_grad, grad_out, grad_query, grad_key, grad_value, grad_down, grad_gate,
        grad_up,
    ) = finish(layer, input_rows, grad_out, grad_qkv, grad_down, gu_rows, unit, hidden_width)
    vectors = vectors.reshape(-1)
    own = width // (fsdp_count * seq_count)
    first = (fsdp_rank * seq_count + seq_rank) * own

    def own_part(offset):
        return lax.dynamic_slice_in_dim(vectors, offset + first, own, 0)

    biases = 2 * width
    return (
        layer_out,
        input_grad,
        own_part(0),
        grad_query,
        own_part(biases),
        grad_key,
        vectors[biases + width : biases + width + kv_width],
        grad_value,
        vectors[biases + width + kv_width :],
        grad_out,
        own_part(width),
        grad_gate,
        grad_up,
        grad_down,
    )


def solution(mesh):
    both = P(("fsdp", "seq"), None)
    both_one = P(("fsdp", "seq"))
    placed = (
        both, both, P("fsdp", None), both_one, P("fsdp"), P("fsdp", None), P("fsdp"),
        P("fsdp", None), P("fsdp"), P("fsdp", None), P("fsdp"), P("fsdp", None), P("fsdp"),
        P("fsdp", None), P("fsdp", None), P("fsdp", None),
    )
    return jax.shard_map(
        per_device if mesh.shape["fsdp"] == 8 else plain_device,
        mesh=mesh,
        in_specs=placed,
        out_specs=(
            both, both, both_one, both, both_one, both, P(), both, P(), both, both_one,
            both, both, both,
        ),
        check_vma=False,
    )
```

```python
import jax
import jax.numpy as jnp
import numpy as np
from jax import lax
from jax.experimental import pallas as pl
from jax.experimental.pallas import tpu as pltpu
from jax.sharding import PartitionSpec as P

HEADS = 12
KV_HEADS = 2
HEAD_DIM = 128

MESH = pl.DeviceIdType.MESH

epsilon = 1e-06
rope_base = 1000000.0


def norm_piece(values, gain):
    return values * lax.rsqrt(jnp.mean(values * values, -1, keepdims=True) + epsilon) * gain


def rope_tables(position):
    half = HEAD_DIM // 2
    inverse = rope_base ** (-(jnp.arange(half, dtype=jnp.float32) * 2.0 / HEAD_DIM))
    angle = position.astype(jnp.float32)[:, None] * inverse[None, :]
    cosine = jnp.concatenate([jnp.cos(angle), jnp.cos(angle)], -1)
    sine = jnp.concatenate([jnp.sin(angle), jnp.sin(angle)], -1)
    return (cosine, sine)


def turn_half(values):
    half = values.shape[-1] // 2
    return jnp.concatenate([-values[..., half:], values[..., :half]], -1)


def rotate(values, cosine, sine):
    return values * cosine[:, None, :] + turn_half(values) * sine[:, None, :]


def rotate_back(grads, cosine, sine):
    return grads * cosine[:, None, :] - turn_half(grads * sine[:, None, :])


def segment_of(slots, starts):
    return (slots >= starts[1]).astype(jnp.int32) + (slots >= starts[2]).astype(jnp.int32)


def contract_rows(left, right):
    return lax.dot_general(
        left, right, (((0,), (0,)), ((), ())), preferred_element_type=jnp.float32
    )


def contract_columns(left, right):
    return lax.dot_general(
        left, right, (((1,), (1,)), ((), ())), preferred_element_type=jnp.float32
    )


def plain_device(
    tokens, cotangent, lengths, balance, norm1_gain, w_query, b_query, w_key, b_key,
    w_value, b_value, w_out, norm2_gain, w_gate, w_up, w_down,
):
    seq_count = lax.axis_size("seq")
    fsdp_count = lax.axis_size("fsdp")
    seq_rank = lax.axis_index("seq")
    rows_here, width = tokens.shape
    group = seq_count * rows_here
    kv_width = KV_HEADS * HEAD_DIM
    qkv_width = width + 2 * kv_width
    hidden_width = w_gate.shape[1]
    unit = hidden_width // (fsdp_count * seq_count)
    own_units = hidden_width // seq_count
    weight_rows = w_gate.shape[0]
    score_scale = HEAD_DIM ** (-0.5)
    repeat = HEADS // KV_HEADS

    slot = balance % group
    slots_all = lax.all_gather(slot, "seq", axis=0, tiled=True)
    seq_lengths = lengths[0]
    starts = jnp.cumsum(seq_lengths) - seq_lengths
    segment = segment_of(slot, starts)
    segments_all = segment_of(slots_all, starts)
    first_row = jnp.where(segment == 0, starts[0], jnp.where(segment == 1, starts[1], starts[2]))
    cosine, sine = rope_tables(slot - first_row)
    allowed = (segment[:, None] == segments_all[None, :]) & (slots_all[None, :] <= slot[:, None])

    small = jnp.concatenate([norm1_gain, norm2_gain, b_query, b_key, b_value], 0)[None]
    small = lax.all_gather(small, "fsdp", axis=0, tiled=True)
    piece = norm1_gain.shape[0]
    bias_piece = b_key.shape[0]
    gain_one = small[:, :piece].reshape(-1).astype(jnp.float32)
    gain_two = small[:, piece : 2 * piece].reshape(-1).astype(jnp.float32)
    bias_qkv = jnp.concatenate(
        [
            small[:, 2 * piece : 3 * piece].reshape(-1),
            small[:, 3 * piece : 3 * piece + bias_piece].reshape(-1),
            small[:, 3 * piece + bias_piece :].reshape(-1),
        ],
        0,
    ).astype(jnp.float32)
    weight_qkv = lax.all_gather(
        jnp.concatenate([w_query, w_key, w_value], 1), "fsdp", axis=0, tiled=True
    )
    weight_out = lax.all_gather(w_out, "fsdp", axis=0, tiled=True)
    upstream_all = lax.all_gather(cotangent, "seq", axis=0, tiled=True)

    def own_columns(weight):
        cut = weight.reshape(weight_rows, fsdp_count, seq_count, unit)
        return lax.dynamic_index_in_dim(cut, seq_rank, 2, False).reshape(weight_rows, own_units)

    weight_gu = lax.all_gather(
        jnp.concatenate([own_columns(w_gate), own_columns(w_up)], 1), "fsdp", axis=0, tiled=True
    )
    weight_down = lax.all_gather(
        lax.dynamic_slice_in_dim(w_down, seq_rank * unit, unit, 0), "fsdp", axis=0, tiled=True
    )

    inputs = tokens.astype(jnp.float32)
    normed_one = norm_piece(inputs, gain_one).astype(jnp.bfloat16)
    projected = jnp.dot(normed_one, weight_qkv, preferred_element_type=jnp.float32) + bias_qkv
    query_pre = projected[:, :width].reshape(rows_here, HEADS, HEAD_DIM)
    key_pre = projected[:, width : width + kv_width].reshape(rows_here, KV_HEADS, HEAD_DIM)
    value_pre = projected[:, width + kv_width :]
    queries = rotate(query_pre, cosine, sine).astype(jnp.bfloat16)
    keys = rotate(key_pre, cosine, sine).astype(jnp.bfloat16).reshape(rows_here, kv_width)
    values = value_pre.astype(jnp.bfloat16)
    paired = lax.all_gather(jnp.concatenate([keys, values], 1), "seq", axis=0, tiled=True)
    keys_all = paired[:, :kv_width].reshape(group, KV_HEADS, HEAD_DIM)
    values_all = paired[:, kv_width:].reshape(group, KV_HEADS, HEAD_DIM)
    grouped = queries.reshape(rows_here, KV_HEADS, repeat, HEAD_DIM)
    raw = (
        jnp.einsum("qgrd,kgd->grqk", grouped, keys_all, preferred_element_type=jnp.float32)
        * score_scale
    )
    scores = jnp.where(allowed, raw, -jnp.inf)
    expo = jnp.exp(scores - jnp.max(scores, -1, keepdims=True))
    probs = expo / jnp.sum(expo, -1, keepdims=True)
    probs_low = probs.astype(jnp.bfloat16)
    attended = jnp.einsum(
        "grqk,kgd->qgrd", probs_low, values_all, preferred_element_type=jnp.float32
    )
    attended = attended.astype(jnp.bfloat16).reshape(rows_here, width)
    resid = inputs + jnp.dot(attended, weight_out, preferred_element_type=jnp.float32)
    normed_two = norm_piece(resid, gain_two).astype(jnp.bfloat16)

    normed_all = lax.all_gather(normed_two, "seq", axis=0, tiled=True)
    both = jnp.dot(normed_all, weight_gu, preferred_element_type=jnp.float32)
    gate = both[:, :own_units]
    up = both[:, own_units:]
    sigma = jax.nn.sigmoid(gate)
    activated = gate * sigma
    hidden = (activated * up).astype(jnp.bfloat16)
    d_hidden = contract_columns(upstream_all, weight_down)
    d_gate = (d_hidden * up * sigma * (1.0 + gate * (1.0 - sigma))).astype(jnp.bfloat16)
    d_up = (d_hidden * activated).astype(jnp.bfloat16)
    d_both = jnp.concatenate([d_gate, d_up], 1)
    columns = lax.psum_scatter(
        contract_columns(d_both, weight_gu).astype(jnp.bfloat16),
        "seq", scatter_dimension=0, tiled=True,
    ).astype(jnp.float32)
    branch = lax.psum_scatter(
        jnp.dot(hidden, weight_down, preferred_element_type=jnp.float32).astype(jnp.bfloat16),
        "seq", scatter_dimension=0, tiled=True,
    ).astype(jnp.float32)
    layer_out = (resid + branch).astype(jnp.bfloat16)
    grad_down = lax.psum_scatter(
        contract_rows(hidden, upstream_all).astype(jnp.bfloat16),
        "fsdp", scatter_dimension=0, tiled=True,
    ).astype(jnp.float32)
    grad_pair = lax.psum_scatter(
        contract_rows(normed_all, d_both).astype(jnp.bfloat16),
        "fsdp", scatter_dimension=0, tiled=True,
    )
    grad_pair = lax.all_to_all(grad_pair, "seq", split_axis=0, concat_axis=0, tiled=True)
    grad_pair = grad_pair.reshape(seq_count, weight_rows // seq_count, 2, fsdp_count, unit)
    grad_pair = grad_pair.transpose(2, 1, 3, 0, 4).astype(jnp.float32)
    grad_pair = grad_pair.reshape(2, weight_rows // seq_count, hidden_width)

    _, pull_two = jax.vjp(norm_piece, resid, gain_two)
    d_resid_norm, grad_gain_two = pull_two(columns)
    d_resid = cotangent.astype(jnp.float32) + d_resid_norm
    d_branch = d_resid.astype(jnp.bfloat16)
    grad_out = contract_rows(attended, d_branch).astype(jnp.bfloat16)
    d_attended = contract_columns(d_branch, weight_out).astype(jnp.bfloat16)
    d_attended = d_attended.reshape(rows_here, KV_HEADS, repeat, HEAD_DIM)
    d_probs = jnp.einsum(
        "qgrd,kgd->grqk", d_attended, values_all, preferred_element_type=jnp.float32
    )
    delta = jnp.sum(probs * d_probs, -1, keepdims=True)
    d_score = (probs * (d_probs - delta)).astype(jnp.bfloat16)
    d_queries = (
        jnp.einsum("grqk,kgd->qgrd", d_score, keys_all, preferred_element_type=jnp.float32)
        * score_scale
    )
    d_keys = (
        jnp.einsum("grqk,qgrd->kgd", d_score, grouped, preferred_element_type=jnp.float32)
        * score_scale
    )
    d_values = jnp.einsum(
        "grqk,qgrd->kgd", probs_low, d_attended, preferred_element_type=jnp.float32
    )
    d_paired = jnp.concatenate([d_keys.reshape(group, kv_width), d_values.reshape(group, kv_width)], 1)
    d_paired = lax.psum_scatter(
        d_paired.astype(jnp.bfloat16), "seq", scatter_dimension=0, tiled=True
    ).astype(jnp.float32)
    d_query_pre = rotate_back(
        d_queries.reshape(rows_here, HEADS, HEAD_DIM), cosine, sine
    ).astype(jnp.bfloat16)
    d_key_pre = rotate_back(
        d_paired[:, :kv_width].reshape(rows_here, KV_HEADS, HEAD_DIM), cosine, sine
    ).astype(jnp.bfloat16)
    d_value_pre = d_paired[:, kv_width:].astype(jnp.bfloat16)
    d_qkv = jnp.concatenate(
        [
            d_query_pre.reshape(rows_here, width),
            d_key_pre.reshape(rows_here, kv_width),
            d_value_pre,
        ],
        1,
    )
    grad_qkv = contract_rows(normed_one, d_qkv).astype(jnp.bfloat16)
    grad_bias = jnp.sum(d_qkv.astype(jnp.float32), 0)
    d_normed_one = contract_columns(d_qkv, weight_qkv)
    _, pull_one = jax.vjp(norm_piece, inputs, gain_one)
    d_input_norm, grad_gain_one = pull_one(d_normed_one)
    input_grad = (d_resid + d_input_norm).astype(jnp.bfloat16)

    def summed(value):
        value = lax.psum_scatter(value, "fsdp", scatter_dimension=0, tiled=True)
        return lax.psum_scatter(value, "seq", scatter_dimension=0, tiled=True).astype(jnp.float32)

    grad_out = summed(grad_out)
    grad_qkv = summed(grad_qkv)
    vectors = lax.psum(
        jnp.concatenate([grad_gain_one, grad_gain_two, grad_bias], 0), ("fsdp", "seq")
    )
    own = width // (fsdp_count * seq_count)
    first = (lax.axis_index("fsdp") * seq_count + seq_rank) * own

    def own_part(offset):
        return lax.dynamic_slice_in_dim(vectors, offset + first, own, 0)

    biases = 2 * width
    return (
        layer_out,
        input_grad,
        own_part(0),
        grad_qkv[:, :width],
        own_part(biases),
        grad_qkv[:, width : width + kv_width],
        vectors[biases + width : biases + width + kv_width],
        grad_qkv[:, width + kv_width :],
        vectors[biases + width + kv_width :],
        grad_out,
        own_part(width),
        grad_pair[0],
        grad_pair[1],
        grad_down,
    )


ORDER = (1, 3, 2, 0)


class SumChain:
    def __init__(self, partial, rows, z_one, z_two, z_three, there, index):
        self.rank = lax.axis_index("seq")
        s = self.rank

        def held(j):
            return partial.at[ORDER.index(j) * rows : (ORDER.index(j) + 1) * rows]

        self.held, self.arrived = held, (z_one, z_two, z_three)
        self.up = [
            there(held(1), z_one, index, seq=s + 1),
            there(held(2), z_two.at[0], index + 2, seq=s + 1),
            there(held(3), z_three.at[0], index + 4, seq=s + 1),
        ]
        self.down = [
            there(held(3), z_one, index + 1, seq=s - 1),
            there(held(2), z_two.at[1], index + 3, seq=s - 1),
            there(held(1), z_three.at[1], index + 5, seq=s - 1),
        ]

    def add(self, j, arrived):
        ref = self.held(j)
        total = ref[...].astype(jnp.float32) + arrived[...].astype(jnp.float32)
        ref[...] = total.astype(jnp.bfloat16)

    def one(self):
        pl.when(self.rank == 0)(self.up[0].start)
        pl.when(self.rank == 3)(self.down[0].start)

    def add_one(self):
        @pl.when(self.rank == 1)
        def _():
            self.up[0].wait_recv()
            self.add(2, self.arrived[0])

        @pl.when(self.rank == 2)
        def _():
            self.down[0].wait_recv()
            self.add(2, self.arrived[0])

    def two(self):
        pl.when(self.rank <= 1)(self.up[1].start)
        pl.when(self.rank >= 2)(self.down[1].start)

    def three(self):
        @pl.when((self.rank == 1) | (self.rank == 2))
        def _():
            self.up[1].wait_recv()
            self.add(3, self.arrived[1].at[0])
            self.down[1].wait_recv()
            self.add(1, self.arrived[1].at[1])

        pl.when(self.rank <= 2)(self.up[2].start)
        pl.when(self.rank >= 1)(self.down[2].start)

    def last(self, out):
        out[...] = self.held(0)[...].astype(jnp.float32)

        @pl.when(self.rank >= 1)
        def _():
            self.up[2].wait_recv()
            out[...] += self.arrived[2][0].astype(jnp.float32)

        @pl.when(self.rank <= 2)
        def _():
            self.down[2].wait_recv()
            out[...] += self.arrived[2][1].astype(jnp.float32)

    def one_sent(self):
        pl.when(self.rank == 0)(self.up[0].wait_send)
        pl.when(self.rank == 3)(self.down[0].wait_send)

    def sent(self):
        pl.when(self.rank <= 1)(self.up[1].wait_send)
        pl.when(self.rank >= 2)(self.down[1].wait_send)
        pl.when(self.rank <= 2)(self.up[2].wait_send)
        pl.when(self.rank >= 1)(self.down[2].wait_send)


class SumPlane:
    def __init__(self, buffer, block, plane, arrived, by_x, by_y, ended, there, index):
        half = buffer.shape[1] // 2
        low, high = pl.ds(0, half), pl.ds(half, half)

        def part(k):
            return buffer.at[pl.ds(pl.multiple_of(plane[k] * block, 16), block)]

        self.parts = own, to_x, to_y, to_both = [part(k) for k in (0, 2, 4, 6)]
        self.arrived, self.by_x, self.by_y, self.ended, self.half = arrived, by_x, by_y, ended, half
        self.core = [
            there(part(2 * i + 1), arrived.at[i], index + i, fsdp=plane[1]) for i in range(4)
        ]
        self.first = [
            there(to_both.at[:, low], by_x.at[1], index + 5, fsdp=plane[2]),
            there(to_both.at[:, high], by_y.at[1], index + 7, fsdp=plane[4]),
            there(to_x.at[:, low], by_x.at[0], index + 4, fsdp=plane[2]),
            there(to_y.at[:, high], by_y.at[0], index + 6, fsdp=plane[4]),
        ]
        self.second = [
            there(to_y.at[:, low], ended.at[0], index + 8, fsdp=plane[4]),
            there(to_x.at[:, high], ended.at[1], index + 9, fsdp=plane[2]),
        ]

    def start_core(self):
        for copy in self.core:
            copy.start()

    def start_first(self):
        for i in (3, 1, 2, 0):
            self.core[i].wait_recv()
            part = self.parts[i]
            total = part[...].astype(jnp.float32) + self.arrived[i].astype(jnp.float32)
            part[...] = total.astype(jnp.bfloat16)
        for copy in self.first:
            copy.start()

    def start_second(self):
        half = self.half
        _, to_x, to_y, _ = self.parts
        self.first[0].wait_recv()
        total = to_y[:, :half].astype(jnp.float32) + self.by_x[1].astype(jnp.float32)
        to_y[:, :half] = total.astype(jnp.bfloat16)
        self.second[0].start()
        self.first[1].wait_recv()
        total = to_x[:, half:].astype(jnp.float32) + self.by_y[1].astype(jnp.float32)
        to_x[:, half:] = total.astype(jnp.bfloat16)
        self.second[1].start()

    def finish(self):
        half = self.half
        own = self.parts[0]
        self.first[2].wait_recv()
        self.second[0].wait_recv()
        total = own[:, :half].astype(jnp.float32) + self.by_x[0].astype(jnp.float32)
        own[:, :half] = (total + self.ended[0].astype(jnp.float32)).astype(jnp.bfloat16)
        self.first[3].wait_recv()
        self.second[1].wait_recv()
        total = own[:, half:].astype(jnp.float32) + self.by_y[0].astype(jnp.float32)
        own[:, half:] = (total + self.ended[1].astype(jnp.float32)).astype(jnp.bfloat16)

    def sent(self):
        for copy in self.core + self.first + self.second:
            copy.wait_send()


def front_kernel(
    lengths, tokens, cotangent, small, balance, inverse,
    w_query, w_key, w_value, w_out, w_gate, w_up, w_down,
    gu_all, down_all, upstream_all, normed_all, hidden, factor_gate, factor_up, qkv_out, out_out,
    queries, paired_out, slots_out, logsum, attended, resid, normed_one, gain_one, gain_two,
    slot_row, first_row, cosine, sine,
    qkv, out_w, gate_v, up_v, gu, normed, kv, small_own, small_all, slots_all, bias,
    down_raw, down_own, hidden_v, gate_part, up_part,
    local, ssem, rsem, zsend, zrecv,
):
    f = lax.axis_index("fsdp")
    s = lax.axis_index("seq")
    rows, width = tokens.shape
    n_f, n_s = 8, slots_all.shape[0]
    group = n_s * rows
    block = w_query.shape[0]
    unit_pad = down_own.shape[0]
    unit = w_gate.shape[1] // (n_f * n_s)
    units = n_f * unit_pad
    kv_width = KV_HEADS * HEAD_DIM
    qkv_width = width + 2 * kv_width
    scale = HEAD_DIM ** (-0.5)
    repeat = HEADS // KV_HEADS
    plane = [f ^ k for k in range(n_f)]

    entry = pltpu.get_barrier_semaphore()
    for k in range(1, n_f):
        pl.semaphore_signal(entry, inc=1, device_id={"fsdp": plane[k]}, device_id_type=MESH)
    for j in range(1, n_s):
        pl.semaphore_signal(
            entry, inc=1, device_id={"seq": lax.rem(s + j, n_s)}, device_id_type=MESH
        )

    def here(source, target, index):
        return pltpu.make_async_copy(source, target, local.at[index])

    def there(source, target, index, **device):
        return pltpu.make_async_remote_copy(
            src_ref=source, dst_ref=target, send_sem=ssem.at[index], recv_sem=rsem.at[index],
            device_id=device, device_id_type=MESH,
        )

    def own_rows(ref, owner, size, start=0, count=None):
        first = pl.multiple_of(owner * size + start, 16)
        return ref.at[pl.ds(first, size if count is None else count)]

    class Gather:
        def __init__(self, source, target, size, index):
            half = size // 2
            x, y, c = plane[2], plane[4], plane[1]
            self.own = here(source, own_rows(target, f, size), index // 8) if source is not None else None
            if source is None:
                source = own_rows(target, f, size)
            mine = own_rows(target, f, size)
            self.first = [
                there(source, mine, index, fsdp=x),
                there(source, mine, index + 1, fsdp=y),
                there(source, mine, index + 2, fsdp=c),
            ]
            from_x, from_y = own_rows(target, x, size), own_rows(target, y, size)
            part_x = own_rows(target, x, size, 0, half)
            part_y = own_rows(target, y, size, half, half)
            self.second = [
                there(part_x, part_x, index + 3, fsdp=y),
                there(part_y, part_y, index + 4, fsdp=x),
                there(from_x, from_x, index + 5, fsdp=c),
                there(from_y, from_y, index + 6, fsdp=c),
            ]
            diagonal = own_rows(target, plane[6], size)
            self.third = there(diagonal, diagonal, index + 7, fsdp=c)

        def start(self):
            if self.own is not None:
                self.own.start()
            for copy in self.first:
                copy.start()

        def forward(self):
            self.first[0].wait_recv()
            self.second[0].start()
            self.second[2].start()
            self.first[1].wait_recv()
            self.second[1].start()
            self.second[3].start()

        def last(self):
            self.second[0].wait_recv()
            self.second[1].wait_recv()
            self.third.start()

        def finish(self):
            if self.own is not None:
                self.own.wait()
            self.first[2].wait_recv()
            self.second[2].wait_recv()
            self.second[3].wait_recv()
            self.third.wait_recv()

        def sent(self):
            for copy in self.first + self.second + [self.third]:
                copy.wait_send()

    class Chain:
        def __init__(self, target, index):
            self.steps = []
            for step in range(1, n_s):
                up = own_rows(target, s - (step - 1), rows)
                down = own_rows(target, s + (step - 1), rows)
                i = index + 2 * (step - 1)
                self.steps.append((
                    pltpu.make_async_remote_copy(
                        src_ref=up, dst_ref=up, send_sem=zsend.at[i], recv_sem=zrecv.at[i],
                        device_id={"seq": s + 1}, device_id_type=MESH,
                    ),
                    pltpu.make_async_remote_copy(
                        src_ref=down, dst_ref=down, send_sem=zsend.at[i + 1], recv_sem=zrecv.at[i + 1],
                        device_id={"seq": s - 1}, device_id_type=MESH,
                    ),
                    (s >= step - 1) & (s < n_s - 1),
                    (s >= 1) & (s <= n_s - step),
                    s >= step,
                    s <= n_s - 1 - step,
                ))

        def send(self, step):
            up, down, can_up, can_down, _, _ = self.steps[step - 1]
            pl.when(can_up)(up.start)
            pl.when(can_down)(down.start)

        def receive(self, step):
            up, down, _, _, from_below, from_above = self.steps[step - 1]
            pl.when(from_below)(up.wait_recv)
            pl.when(from_above)(down.wait_recv)

        def sent(self):
            for up, down, can_up, can_down, _, _ in self.steps:
                pl.when(can_up)(up.wait_send)
                pl.when(can_down)(down.wait_send)

    own_block = pl.ds(pl.multiple_of(f * block, 16), block)
    pieces = [
        here(w_query, qkv.at[own_block, pl.ds(0, width)], 5),
        here(w_key, qkv.at[own_block, pl.ds(width, kv_width)], 6),
        here(w_value, qkv.at[own_block, pl.ds(width + kv_width, kv_width)], 7),
        here(cotangent, own_rows(upstream_all, s, rows), 8),
    ]
    load_gate = here(w_gate, gate_v, 9)
    load_up = here(w_up, up_v, 10)
    first_unit = pl.multiple_of(s * unit // 16 * 16, 16)
    load_down = here(w_down.at[pl.ds(first_unit, unit_pad)], down_raw, 15)
    for copy in pieces:
        copy.start()
    load_gate.start()
    load_up.start()
    load_down.start()

    slot = (balance[...] & (group - 1)).astype(jnp.float32)
    second = lengths[0, 0].astype(jnp.float32)
    third = (lengths[0, 0] + lengths[0, 1]).astype(jnp.float32)
    first = jnp.where(slot >= third, third, jnp.where(slot >= second, second, 0.0))
    slot_row[...] = jnp.broadcast_to(slot, slot_row.shape)
    first_row[...] = jnp.broadcast_to(first, first_row.shape)
    slots_all[s] = jnp.broadcast_to(slot, (128, rows)).T
    lanes = lax.broadcasted_iota(jnp.int32, small.shape, 1)
    sorts = lax.broadcasted_iota(jnp.int32, small.shape, 0)
    small_own[...] = jnp.where(
        sorts < 3,
        pltpu.roll(small[...], lax.rem(f, 2) * block, 1),
        pltpu.roll(small[...], f * (kv_width // n_f), 1),
    )
    small_all[f] = small_own[...]

    gather_qkv = Gather(None, qkv, block, 0)
    gather_out = Gather(w_out, out_w, block, 8)
    gather_gu = Gather(None, gu, block, 16)
    gather_down = Gather(down_own, down_all, unit_pad, 24)
    chain_up = Chain(upstream_all, 0)
    chain_normed = Chain(normed, 6)
    send_small = [
        there(small_own, small_all.at[f], 32 + k, fsdp=plane[k]) for k in range(1, n_f)
    ]
    send_slots = [
        there(slots_all.at[s], slots_all.at[s], 40 + j, seq=lax.rem(s + j, n_s))
        for j in range(1, n_s)
    ]
    send_kv = [
        there(kv.at[s], kv.at[s], 44 + j, seq=lax.rem(s + j, n_s)) for j in range(1, n_s)
    ]
    for copy in pieces[:3]:
        copy.wait()
    pl.semaphore_wait(entry, n_f - 1 + n_s - 1)
    gather_qkv.start()
    for copy in send_small + send_slots:
        copy.start()
    pieces[3].wait()
    chain_up.send(1)

    load_gate.wait()
    load_up.wait()
    pick_units(gate_v, up_v, gu.at[own_block], w_gate.shape[1] // n_f, unit, unit_pad)
    load_down.wait()
    raw = down_raw[...].astype(jnp.float32)
    shifted = jnp.concatenate([raw[8:], jnp.zeros((8, width), jnp.float32)], 0)
    raw = jnp.where(lax.rem(s * unit, 16) == 0, raw, shifted)
    inside = lax.broadcasted_iota(jnp.int32, raw.shape, 0) < unit
    down_own[...] = jnp.where(inside, raw, 0.0).astype(jnp.bfloat16)

    position = slots_all[s] - jnp.broadcast_to(first, (128, rows)).T
    angle = position * inverse[...]
    cosine[...] = jnp.cos(angle)
    sine[...] = jnp.where(
        lax.broadcasted_iota(jnp.int32, angle.shape, 1) < HEAD_DIM // 2, -1.0, 1.0
    ) * jnp.sin(angle)

    for copy in send_small + send_slots:
        copy.wait_recv()
    def joined(sort):
        return jnp.concatenate(
            [
                small_all[2 * i, sort : sort + 1] + small_all[2 * i + 1, sort : sort + 1]
                for i in range(n_f // 2)
            ],
            1,
        )

    gain_one[...] = joined(0)
    gain_two[...] = joined(1)
    bias_query = joined(2)
    bias_key = sum(small_all[i, 3:4, :kv_width] for i in range(n_f))
    bias_value = sum(small_all[i, 4:5, :kv_width] for i in range(n_f))

    inputs = tokens[...].astype(jnp.float32)
    root = lax.rsqrt(jnp.mean(inputs * inputs, -1, keepdims=True) + epsilon)
    normed_one[...] = (inputs * root * gain_one[...]).astype(jnp.bfloat16)
    for j in range(n_s):
        keys_slot = slots_all[j]
        keys_slot = jnp.concatenate([keys_slot] * (rows // 128), 1)
        ok = (keys_slot <= slot) & (keys_slot >= first)
        bias[j * rows : (j + 1) * rows] = jnp.where(ok, 0.0, -1e30)

    gather_qkv.forward()
    chain_up.receive(1)
    chain_up.send(2)
    gather_qkv.last()
    gather_out.start()
    gather_qkv.finish()
    save_qkv = here(qkv, qkv_out, 11)
    save_qkv.start()

    def turned(value):
        return value * cosine[...] + pltpu.roll(value, HEAD_DIM // 2, 1) * sine[...]

    rows_low = normed_one[...]
    pair = jnp.dot(rows_low, qkv[:, width : width + kv_width], preferred_element_type=jnp.float32)
    pair = pair + bias_key
    for g in range(KV_HEADS):
        columns = slice(g * HEAD_DIM, (g + 1) * HEAD_DIM)
        kv[s, :, columns] = turned(pair[:, columns]).astype(jnp.bfloat16)
    pair = jnp.dot(rows_low, qkv[:, width + kv_width :], preferred_element_type=jnp.float32)
    kv[s, :, kv_width:] = (pair + bias_value).astype(jnp.bfloat16)
    for copy in send_kv:
        copy.start()
    for g in range(HEADS // 2):
        columns = slice(g * 2 * HEAD_DIM, (g + 1) * 2 * HEAD_DIM)
        pair = jnp.dot(rows_low, qkv[:, columns], preferred_element_type=jnp.float32)
        pair = pair + bias_query[:, columns]
        for h in range(2):
            part = turned(pair[:, h * HEAD_DIM : (h + 1) * HEAD_DIM]).astype(jnp.bfloat16)
            queries[:, (2 * g + h) * HEAD_DIM : (2 * g + h + 1) * HEAD_DIM] = part

    gather_out.forward()
    gather_gu.start()
    chain_up.receive(2)
    gather_out.last()
    for copy in send_kv:
        copy.wait_recv()
    chain_up.send(3)
    save_kv = here(kv, paired_out, 12)
    save_kv.start()
    slots_out[...] = slots_all[...]

    for g in range(KV_HEADS):
        keys = kv[:, :, g * HEAD_DIM : (g + 1) * HEAD_DIM].reshape(n_s * rows, HEAD_DIM)
        values = kv[:, :, kv_width + g * HEAD_DIM : kv_width + (g + 1) * HEAD_DIM]
        values = values.reshape(n_s * rows, HEAD_DIM)

        def head(i, carry, g=g, keys=keys, values=values):
            h = g * repeat + i
            columns = pl.ds(pl.multiple_of(h * HEAD_DIM, HEAD_DIM), HEAD_DIM)
            raw = lax.dot_general(
                keys, queries[:, columns], (((1,), (1,)), ((), ())),
                preferred_element_type=jnp.float32,
            )
            scores = raw * scale + bias[...]
            top = jnp.max(scores, 0, keepdims=True)
            expo = jnp.exp(scores - top)
            total = jnp.sum(expo, 0, keepdims=True)
            probs = (expo * (1.0 / total)).astype(jnp.bfloat16)
            mixed = lax.dot_general(
                values, probs, (((0,), (0,)), ((), ())), preferred_element_type=jnp.float32
            )
            attended[:, columns] = mixed.T.astype(jnp.bfloat16)
            logsum[pl.ds(pl.multiple_of(h * 8, 8), 8)] = jnp.broadcast_to(
                top + jnp.log(total), (8, rows)
            )
            return carry

        lax.fori_loop(0, repeat, head, 0)

    gather_out.finish()
    save_out = here(out_w, out_out, 13)
    save_out.start()
    mixed = attended[...]
    for g in range(width // 256):
        columns = slice(g * 256, (g + 1) * 256)
        part = jnp.dot(mixed, out_w[:, columns], preferred_element_type=jnp.float32)
        resid[:, columns] = tokens[:, columns].astype(jnp.float32) + part
    value = resid[...]
    root = lax.rsqrt(jnp.mean(value * value, -1, keepdims=True) + epsilon)
    own_tokens = pl.ds(pl.multiple_of(s * rows, rows), rows)
    normed[own_tokens] = (value * root * gain_two[...]).astype(jnp.bfloat16)
    chain_normed.send(1)

    wide = hidden_v.shape[2]
    count = units // wide

    def saves(owner, t, slot):
        place = (
            pl.ds(pl.multiple_of(owner * rows, rows), rows),
            pl.ds(pl.multiple_of(t * wide, wide), wide),
        )
        return [
            here(part.at[slot], whole.at[place], 16 + 3 * slot + i)
            for i, (part, whole) in enumerate(
                ((hidden_v, hidden), (gate_part, factor_gate), (up_part, factor_up))
            )
        ]

    def feed(owner, done):
        def body(t, carry):
            slot = lax.rem(t + done, 2)
            mine = normed[pl.ds(pl.multiple_of(owner * rows, rows), rows)]
            gate_columns = pl.ds(pl.multiple_of(t * wide, wide), wide)
            up_columns = pl.ds(pl.multiple_of(units + t * wide, wide), wide)
            gate = jnp.dot(mine, gu[:, gate_columns], preferred_element_type=jnp.float32)
            up = jnp.dot(mine, gu[:, up_columns], preferred_element_type=jnp.float32)
            sigma = jax.nn.sigmoid(gate)
            activated = gate * sigma

            @pl.when(t + done >= 2)
            def _():
                for copy in saves(owner, t, slot):
                    copy.wait()

            hidden_v[slot] = (activated * up).astype(jnp.bfloat16)
            gate_part[slot] = (up * sigma * (1.0 + gate * (1.0 - sigma))).astype(jnp.bfloat16)
            up_part[slot] = activated.astype(jnp.bfloat16)
            for copy in saves(owner, t, slot):
                copy.start()
            return carry

        lax.fori_loop(0, count, body, 0)

    gather_gu.forward()
    chain_normed.receive(1)
    chain_normed.send(2)
    gather_gu.last()
    gather_down.start()
    gather_gu.finish()
    save_gu = here(gu, gu_all, 22)
    save_gu.start()
    feed(s, 0)
    chain_normed.receive(2)
    chain_normed.send(3)
    feed(s ^ 1, count)
    gather_down.forward()
    feed(s ^ 2, 2 * count)
    chain_normed.receive(3)
    save_normed = here(normed, normed_all, 23)
    save_normed.start()
    gather_down.last()
    feed(s ^ 3, 3 * count)
    for t in (count - 2, count - 1):
        for copy in saves(s ^ 3, t, (t + 3 * count) % 2):
            copy.wait()
    chain_up.receive(3)
    gather_down.finish()
    for copy in (save_qkv, save_kv, save_out, save_gu, save_normed):
        copy.wait()
    for part in (gather_qkv, gather_out, gather_gu, gather_down, chain_up, chain_normed):
        part.sent()
    for copy in send_small + send_slots + send_kv:
        copy.wait_send()


def pick_units(gate, up, out, stride, unit, padded):
    rank = lax.axis_index("seq")
    pieces = gate.shape[1] // stride
    half = out.shape[1] // 2
    window, tile = 512, 128
    rows = lax.broadcasted_iota(jnp.int32, (window, tile), 0)
    columns = lax.broadcasted_iota(jnp.int32, (window, tile), 1)
    for first in range(0, 2 * half, tile):
        source = gate if first < half else up
        local = first % half
        total = jnp.zeros((out.shape[0], tile), jnp.float32)
        for f in range(pieces):
            low = max(local, f * padded)
            high = min(local + tile, f * padded + unit)
            if low >= high:
                continue
            begin = f * stride + rank * unit
            base = jnp.minimum(begin // 128, (source.shape[1] - window) // 128) * 128
            base = pl.multiple_of(base, 128)
            wanted = columns + (local - f * padded + begin - base)
            inside = (columns >= low - local) & (columns < high - local)
            chosen = jnp.where((rows == wanted) & inside, 1.0, 0.0).astype(jnp.bfloat16)
            total += jnp.dot(
                source[:, pl.ds(base, window)], chosen, preferred_element_type=jnp.float32
            )
        out[:, first : first + tile] = total.astype(jnp.bfloat16)


def front(tokens, cotangent, lengths, balance, vectors, weights):
    rows, width = tokens.shape
    n_s = lax.axis_size("seq")
    w_query, w_key, w_value, w_out, w_gate, w_up, w_down = weights
    block = w_query.shape[0]
    unit_pad = -(-w_down.shape[0] // n_s // 16) * 16
    kv_width = KV_HEADS * HEAD_DIM
    qkv_width = width + 2 * kv_width
    units = 8 * unit_pad
    group = n_s * rows
    wide = 768
    low, full = jnp.bfloat16, jnp.float32
    small = sum(
        jnp.pad(v.astype(full)[None], ((i, 7 - i), (0, 2 * block - v.shape[0])))
        for i, v in enumerate(vectors)
    )
    half = HEAD_DIM // 2
    inverse = rope_base ** (-(np.arange(half, dtype=np.float32) * np.float32(2.0 / HEAD_DIM)))
    inverse = jnp.asarray(np.concatenate([inverse, inverse])[None], full)
    smem = pl.BlockSpec(memory_space=pltpu.SMEM)
    vmem = pl.BlockSpec(memory_space=pltpu.VMEM)
    hbm = pl.BlockSpec(memory_space=pl.ANY)
    shape = jax.ShapeDtypeStruct
    return pl.pallas_call(
        front_kernel,
        in_specs=[smem, vmem, hbm, vmem, vmem, vmem] + [hbm] * 7,
        out_specs=[hbm] * 9 + [vmem, hbm] + [vmem] * 11,
        out_shape=[
            shape((width, 2 * units), low),
            shape((units, width), low),
            shape((group, width), low),
            shape((group, width), low),
            shape((group, units), low),
            shape((group, units), low),
            shape((group, units), low),
            shape((width, qkv_width), low),
            shape((width, width), low),
            shape((rows, width), low),
            shape((n_s, rows, 2 * kv_width), low),
            shape((n_s, rows, 128), full),
            shape((8 * HEADS, rows), full),
            shape((rows, width), low),
            shape((rows, width), full),
            shape((rows, width), low),
            shape((1, width), full),
            shape((1, width), full),
            shape((8, rows), full),
            shape((8, rows), full),
            shape((rows, HEAD_DIM), full),
            shape((rows, HEAD_DIM), full),
        ],
        scratch_shapes=[
            pltpu.VMEM((width, qkv_width), low),
            pltpu.VMEM((width, width), low),
            pltpu.VMEM(w_gate.shape, low),
            pltpu.VMEM(w_up.shape, low),
            pltpu.VMEM((width, 2 * units), low),
            pltpu.VMEM((group, width), low),
            pltpu.VMEM((n_s, rows, 2 * kv_width), low),
            pltpu.VMEM((8, 2 * block), full),
            pltpu.VMEM((8, 8, 2 * block), full),
            pltpu.VMEM((n_s, rows, 128), full),
            pltpu.VMEM((group, rows), full),
            pltpu.VMEM((unit_pad, width), low),
            pltpu.VMEM((unit_pad, width), low),
            pltpu.VMEM((2, rows, wide), low),
            pltpu.VMEM((2, rows, wide), low),
            pltpu.VMEM((2, rows, wide), low),
            pltpu.SemaphoreType.DMA((24,)),
            pltpu.SemaphoreType.DMA((48,)),
            pltpu.SemaphoreType.DMA((48,)),
            pltpu.SemaphoreType.DMA((12,)),
            pltpu.SemaphoreType.DMA((12,)),
        ],
        compiler_params=pltpu.CompilerParams(
            collective_id=0, has_side_effects=True, vmem_limit_bytes=62 * 2**20
        ),
        name="front",
    )(
        lengths, tokens, cotangent, small, balance.reshape(1, rows), inverse,
        w_query, w_key, w_value, w_out, w_gate, w_up, w_down,
    )


def ffn_kernel(
    normed_all, upstream_all, w_gu, w_down, hidden_all, factor_gate, factor_up,
    columns, grad_down, gu_sum, gu_far, branch, down_arrived, gu_arrived,
    normed, upstream, gu, down, hidden, d_both, partial, z_one, z_two, z_three,
    down_x, down_y, down_last, down_piece,
    load, ssem, rsem,
):
    f = lax.axis_index("fsdp")
    s = lax.axis_index("seq")
    n_s = len(ORDER)
    group, width = normed.shape
    rows = group // n_s
    half_rows = group // 2
    units = down.shape[0]
    tile = 256
    tiles = units // tile
    wide = 768
    block = gu.shape[0] // 8
    unit = units // 8
    half = width // 2
    plane = [f ^ k for k in range(8)]
    full = jnp.float32

    entry = pltpu.get_barrier_semaphore()
    for k in (1, 2, 4):
        pl.semaphore_signal(entry, inc=1, device_id={"fsdp": plane[k]}, device_id_type=MESH)
    for j in (1, n_s - 1):
        pl.semaphore_signal(
            entry, inc=1, device_id={"seq": lax.rem(s + j, n_s)}, device_id_type=MESH
        )

    def here(source, target, index):
        return pltpu.make_async_copy(source, target, load.at[index])

    def there(source, target, index, **device):
        return pltpu.make_async_remote_copy(
            src_ref=source, dst_ref=target, send_sem=ssem.at[index], recv_sem=rsem.at[index],
            device_id=device, device_id_type=MESH,
        )

    def part(ref, owner, size):
        return ref.at[pl.ds(pl.multiple_of(owner * size, 16), size)]

    early, late = range(0, n_s // 2), range(n_s // 2, n_s)

    def rows_of(p):
        return pl.ds(p * rows, rows)

    def row_loads(p):
        owner = lax.rem(s + n_s - ORDER[p], n_s)
        mine = rows_of(p)
        return [
            here(part(upstream_all, owner, rows), upstream.at[mine], 5 * p),
            here(part(factor_gate, owner, rows), d_both.at[mine, pl.ds(0, units)], 5 * p + 1),
            here(part(factor_up, owner, rows), d_both.at[mine, pl.ds(units, units)], 5 * p + 2),
            here(part(hidden_all, owner, rows), hidden.at[mine], 5 * p + 3),
            here(part(normed_all, owner, rows), normed.at[mine], 5 * p + 4),
        ]

    def down_load(t):
        mine = pl.ds(pl.multiple_of(t * wide, wide), wide)
        return here(w_down.at[mine], down.at[mine], 20 + t)

    def gu_load(n):
        mine = pl.ds(pl.multiple_of(n * 512, 512), 512)
        return here(w_gu.at[mine], gu.at[mine], 23 + n)

    loads = [row_loads(p) for p in range(n_s)]
    order = [loads[0][0], loads[1][0], down_load(0)]
    order += [loads[p][i] for i in (1, 2) for p in early]
    order += [down_load(t) for t in range(1, units // wide)]
    order += [gu_load(n) for n in range(width // 512)]
    order += [loads[p][i] for i in (0, 1, 2) for p in late]
    order += [loads[p][i] for i in (3, 4) for p in range(n_s)]
    for copy in order:
        copy.start()

    def forward(blocks, wait):
        for p in blocks:
            for copy in loads[p][:3]:
                copy.wait()
        mine = pl.ds(blocks[0] * rows, len(blocks) * rows)

        def body(t, carry):
            if wait:
                down_load(t).wait()
            gate_columns = pl.ds(pl.multiple_of(t * wide, wide), wide)
            up_columns = pl.ds(pl.multiple_of(units + t * wide, wide), wide)
            d_hidden = lax.dot_general(
                upstream[mine], down[gate_columns], (((1,), (1,)), ((), ())),
                preferred_element_type=full,
            )
            value = d_hidden * d_both[mine, gate_columns].astype(full)
            d_both[mine, gate_columns] = value.astype(jnp.bfloat16)
            value = d_hidden * d_both[mine, up_columns].astype(full)
            d_both[mine, up_columns] = value.astype(jnp.bfloat16)
            return carry

        lax.fori_loop(0, units // wide, body, 0)

    def backward(blocks, wait):
        part_rows = pl.ds(blocks[0] * rows, len(blocks) * rows)

        def body(n, carry):
            if wait:
                gu_load(n).wait()
            out_columns = pl.ds(pl.multiple_of(n * 512, 512), 512)
            value = lax.dot_general(
                d_both[part_rows], gu[out_columns], (((1,), (1,)), ((), ())),
                preferred_element_type=full,
            )
            partial[part_rows, out_columns] = value.astype(jnp.bfloat16)
            return carry

        lax.fori_loop(0, width // 512, body, 0)

    chain = SumChain(partial, rows, z_one, z_two, z_three, there, 0)
    pieces = [(first, min(group, units - first)) for first in range(0, units, group)]
    forward(early, True)
    backward(early, True)
    pl.semaphore_wait(entry, 5)
    chain.one()
    forward(late, False)
    backward(late, False)
    chain.add_one()
    chain.two()

    for p in range(n_s):
        loads[p][3].wait()
        loads[p][4].wait()

    def down_body(t, carry):
        unit_rows = pl.ds(pl.multiple_of(t * tile, tile), tile)
        value = lax.dot_general(
            hidden[:, unit_rows], upstream[...], (((0,), (0,)), ((), ())),
            preferred_element_type=full,
        )
        down[unit_rows] = value.astype(jnp.bfloat16)
        return carry

    lax.fori_loop(0, tiles, down_body, 0)
    down_core = [
        there(part(down, plane[2 * i + 1], unit), down_arrived.at[i], 6 + i, fsdp=plane[1])
        for i in range(4)
    ]
    for copy in down_core:
        copy.start()

    def gu_body(m, carry):
        in_columns = pl.ds(pl.multiple_of(m * tile, tile), tile)
        turned = normed[:, in_columns].T
        for first in range(0, 2 * units, units // 3):
            value = jnp.dot(turned, d_both[:, first : first + units // 3], preferred_element_type=full)
            gu[in_columns, first : first + units // 3] = value.astype(jnp.bfloat16)
        return carry

    lax.fori_loop(0, 2, gu_body, 0)

    def add_arrived(i, ref, size, arrived, pieces, copies, index):
        copies[i].wait_recv()
        fetch = [
            here(arrived.at[i, :, columns], piece, index + k)
            for k, (columns, piece) in enumerate(pieces)
        ]
        for copy in fetch:
            copy.start()
        target = part(ref, plane[2 * i], size)
        for copy, (columns, piece) in zip(fetch, pieces):
            copy.wait()
            target[:, columns] = (
                target[:, columns].astype(full) + piece[...].astype(full)
            ).astype(jnp.bfloat16)

    down_pieces = [(pl.ds(0, width), down_piece)]
    for i in (3, 1, 2, 0):
        add_arrived(i, down, unit, down_arrived, down_pieces, down_core, 26)
    to_x, to_y, to_both = [part(down, plane[k], unit) for k in (2, 4, 6)]
    low_half, high_half = pl.ds(0, half), pl.ds(half, half)
    down_first = [
        there(to_x.at[:, low_half], down_x.at[0], 10, fsdp=plane[2]),
        there(to_both.at[:, low_half], down_x.at[1], 11, fsdp=plane[2]),
        there(to_y.at[:, high_half], down_y.at[0], 12, fsdp=plane[4]),
        there(to_both.at[:, high_half], down_y.at[1], 13, fsdp=plane[4]),
    ]
    for copy in down_first:
        copy.start()
    chain.three()
    lax.fori_loop(2, width // tile, gu_body, 0)
    gu_core = [
        there(part(gu, plane[2 * i + 1], block), gu_arrived.at[i], 16 + i, fsdp=plane[1])
        for i in range(4)
    ]
    for copy in gu_core:
        copy.start()

    again = [
        here(
            w_down.at[first : first + count],
            d_both.at[:count, i * width : (i + 1) * width], 32 + i,
        )
        for i, (first, count) in enumerate(pieces)
    ]
    for copy in again:
        copy.start()
    for copy in again:
        copy.wait()

    def branch_body(n, carry):
        out_columns = pl.ds(pl.multiple_of(n * wide, wide), wide)
        for m in range(2):
            mine = slice(m * half_rows, (m + 1) * half_rows)
            value = jnp.zeros((half_rows, wide), full)
            for i, (first, count) in enumerate(pieces):
                columns_here = pl.ds(pl.multiple_of(i * width + n * wide, wide), wide)
                value += jnp.dot(
                    hidden[mine, first : first + count], d_both[:count, columns_here],
                    preferred_element_type=full,
                )
            upstream[mine, out_columns] = value.astype(jnp.bfloat16)
        return carry

    lax.fori_loop(0, width // wide, branch_body, 0)
    chain.last(columns)
    chain_branch = SumChain(upstream, rows, z_one, z_two, z_three, there, 22)
    chain_branch.one()
    down_second = [
        there(to_y.at[:, low_half], down_last.at[0], 14, fsdp=plane[4]),
        there(to_x.at[:, high_half], down_last.at[1], 15, fsdp=plane[2]),
    ]
    down_first[1].wait_recv()
    to_y[:, :half] = (to_y[:, :half].astype(full) + down_x[1].astype(full)).astype(jnp.bfloat16)
    down_second[0].start()
    down_first[3].wait_recv()
    to_x[:, half:] = (to_x[:, half:].astype(full) + down_y[1].astype(full)).astype(jnp.bfloat16)
    down_second[1].start()
    gu_pieces = [
        (pl.ds(0, units), hidden.at[:block]),
        (pl.ds(units, units), hidden.at[block : 2 * block]),
    ]
    add_arrived(3, gu, block, gu_arrived, gu_pieces, gu_core, 27)
    far = part(gu, plane[6], block)
    gu_first = [
        there(far.at[:, pl.ds(0, units)], gu_far.at[0], 20, fsdp=plane[2]),
        there(far.at[:, pl.ds(units, units)], gu_far.at[1], 21, fsdp=plane[4]),
    ]
    for copy in gu_first:
        copy.start()
    for i in (1, 2, 0):
        add_arrived(i, gu, block, gu_arrived, gu_pieces, gu_core, 27)
    store = [here(part(gu, plane[2 * i], block), gu_sum.at[i], 29 + i) for i in range(3)]
    for copy in store:
        copy.start()
    down_first[0].wait_recv()
    down_first[2].wait_recv()
    own = part(down, f, unit)
    down_second[0].wait_recv()
    grad_down[:, :half] = (
        own[:, :half].astype(full) + down_x[0].astype(full) + down_last[0].astype(full)
    )
    down_second[1].wait_recv()
    grad_down[:, half:] = (
        own[:, half:].astype(full) + down_y[0].astype(full) + down_last[1].astype(full)
    )
    chain_branch.add_one()
    chain_branch.one_sent()
    store_branch = here(upstream, branch, 35)
    store_branch.start()
    chain.one_sent()
    chain.sent()
    for copy in down_core + down_first + down_second + gu_core + gu_first:
        copy.wait_send()
    for copy in gu_first:
        copy.wait_recv()
    for copy in store + [store_branch]:
        copy.wait()


def ffn(normed_all, upstream_all, w_gu, w_down, hidden, factor_gate, factor_up):
    group, width = normed_all.shape
    units = w_down.shape[0]
    rows = group // len(ORDER)
    unit, block, half = units // 8, width // 8, width // 2
    low, full = jnp.bfloat16, jnp.float32
    vmem = pl.BlockSpec(memory_space=pltpu.VMEM)
    hbm = pl.BlockSpec(memory_space=pl.ANY)
    shape = jax.ShapeDtypeStruct
    return pl.pallas_call(
        ffn_kernel,
        in_specs=[hbm] * 7,
        out_specs=[vmem] * 2 + [hbm] * 5,
        out_shape=[
            shape((rows, width), full),
            shape((unit, width), full),
            shape((3, block, 2 * units), low),
            shape((2, block, units), low),
            shape((group, width), low),
            shape((4, unit, width), low),
            shape((4, block, 2 * units), low),
        ],
        scratch_shapes=[
            pltpu.VMEM((group, width), low),
            pltpu.VMEM((group, width), low),
            pltpu.VMEM((width, 2 * units), low),
            pltpu.VMEM((units, width), low),
            pltpu.VMEM((group, units), low),
            pltpu.VMEM((group, 2 * units), low),
            pltpu.VMEM((group, width), low),
            pltpu.VMEM((rows, width), low),
            pltpu.VMEM((2, rows, width), low),
            pltpu.VMEM((2, rows, width), low),
            pltpu.VMEM((2, unit, half), low),
            pltpu.VMEM((2, unit, half), low),
            pltpu.VMEM((2, unit, half), low),
            pltpu.VMEM((unit, width), low),
            pltpu.SemaphoreType.DMA((36,)),
            pltpu.SemaphoreType.DMA((28,)),
            pltpu.SemaphoreType.DMA((28,)),
        ],
        compiler_params=pltpu.CompilerParams(
            collective_id=1, has_side_effects=True, vmem_limit_bytes=63 * 2**20
        ),
        name="ffn",
    )(normed_all, upstream_all, w_gu, w_down, hidden, factor_gate, factor_up)[:5]


def back_kernel(
    columns, resid, gain_two, cotangent, attended, queries, paired, slots, slot_row, first_row,
    logsum, normed_one, tokens, gain_one, cosine, sine, w_out, w_qkv, gu_sum, gu_far, branch,
    layer, input_rows, vector, grad_out, grad_qkv, gu_rows,
    out_w, qkv, gu_own, gu_to_y, gu_to_x, gu_x, gu_y, gu_ended,
    branch_v, z_one, z_two, z_three, working, bias, d_branch, d_attended, d_qkv, d_resid,
    keys_grad, values_grad, dkv, dkv_in,
    out_arrived, out_x, out_y, out_ended, qkv_arrived, qkv_x, qkv_y, qkv_ended,
    out_in, qkv_in, vector_in,
    load, ssem, rsem,
):
    f = lax.axis_index("fsdp")
    s = lax.axis_index("seq")
    rows, width = tokens.shape
    n_s = paired.shape[0]
    kv_width = KV_HEADS * HEAD_DIM
    repeat = HEADS // KV_HEADS
    scale = HEAD_DIM ** (-0.5)
    block = width // 8
    piece = block // n_s
    units = gu_sum.shape[2] // 2
    tile = 256
    full, low = jnp.float32, jnp.bfloat16
    plane = [f ^ k for k in range(8)]

    entry = pltpu.get_barrier_semaphore()
    for k in (1, 2, 4):
        pl.semaphore_signal(entry, inc=1, device_id={"fsdp": plane[k]}, device_id_type=MESH)
    for j in range(1, n_s):
        pl.semaphore_signal(
            entry, inc=1, device_id={"seq": lax.rem(s + j, n_s)}, device_id_type=MESH
        )

    def here(source, target, index):
        return pltpu.make_async_copy(source, target, load.at[index])

    def there(source, target, index, **device):
        return pltpu.make_async_remote_copy(
            src_ref=source, dst_ref=target, send_sem=ssem.at[index], recv_sem=rsem.at[index],
            device_id=device, device_id_type=MESH,
        )

    low_units, high_units = pl.ds(0, units), pl.ds(units, units)
    load_branch = here(branch, branch_v, 0)
    load_out = here(w_out, out_w, 1)
    load_gu = [
        here(gu_sum.at[0], gu_own, 2),
        here(gu_sum.at[2, :, low_units], gu_to_y, 3),
        here(gu_sum.at[1, :, high_units], gu_to_x, 4),
        here(gu_far.at[0], gu_x.at[1], 8),
        here(gu_far.at[1], gu_y.at[1], 9),
    ]
    load_qkv = here(w_qkv, qkv, 5)
    load_columns = here(columns, working, 7)
    for copy in [load_columns, load_branch, load_out] + load_gu + [load_qkv]:
        copy.start()

    gu_first = [
        there(gu_sum.at[1, :, low_units], gu_x.at[0], 2, fsdp=plane[2]),
        there(gu_sum.at[2, :, high_units], gu_y.at[0], 3, fsdp=plane[4]),
    ]
    gu_second = [
        there(gu_to_y, gu_ended.at[0], 4, fsdp=plane[4]),
        there(gu_to_x, gu_ended.at[1], 5, fsdp=plane[2]),
    ]

    def around(j):
        return {"seq": lax.rem(s + j, n_s)}

    def rows_for(ref, first, j):
        owner = lax.rem(s + j, n_s)
        return ref.at[pl.ds(pl.multiple_of(first + owner * piece, 16), piece)]

    gu_send = [there(rows_for(gu_own, 0, j), gu_rows.at[j], 5 + j, **around(j)) for j in range(1, n_s)]
    dkv_send = [
        [
            there(dkv.at[g, lax.rem(s + j, n_s)], dkv_in.at[g, j], 8 + 3 * g + j, **around(j))
            for j in range(1, n_s)
        ]
        for g in range(KV_HEADS)
    ]
    chain = SumChain(branch_v, rows, z_one, z_two, z_three, there, 16)
    sum_out = SumPlane(out_w, block, plane, out_arrived, out_x, out_y, out_ended, there, 24)
    sum_qkv = SumPlane(qkv, block, plane, qkv_arrived, qkv_x, qkv_y, qkv_ended, there, 36)
    out_send = [there(rows_for(out_w, f * block, j), out_in.at[j], 47 + j, **around(j)) for j in range(1, n_s)]
    qkv_send = [there(rows_for(qkv, f * block, j), qkv_in.at[j], 51 + j, **around(j)) for j in range(1, n_s)]
    vector_send = [
        there(vector_in.at[0], vector_in.at[1], 56, fsdp=plane[1]),
        there(vector_in.at[2], vector_in.at[3], 57, fsdp=plane[2]),
        there(vector_in.at[4], vector_in.at[5], 58, fsdp=plane[4]),
    ] + [there(vector_in.at[6], vector_in.at[6 + j], 58 + j, **around(j)) for j in range(1, n_s)]

    pl.semaphore_wait(entry, 3 + n_s - 1)
    for copy in gu_first:
        copy.start()
    load_branch.wait()
    chain.two()
    for copy in load_gu:
        copy.wait()
    gu_to_y[...] = (gu_to_y[...].astype(full) + gu_x[1].astype(full)).astype(low)
    gu_second[0].start()
    gu_to_x[...] = (gu_to_x[...].astype(full) + gu_y[1].astype(full)).astype(low)
    gu_second[1].start()

    def norm_back(value, gain, grad):
        root = lax.rsqrt(jnp.mean(value * value, -1, keepdims=True) + epsilon)
        scaled = gain * grad
        inner = jnp.mean(scaled * value, -1, keepdims=True)
        gain_grad = jnp.sum(grad * (value * root), 0, keepdims=True)
        return root * scaled - value * (root * root * root * inner), gain_grad

    load_columns.wait()
    d_norm, gain_two_grad = norm_back(resid[...], gain_two[...], working[...])
    d_total = cotangent[...].astype(full) + d_norm
    d_branch[...] = d_total.astype(low)
    d_resid[...] = d_total
    for j in range(n_s):
        keys_slot = slots[j]
        keys_slot = jnp.concatenate([keys_slot] * (rows // 128), 1)
        ok = (keys_slot <= slot_row[0:1]) & (keys_slot >= first_row[0:1])
        bias[j * rows : (j + 1) * rows] = jnp.where(ok, 0.0, -1e30)
    load_out.wait()
    for n in range(width // tile):
        value = lax.dot_general(
            d_branch[...], out_w[n * tile : (n + 1) * tile], (((1,), (1,)), ((), ())),
            preferred_element_type=full,
        )
        d_attended[:, n * tile : (n + 1) * tile] = value.astype(low)

    def turned_back(value):
        return value * cosine[...] + pltpu.roll(value * sine[...], HEAD_DIM // 2, 1)

    for g in range(KV_HEADS):
        keys = paired[:, :, g * HEAD_DIM : (g + 1) * HEAD_DIM].reshape(n_s * rows, HEAD_DIM)
        values = paired[:, :, kv_width + g * HEAD_DIM : kv_width + (g + 1) * HEAD_DIM]
        values = values.reshape(n_s * rows, HEAD_DIM)
        keys_grad[...] = jnp.zeros_like(keys_grad)
        values_grad[...] = jnp.zeros_like(values_grad)

        def head(i, carry, g=g, keys=keys, values=values):
            h = g * repeat + i
            head_columns = pl.ds(pl.multiple_of(h * HEAD_DIM, HEAD_DIM), HEAD_DIM)
            query = queries[:, head_columns]
            grad = d_attended[:, head_columns]
            raw = lax.dot_general(
                keys, query, (((1,), (1,)), ((), ())), preferred_element_type=full
            )
            logs = logsum[pl.ds(pl.multiple_of(h * 8, 8), 8)][0:1]
            probs = jnp.exp(raw * scale + bias[...] - logs)
            d_probs = lax.dot_general(
                values, grad, (((1,), (1,)), ((), ())), preferred_element_type=full
            )
            delta = jnp.sum(probs * d_probs, 0, keepdims=True)
            d_score = (probs * (d_probs - delta)).astype(low)
            turned = lax.dot_general(
                keys, d_score, (((0,), (0,)), ((), ())), preferred_element_type=full
            )
            d_qkv[:, head_columns] = turned_back((turned * scale).T).astype(low)
            keys_grad[...] += jnp.dot(d_score, query, preferred_element_type=full) * scale
            values_grad[...] += jnp.dot(probs.astype(low), grad, preferred_element_type=full)
            return carry

        lax.fori_loop(0, repeat, head, 0)
        dkv[g, :, :, :HEAD_DIM] = keys_grad[...].astype(low).reshape(n_s, rows, HEAD_DIM)
        dkv[g, :, :, HEAD_DIM:] = values_grad[...].astype(low).reshape(n_s, rows, HEAD_DIM)
        for copy in dkv_send[g]:
            copy.start()

    turned = attended[...].T
    for n in range(width // tile):
        n_columns = slice(n * tile, (n + 1) * tile)
        value = jnp.dot(turned, d_branch[:, n_columns], preferred_element_type=full)
        out_w[:, n_columns] = value.astype(low)
    sum_out.start_core()
    load_qkv.wait()

    def back_one(first, count, start):
        for n in range(width // tile):
            n_rows = slice(n * tile, (n + 1) * tile)
            value = lax.dot_general(
                d_qkv[:, first : first + count], qkv[n_rows, first : first + count],
                (((1,), (1,)), ((), ())), preferred_element_type=full,
            )
            working[:, n_rows] = value if start else working[:, n_rows] + value

    back_one(0, width, True)
    normed_turned = normed_one[...].T
    for n in range(width // tile):
        n_columns = slice(n * tile, (n + 1) * tile)
        value = jnp.dot(normed_turned, d_qkv[:, n_columns], preferred_element_type=full)
        qkv[:, n_columns] = value.astype(low)
    sum_out.start_first()

    for g in range(KV_HEADS):
        for copy in dkv_send[g]:
            copy.wait_recv()
        total = dkv[g, s].astype(full)
        for j in range(1, n_s):
            total = total + dkv_in[g, j].astype(full)
        key_columns = slice(width + g * HEAD_DIM, width + (g + 1) * HEAD_DIM)
        value_columns = slice(width + kv_width + g * HEAD_DIM, width + kv_width + (g + 1) * HEAD_DIM)
        d_qkv[:, key_columns] = turned_back(total[:, :HEAD_DIM]).astype(low)
        d_qkv[:, value_columns] = total[:, HEAD_DIM:].astype(low)
    back_one(width, 2 * kv_width, False)
    value = jnp.dot(normed_turned, d_qkv[:, width:], preferred_element_type=full)
    qkv[:, width:] = value.astype(low)
    sum_qkv.start_core()
    chain.three()

    d_norm, gain_one_grad = norm_back(tokens[...].astype(full), gain_one[...], working[...])
    input_rows[...] = (d_resid[...] + d_norm).astype(low)
    bias_grad = jnp.sum(d_qkv[...].astype(full), 0, keepdims=True)
    vectors = jnp.concatenate([gain_one_grad, gain_two_grad, bias_grad], 1)
    part = vectors.shape[1] // 8
    for r in range(8):
        vector_in[0, r : r + 1] = vectors[:, r * part : (r + 1) * part]
    vector_send[0].start()
    sum_qkv.start_first()
    vector_send[0].wait_recv()
    vector_in[2] = vector_in[0] + vector_in[1]
    vector_send[1].start()

    gu_first[0].wait_recv()
    gu_second[0].wait_recv()
    total = gu_own[:, :units].astype(full) + gu_x[0].astype(full) + gu_ended[0].astype(full)
    gu_own[:, :units] = total.astype(low)
    gu_first[1].wait_recv()
    gu_second[1].wait_recv()
    total = gu_own[:, units:].astype(full) + gu_y[0].astype(full) + gu_ended[1].astype(full)
    gu_own[:, units:] = total.astype(low)
    for copy in gu_send:
        copy.start()
    keep_rows = here(rows_for(gu_own, 0, 0), gu_rows.at[0], 6)
    keep_rows.start()
    sum_out.start_second()
    vector_send[1].wait_recv()
    vector_in[4] = vector_in[2] + vector_in[3]
    vector_send[2].start()

    sum_qkv.start_second()
    sum_out.finish()
    for copy in out_send:
        copy.start()
    vector_send[2].wait_recv()
    vector_in[6] = vector_in[4] + vector_in[5]
    for copy in vector_send[3:]:
        copy.start()
    chain.last(working)
    layer[...] = (resid[...] + working[...]).astype(low)
    sum_qkv.finish()
    for copy in qkv_send:
        copy.start()

    def gathered(own, copies, arrived, out):
        total = own[...].astype(full)
        for copy in copies:
            copy.wait_recv()
        for j in range(1, n_s):
            total = total + arrived[j].astype(full)
        out[...] = total

    gathered(rows_for(out_w, f * block, 0), out_send, out_in, grad_out)
    for copy in vector_send[3:]:
        copy.wait_recv()
    vector[...] = vector_in[6] + vector_in[7] + vector_in[8] + vector_in[9]
    gathered(rows_for(qkv, f * block, 0), qkv_send, qkv_in, grad_qkv)
    for copy in gu_send:
        copy.wait_recv()
    keep_rows.wait()
    chain.sent()
    sum_out.sent()
    sum_qkv.sent()
    for copy in gu_first + gu_second + gu_send + out_send + qkv_send + vector_send:
        copy.wait_send()
    for g in range(KV_HEADS):
        for copy in dkv_send[g]:
            copy.wait_send()


def back(
    columns, resid, gain_two, cotangent, attended, queries, paired, slots, slot_row, first_row,
    logsum, normed_one, tokens, gain_one, cosine, sine, w_out, w_qkv, gu_sum, gu_far, branch,
):
    rows, width = tokens.shape
    n_s = paired.shape[0]
    group = n_s * rows
    kv_width = KV_HEADS * HEAD_DIM
    qkv_width = width + 2 * kv_width
    block = width // 8
    piece = block // n_s
    units = gu_sum.shape[2] // 2
    low, full = jnp.bfloat16, jnp.float32
    vmem = pl.BlockSpec(memory_space=pltpu.VMEM)
    hbm = pl.BlockSpec(memory_space=pl.ANY)
    shape = jax.ShapeDtypeStruct
    vectors = (2 * width + qkv_width) // 8
    return pl.pallas_call(
        back_kernel,
        in_specs=[hbm] + [vmem] * 15 + [hbm] * 5,
        out_specs=[vmem] * 5 + [hbm],
        out_shape=[
            shape((rows, width), low),
            shape((rows, width), low),
            shape((8, vectors), full),
            shape((piece, width), full),
            shape((piece, qkv_width), full),
            shape((n_s, piece, 2 * units), low),
        ],
        scratch_shapes=[
            pltpu.VMEM((width, width), low),
            pltpu.VMEM((width, qkv_width), low),
            pltpu.VMEM((block, 2 * units), low),
            pltpu.VMEM((block, units), low),
            pltpu.VMEM((block, units), low),
            pltpu.VMEM((2, block, units), low),
            pltpu.VMEM((2, block, units), low),
            pltpu.VMEM((2, block, units), low),
            pltpu.VMEM((group, width), low),
            pltpu.VMEM((rows, width), low),
            pltpu.VMEM((2, rows, width), low),
            pltpu.VMEM((2, rows, width), low),
            pltpu.VMEM((rows, width), full),
            pltpu.VMEM((group, rows), full),
            pltpu.VMEM((rows, width), low),
            pltpu.VMEM((rows, width), low),
            pltpu.VMEM((rows, qkv_width), low),
            pltpu.VMEM((rows, width), full),
            pltpu.VMEM((group, HEAD_DIM), full),
            pltpu.VMEM((group, HEAD_DIM), full),
            pltpu.VMEM((KV_HEADS, n_s, rows, 2 * HEAD_DIM), low),
            pltpu.VMEM((KV_HEADS, n_s, rows, 2 * HEAD_DIM), low),
            pltpu.VMEM((4, block, width), low),
            pltpu.VMEM((2, block, width // 2), low),
            pltpu.VMEM((2, block, width // 2), low),
            pltpu.VMEM((2, block, width // 2), low),
            pltpu.VMEM((4, block, qkv_width), low),
            pltpu.VMEM((2, block, qkv_width // 2), low),
            pltpu.VMEM((2, block, qkv_width // 2), low),
            pltpu.VMEM((2, block, qkv_width // 2), low),
            pltpu.VMEM((n_s, piece, width), low),
            pltpu.VMEM((n_s, piece, qkv_width), low),
            pltpu.VMEM((10, 8, vectors), full),
            pltpu.SemaphoreType.DMA((10,)),
            pltpu.SemaphoreType.DMA((64,)),
            pltpu.SemaphoreType.DMA((64,)),
        ],
        compiler_params=pltpu.CompilerParams(
            collective_id=2, has_side_effects=True, vmem_limit_bytes=63 * 2**20
        ),
        name="back",
    )(
        columns, resid, gain_two, cotangent, attended, queries, paired, slots, slot_row, first_row,
        logsum, normed_one, tokens, gain_one, cosine, sine, w_out, w_qkv, gu_sum, gu_far, branch,
    )


def finish_kernel(
    layer, input_rows, grad_out, grad_qkv, grad_down, gu_rows,
    layer_out, input_grad, out_out, query_out, key_out, value_out, down_out, gate_out, up_out,
):
    s = lax.axis_index("seq")
    n_s = gu_rows.shape[0]
    width = grad_out.shape[1]
    kv_width = KV_HEADS * HEAD_DIM
    unit_pad = grad_down.shape[0]
    unit = down_out.shape[0]
    units = gu_rows.shape[2] // 2
    layer_out[...] = layer[...]
    input_grad[...] = input_rows[...]
    out_out[...] = grad_out[...]
    query_out[...] = grad_qkv[:, :width]
    key_out[...] = grad_qkv[:, width : width + kv_width]
    value_out[...] = grad_qkv[:, width + kv_width :]
    down_out[...] = grad_down[:unit]
    window = 512
    lanes = lax.broadcasted_iota(jnp.int32, (gu_rows.shape[1], 128), 1)
    for base, out in ((0, gate_out), (units, up_out)):
        for f in range(units // unit_pad):
            for owner in range(n_s):
                source = base + f * unit_pad
                begin = min(source // 128 * 128, 2 * units - window)
                target = (f * n_s + owner) * unit
                first = target // 128 * 128
                slot = lax.rem(s + n_s - owner, n_s)
                value = gu_rows[slot, :, begin : begin + window].astype(jnp.float32)
                turn = ((target - first) - (source - begin)) % window
                if turn:
                    value = pltpu.roll(value, turn, 1)
                for t in range(first, min(target + unit, out.shape[1]), 128):
                    part = value[:, t - first : t - first + 128]
                    if t < target:
                        part = jnp.where(lanes >= target - t, part, out[:, t : t + 128])
                    out[:, t : t + 128] = part


def finish(layer, input_rows, grad_out, grad_qkv, grad_down, gu_rows, unit, hidden_width):
    piece, width = grad_out.shape
    kv_width = KV_HEADS * HEAD_DIM
    low, full = jnp.bfloat16, jnp.float32
    shape = jax.ShapeDtypeStruct
    vmem = pl.BlockSpec(memory_space=pltpu.VMEM)
    return pl.pallas_call(
        finish_kernel,
        in_specs=[vmem] * 6,
        out_specs=[vmem] * 9,
        out_shape=[
            shape(layer.shape, low),
            shape(layer.shape, low),
            shape((piece, width), full),
            shape((piece, width), full),
            shape((piece, kv_width), full),
            shape((piece, kv_width), full),
            shape((unit, width), full),
            shape((piece, hidden_width), full),
            shape((piece, hidden_width), full),
        ],
        compiler_params=pltpu.CompilerParams(vmem_limit_bytes=63 * 2**20),
        name="finish",
    )(layer, input_rows, grad_out, grad_qkv, grad_down, gu_rows)


def per_device(
    tokens, cotangent, lengths, balance, norm1_gain, w_query, b_query, w_key, b_key,
    w_value, b_value, w_out, norm2_gain, w_gate, w_up, w_down,
):
    seq_count = lax.axis_size("seq")
    fsdp_count = lax.axis_size("fsdp")
    seq_rank = lax.axis_index("seq")
    fsdp_rank = lax.axis_index("fsdp")
    rows_here, width = tokens.shape
    kv_width = KV_HEADS * HEAD_DIM
    hidden_width = w_gate.shape[1]
    unit = hidden_width // (fsdp_count * seq_count)
    (
        weight_gu, weight_down, upstream_all, normed_all, hidden, factor_gate, factor_up,
        weight_qkv, weight_out, queries, paired, slots, logsum, attended, resid, normed_one,
        gain_one, gain_two, slot_row, first_row, cosine, sine,
    ) = front(
        tokens, cotangent, lengths, balance, (norm1_gain, norm2_gain, b_query, b_key, b_value),
        (w_query, w_key, w_value, w_out, w_gate, w_up, w_down),
    )
    columns, grad_down, gu_sum, gu_far, branch = ffn(
        normed_all, upstream_all, weight_gu, weight_down, hidden, factor_gate, factor_up
    )
    layer, input_rows, vectors, grad_out, grad_qkv, gu_rows = back(
        columns, resid, gain_two, cotangent, attended, queries, paired, slots, slot_row, first_row,
        logsum, normed_one, tokens, gain_one, cosine, sine, weight_out, weight_qkv, gu_sum, gu_far,
        branch,
    )
    (
        layer_out, input_grad, grad_out, grad_query, grad_key, grad_value, grad_down, grad_gate,
        grad_up,
    ) = finish(layer, input_rows, grad_out, grad_qkv, grad_down, gu_rows, unit, hidden_width)
    vectors = vectors.reshape(-1)
    own = width // (fsdp_count * seq_count)
    first = (fsdp_rank * seq_count + seq_rank) * own

    def own_part(offset):
        return lax.dynamic_slice_in_dim(vectors, offset + first, own, 0)

    biases = 2 * width
    return (
        layer_out,
        input_grad,
        own_part(0),
        grad_query,
        own_part(biases),
        grad_key,
        vectors[biases + width : biases + width + kv_width],
        grad_value,
        vectors[biases + width + kv_width :],
        grad_out,
        own_part(width),
        grad_gate,
        grad_up,
        grad_down,
    )


def solution(mesh):
    both = P(("fsdp", "seq"), None)
    both_one = P(("fsdp", "seq"))
    placed = (
        both, both, P("fsdp", None), both_one, P("fsdp"), P("fsdp", None), P("fsdp"),
        P("fsdp", None), P("fsdp"), P("fsdp", None), P("fsdp"), P("fsdp", None), P("fsdp"),
        P("fsdp", None), P("fsdp", None), P("fsdp", None),
    )
    return jax.shard_map(
        per_device if mesh.shape["fsdp"] == 8 else plain_device,
        mesh=mesh,
        in_specs=placed,
        out_specs=(
            both, both, both_one, both, both_one, both, P(), both, P(), both, both_one,
            both, both, both,
        ),
        check_vma=False,
    )
```

```python
import jax
import jax.numpy as jnp
import numpy as np
from jax import lax
from jax.experimental import pallas as pl
from jax.experimental.pallas import tpu as pltpu
from jax.sharding import PartitionSpec as P

HEADS = 12
KV_HEADS = 2
HEAD_DIM = 128

MESH = pl.DeviceIdType.MESH

epsilon = 1e-06
rope_base = 1000000.0


def norm_piece(values, gain):
    return values * lax.rsqrt(jnp.mean(values * values, -1, keepdims=True) + epsilon) * gain


def rope_tables(position):
    half = HEAD_DIM // 2
    inverse = rope_base ** (-(jnp.arange(half, dtype=jnp.float32) * 2.0 / HEAD_DIM))
    angle = position.astype(jnp.float32)[:, None] * inverse[None, :]
    cosine = jnp.concatenate([jnp.cos(angle), jnp.cos(angle)], -1)
    sine = jnp.concatenate([jnp.sin(angle), jnp.sin(angle)], -1)
    return (cosine, sine)


def turn_half(values):
    half = values.shape[-1] // 2
    return jnp.concatenate([-values[..., half:], values[..., :half]], -1)


def rotate(values, cosine, sine):
    return values * cosine[:, None, :] + turn_half(values) * sine[:, None, :]


def rotate_back(grads, cosine, sine):
    return grads * cosine[:, None, :] - turn_half(grads * sine[:, None, :])


def segment_of(slots, starts):
    return (slots >= starts[1]).astype(jnp.int32) + (slots >= starts[2]).astype(jnp.int32)


def contract_rows(left, right):
    return lax.dot_general(
        left, right, (((0,), (0,)), ((), ())), preferred_element_type=jnp.float32
    )


def contract_columns(left, right):
    return lax.dot_general(
        left, right, (((1,), (1,)), ((), ())), preferred_element_type=jnp.float32
    )


def plain_device(
    tokens, cotangent, lengths, balance, norm1_gain, w_query, b_query, w_key, b_key,
    w_value, b_value, w_out, norm2_gain, w_gate, w_up, w_down,
):
    seq_count = lax.axis_size("seq")
    fsdp_count = lax.axis_size("fsdp")
    seq_rank = lax.axis_index("seq")
    rows_here, width = tokens.shape
    group = seq_count * rows_here
    kv_width = KV_HEADS * HEAD_DIM
    qkv_width = width + 2 * kv_width
    hidden_width = w_gate.shape[1]
    unit = hidden_width // (fsdp_count * seq_count)
    own_units = hidden_width // seq_count
    weight_rows = w_gate.shape[0]
    score_scale = HEAD_DIM ** (-0.5)
    repeat = HEADS // KV_HEADS

    slot = balance % group
    slots_all = lax.all_gather(slot, "seq", axis=0, tiled=True)
    seq_lengths = lengths[0]
    starts = jnp.cumsum(seq_lengths) - seq_lengths
    segment = segment_of(slot, starts)
    segments_all = segment_of(slots_all, starts)
    first_row = jnp.where(segment == 0, starts[0], jnp.where(segment == 1, starts[1], starts[2]))
    cosine, sine = rope_tables(slot - first_row)
    allowed = (segment[:, None] == segments_all[None, :]) & (slots_all[None, :] <= slot[:, None])

    small = jnp.concatenate([norm1_gain, norm2_gain, b_query, b_key, b_value], 0)[None]
    small = lax.all_gather(small, "fsdp", axis=0, tiled=True)
    piece = norm1_gain.shape[0]
    bias_piece = b_key.shape[0]
    gain_one = small[:, :piece].reshape(-1).astype(jnp.float32)
    gain_two = small[:, piece : 2 * piece].reshape(-1).astype(jnp.float32)
    bias_qkv = jnp.concatenate(
        [
            small[:, 2 * piece : 3 * piece].reshape(-1),
            small[:, 3 * piece : 3 * piece + bias_piece].reshape(-1),
            small[:, 3 * piece + bias_piece :].reshape(-1),
        ],
        0,
    ).astype(jnp.float32)
    weight_qkv = lax.all_gather(
        jnp.concatenate([w_query, w_key, w_value], 1), "fsdp", axis=0, tiled=True
    )
    weight_out = lax.all_gather(w_out, "fsdp", axis=0, tiled=True)
    upstream_all = lax.all_gather(cotangent, "seq", axis=0, tiled=True)

    def own_columns(weight):
        cut = weight.reshape(weight_rows, fsdp_count, seq_count, unit)
        return lax.dynamic_index_in_dim(cut, seq_rank, 2, False).reshape(weight_rows, own_units)

    weight_gu = lax.all_gather(
        jnp.concatenate([own_columns(w_gate), own_columns(w_up)], 1), "fsdp", axis=0, tiled=True
    )
    weight_down = lax.all_gather(
        lax.dynamic_slice_in_dim(w_down, seq_rank * unit, unit, 0), "fsdp", axis=0, tiled=True
    )

    inputs = tokens.astype(jnp.float32)
    normed_one = norm_piece(inputs, gain_one).astype(jnp.bfloat16)
    projected = jnp.dot(normed_one, weight_qkv, preferred_element_type=jnp.float32) + bias_qkv
    query_pre = projected[:, :width].reshape(rows_here, HEADS, HEAD_DIM)
    key_pre = projected[:, width : width + kv_width].reshape(rows_here, KV_HEADS, HEAD_DIM)
    value_pre = projected[:, width + kv_width :]
    queries = rotate(query_pre, cosine, sine).astype(jnp.bfloat16)
    keys = rotate(key_pre, cosine, sine).astype(jnp.bfloat16).reshape(rows_here, kv_width)
    values = value_pre.astype(jnp.bfloat16)
    paired = lax.all_gather(jnp.concatenate([keys, values], 1), "seq", axis=0, tiled=True)
    keys_all = paired[:, :kv_width].reshape(group, KV_HEADS, HEAD_DIM)
    values_all = paired[:, kv_width:].reshape(group, KV_HEADS, HEAD_DIM)
    grouped = queries.reshape(rows_here, KV_HEADS, repeat, HEAD_DIM)
    raw = (
        jnp.einsum("qgrd,kgd->grqk", grouped, keys_all, preferred_element_type=jnp.float32)
        * score_scale
    )
    scores = jnp.where(allowed, raw, -jnp.inf)
    expo = jnp.exp(scores - jnp.max(scores, -1, keepdims=True))
    probs = expo / jnp.sum(expo, -1, keepdims=True)
    probs_low = probs.astype(jnp.bfloat16)
    attended = jnp.einsum(
        "grqk,kgd->qgrd", probs_low, values_all, preferred_element_type=jnp.float32
    )
    attended = attended.astype(jnp.bfloat16).reshape(rows_here, width)
    resid = inputs + jnp.dot(attended, weight_out, preferred_element_type=jnp.float32)
    normed_two = norm_piece(resid, gain_two).astype(jnp.bfloat16)

    normed_all = lax.all_gather(normed_two, "seq", axis=0, tiled=True)
    both = jnp.dot(normed_all, weight_gu, preferred_element_type=jnp.float32)
    gate = both[:, :own_units]
    up = both[:, own_units:]
    sigma = jax.nn.sigmoid(gate)
    activated = gate * sigma
    hidden = (activated * up).astype(jnp.bfloat16)
    d_hidden = contract_columns(upstream_all, weight_down)
    d_gate = (d_hidden * up * sigma * (1.0 + gate * (1.0 - sigma))).astype(jnp.bfloat16)
    d_up = (d_hidden * activated).astype(jnp.bfloat16)
    d_both = jnp.concatenate([d_gate, d_up], 1)
    columns = lax.psum_scatter(
        contract_columns(d_both, weight_gu).astype(jnp.bfloat16),
        "seq", scatter_dimension=0, tiled=True,
    ).astype(jnp.float32)
    branch = lax.psum_scatter(
        jnp.dot(hidden, weight_down, preferred_element_type=jnp.float32).astype(jnp.bfloat16),
        "seq", scatter_dimension=0, tiled=True,
    ).astype(jnp.float32)
    layer_out = (resid + branch).astype(jnp.bfloat16)
    grad_down = lax.psum_scatter(
        contract_rows(hidden, upstream_all).astype(jnp.bfloat16),
        "fsdp", scatter_dimension=0, tiled=True,
    ).astype(jnp.float32)
    grad_pair = lax.psum_scatter(
        contract_rows(normed_all, d_both).astype(jnp.bfloat16),
        "fsdp", scatter_dimension=0, tiled=True,
    )
    grad_pair = lax.all_to_all(grad_pair, "seq", split_axis=0, concat_axis=0, tiled=True)
    grad_pair = grad_pair.reshape(seq_count, weight_rows // seq_count, 2, fsdp_count, unit)
    grad_pair = grad_pair.transpose(2, 1, 3, 0, 4).astype(jnp.float32)
    grad_pair = grad_pair.reshape(2, weight_rows // seq_count, hidden_width)

    _, pull_two = jax.vjp(norm_piece, resid, gain_two)
    d_resid_norm, grad_gain_two = pull_two(columns)
    d_resid = cotangent.astype(jnp.float32) + d_resid_norm
    d_branch = d_resid.astype(jnp.bfloat16)
    grad_out = contract_rows(attended, d_branch).astype(jnp.bfloat16)
    d_attended = contract_columns(d_branch, weight_out).astype(jnp.bfloat16)
    d_attended = d_attended.reshape(rows_here, KV_HEADS, repeat, HEAD_DIM)
    d_probs = jnp.einsum(
        "qgrd,kgd->grqk", d_attended, values_all, preferred_element_type=jnp.float32
    )
    delta = jnp.sum(probs * d_probs, -1, keepdims=True)
    d_score = (probs * (d_probs - delta)).astype(jnp.bfloat16)
    d_queries = (
        jnp.einsum("grqk,kgd->qgrd", d_score, keys_all, preferred_element_type=jnp.float32)
        * score_scale
    )
    d_keys = (
        jnp.einsum("grqk,qgrd->kgd", d_score, grouped, preferred_element_type=jnp.float32)
        * score_scale
    )
    d_values = jnp.einsum(
        "grqk,qgrd->kgd", probs_low, d_attended, preferred_element_type=jnp.float32
    )
    d_paired = jnp.concatenate([d_keys.reshape(group, kv_width), d_values.reshape(group, kv_width)], 1)
    d_paired = lax.psum_scatter(
        d_paired.astype(jnp.bfloat16), "seq", scatter_dimension=0, tiled=True
    ).astype(jnp.float32)
    d_query_pre = rotate_back(
        d_queries.reshape(rows_here, HEADS, HEAD_DIM), cosine, sine
    ).astype(jnp.bfloat16)
    d_key_pre = rotate_back(
        d_paired[:, :kv_width].reshape(rows_here, KV_HEADS, HEAD_DIM), cosine, sine
    ).astype(jnp.bfloat16)
    d_value_pre = d_paired[:, kv_width:].astype(jnp.bfloat16)
    d_qkv = jnp.concatenate(
        [
            d_query_pre.reshape(rows_here, width),
            d_key_pre.reshape(rows_here, kv_width),
            d_value_pre,
        ],
        1,
    )
    grad_qkv = contract_rows(normed_one, d_qkv).astype(jnp.bfloat16)
    grad_bias = jnp.sum(d_qkv.astype(jnp.float32), 0)
    d_normed_one = contract_columns(d_qkv, weight_qkv)
    _, pull_one = jax.vjp(norm_piece, inputs, gain_one)
    d_input_norm, grad_gain_one = pull_one(d_normed_one)
    input_grad = (d_resid + d_input_norm).astype(jnp.bfloat16)

    def summed(value):
        value = lax.psum_scatter(value, "fsdp", scatter_dimension=0, tiled=True)
        return lax.psum_scatter(value, "seq", scatter_dimension=0, tiled=True).astype(jnp.float32)

    grad_out = summed(grad_out)
    grad_qkv = summed(grad_qkv)
    vectors = lax.psum(
        jnp.concatenate([grad_gain_one, grad_gain_two, grad_bias], 0), ("fsdp", "seq")
    )
    own = width // (fsdp_count * seq_count)
    first = (lax.axis_index("fsdp") * seq_count + seq_rank) * own

    def own_part(offset):
        return lax.dynamic_slice_in_dim(vectors, offset + first, own, 0)

    biases = 2 * width
    return (
        layer_out,
        input_grad,
        own_part(0),
        grad_qkv[:, :width],
        own_part(biases),
        grad_qkv[:, width : width + kv_width],
        vectors[biases + width : biases + width + kv_width],
        grad_qkv[:, width + kv_width :],
        vectors[biases + width + kv_width :],
        grad_out,
        own_part(width),
        grad_pair[0],
        grad_pair[1],
        grad_down,
    )


ORDER = (1, 3, 2, 0)


class SumChain:
    def __init__(self, held, z_one, z_two, z_three, there, index):
        self.rank = lax.axis_index("seq")
        s = self.rank
        self.held, self.arrived = held, (z_one, z_two, z_three)
        self.up = [
            there(held(1), z_one, index, seq=s + 1),
            there(held(2), z_two.at[0], index + 2, seq=s + 1),
            there(held(3), z_three.at[0], index + 4, seq=s + 1),
        ]
        self.down = [
            there(held(3), z_one, index + 1, seq=s - 1),
            there(held(2), z_two.at[1], index + 3, seq=s - 1),
            there(held(1), z_three.at[1], index + 5, seq=s - 1),
        ]

    def add(self, j, arrived):
        ref = self.held(j)
        total = ref[...].astype(jnp.float32) + arrived[...].astype(jnp.float32)
        ref[...] = total.astype(jnp.bfloat16)

    def one(self):
        pl.when(self.rank == 0)(self.up[0].start)
        pl.when(self.rank == 3)(self.down[0].start)

    def add_one(self):
        @pl.when(self.rank == 1)
        def _():
            self.up[0].wait_recv()
            self.add(2, self.arrived[0])

        @pl.when(self.rank == 2)
        def _():
            self.down[0].wait_recv()
            self.add(2, self.arrived[0])

    def two(self):
        pl.when(self.rank <= 1)(self.up[1].start)
        pl.when(self.rank >= 2)(self.down[1].start)

    def three(self):
        @pl.when((self.rank == 1) | (self.rank == 2))
        def _():
            self.up[1].wait_recv()
            self.add(3, self.arrived[1].at[0])
            self.down[1].wait_recv()
            self.add(1, self.arrived[1].at[1])

        pl.when(self.rank <= 2)(self.up[2].start)
        pl.when(self.rank >= 1)(self.down[2].start)

    def last(self, out):
        out[...] = self.held(0)[...].astype(jnp.float32)

        @pl.when(self.rank >= 1)
        def _():
            self.up[2].wait_recv()
            out[...] += self.arrived[2][0].astype(jnp.float32)

        @pl.when(self.rank <= 2)
        def _():
            self.down[2].wait_recv()
            out[...] += self.arrived[2][1].astype(jnp.float32)

    def one_sent(self):
        pl.when(self.rank == 0)(self.up[0].wait_send)
        pl.when(self.rank == 3)(self.down[0].wait_send)

    def sent(self):
        pl.when(self.rank <= 1)(self.up[1].wait_send)
        pl.when(self.rank >= 2)(self.down[1].wait_send)
        pl.when(self.rank <= 2)(self.up[2].wait_send)
        pl.when(self.rank >= 1)(self.down[2].wait_send)


class SumPlane:
    def __init__(self, buffer, block, plane, arrived, by_x, by_y, ended, there, index):
        half = buffer.shape[1] // 2
        low, high = pl.ds(0, half), pl.ds(half, half)

        def part(k):
            return buffer.at[pl.ds(pl.multiple_of(plane[k] * block, 16), block)]

        self.parts = own, to_x, to_y, to_both = [part(k) for k in (0, 2, 4, 6)]
        self.arrived, self.by_x, self.by_y, self.ended, self.half = arrived, by_x, by_y, ended, half
        self.core = [
            there(part(2 * i + 1), arrived.at[i], index + i, fsdp=plane[1]) for i in range(4)
        ]
        self.first = [
            there(to_both.at[:, low], by_x.at[1], index + 5, fsdp=plane[2]),
            there(to_both.at[:, high], by_y.at[1], index + 7, fsdp=plane[4]),
            there(to_x.at[:, low], by_x.at[0], index + 4, fsdp=plane[2]),
            there(to_y.at[:, high], by_y.at[0], index + 6, fsdp=plane[4]),
        ]
        self.second = [
            there(to_y.at[:, low], ended.at[0], index + 8, fsdp=plane[4]),
            there(to_x.at[:, high], ended.at[1], index + 9, fsdp=plane[2]),
        ]

    def start_core(self):
        for copy in self.core:
            copy.start()

    def start_first(self):
        for i in (3, 1, 2, 0):
            self.core[i].wait_recv()
            part = self.parts[i]
            total = part[...].astype(jnp.float32) + self.arrived[i].astype(jnp.float32)
            part[...] = total.astype(jnp.bfloat16)
        for copy in self.first:
            copy.start()

    def start_second(self):
        half = self.half
        _, to_x, to_y, _ = self.parts
        self.first[0].wait_recv()
        total = to_y[:, :half].astype(jnp.float32) + self.by_x[1].astype(jnp.float32)
        to_y[:, :half] = total.astype(jnp.bfloat16)
        self.second[0].start()
        self.first[1].wait_recv()
        total = to_x[:, half:].astype(jnp.float32) + self.by_y[1].astype(jnp.float32)
        to_x[:, half:] = total.astype(jnp.bfloat16)
        self.second[1].start()

    def finish(self):
        half = self.half
        own = self.parts[0]
        self.first[2].wait_recv()
        self.second[0].wait_recv()
        total = own[:, :half].astype(jnp.float32) + self.by_x[0].astype(jnp.float32)
        own[:, :half] = (total + self.ended[0].astype(jnp.float32)).astype(jnp.bfloat16)
        self.first[3].wait_recv()
        self.second[1].wait_recv()
        total = own[:, half:].astype(jnp.float32) + self.by_y[0].astype(jnp.float32)
        own[:, half:] = (total + self.ended[1].astype(jnp.float32)).astype(jnp.bfloat16)

    def sent(self):
        for copy in self.core + self.first + self.second:
            copy.wait_send()


def in_order(partial, rows):
    def held(j):
        return partial.at[ORDER.index(j) * rows : (ORDER.index(j) + 1) * rows]

    return held


def front_kernel(
    lengths, tokens, cotangent, small, balance, inverse,
    w_query, w_key, w_value, w_out, w_gate, w_up, w_down,
    gu_all, down_all, upstream_all, normed_all, hidden, factor_gate, factor_up, qkv_out, out_out,
    queries, paired_out, slots_out, logsum, attended, resid, normed_one, gain_one, gain_two,
    slot_row, first_row, cosine, sine,
    q_w, kv_w, out_w, gate_v, up_v, gu, normed, kv, small_own, small_all, slots_all, bias,
    down_raw, down_own, hidden_v, gate_part, up_part,
    local, ssem, rsem, zsend, zrecv,
):
    f = lax.axis_index("fsdp")
    s = lax.axis_index("seq")
    rows, width = tokens.shape
    n_f, n_s = 8, slots_all.shape[0]
    group = n_s * rows
    block = w_query.shape[0]
    unit_pad = down_own.shape[0]
    unit = w_gate.shape[1] // (n_f * n_s)
    units = n_f * unit_pad
    kv_width = KV_HEADS * HEAD_DIM
    qkv_width = width + 2 * kv_width
    scale = HEAD_DIM ** (-0.5)
    repeat = HEADS // KV_HEADS
    plane = [f ^ k for k in range(n_f)]

    entry = pltpu.get_barrier_semaphore()
    for k in range(1, n_f):
        pl.semaphore_signal(entry, inc=1, device_id={"fsdp": plane[k]}, device_id_type=MESH)
    for j in range(1, n_s):
        pl.semaphore_signal(
            entry, inc=1, device_id={"seq": lax.rem(s + j, n_s)}, device_id_type=MESH
        )

    def here(source, target, index):
        return pltpu.make_async_copy(source, target, local.at[index])

    def there(source, target, index, **device):
        return pltpu.make_async_remote_copy(
            src_ref=source, dst_ref=target, send_sem=ssem.at[index], recv_sem=rsem.at[index],
            device_id=device, device_id_type=MESH,
        )

    def own_rows(ref, owner, size, start=0, count=None):
        first = pl.multiple_of(owner * size + start, 16)
        return ref.at[pl.ds(first, size if count is None else count)]

    class Gather:
        def __init__(self, source, target, size, index):
            half = size // 2
            x, y, c = plane[2], plane[4], plane[1]
            self.own = here(source, own_rows(target, f, size), index // 8) if source is not None else None
            if source is None:
                source = own_rows(target, f, size)
            mine = own_rows(target, f, size)
            self.first = [
                there(source, mine, index, fsdp=x),
                there(source, mine, index + 1, fsdp=y),
                there(source, mine, index + 2, fsdp=c),
            ]
            from_x, from_y = own_rows(target, x, size), own_rows(target, y, size)
            part_x = own_rows(target, x, size, 0, half)
            part_y = own_rows(target, y, size, half, half)
            self.second = [
                there(part_x, part_x, index + 3, fsdp=y),
                there(part_y, part_y, index + 4, fsdp=x),
                there(from_x, from_x, index + 5, fsdp=c),
                there(from_y, from_y, index + 6, fsdp=c),
            ]
            diagonal = own_rows(target, plane[6], size)
            self.third = there(diagonal, diagonal, index + 7, fsdp=c)

        def start(self):
            if self.own is not None:
                self.own.start()
            for copy in self.first:
                copy.start()

        def forward(self):
            self.first[0].wait_recv()
            self.second[0].start()
            self.second[2].start()
            self.first[1].wait_recv()
            self.second[1].start()
            self.second[3].start()

        def last(self):
            self.second[0].wait_recv()
            self.second[1].wait_recv()
            self.third.start()

        def finish(self):
            if self.own is not None:
                self.own.wait()
            self.first[2].wait_recv()
            self.second[2].wait_recv()
            self.second[3].wait_recv()
            self.third.wait_recv()

        def sent(self):
            for copy in self.first + self.second + [self.third]:
                copy.wait_send()

    class Chain:
        def __init__(self, target, index):
            self.steps = []
            for step in range(1, n_s):
                up = own_rows(target, s - (step - 1), rows)
                down = own_rows(target, s + (step - 1), rows)
                i = index + 2 * (step - 1)
                self.steps.append((
                    pltpu.make_async_remote_copy(
                        src_ref=up, dst_ref=up, send_sem=zsend.at[i], recv_sem=zrecv.at[i],
                        device_id={"seq": s + 1}, device_id_type=MESH,
                    ),
                    pltpu.make_async_remote_copy(
                        src_ref=down, dst_ref=down, send_sem=zsend.at[i + 1], recv_sem=zrecv.at[i + 1],
                        device_id={"seq": s - 1}, device_id_type=MESH,
                    ),
                    (s >= step - 1) & (s < n_s - 1),
                    (s >= 1) & (s <= n_s - step),
                    s >= step,
                    s <= n_s - 1 - step,
                ))

        def send(self, step):
            up, down, can_up, can_down, _, _ = self.steps[step - 1]
            pl.when(can_up)(up.start)
            pl.when(can_down)(down.start)

        def receive(self, step):
            up, down, _, _, from_below, from_above = self.steps[step - 1]
            pl.when(from_below)(up.wait_recv)
            pl.when(from_above)(down.wait_recv)

        def sent(self):
            for up, down, can_up, can_down, _, _ in self.steps:
                pl.when(can_up)(up.wait_send)
                pl.when(can_down)(down.wait_send)

    own_block = pl.ds(pl.multiple_of(f * block, 16), block)
    pieces = [
        here(w_key, kv_w.at[own_block, pl.ds(0, kv_width)], 6),
        here(w_value, kv_w.at[own_block, pl.ds(kv_width, kv_width)], 7),
        here(w_query, q_w.at[own_block], 5),
        here(cotangent, own_rows(upstream_all, s, rows), 8),
    ]
    load_gate = here(w_gate, gate_v, 9)
    load_up = here(w_up, up_v, 10)
    first_unit = pl.multiple_of(s * unit // 16 * 16, 16)
    load_down = here(w_down.at[pl.ds(first_unit, unit_pad)], down_raw, 15)
    for copy in pieces:
        copy.start()
    load_gate.start()
    load_up.start()
    load_down.start()

    slot = (balance[...] & (group - 1)).astype(jnp.float32)
    second = lengths[0, 0].astype(jnp.float32)
    third = (lengths[0, 0] + lengths[0, 1]).astype(jnp.float32)
    first = jnp.where(slot >= third, third, jnp.where(slot >= second, second, 0.0))
    slot_row[...] = jnp.broadcast_to(slot, slot_row.shape)
    first_row[...] = jnp.broadcast_to(first, first_row.shape)
    slots_all[s] = jnp.broadcast_to(slot, (128, rows)).T
    lanes = lax.broadcasted_iota(jnp.int32, small.shape, 1)
    sorts = lax.broadcasted_iota(jnp.int32, small.shape, 0)
    small_own[...] = jnp.where(
        sorts < 3,
        pltpu.roll(small[...], lax.rem(f, 2) * block, 1),
        pltpu.roll(small[...], f * (kv_width // n_f), 1),
    )
    small_all[f] = small_own[...]

    gather_kv = Gather(None, kv_w, block, 0)
    gather_q = Gather(None, q_w, block, 8)
    gather_out = Gather(w_out, out_w, block, 16)
    gather_gu = Gather(None, gu, block, 24)
    gather_down = Gather(down_own, down_all, unit_pad, 32)
    chain_up = Chain(upstream_all, 0)
    chain_normed = Chain(normed, 6)
    send_small = [
        there(small_own, small_all.at[f], 40 + k, fsdp=plane[k]) for k in range(1, n_f)
    ]
    send_slots = [
        there(slots_all.at[s], slots_all.at[s], 48 + j, seq=lax.rem(s + j, n_s))
        for j in range(1, n_s)
    ]
    send_kv = [
        there(kv.at[s], kv.at[s], 52 + j, seq=lax.rem(s + j, n_s)) for j in range(1, n_s)
    ]
    for copy in pieces[:2]:
        copy.wait()
    pl.semaphore_wait(entry, n_f - 1 + n_s - 1)
    gather_kv.start()
    for copy in send_small + send_slots:
        copy.start()
    for copy in pieces[2:]:
        copy.wait()
    position = slots_all[s] - jnp.broadcast_to(first, (128, rows)).T
    angle = position * inverse[...]
    cosine[...] = jnp.cos(angle)
    sine[...] = jnp.where(
        lax.broadcasted_iota(jnp.int32, angle.shape, 1) < HEAD_DIM // 2, -1.0, 1.0
    ) * jnp.sin(angle)

    for copy in send_small + send_slots:
        copy.wait_recv()

    def joined(sort):
        return jnp.concatenate(
            [
                small_all[2 * i, sort : sort + 1] + small_all[2 * i + 1, sort : sort + 1]
                for i in range(n_f // 2)
            ],
            1,
        )

    gain_one[...] = joined(0)
    gain_two[...] = joined(1)
    bias_query = joined(2)
    bias_key = sum(small_all[i, 3:4, :kv_width] for i in range(n_f))
    bias_value = sum(small_all[i, 4:5, :kv_width] for i in range(n_f))

    inputs = tokens[...].astype(jnp.float32)
    root = lax.rsqrt(jnp.mean(inputs * inputs, -1, keepdims=True) + epsilon)
    normed_one[...] = (inputs * root * gain_one[...]).astype(jnp.bfloat16)
    gather_kv.forward()
    gather_q.start()
    gather_kv.last()
    gather_kv.finish()

    def turned(value):
        return value * cosine[...] + pltpu.roll(value, HEAD_DIM // 2, 1) * sine[...]

    rows_low = normed_one[...]
    pair = jnp.dot(rows_low, kv_w[:, :kv_width], preferred_element_type=jnp.float32)
    pair = pair + bias_key
    for g in range(KV_HEADS):
        columns = slice(g * HEAD_DIM, (g + 1) * HEAD_DIM)
        kv[s, :, columns] = turned(pair[:, columns]).astype(jnp.bfloat16)
    pair = jnp.dot(rows_low, kv_w[:, kv_width:], preferred_element_type=jnp.float32)
    kv[s, :, kv_width:] = (pair + bias_value).astype(jnp.bfloat16)
    for copy in send_kv:
        copy.start()
    save_kv_w = here(kv_w, qkv_out.at[:, pl.ds(width, 2 * kv_width)], 11)
    save_kv_w.start()

    load_gate.wait()
    load_up.wait()
    pick_units(gate_v, up_v, gu.at[own_block], w_gate.shape[1] // n_f, unit, unit_pad)
    gather_q.forward()
    load_down.wait()
    raw = down_raw[...].astype(jnp.float32)
    shifted = jnp.concatenate([raw[8:], jnp.zeros((8, width), jnp.float32)], 0)
    raw = jnp.where(lax.rem(s * unit, 16) == 0, raw, shifted)
    inside = lax.broadcasted_iota(jnp.int32, raw.shape, 0) < unit
    down_own[...] = jnp.where(inside, raw, 0.0).astype(jnp.bfloat16)

    for j in range(n_s):
        keys_slot = slots_all[j]
        keys_slot = jnp.concatenate([keys_slot] * (rows // 128), 1)
        ok = (keys_slot <= slot) & (keys_slot >= first)
        bias[j * rows : (j + 1) * rows] = jnp.where(ok, 0.0, -1e30)

    gather_q.last()
    gather_out.start()
    gather_q.finish()
    save_q_w = here(q_w, qkv_out.at[:, pl.ds(0, width)], 0)
    save_q_w.start()
    for g in range(HEADS // 2):
        columns = slice(g * 2 * HEAD_DIM, (g + 1) * 2 * HEAD_DIM)
        pair = jnp.dot(rows_low, q_w[:, columns], preferred_element_type=jnp.float32)
        pair = pair + bias_query[:, columns]
        for h in range(2):
            part = turned(pair[:, h * HEAD_DIM : (h + 1) * HEAD_DIM]).astype(jnp.bfloat16)
            queries[:, (2 * g + h) * HEAD_DIM : (2 * g + h + 1) * HEAD_DIM] = part

    for copy in send_kv:
        copy.wait_recv()
    chain_up.send(1)
    save_kv = here(kv, paired_out, 12)
    save_kv.start()
    slots_out[...] = slots_all[...]

    for g in range(KV_HEADS):
        keys = kv[:, :, g * HEAD_DIM : (g + 1) * HEAD_DIM].reshape(n_s * rows, HEAD_DIM)
        values = kv[:, :, kv_width + g * HEAD_DIM : kv_width + (g + 1) * HEAD_DIM]
        values = values.reshape(n_s * rows, HEAD_DIM)

        def head(i, carry, g=g, keys=keys, values=values):
            h = g * repeat + i
            columns = pl.ds(pl.multiple_of(h * HEAD_DIM, HEAD_DIM), HEAD_DIM)
            raw = lax.dot_general(
                keys, queries[:, columns], (((1,), (1,)), ((), ())),
                preferred_element_type=jnp.float32,
            )
            scores = raw * scale + bias[...]
            top = jnp.max(scores, 0, keepdims=True)
            expo = jnp.exp(scores - top)
            total = jnp.sum(expo, 0, keepdims=True)
            probs = (expo * (1.0 / total)).astype(jnp.bfloat16)
            mixed = lax.dot_general(
                values, probs, (((0,), (0,)), ((), ())), preferred_element_type=jnp.float32
            )
            attended[:, columns] = mixed.T.astype(jnp.bfloat16)
            logsum[pl.ds(pl.multiple_of(h * 8, 8), 8)] = jnp.broadcast_to(
                top + jnp.log(total), (8, rows)
            )
            return carry

        lax.fori_loop(0, repeat, head, 0)
        if g == 0:
            gather_out.forward()

    gather_out.last()
    gather_gu.start()
    gather_out.finish()
    save_out = here(out_w, out_out, 13)
    save_out.start()
    mixed = attended[...]
    for g in range(width // 256):
        columns = slice(g * 256, (g + 1) * 256)
        part = jnp.dot(mixed, out_w[:, columns], preferred_element_type=jnp.float32)
        resid[:, columns] = tokens[:, columns].astype(jnp.float32) + part
    value = resid[...]
    root = lax.rsqrt(jnp.mean(value * value, -1, keepdims=True) + epsilon)
    own_tokens = pl.ds(pl.multiple_of(s * rows, rows), rows)
    normed[own_tokens] = (value * root * gain_two[...]).astype(jnp.bfloat16)
    chain_normed.send(1)

    wide = hidden_v.shape[2]
    count = units // wide

    def saves(owner, t, slot):
        place = (
            pl.ds(pl.multiple_of(owner * rows, rows), rows),
            pl.ds(pl.multiple_of(t * wide, wide), wide),
        )
        return [
            here(part.at[slot], whole.at[place], 16 + 3 * slot + i)
            for i, (part, whole) in enumerate(
                ((hidden_v, hidden), (gate_part, factor_gate), (up_part, factor_up))
            )
        ]

    def feed(owner, done):
        def body(t, carry):
            slot = lax.rem(t + done, 2)
            mine = normed[pl.ds(pl.multiple_of(owner * rows, rows), rows)]
            gate_columns = pl.ds(pl.multiple_of(t * wide, wide), wide)
            up_columns = pl.ds(pl.multiple_of(units + t * wide, wide), wide)
            gate = jnp.dot(mine, gu[:, gate_columns], preferred_element_type=jnp.float32)
            up = jnp.dot(mine, gu[:, up_columns], preferred_element_type=jnp.float32)
            sigma = jax.nn.sigmoid(gate)
            activated = gate * sigma

            @pl.when(t + done >= 2)
            def _():
                for copy in saves(owner, t, slot):
                    copy.wait()

            hidden_v[slot] = (activated * up).astype(jnp.bfloat16)
            gate_part[slot] = (up * sigma * (1.0 + gate * (1.0 - sigma))).astype(jnp.bfloat16)
            up_part[slot] = activated.astype(jnp.bfloat16)
            for copy in saves(owner, t, slot):
                copy.start()
            return carry

        lax.fori_loop(0, count, body, 0)

    chain_normed.receive(1)
    chain_up.receive(1)
    chain_up.send(2)
    gather_gu.forward()
    chain_up.receive(2)
    chain_normed.send(2)
    chain_normed.receive(2)
    chain_normed.send(3)
    gather_gu.last()
    gather_down.start()
    gather_gu.finish()
    save_gu = here(gu, gu_all, 22)
    save_gu.start()
    feed(s, 0)
    feed(s ^ 1, count)
    chain_normed.receive(3)
    chain_up.send(3)
    save_normed = here(normed, normed_all, 23)
    save_normed.start()
    feed(s ^ 2, 2 * count)
    gather_down.forward()
    feed(s ^ 3, 3 * count)
    gather_down.last()
    for t in (count - 2, count - 1):
        for copy in saves(s ^ 3, t, (t + 3 * count) % 2):
            copy.wait()
    chain_up.receive(3)
    gather_down.finish()
    for copy in (save_kv_w, save_q_w, save_kv, save_out, save_gu, save_normed):
        copy.wait()
    for part in (gather_kv, gather_q, gather_out, gather_gu, gather_down, chain_up, chain_normed):
        part.sent()
    for copy in send_small + send_slots + send_kv:
        copy.wait_send()


def pick_units(gate, up, out, stride, unit, padded):
    rank = lax.axis_index("seq")
    pieces = gate.shape[1] // stride
    half = out.shape[1] // 2
    window, tile = 512, 128
    rows = lax.broadcasted_iota(jnp.int32, (window, tile), 0)
    columns = lax.broadcasted_iota(jnp.int32, (window, tile), 1)
    for first in range(0, 2 * half, tile):
        source = gate if first < half else up
        local = first % half
        total = jnp.zeros((out.shape[0], tile), jnp.float32)
        for f in range(pieces):
            low = max(local, f * padded)
            high = min(local + tile, f * padded + unit)
            if low >= high:
                continue
            begin = f * stride + rank * unit
            base = jnp.minimum(begin // 128, (source.shape[1] - window) // 128) * 128
            base = pl.multiple_of(base, 128)
            wanted = columns + (local - f * padded + begin - base)
            inside = (columns >= low - local) & (columns < high - local)
            chosen = jnp.where((rows == wanted) & inside, 1.0, 0.0).astype(jnp.bfloat16)
            total += jnp.dot(
                source[:, pl.ds(base, window)], chosen, preferred_element_type=jnp.float32
            )
        out[:, first : first + tile] = total.astype(jnp.bfloat16)


def front(tokens, cotangent, lengths, balance, vectors, weights):
    rows, width = tokens.shape
    n_s = lax.axis_size("seq")
    w_query, w_key, w_value, w_out, w_gate, w_up, w_down = weights
    block = w_query.shape[0]
    unit_pad = -(-w_down.shape[0] // n_s // 16) * 16
    kv_width = KV_HEADS * HEAD_DIM
    qkv_width = width + 2 * kv_width
    units = 8 * unit_pad
    group = n_s * rows
    wide = 768
    low, full = jnp.bfloat16, jnp.float32
    small = sum(
        jnp.pad(v.astype(full)[None], ((i, 7 - i), (0, 2 * block - v.shape[0])))
        for i, v in enumerate(vectors)
    )
    half = HEAD_DIM // 2
    inverse = rope_base ** (-(np.arange(half, dtype=np.float32) * np.float32(2.0 / HEAD_DIM)))
    inverse = jnp.asarray(np.concatenate([inverse, inverse])[None], full)
    smem = pl.BlockSpec(memory_space=pltpu.SMEM)
    vmem = pl.BlockSpec(memory_space=pltpu.VMEM)
    hbm = pl.BlockSpec(memory_space=pl.ANY)
    shape = jax.ShapeDtypeStruct
    return pl.pallas_call(
        front_kernel,
        in_specs=[smem, vmem, hbm, vmem, vmem, vmem] + [hbm] * 7,
        out_specs=[hbm] * 9 + [vmem, hbm] + [vmem] * 11,
        out_shape=[
            shape((width, 2 * units), low),
            shape((units, width), low),
            shape((group, width), low),
            shape((group, width), low),
            shape((group, units), low),
            shape((group, units), low),
            shape((group, units), low),
            shape((width, qkv_width), low),
            shape((width, width), low),
            shape((rows, width), low),
            shape((n_s, rows, 2 * kv_width), low),
            shape((n_s, rows, 128), full),
            shape((8 * HEADS, rows), full),
            shape((rows, width), low),
            shape((rows, width), full),
            shape((rows, width), low),
            shape((1, width), full),
            shape((1, width), full),
            shape((8, rows), full),
            shape((8, rows), full),
            shape((rows, HEAD_DIM), full),
            shape((rows, HEAD_DIM), full),
        ],
        scratch_shapes=[
            pltpu.VMEM((width, width), low),
            pltpu.VMEM((width, 2 * kv_width), low),
            pltpu.VMEM((width, width), low),
            pltpu.VMEM(w_gate.shape, low),
            pltpu.VMEM(w_up.shape, low),
            pltpu.VMEM((width, 2 * units), low),
            pltpu.VMEM((group, width), low),
            pltpu.VMEM((n_s, rows, 2 * kv_width), low),
            pltpu.VMEM((8, 2 * block), full),
            pltpu.VMEM((8, 8, 2 * block), full),
            pltpu.VMEM((n_s, rows, 128), full),
            pltpu.VMEM((group, rows), full),
            pltpu.VMEM((unit_pad, width), low),
            pltpu.VMEM((unit_pad, width), low),
            pltpu.VMEM((2, rows, wide), low),
            pltpu.VMEM((2, rows, wide), low),
            pltpu.VMEM((2, rows, wide), low),
            pltpu.SemaphoreType.DMA((24,)),
            pltpu.SemaphoreType.DMA((56,)),
            pltpu.SemaphoreType.DMA((56,)),
            pltpu.SemaphoreType.DMA((12,)),
            pltpu.SemaphoreType.DMA((12,)),
        ],
        compiler_params=pltpu.CompilerParams(
            collective_id=0, has_side_effects=True, vmem_limit_bytes=62 * 2**20
        ),
        name="front",
    )(
        lengths, tokens, cotangent, small, balance.reshape(1, rows), inverse,
        w_query, w_key, w_value, w_out, w_gate, w_up, w_down,
    )


def ffn_kernel(
    normed_all, upstream_all, w_gu, w_down, hidden_all, factor_gate, factor_up,
    columns, grad_down, gu_sum, gu_far, branch, down_arrived, gu_arrived,
    normed, upstream, gu, down, hidden, d_both, partial, z_one, z_two, z_three,
    down_x, down_y, down_last, down_piece,
    load, ssem, rsem,
):
    f = lax.axis_index("fsdp")
    s = lax.axis_index("seq")
    n_s = len(ORDER)
    group, width = normed.shape
    rows = group // n_s
    half_rows = group // 2
    units = down.shape[0]
    tile = 256
    tiles = units // tile
    wide = 768
    block = gu.shape[0] // 8
    unit = units // 8
    half = width // 2
    plane = [f ^ k for k in range(8)]
    full = jnp.float32

    entry = pltpu.get_barrier_semaphore()
    for k in (1, 2, 4):
        pl.semaphore_signal(entry, inc=1, device_id={"fsdp": plane[k]}, device_id_type=MESH)
    for j in (1, n_s - 1):
        pl.semaphore_signal(
            entry, inc=1, device_id={"seq": lax.rem(s + j, n_s)}, device_id_type=MESH
        )

    def here(source, target, index):
        return pltpu.make_async_copy(source, target, load.at[index])

    def there(source, target, index, **device):
        return pltpu.make_async_remote_copy(
            src_ref=source, dst_ref=target, send_sem=ssem.at[index], recv_sem=rsem.at[index],
            device_id=device, device_id_type=MESH,
        )

    def part(ref, owner, size):
        return ref.at[pl.ds(pl.multiple_of(owner * size, 16), size)]

    early, late = range(0, n_s // 2), range(n_s // 2, n_s)

    def rows_of(p):
        return pl.ds(p * rows, rows)

    def row_loads(p):
        owner = lax.rem(s + n_s - ORDER[p], n_s)
        mine = rows_of(p)
        return [
            here(part(upstream_all, owner, rows), upstream.at[mine], 5 * p),
            here(part(factor_gate, owner, rows), d_both.at[mine, pl.ds(0, units)], 5 * p + 1),
            here(part(factor_up, owner, rows), d_both.at[mine, pl.ds(units, units)], 5 * p + 2),
            here(part(hidden_all, owner, rows), hidden.at[mine], 5 * p + 3),
            here(part(normed_all, owner, rows), normed.at[mine], 5 * p + 4),
        ]

    def down_load(t):
        mine = pl.ds(pl.multiple_of(t * wide, wide), wide)
        return here(w_down.at[mine], down.at[mine], 20 + t)

    def gu_load(n):
        mine = pl.ds(pl.multiple_of(n * 512, 512), 512)
        return here(w_gu.at[mine], gu.at[mine], 23 + n)

    loads = [row_loads(p) for p in range(n_s)]
    order = [loads[0][0], loads[1][0], down_load(0)]
    order += [loads[p][i] for i in (1, 2) for p in early]
    order += [down_load(t) for t in range(1, units // wide)]
    order += [gu_load(n) for n in range(width // 512)]
    order += [loads[p][i] for i in (0, 1, 2) for p in late]
    order += [loads[p][i] for i in (3, 4) for p in range(n_s)]
    for copy in order:
        copy.start()

    def forward(blocks, wait):
        for p in blocks:
            for copy in loads[p][:3]:
                copy.wait()
        mine = pl.ds(blocks[0] * rows, len(blocks) * rows)

        def body(t, carry):
            if wait:
                down_load(t).wait()
            gate_columns = pl.ds(pl.multiple_of(t * wide, wide), wide)
            up_columns = pl.ds(pl.multiple_of(units + t * wide, wide), wide)
            d_hidden = lax.dot_general(
                upstream[mine], down[gate_columns], (((1,), (1,)), ((), ())),
                preferred_element_type=full,
            )
            value = d_hidden * d_both[mine, gate_columns].astype(full)
            d_both[mine, gate_columns] = value.astype(jnp.bfloat16)
            value = d_hidden * d_both[mine, up_columns].astype(full)
            d_both[mine, up_columns] = value.astype(jnp.bfloat16)
            return carry

        lax.fori_loop(0, units // wide, body, 0)

    def backward(blocks, wait):
        part_rows = pl.ds(blocks[0] * rows, len(blocks) * rows)

        def body(n, carry):
            if wait:
                gu_load(n).wait()
            out_columns = pl.ds(pl.multiple_of(n * 512, 512), 512)
            value = lax.dot_general(
                d_both[part_rows], gu[out_columns], (((1,), (1,)), ((), ())),
                preferred_element_type=full,
            )
            partial[part_rows, out_columns] = value.astype(jnp.bfloat16)
            return carry

        lax.fori_loop(0, width // 512, body, 0)

    chain = SumChain(in_order(partial, rows), z_one, z_two, z_three, there, 0)
    pieces = [(first, min(group, units - first)) for first in range(0, units, group)]
    forward(early, True)
    backward(early, True)
    pl.semaphore_wait(entry, 5)
    chain.one()
    forward(late, False)
    backward(late, False)
    chain.add_one()
    chain.two()

    for p in range(n_s):
        loads[p][3].wait()
        loads[p][4].wait()

    def down_body(t, carry):
        unit_rows = pl.ds(pl.multiple_of(t * tile, tile), tile)
        value = lax.dot_general(
            hidden[:, unit_rows], upstream[...], (((0,), (0,)), ((), ())),
            preferred_element_type=full,
        )
        down[unit_rows] = value.astype(jnp.bfloat16)
        return carry

    lax.fori_loop(0, tiles, down_body, 0)
    down_core = [
        there(part(down, plane[2 * i + 1], unit), down_arrived.at[i], 6 + i, fsdp=plane[1])
        for i in range(4)
    ]
    for copy in down_core:
        copy.start()

    def gu_body(m, carry):
        in_columns = pl.ds(pl.multiple_of(m * tile, tile), tile)
        turned = normed[:, in_columns].T
        for first in range(0, 2 * units, units // 3):
            value = jnp.dot(turned, d_both[:, first : first + units // 3], preferred_element_type=full)
            gu[in_columns, first : first + units // 3] = value.astype(jnp.bfloat16)
        return carry

    lax.fori_loop(0, 2, gu_body, 0)

    def add_arrived(i, ref, size, arrived, pieces, copies, index):
        copies[i].wait_recv()
        fetch = [
            here(arrived.at[i, :, columns], piece, index + k)
            for k, (columns, piece) in enumerate(pieces)
        ]
        for copy in fetch:
            copy.start()
        target = part(ref, plane[2 * i], size)
        for copy, (columns, piece) in zip(fetch, pieces):
            copy.wait()
            target[:, columns] = (
                target[:, columns].astype(full) + piece[...].astype(full)
            ).astype(jnp.bfloat16)

    down_pieces = [(pl.ds(0, width), down_piece)]
    for i in (3, 1, 2, 0):
        add_arrived(i, down, unit, down_arrived, down_pieces, down_core, 26)
    to_x, to_y, to_both = [part(down, plane[k], unit) for k in (2, 4, 6)]
    low_half, high_half = pl.ds(0, half), pl.ds(half, half)
    down_first = [
        there(to_x.at[:, low_half], down_x.at[0], 10, fsdp=plane[2]),
        there(to_both.at[:, low_half], down_x.at[1], 11, fsdp=plane[2]),
        there(to_y.at[:, high_half], down_y.at[0], 12, fsdp=plane[4]),
        there(to_both.at[:, high_half], down_y.at[1], 13, fsdp=plane[4]),
    ]
    for copy in down_first:
        copy.start()
    chain.three()
    lax.fori_loop(2, width // tile, gu_body, 0)
    gu_core = [
        there(part(gu, plane[2 * i + 1], block), gu_arrived.at[i], 16 + i, fsdp=plane[1])
        for i in range(4)
    ]
    for copy in gu_core:
        copy.start()

    again = [
        here(
            w_down.at[first : first + count],
            d_both.at[:count, i * width : (i + 1) * width], 32 + i,
        )
        for i, (first, count) in enumerate(pieces)
    ]
    for copy in again:
        copy.start()
    for copy in again:
        copy.wait()

    def branch_body(n, carry):
        out_columns = pl.ds(pl.multiple_of(n * wide, wide), wide)
        for m in range(2):
            mine = slice(m * half_rows, (m + 1) * half_rows)
            value = jnp.zeros((half_rows, wide), full)
            for i, (first, count) in enumerate(pieces):
                columns_here = pl.ds(pl.multiple_of(i * width + n * wide, wide), wide)
                value += jnp.dot(
                    hidden[mine, first : first + count], d_both[:count, columns_here],
                    preferred_element_type=full,
                )
            upstream[mine, out_columns] = value.astype(jnp.bfloat16)
        return carry

    lax.fori_loop(0, width // wide, branch_body, 0)
    chain.last(columns)
    chain_branch = SumChain(in_order(upstream, rows), z_one, z_two, z_three, there, 22)
    chain_branch.one()
    down_second = [
        there(to_y.at[:, low_half], down_last.at[0], 14, fsdp=plane[4]),
        there(to_x.at[:, high_half], down_last.at[1], 15, fsdp=plane[2]),
    ]
    down_first[1].wait_recv()
    to_y[:, :half] = (to_y[:, :half].astype(full) + down_x[1].astype(full)).astype(jnp.bfloat16)
    down_second[0].start()
    down_first[3].wait_recv()
    to_x[:, half:] = (to_x[:, half:].astype(full) + down_y[1].astype(full)).astype(jnp.bfloat16)
    down_second[1].start()
    gu_pieces = [
        (pl.ds(0, units), hidden.at[:block]),
        (pl.ds(units, units), hidden.at[block : 2 * block]),
    ]
    add_arrived(3, gu, block, gu_arrived, gu_pieces, gu_core, 27)
    far = part(gu, plane[6], block)
    gu_first = [
        there(far.at[:, pl.ds(0, units)], gu_far.at[0], 20, fsdp=plane[2]),
        there(far.at[:, pl.ds(units, units)], gu_far.at[1], 21, fsdp=plane[4]),
    ]
    for copy in gu_first:
        copy.start()
    for i in (1, 2, 0):
        add_arrived(i, gu, block, gu_arrived, gu_pieces, gu_core, 27)
    store = [here(part(gu, plane[2 * i], block), gu_sum.at[i], 29 + i) for i in range(3)]
    for copy in store:
        copy.start()
    down_first[0].wait_recv()
    down_first[2].wait_recv()
    own = part(down, f, unit)
    down_second[0].wait_recv()
    grad_down[:, :half] = (
        own[:, :half].astype(full) + down_x[0].astype(full) + down_last[0].astype(full)
    )
    down_second[1].wait_recv()
    grad_down[:, half:] = (
        own[:, half:].astype(full) + down_y[0].astype(full) + down_last[1].astype(full)
    )
    chain_branch.add_one()
    chain_branch.one_sent()
    store_branch = here(upstream, branch, 35)
    store_branch.start()
    chain.one_sent()
    chain.sent()
    for copy in down_core + down_first + down_second + gu_core + gu_first:
        copy.wait_send()
    for copy in gu_first:
        copy.wait_recv()
    for copy in store + [store_branch]:
        copy.wait()


def ffn(normed_all, upstream_all, w_gu, w_down, hidden, factor_gate, factor_up):
    group, width = normed_all.shape
    units = w_down.shape[0]
    rows = group // len(ORDER)
    unit, block, half = units // 8, width // 8, width // 2
    low, full = jnp.bfloat16, jnp.float32
    vmem = pl.BlockSpec(memory_space=pltpu.VMEM)
    hbm = pl.BlockSpec(memory_space=pl.ANY)
    shape = jax.ShapeDtypeStruct
    return pl.pallas_call(
        ffn_kernel,
        in_specs=[hbm] * 7,
        out_specs=[vmem] * 2 + [hbm] * 5,
        out_shape=[
            shape((rows, width), full),
            shape((unit, width), full),
            shape((3, block, 2 * units), low),
            shape((2, block, units), low),
            shape((group, width), low),
            shape((4, unit, width), low),
            shape((4, block, 2 * units), low),
        ],
        scratch_shapes=[
            pltpu.VMEM((group, width), low),
            pltpu.VMEM((group, width), low),
            pltpu.VMEM((width, 2 * units), low),
            pltpu.VMEM((units, width), low),
            pltpu.VMEM((group, units), low),
            pltpu.VMEM((group, 2 * units), low),
            pltpu.VMEM((group, width), low),
            pltpu.VMEM((rows, width), low),
            pltpu.VMEM((2, rows, width), low),
            pltpu.VMEM((2, rows, width), low),
            pltpu.VMEM((2, unit, half), low),
            pltpu.VMEM((2, unit, half), low),
            pltpu.VMEM((2, unit, half), low),
            pltpu.VMEM((unit, width), low),
            pltpu.SemaphoreType.DMA((36,)),
            pltpu.SemaphoreType.DMA((28,)),
            pltpu.SemaphoreType.DMA((28,)),
        ],
        compiler_params=pltpu.CompilerParams(
            collective_id=1, has_side_effects=True, vmem_limit_bytes=63 * 2**20
        ),
        name="ffn",
    )(normed_all, upstream_all, w_gu, w_down, hidden, factor_gate, factor_up)[:5]


def back_kernel(
    columns, resid, gain_two, cotangent, attended, queries, paired, slots, slot_row, first_row,
    logsum, normed_one, tokens, gain_one, cosine, sine, w_out, w_qkv, gu_sum, gu_far, branch,
    layer, input_rows, vector, grad_out, grad_qkv, gu_rows,
    out_w, qkv, gu_own, gu_to_y, gu_to_x, gu_x, gu_y, gu_ended,
    branch_v, z_one, z_two, z_three, working, bias, d_branch, d_attended, d_qkv, d_resid,
    keys_grad, values_grad, dkv, dkv_in,
    out_arrived, out_x, out_y, out_ended, qkv_arrived, qkv_x, qkv_y, qkv_ended,
    out_one, out_two, out_three, qkv_one, qkv_two, qkv_three, vector_in,
    load, ssem, rsem,
):
    f = lax.axis_index("fsdp")
    s = lax.axis_index("seq")
    rows, width = tokens.shape
    n_s = paired.shape[0]
    kv_width = KV_HEADS * HEAD_DIM
    repeat = HEADS // KV_HEADS
    scale = HEAD_DIM ** (-0.5)
    block = width // 8
    piece = block // n_s
    units = gu_sum.shape[2] // 2
    tile = 256
    full, low = jnp.float32, jnp.bfloat16
    plane = [f ^ k for k in range(8)]

    entry = pltpu.get_barrier_semaphore()
    for k in (1, 2, 4):
        pl.semaphore_signal(entry, inc=1, device_id={"fsdp": plane[k]}, device_id_type=MESH)
    for j in range(1, n_s):
        pl.semaphore_signal(
            entry, inc=1, device_id={"seq": lax.rem(s + j, n_s)}, device_id_type=MESH
        )

    def here(source, target, index):
        return pltpu.make_async_copy(source, target, load.at[index])

    def there(source, target, index, **device):
        return pltpu.make_async_remote_copy(
            src_ref=source, dst_ref=target, send_sem=ssem.at[index], recv_sem=rsem.at[index],
            device_id=device, device_id_type=MESH,
        )

    low_units, high_units = pl.ds(0, units), pl.ds(units, units)
    load_branch = here(branch, branch_v, 0)
    load_out = here(w_out, out_w, 1)
    load_gu = [
        here(gu_sum.at[0], gu_own, 2),
        here(gu_sum.at[2, :, low_units], gu_to_y, 3),
        here(gu_sum.at[1, :, high_units], gu_to_x, 4),
        here(gu_far.at[0], gu_x.at[1], 8),
        here(gu_far.at[1], gu_y.at[1], 9),
    ]
    load_qkv = here(w_qkv, qkv, 5)
    load_columns = here(columns, working, 7)
    for copy in [load_columns, load_branch, load_out] + load_gu + [load_qkv]:
        copy.start()

    gu_first = [
        there(gu_sum.at[1, :, low_units], gu_x.at[0], 2, fsdp=plane[2]),
        there(gu_sum.at[2, :, high_units], gu_y.at[0], 3, fsdp=plane[4]),
    ]
    gu_second = [
        there(gu_to_y, gu_ended.at[0], 4, fsdp=plane[4]),
        there(gu_to_x, gu_ended.at[1], 5, fsdp=plane[2]),
    ]

    def around(j):
        return {"seq": lax.rem(s + j, n_s)}

    def rows_for(ref, first, j):
        owner = lax.rem(s + j, n_s)
        return ref.at[pl.ds(pl.multiple_of(first + owner * piece, 16), piece)]

    gu_send = [there(rows_for(gu_own, 0, j), gu_rows.at[j], 5 + j, **around(j)) for j in range(1, n_s)]
    dkv_send = [
        [
            there(dkv.at[g, lax.rem(s + j, n_s)], dkv_in.at[g, j], 8 + 3 * g + j, **around(j))
            for j in range(1, n_s)
        ]
        for g in range(KV_HEADS)
    ]
    chain = SumChain(in_order(branch_v, rows), z_one, z_two, z_three, there, 16)
    sum_out = SumPlane(out_w, block, plane, out_arrived, out_x, out_y, out_ended, there, 24)
    sum_qkv = SumPlane(qkv, block, plane, qkv_arrived, qkv_x, qkv_y, qkv_ended, there, 36)

    def own_part(ref):
        return lambda j: rows_for(ref, f * block, n_s - j)

    chain_out = SumChain(own_part(out_w), out_one, out_two, out_three, there, 48)
    chain_qkv = SumChain(own_part(qkv), qkv_one, qkv_two, qkv_three, there, 54)
    vector_send = [
        there(vector_in.at[0], vector_in.at[1], 60, fsdp=plane[1]),
        there(vector_in.at[2], vector_in.at[3], 61, fsdp=plane[2]),
        there(vector_in.at[4], vector_in.at[5], 62, fsdp=plane[4]),
    ] + [there(vector_in.at[6], vector_in.at[6 + j], 62 + j, **around(j)) for j in range(1, n_s)]

    pl.semaphore_wait(entry, 3 + n_s - 1)
    for copy in gu_first:
        copy.start()
    load_branch.wait()
    chain.two()
    for copy in load_gu:
        copy.wait()
    gu_to_y[...] = (gu_to_y[...].astype(full) + gu_x[1].astype(full)).astype(low)
    gu_second[0].start()
    gu_to_x[...] = (gu_to_x[...].astype(full) + gu_y[1].astype(full)).astype(low)
    gu_second[1].start()

    def norm_back(value, gain, grad):
        root = lax.rsqrt(jnp.mean(value * value, -1, keepdims=True) + epsilon)
        scaled = gain * grad
        inner = jnp.mean(scaled * value, -1, keepdims=True)
        gain_grad = jnp.sum(grad * (value * root), 0, keepdims=True)
        return root * scaled - value * (root * root * root * inner), gain_grad

    load_columns.wait()
    d_norm, gain_two_grad = norm_back(resid[...], gain_two[...], working[...])
    d_total = cotangent[...].astype(full) + d_norm
    d_branch[...] = d_total.astype(low)
    d_resid[...] = d_total
    for j in range(n_s):
        keys_slot = slots[j]
        keys_slot = jnp.concatenate([keys_slot] * (rows // 128), 1)
        ok = (keys_slot <= slot_row[0:1]) & (keys_slot >= first_row[0:1])
        bias[j * rows : (j + 1) * rows] = jnp.where(ok, 0.0, -1e30)
    load_out.wait()
    for n in range(width // tile):
        value = lax.dot_general(
            d_branch[...], out_w[n * tile : (n + 1) * tile], (((1,), (1,)), ((), ())),
            preferred_element_type=full,
        )
        d_attended[:, n * tile : (n + 1) * tile] = value.astype(low)

    def turned_back(value):
        return value * cosine[...] + pltpu.roll(value * sine[...], HEAD_DIM // 2, 1)

    for g in range(KV_HEADS):
        keys = paired[:, :, g * HEAD_DIM : (g + 1) * HEAD_DIM].reshape(n_s * rows, HEAD_DIM)
        values = paired[:, :, kv_width + g * HEAD_DIM : kv_width + (g + 1) * HEAD_DIM]
        values = values.reshape(n_s * rows, HEAD_DIM)
        keys_grad[...] = jnp.zeros_like(keys_grad)
        values_grad[...] = jnp.zeros_like(values_grad)

        def head(i, carry, g=g, keys=keys, values=values):
            h = g * repeat + i
            head_columns = pl.ds(pl.multiple_of(h * HEAD_DIM, HEAD_DIM), HEAD_DIM)
            query = queries[:, head_columns]
            grad = d_attended[:, head_columns]
            raw = lax.dot_general(
                keys, query, (((1,), (1,)), ((), ())), preferred_element_type=full
            )
            logs = logsum[pl.ds(pl.multiple_of(h * 8, 8), 8)][0:1]
            probs = jnp.exp(raw * scale + bias[...] - logs)
            d_probs = lax.dot_general(
                values, grad, (((1,), (1,)), ((), ())), preferred_element_type=full
            )
            delta = jnp.sum(probs * d_probs, 0, keepdims=True)
            d_score = (probs * (d_probs - delta)).astype(low)
            turned = lax.dot_general(
                keys, d_score, (((0,), (0,)), ((), ())), preferred_element_type=full
            )
            d_qkv[:, head_columns] = turned_back((turned * scale).T).astype(low)
            keys_grad[...] += jnp.dot(d_score, query, preferred_element_type=full) * scale
            values_grad[...] += jnp.dot(probs.astype(low), grad, preferred_element_type=full)
            return carry

        lax.fori_loop(0, repeat, head, 0)
        dkv[g, :, :, :HEAD_DIM] = keys_grad[...].astype(low).reshape(n_s, rows, HEAD_DIM)
        dkv[g, :, :, HEAD_DIM:] = values_grad[...].astype(low).reshape(n_s, rows, HEAD_DIM)
        for copy in dkv_send[g]:
            copy.start()

    turned = attended[...].T
    for n in range(width // tile):
        n_columns = slice(n * tile, (n + 1) * tile)
        value = jnp.dot(turned, d_branch[:, n_columns], preferred_element_type=full)
        out_w[:, n_columns] = value.astype(low)
    sum_out.start_core()
    load_qkv.wait()

    def back_one(first, count, start):
        for n in range(width // tile):
            n_rows = slice(n * tile, (n + 1) * tile)
            value = lax.dot_general(
                d_qkv[:, first : first + count], qkv[n_rows, first : first + count],
                (((1,), (1,)), ((), ())), preferred_element_type=full,
            )
            working[:, n_rows] = value if start else working[:, n_rows] + value

    back_one(0, width, True)
    normed_turned = normed_one[...].T
    for n in range(width // tile):
        n_columns = slice(n * tile, (n + 1) * tile)
        value = jnp.dot(normed_turned, d_qkv[:, n_columns], preferred_element_type=full)
        qkv[:, n_columns] = value.astype(low)
    sum_out.start_first()

    for g in range(KV_HEADS):
        for copy in dkv_send[g]:
            copy.wait_recv()
        total = dkv[g, s].astype(full)
        for j in range(1, n_s):
            total = total + dkv_in[g, j].astype(full)
        key_columns = slice(width + g * HEAD_DIM, width + (g + 1) * HEAD_DIM)
        value_columns = slice(width + kv_width + g * HEAD_DIM, width + kv_width + (g + 1) * HEAD_DIM)
        d_qkv[:, key_columns] = turned_back(total[:, :HEAD_DIM]).astype(low)
        d_qkv[:, value_columns] = total[:, HEAD_DIM:].astype(low)
    back_one(width, 2 * kv_width, False)
    value = jnp.dot(normed_turned, d_qkv[:, width:], preferred_element_type=full)
    qkv[:, width:] = value.astype(low)
    sum_qkv.start_core()
    chain.three()

    d_norm, gain_one_grad = norm_back(tokens[...].astype(full), gain_one[...], working[...])
    input_rows[...] = (d_resid[...] + d_norm).astype(low)
    bias_grad = jnp.sum(d_qkv[...].astype(full), 0, keepdims=True)
    vectors = jnp.concatenate([gain_one_grad, gain_two_grad, bias_grad], 1)
    part = vectors.shape[1] // 8
    for r in range(8):
        vector_in[0, r : r + 1] = vectors[:, r * part : (r + 1) * part]
    vector_send[0].start()
    sum_qkv.start_first()
    vector_send[0].wait_recv()
    vector_in[2] = vector_in[0] + vector_in[1]
    vector_send[1].start()

    gu_first[0].wait_recv()
    gu_second[0].wait_recv()
    total = gu_own[:, :units].astype(full) + gu_x[0].astype(full) + gu_ended[0].astype(full)
    gu_own[:, :units] = total.astype(low)
    gu_first[1].wait_recv()
    gu_second[1].wait_recv()
    total = gu_own[:, units:].astype(full) + gu_y[0].astype(full) + gu_ended[1].astype(full)
    gu_own[:, units:] = total.astype(low)
    for copy in gu_send:
        copy.start()
    keep_rows = here(rows_for(gu_own, 0, 0), gu_rows.at[0], 6)
    keep_rows.start()
    sum_out.start_second()
    vector_send[1].wait_recv()
    vector_in[4] = vector_in[2] + vector_in[3]
    vector_send[2].start()

    sum_qkv.start_second()
    sum_out.finish()
    chain_out.one()
    vector_send[2].wait_recv()
    vector_in[6] = vector_in[4] + vector_in[5]
    for copy in vector_send[3:]:
        copy.start()
    chain_out.add_one()
    chain_out.two()
    sum_qkv.finish()
    chain_qkv.one()
    chain_out.three()
    chain.last(working)
    layer[...] = (resid[...] + working[...]).astype(low)
    chain_qkv.add_one()
    chain_qkv.two()
    for copy in vector_send[3:]:
        copy.wait_recv()
    vector[...] = vector_in[6] + vector_in[7] + vector_in[8] + vector_in[9]
    chain_out.last(grad_out)
    chain_qkv.three()
    chain_qkv.last(grad_qkv)
    for copy in gu_send:
        copy.wait_recv()
    keep_rows.wait()
    for part in (chain_out, chain_qkv):
        part.one_sent()
        part.sent()
    chain.sent()
    sum_out.sent()
    sum_qkv.sent()
    for copy in gu_first + gu_second + gu_send + vector_send:
        copy.wait_send()
    for g in range(KV_HEADS):
        for copy in dkv_send[g]:
            copy.wait_send()


def back(
    columns, resid, gain_two, cotangent, attended, queries, paired, slots, slot_row, first_row,
    logsum, normed_one, tokens, gain_one, cosine, sine, w_out, w_qkv, gu_sum, gu_far, branch,
):
    rows, width = tokens.shape
    n_s = paired.shape[0]
    group = n_s * rows
    kv_width = KV_HEADS * HEAD_DIM
    qkv_width = width + 2 * kv_width
    block = width // 8
    piece = block // n_s
    units = gu_sum.shape[2] // 2
    low, full = jnp.bfloat16, jnp.float32
    vmem = pl.BlockSpec(memory_space=pltpu.VMEM)
    hbm = pl.BlockSpec(memory_space=pl.ANY)
    shape = jax.ShapeDtypeStruct
    vectors = (2 * width + qkv_width) // 8
    return pl.pallas_call(
        back_kernel,
        in_specs=[hbm] + [vmem] * 15 + [hbm] * 5,
        out_specs=[vmem] * 5 + [hbm],
        out_shape=[
            shape((rows, width), low),
            shape((rows, width), low),
            shape((8, vectors), full),
            shape((piece, width), full),
            shape((piece, qkv_width), full),
            shape((n_s, piece, 2 * units), low),
        ],
        scratch_shapes=[
            pltpu.VMEM((width, width), low),
            pltpu.VMEM((width, qkv_width), low),
            pltpu.VMEM((block, 2 * units), low),
            pltpu.VMEM((block, units), low),
            pltpu.VMEM((block, units), low),
            pltpu.VMEM((2, block, units), low),
            pltpu.VMEM((2, block, units), low),
            pltpu.VMEM((2, block, units), low),
            pltpu.VMEM((group, width), low),
            pltpu.VMEM((rows, width), low),
            pltpu.VMEM((2, rows, width), low),
            pltpu.VMEM((2, rows, width), low),
            pltpu.VMEM((rows, width), full),
            pltpu.VMEM((group, rows), full),
            pltpu.VMEM((rows, width), low),
            pltpu.VMEM((rows, width), low),
            pltpu.VMEM((rows, qkv_width), low),
            pltpu.VMEM((rows, width), full),
            pltpu.VMEM((group, HEAD_DIM), full),
            pltpu.VMEM((group, HEAD_DIM), full),
            pltpu.VMEM((KV_HEADS, n_s, rows, 2 * HEAD_DIM), low),
            pltpu.VMEM((KV_HEADS, n_s, rows, 2 * HEAD_DIM), low),
            pltpu.VMEM((4, block, width), low),
            pltpu.VMEM((2, block, width // 2), low),
            pltpu.VMEM((2, block, width // 2), low),
            pltpu.VMEM((2, block, width // 2), low),
            pltpu.VMEM((4, block, qkv_width), low),
            pltpu.VMEM((2, block, qkv_width // 2), low),
            pltpu.VMEM((2, block, qkv_width // 2), low),
            pltpu.VMEM((2, block, qkv_width // 2), low),
            pltpu.VMEM((piece, width), low),
            pltpu.VMEM((2, piece, width), low),
            pltpu.VMEM((2, piece, width), low),
            pltpu.VMEM((piece, qkv_width), low),
            pltpu.VMEM((2, piece, qkv_width), low),
            pltpu.VMEM((2, piece, qkv_width), low),
            pltpu.VMEM((10, 8, vectors), full),
            pltpu.SemaphoreType.DMA((10,)),
            pltpu.SemaphoreType.DMA((68,)),
            pltpu.SemaphoreType.DMA((68,)),
        ],
        compiler_params=pltpu.CompilerParams(
            collective_id=2, has_side_effects=True, vmem_limit_bytes=63 * 2**20
        ),
        name="back",
    )(
        columns, resid, gain_two, cotangent, attended, queries, paired, slots, slot_row, first_row,
        logsum, normed_one, tokens, gain_one, cosine, sine, w_out, w_qkv, gu_sum, gu_far, branch,
    )


def finish_kernel(
    layer, input_rows, grad_out, grad_qkv, grad_down, gu_rows,
    layer_out, input_grad, out_out, query_out, key_out, value_out, down_out, gate_out, up_out,
):
    s = lax.axis_index("seq")
    n_s = gu_rows.shape[0]
    width = grad_out.shape[1]
    kv_width = KV_HEADS * HEAD_DIM
    unit_pad = grad_down.shape[0]
    unit = down_out.shape[0]
    units = gu_rows.shape[2] // 2
    layer_out[...] = layer[...]
    input_grad[...] = input_rows[...]
    out_out[...] = grad_out[...]
    query_out[...] = grad_qkv[:, :width]
    key_out[...] = grad_qkv[:, width : width + kv_width]
    value_out[...] = grad_qkv[:, width + kv_width :]
    down_out[...] = grad_down[:unit]
    window = 512
    lanes = lax.broadcasted_iota(jnp.int32, (gu_rows.shape[1], 128), 1)
    for base, out in ((0, gate_out), (units, up_out)):
        for f in range(units // unit_pad):
            for owner in range(n_s):
                source = base + f * unit_pad
                begin = min(source // 128 * 128, 2 * units - window)
                target = (f * n_s + owner) * unit
                first = target // 128 * 128
                slot = lax.rem(s + n_s - owner, n_s)
                value = gu_rows[slot, :, begin : begin + window].astype(jnp.float32)
                turn = ((target - first) - (source - begin)) % window
                if turn:
                    value = pltpu.roll(value, turn, 1)
                for t in range(first, min(target + unit, out.shape[1]), 128):
                    part = value[:, t - first : t - first + 128]
                    if t < target:
                        part = jnp.where(lanes >= target - t, part, out[:, t : t + 128])
                    out[:, t : t + 128] = part


def finish(layer, input_rows, grad_out, grad_qkv, grad_down, gu_rows, unit, hidden_width):
    piece, width = grad_out.shape
    kv_width = KV_HEADS * HEAD_DIM
    low, full = jnp.bfloat16, jnp.float32
    shape = jax.ShapeDtypeStruct
    vmem = pl.BlockSpec(memory_space=pltpu.VMEM)
    return pl.pallas_call(
        finish_kernel,
        in_specs=[vmem] * 6,
        out_specs=[vmem] * 9,
        out_shape=[
            shape(layer.shape, low),
            shape(layer.shape, low),
            shape((piece, width), full),
            shape((piece, width), full),
            shape((piece, kv_width), full),
            shape((piece, kv_width), full),
            shape((unit, width), full),
            shape((piece, hidden_width), full),
            shape((piece, hidden_width), full),
        ],
        compiler_params=pltpu.CompilerParams(vmem_limit_bytes=63 * 2**20),
        name="finish",
    )(layer, input_rows, grad_out, grad_qkv, grad_down, gu_rows)


def per_device(
    tokens, cotangent, lengths, balance, norm1_gain, w_query, b_query, w_key, b_key,
    w_value, b_value, w_out, norm2_gain, w_gate, w_up, w_down,
):
    seq_count = lax.axis_size("seq")
    fsdp_count = lax.axis_size("fsdp")
    seq_rank = lax.axis_index("seq")
    fsdp_rank = lax.axis_index("fsdp")
    rows_here, width = tokens.shape
    kv_width = KV_HEADS * HEAD_DIM
    hidden_width = w_gate.shape[1]
    unit = hidden_width // (fsdp_count * seq_count)
    (
        weight_gu, weight_down, upstream_all, normed_all, hidden, factor_gate, factor_up,
        weight_qkv, weight_out, queries, paired, slots, logsum, attended, resid, normed_one,
        gain_one, gain_two, slot_row, first_row, cosine, sine,
    ) = front(
        tokens, cotangent, lengths, balance, (norm1_gain, norm2_gain, b_query, b_key, b_value),
        (w_query, w_key, w_value, w_out, w_gate, w_up, w_down),
    )
    columns, grad_down, gu_sum, gu_far, branch = ffn(
        normed_all, upstream_all, weight_gu, weight_down, hidden, factor_gate, factor_up
    )
    layer, input_rows, vectors, grad_out, grad_qkv, gu_rows = back(
        columns, resid, gain_two, cotangent, attended, queries, paired, slots, slot_row, first_row,
        logsum, normed_one, tokens, gain_one, cosine, sine, weight_out, weight_qkv, gu_sum, gu_far,
        branch,
    )
    (
        layer_out, input_grad, grad_out, grad_query, grad_key, grad_value, grad_down, grad_gate,
        grad_up,
    ) = finish(layer, input_rows, grad_out, grad_qkv, grad_down, gu_rows, unit, hidden_width)
    vectors = vectors.reshape(-1)
    own = width // (fsdp_count * seq_count)
    first = (fsdp_rank * seq_count + seq_rank) * own

    def own_part(offset):
        return lax.dynamic_slice_in_dim(vectors, offset + first, own, 0)

    biases = 2 * width
    return (
        layer_out,
        input_grad,
        own_part(0),
        grad_query,
        own_part(biases),
        grad_key,
        vectors[biases + width : biases + width + kv_width],
        grad_value,
        vectors[biases + width + kv_width :],
        grad_out,
        own_part(width),
        grad_gate,
        grad_up,
        grad_down,
    )


def solution(mesh):
    both = P(("fsdp", "seq"), None)
    both_one = P(("fsdp", "seq"))
    placed = (
        both, both, P("fsdp", None), both_one, P("fsdp"), P("fsdp", None), P("fsdp"),
        P("fsdp", None), P("fsdp"), P("fsdp", None), P("fsdp"), P("fsdp", None), P("fsdp"),
        P("fsdp", None), P("fsdp", None), P("fsdp", None),
    )
    return jax.shard_map(
        per_device if mesh.shape["fsdp"] == 8 else plain_device,
        mesh=mesh,
        in_specs=placed,
        out_specs=(
            both, both, both_one, both, both_one, both, P(), both, P(), both, both_one,
            both, both, both,
        ),
        check_vma=False,
    )
```

```python
import jax
import jax.numpy as jnp
import numpy as np
from jax import lax
from jax.experimental import pallas as pl
from jax.experimental.pallas import tpu as pltpu
from jax.sharding import PartitionSpec as P

HEADS = 12
KV_HEADS = 2
HEAD_DIM = 128

MESH = pl.DeviceIdType.MESH

epsilon = 1e-06
rope_base = 1000000.0


def norm_piece(values, gain):
    return values * lax.rsqrt(jnp.mean(values * values, -1, keepdims=True) + epsilon) * gain


def rope_tables(position):
    half = HEAD_DIM // 2
    inverse = rope_base ** (-(jnp.arange(half, dtype=jnp.float32) * 2.0 / HEAD_DIM))
    angle = position.astype(jnp.float32)[:, None] * inverse[None, :]
    cosine = jnp.concatenate([jnp.cos(angle), jnp.cos(angle)], -1)
    sine = jnp.concatenate([jnp.sin(angle), jnp.sin(angle)], -1)
    return (cosine, sine)


def turn_half(values):
    half = values.shape[-1] // 2
    return jnp.concatenate([-values[..., half:], values[..., :half]], -1)


def rotate(values, cosine, sine):
    return values * cosine[:, None, :] + turn_half(values) * sine[:, None, :]


def rotate_back(grads, cosine, sine):
    return grads * cosine[:, None, :] - turn_half(grads * sine[:, None, :])


def segment_of(slots, starts):
    return (slots >= starts[1]).astype(jnp.int32) + (slots >= starts[2]).astype(jnp.int32)


def contract_rows(left, right):
    return lax.dot_general(
        left, right, (((0,), (0,)), ((), ())), preferred_element_type=jnp.float32
    )


def contract_columns(left, right):
    return lax.dot_general(
        left, right, (((1,), (1,)), ((), ())), preferred_element_type=jnp.float32
    )


def plain_device(
    tokens, cotangent, lengths, balance, norm1_gain, w_query, b_query, w_key, b_key,
    w_value, b_value, w_out, norm2_gain, w_gate, w_up, w_down,
):
    seq_count = lax.axis_size("seq")
    fsdp_count = lax.axis_size("fsdp")
    seq_rank = lax.axis_index("seq")
    rows_here, width = tokens.shape
    group = seq_count * rows_here
    kv_width = KV_HEADS * HEAD_DIM
    qkv_width = width + 2 * kv_width
    hidden_width = w_gate.shape[1]
    unit = hidden_width // (fsdp_count * seq_count)
    own_units = hidden_width // seq_count
    weight_rows = w_gate.shape[0]
    score_scale = HEAD_DIM ** (-0.5)
    repeat = HEADS // KV_HEADS

    slot = balance % group
    slots_all = lax.all_gather(slot, "seq", axis=0, tiled=True)
    seq_lengths = lengths[0]
    starts = jnp.cumsum(seq_lengths) - seq_lengths
    segment = segment_of(slot, starts)
    segments_all = segment_of(slots_all, starts)
    first_row = jnp.where(segment == 0, starts[0], jnp.where(segment == 1, starts[1], starts[2]))
    cosine, sine = rope_tables(slot - first_row)
    allowed = (segment[:, None] == segments_all[None, :]) & (slots_all[None, :] <= slot[:, None])

    small = jnp.concatenate([norm1_gain, norm2_gain, b_query, b_key, b_value], 0)[None]
    small = lax.all_gather(small, "fsdp", axis=0, tiled=True)
    piece = norm1_gain.shape[0]
    bias_piece = b_key.shape[0]
    gain_one = small[:, :piece].reshape(-1).astype(jnp.float32)
    gain_two = small[:, piece : 2 * piece].reshape(-1).astype(jnp.float32)
    bias_qkv = jnp.concatenate(
        [
            small[:, 2 * piece : 3 * piece].reshape(-1),
            small[:, 3 * piece : 3 * piece + bias_piece].reshape(-1),
            small[:, 3 * piece + bias_piece :].reshape(-1),
        ],
        0,
    ).astype(jnp.float32)
    weight_qkv = lax.all_gather(
        jnp.concatenate([w_query, w_key, w_value], 1), "fsdp", axis=0, tiled=True
    )
    weight_out = lax.all_gather(w_out, "fsdp", axis=0, tiled=True)
    upstream_all = lax.all_gather(cotangent, "seq", axis=0, tiled=True)

    def own_columns(weight):
        cut = weight.reshape(weight_rows, fsdp_count, seq_count, unit)
        return lax.dynamic_index_in_dim(cut, seq_rank, 2, False).reshape(weight_rows, own_units)

    weight_gu = lax.all_gather(
        jnp.concatenate([own_columns(w_gate), own_columns(w_up)], 1), "fsdp", axis=0, tiled=True
    )
    weight_down = lax.all_gather(
        lax.dynamic_slice_in_dim(w_down, seq_rank * unit, unit, 0), "fsdp", axis=0, tiled=True
    )

    inputs = tokens.astype(jnp.float32)
    normed_one = norm_piece(inputs, gain_one).astype(jnp.bfloat16)
    projected = jnp.dot(normed_one, weight_qkv, preferred_element_type=jnp.float32) + bias_qkv
    query_pre = projected[:, :width].reshape(rows_here, HEADS, HEAD_DIM)
    key_pre = projected[:, width : width + kv_width].reshape(rows_here, KV_HEADS, HEAD_DIM)
    value_pre = projected[:, width + kv_width :]
    queries = rotate(query_pre, cosine, sine).astype(jnp.bfloat16)
    keys = rotate(key_pre, cosine, sine).astype(jnp.bfloat16).reshape(rows_here, kv_width)
    values = value_pre.astype(jnp.bfloat16)
    paired = lax.all_gather(jnp.concatenate([keys, values], 1), "seq", axis=0, tiled=True)
    keys_all = paired[:, :kv_width].reshape(group, KV_HEADS, HEAD_DIM)
    values_all = paired[:, kv_width:].reshape(group, KV_HEADS, HEAD_DIM)
    grouped = queries.reshape(rows_here, KV_HEADS, repeat, HEAD_DIM)
    raw = (
        jnp.einsum("qgrd,kgd->grqk", grouped, keys_all, preferred_element_type=jnp.float32)
        * score_scale
    )
    scores = jnp.where(allowed, raw, -jnp.inf)
    expo = jnp.exp(scores - jnp.max(scores, -1, keepdims=True))
    probs = expo / jnp.sum(expo, -1, keepdims=True)
    probs_low = probs.astype(jnp.bfloat16)
    attended = jnp.einsum(
        "grqk,kgd->qgrd", probs_low, values_all, preferred_element_type=jnp.float32
    )
    attended = attended.astype(jnp.bfloat16).reshape(rows_here, width)
    resid = inputs + jnp.dot(attended, weight_out, preferred_element_type=jnp.float32)
    normed_two = norm_piece(resid, gain_two).astype(jnp.bfloat16)

    normed_all = lax.all_gather(normed_two, "seq", axis=0, tiled=True)
    both = jnp.dot(normed_all, weight_gu, preferred_element_type=jnp.float32)
    gate = both[:, :own_units]
    up = both[:, own_units:]
    sigma = jax.nn.sigmoid(gate)
    activated = gate * sigma
    hidden = (activated * up).astype(jnp.bfloat16)
    d_hidden = contract_columns(upstream_all, weight_down)
    d_gate = (d_hidden * up * sigma * (1.0 + gate * (1.0 - sigma))).astype(jnp.bfloat16)
    d_up = (d_hidden * activated).astype(jnp.bfloat16)
    d_both = jnp.concatenate([d_gate, d_up], 1)
    columns = lax.psum_scatter(
        contract_columns(d_both, weight_gu).astype(jnp.bfloat16),
        "seq", scatter_dimension=0, tiled=True,
    ).astype(jnp.float32)
    branch = lax.psum_scatter(
        jnp.dot(hidden, weight_down, preferred_element_type=jnp.float32).astype(jnp.bfloat16),
        "seq", scatter_dimension=0, tiled=True,
    ).astype(jnp.float32)
    layer_out = (resid + branch).astype(jnp.bfloat16)
    grad_down = lax.psum_scatter(
        contract_rows(hidden, upstream_all).astype(jnp.bfloat16),
        "fsdp", scatter_dimension=0, tiled=True,
    ).astype(jnp.float32)
    grad_pair = lax.psum_scatter(
        contract_rows(normed_all, d_both).astype(jnp.bfloat16),
        "fsdp", scatter_dimension=0, tiled=True,
    )
    grad_pair = lax.all_to_all(grad_pair, "seq", split_axis=0, concat_axis=0, tiled=True)
    grad_pair = grad_pair.reshape(seq_count, weight_rows // seq_count, 2, fsdp_count, unit)
    grad_pair = grad_pair.transpose(2, 1, 3, 0, 4).astype(jnp.float32)
    grad_pair = grad_pair.reshape(2, weight_rows // seq_count, hidden_width)

    _, pull_two = jax.vjp(norm_piece, resid, gain_two)
    d_resid_norm, grad_gain_two = pull_two(columns)
    d_resid = cotangent.astype(jnp.float32) + d_resid_norm
    d_branch = d_resid.astype(jnp.bfloat16)
    grad_out = contract_rows(attended, d_branch).astype(jnp.bfloat16)
    d_attended = contract_columns(d_branch, weight_out).astype(jnp.bfloat16)
    d_attended = d_attended.reshape(rows_here, KV_HEADS, repeat, HEAD_DIM)
    d_probs = jnp.einsum(
        "qgrd,kgd->grqk", d_attended, values_all, preferred_element_type=jnp.float32
    )
    delta = jnp.sum(probs * d_probs, -1, keepdims=True)
    d_score = (probs * (d_probs - delta)).astype(jnp.bfloat16)
    d_queries = (
        jnp.einsum("grqk,kgd->qgrd", d_score, keys_all, preferred_element_type=jnp.float32)
        * score_scale
    )
    d_keys = (
        jnp.einsum("grqk,qgrd->kgd", d_score, grouped, preferred_element_type=jnp.float32)
        * score_scale
    )
    d_values = jnp.einsum(
        "grqk,qgrd->kgd", probs_low, d_attended, preferred_element_type=jnp.float32
    )
    d_paired = jnp.concatenate([d_keys.reshape(group, kv_width), d_values.reshape(group, kv_width)], 1)
    d_paired = lax.psum_scatter(
        d_paired.astype(jnp.bfloat16), "seq", scatter_dimension=0, tiled=True
    ).astype(jnp.float32)
    d_query_pre = rotate_back(
        d_queries.reshape(rows_here, HEADS, HEAD_DIM), cosine, sine
    ).astype(jnp.bfloat16)
    d_key_pre = rotate_back(
        d_paired[:, :kv_width].reshape(rows_here, KV_HEADS, HEAD_DIM), cosine, sine
    ).astype(jnp.bfloat16)
    d_value_pre = d_paired[:, kv_width:].astype(jnp.bfloat16)
    d_qkv = jnp.concatenate(
        [
            d_query_pre.reshape(rows_here, width),
            d_key_pre.reshape(rows_here, kv_width),
            d_value_pre,
        ],
        1,
    )
    grad_qkv = contract_rows(normed_one, d_qkv).astype(jnp.bfloat16)
    grad_bias = jnp.sum(d_qkv.astype(jnp.float32), 0)
    d_normed_one = contract_columns(d_qkv, weight_qkv)
    _, pull_one = jax.vjp(norm_piece, inputs, gain_one)
    d_input_norm, grad_gain_one = pull_one(d_normed_one)
    input_grad = (d_resid + d_input_norm).astype(jnp.bfloat16)

    def summed(value):
        value = lax.psum_scatter(value, "fsdp", scatter_dimension=0, tiled=True)
        return lax.psum_scatter(value, "seq", scatter_dimension=0, tiled=True).astype(jnp.float32)

    grad_out = summed(grad_out)
    grad_qkv = summed(grad_qkv)
    vectors = lax.psum(
        jnp.concatenate([grad_gain_one, grad_gain_two, grad_bias], 0), ("fsdp", "seq")
    )
    own = width // (fsdp_count * seq_count)
    first = (lax.axis_index("fsdp") * seq_count + seq_rank) * own

    def own_part(offset):
        return lax.dynamic_slice_in_dim(vectors, offset + first, own, 0)

    biases = 2 * width
    return (
        layer_out,
        input_grad,
        own_part(0),
        grad_qkv[:, :width],
        own_part(biases),
        grad_qkv[:, width : width + kv_width],
        vectors[biases + width : biases + width + kv_width],
        grad_qkv[:, width + kv_width :],
        vectors[biases + width + kv_width :],
        grad_out,
        own_part(width),
        grad_pair[0],
        grad_pair[1],
        grad_down,
    )


ORDER = (1, 3, 2, 0)


class SumChain:
    def __init__(self, held, z_one, z_two, z_three, there, index):
        self.rank = lax.axis_index("seq")
        s = self.rank
        self.held, self.arrived = held, (z_one, z_two, z_three)
        self.up = [
            there(held(1), z_one, index, seq=s + 1),
            there(held(2), z_two.at[0], index + 2, seq=s + 1),
            there(held(3), z_three.at[0], index + 4, seq=s + 1),
        ]
        self.down = [
            there(held(3), z_one, index + 1, seq=s - 1),
            there(held(2), z_two.at[1], index + 3, seq=s - 1),
            there(held(1), z_three.at[1], index + 5, seq=s - 1),
        ]

    def add(self, j, arrived):
        ref = self.held(j)
        total = ref[...].astype(jnp.float32) + arrived[...].astype(jnp.float32)
        ref[...] = total.astype(jnp.bfloat16)

    def one(self):
        pl.when(self.rank == 0)(self.up[0].start)
        pl.when(self.rank == 3)(self.down[0].start)

    def add_one(self):
        @pl.when(self.rank == 1)
        def _():
            self.up[0].wait_recv()
            self.add(2, self.arrived[0])

        @pl.when(self.rank == 2)
        def _():
            self.down[0].wait_recv()
            self.add(2, self.arrived[0])

    def two(self):
        pl.when(self.rank <= 1)(self.up[1].start)
        pl.when(self.rank >= 2)(self.down[1].start)

    def three(self):
        @pl.when((self.rank == 1) | (self.rank == 2))
        def _():
            self.up[1].wait_recv()
            self.add(3, self.arrived[1].at[0])
            self.down[1].wait_recv()
            self.add(1, self.arrived[1].at[1])

        pl.when(self.rank <= 2)(self.up[2].start)
        pl.when(self.rank >= 1)(self.down[2].start)

    def last(self, out):
        out[...] = self.held(0)[...].astype(jnp.float32)

        @pl.when(self.rank >= 1)
        def _():
            self.up[2].wait_recv()
            out[...] += self.arrived[2][0].astype(jnp.float32)

        @pl.when(self.rank <= 2)
        def _():
            self.down[2].wait_recv()
            out[...] += self.arrived[2][1].astype(jnp.float32)

    def one_sent(self):
        pl.when(self.rank == 0)(self.up[0].wait_send)
        pl.when(self.rank == 3)(self.down[0].wait_send)

    def sent(self):
        pl.when(self.rank <= 1)(self.up[1].wait_send)
        pl.when(self.rank >= 2)(self.down[1].wait_send)
        pl.when(self.rank <= 2)(self.up[2].wait_send)
        pl.when(self.rank >= 1)(self.down[2].wait_send)


class SumPlane:
    def __init__(self, buffer, block, plane, arrived, by_x, by_y, ended, there, index):
        half = buffer.shape[1] // 2
        low, high = pl.ds(0, half), pl.ds(half, half)

        def part(k):
            return buffer.at[pl.ds(pl.multiple_of(plane[k] * block, 16), block)]

        self.parts = own, to_x, to_y, to_both = [part(k) for k in (0, 2, 4, 6)]
        self.arrived, self.by_x, self.by_y, self.ended, self.half = arrived, by_x, by_y, ended, half
        self.core = [
            there(part(2 * i + 1), arrived.at[i], index + i, fsdp=plane[1]) for i in range(4)
        ]
        self.first = [
            there(to_both.at[:, low], by_x.at[1], index + 5, fsdp=plane[2]),
            there(to_both.at[:, high], by_y.at[1], index + 7, fsdp=plane[4]),
            there(to_x.at[:, low], by_x.at[0], index + 4, fsdp=plane[2]),
            there(to_y.at[:, high], by_y.at[0], index + 6, fsdp=plane[4]),
        ]
        self.second = [
            there(to_y.at[:, low], ended.at[0], index + 8, fsdp=plane[4]),
            there(to_x.at[:, high], ended.at[1], index + 9, fsdp=plane[2]),
        ]

    def start_core(self):
        for copy in self.core:
            copy.start()

    def start_first(self):
        for i in (3, 1, 2, 0):
            self.core[i].wait_recv()
            part = self.parts[i]
            total = part[...].astype(jnp.float32) + self.arrived[i].astype(jnp.float32)
            part[...] = total.astype(jnp.bfloat16)
        for copy in self.first:
            copy.start()

    def start_second(self):
        half = self.half
        _, to_x, to_y, _ = self.parts
        self.first[0].wait_recv()
        total = to_y[:, :half].astype(jnp.float32) + self.by_x[1].astype(jnp.float32)
        to_y[:, :half] = total.astype(jnp.bfloat16)
        self.second[0].start()
        self.first[1].wait_recv()
        total = to_x[:, half:].astype(jnp.float32) + self.by_y[1].astype(jnp.float32)
        to_x[:, half:] = total.astype(jnp.bfloat16)
        self.second[1].start()

    def finish(self):
        half = self.half
        own = self.parts[0]
        self.first[2].wait_recv()
        self.second[0].wait_recv()
        total = own[:, :half].astype(jnp.float32) + self.by_x[0].astype(jnp.float32)
        own[:, :half] = (total + self.ended[0].astype(jnp.float32)).astype(jnp.bfloat16)
        self.first[3].wait_recv()
        self.second[1].wait_recv()
        total = own[:, half:].astype(jnp.float32) + self.by_y[0].astype(jnp.float32)
        own[:, half:] = (total + self.ended[1].astype(jnp.float32)).astype(jnp.bfloat16)

    def sent(self):
        for copy in self.core + self.first + self.second:
            copy.wait_send()


def in_order(partial, rows):
    def held(j):
        return partial.at[ORDER.index(j) * rows : (ORDER.index(j) + 1) * rows]

    return held


def front_kernel(
    lengths, tokens, cotangent, small, balance, inverse,
    w_query, w_key, w_value, w_out, w_gate, w_up, w_down,
    gu_all, down_all, upstream_all, normed_all, hidden, factor_gate, factor_up, qkv_out, out_out,
    queries, paired_out, slots_out, logsum, attended, resid, normed_one, gain_one, gain_two,
    slot_row, first_row, cosine, sine,
    q_w, kv_w, out_w, gate_v, up_v, gu, normed, kv, small_own, small_all, slots_all, bias,
    cotangent_v, down_raw, down_own, hidden_v, gate_part, up_part,
    local, ssem, rsem, zsend, zrecv,
):
    f = lax.axis_index("fsdp")
    s = lax.axis_index("seq")
    rows, width = tokens.shape
    n_f, n_s = 8, slots_all.shape[0]
    group = n_s * rows
    block = w_query.shape[0]
    unit_pad = down_own.shape[0]
    unit = w_gate.shape[1] // (n_f * n_s)
    units = n_f * unit_pad
    kv_width = KV_HEADS * HEAD_DIM
    qkv_width = width + 2 * kv_width
    scale = HEAD_DIM ** (-0.5)
    repeat = HEADS // KV_HEADS
    plane = [f ^ k for k in range(n_f)]

    entry = pltpu.get_barrier_semaphore()
    for k in range(1, n_f):
        pl.semaphore_signal(entry, inc=1, device_id={"fsdp": plane[k]}, device_id_type=MESH)
    for j in range(1, n_s):
        pl.semaphore_signal(
            entry, inc=1, device_id={"seq": lax.rem(s + j, n_s)}, device_id_type=MESH
        )

    def here(source, target, index):
        return pltpu.make_async_copy(source, target, local.at[index])

    def there(source, target, index, **device):
        return pltpu.make_async_remote_copy(
            src_ref=source, dst_ref=target, send_sem=ssem.at[index], recv_sem=rsem.at[index],
            device_id=device, device_id_type=MESH,
        )

    def own_rows(ref, owner, size, start=0, count=None):
        first = pl.multiple_of(owner * size + start, 16)
        return ref.at[pl.ds(first, size if count is None else count)]

    class Gather:
        def __init__(self, source, target, size, index):
            half = size // 2
            x, y, c = plane[2], plane[4], plane[1]
            self.own = here(source, own_rows(target, f, size), index // 8) if source is not None else None
            if source is None:
                source = own_rows(target, f, size)
            mine = own_rows(target, f, size)
            self.first = [
                there(source, mine, index, fsdp=x),
                there(source, mine, index + 1, fsdp=y),
                there(source, mine, index + 2, fsdp=c),
            ]
            from_x, from_y = own_rows(target, x, size), own_rows(target, y, size)
            part_x = own_rows(target, x, size, 0, half)
            part_y = own_rows(target, y, size, half, half)
            self.second = [
                there(part_x, part_x, index + 3, fsdp=y),
                there(part_y, part_y, index + 4, fsdp=x),
                there(from_x, from_x, index + 5, fsdp=c),
                there(from_y, from_y, index + 6, fsdp=c),
            ]
            diagonal = own_rows(target, plane[6], size)
            self.third = there(diagonal, diagonal, index + 7, fsdp=c)

        def start(self):
            if self.own is not None:
                self.own.start()
            for copy in self.first:
                copy.start()

        def forward(self):
            self.first[0].wait_recv()
            self.second[0].start()
            self.second[2].start()
            self.first[1].wait_recv()
            self.second[1].start()
            self.second[3].start()

        def last(self):
            self.second[0].wait_recv()
            self.second[1].wait_recv()
            self.third.start()

        def finish(self):
            if self.own is not None:
                self.own.wait()
            self.first[2].wait_recv()
            self.second[2].wait_recv()
            self.second[3].wait_recv()
            self.third.wait_recv()

        def sent(self):
            for copy in self.first + self.second + [self.third]:
                copy.wait_send()

    class Chain:
        def __init__(self, target, index, own=None):
            self.steps = []
            for step in range(1, n_s):
                up = own_rows(target, s - (step - 1), rows)
                down = own_rows(target, s + (step - 1), rows)
                source = own if own is not None and step == 1 else up
                i = index + 2 * (step - 1)
                self.steps.append((
                    pltpu.make_async_remote_copy(
                        src_ref=source, dst_ref=up, send_sem=zsend.at[i], recv_sem=zrecv.at[i],
                        device_id={"seq": s + 1}, device_id_type=MESH,
                    ),
                    pltpu.make_async_remote_copy(
                        src_ref=down if source is up else source, dst_ref=down, send_sem=zsend.at[i + 1], recv_sem=zrecv.at[i + 1],
                        device_id={"seq": s - 1}, device_id_type=MESH,
                    ),
                    (s >= step - 1) & (s < n_s - 1),
                    (s >= 1) & (s <= n_s - step),
                    s >= step,
                    s <= n_s - 1 - step,
                ))

        def send(self, step):
            up, down, can_up, can_down, _, _ = self.steps[step - 1]
            pl.when(can_up)(up.start)
            pl.when(can_down)(down.start)

        def receive(self, step):
            up, down, _, _, from_below, from_above = self.steps[step - 1]
            pl.when(from_below)(up.wait_recv)
            pl.when(from_above)(down.wait_recv)

        def sent(self):
            for up, down, can_up, can_down, _, _ in self.steps:
                pl.when(can_up)(up.wait_send)
                pl.when(can_down)(down.wait_send)

    own_block = pl.ds(pl.multiple_of(f * block, 16), block)
    pieces = [
        here(w_key, kv_w.at[own_block, pl.ds(0, kv_width)], 6),
        here(w_value, kv_w.at[own_block, pl.ds(kv_width, kv_width)], 7),
        here(w_query, q_w.at[own_block], 5),
        here(cotangent, cotangent_v, 8),
    ]
    load_gate = here(w_gate, gate_v, 9)
    load_up = here(w_up, up_v, 10)
    first_unit = pl.multiple_of(s * unit // 16 * 16, 16)
    load_down = here(w_down.at[pl.ds(first_unit, unit_pad)], down_raw, 15)
    for copy in pieces:
        copy.start()
    load_gate.start()
    load_up.start()
    load_down.start()

    slot = (balance[...] & (group - 1)).astype(jnp.float32)
    second = lengths[0, 0].astype(jnp.float32)
    third = (lengths[0, 0] + lengths[0, 1]).astype(jnp.float32)
    first = jnp.where(slot >= third, third, jnp.where(slot >= second, second, 0.0))
    slot_row[...] = jnp.broadcast_to(slot, slot_row.shape)
    first_row[...] = jnp.broadcast_to(first, first_row.shape)
    slots_all[s] = jnp.broadcast_to(slot, (128, rows)).T
    lanes = lax.broadcasted_iota(jnp.int32, small.shape, 1)
    sorts = lax.broadcasted_iota(jnp.int32, small.shape, 0)
    small_own[...] = jnp.where(
        sorts < 3,
        pltpu.roll(small[...], lax.rem(f, 2) * block, 1),
        pltpu.roll(small[...], f * (kv_width // n_f), 1),
    )
    small_all[f] = small_own[...]

    gather_kv = Gather(None, kv_w, block, 0)
    gather_q = Gather(None, q_w, block, 8)
    gather_out = Gather(w_out, out_w, block, 16)
    gather_gu = Gather(None, gu, block, 24)
    gather_down = Gather(down_own, down_all, unit_pad, 32)
    chain_up = Chain(upstream_all, 0, cotangent_v)
    chain_normed = Chain(normed, 6)
    send_small = [
        there(small_own, small_all.at[f], 40 + k, fsdp=plane[k]) for k in range(1, n_f)
    ]
    send_slots = [
        there(slots_all.at[s], slots_all.at[s], 48 + j, seq=lax.rem(s + j, n_s))
        for j in range(1, n_s)
    ]
    send_kv = [
        there(kv.at[s], kv.at[s], 52 + j, seq=lax.rem(s + j, n_s)) for j in range(1, n_s)
    ]
    for copy in pieces[:2]:
        copy.wait()
    pl.semaphore_wait(entry, n_f - 1 + n_s - 1)
    gather_kv.start()
    for copy in send_small + send_slots:
        copy.start()
    for copy in pieces[2:]:
        copy.wait()
    chain_up.send(1)
    save_own = here(cotangent_v, own_rows(upstream_all, s, rows), 8)
    save_own.start()
    position = slots_all[s] - jnp.broadcast_to(first, (128, rows)).T
    angle = position * inverse[...]
    cosine[...] = jnp.cos(angle)
    sine[...] = jnp.where(
        lax.broadcasted_iota(jnp.int32, angle.shape, 1) < HEAD_DIM // 2, -1.0, 1.0
    ) * jnp.sin(angle)

    for copy in send_small + send_slots:
        copy.wait_recv()

    def joined(sort):
        return jnp.concatenate(
            [
                small_all[2 * i, sort : sort + 1] + small_all[2 * i + 1, sort : sort + 1]
                for i in range(n_f // 2)
            ],
            1,
        )

    gain_one[...] = joined(0)
    gain_two[...] = joined(1)
    bias_query = joined(2)
    bias_key = sum(small_all[i, 3:4, :kv_width] for i in range(n_f))
    bias_value = sum(small_all[i, 4:5, :kv_width] for i in range(n_f))

    inputs = tokens[...].astype(jnp.float32)
    root = lax.rsqrt(jnp.mean(inputs * inputs, -1, keepdims=True) + epsilon)
    normed_one[...] = (inputs * root * gain_one[...]).astype(jnp.bfloat16)
    gather_kv.forward()
    gather_q.start()
    gather_kv.last()
    gather_kv.finish()

    def turned(value):
        return value * cosine[...] + pltpu.roll(value, HEAD_DIM // 2, 1) * sine[...]

    rows_low = normed_one[...]
    pair = jnp.dot(rows_low, kv_w[:, :kv_width], preferred_element_type=jnp.float32)
    pair = pair + bias_key
    for g in range(KV_HEADS):
        columns = slice(g * HEAD_DIM, (g + 1) * HEAD_DIM)
        kv[s, :, columns] = turned(pair[:, columns]).astype(jnp.bfloat16)
    pair = jnp.dot(rows_low, kv_w[:, kv_width:], preferred_element_type=jnp.float32)
    kv[s, :, kv_width:] = (pair + bias_value).astype(jnp.bfloat16)
    for copy in send_kv:
        copy.start()
    save_kv_w = here(kv_w, qkv_out.at[:, pl.ds(width, 2 * kv_width)], 11)
    save_kv_w.start()

    load_gate.wait()
    load_up.wait()
    pick_units(gate_v, up_v, gu.at[own_block], w_gate.shape[1] // n_f, unit, unit_pad)
    gather_q.forward()
    load_down.wait()
    raw = down_raw[...].astype(jnp.float32)
    shifted = jnp.concatenate([raw[8:], jnp.zeros((8, width), jnp.float32)], 0)
    raw = jnp.where(lax.rem(s * unit, 16) == 0, raw, shifted)
    inside = lax.broadcasted_iota(jnp.int32, raw.shape, 0) < unit
    down_own[...] = jnp.where(inside, raw, 0.0).astype(jnp.bfloat16)

    for j in range(n_s):
        keys_slot = slots_all[j]
        keys_slot = jnp.concatenate([keys_slot] * (rows // 128), 1)
        ok = (keys_slot <= slot) & (keys_slot >= first)
        bias[j * rows : (j + 1) * rows] = jnp.where(ok, 0.0, -1e30)

    gather_q.last()
    gather_out.start()
    gather_q.finish()
    save_q_w = here(q_w, qkv_out.at[:, pl.ds(0, width)], 0)
    save_q_w.start()
    for g in range(HEADS // 2):
        columns = slice(g * 2 * HEAD_DIM, (g + 1) * 2 * HEAD_DIM)
        pair = jnp.dot(rows_low, q_w[:, columns], preferred_element_type=jnp.float32)
        pair = pair + bias_query[:, columns]
        for h in range(2):
            part = turned(pair[:, h * HEAD_DIM : (h + 1) * HEAD_DIM]).astype(jnp.bfloat16)
            queries[:, (2 * g + h) * HEAD_DIM : (2 * g + h + 1) * HEAD_DIM] = part

    chain_up.receive(1)
    for copy in send_kv:
        copy.wait_recv()
    chain_up.send(2)
    save_kv = here(kv, paired_out, 12)
    save_kv.start()
    slots_out[...] = slots_all[...]

    for g in range(KV_HEADS):
        keys = kv[:, :, g * HEAD_DIM : (g + 1) * HEAD_DIM].reshape(n_s * rows, HEAD_DIM)
        values = kv[:, :, kv_width + g * HEAD_DIM : kv_width + (g + 1) * HEAD_DIM]
        values = values.reshape(n_s * rows, HEAD_DIM)

        def head(i, carry, g=g, keys=keys, values=values):
            h = g * repeat + i
            columns = pl.ds(pl.multiple_of(h * HEAD_DIM, HEAD_DIM), HEAD_DIM)
            raw = lax.dot_general(
                keys, queries[:, columns], (((1,), (1,)), ((), ())),
                preferred_element_type=jnp.float32,
            )
            scores = raw * scale + bias[...]
            top = jnp.max(scores, 0, keepdims=True)
            expo = jnp.exp(scores - top)
            total = jnp.sum(expo, 0, keepdims=True)
            probs = (expo * (1.0 / total)).astype(jnp.bfloat16)
            mixed = lax.dot_general(
                values, probs, (((0,), (0,)), ((), ())), preferred_element_type=jnp.float32
            )
            attended[:, columns] = mixed.T.astype(jnp.bfloat16)
            logsum[pl.ds(pl.multiple_of(h * 8, 8), 8)] = jnp.broadcast_to(
                top + jnp.log(total), (8, rows)
            )
            return carry

        lax.fori_loop(0, repeat, head, 0)
        if g == 0:
            gather_out.forward()

    gather_out.last()
    gather_gu.start()
    gather_out.finish()
    save_out = here(out_w, out_out, 13)
    save_out.start()
    mixed = attended[...]
    for g in range(width // 256):
        columns = slice(g * 256, (g + 1) * 256)
        part = jnp.dot(mixed, out_w[:, columns], preferred_element_type=jnp.float32)
        resid[:, columns] = tokens[:, columns].astype(jnp.float32) + part
    value = resid[...]
    root = lax.rsqrt(jnp.mean(value * value, -1, keepdims=True) + epsilon)
    own_tokens = pl.ds(pl.multiple_of(s * rows, rows), rows)
    normed[own_tokens] = (value * root * gain_two[...]).astype(jnp.bfloat16)
    chain_normed.send(1)

    wide = hidden_v.shape[2]
    count = units // wide

    def saves(owner, t, slot):
        place = (
            pl.ds(pl.multiple_of(owner * rows, rows), rows),
            pl.ds(pl.multiple_of(t * wide, wide), wide),
        )
        return [
            here(part.at[slot], whole.at[place], 16 + 3 * slot + i)
            for i, (part, whole) in enumerate(
                ((hidden_v, hidden), (gate_part, factor_gate), (up_part, factor_up))
            )
        ]

    def feed(owner, done):
        def body(t, carry):
            slot = lax.rem(t + done, 2)
            mine = normed[pl.ds(pl.multiple_of(owner * rows, rows), rows)]
            gate_columns = pl.ds(pl.multiple_of(t * wide, wide), wide)
            up_columns = pl.ds(pl.multiple_of(units + t * wide, wide), wide)
            gate = jnp.dot(mine, gu[:, gate_columns], preferred_element_type=jnp.float32)
            up = jnp.dot(mine, gu[:, up_columns], preferred_element_type=jnp.float32)
            sigma = jax.nn.sigmoid(gate)
            activated = gate * sigma

            @pl.when(t + done >= 2)
            def _():
                for copy in saves(owner, t, slot):
                    copy.wait()

            hidden_v[slot] = (activated * up).astype(jnp.bfloat16)
            gate_part[slot] = (up * sigma * (1.0 + gate * (1.0 - sigma))).astype(jnp.bfloat16)
            up_part[slot] = activated.astype(jnp.bfloat16)
            for copy in saves(owner, t, slot):
                copy.start()
            return carry

        lax.fori_loop(0, count, body, 0)

    chain_up.receive(2)
    chain_normed.receive(1)
    chain_normed.send(2)
    gather_gu.forward()
    chain_normed.receive(2)
    chain_normed.send(3)
    gather_gu.last()
    gather_down.start()
    gather_gu.finish()
    save_gu = here(gu, gu_all, 22)
    save_gu.start()
    chain_normed.receive(3)
    chain_up.send(3)
    save_normed = here(normed, normed_all, 23)
    save_normed.start()
    feed(s, 0)
    feed(s ^ 1, count)
    feed(s ^ 2, 2 * count)
    gather_down.forward()
    feed(s ^ 3, 3 * count)
    gather_down.last()
    for t in (count - 2, count - 1):
        for copy in saves(s ^ 3, t, (t + 3 * count) % 2):
            copy.wait()
    chain_up.receive(3)
    gather_down.finish()
    for copy in (save_own, save_kv_w, save_q_w, save_kv, save_out, save_gu, save_normed):
        copy.wait()
    for part in (gather_kv, gather_q, gather_out, gather_gu, gather_down, chain_up, chain_normed):
        part.sent()
    for copy in send_small + send_slots + send_kv:
        copy.wait_send()


def pick_units(gate, up, out, stride, unit, padded):
    rank = lax.axis_index("seq")
    pieces = gate.shape[1] // stride
    half = out.shape[1] // 2
    window, tile = 512, 128
    rows = lax.broadcasted_iota(jnp.int32, (window, tile), 0)
    columns = lax.broadcasted_iota(jnp.int32, (window, tile), 1)
    for first in range(0, 2 * half, tile):
        source = gate if first < half else up
        local = first % half
        total = jnp.zeros((out.shape[0], tile), jnp.float32)
        for f in range(pieces):
            low = max(local, f * padded)
            high = min(local + tile, f * padded + unit)
            if low >= high:
                continue
            begin = f * stride + rank * unit
            base = jnp.minimum(begin // 128, (source.shape[1] - window) // 128) * 128
            base = pl.multiple_of(base, 128)
            wanted = columns + (local - f * padded + begin - base)
            inside = (columns >= low - local) & (columns < high - local)
            chosen = jnp.where((rows == wanted) & inside, 1.0, 0.0).astype(jnp.bfloat16)
            total += jnp.dot(
                source[:, pl.ds(base, window)], chosen, preferred_element_type=jnp.float32
            )
        out[:, first : first + tile] = total.astype(jnp.bfloat16)


def front(tokens, cotangent, lengths, balance, vectors, weights):
    rows, width = tokens.shape
    n_s = lax.axis_size("seq")
    w_query, w_key, w_value, w_out, w_gate, w_up, w_down = weights
    block = w_query.shape[0]
    unit_pad = -(-w_down.shape[0] // n_s // 16) * 16
    kv_width = KV_HEADS * HEAD_DIM
    qkv_width = width + 2 * kv_width
    units = 8 * unit_pad
    group = n_s * rows
    wide = 768
    low, full = jnp.bfloat16, jnp.float32
    small = sum(
        jnp.pad(v.astype(full)[None], ((i, 7 - i), (0, 2 * block - v.shape[0])))
        for i, v in enumerate(vectors)
    )
    half = HEAD_DIM // 2
    inverse = rope_base ** (-(np.arange(half, dtype=np.float32) * np.float32(2.0 / HEAD_DIM)))
    inverse = jnp.asarray(np.concatenate([inverse, inverse])[None], full)
    smem = pl.BlockSpec(memory_space=pltpu.SMEM)
    vmem = pl.BlockSpec(memory_space=pltpu.VMEM)
    hbm = pl.BlockSpec(memory_space=pl.ANY)
    shape = jax.ShapeDtypeStruct
    return pl.pallas_call(
        front_kernel,
        in_specs=[smem, vmem, hbm, vmem, vmem, vmem] + [hbm] * 7,
        out_specs=[hbm] * 9 + [vmem, hbm] + [vmem] * 11,
        out_shape=[
            shape((width, 2 * units), low),
            shape((units, width), low),
            shape((group, width), low),
            shape((group, width), low),
            shape((group, units), low),
            shape((group, units), low),
            shape((group, units), low),
            shape((width, qkv_width), low),
            shape((width, width), low),
            shape((rows, width), low),
            shape((n_s, rows, 2 * kv_width), low),
            shape((n_s, rows, 128), full),
            shape((8 * HEADS, rows), full),
            shape((rows, width), low),
            shape((rows, width), full),
            shape((rows, width), low),
            shape((1, width), full),
            shape((1, width), full),
            shape((8, rows), full),
            shape((8, rows), full),
            shape((rows, HEAD_DIM), full),
            shape((rows, HEAD_DIM), full),
        ],
        scratch_shapes=[
            pltpu.VMEM((width, width), low),
            pltpu.VMEM((width, 2 * kv_width), low),
            pltpu.VMEM((width, width), low),
            pltpu.VMEM(w_gate.shape, low),
            pltpu.VMEM(w_up.shape, low),
            pltpu.VMEM((width, 2 * units), low),
            pltpu.VMEM((group, width), low),
            pltpu.VMEM((n_s, rows, 2 * kv_width), low),
            pltpu.VMEM((8, 2 * block), full),
            pltpu.VMEM((8, 8, 2 * block), full),
            pltpu.VMEM((n_s, rows, 128), full),
            pltpu.VMEM((group, rows), full),
            pltpu.VMEM((rows, width), low),
            pltpu.VMEM((unit_pad, width), low),
            pltpu.VMEM((unit_pad, width), low),
            pltpu.VMEM((2, rows, wide), low),
            pltpu.VMEM((2, rows, wide), low),
            pltpu.VMEM((2, rows, wide), low),
            pltpu.SemaphoreType.DMA((24,)),
            pltpu.SemaphoreType.DMA((56,)),
            pltpu.SemaphoreType.DMA((56,)),
            pltpu.SemaphoreType.DMA((12,)),
            pltpu.SemaphoreType.DMA((12,)),
        ],
        compiler_params=pltpu.CompilerParams(
            collective_id=0, has_side_effects=True, vmem_limit_bytes=62 * 2**20
        ),
        name="front",
    )(
        lengths, tokens, cotangent, small, balance.reshape(1, rows), inverse,
        w_query, w_key, w_value, w_out, w_gate, w_up, w_down,
    )


def ffn_kernel(
    normed_all, upstream_all, w_gu, w_down, hidden_all, factor_gate, factor_up,
    columns, grad_down, gu_sum, gu_far, branch, down_arrived, gu_arrived,
    normed, upstream, gu, down, hidden, d_both, partial, z_one, z_two, z_three,
    down_x, down_y, down_last, down_piece,
    load, ssem, rsem,
):
    f = lax.axis_index("fsdp")
    s = lax.axis_index("seq")
    n_s = len(ORDER)
    group, width = normed.shape
    rows = group // n_s
    half_rows = group // 2
    units = down.shape[0]
    tile = 256
    tiles = units // tile
    wide = 768
    block = gu.shape[0] // 8
    unit = units // 8
    half = width // 2
    plane = [f ^ k for k in range(8)]
    full = jnp.float32

    entry = pltpu.get_barrier_semaphore()
    for k in (1, 2, 4):
        pl.semaphore_signal(entry, inc=1, device_id={"fsdp": plane[k]}, device_id_type=MESH)
    for j in (1, n_s - 1):
        pl.semaphore_signal(
            entry, inc=1, device_id={"seq": lax.rem(s + j, n_s)}, device_id_type=MESH
        )

    def here(source, target, index):
        return pltpu.make_async_copy(source, target, load.at[index])

    def there(source, target, index, **device):
        return pltpu.make_async_remote_copy(
            src_ref=source, dst_ref=target, send_sem=ssem.at[index], recv_sem=rsem.at[index],
            device_id=device, device_id_type=MESH,
        )

    def part(ref, owner, size):
        return ref.at[pl.ds(pl.multiple_of(owner * size, 16), size)]

    early, late = range(0, n_s // 2), range(n_s // 2, n_s)

    def rows_of(p):
        return pl.ds(p * rows, rows)

    def row_loads(p):
        owner = lax.rem(s + n_s - ORDER[p], n_s)
        mine = rows_of(p)
        return [
            here(part(upstream_all, owner, rows), upstream.at[mine], 5 * p),
            here(part(factor_gate, owner, rows), d_both.at[mine, pl.ds(0, units)], 5 * p + 1),
            here(part(factor_up, owner, rows), d_both.at[mine, pl.ds(units, units)], 5 * p + 2),
            here(part(hidden_all, owner, rows), hidden.at[mine], 5 * p + 3),
            here(part(normed_all, owner, rows), normed.at[mine], 5 * p + 4),
        ]

    def down_load(t):
        mine = pl.ds(pl.multiple_of(t * wide, wide), wide)
        return here(w_down.at[mine], down.at[mine], 20 + t)

    def gu_load(n):
        mine = pl.ds(pl.multiple_of(n * 512, 512), 512)
        return here(w_gu.at[mine], gu.at[mine], 23 + n)

    loads = [row_loads(p) for p in range(n_s)]
    order = [loads[0][0], loads[1][0], down_load(0)]
    order += [loads[p][i] for i in (1, 2) for p in early]
    order += [down_load(t) for t in range(1, units // wide)]
    order += [gu_load(n) for n in range(width // 512)]
    order += [loads[p][i] for i in (0, 1, 2) for p in late]
    order += [loads[p][i] for i in (3, 4) for p in range(n_s)]
    for copy in order:
        copy.start()

    def forward(blocks, wait):
        for p in blocks:
            for copy in loads[p][:3]:
                copy.wait()
        mine = pl.ds(blocks[0] * rows, len(blocks) * rows)

        def body(t, carry):
            if wait:
                down_load(t).wait()
            gate_columns = pl.ds(pl.multiple_of(t * wide, wide), wide)
            up_columns = pl.ds(pl.multiple_of(units + t * wide, wide), wide)
            d_hidden = lax.dot_general(
                upstream[mine], down[gate_columns], (((1,), (1,)), ((), ())),
                preferred_element_type=full,
            )
            value = d_hidden * d_both[mine, gate_columns].astype(full)
            d_both[mine, gate_columns] = value.astype(jnp.bfloat16)
            value = d_hidden * d_both[mine, up_columns].astype(full)
            d_both[mine, up_columns] = value.astype(jnp.bfloat16)
            return carry

        lax.fori_loop(0, units // wide, body, 0)

    def backward(blocks, wait):
        part_rows = pl.ds(blocks[0] * rows, len(blocks) * rows)

        def body(n, carry):
            if wait:
                gu_load(n).wait()
            out_columns = pl.ds(pl.multiple_of(n * 512, 512), 512)
            value = lax.dot_general(
                d_both[part_rows], gu[out_columns], (((1,), (1,)), ((), ())),
                preferred_element_type=full,
            )
            partial[part_rows, out_columns] = value.astype(jnp.bfloat16)
            return carry

        lax.fori_loop(0, width // 512, body, 0)

    chain = SumChain(in_order(partial, rows), z_one, z_two, z_three, there, 0)
    pieces = [(first, min(group, units - first)) for first in range(0, units, group)]
    forward(early, True)
    backward(early, True)
    pl.semaphore_wait(entry, 5)
    chain.one()
    forward(late, False)
    backward(late, False)
    chain.add_one()
    chain.two()

    for p in range(n_s):
        loads[p][3].wait()
        loads[p][4].wait()

    def down_body(t, carry):
        unit_rows = pl.ds(pl.multiple_of(t * tile, tile), tile)
        value = lax.dot_general(
            hidden[:, unit_rows], upstream[...], (((0,), (0,)), ((), ())),
            preferred_element_type=full,
        )
        down[unit_rows] = value.astype(jnp.bfloat16)
        return carry

    lax.fori_loop(0, tiles, down_body, 0)
    down_core = [
        there(part(down, plane[2 * i + 1], unit), down_arrived.at[i], 6 + i, fsdp=plane[1])
        for i in range(4)
    ]
    for copy in down_core:
        copy.start()

    def gu_body(m, carry):
        in_columns = pl.ds(pl.multiple_of(m * tile, tile), tile)
        turned = normed[:, in_columns].T
        for first in range(0, 2 * units, units // 3):
            value = jnp.dot(turned, d_both[:, first : first + units // 3], preferred_element_type=full)
            gu[in_columns, first : first + units // 3] = value.astype(jnp.bfloat16)
        return carry

    lax.fori_loop(0, 2, gu_body, 0)

    def add_arrived(i, ref, size, arrived, pieces, copies, index):
        copies[i].wait_recv()
        fetch = [
            here(arrived.at[i, :, columns], piece, index + k)
            for k, (columns, piece) in enumerate(pieces)
        ]
        for copy in fetch:
            copy.start()
        target = part(ref, plane[2 * i], size)
        for copy, (columns, piece) in zip(fetch, pieces):
            copy.wait()
            target[:, columns] = (
                target[:, columns].astype(full) + piece[...].astype(full)
            ).astype(jnp.bfloat16)

    down_pieces = [(pl.ds(0, width), down_piece)]
    for i in (3, 1, 2, 0):
        add_arrived(i, down, unit, down_arrived, down_pieces, down_core, 26)
    to_x, to_y, to_both = [part(down, plane[k], unit) for k in (2, 4, 6)]
    low_half, high_half = pl.ds(0, half), pl.ds(half, half)
    down_first = [
        there(to_x.at[:, low_half], down_x.at[0], 10, fsdp=plane[2]),
        there(to_both.at[:, low_half], down_x.at[1], 11, fsdp=plane[2]),
        there(to_y.at[:, high_half], down_y.at[0], 12, fsdp=plane[4]),
        there(to_both.at[:, high_half], down_y.at[1], 13, fsdp=plane[4]),
    ]
    for copy in down_first:
        copy.start()
    chain.three()
    lax.fori_loop(2, width // tile, gu_body, 0)
    gu_core = [
        there(part(gu, plane[2 * i + 1], block), gu_arrived.at[i], 16 + i, fsdp=plane[1])
        for i in range(4)
    ]
    for copy in gu_core:
        copy.start()

    again = [
        here(
            w_down.at[first : first + count],
            d_both.at[:count, i * width : (i + 1) * width], 32 + i,
        )
        for i, (first, count) in enumerate(pieces)
    ]
    for copy in again:
        copy.start()
    for copy in again:
        copy.wait()

    def branch_body(n, carry):
        out_columns = pl.ds(pl.multiple_of(n * wide, wide), wide)
        for m in range(2):
            mine = slice(m * half_rows, (m + 1) * half_rows)
            value = jnp.zeros((half_rows, wide), full)
            for i, (first, count) in enumerate(pieces):
                columns_here = pl.ds(pl.multiple_of(i * width + n * wide, wide), wide)
                value += jnp.dot(
                    hidden[mine, first : first + count], d_both[:count, columns_here],
                    preferred_element_type=full,
                )
            upstream[mine, out_columns] = value.astype(jnp.bfloat16)
        return carry

    lax.fori_loop(0, width // wide, branch_body, 0)
    chain.last(columns)
    chain_branch = SumChain(in_order(upstream, rows), z_one, z_two, z_three, there, 22)
    chain_branch.one()
    down_second = [
        there(to_y.at[:, low_half], down_last.at[0], 14, fsdp=plane[4]),
        there(to_x.at[:, high_half], down_last.at[1], 15, fsdp=plane[2]),
    ]
    down_first[1].wait_recv()
    to_y[:, :half] = (to_y[:, :half].astype(full) + down_x[1].astype(full)).astype(jnp.bfloat16)
    down_second[0].start()
    down_first[3].wait_recv()
    to_x[:, half:] = (to_x[:, half:].astype(full) + down_y[1].astype(full)).astype(jnp.bfloat16)
    down_second[1].start()
    gu_pieces = [
        (pl.ds(0, units), hidden.at[:block]),
        (pl.ds(units, units), hidden.at[block : 2 * block]),
    ]
    add_arrived(3, gu, block, gu_arrived, gu_pieces, gu_core, 27)
    far = part(gu, plane[6], block)
    gu_first = [
        there(far.at[:, pl.ds(0, units)], gu_far.at[0], 20, fsdp=plane[2]),
        there(far.at[:, pl.ds(units, units)], gu_far.at[1], 21, fsdp=plane[4]),
    ]
    for copy in gu_first:
        copy.start()
    for i in (1, 2, 0):
        add_arrived(i, gu, block, gu_arrived, gu_pieces, gu_core, 27)
    store = [here(part(gu, plane[2 * i], block), gu_sum.at[i], 29 + i) for i in range(3)]
    for copy in store:
        copy.start()
    down_first[0].wait_recv()
    down_first[2].wait_recv()
    own = part(down, f, unit)
    down_second[0].wait_recv()
    grad_down[:, :half] = (
        own[:, :half].astype(full) + down_x[0].astype(full) + down_last[0].astype(full)
    )
    down_second[1].wait_recv()
    grad_down[:, half:] = (
        own[:, half:].astype(full) + down_y[0].astype(full) + down_last[1].astype(full)
    )
    chain_branch.add_one()
    chain_branch.one_sent()
    store_branch = here(upstream, branch, 35)
    store_branch.start()
    chain.one_sent()
    chain.sent()
    for copy in down_core + down_first + down_second + gu_core + gu_first:
        copy.wait_send()
    for copy in gu_first:
        copy.wait_recv()
    for copy in store + [store_branch]:
        copy.wait()


def ffn(normed_all, upstream_all, w_gu, w_down, hidden, factor_gate, factor_up):
    group, width = normed_all.shape
    units = w_down.shape[0]
    rows = group // len(ORDER)
    unit, block, half = units // 8, width // 8, width // 2
    low, full = jnp.bfloat16, jnp.float32
    vmem = pl.BlockSpec(memory_space=pltpu.VMEM)
    hbm = pl.BlockSpec(memory_space=pl.ANY)
    shape = jax.ShapeDtypeStruct
    return pl.pallas_call(
        ffn_kernel,
        in_specs=[hbm] * 7,
        out_specs=[vmem] * 2 + [hbm] * 5,
        out_shape=[
            shape((rows, width), full),
            shape((unit, width), full),
            shape((3, block, 2 * units), low),
            shape((2, block, units), low),
            shape((group, width), low),
            shape((4, unit, width), low),
            shape((4, block, 2 * units), low),
        ],
        scratch_shapes=[
            pltpu.VMEM((group, width), low),
            pltpu.VMEM((group, width), low),
            pltpu.VMEM((width, 2 * units), low),
            pltpu.VMEM((units, width), low),
            pltpu.VMEM((group, units), low),
            pltpu.VMEM((group, 2 * units), low),
            pltpu.VMEM((group, width), low),
            pltpu.VMEM((rows, width), low),
            pltpu.VMEM((2, rows, width), low),
            pltpu.VMEM((2, rows, width), low),
            pltpu.VMEM((2, unit, half), low),
            pltpu.VMEM((2, unit, half), low),
            pltpu.VMEM((2, unit, half), low),
            pltpu.VMEM((unit, width), low),
            pltpu.SemaphoreType.DMA((36,)),
            pltpu.SemaphoreType.DMA((28,)),
            pltpu.SemaphoreType.DMA((28,)),
        ],
        compiler_params=pltpu.CompilerParams(
            collective_id=1, has_side_effects=True, vmem_limit_bytes=63 * 2**20
        ),
        name="ffn",
    )(normed_all, upstream_all, w_gu, w_down, hidden, factor_gate, factor_up)[:5]


def back_kernel(
    columns, resid, gain_two, cotangent, attended, queries, paired, slots, slot_row, first_row,
    logsum, normed_one, tokens, gain_one, cosine, sine, w_out, w_qkv, gu_sum, gu_far, branch,
    layer, input_rows, vector, grad_out, grad_qkv, gu_rows,
    out_w, qkv, gu_own, gu_to_y, gu_to_x, gu_x, gu_y, gu_ended,
    branch_v, z_one, z_two, z_three, working, bias, d_branch, d_attended, d_qkv, d_resid,
    keys_grad, values_grad, dkv, dkv_in,
    out_arrived, out_x, out_y, out_ended, qkv_arrived, qkv_x, qkv_y, qkv_ended,
    out_one, out_two, out_three, qkv_one, qkv_two, qkv_three, vector_in,
    load, ssem, rsem,
):
    f = lax.axis_index("fsdp")
    s = lax.axis_index("seq")
    rows, width = tokens.shape
    n_s = paired.shape[0]
    kv_width = KV_HEADS * HEAD_DIM
    repeat = HEADS // KV_HEADS
    scale = HEAD_DIM ** (-0.5)
    block = width // 8
    piece = block // n_s
    units = gu_sum.shape[2] // 2
    tile = 256
    full, low = jnp.float32, jnp.bfloat16
    plane = [f ^ k for k in range(8)]

    entry = pltpu.get_barrier_semaphore()
    for k in (1, 2, 4):
        pl.semaphore_signal(entry, inc=1, device_id={"fsdp": plane[k]}, device_id_type=MESH)
    for j in range(1, n_s):
        pl.semaphore_signal(
            entry, inc=1, device_id={"seq": lax.rem(s + j, n_s)}, device_id_type=MESH
        )

    def here(source, target, index):
        return pltpu.make_async_copy(source, target, load.at[index])

    def there(source, target, index, **device):
        return pltpu.make_async_remote_copy(
            src_ref=source, dst_ref=target, send_sem=ssem.at[index], recv_sem=rsem.at[index],
            device_id=device, device_id_type=MESH,
        )

    low_units, high_units = pl.ds(0, units), pl.ds(units, units)
    load_branch = here(branch, branch_v, 0)
    load_out = here(w_out, out_w, 1)
    load_gu = [
        here(gu_sum.at[0], gu_own, 2),
        here(gu_sum.at[2, :, low_units], gu_to_y, 3),
        here(gu_sum.at[1, :, high_units], gu_to_x, 4),
        here(gu_far.at[0], gu_x.at[1], 8),
        here(gu_far.at[1], gu_y.at[1], 9),
    ]
    load_qkv = here(w_qkv, qkv, 5)
    load_columns = here(columns, working, 7)
    for copy in [load_columns, load_branch, load_out] + load_gu + [load_qkv]:
        copy.start()

    gu_first = [
        there(gu_sum.at[1, :, low_units], gu_x.at[0], 2, fsdp=plane[2]),
        there(gu_sum.at[2, :, high_units], gu_y.at[0], 3, fsdp=plane[4]),
    ]
    gu_second = [
        there(gu_to_y, gu_ended.at[0], 4, fsdp=plane[4]),
        there(gu_to_x, gu_ended.at[1], 5, fsdp=plane[2]),
    ]

    def around(j):
        return {"seq": lax.rem(s + j, n_s)}

    def rows_for(ref, first, j):
        owner = lax.rem(s + j, n_s)
        return ref.at[pl.ds(pl.multiple_of(first + owner * piece, 16), piece)]

    gu_send = [there(rows_for(gu_own, 0, j), gu_rows.at[j], 5 + j, **around(j)) for j in range(1, n_s)]
    dkv_send = [
        [
            there(dkv.at[g, lax.rem(s + j, n_s)], dkv_in.at[g, j], 8 + 3 * g + j, **around(j))
            for j in range(1, n_s)
        ]
        for g in range(KV_HEADS)
    ]
    chain = SumChain(in_order(branch_v, rows), z_one, z_two, z_three, there, 16)
    sum_out = SumPlane(out_w, block, plane, out_arrived, out_x, out_y, out_ended, there, 24)
    sum_qkv = SumPlane(qkv, block, plane, qkv_arrived, qkv_x, qkv_y, qkv_ended, there, 36)

    def own_part(ref):
        return lambda j: rows_for(ref, f * block, n_s - j)

    chain_out = SumChain(own_part(out_w), out_one, out_two, out_three, there, 48)
    chain_qkv = SumChain(own_part(qkv), qkv_one, qkv_two, qkv_three, there, 54)
    vector_send = [
        there(vector_in.at[0], vector_in.at[1], 60, fsdp=plane[1]),
        there(vector_in.at[2], vector_in.at[3], 61, fsdp=plane[2]),
        there(vector_in.at[4], vector_in.at[5], 62, fsdp=plane[4]),
    ] + [there(vector_in.at[6], vector_in.at[6 + j], 62 + j, **around(j)) for j in range(1, n_s)]

    pl.semaphore_wait(entry, 3 + n_s - 1)
    for copy in gu_first:
        copy.start()
    load_branch.wait()
    chain.two()
    for copy in load_gu:
        copy.wait()
    gu_to_y[...] = (gu_to_y[...].astype(full) + gu_x[1].astype(full)).astype(low)
    gu_second[0].start()
    gu_to_x[...] = (gu_to_x[...].astype(full) + gu_y[1].astype(full)).astype(low)
    gu_second[1].start()

    def norm_back(value, gain, grad):
        root = lax.rsqrt(jnp.mean(value * value, -1, keepdims=True) + epsilon)
        scaled = gain * grad
        inner = jnp.mean(scaled * value, -1, keepdims=True)
        gain_grad = jnp.sum(grad * (value * root), 0, keepdims=True)
        return root * scaled - value * (root * root * root * inner), gain_grad

    load_columns.wait()
    d_norm, gain_two_grad = norm_back(resid[...], gain_two[...], working[...])
    d_total = cotangent[...].astype(full) + d_norm
    d_branch[...] = d_total.astype(low)
    d_resid[...] = d_total
    for j in range(n_s):
        keys_slot = slots[j]
        keys_slot = jnp.concatenate([keys_slot] * (rows // 128), 1)
        ok = (keys_slot <= slot_row[0:1]) & (keys_slot >= first_row[0:1])
        bias[j * rows : (j + 1) * rows] = jnp.where(ok, 0.0, -1e30)
    load_out.wait()
    for n in range(width // tile):
        value = lax.dot_general(
            d_branch[...], out_w[n * tile : (n + 1) * tile], (((1,), (1,)), ((), ())),
            preferred_element_type=full,
        )
        d_attended[:, n * tile : (n + 1) * tile] = value.astype(low)

    def turned_back(value):
        return value * cosine[...] + pltpu.roll(value * sine[...], HEAD_DIM // 2, 1)

    for g in range(KV_HEADS):
        keys = paired[:, :, g * HEAD_DIM : (g + 1) * HEAD_DIM].reshape(n_s * rows, HEAD_DIM)
        values = paired[:, :, kv_width + g * HEAD_DIM : kv_width + (g + 1) * HEAD_DIM]
        values = values.reshape(n_s * rows, HEAD_DIM)
        keys_grad[...] = jnp.zeros_like(keys_grad)
        values_grad[...] = jnp.zeros_like(values_grad)

        def head(i, carry, g=g, keys=keys, values=values):
            h = g * repeat + i
            head_columns = pl.ds(pl.multiple_of(h * HEAD_DIM, HEAD_DIM), HEAD_DIM)
            query = queries[:, head_columns]
            grad = d_attended[:, head_columns]
            raw = lax.dot_general(
                keys, query, (((1,), (1,)), ((), ())), preferred_element_type=full
            )
            logs = logsum[pl.ds(pl.multiple_of(h * 8, 8), 8)][0:1]
            probs = jnp.exp(raw * scale + bias[...] - logs)
            d_probs = lax.dot_general(
                values, grad, (((1,), (1,)), ((), ())), preferred_element_type=full
            )
            delta = jnp.sum(probs * d_probs, 0, keepdims=True)
            d_score = (probs * (d_probs - delta)).astype(low)
            turned = lax.dot_general(
                keys, d_score, (((0,), (0,)), ((), ())), preferred_element_type=full
            )
            d_qkv[:, head_columns] = turned_back((turned * scale).T).astype(low)
            keys_grad[...] += jnp.dot(d_score, query, preferred_element_type=full) * scale
            values_grad[...] += jnp.dot(probs.astype(low), grad, preferred_element_type=full)
            return carry

        lax.fori_loop(0, repeat, head, 0)
        dkv[g, :, :, :HEAD_DIM] = keys_grad[...].astype(low).reshape(n_s, rows, HEAD_DIM)
        dkv[g, :, :, HEAD_DIM:] = values_grad[...].astype(low).reshape(n_s, rows, HEAD_DIM)
        for copy in dkv_send[g]:
            copy.start()

    turned = attended[...].T
    for n in range(width // tile):
        n_columns = slice(n * tile, (n + 1) * tile)
        value = jnp.dot(turned, d_branch[:, n_columns], preferred_element_type=full)
        out_w[:, n_columns] = value.astype(low)
    sum_out.start_core()
    load_qkv.wait()

    def back_one(first, count, start):
        for n in range(width // tile):
            n_rows = slice(n * tile, (n + 1) * tile)
            value = lax.dot_general(
                d_qkv[:, first : first + count], qkv[n_rows, first : first + count],
                (((1,), (1,)), ((), ())), preferred_element_type=full,
            )
            working[:, n_rows] = value if start else working[:, n_rows] + value

    back_one(0, width, True)
    normed_turned = normed_one[...].T
    for n in range(width // tile):
        n_columns = slice(n * tile, (n + 1) * tile)
        value = jnp.dot(normed_turned, d_qkv[:, n_columns], preferred_element_type=full)
        qkv[:, n_columns] = value.astype(low)
    sum_out.start_first()

    for g in range(KV_HEADS):
        for copy in dkv_send[g]:
            copy.wait_recv()
        total = dkv[g, s].astype(full)
        for j in range(1, n_s):
            total = total + dkv_in[g, j].astype(full)
        key_columns = slice(width + g * HEAD_DIM, width + (g + 1) * HEAD_DIM)
        value_columns = slice(width + kv_width + g * HEAD_DIM, width + kv_width + (g + 1) * HEAD_DIM)
        d_qkv[:, key_columns] = turned_back(total[:, :HEAD_DIM]).astype(low)
        d_qkv[:, value_columns] = total[:, HEAD_DIM:].astype(low)
    back_one(width, 2 * kv_width, False)
    value = jnp.dot(normed_turned, d_qkv[:, width:], preferred_element_type=full)
    qkv[:, width:] = value.astype(low)
    sum_qkv.start_core()
    chain.three()

    d_norm, gain_one_grad = norm_back(tokens[...].astype(full), gain_one[...], working[...])
    input_rows[...] = (d_resid[...] + d_norm).astype(low)
    bias_grad = jnp.sum(d_qkv[...].astype(full), 0, keepdims=True)
    vectors = jnp.concatenate([gain_one_grad, gain_two_grad, bias_grad], 1)
    part = vectors.shape[1] // 8
    for r in range(8):
        vector_in[0, r : r + 1] = vectors[:, r * part : (r + 1) * part]
    vector_send[0].start()
    sum_qkv.start_first()
    vector_send[0].wait_recv()
    vector_in[2] = vector_in[0] + vector_in[1]
    vector_send[1].start()

    gu_first[0].wait_recv()
    gu_second[0].wait_recv()
    total = gu_own[:, :units].astype(full) + gu_x[0].astype(full) + gu_ended[0].astype(full)
    gu_own[:, :units] = total.astype(low)
    gu_first[1].wait_recv()
    gu_second[1].wait_recv()
    total = gu_own[:, units:].astype(full) + gu_y[0].astype(full) + gu_ended[1].astype(full)
    gu_own[:, units:] = total.astype(low)
    for copy in gu_send:
        copy.start()
    keep_rows = here(rows_for(gu_own, 0, 0), gu_rows.at[0], 6)
    keep_rows.start()
    sum_out.start_second()
    vector_send[1].wait_recv()
    vector_in[4] = vector_in[2] + vector_in[3]
    vector_send[2].start()

    sum_qkv.start_second()
    sum_out.finish()
    chain_out.one()
    vector_send[2].wait_recv()
    vector_in[6] = vector_in[4] + vector_in[5]
    for copy in vector_send[3:]:
        copy.start()
    chain_out.add_one()
    chain_out.two()
    sum_qkv.finish()
    chain_qkv.one()
    chain_out.three()
    chain.last(working)
    layer[...] = (resid[...] + working[...]).astype(low)
    chain_qkv.add_one()
    chain_qkv.two()
    for copy in vector_send[3:]:
        copy.wait_recv()
    vector[...] = vector_in[6] + vector_in[7] + vector_in[8] + vector_in[9]
    chain_out.last(grad_out)
    chain_qkv.three()
    chain_qkv.last(grad_qkv)
    for copy in gu_send:
        copy.wait_recv()
    keep_rows.wait()
    for part in (chain_out, chain_qkv):
        part.one_sent()
        part.sent()
    chain.sent()
    sum_out.sent()
    sum_qkv.sent()
    for copy in gu_first + gu_second + gu_send + vector_send:
        copy.wait_send()
    for g in range(KV_HEADS):
        for copy in dkv_send[g]:
            copy.wait_send()


def back(
    columns, resid, gain_two, cotangent, attended, queries, paired, slots, slot_row, first_row,
    logsum, normed_one, tokens, gain_one, cosine, sine, w_out, w_qkv, gu_sum, gu_far, branch,
):
    rows, width = tokens.shape
    n_s = paired.shape[0]
    group = n_s * rows
    kv_width = KV_HEADS * HEAD_DIM
    qkv_width = width + 2 * kv_width
    block = width // 8
    piece = block // n_s
    units = gu_sum.shape[2] // 2
    low, full = jnp.bfloat16, jnp.float32
    vmem = pl.BlockSpec(memory_space=pltpu.VMEM)
    hbm = pl.BlockSpec(memory_space=pl.ANY)
    shape = jax.ShapeDtypeStruct
    vectors = (2 * width + qkv_width) // 8
    return pl.pallas_call(
        back_kernel,
        in_specs=[hbm] + [vmem] * 15 + [hbm] * 5,
        out_specs=[vmem] * 5 + [hbm],
        out_shape=[
            shape((rows, width), low),
            shape((rows, width), low),
            shape((8, vectors), full),
            shape((piece, width), full),
            shape((piece, qkv_width), full),
            shape((n_s, piece, 2 * units), low),
        ],
        scratch_shapes=[
            pltpu.VMEM((width, width), low),
            pltpu.VMEM((width, qkv_width), low),
            pltpu.VMEM((block, 2 * units), low),
            pltpu.VMEM((block, units), low),
            pltpu.VMEM((block, units), low),
            pltpu.VMEM((2, block, units), low),
            pltpu.VMEM((2, block, units), low),
            pltpu.VMEM((2, block, units), low),
            pltpu.VMEM((group, width), low),
            pltpu.VMEM((rows, width), low),
            pltpu.VMEM((2, rows, width), low),
            pltpu.VMEM((2, rows, width), low),
            pltpu.VMEM((rows, width), full),
            pltpu.VMEM((group, rows), full),
            pltpu.VMEM((rows, width), low),
            pltpu.VMEM((rows, width), low),
            pltpu.VMEM((rows, qkv_width), low),
            pltpu.VMEM((rows, width), full),
            pltpu.VMEM((group, HEAD_DIM), full),
            pltpu.VMEM((group, HEAD_DIM), full),
            pltpu.VMEM((KV_HEADS, n_s, rows, 2 * HEAD_DIM), low),
            pltpu.VMEM((KV_HEADS, n_s, rows, 2 * HEAD_DIM), low),
            pltpu.VMEM((4, block, width), low),
            pltpu.VMEM((2, block, width // 2), low),
            pltpu.VMEM((2, block, width // 2), low),
            pltpu.VMEM((2, block, width // 2), low),
            pltpu.VMEM((4, block, qkv_width), low),
            pltpu.VMEM((2, block, qkv_width // 2), low),
            pltpu.VMEM((2, block, qkv_width // 2), low),
            pltpu.VMEM((2, block, qkv_width // 2), low),
            pltpu.VMEM((piece, width), low),
            pltpu.VMEM((2, piece, width), low),
            pltpu.VMEM((2, piece, width), low),
            pltpu.VMEM((piece, qkv_width), low),
            pltpu.VMEM((2, piece, qkv_width), low),
            pltpu.VMEM((2, piece, qkv_width), low),
            pltpu.VMEM((10, 8, vectors), full),
            pltpu.SemaphoreType.DMA((10,)),
            pltpu.SemaphoreType.DMA((68,)),
            pltpu.SemaphoreType.DMA((68,)),
        ],
        compiler_params=pltpu.CompilerParams(
            collective_id=2, has_side_effects=True, vmem_limit_bytes=63 * 2**20
        ),
        name="back",
    )(
        columns, resid, gain_two, cotangent, attended, queries, paired, slots, slot_row, first_row,
        logsum, normed_one, tokens, gain_one, cosine, sine, w_out, w_qkv, gu_sum, gu_far, branch,
    )


def finish_kernel(
    layer, input_rows, grad_out, grad_qkv, grad_down, gu_rows,
    layer_out, input_grad, out_out, query_out, key_out, value_out, down_out, gate_out, up_out,
):
    s = lax.axis_index("seq")
    n_s = gu_rows.shape[0]
    width = grad_out.shape[1]
    kv_width = KV_HEADS * HEAD_DIM
    unit_pad = grad_down.shape[0]
    unit = down_out.shape[0]
    units = gu_rows.shape[2] // 2
    layer_out[...] = layer[...]
    input_grad[...] = input_rows[...]
    out_out[...] = grad_out[...]
    query_out[...] = grad_qkv[:, :width]
    key_out[...] = grad_qkv[:, width : width + kv_width]
    value_out[...] = grad_qkv[:, width + kv_width :]
    down_out[...] = grad_down[:unit]
    window = 512
    lanes = lax.broadcasted_iota(jnp.int32, (gu_rows.shape[1], 128), 1)
    for base, out in ((0, gate_out), (units, up_out)):
        for f in range(units // unit_pad):
            for owner in range(n_s):
                source = base + f * unit_pad
                begin = min(source // 128 * 128, 2 * units - window)
                target = (f * n_s + owner) * unit
                first = target // 128 * 128
                slot = lax.rem(s + n_s - owner, n_s)
                value = gu_rows[slot, :, begin : begin + window].astype(jnp.float32)
                turn = ((target - first) - (source - begin)) % window
                if turn:
                    value = pltpu.roll(value, turn, 1)
                for t in range(first, min(target + unit, out.shape[1]), 128):
                    part = value[:, t - first : t - first + 128]
                    if t < target:
                        part = jnp.where(lanes >= target - t, part, out[:, t : t + 128])
                    out[:, t : t + 128] = part


def finish(layer, input_rows, grad_out, grad_qkv, grad_down, gu_rows, unit, hidden_width):
    piece, width = grad_out.shape
    kv_width = KV_HEADS * HEAD_DIM
    low, full = jnp.bfloat16, jnp.float32
    shape = jax.ShapeDtypeStruct
    vmem = pl.BlockSpec(memory_space=pltpu.VMEM)
    return pl.pallas_call(
        finish_kernel,
        in_specs=[vmem] * 6,
        out_specs=[vmem] * 9,
        out_shape=[
            shape(layer.shape, low),
            shape(layer.shape, low),
            shape((piece, width), full),
            shape((piece, width), full),
            shape((piece, kv_width), full),
            shape((piece, kv_width), full),
            shape((unit, width), full),
            shape((piece, hidden_width), full),
            shape((piece, hidden_width), full),
        ],
        compiler_params=pltpu.CompilerParams(vmem_limit_bytes=63 * 2**20),
        name="finish",
    )(layer, input_rows, grad_out, grad_qkv, grad_down, gu_rows)


def per_device(
    tokens, cotangent, lengths, balance, norm1_gain, w_query, b_query, w_key, b_key,
    w_value, b_value, w_out, norm2_gain, w_gate, w_up, w_down,
):
    seq_count = lax.axis_size("seq")
    fsdp_count = lax.axis_size("fsdp")
    seq_rank = lax.axis_index("seq")
    fsdp_rank = lax.axis_index("fsdp")
    rows_here, width = tokens.shape
    kv_width = KV_HEADS * HEAD_DIM
    hidden_width = w_gate.shape[1]
    unit = hidden_width // (fsdp_count * seq_count)
    (
        weight_gu, weight_down, upstream_all, normed_all, hidden, factor_gate, factor_up,
        weight_qkv, weight_out, queries, paired, slots, logsum, attended, resid, normed_one,
        gain_one, gain_two, slot_row, first_row, cosine, sine,
    ) = front(
        tokens, cotangent, lengths, balance, (norm1_gain, norm2_gain, b_query, b_key, b_value),
        (w_query, w_key, w_value, w_out, w_gate, w_up, w_down),
    )
    columns, grad_down, gu_sum, gu_far, branch = ffn(
        normed_all, upstream_all, weight_gu, weight_down, hidden, factor_gate, factor_up
    )
    layer, input_rows, vectors, grad_out, grad_qkv, gu_rows = back(
        columns, resid, gain_two, cotangent, attended, queries, paired, slots, slot_row, first_row,
        logsum, normed_one, tokens, gain_one, cosine, sine, weight_out, weight_qkv, gu_sum, gu_far,
        branch,
    )
    (
        layer_out, input_grad, grad_out, grad_query, grad_key, grad_value, grad_down, grad_gate,
        grad_up,
    ) = finish(layer, input_rows, grad_out, grad_qkv, grad_down, gu_rows, unit, hidden_width)
    vectors = vectors.reshape(-1)
    own = width // (fsdp_count * seq_count)
    first = (fsdp_rank * seq_count + seq_rank) * own

    def own_part(offset):
        return lax.dynamic_slice_in_dim(vectors, offset + first, own, 0)

    biases = 2 * width
    return (
        layer_out,
        input_grad,
        own_part(0),
        grad_query,
        own_part(biases),
        grad_key,
        vectors[biases + width : biases + width + kv_width],
        grad_value,
        vectors[biases + width + kv_width :],
        grad_out,
        own_part(width),
        grad_gate,
        grad_up,
        grad_down,
    )


def solution(mesh):
    both = P(("fsdp", "seq"), None)
    both_one = P(("fsdp", "seq"))
    placed = (
        both, both, P("fsdp", None), both_one, P("fsdp"), P("fsdp", None), P("fsdp"),
        P("fsdp", None), P("fsdp"), P("fsdp", None), P("fsdp"), P("fsdp", None), P("fsdp"),
        P("fsdp", None), P("fsdp", None), P("fsdp", None),
    )
    return jax.shard_map(
        per_device if mesh.shape["fsdp"] == 8 else plain_device,
        mesh=mesh,
        in_specs=placed,
        out_specs=(
            both, both, both_one, both, both_one, both, P(), both, P(), both, both_one,
            both, both, both,
        ),
        check_vma=False,
    )
```

```python
import jax
import jax.numpy as jnp
import numpy as np
from jax import lax
from jax.experimental import pallas as pl
from jax.experimental.pallas import tpu as pltpu
from jax.sharding import PartitionSpec as P

HEADS = 12
KV_HEADS = 2
HEAD_DIM = 128

MESH = pl.DeviceIdType.MESH

epsilon = 1e-06
rope_base = 1000000.0


def norm_piece(values, gain):
    return values * lax.rsqrt(jnp.mean(values * values, -1, keepdims=True) + epsilon) * gain


def rope_tables(position):
    half = HEAD_DIM // 2
    inverse = rope_base ** (-(jnp.arange(half, dtype=jnp.float32) * 2.0 / HEAD_DIM))
    angle = position.astype(jnp.float32)[:, None] * inverse[None, :]
    cosine = jnp.concatenate([jnp.cos(angle), jnp.cos(angle)], -1)
    sine = jnp.concatenate([jnp.sin(angle), jnp.sin(angle)], -1)
    return (cosine, sine)


def turn_half(values):
    half = values.shape[-1] // 2
    return jnp.concatenate([-values[..., half:], values[..., :half]], -1)


def rotate(values, cosine, sine):
    return values * cosine[:, None, :] + turn_half(values) * sine[:, None, :]


def rotate_back(grads, cosine, sine):
    return grads * cosine[:, None, :] - turn_half(grads * sine[:, None, :])


def segment_of(slots, starts):
    return (slots >= starts[1]).astype(jnp.int32) + (slots >= starts[2]).astype(jnp.int32)


def contract_rows(left, right):
    return lax.dot_general(
        left, right, (((0,), (0,)), ((), ())), preferred_element_type=jnp.float32
    )


def contract_columns(left, right):
    return lax.dot_general(
        left, right, (((1,), (1,)), ((), ())), preferred_element_type=jnp.float32
    )


def plain_device(
    tokens, cotangent, lengths, balance, norm1_gain, w_query, b_query, w_key, b_key,
    w_value, b_value, w_out, norm2_gain, w_gate, w_up, w_down,
):
    seq_count = lax.axis_size("seq")
    fsdp_count = lax.axis_size("fsdp")
    seq_rank = lax.axis_index("seq")
    rows_here, width = tokens.shape
    group = seq_count * rows_here
    kv_width = KV_HEADS * HEAD_DIM
    qkv_width = width + 2 * kv_width
    hidden_width = w_gate.shape[1]
    unit = hidden_width // (fsdp_count * seq_count)
    own_units = hidden_width // seq_count
    weight_rows = w_gate.shape[0]
    score_scale = HEAD_DIM ** (-0.5)
    repeat = HEADS // KV_HEADS

    slot = balance % group
    slots_all = lax.all_gather(slot, "seq", axis=0, tiled=True)
    seq_lengths = lengths[0]
    starts = jnp.cumsum(seq_lengths) - seq_lengths
    segment = segment_of(slot, starts)
    segments_all = segment_of(slots_all, starts)
    first_row = jnp.where(segment == 0, starts[0], jnp.where(segment == 1, starts[1], starts[2]))
    cosine, sine = rope_tables(slot - first_row)
    allowed = (segment[:, None] == segments_all[None, :]) & (slots_all[None, :] <= slot[:, None])

    small = jnp.concatenate([norm1_gain, norm2_gain, b_query, b_key, b_value], 0)[None]
    small = lax.all_gather(small, "fsdp", axis=0, tiled=True)
    piece = norm1_gain.shape[0]
    bias_piece = b_key.shape[0]
    gain_one = small[:, :piece].reshape(-1).astype(jnp.float32)
    gain_two = small[:, piece : 2 * piece].reshape(-1).astype(jnp.float32)
    bias_qkv = jnp.concatenate(
        [
            small[:, 2 * piece : 3 * piece].reshape(-1),
            small[:, 3 * piece : 3 * piece + bias_piece].reshape(-1),
            small[:, 3 * piece + bias_piece :].reshape(-1),
        ],
        0,
    ).astype(jnp.float32)
    weight_qkv = lax.all_gather(
        jnp.concatenate([w_query, w_key, w_value], 1), "fsdp", axis=0, tiled=True
    )
    weight_out = lax.all_gather(w_out, "fsdp", axis=0, tiled=True)
    upstream_all = lax.all_gather(cotangent, "seq", axis=0, tiled=True)

    def own_columns(weight):
        cut = weight.reshape(weight_rows, fsdp_count, seq_count, unit)
        return lax.dynamic_index_in_dim(cut, seq_rank, 2, False).reshape(weight_rows, own_units)

    weight_gu = lax.all_gather(
        jnp.concatenate([own_columns(w_gate), own_columns(w_up)], 1), "fsdp", axis=0, tiled=True
    )
    weight_down = lax.all_gather(
        lax.dynamic_slice_in_dim(w_down, seq_rank * unit, unit, 0), "fsdp", axis=0, tiled=True
    )

    inputs = tokens.astype(jnp.float32)
    normed_one = norm_piece(inputs, gain_one).astype(jnp.bfloat16)
    projected = jnp.dot(normed_one, weight_qkv, preferred_element_type=jnp.float32) + bias_qkv
    query_pre = projected[:, :width].reshape(rows_here, HEADS, HEAD_DIM)
    key_pre = projected[:, width : width + kv_width].reshape(rows_here, KV_HEADS, HEAD_DIM)
    value_pre = projected[:, width + kv_width :]
    queries = rotate(query_pre, cosine, sine).astype(jnp.bfloat16)
    keys = rotate(key_pre, cosine, sine).astype(jnp.bfloat16).reshape(rows_here, kv_width)
    values = value_pre.astype(jnp.bfloat16)
    paired = lax.all_gather(jnp.concatenate([keys, values], 1), "seq", axis=0, tiled=True)
    keys_all = paired[:, :kv_width].reshape(group, KV_HEADS, HEAD_DIM)
    values_all = paired[:, kv_width:].reshape(group, KV_HEADS, HEAD_DIM)
    grouped = queries.reshape(rows_here, KV_HEADS, repeat, HEAD_DIM)
    raw = (
        jnp.einsum("qgrd,kgd->grqk", grouped, keys_all, preferred_element_type=jnp.float32)
        * score_scale
    )
    scores = jnp.where(allowed, raw, -jnp.inf)
    expo = jnp.exp(scores - jnp.max(scores, -1, keepdims=True))
    probs = expo / jnp.sum(expo, -1, keepdims=True)
    probs_low = probs.astype(jnp.bfloat16)
    attended = jnp.einsum(
        "grqk,kgd->qgrd", probs_low, values_all, preferred_element_type=jnp.float32
    )
    attended = attended.astype(jnp.bfloat16).reshape(rows_here, width)
    resid = inputs + jnp.dot(attended, weight_out, preferred_element_type=jnp.float32)
    normed_two = norm_piece(resid, gain_two).astype(jnp.bfloat16)

    normed_all = lax.all_gather(normed_two, "seq", axis=0, tiled=True)
    both = jnp.dot(normed_all, weight_gu, preferred_element_type=jnp.float32)
    gate = both[:, :own_units]
    up = both[:, own_units:]
    sigma = jax.nn.sigmoid(gate)
    activated = gate * sigma
    hidden = (activated * up).astype(jnp.bfloat16)
    d_hidden = contract_columns(upstream_all, weight_down)
    d_gate = (d_hidden * up * sigma * (1.0 + gate * (1.0 - sigma))).astype(jnp.bfloat16)
    d_up = (d_hidden * activated).astype(jnp.bfloat16)
    d_both = jnp.concatenate([d_gate, d_up], 1)
    columns = lax.psum_scatter(
        contract_columns(d_both, weight_gu).astype(jnp.bfloat16),
        "seq", scatter_dimension=0, tiled=True,
    ).astype(jnp.float32)
    branch = lax.psum_scatter(
        jnp.dot(hidden, weight_down, preferred_element_type=jnp.float32).astype(jnp.bfloat16),
        "seq", scatter_dimension=0, tiled=True,
    ).astype(jnp.float32)
    layer_out = (resid + branch).astype(jnp.bfloat16)
    grad_down = lax.psum_scatter(
        contract_rows(hidden, upstream_all).astype(jnp.bfloat16),
        "fsdp", scatter_dimension=0, tiled=True,
    ).astype(jnp.float32)
    grad_pair = lax.psum_scatter(
        contract_rows(normed_all, d_both).astype(jnp.bfloat16),
        "fsdp", scatter_dimension=0, tiled=True,
    )
    grad_pair = lax.all_to_all(grad_pair, "seq", split_axis=0, concat_axis=0, tiled=True)
    grad_pair = grad_pair.reshape(seq_count, weight_rows // seq_count, 2, fsdp_count, unit)
    grad_pair = grad_pair.transpose(2, 1, 3, 0, 4).astype(jnp.float32)
    grad_pair = grad_pair.reshape(2, weight_rows // seq_count, hidden_width)

    _, pull_two = jax.vjp(norm_piece, resid, gain_two)
    d_resid_norm, grad_gain_two = pull_two(columns)
    d_resid = cotangent.astype(jnp.float32) + d_resid_norm
    d_branch = d_resid.astype(jnp.bfloat16)
    grad_out = contract_rows(attended, d_branch).astype(jnp.bfloat16)
    d_attended = contract_columns(d_branch, weight_out).astype(jnp.bfloat16)
    d_attended = d_attended.reshape(rows_here, KV_HEADS, repeat, HEAD_DIM)
    d_probs = jnp.einsum(
        "qgrd,kgd->grqk", d_attended, values_all, preferred_element_type=jnp.float32
    )
    delta = jnp.sum(probs * d_probs, -1, keepdims=True)
    d_score = (probs * (d_probs - delta)).astype(jnp.bfloat16)
    d_queries = (
        jnp.einsum("grqk,kgd->qgrd", d_score, keys_all, preferred_element_type=jnp.float32)
        * score_scale
    )
    d_keys = (
        jnp.einsum("grqk,qgrd->kgd", d_score, grouped, preferred_element_type=jnp.float32)
        * score_scale
    )
    d_values = jnp.einsum(
        "grqk,qgrd->kgd", probs_low, d_attended, preferred_element_type=jnp.float32
    )
    d_paired = jnp.concatenate([d_keys.reshape(group, kv_width), d_values.reshape(group, kv_width)], 1)
    d_paired = lax.psum_scatter(
        d_paired.astype(jnp.bfloat16), "seq", scatter_dimension=0, tiled=True
    ).astype(jnp.float32)
    d_query_pre = rotate_back(
        d_queries.reshape(rows_here, HEADS, HEAD_DIM), cosine, sine
    ).astype(jnp.bfloat16)
    d_key_pre = rotate_back(
        d_paired[:, :kv_width].reshape(rows_here, KV_HEADS, HEAD_DIM), cosine, sine
    ).astype(jnp.bfloat16)
    d_value_pre = d_paired[:, kv_width:].astype(jnp.bfloat16)
    d_qkv = jnp.concatenate(
        [
            d_query_pre.reshape(rows_here, width),
            d_key_pre.reshape(rows_here, kv_width),
            d_value_pre,
        ],
        1,
    )
    grad_qkv = contract_rows(normed_one, d_qkv).astype(jnp.bfloat16)
    grad_bias = jnp.sum(d_qkv.astype(jnp.float32), 0)
    d_normed_one = contract_columns(d_qkv, weight_qkv)
    _, pull_one = jax.vjp(norm_piece, inputs, gain_one)
    d_input_norm, grad_gain_one = pull_one(d_normed_one)
    input_grad = (d_resid + d_input_norm).astype(jnp.bfloat16)

    def summed(value):
        value = lax.psum_scatter(value, "fsdp", scatter_dimension=0, tiled=True)
        return lax.psum_scatter(value, "seq", scatter_dimension=0, tiled=True).astype(jnp.float32)

    grad_out = summed(grad_out)
    grad_qkv = summed(grad_qkv)
    vectors = lax.psum(
        jnp.concatenate([grad_gain_one, grad_gain_two, grad_bias], 0), ("fsdp", "seq")
    )
    own = width // (fsdp_count * seq_count)
    first = (lax.axis_index("fsdp") * seq_count + seq_rank) * own

    def own_part(offset):
        return lax.dynamic_slice_in_dim(vectors, offset + first, own, 0)

    biases = 2 * width
    return (
        layer_out,
        input_grad,
        own_part(0),
        grad_qkv[:, :width],
        own_part(biases),
        grad_qkv[:, width : width + kv_width],
        vectors[biases + width : biases + width + kv_width],
        grad_qkv[:, width + kv_width :],
        vectors[biases + width + kv_width :],
        grad_out,
        own_part(width),
        grad_pair[0],
        grad_pair[1],
        grad_down,
    )


ORDER = (1, 3, 2, 0)


class SumChain:
    def __init__(self, held, z_one, z_two, z_three, there, index):
        self.rank = lax.axis_index("seq")
        s = self.rank
        self.held, self.arrived = held, (z_one, z_two, z_three)
        self.up = [
            there(held(1), z_one, index, seq=s + 1),
            there(held(2), z_two.at[0], index + 2, seq=s + 1),
            there(held(3), z_three.at[0], index + 4, seq=s + 1),
        ]
        self.down = [
            there(held(3), z_one, index + 1, seq=s - 1),
            there(held(2), z_two.at[1], index + 3, seq=s - 1),
            there(held(1), z_three.at[1], index + 5, seq=s - 1),
        ]

    def add(self, j, arrived):
        ref = self.held(j)
        total = ref[...].astype(jnp.float32) + arrived[...].astype(jnp.float32)
        ref[...] = total.astype(jnp.bfloat16)

    def one(self):
        pl.when(self.rank == 0)(self.up[0].start)
        pl.when(self.rank == 3)(self.down[0].start)

    def add_one(self):
        @pl.when(self.rank == 1)
        def _():
            self.up[0].wait_recv()
            self.add(2, self.arrived[0])

        @pl.when(self.rank == 2)
        def _():
            self.down[0].wait_recv()
            self.add(2, self.arrived[0])

    def two(self):
        pl.when(self.rank <= 1)(self.up[1].start)
        pl.when(self.rank >= 2)(self.down[1].start)

    def add_two(self):
        @pl.when((self.rank == 1) | (self.rank == 2))
        def _():
            self.up[1].wait_recv()
            self.add(3, self.arrived[1].at[0])
            self.down[1].wait_recv()
            self.add(1, self.arrived[1].at[1])

    def three(self):
        pl.when(self.rank <= 2)(self.up[2].start)
        pl.when(self.rank >= 1)(self.down[2].start)

    def last(self, out):
        out[...] = self.held(0)[...].astype(jnp.float32)

        @pl.when(self.rank >= 1)
        def _():
            self.up[2].wait_recv()
            out[...] += self.arrived[2][0].astype(jnp.float32)

        @pl.when(self.rank <= 2)
        def _():
            self.down[2].wait_recv()
            out[...] += self.arrived[2][1].astype(jnp.float32)

    def one_sent(self):
        pl.when(self.rank == 0)(self.up[0].wait_send)
        pl.when(self.rank == 3)(self.down[0].wait_send)

    def two_sent(self):
        pl.when(self.rank <= 1)(self.up[1].wait_send)
        pl.when(self.rank >= 2)(self.down[1].wait_send)

    def three_sent(self):
        pl.when(self.rank <= 2)(self.up[2].wait_send)
        pl.when(self.rank >= 1)(self.down[2].wait_send)


class SumPlane:
    def __init__(self, buffer, block, plane, arrived, by_x, by_y, ended, there, index):
        half = buffer.shape[1] // 2
        low, high = pl.ds(0, half), pl.ds(half, half)

        def part(k):
            return buffer.at[pl.ds(pl.multiple_of(plane[k] * block, 16), block)]

        self.parts = own, to_x, to_y, to_both = [part(k) for k in (0, 2, 4, 6)]
        self.arrived, self.by_x, self.by_y, self.ended, self.half = arrived, by_x, by_y, ended, half
        self.core = [
            there(part(2 * i + 1), arrived.at[i], index + i, fsdp=plane[1]) for i in range(4)
        ]
        self.first = [
            there(to_both.at[:, low], by_x.at[1], index + 5, fsdp=plane[2]),
            there(to_both.at[:, high], by_y.at[1], index + 7, fsdp=plane[4]),
            there(to_x.at[:, low], by_x.at[0], index + 4, fsdp=plane[2]),
            there(to_y.at[:, high], by_y.at[0], index + 6, fsdp=plane[4]),
        ]
        self.second = [
            there(to_y.at[:, low], ended.at[0], index + 8, fsdp=plane[4]),
            there(to_x.at[:, high], ended.at[1], index + 9, fsdp=plane[2]),
        ]

    def start_core(self):
        for copy in self.core:
            copy.start()

    def start_first(self):
        for i in (3, 1, 2, 0):
            self.core[i].wait_recv()
            part = self.parts[i]
            total = part[...].astype(jnp.float32) + self.arrived[i].astype(jnp.float32)
            part[...] = total.astype(jnp.bfloat16)
        for copy in self.first:
            copy.start()

    def start_second(self):
        half = self.half
        _, to_x, to_y, _ = self.parts
        self.first[0].wait_recv()
        total = to_y[:, :half].astype(jnp.float32) + self.by_x[1].astype(jnp.float32)
        to_y[:, :half] = total.astype(jnp.bfloat16)
        self.second[0].start()
        self.first[1].wait_recv()
        total = to_x[:, half:].astype(jnp.float32) + self.by_y[1].astype(jnp.float32)
        to_x[:, half:] = total.astype(jnp.bfloat16)
        self.second[1].start()

    def finish(self):
        half = self.half
        own = self.parts[0]
        self.first[2].wait_recv()
        self.second[0].wait_recv()
        total = own[:, :half].astype(jnp.float32) + self.by_x[0].astype(jnp.float32)
        own[:, :half] = (total + self.ended[0].astype(jnp.float32)).astype(jnp.bfloat16)
        self.first[3].wait_recv()
        self.second[1].wait_recv()
        total = own[:, half:].astype(jnp.float32) + self.by_y[0].astype(jnp.float32)
        own[:, half:] = (total + self.ended[1].astype(jnp.float32)).astype(jnp.bfloat16)

    def sent(self):
        for copy in self.core + self.first + self.second:
            copy.wait_send()


def in_order(partial, rows):
    def held(j):
        return partial.at[ORDER.index(j) * rows : (ORDER.index(j) + 1) * rows]

    return held


def front_kernel(
    lengths, tokens, cotangent, small, balance, inverse,
    w_query, w_key, w_value, w_out, w_gate, w_up, w_down,
    gu_all, down_all, upstream_all, normed_all, hidden, factor_gate, factor_up, qkv_out, out_out,
    queries, paired_out, slots_out, logsum, attended, resid, normed_one, gain_one, gain_two,
    slot_row, first_row, cosine, sine,
    q_w, kv_w, out_w, gate_v, up_v, gu, normed, kv, small_own, small_all, slots_all, bias,
    cotangent_v, down_raw, down_own, hidden_v, gate_part, up_part,
    local, ssem, rsem, zsend, zrecv,
):
    f = lax.axis_index("fsdp")
    s = lax.axis_index("seq")
    rows, width = tokens.shape
    n_f, n_s = 8, slots_all.shape[0]
    group = n_s * rows
    block = w_query.shape[0]
    unit_pad = down_own.shape[0]
    unit = w_gate.shape[1] // (n_f * n_s)
    units = n_f * unit_pad
    kv_width = KV_HEADS * HEAD_DIM
    qkv_width = width + 2 * kv_width
    scale = HEAD_DIM ** (-0.5)
    repeat = HEADS // KV_HEADS
    plane = [f ^ k for k in range(n_f)]

    entry = pltpu.get_barrier_semaphore()
    for k in range(1, n_f):
        pl.semaphore_signal(entry, inc=1, device_id={"fsdp": plane[k]}, device_id_type=MESH)
    for j in range(1, n_s):
        pl.semaphore_signal(
            entry, inc=1, device_id={"seq": lax.rem(s + j, n_s)}, device_id_type=MESH
        )

    def here(source, target, index):
        return pltpu.make_async_copy(source, target, local.at[index])

    def there(source, target, index, **device):
        return pltpu.make_async_remote_copy(
            src_ref=source, dst_ref=target, send_sem=ssem.at[index], recv_sem=rsem.at[index],
            device_id=device, device_id_type=MESH,
        )

    def own_rows(ref, owner, size, start=0, count=None):
        first = pl.multiple_of(owner * size + start, 16)
        return ref.at[pl.ds(first, size if count is None else count)]

    class Gather:
        def __init__(self, source, target, size, index):
            half = size // 2
            x, y, c = plane[2], plane[4], plane[1]
            self.own = here(source, own_rows(target, f, size), index // 8) if source is not None else None
            if source is None:
                source = own_rows(target, f, size)
            mine = own_rows(target, f, size)
            self.first = [
                there(source, mine, index, fsdp=x),
                there(source, mine, index + 1, fsdp=y),
                there(source, mine, index + 2, fsdp=c),
            ]
            from_x, from_y = own_rows(target, x, size), own_rows(target, y, size)
            part_x = own_rows(target, x, size, 0, half)
            part_y = own_rows(target, y, size, half, half)
            self.second = [
                there(part_x, part_x, index + 3, fsdp=y),
                there(part_y, part_y, index + 4, fsdp=x),
                there(from_x, from_x, index + 5, fsdp=c),
                there(from_y, from_y, index + 6, fsdp=c),
            ]
            diagonal = own_rows(target, plane[6], size)
            self.third = there(diagonal, diagonal, index + 7, fsdp=c)

        def start(self):
            if self.own is not None:
                self.own.start()
            for copy in self.first:
                copy.start()

        def forward(self):
            self.first[0].wait_recv()
            self.second[0].start()
            self.second[2].start()
            self.first[1].wait_recv()
            self.second[1].start()
            self.second[3].start()

        def last(self):
            self.second[0].wait_recv()
            self.second[1].wait_recv()
            self.third.start()

        def finish(self):
            if self.own is not None:
                self.own.wait()
            self.first[2].wait_recv()
            self.second[2].wait_recv()
            self.second[3].wait_recv()
            self.third.wait_recv()

        def sent(self):
            for copy in self.first + self.second + [self.third]:
                copy.wait_send()

    class Chain:
        def __init__(self, target, index, own=None):
            self.steps = []
            for step in range(1, n_s):
                up = own_rows(target, s - (step - 1), rows)
                down = own_rows(target, s + (step - 1), rows)
                source = own if own is not None and step == 1 else up
                i = index + 2 * (step - 1)
                self.steps.append((
                    pltpu.make_async_remote_copy(
                        src_ref=source, dst_ref=up, send_sem=zsend.at[i], recv_sem=zrecv.at[i],
                        device_id={"seq": s + 1}, device_id_type=MESH,
                    ),
                    pltpu.make_async_remote_copy(
                        src_ref=down if source is up else source, dst_ref=down, send_sem=zsend.at[i + 1], recv_sem=zrecv.at[i + 1],
                        device_id={"seq": s - 1}, device_id_type=MESH,
                    ),
                    (s >= step - 1) & (s < n_s - 1),
                    (s >= 1) & (s <= n_s - step),
                    s >= step,
                    s <= n_s - 1 - step,
                ))

        def send(self, step):
            up, down, can_up, can_down, _, _ = self.steps[step - 1]
            pl.when(can_up)(up.start)
            pl.when(can_down)(down.start)

        def receive(self, step):
            up, down, _, _, from_below, from_above = self.steps[step - 1]
            pl.when(from_below)(up.wait_recv)
            pl.when(from_above)(down.wait_recv)

        def sent(self):
            for up, down, can_up, can_down, _, _ in self.steps:
                pl.when(can_up)(up.wait_send)
                pl.when(can_down)(down.wait_send)

    own_block = pl.ds(pl.multiple_of(f * block, 16), block)
    pieces = [
        here(w_key, kv_w.at[own_block, pl.ds(0, kv_width)], 6),
        here(w_value, kv_w.at[own_block, pl.ds(kv_width, kv_width)], 7),
        here(w_query, q_w.at[own_block], 5),
        here(cotangent, cotangent_v, 8),
    ]
    load_gate = here(w_gate, gate_v, 9)
    load_up = here(w_up, up_v, 10)
    first_unit = pl.multiple_of(s * unit // 16 * 16, 16)
    load_down = here(w_down.at[pl.ds(first_unit, unit_pad)], down_raw, 15)
    for copy in pieces:
        copy.start()
    load_gate.start()
    load_up.start()
    load_down.start()

    slot = (balance[...] & (group - 1)).astype(jnp.float32)
    second = lengths[0, 0].astype(jnp.float32)
    third = (lengths[0, 0] + lengths[0, 1]).astype(jnp.float32)
    first = jnp.where(slot >= third, third, jnp.where(slot >= second, second, 0.0))
    slot_row[...] = jnp.broadcast_to(slot, slot_row.shape)
    first_row[...] = jnp.broadcast_to(first, first_row.shape)
    slots_all[s] = jnp.broadcast_to(slot, (128, rows)).T
    lanes = lax.broadcasted_iota(jnp.int32, small.shape, 1)
    sorts = lax.broadcasted_iota(jnp.int32, small.shape, 0)
    small_own[...] = jnp.where(
        sorts < 3,
        pltpu.roll(small[...], lax.rem(f, 2) * block, 1),
        pltpu.roll(small[...], f * (kv_width // n_f), 1),
    )
    small_all[f] = small_own[...]

    gather_kv = Gather(None, kv_w, block, 0)
    gather_q = Gather(None, q_w, block, 8)
    gather_out = Gather(w_out, out_w, block, 16)
    gather_gu = Gather(None, gu, block, 24)
    gather_down = Gather(down_own, down_all, unit_pad, 32)
    chain_up = Chain(upstream_all, 0, cotangent_v)
    chain_normed = Chain(normed, 6)
    send_small = [
        there(small_own, small_all.at[f], 40 + k, fsdp=plane[k]) for k in range(1, n_f)
    ]
    send_slots = [
        there(slots_all.at[s], slots_all.at[s], 48 + j, seq=lax.rem(s + j, n_s))
        for j in range(1, n_s)
    ]
    send_kv = [
        there(kv.at[s], kv.at[s], 52 + j, seq=lax.rem(s + j, n_s)) for j in range(1, n_s)
    ]
    for copy in pieces[:2]:
        copy.wait()
    pl.semaphore_wait(entry, n_f - 1 + n_s - 1)
    gather_kv.start()
    for copy in send_small + send_slots:
        copy.start()
    for copy in pieces[2:]:
        copy.wait()
    chain_up.send(1)
    save_own = here(cotangent_v, own_rows(upstream_all, s, rows), 8)
    save_own.start()
    position = slots_all[s] - jnp.broadcast_to(first, (128, rows)).T
    angle = position * inverse[...]
    cosine[...] = jnp.cos(angle)
    sine[...] = jnp.where(
        lax.broadcasted_iota(jnp.int32, angle.shape, 1) < HEAD_DIM // 2, -1.0, 1.0
    ) * jnp.sin(angle)

    for copy in send_small + send_slots:
        copy.wait_recv()

    def joined(sort):
        return jnp.concatenate(
            [
                small_all[2 * i, sort : sort + 1] + small_all[2 * i + 1, sort : sort + 1]
                for i in range(n_f // 2)
            ],
            1,
        )

    gain_one[...] = joined(0)
    gain_two[...] = joined(1)
    bias_query = joined(2)
    bias_key = sum(small_all[i, 3:4, :kv_width] for i in range(n_f))
    bias_value = sum(small_all[i, 4:5, :kv_width] for i in range(n_f))

    inputs = tokens[...].astype(jnp.float32)
    root = lax.rsqrt(jnp.mean(inputs * inputs, -1, keepdims=True) + epsilon)
    normed_one[...] = (inputs * root * gain_one[...]).astype(jnp.bfloat16)
    gather_kv.forward()
    gather_q.start()
    gather_kv.last()
    gather_kv.finish()

    def turned(value):
        return value * cosine[...] + pltpu.roll(value, HEAD_DIM // 2, 1) * sine[...]

    rows_low = normed_one[...]
    pair = jnp.dot(rows_low, kv_w[:, :kv_width], preferred_element_type=jnp.float32)
    pair = pair + bias_key
    for g in range(KV_HEADS):
        columns = slice(g * HEAD_DIM, (g + 1) * HEAD_DIM)
        kv[s, :, columns] = turned(pair[:, columns]).astype(jnp.bfloat16)
    pair = jnp.dot(rows_low, kv_w[:, kv_width:], preferred_element_type=jnp.float32)
    kv[s, :, kv_width:] = (pair + bias_value).astype(jnp.bfloat16)
    for copy in send_kv:
        copy.start()
    save_kv_w = here(kv_w, qkv_out.at[:, pl.ds(width, 2 * kv_width)], 11)
    save_kv_w.start()

    load_gate.wait()
    load_up.wait()
    pick_units(gate_v, up_v, gu.at[own_block], w_gate.shape[1] // n_f, unit, unit_pad)
    gather_q.forward()
    gather_out.start()
    load_down.wait()
    raw = down_raw[...].astype(jnp.float32)
    shifted = jnp.concatenate([raw[8:], jnp.zeros((8, width), jnp.float32)], 0)
    raw = jnp.where(lax.rem(s * unit, 16) == 0, raw, shifted)
    inside = lax.broadcasted_iota(jnp.int32, raw.shape, 0) < unit
    down_own[...] = jnp.where(inside, raw, 0.0).astype(jnp.bfloat16)

    for j in range(n_s):
        keys_slot = slots_all[j]
        keys_slot = jnp.concatenate([keys_slot] * (rows // 128), 1)
        ok = (keys_slot <= slot) & (keys_slot >= first)
        bias[j * rows : (j + 1) * rows] = jnp.where(ok, 0.0, -1e30)

    gather_q.last()
    gather_q.finish()
    save_q_w = here(q_w, qkv_out.at[:, pl.ds(0, width)], 0)
    save_q_w.start()
    for g in range(HEADS // 2):
        columns = slice(g * 2 * HEAD_DIM, (g + 1) * 2 * HEAD_DIM)
        pair = jnp.dot(rows_low, q_w[:, columns], preferred_element_type=jnp.float32)
        pair = pair + bias_query[:, columns]
        for h in range(2):
            part = turned(pair[:, h * HEAD_DIM : (h + 1) * HEAD_DIM]).astype(jnp.bfloat16)
            queries[:, (2 * g + h) * HEAD_DIM : (2 * g + h + 1) * HEAD_DIM] = part

    gather_out.forward()
    chain_up.receive(1)
    for copy in send_kv:
        copy.wait_recv()
    chain_up.send(2)
    save_kv = here(kv, paired_out, 12)
    save_kv.start()
    slots_out[...] = slots_all[...]

    for g in range(KV_HEADS):
        keys = kv[:, :, g * HEAD_DIM : (g + 1) * HEAD_DIM].reshape(n_s * rows, HEAD_DIM)
        values = kv[:, :, kv_width + g * HEAD_DIM : kv_width + (g + 1) * HEAD_DIM]
        values = values.reshape(n_s * rows, HEAD_DIM)

        def head(i, carry, g=g, keys=keys, values=values):
            h = g * repeat + i
            columns = pl.ds(pl.multiple_of(h * HEAD_DIM, HEAD_DIM), HEAD_DIM)
            raw = lax.dot_general(
                keys, queries[:, columns], (((1,), (1,)), ((), ())),
                preferred_element_type=jnp.float32,
            )
            scores = raw * scale + bias[...]
            top = jnp.max(scores, 0, keepdims=True)
            expo = jnp.exp(scores - top)
            total = jnp.sum(expo, 0, keepdims=True)
            probs = (expo * (1.0 / total)).astype(jnp.bfloat16)
            mixed = lax.dot_general(
                values, probs, (((0,), (0,)), ((), ())), preferred_element_type=jnp.float32
            )
            attended[:, columns] = mixed.T.astype(jnp.bfloat16)
            logsum[pl.ds(pl.multiple_of(h * 8, 8), 8)] = jnp.broadcast_to(
                top + jnp.log(total), (8, rows)
            )
            return carry

        lax.fori_loop(0, repeat, head, 0)
        if g == 0:
            gather_out.last()
            gather_gu.start()

    gather_out.finish()
    save_out = here(out_w, out_out, 13)
    save_out.start()
    mixed = attended[...]
    for g in range(width // 256):
        columns = slice(g * 256, (g + 1) * 256)
        part = jnp.dot(mixed, out_w[:, columns], preferred_element_type=jnp.float32)
        resid[:, columns] = tokens[:, columns].astype(jnp.float32) + part
    value = resid[...]
    root = lax.rsqrt(jnp.mean(value * value, -1, keepdims=True) + epsilon)
    own_tokens = pl.ds(pl.multiple_of(s * rows, rows), rows)
    normed[own_tokens] = (value * root * gain_two[...]).astype(jnp.bfloat16)
    chain_normed.send(1)

    wide = hidden_v.shape[2]
    count = units // wide

    def saves(owner, t, slot):
        place = (
            pl.ds(pl.multiple_of(owner * rows, rows), rows),
            pl.ds(pl.multiple_of(t * wide, wide), wide),
        )
        return [
            here(part.at[slot], whole.at[place], 16 + 3 * slot + i)
            for i, (part, whole) in enumerate(
                ((hidden_v, hidden), (gate_part, factor_gate), (up_part, factor_up))
            )
        ]

    def feed(owner, done):
        def body(t, carry):
            slot = lax.rem(t + done, 2)
            mine = normed[pl.ds(pl.multiple_of(owner * rows, rows), rows)]
            gate_columns = pl.ds(pl.multiple_of(t * wide, wide), wide)
            up_columns = pl.ds(pl.multiple_of(units + t * wide, wide), wide)
            gate = jnp.dot(mine, gu[:, gate_columns], preferred_element_type=jnp.float32)
            up = jnp.dot(mine, gu[:, up_columns], preferred_element_type=jnp.float32)
            sigma = jax.nn.sigmoid(gate)
            activated = gate * sigma

            @pl.when(t + done >= 2)
            def _():
                for copy in saves(owner, t, slot):
                    copy.wait()

            hidden_v[slot] = (activated * up).astype(jnp.bfloat16)
            gate_part[slot] = (up * sigma * (1.0 + gate * (1.0 - sigma))).astype(jnp.bfloat16)
            up_part[slot] = activated.astype(jnp.bfloat16)
            for copy in saves(owner, t, slot):
                copy.start()
            return carry

        lax.fori_loop(0, count, body, 0)

    chain_up.receive(2)
    chain_normed.receive(1)
    chain_normed.send(2)
    gather_gu.forward()
    chain_normed.receive(2)
    chain_normed.send(3)
    gather_gu.last()
    gather_down.start()
    gather_gu.finish()
    save_gu = here(gu, gu_all, 22)
    save_gu.start()
    chain_normed.receive(3)
    chain_up.send(3)
    save_normed = here(normed, normed_all, 23)
    save_normed.start()
    feed(s, 0)
    feed(s ^ 1, count)
    feed(s ^ 2, 2 * count)
    gather_down.forward()
    feed(s ^ 3, 3 * count)
    gather_down.last()
    for t in (count - 2, count - 1):
        for copy in saves(s ^ 3, t, (t + 3 * count) % 2):
            copy.wait()
    chain_up.receive(3)
    gather_down.finish()
    for copy in (save_own, save_kv_w, save_q_w, save_kv, save_out, save_gu, save_normed):
        copy.wait()
    for part in (gather_kv, gather_q, gather_out, gather_gu, gather_down, chain_up, chain_normed):
        part.sent()
    for copy in send_small + send_slots + send_kv:
        copy.wait_send()


def pick_units(gate, up, out, stride, unit, padded):
    rank = lax.axis_index("seq")
    pieces = gate.shape[1] // stride
    half = out.shape[1] // 2
    window, tile = 512, 128
    rows = lax.broadcasted_iota(jnp.int32, (window, tile), 0)
    columns = lax.broadcasted_iota(jnp.int32, (window, tile), 1)
    for first in range(0, 2 * half, tile):
        source = gate if first < half else up
        local = first % half
        total = jnp.zeros((out.shape[0], tile), jnp.float32)
        for f in range(pieces):
            low = max(local, f * padded)
            high = min(local + tile, f * padded + unit)
            if low >= high:
                continue
            begin = f * stride + rank * unit
            base = jnp.minimum(begin // 128, (source.shape[1] - window) // 128) * 128
            base = pl.multiple_of(base, 128)
            wanted = columns + (local - f * padded + begin - base)
            inside = (columns >= low - local) & (columns < high - local)
            chosen = jnp.where((rows == wanted) & inside, 1.0, 0.0).astype(jnp.bfloat16)
            total += jnp.dot(
                source[:, pl.ds(base, window)], chosen, preferred_element_type=jnp.float32
            )
        out[:, first : first + tile] = total.astype(jnp.bfloat16)


def front(tokens, cotangent, lengths, balance, vectors, weights):
    rows, width = tokens.shape
    n_s = lax.axis_size("seq")
    w_query, w_key, w_value, w_out, w_gate, w_up, w_down = weights
    block = w_query.shape[0]
    unit_pad = -(-w_down.shape[0] // n_s // 16) * 16
    kv_width = KV_HEADS * HEAD_DIM
    qkv_width = width + 2 * kv_width
    units = 8 * unit_pad
    group = n_s * rows
    wide = 768
    low, full = jnp.bfloat16, jnp.float32
    small = sum(
        jnp.pad(v.astype(full)[None], ((i, 7 - i), (0, 2 * block - v.shape[0])))
        for i, v in enumerate(vectors)
    )
    half = HEAD_DIM // 2
    inverse = rope_base ** (-(np.arange(half, dtype=np.float32) * np.float32(2.0 / HEAD_DIM)))
    inverse = jnp.asarray(np.concatenate([inverse, inverse])[None], full)
    smem = pl.BlockSpec(memory_space=pltpu.SMEM)
    vmem = pl.BlockSpec(memory_space=pltpu.VMEM)
    hbm = pl.BlockSpec(memory_space=pl.ANY)
    shape = jax.ShapeDtypeStruct
    return pl.pallas_call(
        front_kernel,
        in_specs=[smem, vmem, hbm, vmem, vmem, vmem] + [hbm] * 7,
        out_specs=[hbm] * 9 + [vmem, hbm] + [vmem] * 11,
        out_shape=[
            shape((width, 2 * units), low),
            shape((units, width), low),
            shape((group, width), low),
            shape((group, width), low),
            shape((group, units), low),
            shape((group, units), low),
            shape((group, units), low),
            shape((width, qkv_width), low),
            shape((width, width), low),
            shape((rows, width), low),
            shape((n_s, rows, 2 * kv_width), low),
            shape((n_s, rows, 128), full),
            shape((8 * HEADS, rows), full),
            shape((rows, width), low),
            shape((rows, width), full),
            shape((rows, width), low),
            shape((1, width), full),
            shape((1, width), full),
            shape((8, rows), full),
            shape((8, rows), full),
            shape((rows, HEAD_DIM), full),
            shape((rows, HEAD_DIM), full),
        ],
        scratch_shapes=[
            pltpu.VMEM((width, width), low),
            pltpu.VMEM((width, 2 * kv_width), low),
            pltpu.VMEM((width, width), low),
            pltpu.VMEM(w_gate.shape, low),
            pltpu.VMEM(w_up.shape, low),
            pltpu.VMEM((width, 2 * units), low),
            pltpu.VMEM((group, width), low),
            pltpu.VMEM((n_s, rows, 2 * kv_width), low),
            pltpu.VMEM((8, 2 * block), full),
            pltpu.VMEM((8, 8, 2 * block), full),
            pltpu.VMEM((n_s, rows, 128), full),
            pltpu.VMEM((group, rows), full),
            pltpu.VMEM((rows, width), low),
            pltpu.VMEM((unit_pad, width), low),
            pltpu.VMEM((unit_pad, width), low),
            pltpu.VMEM((2, rows, wide), low),
            pltpu.VMEM((2, rows, wide), low),
            pltpu.VMEM((2, rows, wide), low),
            pltpu.SemaphoreType.DMA((24,)),
            pltpu.SemaphoreType.DMA((56,)),
            pltpu.SemaphoreType.DMA((56,)),
            pltpu.SemaphoreType.DMA((12,)),
            pltpu.SemaphoreType.DMA((12,)),
        ],
        compiler_params=pltpu.CompilerParams(
            collective_id=0, has_side_effects=True, vmem_limit_bytes=62 * 2**20
        ),
        name="front",
    )(
        lengths, tokens, cotangent, small, balance.reshape(1, rows), inverse,
        w_query, w_key, w_value, w_out, w_gate, w_up, w_down,
    )


def ffn_kernel(
    normed_all, upstream_all, w_gu, w_down, hidden_all, factor_gate, factor_up,
    columns, grad_down, gu_sum, branch, down_arrived, gu_arrived,
    normed, upstream, gu, down, hidden, d_both, partial, z_one, z_two, z_three,
    down_x, down_y, down_last, down_piece,
    load, ssem, rsem,
):
    f = lax.axis_index("fsdp")
    s = lax.axis_index("seq")
    n_s = len(ORDER)
    group, width = normed.shape
    rows = group // n_s
    half_rows = group // 2
    units = down.shape[0]
    tile = 256
    tiles = units // tile
    wide = 768
    block = gu.shape[0] // 8
    unit = units // 8
    half = width // 2
    plane = [f ^ k for k in range(8)]
    full = jnp.float32

    entry = pltpu.get_barrier_semaphore()
    for k in (1, 2, 4):
        pl.semaphore_signal(entry, inc=1, device_id={"fsdp": plane[k]}, device_id_type=MESH)
    for j in (1, n_s - 1):
        pl.semaphore_signal(
            entry, inc=1, device_id={"seq": lax.rem(s + j, n_s)}, device_id_type=MESH
        )

    def here(source, target, index):
        return pltpu.make_async_copy(source, target, load.at[index])

    def there(source, target, index, **device):
        return pltpu.make_async_remote_copy(
            src_ref=source, dst_ref=target, send_sem=ssem.at[index], recv_sem=rsem.at[index],
            device_id=device, device_id_type=MESH,
        )

    def part(ref, owner, size):
        return ref.at[pl.ds(pl.multiple_of(owner * size, 16), size)]

    early, late = range(0, n_s // 2), range(n_s // 2, n_s)

    def rows_of(p):
        return pl.ds(p * rows, rows)

    def row_loads(p):
        owner = lax.rem(s + n_s - ORDER[p], n_s)
        mine = rows_of(p)
        return [
            here(part(upstream_all, owner, rows), upstream.at[mine], 5 * p),
            here(part(factor_gate, owner, rows), d_both.at[mine, pl.ds(0, units)], 5 * p + 1),
            here(part(factor_up, owner, rows), d_both.at[mine, pl.ds(units, units)], 5 * p + 2),
            here(part(hidden_all, owner, rows), hidden.at[mine], 5 * p + 3),
            here(part(normed_all, owner, rows), normed.at[mine], 5 * p + 4),
        ]

    def down_load(t):
        mine = pl.ds(pl.multiple_of(t * wide, wide), wide)
        return here(w_down.at[mine], down.at[mine], 20 + t)

    def gu_load(n):
        mine = pl.ds(pl.multiple_of(n * 512, 512), 512)
        return here(w_gu.at[mine], gu.at[mine], 23 + n)

    loads = [row_loads(p) for p in range(n_s)]
    order = [loads[0][0], loads[1][0], down_load(0)]
    order += [loads[p][i] for i in (1, 2) for p in early]
    order += [down_load(t) for t in range(1, units // wide)]
    order += [gu_load(n) for n in range(width // 512)]
    order += [loads[p][i] for i in (0, 1, 2) for p in late]
    order += [loads[p][i] for i in (3, 4) for p in range(n_s)]
    for copy in order:
        copy.start()

    def forward(blocks, wait):
        for p in blocks:
            for copy in loads[p][:3]:
                copy.wait()
        mine = pl.ds(blocks[0] * rows, len(blocks) * rows)

        def body(t, carry):
            if wait:
                down_load(t).wait()
            gate_columns = pl.ds(pl.multiple_of(t * wide, wide), wide)
            up_columns = pl.ds(pl.multiple_of(units + t * wide, wide), wide)
            d_hidden = lax.dot_general(
                upstream[mine], down[gate_columns], (((1,), (1,)), ((), ())),
                preferred_element_type=full,
            )
            value = d_hidden * d_both[mine, gate_columns].astype(full)
            d_both[mine, gate_columns] = value.astype(jnp.bfloat16)
            value = d_hidden * d_both[mine, up_columns].astype(full)
            d_both[mine, up_columns] = value.astype(jnp.bfloat16)
            return carry

        lax.fori_loop(0, units // wide, body, 0)

    def backward(blocks, wait):
        part_rows = pl.ds(blocks[0] * rows, len(blocks) * rows)

        def body(n, carry):
            if wait:
                gu_load(n).wait()
            out_columns = pl.ds(pl.multiple_of(n * 512, 512), 512)
            value = lax.dot_general(
                d_both[part_rows], gu[out_columns], (((1,), (1,)), ((), ())),
                preferred_element_type=full,
            )
            partial[part_rows, out_columns] = value.astype(jnp.bfloat16)
            return carry

        lax.fori_loop(0, width // 512, body, 0)

    chain = SumChain(in_order(partial, rows), z_one, z_two, z_three, there, 0)
    pieces = [(first, min(group, units - first)) for first in range(0, units, group)]
    forward(early, True)
    backward(early, True)
    pl.semaphore_wait(entry, 5)
    chain.one()
    forward(late, False)
    backward(late, False)
    chain.add_one()
    chain.two()

    for p in range(n_s):
        loads[p][3].wait()
        loads[p][4].wait()

    def down_body(t, carry):
        unit_rows = pl.ds(pl.multiple_of(t * tile, tile), tile)
        value = lax.dot_general(
            hidden[:, unit_rows], upstream[...], (((0,), (0,)), ((), ())),
            preferred_element_type=full,
        )
        down[unit_rows] = value.astype(jnp.bfloat16)
        return carry

    lax.fori_loop(0, tiles, down_body, 0)
    down_core = [
        there(part(down, plane[2 * i + 1], unit), down_arrived.at[i], 6 + i, fsdp=plane[1])
        for i in range(4)
    ]
    for copy in down_core:
        copy.start()

    def gu_body(m, carry):
        in_columns = pl.ds(pl.multiple_of(m * tile, tile), tile)
        turned = normed[:, in_columns].T
        for first in range(0, 2 * units, units // 3):
            value = jnp.dot(turned, d_both[:, first : first + units // 3], preferred_element_type=full)
            gu[in_columns, first : first + units // 3] = value.astype(jnp.bfloat16)
        return carry

    lax.fori_loop(0, 2, gu_body, 0)

    def add_arrived(i, ref, size, arrived, pieces, copies, index):
        copies[i].wait_recv()
        fetch = [
            here(arrived.at[i, :, columns], piece, index + k)
            for k, (columns, piece) in enumerate(pieces)
        ]
        for copy in fetch:
            copy.start()
        target = part(ref, plane[2 * i], size)
        for copy, (columns, piece) in zip(fetch, pieces):
            copy.wait()
            target[:, columns] = (
                target[:, columns].astype(full) + piece[...].astype(full)
            ).astype(jnp.bfloat16)

    down_pieces = [(pl.ds(0, width), down_piece)]
    for i in (3, 1, 2, 0):
        add_arrived(i, down, unit, down_arrived, down_pieces, down_core, 26)
    to_x, to_y, to_both = [part(down, plane[k], unit) for k in (2, 4, 6)]
    low_half, high_half = pl.ds(0, half), pl.ds(half, half)
    down_first = [
        there(to_x.at[:, low_half], down_x.at[0], 10, fsdp=plane[2]),
        there(to_both.at[:, low_half], down_x.at[1], 11, fsdp=plane[2]),
        there(to_y.at[:, high_half], down_y.at[0], 12, fsdp=plane[4]),
        there(to_both.at[:, high_half], down_y.at[1], 13, fsdp=plane[4]),
    ]
    for copy in down_first:
        copy.start()
    lax.fori_loop(2, width // tile - 1, gu_body, 0)
    chain.add_two()
    chain.three()
    lax.fori_loop(width // tile - 1, width // tile, gu_body, 0)
    gu_core = [
        there(part(gu, plane[2 * i + 1], block), gu_arrived.at[i], 16 + i, fsdp=plane[1])
        for i in range(4)
    ]
    for copy in gu_core:
        copy.start()

    again = [
        here(
            w_down.at[first : first + count],
            d_both.at[:count, i * width : (i + 1) * width], 33 + i,
        )
        for i, (first, count) in enumerate(pieces)
    ]
    for copy in again:
        copy.start()
    for copy in again:
        copy.wait()

    def branch_body(n, carry):
        out_columns = pl.ds(pl.multiple_of(n * wide, wide), wide)
        for m in range(2):
            mine = slice(m * half_rows, (m + 1) * half_rows)
            value = jnp.zeros((half_rows, wide), full)
            for i, (first, count) in enumerate(pieces):
                columns_here = pl.ds(pl.multiple_of(i * width + n * wide, wide), wide)
                value += jnp.dot(
                    hidden[mine, first : first + count], d_both[:count, columns_here],
                    preferred_element_type=full,
                )
            upstream[mine, out_columns] = value.astype(jnp.bfloat16)
        return carry

    lax.fori_loop(0, width // wide, branch_body, 0)
    chain.last(columns)
    chain_branch = SumChain(in_order(upstream, rows), z_one, z_two, z_three, there, 22)
    chain_branch.one()
    down_second = [
        there(to_y.at[:, low_half], down_last.at[0], 14, fsdp=plane[4]),
        there(to_x.at[:, high_half], down_last.at[1], 15, fsdp=plane[2]),
    ]
    down_first[1].wait_recv()
    to_y[:, :half] = (to_y[:, :half].astype(full) + down_x[1].astype(full)).astype(jnp.bfloat16)
    down_second[0].start()
    down_first[3].wait_recv()
    to_x[:, half:] = (to_x[:, half:].astype(full) + down_y[1].astype(full)).astype(jnp.bfloat16)
    down_second[1].start()
    gu_pieces = [
        (pl.ds(0, units), hidden.at[:block]),
        (pl.ds(units, units), hidden.at[block : 2 * block]),
    ]
    store = [here(part(gu, plane[2 * i], block), gu_sum.at[i], 29 + i) for i in range(4)]
    for i in (3, 1, 2, 0):
        add_arrived(i, gu, block, gu_arrived, gu_pieces, gu_core, 27)
        store[i].start()
    down_first[0].wait_recv()
    down_first[2].wait_recv()
    own = part(down, f, unit)
    down_second[0].wait_recv()
    grad_down[:, :half] = (
        own[:, :half].astype(full) + down_x[0].astype(full) + down_last[0].astype(full)
    )
    down_second[1].wait_recv()
    grad_down[:, half:] = (
        own[:, half:].astype(full) + down_y[0].astype(full) + down_last[1].astype(full)
    )
    chain_branch.add_one()
    chain_branch.one_sent()
    store_branch = here(upstream, branch, 36)
    store_branch.start()
    chain.one_sent()
    chain.two_sent()
    chain.three_sent()
    for copy in down_core + down_first + down_second + gu_core:
        copy.wait_send()
    for copy in store + [store_branch]:
        copy.wait()


def ffn(normed_all, upstream_all, w_gu, w_down, hidden, factor_gate, factor_up):
    group, width = normed_all.shape
    units = w_down.shape[0]
    rows = group // len(ORDER)
    unit, block, half = units // 8, width // 8, width // 2
    low, full = jnp.bfloat16, jnp.float32
    vmem = pl.BlockSpec(memory_space=pltpu.VMEM)
    hbm = pl.BlockSpec(memory_space=pl.ANY)
    shape = jax.ShapeDtypeStruct
    return pl.pallas_call(
        ffn_kernel,
        in_specs=[hbm] * 7,
        out_specs=[vmem] * 2 + [hbm] * 4,
        out_shape=[
            shape((rows, width), full),
            shape((unit, width), full),
            shape((4, block, 2 * units), low),
            shape((group, width), low),
            shape((4, unit, width), low),
            shape((4, block, 2 * units), low),
        ],
        scratch_shapes=[
            pltpu.VMEM((group, width), low),
            pltpu.VMEM((group, width), low),
            pltpu.VMEM((width, 2 * units), low),
            pltpu.VMEM((units, width), low),
            pltpu.VMEM((group, units), low),
            pltpu.VMEM((group, 2 * units), low),
            pltpu.VMEM((group, width), low),
            pltpu.VMEM((rows, width), low),
            pltpu.VMEM((2, rows, width), low),
            pltpu.VMEM((2, rows, width), low),
            pltpu.VMEM((2, unit, half), low),
            pltpu.VMEM((2, unit, half), low),
            pltpu.VMEM((2, unit, half), low),
            pltpu.VMEM((unit, width), low),
            pltpu.SemaphoreType.DMA((40,)),
            pltpu.SemaphoreType.DMA((28,)),
            pltpu.SemaphoreType.DMA((28,)),
        ],
        compiler_params=pltpu.CompilerParams(
            collective_id=1, has_side_effects=True, vmem_limit_bytes=63 * 2**20
        ),
        name="ffn",
    )(normed_all, upstream_all, w_gu, w_down, hidden, factor_gate, factor_up)[:4]


def back_kernel(
    columns, resid, gain_two, cotangent, attended, queries, paired, slots, slot_row, first_row,
    logsum, normed_one, tokens, gain_one, cosine, sine, w_out, w_qkv, gu_sum, branch,
    layer, input_rows, vector, grad_out, grad_qkv, gu_rows,
    out_w, qkv, gu_own, gu_to_y, gu_to_x, gu_x, gu_y, gu_ended,
    branch_v, z_one, z_two, z_three, working, bias, d_branch, d_attended, d_qkv, d_resid,
    keys_grad, values_grad, dkv, dkv_in,
    out_arrived, out_x, out_y, out_ended, qkv_arrived, qkv_x, qkv_y, qkv_ended,
    out_one, out_two, out_three, qkv_one, qkv_two, qkv_three, vector_in,
    load, ssem, rsem,
):
    f = lax.axis_index("fsdp")
    s = lax.axis_index("seq")
    rows, width = tokens.shape
    n_s = paired.shape[0]
    kv_width = KV_HEADS * HEAD_DIM
    repeat = HEADS // KV_HEADS
    scale = HEAD_DIM ** (-0.5)
    block = width // 8
    piece = block // n_s
    units = gu_sum.shape[2] // 2
    tile = 256
    full, low = jnp.float32, jnp.bfloat16
    plane = [f ^ k for k in range(8)]

    entry = pltpu.get_barrier_semaphore()
    for k in (1, 2, 4):
        pl.semaphore_signal(entry, inc=1, device_id={"fsdp": plane[k]}, device_id_type=MESH)
    for j in range(1, n_s):
        pl.semaphore_signal(
            entry, inc=1, device_id={"seq": lax.rem(s + j, n_s)}, device_id_type=MESH
        )

    def here(source, target, index):
        return pltpu.make_async_copy(source, target, load.at[index])

    def there(source, target, index, **device):
        return pltpu.make_async_remote_copy(
            src_ref=source, dst_ref=target, send_sem=ssem.at[index], recv_sem=rsem.at[index],
            device_id=device, device_id_type=MESH,
        )

    low_units, high_units = pl.ds(0, units), pl.ds(units, units)
    load_branch = here(branch, branch_v, 0)
    load_out = here(w_out, out_w, 1)
    load_gu = [
        here(gu_sum.at[0], gu_own, 2),
        here(gu_sum.at[2, :, low_units], gu_to_y, 3),
        here(gu_sum.at[1, :, high_units], gu_to_x, 4),
    ]
    load_qkv = here(w_qkv, qkv, 5)
    load_columns = here(columns, working, 7)
    for copy in [load_columns, load_branch, load_out] + load_gu + [load_qkv]:
        copy.start()

    gu_first = [
        there(gu_sum.at[3, :, low_units], gu_x.at[1], 0, fsdp=plane[2]),
        there(gu_sum.at[3, :, high_units], gu_y.at[1], 1, fsdp=plane[4]),
        there(gu_sum.at[1, :, low_units], gu_x.at[0], 2, fsdp=plane[2]),
        there(gu_sum.at[2, :, high_units], gu_y.at[0], 3, fsdp=plane[4]),
    ]
    gu_second = [
        there(gu_to_y, gu_ended.at[0], 4, fsdp=plane[4]),
        there(gu_to_x, gu_ended.at[1], 5, fsdp=plane[2]),
    ]

    def around(j):
        return {"seq": lax.rem(s + j, n_s)}

    def rows_for(ref, first, j):
        owner = lax.rem(s + j, n_s)
        return ref.at[pl.ds(pl.multiple_of(first + owner * piece, 16), piece)]

    gu_send = [there(rows_for(gu_own, 0, j), gu_rows.at[j], 5 + j, **around(j)) for j in range(1, n_s)]
    dkv_send = [
        [
            there(dkv.at[g, lax.rem(s + j, n_s)], dkv_in.at[g, j], 8 + 3 * g + j, **around(j))
            for j in range(1, n_s)
        ]
        for g in range(KV_HEADS)
    ]
    chain = SumChain(in_order(branch_v, rows), z_one, z_two, z_three, there, 16)
    sum_out = SumPlane(out_w, block, plane, out_arrived, out_x, out_y, out_ended, there, 24)
    sum_qkv = SumPlane(qkv, block, plane, qkv_arrived, qkv_x, qkv_y, qkv_ended, there, 36)

    def own_part(ref):
        return lambda j: rows_for(ref, f * block, n_s - j)

    chain_out = SumChain(own_part(out_w), out_one, out_two, out_three, there, 48)
    chain_qkv = SumChain(own_part(qkv), qkv_one, qkv_two, qkv_three, there, 54)
    vector_send = [
        there(vector_in.at[0], vector_in.at[1], 60, fsdp=plane[1]),
        there(vector_in.at[2], vector_in.at[3], 61, fsdp=plane[2]),
        there(vector_in.at[4], vector_in.at[5], 62, fsdp=plane[4]),
    ] + [there(vector_in.at[6], vector_in.at[6 + j], 62 + j, **around(j)) for j in range(1, n_s)]

    pl.semaphore_wait(entry, 3 + n_s - 1)
    for copy in gu_first:
        copy.start()
    load_branch.wait()
    chain.two()

    def norm_back(value, gain, grad):
        root = lax.rsqrt(jnp.mean(value * value, -1, keepdims=True) + epsilon)
        scaled = gain * grad
        inner = jnp.mean(scaled * value, -1, keepdims=True)
        gain_grad = jnp.sum(grad * (value * root), 0, keepdims=True)
        return root * scaled - value * (root * root * root * inner), gain_grad

    load_columns.wait()
    d_norm, gain_two_grad = norm_back(resid[...], gain_two[...], working[...])
    d_total = cotangent[...].astype(full) + d_norm
    d_branch[...] = d_total.astype(low)
    d_resid[...] = d_total
    for j in range(n_s):
        keys_slot = slots[j]
        keys_slot = jnp.concatenate([keys_slot] * (rows // 128), 1)
        ok = (keys_slot <= slot_row[0:1]) & (keys_slot >= first_row[0:1])
        bias[j * rows : (j + 1) * rows] = jnp.where(ok, 0.0, -1e30)
    load_out.wait()
    for n in range(width // tile):
        value = lax.dot_general(
            d_branch[...], out_w[n * tile : (n + 1) * tile], (((1,), (1,)), ((), ())),
            preferred_element_type=full,
        )
        d_attended[:, n * tile : (n + 1) * tile] = value.astype(low)

    def turned_back(value):
        return value * cosine[...] + pltpu.roll(value * sine[...], HEAD_DIM // 2, 1)

    for g in range(KV_HEADS):
        keys = paired[:, :, g * HEAD_DIM : (g + 1) * HEAD_DIM].reshape(n_s * rows, HEAD_DIM)
        values = paired[:, :, kv_width + g * HEAD_DIM : kv_width + (g + 1) * HEAD_DIM]
        values = values.reshape(n_s * rows, HEAD_DIM)
        keys_grad[...] = jnp.zeros_like(keys_grad)
        values_grad[...] = jnp.zeros_like(values_grad)

        def head(i, carry, g=g, keys=keys, values=values):
            h = g * repeat + i
            head_columns = pl.ds(pl.multiple_of(h * HEAD_DIM, HEAD_DIM), HEAD_DIM)
            query = queries[:, head_columns]
            grad = d_attended[:, head_columns]
            raw = lax.dot_general(
                keys, query, (((1,), (1,)), ((), ())), preferred_element_type=full
            )
            logs = logsum[pl.ds(pl.multiple_of(h * 8, 8), 8)][0:1]
            probs = jnp.exp(raw * scale + bias[...] - logs)
            d_probs = lax.dot_general(
                values, grad, (((1,), (1,)), ((), ())), preferred_element_type=full
            )
            delta = jnp.sum(probs * d_probs, 0, keepdims=True)
            d_score = (probs * (d_probs - delta)).astype(low)
            turned = lax.dot_general(
                keys, d_score, (((0,), (0,)), ((), ())), preferred_element_type=full
            )
            d_qkv[:, head_columns] = turned_back((turned * scale).T).astype(low)
            keys_grad[...] += jnp.dot(d_score, query, preferred_element_type=full) * scale
            values_grad[...] += jnp.dot(probs.astype(low), grad, preferred_element_type=full)
            return carry

        lax.fori_loop(0, repeat, head, 0)
        dkv[g, :, :, :HEAD_DIM] = keys_grad[...].astype(low).reshape(n_s, rows, HEAD_DIM)
        dkv[g, :, :, HEAD_DIM:] = values_grad[...].astype(low).reshape(n_s, rows, HEAD_DIM)
        for copy in dkv_send[g]:
            copy.start()

    turned = attended[...].T
    for n in range(width // tile):
        n_columns = slice(n * tile, (n + 1) * tile)
        value = jnp.dot(turned, d_branch[:, n_columns], preferred_element_type=full)
        out_w[:, n_columns] = value.astype(low)
    sum_out.start_core()
    load_qkv.wait()

    def back_one(first, count, start):
        for n in range(width // tile):
            n_rows = slice(n * tile, (n + 1) * tile)
            value = lax.dot_general(
                d_qkv[:, first : first + count], qkv[n_rows, first : first + count],
                (((1,), (1,)), ((), ())), preferred_element_type=full,
            )
            working[:, n_rows] = value if start else working[:, n_rows] + value

    back_one(0, width, True)
    normed_turned = normed_one[...].T
    for n in range(width // tile):
        n_columns = slice(n * tile, (n + 1) * tile)
        value = jnp.dot(normed_turned, d_qkv[:, n_columns], preferred_element_type=full)
        qkv[:, n_columns] = value.astype(low)
    for copy in load_gu:
        copy.wait()
    gu_first[0].wait_recv()
    gu_to_y[...] = (gu_to_y[...].astype(full) + gu_x[1].astype(full)).astype(low)
    gu_second[0].start()
    gu_first[1].wait_recv()
    gu_to_x[...] = (gu_to_x[...].astype(full) + gu_y[1].astype(full)).astype(low)
    gu_second[1].start()
    sum_out.start_first()

    for g in range(KV_HEADS):
        for copy in dkv_send[g]:
            copy.wait_recv()
        total = dkv[g, s].astype(full)
        for j in range(1, n_s):
            total = total + dkv_in[g, j].astype(full)
        key_columns = slice(width + g * HEAD_DIM, width + (g + 1) * HEAD_DIM)
        value_columns = slice(width + kv_width + g * HEAD_DIM, width + kv_width + (g + 1) * HEAD_DIM)
        d_qkv[:, key_columns] = turned_back(total[:, :HEAD_DIM]).astype(low)
        d_qkv[:, value_columns] = total[:, HEAD_DIM:].astype(low)
    back_one(width, 2 * kv_width, False)
    value = jnp.dot(normed_turned, d_qkv[:, width:], preferred_element_type=full)
    qkv[:, width:] = value.astype(low)
    sum_qkv.start_core()
    chain.add_two()
    chain.three()

    d_norm, gain_one_grad = norm_back(tokens[...].astype(full), gain_one[...], working[...])
    input_rows[...] = (d_resid[...] + d_norm).astype(low)
    bias_grad = jnp.sum(d_qkv[...].astype(full), 0, keepdims=True)
    vectors = jnp.concatenate([gain_one_grad, gain_two_grad, bias_grad], 1)
    part = vectors.shape[1] // 8
    for r in range(8):
        vector_in[0, r : r + 1] = vectors[:, r * part : (r + 1) * part]
    vector_send[0].start()
    sum_qkv.start_first()
    vector_send[0].wait_recv()
    vector_in[2] = vector_in[0] + vector_in[1]
    vector_send[1].start()

    gu_first[2].wait_recv()
    gu_second[0].wait_recv()
    total = gu_own[:, :units].astype(full) + gu_x[0].astype(full) + gu_ended[0].astype(full)
    gu_own[:, :units] = total.astype(low)
    gu_first[3].wait_recv()
    gu_second[1].wait_recv()
    total = gu_own[:, units:].astype(full) + gu_y[0].astype(full) + gu_ended[1].astype(full)
    gu_own[:, units:] = total.astype(low)
    for copy in gu_send:
        copy.start()
    keep_rows = here(rows_for(gu_own, 0, 0), gu_rows.at[0], 6)
    keep_rows.start()
    sum_out.start_second()
    vector_send[1].wait_recv()
    vector_in[4] = vector_in[2] + vector_in[3]
    vector_send[2].start()

    sum_qkv.start_second()
    sum_out.finish()
    chain_out.one()
    vector_send[2].wait_recv()
    vector_in[6] = vector_in[4] + vector_in[5]
    for copy in vector_send[3:]:
        copy.start()
    chain_out.add_one()
    chain_out.two()
    sum_qkv.finish()
    chain_qkv.one()
    chain_out.add_two()
    chain_out.three()
    chain.last(working)
    layer[...] = (resid[...] + working[...]).astype(low)
    chain_qkv.add_one()
    chain_qkv.two()
    for copy in vector_send[3:]:
        copy.wait_recv()
    vector[...] = vector_in[6] + vector_in[7] + vector_in[8] + vector_in[9]
    chain_out.last(grad_out)
    chain_qkv.add_two()
    chain_qkv.three()
    chain_qkv.last(grad_qkv)
    for copy in gu_send:
        copy.wait_recv()
    keep_rows.wait()
    for part in (chain_out, chain_qkv):
        part.one_sent()
        part.two_sent()
        part.three_sent()
    chain.two_sent()
    chain.three_sent()
    sum_out.sent()
    sum_qkv.sent()
    for copy in gu_first + gu_second + gu_send + vector_send:
        copy.wait_send()
    for g in range(KV_HEADS):
        for copy in dkv_send[g]:
            copy.wait_send()


def back(
    columns, resid, gain_two, cotangent, attended, queries, paired, slots, slot_row, first_row,
    logsum, normed_one, tokens, gain_one, cosine, sine, w_out, w_qkv, gu_sum, branch,
):
    rows, width = tokens.shape
    n_s = paired.shape[0]
    group = n_s * rows
    kv_width = KV_HEADS * HEAD_DIM
    qkv_width = width + 2 * kv_width
    block = width // 8
    piece = block // n_s
    units = gu_sum.shape[2] // 2
    low, full = jnp.bfloat16, jnp.float32
    vmem = pl.BlockSpec(memory_space=pltpu.VMEM)
    hbm = pl.BlockSpec(memory_space=pl.ANY)
    shape = jax.ShapeDtypeStruct
    vectors = (2 * width + qkv_width) // 8
    return pl.pallas_call(
        back_kernel,
        in_specs=[hbm] + [vmem] * 15 + [hbm] * 4,
        out_specs=[vmem] * 5 + [hbm],
        out_shape=[
            shape((rows, width), low),
            shape((rows, width), low),
            shape((8, vectors), full),
            shape((piece, width), full),
            shape((piece, qkv_width), full),
            shape((n_s, piece, 2 * units), low),
        ],
        scratch_shapes=[
            pltpu.VMEM((width, width), low),
            pltpu.VMEM((width, qkv_width), low),
            pltpu.VMEM((block, 2 * units), low),
            pltpu.VMEM((block, units), low),
            pltpu.VMEM((block, units), low),
            pltpu.VMEM((2, block, units), low),
            pltpu.VMEM((2, block, units), low),
            pltpu.VMEM((2, block, units), low),
            pltpu.VMEM((group, width), low),
            pltpu.VMEM((rows, width), low),
            pltpu.VMEM((2, rows, width), low),
            pltpu.VMEM((2, rows, width), low),
            pltpu.VMEM((rows, width), full),
            pltpu.VMEM((group, rows), full),
            pltpu.VMEM((rows, width), low),
            pltpu.VMEM((rows, width), low),
            pltpu.VMEM((rows, qkv_width), low),
            pltpu.VMEM((rows, width), full),
            pltpu.VMEM((group, HEAD_DIM), full),
            pltpu.VMEM((group, HEAD_DIM), full),
            pltpu.VMEM((KV_HEADS, n_s, rows, 2 * HEAD_DIM), low),
            pltpu.VMEM((KV_HEADS, n_s, rows, 2 * HEAD_DIM), low),
            pltpu.VMEM((4, block, width), low),
            pltpu.VMEM((2, block, width // 2), low),
            pltpu.VMEM((2, block, width // 2), low),
            pltpu.VMEM((2, block, width // 2), low),
            pltpu.VMEM((4, block, qkv_width), low),
            pltpu.VMEM((2, block, qkv_width // 2), low),
            pltpu.VMEM((2, block, qkv_width // 2), low),
            pltpu.VMEM((2, block, qkv_width // 2), low),
            pltpu.VMEM((piece, width), low),
            pltpu.VMEM((2, piece, width), low),
            pltpu.VMEM((2, piece, width), low),
            pltpu.VMEM((piece, qkv_width), low),
            pltpu.VMEM((2, piece, qkv_width), low),
            pltpu.VMEM((2, piece, qkv_width), low),
            pltpu.VMEM((10, 8, vectors), full),
            pltpu.SemaphoreType.DMA((10,)),
            pltpu.SemaphoreType.DMA((68,)),
            pltpu.SemaphoreType.DMA((68,)),
        ],
        compiler_params=pltpu.CompilerParams(
            collective_id=2, has_side_effects=True, vmem_limit_bytes=63 * 2**20
        ),
        name="back",
    )(
        columns, resid, gain_two, cotangent, attended, queries, paired, slots, slot_row, first_row,
        logsum, normed_one, tokens, gain_one, cosine, sine, w_out, w_qkv, gu_sum, branch,
    )


def finish_kernel(
    layer, input_rows, grad_out, grad_qkv, grad_down, gu_rows,
    layer_out, input_grad, out_out, query_out, key_out, value_out, down_out, gate_out, up_out,
):
    s = lax.axis_index("seq")
    n_s = gu_rows.shape[0]
    width = grad_out.shape[1]
    kv_width = KV_HEADS * HEAD_DIM
    unit_pad = grad_down.shape[0]
    unit = down_out.shape[0]
    units = gu_rows.shape[2] // 2
    layer_out[...] = layer[...]
    input_grad[...] = input_rows[...]
    out_out[...] = grad_out[...]
    query_out[...] = grad_qkv[:, :width]
    key_out[...] = grad_qkv[:, width : width + kv_width]
    value_out[...] = grad_qkv[:, width + kv_width :]
    down_out[...] = grad_down[:unit]
    window = 512
    lanes = lax.broadcasted_iota(jnp.int32, (gu_rows.shape[1], 128), 1)
    for base, out in ((0, gate_out), (units, up_out)):
        for f in range(units // unit_pad):
            for owner in range(n_s):
                source = base + f * unit_pad
                begin = min(source // 128 * 128, 2 * units - window)
                target = (f * n_s + owner) * unit
                first = target // 128 * 128
                slot = lax.rem(s + n_s - owner, n_s)
                value = gu_rows[slot, :, begin : begin + window].astype(jnp.float32)
                turn = ((target - first) - (source - begin)) % window
                if turn:
                    value = pltpu.roll(value, turn, 1)
                for t in range(first, min(target + unit, out.shape[1]), 128):
                    part = value[:, t - first : t - first + 128]
                    if t < target:
                        part = jnp.where(lanes >= target - t, part, out[:, t : t + 128])
                    out[:, t : t + 128] = part


def finish(layer, input_rows, grad_out, grad_qkv, grad_down, gu_rows, unit, hidden_width):
    piece, width = grad_out.shape
    kv_width = KV_HEADS * HEAD_DIM
    low, full = jnp.bfloat16, jnp.float32
    shape = jax.ShapeDtypeStruct
    vmem = pl.BlockSpec(memory_space=pltpu.VMEM)
    return pl.pallas_call(
        finish_kernel,
        in_specs=[vmem] * 6,
        out_specs=[vmem] * 9,
        out_shape=[
            shape(layer.shape, low),
            shape(layer.shape, low),
            shape((piece, width), full),
            shape((piece, width), full),
            shape((piece, kv_width), full),
            shape((piece, kv_width), full),
            shape((unit, width), full),
            shape((piece, hidden_width), full),
            shape((piece, hidden_width), full),
        ],
        compiler_params=pltpu.CompilerParams(vmem_limit_bytes=63 * 2**20),
        name="finish",
    )(layer, input_rows, grad_out, grad_qkv, grad_down, gu_rows)


def per_device(
    tokens, cotangent, lengths, balance, norm1_gain, w_query, b_query, w_key, b_key,
    w_value, b_value, w_out, norm2_gain, w_gate, w_up, w_down,
):
    seq_count = lax.axis_size("seq")
    fsdp_count = lax.axis_size("fsdp")
    seq_rank = lax.axis_index("seq")
    fsdp_rank = lax.axis_index("fsdp")
    rows_here, width = tokens.shape
    kv_width = KV_HEADS * HEAD_DIM
    hidden_width = w_gate.shape[1]
    unit = hidden_width // (fsdp_count * seq_count)
    (
        weight_gu, weight_down, upstream_all, normed_all, hidden, factor_gate, factor_up,
        weight_qkv, weight_out, queries, paired, slots, logsum, attended, resid, normed_one,
        gain_one, gain_two, slot_row, first_row, cosine, sine,
    ) = front(
        tokens, cotangent, lengths, balance, (norm1_gain, norm2_gain, b_query, b_key, b_value),
        (w_query, w_key, w_value, w_out, w_gate, w_up, w_down),
    )
    columns, grad_down, gu_sum, branch = ffn(
        normed_all, upstream_all, weight_gu, weight_down, hidden, factor_gate, factor_up
    )
    layer, input_rows, vectors, grad_out, grad_qkv, gu_rows = back(
        columns, resid, gain_two, cotangent, attended, queries, paired, slots, slot_row, first_row,
        logsum, normed_one, tokens, gain_one, cosine, sine, weight_out, weight_qkv, gu_sum, branch,
    )
    (
        layer_out, input_grad, grad_out, grad_query, grad_key, grad_value, grad_down, grad_gate,
        grad_up,
    ) = finish(layer, input_rows, grad_out, grad_qkv, grad_down, gu_rows, unit, hidden_width)
    vectors = vectors.reshape(-1)
    own = width // (fsdp_count * seq_count)
    first = (fsdp_rank * seq_count + seq_rank) * own

    def own_part(offset):
        return lax.dynamic_slice_in_dim(vectors, offset + first, own, 0)

    biases = 2 * width
    return (
        layer_out,
        input_grad,
        own_part(0),
        grad_query,
        own_part(biases),
        grad_key,
        vectors[biases + width : biases + width + kv_width],
        grad_value,
        vectors[biases + width + kv_width :],
        grad_out,
        own_part(width),
        grad_gate,
        grad_up,
        grad_down,
    )


def solution(mesh):
    both = P(("fsdp", "seq"), None)
    both_one = P(("fsdp", "seq"))
    placed = (
        both, both, P("fsdp", None), both_one, P("fsdp"), P("fsdp", None), P("fsdp"),
        P("fsdp", None), P("fsdp"), P("fsdp", None), P("fsdp"), P("fsdp", None), P("fsdp"),
        P("fsdp", None), P("fsdp", None), P("fsdp", None),
    )
    return jax.shard_map(
        per_device if mesh.shape["fsdp"] == 8 else plain_device,
        mesh=mesh,
        in_specs=placed,
        out_specs=(
            both, both, both_one, both, both_one, both, P(), both, P(), both, both_one,
            both, both, both,
        ),
        check_vma=False,
    )
```

```python
import jax
import jax.numpy as jnp
import numpy as np
from jax import lax
from jax.experimental import pallas as pl
from jax.experimental.pallas import tpu as pltpu
from jax.sharding import PartitionSpec as P

HEADS = 12
KV_HEADS = 2
HEAD_DIM = 128

MESH = pl.DeviceIdType.MESH

epsilon = 1e-06
rope_base = 1000000.0


def norm_piece(values, gain):
    return values * lax.rsqrt(jnp.mean(values * values, -1, keepdims=True) + epsilon) * gain


def rope_tables(position):
    half = HEAD_DIM // 2
    inverse = rope_base ** (-(jnp.arange(half, dtype=jnp.float32) * 2.0 / HEAD_DIM))
    angle = position.astype(jnp.float32)[:, None] * inverse[None, :]
    cosine = jnp.concatenate([jnp.cos(angle), jnp.cos(angle)], -1)
    sine = jnp.concatenate([jnp.sin(angle), jnp.sin(angle)], -1)
    return (cosine, sine)


def turn_half(values):
    half = values.shape[-1] // 2
    return jnp.concatenate([-values[..., half:], values[..., :half]], -1)


def rotate(values, cosine, sine):
    return values * cosine[:, None, :] + turn_half(values) * sine[:, None, :]


def rotate_back(grads, cosine, sine):
    return grads * cosine[:, None, :] - turn_half(grads * sine[:, None, :])


def segment_of(slots, starts):
    return (slots >= starts[1]).astype(jnp.int32) + (slots >= starts[2]).astype(jnp.int32)


def contract_rows(left, right):
    return lax.dot_general(
        left, right, (((0,), (0,)), ((), ())), preferred_element_type=jnp.float32
    )


def contract_columns(left, right):
    return lax.dot_general(
        left, right, (((1,), (1,)), ((), ())), preferred_element_type=jnp.float32
    )


def plain_device(
    tokens, cotangent, lengths, balance, norm1_gain, w_query, b_query, w_key, b_key,
    w_value, b_value, w_out, norm2_gain, w_gate, w_up, w_down,
):
    seq_count = lax.axis_size("seq")
    fsdp_count = lax.axis_size("fsdp")
    seq_rank = lax.axis_index("seq")
    rows_here, width = tokens.shape
    group = seq_count * rows_here
    kv_width = KV_HEADS * HEAD_DIM
    qkv_width = width + 2 * kv_width
    hidden_width = w_gate.shape[1]
    unit = hidden_width // (fsdp_count * seq_count)
    own_units = hidden_width // seq_count
    weight_rows = w_gate.shape[0]
    score_scale = HEAD_DIM ** (-0.5)
    repeat = HEADS // KV_HEADS

    slot = balance % group
    slots_all = lax.all_gather(slot, "seq", axis=0, tiled=True)
    seq_lengths = lengths[0]
    starts = jnp.cumsum(seq_lengths) - seq_lengths
    segment = segment_of(slot, starts)
    segments_all = segment_of(slots_all, starts)
    first_row = jnp.where(segment == 0, starts[0], jnp.where(segment == 1, starts[1], starts[2]))
    cosine, sine = rope_tables(slot - first_row)
    allowed = (segment[:, None] == segments_all[None, :]) & (slots_all[None, :] <= slot[:, None])

    small = jnp.concatenate([norm1_gain, norm2_gain, b_query, b_key, b_value], 0)[None]
    small = lax.all_gather(small, "fsdp", axis=0, tiled=True)
    piece = norm1_gain.shape[0]
    bias_piece = b_key.shape[0]
    gain_one = small[:, :piece].reshape(-1).astype(jnp.float32)
    gain_two = small[:, piece : 2 * piece].reshape(-1).astype(jnp.float32)
    bias_qkv = jnp.concatenate(
        [
            small[:, 2 * piece : 3 * piece].reshape(-1),
            small[:, 3 * piece : 3 * piece + bias_piece].reshape(-1),
            small[:, 3 * piece + bias_piece :].reshape(-1),
        ],
        0,
    ).astype(jnp.float32)
    weight_qkv = lax.all_gather(
        jnp.concatenate([w_query, w_key, w_value], 1), "fsdp", axis=0, tiled=True
    )
    weight_out = lax.all_gather(w_out, "fsdp", axis=0, tiled=True)
    upstream_all = lax.all_gather(cotangent, "seq", axis=0, tiled=True)

    def own_columns(weight):
        cut = weight.reshape(weight_rows, fsdp_count, seq_count, unit)
        return lax.dynamic_index_in_dim(cut, seq_rank, 2, False).reshape(weight_rows, own_units)

    weight_gu = lax.all_gather(
        jnp.concatenate([own_columns(w_gate), own_columns(w_up)], 1), "fsdp", axis=0, tiled=True
    )
    weight_down = lax.all_gather(
        lax.dynamic_slice_in_dim(w_down, seq_rank * unit, unit, 0), "fsdp", axis=0, tiled=True
    )

    inputs = tokens.astype(jnp.float32)
    normed_one = norm_piece(inputs, gain_one).astype(jnp.bfloat16)
    projected = jnp.dot(normed_one, weight_qkv, preferred_element_type=jnp.float32) + bias_qkv
    query_pre = projected[:, :width].reshape(rows_here, HEADS, HEAD_DIM)
    key_pre = projected[:, width : width + kv_width].reshape(rows_here, KV_HEADS, HEAD_DIM)
    value_pre = projected[:, width + kv_width :]
    queries = rotate(query_pre, cosine, sine).astype(jnp.bfloat16)
    keys = rotate(key_pre, cosine, sine).astype(jnp.bfloat16).reshape(rows_here, kv_width)
    values = value_pre.astype(jnp.bfloat16)
    paired = lax.all_gather(jnp.concatenate([keys, values], 1), "seq", axis=0, tiled=True)
    keys_all = paired[:, :kv_width].reshape(group, KV_HEADS, HEAD_DIM)
    values_all = paired[:, kv_width:].reshape(group, KV_HEADS, HEAD_DIM)
    grouped = queries.reshape(rows_here, KV_HEADS, repeat, HEAD_DIM)
    raw = (
        jnp.einsum("qgrd,kgd->grqk", grouped, keys_all, preferred_element_type=jnp.float32)
        * score_scale
    )
    scores = jnp.where(allowed, raw, -jnp.inf)
    expo = jnp.exp(scores - jnp.max(scores, -1, keepdims=True))
    probs = expo / jnp.sum(expo, -1, keepdims=True)
    probs_low = probs.astype(jnp.bfloat16)
    attended = jnp.einsum(
        "grqk,kgd->qgrd", probs_low, values_all, preferred_element_type=jnp.float32
    )
    attended = attended.astype(jnp.bfloat16).reshape(rows_here, width)
    resid = inputs + jnp.dot(attended, weight_out, preferred_element_type=jnp.float32)
    normed_two = norm_piece(resid, gain_two).astype(jnp.bfloat16)

    normed_all = lax.all_gather(normed_two, "seq", axis=0, tiled=True)
    both = jnp.dot(normed_all, weight_gu, preferred_element_type=jnp.float32)
    gate = both[:, :own_units]
    up = both[:, own_units:]
    sigma = jax.nn.sigmoid(gate)
    activated = gate * sigma
    hidden = (activated * up).astype(jnp.bfloat16)
    d_hidden = contract_columns(upstream_all, weight_down)
    d_gate = (d_hidden * up * sigma * (1.0 + gate * (1.0 - sigma))).astype(jnp.bfloat16)
    d_up = (d_hidden * activated).astype(jnp.bfloat16)
    d_both = jnp.concatenate([d_gate, d_up], 1)
    columns = lax.psum_scatter(
        contract_columns(d_both, weight_gu).astype(jnp.bfloat16),
        "seq", scatter_dimension=0, tiled=True,
    ).astype(jnp.float32)
    branch = lax.psum_scatter(
        jnp.dot(hidden, weight_down, preferred_element_type=jnp.float32).astype(jnp.bfloat16),
        "seq", scatter_dimension=0, tiled=True,
    ).astype(jnp.float32)
    layer_out = (resid + branch).astype(jnp.bfloat16)
    grad_down = lax.psum_scatter(
        contract_rows(hidden, upstream_all).astype(jnp.bfloat16),
        "fsdp", scatter_dimension=0, tiled=True,
    ).astype(jnp.float32)
    grad_pair = lax.psum_scatter(
        contract_rows(normed_all, d_both).astype(jnp.bfloat16),
        "fsdp", scatter_dimension=0, tiled=True,
    )
    grad_pair = lax.all_to_all(grad_pair, "seq", split_axis=0, concat_axis=0, tiled=True)
    grad_pair = grad_pair.reshape(seq_count, weight_rows // seq_count, 2, fsdp_count, unit)
    grad_pair = grad_pair.transpose(2, 1, 3, 0, 4).astype(jnp.float32)
    grad_pair = grad_pair.reshape(2, weight_rows // seq_count, hidden_width)

    _, pull_two = jax.vjp(norm_piece, resid, gain_two)
    d_resid_norm, grad_gain_two = pull_two(columns)
    d_resid = cotangent.astype(jnp.float32) + d_resid_norm
    d_branch = d_resid.astype(jnp.bfloat16)
    grad_out = contract_rows(attended, d_branch).astype(jnp.bfloat16)
    d_attended = contract_columns(d_branch, weight_out).astype(jnp.bfloat16)
    d_attended = d_attended.reshape(rows_here, KV_HEADS, repeat, HEAD_DIM)
    d_probs = jnp.einsum(
        "qgrd,kgd->grqk", d_attended, values_all, preferred_element_type=jnp.float32
    )
    delta = jnp.sum(probs * d_probs, -1, keepdims=True)
    d_score = (probs * (d_probs - delta)).astype(jnp.bfloat16)
    d_queries = (
        jnp.einsum("grqk,kgd->qgrd", d_score, keys_all, preferred_element_type=jnp.float32)
        * score_scale
    )
    d_keys = (
        jnp.einsum("grqk,qgrd->kgd", d_score, grouped, preferred_element_type=jnp.float32)
        * score_scale
    )
    d_values = jnp.einsum(
        "grqk,qgrd->kgd", probs_low, d_attended, preferred_element_type=jnp.float32
    )
    d_paired = jnp.concatenate([d_keys.reshape(group, kv_width), d_values.reshape(group, kv_width)], 1)
    d_paired = lax.psum_scatter(
        d_paired.astype(jnp.bfloat16), "seq", scatter_dimension=0, tiled=True
    ).astype(jnp.float32)
    d_query_pre = rotate_back(
        d_queries.reshape(rows_here, HEADS, HEAD_DIM), cosine, sine
    ).astype(jnp.bfloat16)
    d_key_pre = rotate_back(
        d_paired[:, :kv_width].reshape(rows_here, KV_HEADS, HEAD_DIM), cosine, sine
    ).astype(jnp.bfloat16)
    d_value_pre = d_paired[:, kv_width:].astype(jnp.bfloat16)
    d_qkv = jnp.concatenate(
        [
            d_query_pre.reshape(rows_here, width),
            d_key_pre.reshape(rows_here, kv_width),
            d_value_pre,
        ],
        1,
    )
    grad_qkv = contract_rows(normed_one, d_qkv).astype(jnp.bfloat16)
    grad_bias = jnp.sum(d_qkv.astype(jnp.float32), 0)
    d_normed_one = contract_columns(d_qkv, weight_qkv)
    _, pull_one = jax.vjp(norm_piece, inputs, gain_one)
    d_input_norm, grad_gain_one = pull_one(d_normed_one)
    input_grad = (d_resid + d_input_norm).astype(jnp.bfloat16)

    def summed(value):
        value = lax.psum_scatter(value, "fsdp", scatter_dimension=0, tiled=True)
        return lax.psum_scatter(value, "seq", scatter_dimension=0, tiled=True).astype(jnp.float32)

    grad_out = summed(grad_out)
    grad_qkv = summed(grad_qkv)
    vectors = lax.psum(
        jnp.concatenate([grad_gain_one, grad_gain_two, grad_bias], 0), ("fsdp", "seq")
    )
    own = width // (fsdp_count * seq_count)
    first = (lax.axis_index("fsdp") * seq_count + seq_rank) * own

    def own_part(offset):
        return lax.dynamic_slice_in_dim(vectors, offset + first, own, 0)

    biases = 2 * width
    return (
        layer_out,
        input_grad,
        own_part(0),
        grad_qkv[:, :width],
        own_part(biases),
        grad_qkv[:, width : width + kv_width],
        vectors[biases + width : biases + width + kv_width],
        grad_qkv[:, width + kv_width :],
        vectors[biases + width + kv_width :],
        grad_out,
        own_part(width),
        grad_pair[0],
        grad_pair[1],
        grad_down,
    )


ORDER = (1, 3, 2, 0)


class SumChain:
    def __init__(self, held, z_one, z_two, z_three, there, index):
        self.rank = lax.axis_index("seq")
        s = self.rank
        self.held, self.arrived = held, (z_one, z_two, z_three)
        self.up = [
            there(held(1), z_one, index, seq=s + 1),
            there(held(2), z_two.at[0], index + 2, seq=s + 1),
            there(held(3), z_three.at[0], index + 4, seq=s + 1),
        ]
        self.down = [
            there(held(3), z_one, index + 1, seq=s - 1),
            there(held(2), z_two.at[1], index + 3, seq=s - 1),
            there(held(1), z_three.at[1], index + 5, seq=s - 1),
        ]

    def add(self, j, arrived):
        ref = self.held(j)
        ref[...] = ref[...] + arrived[...]

    def one(self):
        pl.when(self.rank == 0)(self.up[0].start)
        pl.when(self.rank == 3)(self.down[0].start)

    def add_one(self):
        @pl.when(self.rank == 1)
        def _():
            self.up[0].wait_recv()
            self.add(2, self.arrived[0])

        @pl.when(self.rank == 2)
        def _():
            self.down[0].wait_recv()
            self.add(2, self.arrived[0])

    def two(self):
        pl.when(self.rank <= 1)(self.up[1].start)
        pl.when(self.rank >= 2)(self.down[1].start)

    def three(self):
        @pl.when((self.rank == 1) | (self.rank == 2))
        def _():
            self.up[1].wait_recv()
            self.add(3, self.arrived[1].at[0])
            self.down[1].wait_recv()
            self.add(1, self.arrived[1].at[1])

        pl.when(self.rank <= 2)(self.up[2].start)
        pl.when(self.rank >= 1)(self.down[2].start)

    def last(self, out):
        out[...] = self.held(0)[...].astype(jnp.float32)

        @pl.when(self.rank >= 1)
        def _():
            self.up[2].wait_recv()
            out[...] += self.arrived[2][0].astype(jnp.float32)

        @pl.when(self.rank <= 2)
        def _():
            self.down[2].wait_recv()
            out[...] += self.arrived[2][1].astype(jnp.float32)

    def one_sent(self):
        pl.when(self.rank == 0)(self.up[0].wait_send)
        pl.when(self.rank == 3)(self.down[0].wait_send)

    def sent(self):
        pl.when(self.rank <= 1)(self.up[1].wait_send)
        pl.when(self.rank >= 2)(self.down[1].wait_send)
        pl.when(self.rank <= 2)(self.up[2].wait_send)
        pl.when(self.rank >= 1)(self.down[2].wait_send)


class SumPlane:
    def __init__(self, buffer, block, plane, arrived, by_x, by_y, ended, there, index):
        half = buffer.shape[1] // 2
        low, high = pl.ds(0, half), pl.ds(half, half)

        def part(k):
            return buffer.at[pl.ds(pl.multiple_of(plane[k] * block, 16), block)]

        self.parts = own, to_x, to_y, to_both = [part(k) for k in (0, 2, 4, 6)]
        self.arrived, self.by_x, self.by_y, self.ended, self.half = arrived, by_x, by_y, ended, half
        self.core = [
            there(part(2 * i + 1), arrived.at[i], index + i, fsdp=plane[1]) for i in range(4)
        ]
        self.first = [
            there(to_both.at[:, low], by_x.at[1], index + 5, fsdp=plane[2]),
            there(to_both.at[:, high], by_y.at[1], index + 7, fsdp=plane[4]),
            there(to_x.at[:, low], by_x.at[0], index + 4, fsdp=plane[2]),
            there(to_y.at[:, high], by_y.at[0], index + 6, fsdp=plane[4]),
        ]
        self.second = [
            there(to_y.at[:, low], ended.at[0], index + 8, fsdp=plane[4]),
            there(to_x.at[:, high], ended.at[1], index + 9, fsdp=plane[2]),
        ]

    def start_core(self):
        for copy in self.core:
            copy.start()

    def start_first(self):
        for i in (3, 1, 2, 0):
            self.core[i].wait_recv()
            part = self.parts[i]
            part[...] = part[...] + self.arrived[i]
        for copy in self.first:
            copy.start()

    def start_second(self):
        half = self.half
        _, to_x, to_y, _ = self.parts
        self.first[0].wait_recv()
        to_y[:, :half] = to_y[:, :half] + self.by_x[1]
        self.second[0].start()
        self.first[1].wait_recv()
        to_x[:, half:] = to_x[:, half:] + self.by_y[1]
        self.second[1].start()

    def finish(self):
        half = self.half
        own = self.parts[0]
        self.first[2].wait_recv()
        self.second[0].wait_recv()
        total = own[:, :half].astype(jnp.float32) + self.by_x[0].astype(jnp.float32)
        own[:, :half] = (total + self.ended[0].astype(jnp.float32)).astype(jnp.bfloat16)
        self.first[3].wait_recv()
        self.second[1].wait_recv()
        total = own[:, half:].astype(jnp.float32) + self.by_y[0].astype(jnp.float32)
        own[:, half:] = (total + self.ended[1].astype(jnp.float32)).astype(jnp.bfloat16)

    def sent(self):
        for copy in self.core + self.first + self.second:
            copy.wait_send()


def in_order(partial, rows):
    def held(j):
        return partial.at[ORDER.index(j) * rows : (ORDER.index(j) + 1) * rows]

    return held


def front_kernel(
    lengths, tokens, cotangent, small, balance, inverse,
    w_query, w_key, w_value, w_out, w_gate, w_up, w_down,
    gu_all, down_all, upstream_all, normed_all, hidden, factor_gate, factor_up, qkv_out, out_out,
    queries, paired_out, slots_out, logsum, attended, resid, normed_one, gain_one, gain_two,
    slot_row, first_row, cosine, sine,
    q_w, kv_w, out_w, gate_v, up_v, gu, normed, kv, small_own, small_all, slots_all, bias,
    cotangent_v, down_raw, down_own, hidden_v, gate_part, up_part,
    local, ssem, rsem, zsend, zrecv,
):
    f = lax.axis_index("fsdp")
    s = lax.axis_index("seq")
    rows, width = tokens.shape
    n_f, n_s = 8, slots_all.shape[0]
    group = n_s * rows
    block = w_query.shape[0]
    unit_pad = down_own.shape[0]
    unit = w_gate.shape[1] // (n_f * n_s)
    units = n_f * unit_pad
    kv_width = KV_HEADS * HEAD_DIM
    qkv_width = width + 2 * kv_width
    scale = HEAD_DIM ** (-0.5)
    repeat = HEADS // KV_HEADS
    plane = [f ^ k for k in range(n_f)]

    entry = pltpu.get_barrier_semaphore()
    for k in range(1, n_f):
        pl.semaphore_signal(entry, inc=1, device_id={"fsdp": plane[k]}, device_id_type=MESH)
    for j in range(1, n_s):
        pl.semaphore_signal(
            entry, inc=1, device_id={"seq": lax.rem(s + j, n_s)}, device_id_type=MESH
        )

    def here(source, target, index):
        return pltpu.make_async_copy(source, target, local.at[index])

    def there(source, target, index, **device):
        return pltpu.make_async_remote_copy(
            src_ref=source, dst_ref=target, send_sem=ssem.at[index], recv_sem=rsem.at[index],
            device_id=device, device_id_type=MESH,
        )

    def own_rows(ref, owner, size, start=0, count=None):
        first = pl.multiple_of(owner * size + start, 16)
        return ref.at[pl.ds(first, size if count is None else count)]

    class Gather:
        def __init__(self, source, target, size, index):
            half = size // 2
            x, y, c = plane[2], plane[4], plane[1]
            self.own = here(source, own_rows(target, f, size), index // 8) if source is not None else None
            if source is None:
                source = own_rows(target, f, size)
            mine = own_rows(target, f, size)
            self.first = [
                there(source, mine, index, fsdp=x),
                there(source, mine, index + 1, fsdp=y),
                there(source, mine, index + 2, fsdp=c),
            ]
            from_x, from_y = own_rows(target, x, size), own_rows(target, y, size)
            part_x = own_rows(target, x, size, 0, half)
            part_y = own_rows(target, y, size, half, half)
            self.second = [
                there(part_x, part_x, index + 3, fsdp=y),
                there(part_y, part_y, index + 4, fsdp=x),
                there(from_x, from_x, index + 5, fsdp=c),
                there(from_y, from_y, index + 6, fsdp=c),
            ]
            diagonal = own_rows(target, plane[6], size)
            self.third = there(diagonal, diagonal, index + 7, fsdp=c)

        def start(self):
            if self.own is not None:
                self.own.start()
            for copy in self.first:
                copy.start()

        def forward(self):
            self.first[0].wait_recv()
            self.second[0].start()
            self.second[2].start()
            self.first[1].wait_recv()
            self.second[1].start()
            self.second[3].start()

        def last(self):
            self.second[0].wait_recv()
            self.second[1].wait_recv()
            self.third.start()

        def finish(self):
            if self.own is not None:
                self.own.wait()
            self.first[2].wait_recv()
            self.second[2].wait_recv()
            self.second[3].wait_recv()
            self.third.wait_recv()

        def sent(self):
            for copy in self.first + self.second + [self.third]:
                copy.wait_send()

    class Chain:
        def __init__(self, target, index, own=None):
            self.steps = []
            for step in range(1, n_s):
                up = own_rows(target, s - (step - 1), rows)
                down = own_rows(target, s + (step - 1), rows)
                source = own if own is not None and step == 1 else up
                i = index + 2 * (step - 1)
                self.steps.append((
                    pltpu.make_async_remote_copy(
                        src_ref=source, dst_ref=up, send_sem=zsend.at[i], recv_sem=zrecv.at[i],
                        device_id={"seq": s + 1}, device_id_type=MESH,
                    ),
                    pltpu.make_async_remote_copy(
                        src_ref=down if source is up else source, dst_ref=down, send_sem=zsend.at[i + 1], recv_sem=zrecv.at[i + 1],
                        device_id={"seq": s - 1}, device_id_type=MESH,
                    ),
                    (s >= step - 1) & (s < n_s - 1),
                    (s >= 1) & (s <= n_s - step),
                    s >= step,
                    s <= n_s - 1 - step,
                ))

        def send(self, step):
            up, down, can_up, can_down, _, _ = self.steps[step - 1]
            pl.when(can_up)(up.start)
            pl.when(can_down)(down.start)

        def receive(self, step):
            up, down, _, _, from_below, from_above = self.steps[step - 1]
            pl.when(from_below)(up.wait_recv)
            pl.when(from_above)(down.wait_recv)

        def sent(self):
            for up, down, can_up, can_down, _, _ in self.steps:
                pl.when(can_up)(up.wait_send)
                pl.when(can_down)(down.wait_send)

    own_block = pl.ds(pl.multiple_of(f * block, 16), block)
    pieces = [
        here(w_key, kv_w.at[own_block, pl.ds(0, kv_width)], 6),
        here(w_value, kv_w.at[own_block, pl.ds(kv_width, kv_width)], 7),
        here(w_query, q_w.at[own_block], 5),
        here(cotangent, cotangent_v, 8),
    ]
    load_gate = here(w_gate, gate_v, 9)
    load_up = here(w_up, up_v, 10)
    first_unit = pl.multiple_of(s * unit // 16 * 16, 16)
    load_down = here(w_down.at[pl.ds(first_unit, unit_pad)], down_raw, 15)
    for copy in pieces:
        copy.start()
    load_gate.start()
    load_up.start()
    load_down.start()

    slot = (balance[...] & (group - 1)).astype(jnp.float32)
    second = lengths[0, 0].astype(jnp.float32)
    third = (lengths[0, 0] + lengths[0, 1]).astype(jnp.float32)
    first = jnp.where(slot >= third, third, jnp.where(slot >= second, second, 0.0))
    slot_row[...] = jnp.broadcast_to(slot, slot_row.shape)
    first_row[...] = jnp.broadcast_to(first, first_row.shape)
    slots_all[s] = jnp.broadcast_to(slot, (128, rows)).T
    lanes = lax.broadcasted_iota(jnp.int32, small.shape, 1)
    sorts = lax.broadcasted_iota(jnp.int32, small.shape, 0)
    small_own[...] = jnp.where(
        sorts < 3,
        pltpu.roll(small[...], lax.rem(f, 2) * block, 1),
        pltpu.roll(small[...], f * (kv_width // n_f), 1),
    )
    small_all[f] = small_own[...]

    gather_kv = Gather(None, kv_w, block, 0)
    gather_q = Gather(None, q_w, block, 8)
    gather_out = Gather(w_out, out_w, block, 16)
    gather_gu = Gather(None, gu, block, 24)
    gather_down = Gather(down_own, down_all, unit_pad, 32)
    chain_up = Chain(upstream_all, 0, cotangent_v)
    chain_normed = Chain(normed, 6)
    send_small = [
        there(small_own, small_all.at[f], 40 + k, fsdp=plane[k]) for k in range(1, n_f)
    ]
    send_slots = [
        there(slots_all.at[s], slots_all.at[s], 48 + j, seq=lax.rem(s + j, n_s))
        for j in range(1, n_s)
    ]
    send_kv = [
        there(kv.at[s], kv.at[s], 52 + j, seq=lax.rem(s + j, n_s)) for j in range(1, n_s)
    ]
    for copy in pieces[:2]:
        copy.wait()
    pl.semaphore_wait(entry, n_f - 1 + n_s - 1)
    gather_kv.start()
    for copy in send_small + send_slots:
        copy.start()
    for copy in pieces[2:]:
        copy.wait()
    chain_up.send(1)
    save_own = here(cotangent_v, own_rows(upstream_all, s, rows), 8)
    save_own.start()
    position = slots_all[s] - jnp.broadcast_to(first, (128, rows)).T
    angle = position * inverse[...]
    cosine[...] = jnp.cos(angle)
    sine[...] = jnp.where(
        lax.broadcasted_iota(jnp.int32, angle.shape, 1) < HEAD_DIM // 2, -1.0, 1.0
    ) * jnp.sin(angle)

    for copy in send_small + send_slots:
        copy.wait_recv()

    def joined(sort):
        return jnp.concatenate(
            [
                small_all[2 * i, sort : sort + 1] + small_all[2 * i + 1, sort : sort + 1]
                for i in range(n_f // 2)
            ],
            1,
        )

    gain_one[...] = joined(0)
    gain_two[...] = joined(1)
    bias_query = joined(2)
    bias_key = sum(small_all[i, 3:4, :kv_width] for i in range(n_f))
    bias_value = sum(small_all[i, 4:5, :kv_width] for i in range(n_f))

    inputs = tokens[...].astype(jnp.float32)
    root = lax.rsqrt(jnp.mean(inputs * inputs, -1, keepdims=True) + epsilon)
    normed_one[...] = (inputs * root * gain_one[...]).astype(jnp.bfloat16)
    gather_kv.forward()
    gather_q.start()
    gather_kv.last()
    gather_kv.finish()

    def turned(value):
        return value * cosine[...] + pltpu.roll(value, HEAD_DIM // 2, 1) * sine[...]

    rows_low = normed_one[...]
    pair = jnp.dot(rows_low, kv_w[:, :kv_width], preferred_element_type=jnp.float32)
    pair = pair + bias_key
    for g in range(KV_HEADS):
        columns = slice(g * HEAD_DIM, (g + 1) * HEAD_DIM)
        kv[s, :, columns] = turned(pair[:, columns]).astype(jnp.bfloat16)
    pair = jnp.dot(rows_low, kv_w[:, kv_width:], preferred_element_type=jnp.float32)
    kv[s, :, kv_width:] = (pair + bias_value).astype(jnp.bfloat16)
    for copy in send_kv:
        copy.start()
    save_kv_w = here(kv_w, qkv_out.at[:, pl.ds(width, 2 * kv_width)], 11)
    save_kv_w.start()

    load_gate.wait()
    load_up.wait()
    pick_units(gate_v, up_v, gu.at[own_block], w_gate.shape[1] // n_f, unit, unit_pad)
    gather_q.forward()
    gather_out.start()
    load_down.wait()
    raw = down_raw[...].astype(jnp.float32)
    shifted = jnp.concatenate([raw[8:], jnp.zeros((8, width), jnp.float32)], 0)
    raw = jnp.where(lax.rem(s * unit, 16) == 0, raw, shifted)
    inside = lax.broadcasted_iota(jnp.int32, raw.shape, 0) < unit
    down_own[...] = jnp.where(inside, raw, 0.0).astype(jnp.bfloat16)

    for j in range(n_s):
        keys_slot = slots_all[j]
        keys_slot = jnp.concatenate([keys_slot] * (rows // 128), 1)
        ok = (keys_slot <= slot) & (keys_slot >= first)
        bias[j * rows : (j + 1) * rows] = jnp.where(ok, 0.0, -1e30)

    gather_q.last()
    gather_q.finish()
    save_q_w = here(q_w, qkv_out.at[:, pl.ds(0, width)], 0)
    save_q_w.start()
    for g in range(HEADS // 2):
        columns = slice(g * 2 * HEAD_DIM, (g + 1) * 2 * HEAD_DIM)
        pair = jnp.dot(rows_low, q_w[:, columns], preferred_element_type=jnp.float32)
        pair = pair + bias_query[:, columns]
        for h in range(2):
            part = turned(pair[:, h * HEAD_DIM : (h + 1) * HEAD_DIM]).astype(jnp.bfloat16)
            queries[:, (2 * g + h) * HEAD_DIM : (2 * g + h + 1) * HEAD_DIM] = part

    gather_out.forward()
    chain_up.receive(1)
    for copy in send_kv:
        copy.wait_recv()
    chain_up.send(2)
    save_kv = here(kv, paired_out, 12)
    save_kv.start()
    slots_out[...] = slots_all[...]

    for g in range(KV_HEADS):
        keys = kv[:, :, g * HEAD_DIM : (g + 1) * HEAD_DIM].reshape(n_s * rows, HEAD_DIM)
        values = kv[:, :, kv_width + g * HEAD_DIM : kv_width + (g + 1) * HEAD_DIM]
        values = values.reshape(n_s * rows, HEAD_DIM)

        def head(i, carry, g=g, keys=keys, values=values):
            h = g * repeat + i
            columns = pl.ds(pl.multiple_of(h * HEAD_DIM, HEAD_DIM), HEAD_DIM)
            raw = lax.dot_general(
                keys, queries[:, columns], (((1,), (1,)), ((), ())),
                preferred_element_type=jnp.float32,
            )
            scores = raw * scale + bias[...]
            top = jnp.max(scores, 0, keepdims=True)
            expo = jnp.exp(scores - top)
            total = jnp.sum(expo, 0, keepdims=True)
            probs = (expo * (1.0 / total)).astype(jnp.bfloat16)
            mixed = lax.dot_general(
                values, probs, (((0,), (0,)), ((), ())), preferred_element_type=jnp.float32
            )
            attended[:, columns] = mixed.T.astype(jnp.bfloat16)
            logsum[pl.ds(pl.multiple_of(h * 8, 8), 8)] = jnp.broadcast_to(
                top + jnp.log(total), (8, rows)
            )
            return carry

        lax.fori_loop(0, repeat, head, 0)
        if g == 0:
            gather_out.last()
            gather_gu.start()

    gather_out.finish()
    save_out = here(out_w, out_out, 13)
    save_out.start()
    mixed = attended[...]
    for g in range(width // 256):
        columns = slice(g * 256, (g + 1) * 256)
        part = jnp.dot(mixed, out_w[:, columns], preferred_element_type=jnp.float32)
        resid[:, columns] = tokens[:, columns].astype(jnp.float32) + part
    value = resid[...]
    root = lax.rsqrt(jnp.mean(value * value, -1, keepdims=True) + epsilon)
    own_tokens = pl.ds(pl.multiple_of(s * rows, rows), rows)
    normed[own_tokens] = (value * root * gain_two[...]).astype(jnp.bfloat16)
    chain_normed.send(1)

    wide = hidden_v.shape[2]
    count = units // wide

    def saves(owner, t, slot):
        place = (
            pl.ds(pl.multiple_of(owner * rows, rows), rows),
            pl.ds(pl.multiple_of(t * wide, wide), wide),
        )
        return [
            here(part.at[slot], whole.at[place], 16 + 3 * slot + i)
            for i, (part, whole) in enumerate(
                ((hidden_v, hidden), (gate_part, factor_gate), (up_part, factor_up))
            )
        ]

    def feed(owner, done):
        def body(t, carry):
            slot = lax.rem(t + done, 2)
            mine = normed[pl.ds(pl.multiple_of(owner * rows, rows), rows)]
            gate_columns = pl.ds(pl.multiple_of(t * wide, wide), wide)
            up_columns = pl.ds(pl.multiple_of(units + t * wide, wide), wide)
            gate = jnp.dot(mine, gu[:, gate_columns], preferred_element_type=jnp.float32)
            up = jnp.dot(mine, gu[:, up_columns], preferred_element_type=jnp.float32)
            sigma = jax.nn.sigmoid(gate)
            activated = gate * sigma

            @pl.when(t + done >= 2)
            def _():
                for copy in saves(owner, t, slot):
                    copy.wait()

            hidden_v[slot] = (activated * up).astype(jnp.bfloat16)
            gate_part[slot] = (up * sigma * (1.0 + gate * (1.0 - sigma))).astype(jnp.bfloat16)
            up_part[slot] = activated.astype(jnp.bfloat16)
            for copy in saves(owner, t, slot):
                copy.start()
            return carry

        lax.fori_loop(0, count, body, 0)

    chain_up.receive(2)
    chain_normed.receive(1)
    chain_normed.send(2)
    gather_gu.forward()
    chain_normed.receive(2)
    chain_normed.send(3)
    gather_gu.last()
    gather_down.start()
    gather_gu.finish()
    save_gu = here(gu, gu_all, 22)
    save_gu.start()
    chain_normed.receive(3)
    chain_up.send(3)
    save_normed = here(normed, normed_all, 23)
    save_normed.start()
    feed(s, 0)
    feed(s ^ 1, count)
    feed(s ^ 2, 2 * count)
    gather_down.forward()
    feed(s ^ 3, 3 * count)
    gather_down.last()
    for t in (count - 2, count - 1):
        for copy in saves(s ^ 3, t, (t + 3 * count) % 2):
            copy.wait()
    chain_up.receive(3)
    gather_down.finish()
    for copy in (save_own, save_kv_w, save_q_w, save_kv, save_out, save_gu, save_normed):
        copy.wait()
    for part in (gather_kv, gather_q, gather_out, gather_gu, gather_down, chain_up, chain_normed):
        part.sent()
    for copy in send_small + send_slots + send_kv:
        copy.wait_send()


def pick_units(gate, up, out, stride, unit, padded):
    rank = lax.axis_index("seq")
    pieces = gate.shape[1] // stride
    half = out.shape[1] // 2
    window, tile = 512, 128
    rows = lax.broadcasted_iota(jnp.int32, (window, tile), 0)
    columns = lax.broadcasted_iota(jnp.int32, (window, tile), 1)
    for first in range(0, 2 * half, tile):
        source = gate if first < half else up
        local = first % half
        total = jnp.zeros((out.shape[0], tile), jnp.float32)
        for f in range(pieces):
            low = max(local, f * padded)
            high = min(local + tile, f * padded + unit)
            if low >= high:
                continue
            begin = f * stride + rank * unit
            base = jnp.minimum(begin // 128, (source.shape[1] - window) // 128) * 128
            base = pl.multiple_of(base, 128)
            wanted = columns + (local - f * padded + begin - base)
            inside = (columns >= low - local) & (columns < high - local)
            chosen = jnp.where((rows == wanted) & inside, 1.0, 0.0).astype(jnp.bfloat16)
            total += jnp.dot(
                source[:, pl.ds(base, window)], chosen, preferred_element_type=jnp.float32
            )
        out[:, first : first + tile] = total.astype(jnp.bfloat16)


def front(tokens, cotangent, lengths, balance, vectors, weights):
    rows, width = tokens.shape
    n_s = lax.axis_size("seq")
    w_query, w_key, w_value, w_out, w_gate, w_up, w_down = weights
    block = w_query.shape[0]
    unit_pad = -(-w_down.shape[0] // n_s // 16) * 16
    kv_width = KV_HEADS * HEAD_DIM
    qkv_width = width + 2 * kv_width
    units = 8 * unit_pad
    group = n_s * rows
    wide = 768
    low, full = jnp.bfloat16, jnp.float32
    small = sum(
        jnp.pad(v.astype(full)[None], ((i, 7 - i), (0, 2 * block - v.shape[0])))
        for i, v in enumerate(vectors)
    )
    half = HEAD_DIM // 2
    inverse = rope_base ** (-(np.arange(half, dtype=np.float32) * np.float32(2.0 / HEAD_DIM)))
    inverse = jnp.asarray(np.concatenate([inverse, inverse])[None], full)
    smem = pl.BlockSpec(memory_space=pltpu.SMEM)
    vmem = pl.BlockSpec(memory_space=pltpu.VMEM)
    hbm = pl.BlockSpec(memory_space=pl.ANY)
    shape = jax.ShapeDtypeStruct
    return pl.pallas_call(
        front_kernel,
        in_specs=[smem, vmem, hbm, vmem, vmem, vmem] + [hbm] * 7,
        out_specs=[hbm] * 9 + [vmem, hbm] + [vmem] * 11,
        out_shape=[
            shape((width, 2 * units), low),
            shape((units, width), low),
            shape((group, width), low),
            shape((group, width), low),
            shape((group, units), low),
            shape((group, units), low),
            shape((group, units), low),
            shape((width, qkv_width), low),
            shape((width, width), low),
            shape((rows, width), low),
            shape((n_s, rows, 2 * kv_width), low),
            shape((n_s, rows, 128), full),
            shape((8 * HEADS, rows), full),
            shape((rows, width), low),
            shape((rows, width), full),
            shape((rows, width), low),
            shape((1, width), full),
            shape((1, width), full),
            shape((8, rows), full),
            shape((8, rows), full),
            shape((rows, HEAD_DIM), full),
            shape((rows, HEAD_DIM), full),
        ],
        scratch_shapes=[
            pltpu.VMEM((width, width), low),
            pltpu.VMEM((width, 2 * kv_width), low),
            pltpu.VMEM((width, width), low),
            pltpu.VMEM(w_gate.shape, low),
            pltpu.VMEM(w_up.shape, low),
            pltpu.VMEM((width, 2 * units), low),
            pltpu.VMEM((group, width), low),
            pltpu.VMEM((n_s, rows, 2 * kv_width), low),
            pltpu.VMEM((8, 2 * block), full),
            pltpu.VMEM((8, 8, 2 * block), full),
            pltpu.VMEM((n_s, rows, 128), full),
            pltpu.VMEM((group, rows), full),
            pltpu.VMEM((rows, width), low),
            pltpu.VMEM((unit_pad, width), low),
            pltpu.VMEM((unit_pad, width), low),
            pltpu.VMEM((2, rows, wide), low),
            pltpu.VMEM((2, rows, wide), low),
            pltpu.VMEM((2, rows, wide), low),
            pltpu.SemaphoreType.DMA((24,)),
            pltpu.SemaphoreType.DMA((56,)),
            pltpu.SemaphoreType.DMA((56,)),
            pltpu.SemaphoreType.DMA((12,)),
            pltpu.SemaphoreType.DMA((12,)),
        ],
        compiler_params=pltpu.CompilerParams(
            collective_id=0, has_side_effects=True, vmem_limit_bytes=62 * 2**20
        ),
        name="front",
    )(
        lengths, tokens, cotangent, small, balance.reshape(1, rows), inverse,
        w_query, w_key, w_value, w_out, w_gate, w_up, w_down,
    )


def ffn_kernel(
    normed_all, upstream_all, w_gu, w_down, hidden_all, factor_gate, factor_up,
    columns, grad_down, gu_sum, branch, down_arrived, gu_arrived,
    normed, upstream, gu, down, hidden, d_both, partial, z_one, z_two, z_three,
    down_x, down_y, down_last, down_piece,
    load, ssem, rsem,
):
    f = lax.axis_index("fsdp")
    s = lax.axis_index("seq")
    n_s = len(ORDER)
    group, width = normed.shape
    rows = group // n_s
    half_rows = group // 2
    units = down.shape[0]
    tile = 256
    tiles = units // tile
    wide = 768
    block = gu.shape[0] // 8
    unit = units // 8
    half = width // 2
    plane = [f ^ k for k in range(8)]
    full = jnp.float32

    entry = pltpu.get_barrier_semaphore()
    for k in (1, 2, 4):
        pl.semaphore_signal(entry, inc=1, device_id={"fsdp": plane[k]}, device_id_type=MESH)
    for j in (1, n_s - 1):
        pl.semaphore_signal(
            entry, inc=1, device_id={"seq": lax.rem(s + j, n_s)}, device_id_type=MESH
        )

    def here(source, target, index):
        return pltpu.make_async_copy(source, target, load.at[index])

    def there(source, target, index, **device):
        return pltpu.make_async_remote_copy(
            src_ref=source, dst_ref=target, send_sem=ssem.at[index], recv_sem=rsem.at[index],
            device_id=device, device_id_type=MESH,
        )

    def part(ref, owner, size):
        return ref.at[pl.ds(pl.multiple_of(owner * size, 16), size)]

    early, late = range(0, n_s // 2), range(n_s // 2, n_s)

    def rows_of(p):
        return pl.ds(p * rows, rows)

    def row_loads(p):
        owner = lax.rem(s + n_s - ORDER[p], n_s)
        mine = rows_of(p)
        return [
            here(part(upstream_all, owner, rows), upstream.at[mine], 5 * p),
            here(part(factor_gate, owner, rows), d_both.at[mine, pl.ds(0, units)], 5 * p + 1),
            here(part(factor_up, owner, rows), d_both.at[mine, pl.ds(units, units)], 5 * p + 2),
            here(part(hidden_all, owner, rows), hidden.at[mine], 5 * p + 3),
            here(part(normed_all, owner, rows), normed.at[mine], 5 * p + 4),
        ]

    def down_load(t):
        mine = pl.ds(pl.multiple_of(t * wide, wide), wide)
        return here(w_down.at[mine], down.at[mine], 20 + t)

    def gu_load(n):
        mine = pl.ds(pl.multiple_of(n * 512, 512), 512)
        return here(w_gu.at[mine], gu.at[mine], 23 + n)

    loads = [row_loads(p) for p in range(n_s)]
    order = [loads[0][0], loads[1][0], down_load(0)]
    order += [loads[p][i] for i in (1, 2) for p in early]
    order += [down_load(t) for t in range(1, units // wide)]
    order += [gu_load(n) for n in range(width // 512)]
    order += [loads[p][i] for i in (0, 1, 2) for p in late]
    order += [loads[p][i] for i in (3, 4) for p in range(n_s)]
    for copy in order:
        copy.start()

    def forward(blocks, wait):
        for p in blocks:
            for copy in loads[p][:3]:
                copy.wait()
        mine = pl.ds(blocks[0] * rows, len(blocks) * rows)

        def body(t, carry):
            if wait:
                down_load(t).wait()
            gate_columns = pl.ds(pl.multiple_of(t * wide, wide), wide)
            up_columns = pl.ds(pl.multiple_of(units + t * wide, wide), wide)
            d_hidden = lax.dot_general(
                upstream[mine], down[gate_columns], (((1,), (1,)), ((), ())),
                preferred_element_type=full,
            )
            value = d_hidden * d_both[mine, gate_columns].astype(full)
            d_both[mine, gate_columns] = value.astype(jnp.bfloat16)
            value = d_hidden * d_both[mine, up_columns].astype(full)
            d_both[mine, up_columns] = value.astype(jnp.bfloat16)
            return carry

        lax.fori_loop(0, units // wide, body, 0)

    def backward(blocks, wait):
        part_rows = pl.ds(blocks[0] * rows, len(blocks) * rows)

        def body(n, carry):
            if wait:
                gu_load(n).wait()
            out_columns = pl.ds(pl.multiple_of(n * 512, 512), 512)
            value = lax.dot_general(
                d_both[part_rows], gu[out_columns], (((1,), (1,)), ((), ())),
                preferred_element_type=full,
            )
            partial[part_rows, out_columns] = value.astype(jnp.bfloat16)
            return carry

        lax.fori_loop(0, width // 512, body, 0)

    chain = SumChain(in_order(partial, rows), z_one, z_two, z_three, there, 0)
    pieces = [(first, min(group, units - first)) for first in range(0, units, group)]
    forward(early, True)
    backward(early, True)
    pl.semaphore_wait(entry, 5)
    chain.one()
    forward(late, False)
    backward(late, False)
    chain.add_one()
    chain.two()

    for p in range(n_s):
        loads[p][3].wait()
        loads[p][4].wait()

    def down_body(t, carry):
        unit_rows = pl.ds(pl.multiple_of(t * tile, tile), tile)
        value = lax.dot_general(
            hidden[:, unit_rows], upstream[...], (((0,), (0,)), ((), ())),
            preferred_element_type=full,
        )
        down[unit_rows] = value.astype(jnp.bfloat16)
        return carry

    lax.fori_loop(0, tiles, down_body, 0)
    down_core = [
        there(part(down, plane[2 * i + 1], unit), down_arrived.at[i], 6 + i, fsdp=plane[1])
        for i in range(4)
    ]
    for i in (3, 1, 2, 0):
        down_core[i].start()

    def gu_body(m, carry):
        in_columns = pl.ds(pl.multiple_of(m * tile, tile), tile)
        turned = normed[:, in_columns].T
        for first in range(0, 2 * units, units // 3):
            value = jnp.dot(turned, d_both[:, first : first + units // 3], preferred_element_type=full)
            gu[in_columns, first : first + units // 3] = value.astype(jnp.bfloat16)
        return carry

    lax.fori_loop(0, 2, gu_body, 0)

    class Arrivals:
        def __init__(self, ref, size, arrived, copies, turns, index):
            self.ref, self.size, self.copies = ref, size, copies
            self.pieces = {}
            for n, i in enumerate((3, 1, 2, 0)):
                self.pieces[i] = [
                    (here(arrived.at[i, :, columns], piece, index + 3 * (n % 2) + k), columns, piece)
                    for k, (columns, piece) in enumerate(turns[n % 2])
                ]

        def fetch(self, i):
            self.copies[i].wait_recv()
            for copy, _, _ in self.pieces[i]:
                copy.start()

        def add(self, i):
            target = part(self.ref, plane[2 * i], self.size)
            for copy, columns, piece in self.pieces[i]:
                copy.wait()
                target[:, columns] = target[:, columns] + piece[...]

    down_turns = [[(pl.ds(0, width), piece)] for piece in (down_piece.at[0], down_piece.at[1])]
    down_sum = Arrivals(down, unit, down_arrived, down_core, down_turns, 26)
    down_sum.fetch(3)
    for i, following in ((3, 1), (1, 2), (2, 0), (0, None)):
        if following is not None:
            down_sum.fetch(following)
        down_sum.add(i)
    to_x, to_y, to_both = [part(down, plane[k], unit) for k in (2, 4, 6)]
    low_half, high_half = pl.ds(0, half), pl.ds(half, half)
    down_first = [
        there(to_x.at[:, low_half], down_x.at[0], 10, fsdp=plane[2]),
        there(to_both.at[:, low_half], down_x.at[1], 11, fsdp=plane[2]),
        there(to_y.at[:, high_half], down_y.at[0], 12, fsdp=plane[4]),
        there(to_both.at[:, high_half], down_y.at[1], 13, fsdp=plane[4]),
    ]
    for copy in down_first:
        copy.start()
    chain.three()
    lax.fori_loop(2, width // tile, gu_body, 0)
    gu_core = [
        there(part(gu, plane[2 * i + 1], block), gu_arrived.at[i], 16 + i, fsdp=plane[1])
        for i in range(4)
    ]
    for i in (3, 1, 2, 0):
        gu_core[i].start()

    again = [
        here(
            w_down.at[first : first + count],
            d_both.at[:count, i * width : (i + 1) * width], 36 + i,
        )
        for i, (first, count) in enumerate(pieces)
    ]
    for copy in again:
        copy.start()
    for copy in again:
        copy.wait()

    def branch_body(n, carry):
        out_columns = pl.ds(pl.multiple_of(n * wide, wide), wide)
        for m in range(2):
            mine = slice(m * half_rows, (m + 1) * half_rows)
            value = jnp.zeros((half_rows, wide), full)
            for i, (first, count) in enumerate(pieces):
                columns_here = pl.ds(pl.multiple_of(i * width + n * wide, wide), wide)
                value += jnp.dot(
                    hidden[mine, first : first + count], d_both[:count, columns_here],
                    preferred_element_type=full,
                )
            upstream[mine, out_columns] = value.astype(jnp.bfloat16)
        return carry

    lax.fori_loop(0, width // wide, branch_body, 0)
    chain.last(columns)
    chain_branch = SumChain(in_order(upstream, rows), z_one, z_two, z_three, there, 22)
    chain_branch.one()
    down_second = [
        there(to_y.at[:, low_half], down_last.at[0], 14, fsdp=plane[4]),
        there(to_x.at[:, high_half], down_last.at[1], 15, fsdp=plane[2]),
    ]
    down_first[1].wait_recv()
    to_y[:, :half] = to_y[:, :half] + down_x[1]
    down_second[0].start()
    down_first[3].wait_recv()
    to_x[:, half:] = to_x[:, half:] + down_y[1]
    down_second[1].start()
    gu_turns = [
        [(pl.ds(k * units, units), hidden.at[(2 * n + k) * block : (2 * n + k + 1) * block]) for k in range(2)]
        for n in range(2)
    ]
    gu_arrivals = Arrivals(gu, block, gu_arrived, gu_core, gu_turns, 26)
    store = [here(part(gu, plane[2 * i], block), gu_sum.at[i], 32 + i) for i in range(4)]
    gu_arrivals.fetch(3)
    for i, following in ((3, 1), (1, 2), (2, 0), (0, None)):
        if following is not None:
            gu_arrivals.fetch(following)
        gu_arrivals.add(i)
        store[i].start()
    down_first[0].wait_recv()
    down_first[2].wait_recv()
    own = part(down, f, unit)
    down_second[0].wait_recv()
    grad_down[:, :half] = (
        own[:, :half].astype(full) + down_x[0].astype(full) + down_last[0].astype(full)
    )
    down_second[1].wait_recv()
    grad_down[:, half:] = (
        own[:, half:].astype(full) + down_y[0].astype(full) + down_last[1].astype(full)
    )
    chain_branch.add_one()
    chain_branch.one_sent()
    store_branch = here(upstream, branch, 39)
    store_branch.start()
    chain.one_sent()
    chain.sent()
    for copy in down_core + down_first + down_second + gu_core:
        copy.wait_send()
    for copy in store + [store_branch]:
        copy.wait()


def ffn(normed_all, upstream_all, w_gu, w_down, hidden, factor_gate, factor_up):
    group, width = normed_all.shape
    units = w_down.shape[0]
    rows = group // len(ORDER)
    unit, block, half = units // 8, width // 8, width // 2
    low, full = jnp.bfloat16, jnp.float32
    vmem = pl.BlockSpec(memory_space=pltpu.VMEM)
    hbm = pl.BlockSpec(memory_space=pl.ANY)
    shape = jax.ShapeDtypeStruct
    return pl.pallas_call(
        ffn_kernel,
        in_specs=[hbm] * 7,
        out_specs=[vmem] * 2 + [hbm] * 4,
        out_shape=[
            shape((rows, width), full),
            shape((unit, width), full),
            shape((4, block, 2 * units), low),
            shape((group, width), low),
            shape((4, unit, width), low),
            shape((4, block, 2 * units), low),
        ],
        scratch_shapes=[
            pltpu.VMEM((group, width), low),
            pltpu.VMEM((group, width), low),
            pltpu.VMEM((width, 2 * units), low),
            pltpu.VMEM((units, width), low),
            pltpu.VMEM((group, units), low),
            pltpu.VMEM((group, 2 * units), low),
            pltpu.VMEM((group, width), low),
            pltpu.VMEM((rows, width), low),
            pltpu.VMEM((2, rows, width), low),
            pltpu.VMEM((2, rows, width), low),
            pltpu.VMEM((2, unit, half), low),
            pltpu.VMEM((2, unit, half), low),
            pltpu.VMEM((2, unit, half), low),
            pltpu.VMEM((2, unit, width), low),
            pltpu.SemaphoreType.DMA((40,)),
            pltpu.SemaphoreType.DMA((28,)),
            pltpu.SemaphoreType.DMA((28,)),
        ],
        compiler_params=pltpu.CompilerParams(
            collective_id=1, has_side_effects=True, vmem_limit_bytes=63 * 2**20
        ),
        name="ffn",
    )(normed_all, upstream_all, w_gu, w_down, hidden, factor_gate, factor_up)[:4]


def back_kernel(
    columns, resid, gain_two, cotangent, attended, queries, paired, slots, slot_row, first_row,
    logsum, normed_one, tokens, gain_one, cosine, sine, w_out, w_qkv, gu_sum, branch,
    layer, input_rows, vector, grad_out, grad_qkv, gu_rows,
    out_w, qkv, gu_own, gu_to_y, gu_to_x, gu_x, gu_y, gu_ended,
    branch_v, z_one, z_two, z_three, working, bias, d_branch, d_attended, d_qkv, d_resid,
    keys_grad, values_grad, dkv, dkv_in,
    out_arrived, out_x, out_y, out_ended, qkv_arrived, qkv_x, qkv_y, qkv_ended,
    out_one, out_two, out_three, qkv_one, qkv_two, qkv_three, vector_in,
    load, ssem, rsem,
):
    f = lax.axis_index("fsdp")
    s = lax.axis_index("seq")
    rows, width = tokens.shape
    n_s = paired.shape[0]
    kv_width = KV_HEADS * HEAD_DIM
    repeat = HEADS // KV_HEADS
    scale = HEAD_DIM ** (-0.5)
    block = width // 8
    piece = block // n_s
    units = gu_sum.shape[2] // 2
    tile = 256
    full, low = jnp.float32, jnp.bfloat16
    plane = [f ^ k for k in range(8)]

    entry = pltpu.get_barrier_semaphore()
    for k in (1, 2, 4):
        pl.semaphore_signal(entry, inc=1, device_id={"fsdp": plane[k]}, device_id_type=MESH)
    for j in range(1, n_s):
        pl.semaphore_signal(
            entry, inc=1, device_id={"seq": lax.rem(s + j, n_s)}, device_id_type=MESH
        )

    def here(source, target, index):
        return pltpu.make_async_copy(source, target, load.at[index])

    def there(source, target, index, **device):
        return pltpu.make_async_remote_copy(
            src_ref=source, dst_ref=target, send_sem=ssem.at[index], recv_sem=rsem.at[index],
            device_id=device, device_id_type=MESH,
        )

    low_units, high_units = pl.ds(0, units), pl.ds(units, units)
    load_branch = here(branch, branch_v, 0)
    load_out = here(w_out, out_w, 1)
    load_gu = [
        here(gu_sum.at[0], gu_own, 2),
        here(gu_sum.at[2, :, low_units], gu_to_y, 3),
        here(gu_sum.at[1, :, high_units], gu_to_x, 4),
    ]
    load_qkv = here(w_qkv, qkv, 5)
    load_columns = here(columns, working, 7)
    for copy in [load_columns, load_branch, load_out] + load_gu + [load_qkv]:
        copy.start()

    gu_first = [
        there(gu_sum.at[3, :, low_units], gu_x.at[1], 0, fsdp=plane[2]),
        there(gu_sum.at[3, :, high_units], gu_y.at[1], 1, fsdp=plane[4]),
        there(gu_sum.at[1, :, low_units], gu_x.at[0], 2, fsdp=plane[2]),
        there(gu_sum.at[2, :, high_units], gu_y.at[0], 3, fsdp=plane[4]),
    ]
    gu_second = [
        there(gu_to_y, gu_ended.at[0], 4, fsdp=plane[4]),
        there(gu_to_x, gu_ended.at[1], 5, fsdp=plane[2]),
    ]

    def around(j):
        return {"seq": lax.rem(s + j, n_s)}

    def rows_for(ref, first, j):
        owner = lax.rem(s + j, n_s)
        return ref.at[pl.ds(pl.multiple_of(first + owner * piece, 16), piece)]

    gu_send = [there(rows_for(gu_own, 0, j), gu_rows.at[j], 5 + j, **around(j)) for j in range(1, n_s)]
    dkv_send = [
        [
            there(dkv.at[g, lax.rem(s + j, n_s)], dkv_in.at[g, j], 8 + 3 * g + j, **around(j))
            for j in range(1, n_s)
        ]
        for g in range(KV_HEADS)
    ]
    chain = SumChain(in_order(branch_v, rows), z_one, z_two, z_three, there, 16)
    sum_out = SumPlane(out_w, block, plane, out_arrived, out_x, out_y, out_ended, there, 24)
    sum_qkv = SumPlane(qkv, block, plane, qkv_arrived, qkv_x, qkv_y, qkv_ended, there, 36)

    def own_part(ref):
        return lambda j: rows_for(ref, f * block, n_s - j)

    chain_out = SumChain(own_part(out_w), out_one, out_two, out_three, there, 48)
    chain_qkv = SumChain(own_part(qkv), qkv_one, qkv_two, qkv_three, there, 54)
    vector_send = [
        there(vector_in.at[0], vector_in.at[1], 60, fsdp=plane[1]),
        there(vector_in.at[2], vector_in.at[3], 61, fsdp=plane[2]),
        there(vector_in.at[4], vector_in.at[5], 62, fsdp=plane[4]),
    ] + [there(vector_in.at[6], vector_in.at[6 + j], 62 + j, **around(j)) for j in range(1, n_s)]

    pl.semaphore_wait(entry, 3 + n_s - 1)
    for copy in gu_first:
        copy.start()
    load_branch.wait()
    chain.two()

    def norm_back(value, gain, grad):
        root = lax.rsqrt(jnp.mean(value * value, -1, keepdims=True) + epsilon)
        scaled = gain * grad
        inner = jnp.mean(scaled * value, -1, keepdims=True)
        gain_grad = jnp.sum(grad * (value * root), 0, keepdims=True)
        return root * scaled - value * (root * root * root * inner), gain_grad

    load_columns.wait()
    d_norm, gain_two_grad = norm_back(resid[...], gain_two[...], working[...])
    d_total = cotangent[...].astype(full) + d_norm
    d_branch[...] = d_total.astype(low)
    d_resid[...] = d_total
    for j in range(n_s):
        keys_slot = slots[j]
        keys_slot = jnp.concatenate([keys_slot] * (rows // 128), 1)
        ok = (keys_slot <= slot_row[0:1]) & (keys_slot >= first_row[0:1])
        bias[j * rows : (j + 1) * rows] = jnp.where(ok, 0.0, -1e30)
    load_out.wait()
    for n in range(width // tile):
        value = lax.dot_general(
            d_branch[...], out_w[n * tile : (n + 1) * tile], (((1,), (1,)), ((), ())),
            preferred_element_type=full,
        )
        d_attended[:, n * tile : (n + 1) * tile] = value.astype(low)

    def turned_back(value):
        return value * cosine[...] + pltpu.roll(value * sine[...], HEAD_DIM // 2, 1)

    for g in range(KV_HEADS):
        keys = paired[:, :, g * HEAD_DIM : (g + 1) * HEAD_DIM].reshape(n_s * rows, HEAD_DIM)
        values = paired[:, :, kv_width + g * HEAD_DIM : kv_width + (g + 1) * HEAD_DIM]
        values = values.reshape(n_s * rows, HEAD_DIM)
        keys_grad[...] = jnp.zeros_like(keys_grad)
        values_grad[...] = jnp.zeros_like(values_grad)

        def head(i, carry, g=g, keys=keys, values=values):
            h = g * repeat + i
            head_columns = pl.ds(pl.multiple_of(h * HEAD_DIM, HEAD_DIM), HEAD_DIM)
            query = queries[:, head_columns]
            grad = d_attended[:, head_columns]
            raw = lax.dot_general(
                keys, query, (((1,), (1,)), ((), ())), preferred_element_type=full
            )
            logs = logsum[pl.ds(pl.multiple_of(h * 8, 8), 8)][0:1]
            probs = jnp.exp(raw * scale + bias[...] - logs)
            d_probs = lax.dot_general(
                values, grad, (((1,), (1,)), ((), ())), preferred_element_type=full
            )
            delta = jnp.sum(probs * d_probs, 0, keepdims=True)
            d_score = (probs * (d_probs - delta)).astype(low)
            turned = lax.dot_general(
                keys, d_score, (((0,), (0,)), ((), ())), preferred_element_type=full
            )
            d_qkv[:, head_columns] = turned_back((turned * scale).T).astype(low)
            keys_grad[...] += jnp.dot(d_score, query, preferred_element_type=full) * scale
            values_grad[...] += jnp.dot(probs.astype(low), grad, preferred_element_type=full)
            return carry

        lax.fori_loop(0, repeat, head, 0)
        dkv[g, :, :, :HEAD_DIM] = keys_grad[...].astype(low).reshape(n_s, rows, HEAD_DIM)
        dkv[g, :, :, HEAD_DIM:] = values_grad[...].astype(low).reshape(n_s, rows, HEAD_DIM)
        for copy in dkv_send[g]:
            copy.start()

    turned = attended[...].T
    for n in range(width // tile):
        n_columns = slice(n * tile, (n + 1) * tile)
        value = jnp.dot(turned, d_branch[:, n_columns], preferred_element_type=full)
        out_w[:, n_columns] = value.astype(low)
    sum_out.start_core()
    load_qkv.wait()

    def back_one(first, count, start):
        for n in range(width // tile):
            n_rows = slice(n * tile, (n + 1) * tile)
            value = lax.dot_general(
                d_qkv[:, first : first + count], qkv[n_rows, first : first + count],
                (((1,), (1,)), ((), ())), preferred_element_type=full,
            )
            working[:, n_rows] = value if start else working[:, n_rows] + value

    back_one(0, width, True)
    normed_turned = normed_one[...].T
    for n in range(width // tile):
        n_columns = slice(n * tile, (n + 1) * tile)
        value = jnp.dot(normed_turned, d_qkv[:, n_columns], preferred_element_type=full)
        qkv[:, n_columns] = value.astype(low)
    for copy in load_gu:
        copy.wait()
    gu_first[0].wait_recv()
    gu_to_y[...] = gu_to_y[...] + gu_x[1]
    gu_second[0].start()
    gu_first[1].wait_recv()
    gu_to_x[...] = gu_to_x[...] + gu_y[1]
    gu_second[1].start()
    sum_out.start_first()

    for g in range(KV_HEADS):
        for copy in dkv_send[g]:
            copy.wait_recv()
        total = dkv[g, s].astype(full)
        for j in range(1, n_s):
            total = total + dkv_in[g, j].astype(full)
        key_columns = slice(width + g * HEAD_DIM, width + (g + 1) * HEAD_DIM)
        value_columns = slice(width + kv_width + g * HEAD_DIM, width + kv_width + (g + 1) * HEAD_DIM)
        d_qkv[:, key_columns] = turned_back(total[:, :HEAD_DIM]).astype(low)
        d_qkv[:, value_columns] = total[:, HEAD_DIM:].astype(low)
    back_one(width, 2 * kv_width, False)
    value = jnp.dot(normed_turned, d_qkv[:, width:], preferred_element_type=full)
    qkv[:, width:] = value.astype(low)
    sum_qkv.start_core()
    chain.three()

    d_norm, gain_one_grad = norm_back(tokens[...].astype(full), gain_one[...], working[...])
    input_rows[...] = (d_resid[...] + d_norm).astype(low)
    bias_grad = jnp.sum(d_qkv[...].astype(full), 0, keepdims=True)
    vectors = jnp.concatenate([gain_one_grad, gain_two_grad, bias_grad], 1)
    part = vectors.shape[1] // 8
    for r in range(8):
        vector_in[0, r : r + 1] = vectors[:, r * part : (r + 1) * part]
    vector_send[0].start()
    sum_qkv.start_first()
    vector_send[0].wait_recv()
    vector_in[2] = vector_in[0] + vector_in[1]
    vector_send[1].start()

    gu_first[2].wait_recv()
    gu_second[0].wait_recv()
    total = gu_own[:, :units].astype(full) + gu_x[0].astype(full) + gu_ended[0].astype(full)
    gu_own[:, :units] = total.astype(low)
    gu_first[3].wait_recv()
    gu_second[1].wait_recv()
    total = gu_own[:, units:].astype(full) + gu_y[0].astype(full) + gu_ended[1].astype(full)
    gu_own[:, units:] = total.astype(low)
    for copy in gu_send:
        copy.start()
    keep_rows = here(rows_for(gu_own, 0, 0), gu_rows.at[0], 6)
    keep_rows.start()
    sum_out.start_second()
    vector_send[1].wait_recv()
    vector_in[4] = vector_in[2] + vector_in[3]
    vector_send[2].start()

    sum_qkv.start_second()
    sum_out.finish()
    chain_out.one()
    vector_send[2].wait_recv()
    vector_in[6] = vector_in[4] + vector_in[5]
    for copy in vector_send[3:]:
        copy.start()
    chain_out.add_one()
    chain_out.two()
    sum_qkv.finish()
    chain_qkv.one()
    chain_out.three()
    chain.last(working)
    layer[...] = (resid[...] + working[...]).astype(low)
    chain_qkv.add_one()
    chain_qkv.two()
    for copy in vector_send[3:]:
        copy.wait_recv()
    vector[...] = vector_in[6] + vector_in[7] + vector_in[8] + vector_in[9]
    chain_out.last(grad_out)
    chain_qkv.three()
    chain_qkv.last(grad_qkv)
    for copy in gu_send:
        copy.wait_recv()
    keep_rows.wait()
    for part in (chain_out, chain_qkv):
        part.one_sent()
        part.sent()
    chain.sent()
    sum_out.sent()
    sum_qkv.sent()
    for copy in gu_first + gu_second + gu_send + vector_send:
        copy.wait_send()
    for g in range(KV_HEADS):
        for copy in dkv_send[g]:
            copy.wait_send()


def back(
    columns, resid, gain_two, cotangent, attended, queries, paired, slots, slot_row, first_row,
    logsum, normed_one, tokens, gain_one, cosine, sine, w_out, w_qkv, gu_sum, branch,
):
    rows, width = tokens.shape
    n_s = paired.shape[0]
    group = n_s * rows
    kv_width = KV_HEADS * HEAD_DIM
    qkv_width = width + 2 * kv_width
    block = width // 8
    piece = block // n_s
    units = gu_sum.shape[2] // 2
    low, full = jnp.bfloat16, jnp.float32
    vmem = pl.BlockSpec(memory_space=pltpu.VMEM)
    hbm = pl.BlockSpec(memory_space=pl.ANY)
    shape = jax.ShapeDtypeStruct
    vectors = (2 * width + qkv_width) // 8
    return pl.pallas_call(
        back_kernel,
        in_specs=[hbm] + [vmem] * 15 + [hbm] * 4,
        out_specs=[vmem] * 5 + [hbm],
        out_shape=[
            shape((rows, width), low),
            shape((rows, width), low),
            shape((8, vectors), full),
            shape((piece, width), full),
            shape((piece, qkv_width), full),
            shape((n_s, piece, 2 * units), low),
        ],
        scratch_shapes=[
            pltpu.VMEM((width, width), low),
            pltpu.VMEM((width, qkv_width), low),
            pltpu.VMEM((block, 2 * units), low),
            pltpu.VMEM((block, units), low),
            pltpu.VMEM((block, units), low),
            pltpu.VMEM((2, block, units), low),
            pltpu.VMEM((2, block, units), low),
            pltpu.VMEM((2, block, units), low),
            pltpu.VMEM((group, width), low),
            pltpu.VMEM((rows, width), low),
            pltpu.VMEM((2, rows, width), low),
            pltpu.VMEM((2, rows, width), low),
            pltpu.VMEM((rows, width), full),
            pltpu.VMEM((group, rows), full),
            pltpu.VMEM((rows, width), low),
            pltpu.VMEM((rows, width), low),
            pltpu.VMEM((rows, qkv_width), low),
            pltpu.VMEM((rows, width), full),
            pltpu.VMEM((group, HEAD_DIM), full),
            pltpu.VMEM((group, HEAD_DIM), full),
            pltpu.VMEM((KV_HEADS, n_s, rows, 2 * HEAD_DIM), low),
            pltpu.VMEM((KV_HEADS, n_s, rows, 2 * HEAD_DIM), low),
            pltpu.VMEM((4, block, width), low),
            pltpu.VMEM((2, block, width // 2), low),
            pltpu.VMEM((2, block, width // 2), low),
            pltpu.VMEM((2, block, width // 2), low),
            pltpu.VMEM((4, block, qkv_width), low),
            pltpu.VMEM((2, block, qkv_width // 2), low),
            pltpu.VMEM((2, block, qkv_width // 2), low),
            pltpu.VMEM((2, block, qkv_width // 2), low),
            pltpu.VMEM((piece, width), low),
            pltpu.VMEM((2, piece, width), low),
            pltpu.VMEM((2, piece, width), low),
            pltpu.VMEM((piece, qkv_width), low),
            pltpu.VMEM((2, piece, qkv_width), low),
            pltpu.VMEM((2, piece, qkv_width), low),
            pltpu.VMEM((10, 8, vectors), full),
            pltpu.SemaphoreType.DMA((10,)),
            pltpu.SemaphoreType.DMA((68,)),
            pltpu.SemaphoreType.DMA((68,)),
        ],
        compiler_params=pltpu.CompilerParams(
            collective_id=2, has_side_effects=True, vmem_limit_bytes=63 * 2**20
        ),
        name="back",
    )(
        columns, resid, gain_two, cotangent, attended, queries, paired, slots, slot_row, first_row,
        logsum, normed_one, tokens, gain_one, cosine, sine, w_out, w_qkv, gu_sum, branch,
    )


def finish_kernel(
    layer, input_rows, grad_out, grad_qkv, grad_down, gu_rows,
    layer_out, input_grad, out_out, query_out, key_out, value_out, down_out, gate_out, up_out,
):
    s = lax.axis_index("seq")
    n_s = gu_rows.shape[0]
    width = grad_out.shape[1]
    kv_width = KV_HEADS * HEAD_DIM
    unit_pad = grad_down.shape[0]
    unit = down_out.shape[0]
    units = gu_rows.shape[2] // 2
    layer_out[...] = layer[...]
    input_grad[...] = input_rows[...]
    out_out[...] = grad_out[...]
    query_out[...] = grad_qkv[:, :width]
    key_out[...] = grad_qkv[:, width : width + kv_width]
    value_out[...] = grad_qkv[:, width + kv_width :]
    down_out[...] = grad_down[:unit]
    window = 512
    lanes = lax.broadcasted_iota(jnp.int32, (gu_rows.shape[1], 128), 1)
    for base, out in ((0, gate_out), (units, up_out)):
        for f in range(units // unit_pad):
            for owner in range(n_s):
                source = base + f * unit_pad
                begin = min(source // 128 * 128, 2 * units - window)
                target = (f * n_s + owner) * unit
                first = target // 128 * 128
                slot = lax.rem(s + n_s - owner, n_s)
                value = gu_rows[slot, :, begin : begin + window].astype(jnp.float32)
                turn = ((target - first) - (source - begin)) % window
                if turn:
                    value = pltpu.roll(value, turn, 1)
                for t in range(first, min(target + unit, out.shape[1]), 128):
                    part = value[:, t - first : t - first + 128]
                    if t < target:
                        part = jnp.where(lanes >= target - t, part, out[:, t : t + 128])
                    out[:, t : t + 128] = part


def finish(layer, input_rows, grad_out, grad_qkv, grad_down, gu_rows, unit, hidden_width):
    piece, width = grad_out.shape
    kv_width = KV_HEADS * HEAD_DIM
    low, full = jnp.bfloat16, jnp.float32
    shape = jax.ShapeDtypeStruct
    vmem = pl.BlockSpec(memory_space=pltpu.VMEM)
    return pl.pallas_call(
        finish_kernel,
        in_specs=[vmem] * 6,
        out_specs=[vmem] * 9,
        out_shape=[
            shape(layer.shape, low),
            shape(layer.shape, low),
            shape((piece, width), full),
            shape((piece, width), full),
            shape((piece, kv_width), full),
            shape((piece, kv_width), full),
            shape((unit, width), full),
            shape((piece, hidden_width), full),
            shape((piece, hidden_width), full),
        ],
        compiler_params=pltpu.CompilerParams(vmem_limit_bytes=63 * 2**20),
        name="finish",
    )(layer, input_rows, grad_out, grad_qkv, grad_down, gu_rows)


def per_device(
    tokens, cotangent, lengths, balance, norm1_gain, w_query, b_query, w_key, b_key,
    w_value, b_value, w_out, norm2_gain, w_gate, w_up, w_down,
):
    seq_count = lax.axis_size("seq")
    fsdp_count = lax.axis_size("fsdp")
    seq_rank = lax.axis_index("seq")
    fsdp_rank = lax.axis_index("fsdp")
    rows_here, width = tokens.shape
    kv_width = KV_HEADS * HEAD_DIM
    hidden_width = w_gate.shape[1]
    unit = hidden_width // (fsdp_count * seq_count)
    (
        weight_gu, weight_down, upstream_all, normed_all, hidden, factor_gate, factor_up,
        weight_qkv, weight_out, queries, paired, slots, logsum, attended, resid, normed_one,
        gain_one, gain_two, slot_row, first_row, cosine, sine,
    ) = front(
        tokens, cotangent, lengths, balance, (norm1_gain, norm2_gain, b_query, b_key, b_value),
        (w_query, w_key, w_value, w_out, w_gate, w_up, w_down),
    )
    columns, grad_down, gu_sum, branch = ffn(
        normed_all, upstream_all, weight_gu, weight_down, hidden, factor_gate, factor_up
    )
    layer, input_rows, vectors, grad_out, grad_qkv, gu_rows = back(
        columns, resid, gain_two, cotangent, attended, queries, paired, slots, slot_row, first_row,
        logsum, normed_one, tokens, gain_one, cosine, sine, weight_out, weight_qkv, gu_sum, branch,
    )
    (
        layer_out, input_grad, grad_out, grad_query, grad_key, grad_value, grad_down, grad_gate,
        grad_up,
    ) = finish(layer, input_rows, grad_out, grad_qkv, grad_down, gu_rows, unit, hidden_width)
    vectors = vectors.reshape(-1)
    own = width // (fsdp_count * seq_count)
    first = (fsdp_rank * seq_count + seq_rank) * own

    def own_part(offset):
        return lax.dynamic_slice_in_dim(vectors, offset + first, own, 0)

    biases = 2 * width
    return (
        layer_out,
        input_grad,
        own_part(0),
        grad_query,
        own_part(biases),
        grad_key,
        vectors[biases + width : biases + width + kv_width],
        grad_value,
        vectors[biases + width + kv_width :],
        grad_out,
        own_part(width),
        grad_gate,
        grad_up,
        grad_down,
    )


def solution(mesh):
    both = P(("fsdp", "seq"), None)
    both_one = P(("fsdp", "seq"))
    placed = (
        both, both, P("fsdp", None), both_one, P("fsdp"), P("fsdp", None), P("fsdp"),
        P("fsdp", None), P("fsdp"), P("fsdp", None), P("fsdp"), P("fsdp", None), P("fsdp"),
        P("fsdp", None), P("fsdp", None), P("fsdp", None),
    )
    return jax.shard_map(
        per_device if mesh.shape["fsdp"] == 8 else plain_device,
        mesh=mesh,
        in_specs=placed,
        out_specs=(
            both, both, both_one, both, both_one, both, P(), both, P(), both, both_one,
            both, both, both,
        ),
        check_vma=False,
    )
```

```python
import jax
import jax.numpy as jnp
import numpy as np
from jax import lax
from jax.experimental import pallas as pl
from jax.experimental.pallas import tpu as pltpu
from jax.sharding import PartitionSpec as P

HEADS = 12
KV_HEADS = 2
HEAD_DIM = 128

MESH = pl.DeviceIdType.MESH

epsilon = 1e-06
rope_base = 1000000.0


def norm_piece(values, gain):
    return values * lax.rsqrt(jnp.mean(values * values, -1, keepdims=True) + epsilon) * gain


def rope_tables(position):
    half = HEAD_DIM // 2
    inverse = rope_base ** (-(jnp.arange(half, dtype=jnp.float32) * 2.0 / HEAD_DIM))
    angle = position.astype(jnp.float32)[:, None] * inverse[None, :]
    cosine = jnp.concatenate([jnp.cos(angle), jnp.cos(angle)], -1)
    sine = jnp.concatenate([jnp.sin(angle), jnp.sin(angle)], -1)
    return (cosine, sine)


def turn_half(values):
    half = values.shape[-1] // 2
    return jnp.concatenate([-values[..., half:], values[..., :half]], -1)


def rotate(values, cosine, sine):
    return values * cosine[:, None, :] + turn_half(values) * sine[:, None, :]


def rotate_back(grads, cosine, sine):
    return grads * cosine[:, None, :] - turn_half(grads * sine[:, None, :])


def segment_of(slots, starts):
    return (slots >= starts[1]).astype(jnp.int32) + (slots >= starts[2]).astype(jnp.int32)


def contract_rows(left, right):
    return lax.dot_general(
        left, right, (((0,), (0,)), ((), ())), preferred_element_type=jnp.float32
    )


def contract_columns(left, right):
    return lax.dot_general(
        left, right, (((1,), (1,)), ((), ())), preferred_element_type=jnp.float32
    )


def plain_device(
    tokens, cotangent, lengths, balance, norm1_gain, w_query, b_query, w_key, b_key,
    w_value, b_value, w_out, norm2_gain, w_gate, w_up, w_down,
):
    seq_count = lax.axis_size("seq")
    fsdp_count = lax.axis_size("fsdp")
    seq_rank = lax.axis_index("seq")
    rows_here, width = tokens.shape
    group = seq_count * rows_here
    kv_width = KV_HEADS * HEAD_DIM
    qkv_width = width + 2 * kv_width
    hidden_width = w_gate.shape[1]
    unit = hidden_width // (fsdp_count * seq_count)
    own_units = hidden_width // seq_count
    weight_rows = w_gate.shape[0]
    score_scale = HEAD_DIM ** (-0.5)
    repeat = HEADS // KV_HEADS

    slot = balance % group
    slots_all = lax.all_gather(slot, "seq", axis=0, tiled=True)
    seq_lengths = lengths[0]
    starts = jnp.cumsum(seq_lengths) - seq_lengths
    segment = segment_of(slot, starts)
    segments_all = segment_of(slots_all, starts)
    first_row = jnp.where(segment == 0, starts[0], jnp.where(segment == 1, starts[1], starts[2]))
    cosine, sine = rope_tables(slot - first_row)
    allowed = (segment[:, None] == segments_all[None, :]) & (slots_all[None, :] <= slot[:, None])

    small = jnp.concatenate([norm1_gain, norm2_gain, b_query, b_key, b_value], 0)[None]
    small = lax.all_gather(small, "fsdp", axis=0, tiled=True)
    piece = norm1_gain.shape[0]
    bias_piece = b_key.shape[0]
    gain_one = small[:, :piece].reshape(-1).astype(jnp.float32)
    gain_two = small[:, piece : 2 * piece].reshape(-1).astype(jnp.float32)
    bias_qkv = jnp.concatenate(
        [
            small[:, 2 * piece : 3 * piece].reshape(-1),
            small[:, 3 * piece : 3 * piece + bias_piece].reshape(-1),
            small[:, 3 * piece + bias_piece :].reshape(-1),
        ],
        0,
    ).astype(jnp.float32)
    weight_qkv = lax.all_gather(
        jnp.concatenate([w_query, w_key, w_value], 1), "fsdp", axis=0, tiled=True
    )
    weight_out = lax.all_gather(w_out, "fsdp", axis=0, tiled=True)
    upstream_all = lax.all_gather(cotangent, "seq", axis=0, tiled=True)

    def own_columns(weight):
        cut = weight.reshape(weight_rows, fsdp_count, seq_count, unit)
        return lax.dynamic_index_in_dim(cut, seq_rank, 2, False).reshape(weight_rows, own_units)

    weight_gu = lax.all_gather(
        jnp.concatenate([own_columns(w_gate), own_columns(w_up)], 1), "fsdp", axis=0, tiled=True
    )
    weight_down = lax.all_gather(
        lax.dynamic_slice_in_dim(w_down, seq_rank * unit, unit, 0), "fsdp", axis=0, tiled=True
    )

    inputs = tokens.astype(jnp.float32)
    normed_one = norm_piece(inputs, gain_one).astype(jnp.bfloat16)
    projected = jnp.dot(normed_one, weight_qkv, preferred_element_type=jnp.float32) + bias_qkv
    query_pre = projected[:, :width].reshape(rows_here, HEADS, HEAD_DIM)
    key_pre = projected[:, width : width + kv_width].reshape(rows_here, KV_HEADS, HEAD_DIM)
    value_pre = projected[:, width + kv_width :]
    queries = rotate(query_pre, cosine, sine).astype(jnp.bfloat16)
    keys = rotate(key_pre, cosine, sine).astype(jnp.bfloat16).reshape(rows_here, kv_width)
    values = value_pre.astype(jnp.bfloat16)
    paired = lax.all_gather(jnp.concatenate([keys, values], 1), "seq", axis=0, tiled=True)
    keys_all = paired[:, :kv_width].reshape(group, KV_HEADS, HEAD_DIM)
    values_all = paired[:, kv_width:].reshape(group, KV_HEADS, HEAD_DIM)
    grouped = queries.reshape(rows_here, KV_HEADS, repeat, HEAD_DIM)
    raw = (
        jnp.einsum("qgrd,kgd->grqk", grouped, keys_all, preferred_element_type=jnp.float32)
        * score_scale
    )
    scores = jnp.where(allowed, raw, -jnp.inf)
    expo = jnp.exp(scores - jnp.max(scores, -1, keepdims=True))
    probs = expo / jnp.sum(expo, -1, keepdims=True)
    probs_low = probs.astype(jnp.bfloat16)
    attended = jnp.einsum(
        "grqk,kgd->qgrd", probs_low, values_all, preferred_element_type=jnp.float32
    )
    attended = attended.astype(jnp.bfloat16).reshape(rows_here, width)
    resid = inputs + jnp.dot(attended, weight_out, preferred_element_type=jnp.float32)
    normed_two = norm_piece(resid, gain_two).astype(jnp.bfloat16)

    normed_all = lax.all_gather(normed_two, "seq", axis=0, tiled=True)
    both = jnp.dot(normed_all, weight_gu, preferred_element_type=jnp.float32)
    gate = both[:, :own_units]
    up = both[:, own_units:]
    sigma = jax.nn.sigmoid(gate)
    activated = gate * sigma
    hidden = (activated * up).astype(jnp.bfloat16)
    d_hidden = contract_columns(upstream_all, weight_down)
    d_gate = (d_hidden * up * sigma * (1.0 + gate * (1.0 - sigma))).astype(jnp.bfloat16)
    d_up = (d_hidden * activated).astype(jnp.bfloat16)
    d_both = jnp.concatenate([d_gate, d_up], 1)
    columns = lax.psum_scatter(
        contract_columns(d_both, weight_gu).astype(jnp.bfloat16),
        "seq", scatter_dimension=0, tiled=True,
    ).astype(jnp.float32)
    branch = lax.psum_scatter(
        jnp.dot(hidden, weight_down, preferred_element_type=jnp.float32).astype(jnp.bfloat16),
        "seq", scatter_dimension=0, tiled=True,
    ).astype(jnp.float32)
    layer_out = (resid + branch).astype(jnp.bfloat16)
    grad_down = lax.psum_scatter(
        contract_rows(hidden, upstream_all).astype(jnp.bfloat16),
        "fsdp", scatter_dimension=0, tiled=True,
    ).astype(jnp.float32)
    grad_pair = lax.psum_scatter(
        contract_rows(normed_all, d_both).astype(jnp.bfloat16),
        "fsdp", scatter_dimension=0, tiled=True,
    )
    grad_pair = lax.all_to_all(grad_pair, "seq", split_axis=0, concat_axis=0, tiled=True)
    grad_pair = grad_pair.reshape(seq_count, weight_rows // seq_count, 2, fsdp_count, unit)
    grad_pair = grad_pair.transpose(2, 1, 3, 0, 4).astype(jnp.float32)
    grad_pair = grad_pair.reshape(2, weight_rows // seq_count, hidden_width)

    _, pull_two = jax.vjp(norm_piece, resid, gain_two)
    d_resid_norm, grad_gain_two = pull_two(columns)
    d_resid = cotangent.astype(jnp.float32) + d_resid_norm
    d_branch = d_resid.astype(jnp.bfloat16)
    grad_out = contract_rows(attended, d_branch).astype(jnp.bfloat16)
    d_attended = contract_columns(d_branch, weight_out).astype(jnp.bfloat16)
    d_attended = d_attended.reshape(rows_here, KV_HEADS, repeat, HEAD_DIM)
    d_probs = jnp.einsum(
        "qgrd,kgd->grqk", d_attended, values_all, preferred_element_type=jnp.float32
    )
    delta = jnp.sum(probs * d_probs, -1, keepdims=True)
    d_score = (probs * (d_probs - delta)).astype(jnp.bfloat16)
    d_queries = (
        jnp.einsum("grqk,kgd->qgrd", d_score, keys_all, preferred_element_type=jnp.float32)
        * score_scale
    )
    d_keys = (
        jnp.einsum("grqk,qgrd->kgd", d_score, grouped, preferred_element_type=jnp.float32)
        * score_scale
    )
    d_values = jnp.einsum(
        "grqk,qgrd->kgd", probs_low, d_attended, preferred_element_type=jnp.float32
    )
    d_paired = jnp.concatenate([d_keys.reshape(group, kv_width), d_values.reshape(group, kv_width)], 1)
    d_paired = lax.psum_scatter(
        d_paired.astype(jnp.bfloat16), "seq", scatter_dimension=0, tiled=True
    ).astype(jnp.float32)
    d_query_pre = rotate_back(
        d_queries.reshape(rows_here, HEADS, HEAD_DIM), cosine, sine
    ).astype(jnp.bfloat16)
    d_key_pre = rotate_back(
        d_paired[:, :kv_width].reshape(rows_here, KV_HEADS, HEAD_DIM), cosine, sine
    ).astype(jnp.bfloat16)
    d_value_pre = d_paired[:, kv_width:].astype(jnp.bfloat16)
    d_qkv = jnp.concatenate(
        [
            d_query_pre.reshape(rows_here, width),
            d_key_pre.reshape(rows_here, kv_width),
            d_value_pre,
        ],
        1,
    )
    grad_qkv = contract_rows(normed_one, d_qkv).astype(jnp.bfloat16)
    grad_bias = jnp.sum(d_qkv.astype(jnp.float32), 0)
    d_normed_one = contract_columns(d_qkv, weight_qkv)
    _, pull_one = jax.vjp(norm_piece, inputs, gain_one)
    d_input_norm, grad_gain_one = pull_one(d_normed_one)
    input_grad = (d_resid + d_input_norm).astype(jnp.bfloat16)

    def summed(value):
        value = lax.psum_scatter(value, "fsdp", scatter_dimension=0, tiled=True)
        return lax.psum_scatter(value, "seq", scatter_dimension=0, tiled=True).astype(jnp.float32)

    grad_out = summed(grad_out)
    grad_qkv = summed(grad_qkv)
    vectors = lax.psum(
        jnp.concatenate([grad_gain_one, grad_gain_two, grad_bias], 0), ("fsdp", "seq")
    )
    own = width // (fsdp_count * seq_count)
    first = (lax.axis_index("fsdp") * seq_count + seq_rank) * own

    def own_part(offset):
        return lax.dynamic_slice_in_dim(vectors, offset + first, own, 0)

    biases = 2 * width
    return (
        layer_out,
        input_grad,
        own_part(0),
        grad_qkv[:, :width],
        own_part(biases),
        grad_qkv[:, width : width + kv_width],
        vectors[biases + width : biases + width + kv_width],
        grad_qkv[:, width + kv_width :],
        vectors[biases + width + kv_width :],
        grad_out,
        own_part(width),
        grad_pair[0],
        grad_pair[1],
        grad_down,
    )


ORDER = (1, 3, 2, 0)


class SumChain:
    def __init__(self, held, z_one, z_two, z_three, there, index):
        self.rank = lax.axis_index("seq")
        s = self.rank
        self.held, self.arrived = held, (z_one, z_two, z_three)
        self.up = [
            there(held(1), z_one, index, seq=s + 1),
            there(held(2), z_two.at[0], index + 2, seq=s + 1),
            there(held(3), z_three.at[0], index + 4, seq=s + 1),
        ]
        self.down = [
            there(held(3), z_one, index + 1, seq=s - 1),
            there(held(2), z_two.at[1], index + 3, seq=s - 1),
            there(held(1), z_three.at[1], index + 5, seq=s - 1),
        ]

    def add(self, j, arrived):
        ref = self.held(j)
        ref[...] = ref[...] + arrived[...]

    def one(self):
        pl.when(self.rank == 0)(self.up[0].start)
        pl.when(self.rank == 3)(self.down[0].start)

    def add_one(self):
        @pl.when(self.rank == 1)
        def _():
            self.up[0].wait_recv()
            self.add(2, self.arrived[0])

        @pl.when(self.rank == 2)
        def _():
            self.down[0].wait_recv()
            self.add(2, self.arrived[0])

    def two(self):
        pl.when(self.rank <= 1)(self.up[1].start)
        pl.when(self.rank >= 2)(self.down[1].start)

    def three(self):
        @pl.when((self.rank == 1) | (self.rank == 2))
        def _():
            self.up[1].wait_recv()
            self.add(3, self.arrived[1].at[0])
            self.down[1].wait_recv()
            self.add(1, self.arrived[1].at[1])

        pl.when(self.rank <= 2)(self.up[2].start)
        pl.when(self.rank >= 1)(self.down[2].start)

    def last(self, out):
        out[...] = self.held(0)[...].astype(jnp.float32)

        @pl.when(self.rank >= 1)
        def _():
            self.up[2].wait_recv()
            out[...] += self.arrived[2][0].astype(jnp.float32)

        @pl.when(self.rank <= 2)
        def _():
            self.down[2].wait_recv()
            out[...] += self.arrived[2][1].astype(jnp.float32)

    def one_sent(self):
        pl.when(self.rank == 0)(self.up[0].wait_send)
        pl.when(self.rank == 3)(self.down[0].wait_send)

    def sent(self):
        pl.when(self.rank <= 1)(self.up[1].wait_send)
        pl.when(self.rank >= 2)(self.down[1].wait_send)
        pl.when(self.rank <= 2)(self.up[2].wait_send)
        pl.when(self.rank >= 1)(self.down[2].wait_send)


class SumPlane:
    def __init__(self, buffer, block, plane, arrived, by_x, by_y, ended, there, index):
        half = buffer.shape[1] // 2
        low, high = pl.ds(0, half), pl.ds(half, half)

        def part(k):
            return buffer.at[pl.ds(pl.multiple_of(plane[k] * block, 16), block)]

        self.parts = own, to_x, to_y, to_both = [part(k) for k in (0, 2, 4, 6)]
        self.arrived, self.by_x, self.by_y, self.ended, self.half = arrived, by_x, by_y, ended, half
        self.core = [
            there(part(2 * i + 1), arrived.at[i], index + i, fsdp=plane[1]) for i in range(4)
        ]
        self.first = [
            there(to_both.at[:, low], by_x.at[1], index + 5, fsdp=plane[2]),
            there(to_both.at[:, high], by_y.at[1], index + 7, fsdp=plane[4]),
            there(to_x.at[:, low], by_x.at[0], index + 4, fsdp=plane[2]),
            there(to_y.at[:, high], by_y.at[0], index + 6, fsdp=plane[4]),
        ]
        self.second = [
            there(to_y.at[:, low], ended.at[0], index + 8, fsdp=plane[4]),
            there(to_x.at[:, high], ended.at[1], index + 9, fsdp=plane[2]),
        ]

    def start_core(self):
        for copy in self.core:
            copy.start()

    def start_first(self):
        for i in (3, 1, 2, 0):
            self.core[i].wait_recv()
            part = self.parts[i]
            part[...] = part[...] + self.arrived[i]
        for copy in self.first:
            copy.start()

    def start_second(self):
        half = self.half
        _, to_x, to_y, _ = self.parts
        self.first[0].wait_recv()
        to_y[:, :half] = to_y[:, :half] + self.by_x[1]
        self.second[0].start()
        self.first[1].wait_recv()
        to_x[:, half:] = to_x[:, half:] + self.by_y[1]
        self.second[1].start()

    def finish(self):
        half = self.half
        own = self.parts[0]
        self.first[2].wait_recv()
        self.second[0].wait_recv()
        total = own[:, :half].astype(jnp.float32) + self.by_x[0].astype(jnp.float32)
        own[:, :half] = (total + self.ended[0].astype(jnp.float32)).astype(jnp.bfloat16)
        self.first[3].wait_recv()
        self.second[1].wait_recv()
        total = own[:, half:].astype(jnp.float32) + self.by_y[0].astype(jnp.float32)
        own[:, half:] = (total + self.ended[1].astype(jnp.float32)).astype(jnp.bfloat16)

    def sent(self):
        for copy in self.core + self.first + self.second:
            copy.wait_send()


def in_order(partial, rows):
    def held(j):
        return partial.at[ORDER.index(j) * rows : (ORDER.index(j) + 1) * rows]

    return held


def front_kernel(
    lengths, tokens, cotangent, small, balance, inverse,
    w_query, w_key, w_value, w_out, w_gate, w_up, w_down,
    gu_all, down_all, upstream_all, normed_all, hidden, factor_gate, factor_up, qkv_out, out_out,
    queries, paired_out, slots_out, logsum, attended, resid, normed_one, gain_one, gain_two,
    slot_row, first_row, cosine, sine,
    q_w, kv_w, out_w, gate_v, up_v, gu, normed, kv, small_own, small_all, slots_all, bias,
    cotangent_v, down_raw, down_own, hidden_v, gate_part, up_part,
    local, ssem, rsem, zsend, zrecv,
):
    f = lax.axis_index("fsdp")
    s = lax.axis_index("seq")
    rows, width = tokens.shape
    n_f, n_s = 8, slots_all.shape[0]
    group = n_s * rows
    block = w_query.shape[0]
    unit_pad = down_own.shape[0]
    unit = w_gate.shape[1] // (n_f * n_s)
    units = n_f * unit_pad
    kv_width = KV_HEADS * HEAD_DIM
    qkv_width = width + 2 * kv_width
    scale = HEAD_DIM ** (-0.5)
    repeat = HEADS // KV_HEADS
    plane = [f ^ k for k in range(n_f)]

    entry = pltpu.get_barrier_semaphore()
    for k in range(1, n_f):
        pl.semaphore_signal(entry, inc=1, device_id={"fsdp": plane[k]}, device_id_type=MESH)
    for j in range(1, n_s):
        pl.semaphore_signal(
            entry, inc=1, device_id={"seq": lax.rem(s + j, n_s)}, device_id_type=MESH
        )

    def here(source, target, index):
        return pltpu.make_async_copy(source, target, local.at[index])

    def there(source, target, index, **device):
        return pltpu.make_async_remote_copy(
            src_ref=source, dst_ref=target, send_sem=ssem.at[index], recv_sem=rsem.at[index],
            device_id=device, device_id_type=MESH,
        )

    def own_rows(ref, owner, size, start=0, count=None):
        first = pl.multiple_of(owner * size + start, 16)
        return ref.at[pl.ds(first, size if count is None else count)]

    class Gather:
        def __init__(self, source, target, size, index):
            half = size // 2
            x, y, c = plane[2], plane[4], plane[1]
            self.own = here(source, own_rows(target, f, size), index // 8) if source is not None else None
            if source is None:
                source = own_rows(target, f, size)
            mine = own_rows(target, f, size)
            self.first = [
                there(source, mine, index, fsdp=x),
                there(source, mine, index + 1, fsdp=y),
                there(source, mine, index + 2, fsdp=c),
            ]
            from_x, from_y = own_rows(target, x, size), own_rows(target, y, size)
            part_x = own_rows(target, x, size, 0, half)
            part_y = own_rows(target, y, size, half, half)
            self.second = [
                there(part_x, part_x, index + 3, fsdp=y),
                there(part_y, part_y, index + 4, fsdp=x),
                there(from_x, from_x, index + 5, fsdp=c),
                there(from_y, from_y, index + 6, fsdp=c),
            ]
            diagonal = own_rows(target, plane[6], size)
            self.third = there(diagonal, diagonal, index + 7, fsdp=c)

        def start(self):
            if self.own is not None:
                self.own.start()
            for copy in self.first:
                copy.start()

        def forward(self):
            self.first[0].wait_recv()
            self.second[0].start()
            self.second[2].start()
            self.first[1].wait_recv()
            self.second[1].start()
            self.second[3].start()

        def last(self):
            self.second[0].wait_recv()
            self.second[1].wait_recv()
            self.third.start()

        def finish(self):
            if self.own is not None:
                self.own.wait()
            self.first[2].wait_recv()
            self.second[2].wait_recv()
            self.second[3].wait_recv()
            self.third.wait_recv()

        def sent(self):
            for copy in self.first + self.second + [self.third]:
                copy.wait_send()

    class Chain:
        def __init__(self, target, index, own=None):
            self.steps = []
            for step in range(1, n_s):
                up = own_rows(target, s - (step - 1), rows)
                down = own_rows(target, s + (step - 1), rows)
                source = own if own is not None and step == 1 else up
                i = index + 2 * (step - 1)
                self.steps.append((
                    pltpu.make_async_remote_copy(
                        src_ref=source, dst_ref=up, send_sem=zsend.at[i], recv_sem=zrecv.at[i],
                        device_id={"seq": s + 1}, device_id_type=MESH,
                    ),
                    pltpu.make_async_remote_copy(
                        src_ref=down if source is up else source, dst_ref=down, send_sem=zsend.at[i + 1], recv_sem=zrecv.at[i + 1],
                        device_id={"seq": s - 1}, device_id_type=MESH,
                    ),
                    (s >= step - 1) & (s < n_s - 1),
                    (s >= 1) & (s <= n_s - step),
                    s >= step,
                    s <= n_s - 1 - step,
                ))

        def send(self, step):
            up, down, can_up, can_down, _, _ = self.steps[step - 1]
            pl.when(can_up)(up.start)
            pl.when(can_down)(down.start)

        def receive(self, step):
            up, down, _, _, from_below, from_above = self.steps[step - 1]
            pl.when(from_below)(up.wait_recv)
            pl.when(from_above)(down.wait_recv)

        def sent(self):
            for up, down, can_up, can_down, _, _ in self.steps:
                pl.when(can_up)(up.wait_send)
                pl.when(can_down)(down.wait_send)

    own_block = pl.ds(pl.multiple_of(f * block, 16), block)
    pieces = [
        here(w_key, kv_w.at[own_block, pl.ds(0, kv_width)], 6),
        here(w_value, kv_w.at[own_block, pl.ds(kv_width, kv_width)], 7),
        here(w_query, q_w.at[own_block], 5),
        here(cotangent, cotangent_v, 8),
    ]
    load_gate = here(w_gate, gate_v, 9)
    load_up = here(w_up, up_v, 10)
    first_unit = pl.multiple_of(s * unit // 16 * 16, 16)
    load_down = here(w_down.at[pl.ds(first_unit, unit_pad)], down_raw, 15)
    for copy in pieces:
        copy.start()
    load_gate.start()
    load_up.start()
    load_down.start()

    slot = (balance[...] & (group - 1)).astype(jnp.float32)
    second = lengths[0, 0].astype(jnp.float32)
    third = (lengths[0, 0] + lengths[0, 1]).astype(jnp.float32)
    first = jnp.where(slot >= third, third, jnp.where(slot >= second, second, 0.0))
    slot_row[...] = jnp.broadcast_to(slot, slot_row.shape)
    first_row[...] = jnp.broadcast_to(first, first_row.shape)
    slots_all[s] = jnp.broadcast_to(slot, (128, rows)).T
    lanes = lax.broadcasted_iota(jnp.int32, small.shape, 1)
    sorts = lax.broadcasted_iota(jnp.int32, small.shape, 0)
    small_own[...] = jnp.where(
        sorts < 3,
        pltpu.roll(small[...], lax.rem(f, 2) * block, 1),
        pltpu.roll(small[...], f * (kv_width // n_f), 1),
    )
    small_all[f] = small_own[...]

    gather_kv = Gather(None, kv_w, block, 0)
    gather_q = Gather(None, q_w, block, 8)
    gather_out = Gather(w_out, out_w, block, 16)
    gather_gu = Gather(None, gu, block, 24)
    gather_down = Gather(down_own, down_all, unit_pad, 32)
    chain_up = Chain(upstream_all, 0, cotangent_v)
    chain_normed = Chain(normed, 6)
    send_small = [
        there(small_own, small_all.at[f], 40 + k, fsdp=plane[k]) for k in range(1, n_f)
    ]
    send_slots = [
        there(slots_all.at[s], slots_all.at[s], 48 + j, seq=lax.rem(s + j, n_s))
        for j in range(1, n_s)
    ]
    send_kv = [
        there(kv.at[s], kv.at[s], 52 + j, seq=lax.rem(s + j, n_s)) for j in range(1, n_s)
    ]
    for copy in pieces[:2]:
        copy.wait()
    pl.semaphore_wait(entry, n_f - 1 + n_s - 1)
    gather_kv.start()
    for copy in send_small + send_slots:
        copy.start()
    for copy in pieces[2:]:
        copy.wait()
    chain_up.send(1)
    save_own = here(cotangent_v, own_rows(upstream_all, s, rows), 8)
    save_own.start()
    position = slots_all[s] - jnp.broadcast_to(first, (128, rows)).T
    angle = position * inverse[...]
    cosine[...] = jnp.cos(angle)
    sine[...] = jnp.where(
        lax.broadcasted_iota(jnp.int32, angle.shape, 1) < HEAD_DIM // 2, -1.0, 1.0
    ) * jnp.sin(angle)

    for copy in send_small + send_slots:
        copy.wait_recv()

    def joined(sort):
        return jnp.concatenate(
            [
                small_all[2 * i, sort : sort + 1] + small_all[2 * i + 1, sort : sort + 1]
                for i in range(n_f // 2)
            ],
            1,
        )

    gain_one[...] = joined(0)
    gain_two[...] = joined(1)
    bias_query = joined(2)
    bias_key = sum(small_all[i, 3:4, :kv_width] for i in range(n_f))
    bias_value = sum(small_all[i, 4:5, :kv_width] for i in range(n_f))

    inputs = tokens[...].astype(jnp.float32)
    root = lax.rsqrt(jnp.mean(inputs * inputs, -1, keepdims=True) + epsilon)
    normed_one[...] = (inputs * root * gain_one[...]).astype(jnp.bfloat16)
    gather_kv.forward()
    gather_q.start()
    gather_kv.last()
    gather_kv.finish()

    def turned(value):
        return value * cosine[...] + pltpu.roll(value, HEAD_DIM // 2, 1) * sine[...]

    rows_low = normed_one[...]
    pair = jnp.dot(rows_low, kv_w[:, :kv_width], preferred_element_type=jnp.float32)
    pair = pair + bias_key
    for g in range(KV_HEADS):
        columns = slice(g * HEAD_DIM, (g + 1) * HEAD_DIM)
        kv[s, :, columns] = turned(pair[:, columns]).astype(jnp.bfloat16)
    pair = jnp.dot(rows_low, kv_w[:, kv_width:], preferred_element_type=jnp.float32)
    kv[s, :, kv_width:] = (pair + bias_value).astype(jnp.bfloat16)
    for copy in send_kv:
        copy.start()
    save_kv_w = here(kv_w, qkv_out.at[:, pl.ds(width, 2 * kv_width)], 11)
    save_kv_w.start()

    load_gate.wait()
    load_up.wait()
    pick_units(gate_v, up_v, gu.at[own_block], w_gate.shape[1] // n_f, unit, unit_pad)
    gather_q.forward()
    gather_out.start()
    load_down.wait()
    raw = down_raw[...].astype(jnp.float32)
    shifted = jnp.concatenate([raw[8:], jnp.zeros((8, width), jnp.float32)], 0)
    raw = jnp.where(lax.rem(s * unit, 16) == 0, raw, shifted)
    inside = lax.broadcasted_iota(jnp.int32, raw.shape, 0) < unit
    down_own[...] = jnp.where(inside, raw, 0.0).astype(jnp.bfloat16)

    for j in range(n_s):
        keys_slot = slots_all[j]
        keys_slot = jnp.concatenate([keys_slot] * (rows // 128), 1)
        ok = (keys_slot <= slot) & (keys_slot >= first)
        bias[j * rows : (j + 1) * rows] = jnp.where(ok, 0.0, -1e30)

    gather_q.last()
    gather_q.finish()
    save_q_w = here(q_w, qkv_out.at[:, pl.ds(0, width)], 0)
    save_q_w.start()
    for g in range(HEADS // 2):
        columns = slice(g * 2 * HEAD_DIM, (g + 1) * 2 * HEAD_DIM)
        pair = jnp.dot(rows_low, q_w[:, columns], preferred_element_type=jnp.float32)
        pair = pair + bias_query[:, columns]
        for h in range(2):
            part = turned(pair[:, h * HEAD_DIM : (h + 1) * HEAD_DIM]).astype(jnp.bfloat16)
            queries[:, (2 * g + h) * HEAD_DIM : (2 * g + h + 1) * HEAD_DIM] = part

    gather_out.forward()
    chain_up.receive(1)
    for copy in send_kv:
        copy.wait_recv()
    chain_up.send(2)
    save_kv = here(kv, paired_out, 12)
    save_kv.start()
    slots_out[...] = slots_all[...]

    for g in range(KV_HEADS):
        keys = kv[:, :, g * HEAD_DIM : (g + 1) * HEAD_DIM].reshape(n_s * rows, HEAD_DIM)
        values = kv[:, :, kv_width + g * HEAD_DIM : kv_width + (g + 1) * HEAD_DIM]
        values = values.reshape(n_s * rows, HEAD_DIM)

        def head(i, carry, g=g, keys=keys, values=values):
            h = g * repeat + i
            columns = pl.ds(pl.multiple_of(h * HEAD_DIM, HEAD_DIM), HEAD_DIM)
            raw = lax.dot_general(
                keys, queries[:, columns], (((1,), (1,)), ((), ())),
                preferred_element_type=jnp.float32,
            )
            scores = raw * scale + bias[...]
            top = jnp.max(scores, 0, keepdims=True)
            expo = jnp.exp(scores - top)
            total = jnp.sum(expo, 0, keepdims=True)
            probs = (expo * (1.0 / total)).astype(jnp.bfloat16)
            mixed = lax.dot_general(
                values, probs, (((0,), (0,)), ((), ())), preferred_element_type=jnp.float32
            )
            attended[:, columns] = mixed.T.astype(jnp.bfloat16)
            logsum[pl.ds(pl.multiple_of(h * 8, 8), 8)] = jnp.broadcast_to(
                top + jnp.log(total), (8, rows)
            )
            return carry

        lax.fori_loop(0, repeat, head, 0)
        if g == 0:
            gather_out.last()
            gather_gu.start()

    gather_out.finish()
    save_out = here(out_w, out_out, 13)
    save_out.start()
    mixed = attended[...]
    for g in range(width // 256):
        columns = slice(g * 256, (g + 1) * 256)
        part = jnp.dot(mixed, out_w[:, columns], preferred_element_type=jnp.float32)
        resid[:, columns] = tokens[:, columns].astype(jnp.float32) + part
    value = resid[...]
    root = lax.rsqrt(jnp.mean(value * value, -1, keepdims=True) + epsilon)
    own_tokens = pl.ds(pl.multiple_of(s * rows, rows), rows)
    normed[own_tokens] = (value * root * gain_two[...]).astype(jnp.bfloat16)
    chain_normed.send(1)

    wide = hidden_v.shape[2]
    count = units // wide

    def saves(owner, t, slot):
        place = (
            pl.ds(pl.multiple_of(owner * rows, rows), rows),
            pl.ds(pl.multiple_of(t * wide, wide), wide),
        )
        return [
            here(part.at[slot], whole.at[place], 16 + 3 * slot + i)
            for i, (part, whole) in enumerate(
                ((hidden_v, hidden), (gate_part, factor_gate), (up_part, factor_up))
            )
        ]

    def feed(owner, done):
        def body(t, carry):
            slot = lax.rem(t + done, 2)
            mine = normed[pl.ds(pl.multiple_of(owner * rows, rows), rows)]
            gate_columns = pl.ds(pl.multiple_of(t * wide, wide), wide)
            up_columns = pl.ds(pl.multiple_of(units + t * wide, wide), wide)
            gate = jnp.dot(mine, gu[:, gate_columns], preferred_element_type=jnp.float32)
            up = jnp.dot(mine, gu[:, up_columns], preferred_element_type=jnp.float32)
            sigma = jax.nn.sigmoid(gate)
            activated = gate * sigma

            @pl.when(t + done >= 2)
            def _():
                for copy in saves(owner, t, slot):
                    copy.wait()

            hidden_v[slot] = (activated * up).astype(jnp.bfloat16)
            gate_part[slot] = (up * sigma * (1.0 + gate * (1.0 - sigma))).astype(jnp.bfloat16)
            up_part[slot] = activated.astype(jnp.bfloat16)
            for copy in saves(owner, t, slot):
                copy.start()
            return carry

        lax.fori_loop(0, count, body, 0)

    chain_up.receive(2)
    chain_normed.receive(1)
    chain_normed.send(2)
    gather_gu.forward()
    chain_normed.receive(2)
    chain_normed.send(3)
    gather_gu.last()
    gather_down.start()
    gather_gu.finish()
    save_gu = here(gu, gu_all, 22)
    save_gu.start()
    feed(s, 0)
    feed(s ^ 1, count)
    chain_normed.receive(3)
    chain_up.send(3)
    save_normed = here(normed, normed_all, 23)
    save_normed.start()
    feed(s ^ 2, 2 * count)
    gather_down.forward()
    feed(s ^ 3, 3 * count)
    gather_down.last()
    for t in (count - 2, count - 1):
        for copy in saves(s ^ 3, t, (t + 3 * count) % 2):
            copy.wait()
    chain_up.receive(3)
    gather_down.finish()
    for copy in (save_own, save_kv_w, save_q_w, save_kv, save_out, save_gu, save_normed):
        copy.wait()
    for part in (gather_kv, gather_q, gather_out, gather_gu, gather_down, chain_up, chain_normed):
        part.sent()
    for copy in send_small + send_slots + send_kv:
        copy.wait_send()


def pick_units(gate, up, out, stride, unit, padded):
    rank = lax.axis_index("seq")
    pieces = gate.shape[1] // stride
    half = out.shape[1] // 2
    window, tile = 512, 128
    rows = lax.broadcasted_iota(jnp.int32, (window, tile), 0)
    columns = lax.broadcasted_iota(jnp.int32, (window, tile), 1)
    for first in range(0, 2 * half, tile):
        source = gate if first < half else up
        local = first % half
        total = jnp.zeros((out.shape[0], tile), jnp.float32)
        for f in range(pieces):
            low = max(local, f * padded)
            high = min(local + tile, f * padded + unit)
            if low >= high:
                continue
            begin = f * stride + rank * unit
            base = jnp.minimum(begin // 128, (source.shape[1] - window) // 128) * 128
            base = pl.multiple_of(base, 128)
            wanted = columns + (local - f * padded + begin - base)
            inside = (columns >= low - local) & (columns < high - local)
            chosen = jnp.where((rows == wanted) & inside, 1.0, 0.0).astype(jnp.bfloat16)
            total += jnp.dot(
                source[:, pl.ds(base, window)], chosen, preferred_element_type=jnp.float32
            )
        out[:, first : first + tile] = total.astype(jnp.bfloat16)


def front(tokens, cotangent, lengths, balance, vectors, weights):
    rows, width = tokens.shape
    n_s = lax.axis_size("seq")
    w_query, w_key, w_value, w_out, w_gate, w_up, w_down = weights
    block = w_query.shape[0]
    unit_pad = -(-w_down.shape[0] // n_s // 16) * 16
    kv_width = KV_HEADS * HEAD_DIM
    qkv_width = width + 2 * kv_width
    units = 8 * unit_pad
    group = n_s * rows
    wide = 768
    low, full = jnp.bfloat16, jnp.float32
    small = sum(
        jnp.pad(v.astype(full)[None], ((i, 7 - i), (0, 2 * block - v.shape[0])))
        for i, v in enumerate(vectors)
    )
    half = HEAD_DIM // 2
    inverse = rope_base ** (-(np.arange(half, dtype=np.float32) * np.float32(2.0 / HEAD_DIM)))
    inverse = jnp.asarray(np.concatenate([inverse, inverse])[None], full)
    smem = pl.BlockSpec(memory_space=pltpu.SMEM)
    vmem = pl.BlockSpec(memory_space=pltpu.VMEM)
    hbm = pl.BlockSpec(memory_space=pl.ANY)
    shape = jax.ShapeDtypeStruct
    return pl.pallas_call(
        front_kernel,
        in_specs=[smem, vmem, hbm, vmem, vmem, vmem] + [hbm] * 7,
        out_specs=[hbm] * 9 + [vmem, hbm] + [vmem] * 11,
        out_shape=[
            shape((width, 2 * units), low),
            shape((units, width), low),
            shape((group, width), low),
            shape((group, width), low),
            shape((group, units), low),
            shape((group, units), low),
            shape((group, units), low),
            shape((width, qkv_width), low),
            shape((width, width), low),
            shape((rows, width), low),
            shape((n_s, rows, 2 * kv_width), low),
            shape((n_s, rows, 128), full),
            shape((8 * HEADS, rows), full),
            shape((rows, width), low),
            shape((rows, width), full),
            shape((rows, width), low),
            shape((1, width), full),
            shape((1, width), full),
            shape((8, rows), full),
            shape((8, rows), full),
            shape((rows, HEAD_DIM), full),
            shape((rows, HEAD_DIM), full),
        ],
        scratch_shapes=[
            pltpu.VMEM((width, width), low),
            pltpu.VMEM((width, 2 * kv_width), low),
            pltpu.VMEM((width, width), low),
            pltpu.VMEM(w_gate.shape, low),
            pltpu.VMEM(w_up.shape, low),
            pltpu.VMEM((width, 2 * units), low),
            pltpu.VMEM((group, width), low),
            pltpu.VMEM((n_s, rows, 2 * kv_width), low),
            pltpu.VMEM((8, 2 * block), full),
            pltpu.VMEM((8, 8, 2 * block), full),
            pltpu.VMEM((n_s, rows, 128), full),
            pltpu.VMEM((group, rows), full),
            pltpu.VMEM((rows, width), low),
            pltpu.VMEM((unit_pad, width), low),
            pltpu.VMEM((unit_pad, width), low),
            pltpu.VMEM((2, rows, wide), low),
            pltpu.VMEM((2, rows, wide), low),
            pltpu.VMEM((2, rows, wide), low),
            pltpu.SemaphoreType.DMA((24,)),
            pltpu.SemaphoreType.DMA((56,)),
            pltpu.SemaphoreType.DMA((56,)),
            pltpu.SemaphoreType.DMA((12,)),
            pltpu.SemaphoreType.DMA((12,)),
        ],
        compiler_params=pltpu.CompilerParams(
            collective_id=0, has_side_effects=True, vmem_limit_bytes=62 * 2**20
        ),
        name="front",
    )(
        lengths, tokens, cotangent, small, balance.reshape(1, rows), inverse,
        w_query, w_key, w_value, w_out, w_gate, w_up, w_down,
    )


def ffn_kernel(
    normed_all, upstream_all, w_gu, w_down, hidden_all, factor_gate, factor_up,
    columns, grad_down, gu_sum, branch, down_arrived, gu_arrived,
    normed, upstream, gu, down, hidden, d_both, partial, z_one, z_two, z_three,
    down_x, down_y, down_last, down_piece,
    load, ssem, rsem,
):
    f = lax.axis_index("fsdp")
    s = lax.axis_index("seq")
    n_s = len(ORDER)
    group, width = normed.shape
    rows = group // n_s
    half_rows = group // 2
    units = down.shape[0]
    tile = 256
    tiles = units // tile
    wide = 768
    block = gu.shape[0] // 8
    unit = units // 8
    half = width // 2
    plane = [f ^ k for k in range(8)]
    full = jnp.float32

    entry = pltpu.get_barrier_semaphore()
    for k in (1, 2, 4):
        pl.semaphore_signal(entry, inc=1, device_id={"fsdp": plane[k]}, device_id_type=MESH)
    for j in (1, n_s - 1):
        pl.semaphore_signal(
            entry, inc=1, device_id={"seq": lax.rem(s + j, n_s)}, device_id_type=MESH
        )

    def here(source, target, index):
        return pltpu.make_async_copy(source, target, load.at[index])

    def there(source, target, index, **device):
        return pltpu.make_async_remote_copy(
            src_ref=source, dst_ref=target, send_sem=ssem.at[index], recv_sem=rsem.at[index],
            device_id=device, device_id_type=MESH,
        )

    def part(ref, owner, size):
        return ref.at[pl.ds(pl.multiple_of(owner * size, 16), size)]

    early, late = range(0, n_s // 2), range(n_s // 2, n_s)

    def rows_of(p):
        return pl.ds(p * rows, rows)

    def row_loads(p):
        owner = lax.rem(s + n_s - ORDER[p], n_s)
        mine = rows_of(p)
        return [
            here(part(upstream_all, owner, rows), upstream.at[mine], 5 * p),
            here(part(factor_gate, owner, rows), d_both.at[mine, pl.ds(0, units)], 5 * p + 1),
            here(part(factor_up, owner, rows), d_both.at[mine, pl.ds(units, units)], 5 * p + 2),
            here(part(hidden_all, owner, rows), hidden.at[mine], 5 * p + 3),
            here(part(normed_all, owner, rows), normed.at[mine], 5 * p + 4),
        ]

    def down_load(t):
        mine = pl.ds(pl.multiple_of(t * wide, wide), wide)
        return here(w_down.at[mine], down.at[mine], 20 + t)

    def gu_load(n):
        mine = pl.ds(pl.multiple_of(n * 512, 512), 512)
        return here(w_gu.at[mine], gu.at[mine], 23 + n)

    loads = [row_loads(p) for p in range(n_s)]
    order = [loads[0][0], loads[1][0], down_load(0)]
    order += [loads[p][i] for i in (1, 2) for p in early]
    order += [down_load(t) for t in range(1, units // wide)]
    order += [gu_load(n) for n in range(width // 512)]
    order += [loads[p][i] for i in (0, 1, 2) for p in late]
    order += [loads[p][i] for i in (3, 4) for p in range(n_s)]
    for copy in order:
        copy.start()

    def forward(blocks, wait):
        for p in blocks:
            for copy in loads[p][:3]:
                copy.wait()
        mine = pl.ds(blocks[0] * rows, len(blocks) * rows)

        def body(t, carry):
            if wait:
                down_load(t).wait()
            gate_columns = pl.ds(pl.multiple_of(t * wide, wide), wide)
            up_columns = pl.ds(pl.multiple_of(units + t * wide, wide), wide)
            d_hidden = lax.dot_general(
                upstream[mine], down[gate_columns], (((1,), (1,)), ((), ())),
                preferred_element_type=full,
            )
            value = d_hidden * d_both[mine, gate_columns].astype(full)
            d_both[mine, gate_columns] = value.astype(jnp.bfloat16)
            value = d_hidden * d_both[mine, up_columns].astype(full)
            d_both[mine, up_columns] = value.astype(jnp.bfloat16)
            return carry

        lax.fori_loop(0, units // wide, body, 0)

    def backward(blocks, wait):
        part_rows = pl.ds(blocks[0] * rows, len(blocks) * rows)

        def body(n, carry):
            if wait:
                gu_load(n).wait()
            out_columns = pl.ds(pl.multiple_of(n * 512, 512), 512)
            value = lax.dot_general(
                d_both[part_rows], gu[out_columns], (((1,), (1,)), ((), ())),
                preferred_element_type=full,
            )
            partial[part_rows, out_columns] = value.astype(jnp.bfloat16)
            return carry

        lax.fori_loop(0, width // 512, body, 0)

    chain = SumChain(in_order(partial, rows), z_one, z_two, z_three, there, 0)
    pieces = [(first, min(group, units - first)) for first in range(0, units, group)]
    forward(early, True)
    backward(early, True)
    pl.semaphore_wait(entry, 5)
    chain.one()
    forward(late, False)
    backward(late, False)
    chain.add_one()
    chain.two()

    for p in range(n_s):
        loads[p][3].wait()
        loads[p][4].wait()

    def down_body(t, carry):
        unit_rows = pl.ds(pl.multiple_of(t * tile, tile), tile)
        value = lax.dot_general(
            hidden[:, unit_rows], upstream[...], (((0,), (0,)), ((), ())),
            preferred_element_type=full,
        )
        down[unit_rows] = value.astype(jnp.bfloat16)
        return carry

    lax.fori_loop(0, tiles, down_body, 0)
    down_core = [
        there(part(down, plane[2 * i + 1], unit), down_arrived.at[i], 6 + i, fsdp=plane[1])
        for i in range(4)
    ]
    for i in (3, 1, 2, 0):
        down_core[i].start()

    again_in = [upstream] + [
        d_both.at[:count, i * width : (i + 1) * width] for i, (_, count) in enumerate(pieces[1:])
    ]
    again = [
        here(w_down.at[first : first + count], place, 36 + i)
        for i, ((first, count), place) in enumerate(zip(pieces, again_in))
    ]
    again[0].start()

    def gu_body(m, carry):
        in_columns = pl.ds(pl.multiple_of(m * tile, tile), tile)
        turned = normed[:, in_columns].T
        for first in range(0, 2 * units, units // 3):
            value = jnp.dot(turned, d_both[:, first : first + units // 3], preferred_element_type=full)
            gu[in_columns, first : first + units // 3] = value.astype(jnp.bfloat16)
        return carry

    lax.fori_loop(0, 2, gu_body, 0)

    class Arrivals:
        def __init__(self, ref, size, arrived, copies, turns, index):
            self.ref, self.size, self.copies = ref, size, copies
            self.pieces = {}
            for n, i in enumerate((3, 1, 2, 0)):
                self.pieces[i] = [
                    (here(arrived.at[i, :, columns], piece, index + 3 * (n % 2) + k), columns, piece)
                    for k, (columns, piece) in enumerate(turns[n % 2])
                ]

        def fetch(self, i):
            self.copies[i].wait_recv()
            for copy, _, _ in self.pieces[i]:
                copy.start()

        def add(self, i):
            target = part(self.ref, plane[2 * i], self.size)
            for copy, columns, piece in self.pieces[i]:
                copy.wait()
                target[:, columns] = target[:, columns] + piece[...]

    down_turns = [[(pl.ds(0, width), piece)] for piece in (down_piece.at[0], down_piece.at[1])]
    down_sum = Arrivals(down, unit, down_arrived, down_core, down_turns, 26)
    down_sum.fetch(3)
    for i, following in ((3, 1), (1, 2), (2, 0), (0, None)):
        if following is not None:
            down_sum.fetch(following)
        down_sum.add(i)
    to_x, to_y, to_both = [part(down, plane[k], unit) for k in (2, 4, 6)]
    low_half, high_half = pl.ds(0, half), pl.ds(half, half)
    down_first = [
        there(to_x.at[:, low_half], down_x.at[0], 10, fsdp=plane[2]),
        there(to_both.at[:, low_half], down_x.at[1], 11, fsdp=plane[2]),
        there(to_y.at[:, high_half], down_y.at[0], 12, fsdp=plane[4]),
        there(to_both.at[:, high_half], down_y.at[1], 13, fsdp=plane[4]),
    ]
    for copy in down_first:
        copy.start()
    chain.three()
    lax.fori_loop(2, width // tile, gu_body, 0)
    gu_core = [
        there(part(gu, plane[2 * i + 1], block), gu_arrived.at[i], 16 + i, fsdp=plane[1])
        for i in range(4)
    ]
    for i in (3, 1, 2, 0):
        gu_core[i].start()

    for copy in again[1:]:
        copy.start()
    for copy in again:
        copy.wait()

    def branch_body(n, carry):
        out_columns = pl.ds(pl.multiple_of(n * wide, wide), wide)
        for m in range(2):
            mine = slice(m * half_rows, (m + 1) * half_rows)
            value = jnp.zeros((half_rows, wide), full)
            for i, (first, count) in enumerate(pieces):
                value += jnp.dot(
                    hidden[mine, first : first + count], again_in[i][:, out_columns],
                    preferred_element_type=full,
                )
            normed[mine, out_columns] = value.astype(jnp.bfloat16)
        return carry

    lax.fori_loop(0, width // wide, branch_body, 0)
    chain.last(columns)
    chain_branch = SumChain(in_order(normed, rows), z_one, z_two, z_three, there, 22)
    chain_branch.one()
    down_second = [
        there(to_y.at[:, low_half], down_last.at[0], 14, fsdp=plane[4]),
        there(to_x.at[:, high_half], down_last.at[1], 15, fsdp=plane[2]),
    ]
    down_first[1].wait_recv()
    to_y[:, :half] = to_y[:, :half] + down_x[1]
    down_second[0].start()
    down_first[3].wait_recv()
    to_x[:, half:] = to_x[:, half:] + down_y[1]
    down_second[1].start()
    gu_turns = [
        [(pl.ds(k * units, units), hidden.at[(2 * n + k) * block : (2 * n + k + 1) * block]) for k in range(2)]
        for n in range(2)
    ]
    gu_arrivals = Arrivals(gu, block, gu_arrived, gu_core, gu_turns, 26)
    store = [here(part(gu, plane[2 * i], block), gu_sum.at[i], 32 + i) for i in range(4)]
    gu_arrivals.fetch(3)
    for i, following in ((3, 1), (1, 2), (2, 0), (0, None)):
        if following is not None:
            gu_arrivals.fetch(following)
        gu_arrivals.add(i)
        store[i].start()
    down_first[0].wait_recv()
    down_first[2].wait_recv()
    own = part(down, f, unit)
    down_second[0].wait_recv()
    grad_down[:, :half] = (
        own[:, :half].astype(full) + down_x[0].astype(full) + down_last[0].astype(full)
    )
    down_second[1].wait_recv()
    grad_down[:, half:] = (
        own[:, half:].astype(full) + down_y[0].astype(full) + down_last[1].astype(full)
    )
    chain_branch.add_one()
    chain_branch.one_sent()
    store_branch = here(normed, branch, 39)
    store_branch.start()
    chain.one_sent()
    chain.sent()
    for copy in down_core + down_first + down_second + gu_core:
        copy.wait_send()
    for copy in store + [store_branch]:
        copy.wait()


def ffn(normed_all, upstream_all, w_gu, w_down, hidden, factor_gate, factor_up):
    group, width = normed_all.shape
    units = w_down.shape[0]
    rows = group // len(ORDER)
    unit, block, half = units // 8, width // 8, width // 2
    low, full = jnp.bfloat16, jnp.float32
    vmem = pl.BlockSpec(memory_space=pltpu.VMEM)
    hbm = pl.BlockSpec(memory_space=pl.ANY)
    shape = jax.ShapeDtypeStruct
    return pl.pallas_call(
        ffn_kernel,
        in_specs=[hbm] * 7,
        out_specs=[vmem] * 2 + [hbm] * 4,
        out_shape=[
            shape((rows, width), full),
            shape((unit, width), full),
            shape((4, block, 2 * units), low),
            shape((group, width), low),
            shape((4, unit, width), low),
            shape((4, block, 2 * units), low),
        ],
        scratch_shapes=[
            pltpu.VMEM((group, width), low),
            pltpu.VMEM((group, width), low),
            pltpu.VMEM((width, 2 * units), low),
            pltpu.VMEM((units, width), low),
            pltpu.VMEM((group, units), low),
            pltpu.VMEM((group, 2 * units), low),
            pltpu.VMEM((group, width), low),
            pltpu.VMEM((rows, width), low),
            pltpu.VMEM((2, rows, width), low),
            pltpu.VMEM((2, rows, width), low),
            pltpu.VMEM((2, unit, half), low),
            pltpu.VMEM((2, unit, half), low),
            pltpu.VMEM((2, unit, half), low),
            pltpu.VMEM((2, unit, width), low),
            pltpu.SemaphoreType.DMA((40,)),
            pltpu.SemaphoreType.DMA((28,)),
            pltpu.SemaphoreType.DMA((28,)),
        ],
        compiler_params=pltpu.CompilerParams(
            collective_id=1, has_side_effects=True, vmem_limit_bytes=63 * 2**20
        ),
        name="ffn",
    )(normed_all, upstream_all, w_gu, w_down, hidden, factor_gate, factor_up)[:4]


def back_kernel(
    columns, resid, gain_two, cotangent, attended, queries, paired, slots, slot_row, first_row,
    logsum, normed_one, tokens, gain_one, cosine, sine, w_out, w_qkv, gu_sum, branch,
    layer, input_rows, vector, grad_out, grad_qkv, gu_rows,
    out_w, qkv, gu_own, gu_to_y, gu_to_x, gu_x, gu_y, gu_ended,
    branch_v, z_one, z_two, z_three, working, bias, d_branch, d_attended, d_qkv, d_resid,
    keys_grad, values_grad, dkv, dkv_in,
    out_arrived, out_x, out_y, out_ended, qkv_arrived, qkv_x, qkv_y, qkv_ended,
    out_one, out_two, out_three, qkv_one, qkv_two, qkv_three, vector_in,
    load, ssem, rsem,
):
    f = lax.axis_index("fsdp")
    s = lax.axis_index("seq")
    rows, width = tokens.shape
    n_s = paired.shape[0]
    kv_width = KV_HEADS * HEAD_DIM
    repeat = HEADS // KV_HEADS
    scale = HEAD_DIM ** (-0.5)
    block = width // 8
    piece = block // n_s
    units = gu_sum.shape[2] // 2
    tile = 256
    full, low = jnp.float32, jnp.bfloat16
    plane = [f ^ k for k in range(8)]

    entry = pltpu.get_barrier_semaphore()
    for k in (1, 2, 4):
        pl.semaphore_signal(entry, inc=1, device_id={"fsdp": plane[k]}, device_id_type=MESH)
    for j in range(1, n_s):
        pl.semaphore_signal(
            entry, inc=1, device_id={"seq": lax.rem(s + j, n_s)}, device_id_type=MESH
        )

    def here(source, target, index):
        return pltpu.make_async_copy(source, target, load.at[index])

    def there(source, target, index, **device):
        return pltpu.make_async_remote_copy(
            src_ref=source, dst_ref=target, send_sem=ssem.at[index], recv_sem=rsem.at[index],
            device_id=device, device_id_type=MESH,
        )

    low_units, high_units = pl.ds(0, units), pl.ds(units, units)
    load_branch = here(branch, branch_v, 0)
    load_out = here(w_out, out_w, 1)
    load_gu = [
        here(gu_sum.at[0], gu_own, 2),
        here(gu_sum.at[2, :, low_units], gu_to_y, 3),
        here(gu_sum.at[1, :, high_units], gu_to_x, 4),
    ]
    load_qkv = here(w_qkv, qkv, 5)
    load_columns = here(columns, working, 7)
    for copy in [load_columns, load_branch, load_out] + load_gu + [load_qkv]:
        copy.start()

    gu_first = [
        there(gu_sum.at[3, :, low_units], gu_x.at[1], 0, fsdp=plane[2]),
        there(gu_sum.at[3, :, high_units], gu_y.at[1], 1, fsdp=plane[4]),
        there(gu_sum.at[1, :, low_units], gu_x.at[0], 2, fsdp=plane[2]),
        there(gu_sum.at[2, :, high_units], gu_y.at[0], 3, fsdp=plane[4]),
    ]
    gu_second = [
        there(gu_to_y, gu_ended.at[0], 4, fsdp=plane[4]),
        there(gu_to_x, gu_ended.at[1], 5, fsdp=plane[2]),
    ]

    def around(j):
        return {"seq": lax.rem(s + j, n_s)}

    def rows_for(ref, first, j):
        owner = lax.rem(s + j, n_s)
        return ref.at[pl.ds(pl.multiple_of(first + owner * piece, 16), piece)]

    gu_send = [there(rows_for(gu_own, 0, j), gu_rows.at[j], 5 + j, **around(j)) for j in range(1, n_s)]
    dkv_send = [
        [
            there(dkv.at[g, lax.rem(s + j, n_s)], dkv_in.at[g, j], 8 + 3 * g + j, **around(j))
            for j in range(1, n_s)
        ]
        for g in range(KV_HEADS)
    ]
    chain = SumChain(in_order(branch_v, rows), z_one, z_two, z_three, there, 16)
    sum_out = SumPlane(out_w, block, plane, out_arrived, out_x, out_y, out_ended, there, 24)
    sum_qkv = SumPlane(qkv, block, plane, qkv_arrived, qkv_x, qkv_y, qkv_ended, there, 36)

    def own_part(ref):
        return lambda j: rows_for(ref, f * block, n_s - j)

    chain_out = SumChain(own_part(out_w), out_one, out_two, out_three, there, 48)
    chain_qkv = SumChain(own_part(qkv), qkv_one, qkv_two, qkv_three, there, 54)
    vector_send = [
        there(vector_in.at[0], vector_in.at[1], 60, fsdp=plane[1]),
        there(vector_in.at[2], vector_in.at[3], 61, fsdp=plane[2]),
        there(vector_in.at[4], vector_in.at[5], 62, fsdp=plane[4]),
    ] + [there(vector_in.at[6], vector_in.at[6 + j], 62 + j, **around(j)) for j in range(1, n_s)]

    pl.semaphore_wait(entry, 3 + n_s - 1)
    for copy in gu_first:
        copy.start()
    load_branch.wait()
    chain.two()

    def norm_back(value, gain, grad):
        root = lax.rsqrt(jnp.mean(value * value, -1, keepdims=True) + epsilon)
        scaled = gain * grad
        inner = jnp.mean(scaled * value, -1, keepdims=True)
        gain_grad = jnp.sum(grad * (value * root), 0, keepdims=True)
        return root * scaled - value * (root * root * root * inner), gain_grad

    load_columns.wait()
    d_norm, gain_two_grad = norm_back(resid[...], gain_two[...], working[...])
    d_total = cotangent[...].astype(full) + d_norm
    d_branch[...] = d_total.astype(low)
    d_resid[...] = d_total
    for j in range(n_s):
        keys_slot = slots[j]
        keys_slot = jnp.concatenate([keys_slot] * (rows // 128), 1)
        ok = (keys_slot <= slot_row[0:1]) & (keys_slot >= first_row[0:1])
        bias[j * rows : (j + 1) * rows] = jnp.where(ok, 0.0, -1e30)
    load_out.wait()
    for n in range(width // tile):
        value = lax.dot_general(
            d_branch[...], out_w[n * tile : (n + 1) * tile], (((1,), (1,)), ((), ())),
            preferred_element_type=full,
        )
        d_attended[:, n * tile : (n + 1) * tile] = value.astype(low)

    def turned_back(value):
        return value * cosine[...] + pltpu.roll(value * sine[...], HEAD_DIM // 2, 1)

    for g in range(KV_HEADS):
        keys = paired[:, :, g * HEAD_DIM : (g + 1) * HEAD_DIM].reshape(n_s * rows, HEAD_DIM)
        values = paired[:, :, kv_width + g * HEAD_DIM : kv_width + (g + 1) * HEAD_DIM]
        values = values.reshape(n_s * rows, HEAD_DIM)
        keys_grad[...] = jnp.zeros_like(keys_grad)
        values_grad[...] = jnp.zeros_like(values_grad)

        def head(i, carry, g=g, keys=keys, values=values):
            h = g * repeat + i
            head_columns = pl.ds(pl.multiple_of(h * HEAD_DIM, HEAD_DIM), HEAD_DIM)
            query = queries[:, head_columns]
            grad = d_attended[:, head_columns]
            raw = lax.dot_general(
                keys, query, (((1,), (1,)), ((), ())), preferred_element_type=full
            )
            logs = logsum[pl.ds(pl.multiple_of(h * 8, 8), 8)][0:1]
            probs = jnp.exp(raw * scale + bias[...] - logs)
            d_probs = lax.dot_general(
                values, grad, (((1,), (1,)), ((), ())), preferred_element_type=full
            )
            delta = jnp.sum(probs * d_probs, 0, keepdims=True)
            d_score = (probs * (d_probs - delta)).astype(low)
            turned = lax.dot_general(
                keys, d_score, (((0,), (0,)), ((), ())), preferred_element_type=full
            )
            d_qkv[:, head_columns] = turned_back((turned * scale).T).astype(low)
            keys_grad[...] += jnp.dot(d_score, query, preferred_element_type=full) * scale
            values_grad[...] += jnp.dot(probs.astype(low), grad, preferred_element_type=full)
            return carry

        lax.fori_loop(0, repeat, head, 0)
        dkv[g, :, :, :HEAD_DIM] = keys_grad[...].astype(low).reshape(n_s, rows, HEAD_DIM)
        dkv[g, :, :, HEAD_DIM:] = values_grad[...].astype(low).reshape(n_s, rows, HEAD_DIM)
        for copy in dkv_send[g]:
            copy.start()

    turned = attended[...].T
    for n in range(width // tile):
        n_columns = slice(n * tile, (n + 1) * tile)
        value = jnp.dot(turned, d_branch[:, n_columns], preferred_element_type=full)
        out_w[:, n_columns] = value.astype(low)
    sum_out.start_core()
    load_qkv.wait()

    def back_one(first, count, start):
        for n in range(width // tile):
            n_rows = slice(n * tile, (n + 1) * tile)
            value = lax.dot_general(
                d_qkv[:, first : first + count], qkv[n_rows, first : first + count],
                (((1,), (1,)), ((), ())), preferred_element_type=full,
            )
            working[:, n_rows] = value if start else working[:, n_rows] + value

    back_one(0, width, True)
    normed_turned = normed_one[...].T
    for n in range(width // tile):
        n_columns = slice(n * tile, (n + 1) * tile)
        value = jnp.dot(normed_turned, d_qkv[:, n_columns], preferred_element_type=full)
        qkv[:, n_columns] = value.astype(low)
    for copy in load_gu:
        copy.wait()
    gu_first[0].wait_recv()
    gu_to_y[...] = gu_to_y[...] + gu_x[1]
    gu_second[0].start()
    gu_first[1].wait_recv()
    gu_to_x[...] = gu_to_x[...] + gu_y[1]
    gu_second[1].start()
    sum_out.start_first()

    for g in range(KV_HEADS):
        for copy in dkv_send[g]:
            copy.wait_recv()
        total = dkv[g, s].astype(full)
        for j in range(1, n_s):
            total = total + dkv_in[g, j].astype(full)
        key_columns = slice(width + g * HEAD_DIM, width + (g + 1) * HEAD_DIM)
        value_columns = slice(width + kv_width + g * HEAD_DIM, width + kv_width + (g + 1) * HEAD_DIM)
        d_qkv[:, key_columns] = turned_back(total[:, :HEAD_DIM]).astype(low)
        d_qkv[:, value_columns] = total[:, HEAD_DIM:].astype(low)
    back_one(width, 2 * kv_width, False)
    value = jnp.dot(normed_turned, d_qkv[:, width:], preferred_element_type=full)
    qkv[:, width:] = value.astype(low)
    sum_qkv.start_core()
    chain.three()

    d_norm, gain_one_grad = norm_back(tokens[...].astype(full), gain_one[...], working[...])
    input_rows[...] = (d_resid[...] + d_norm).astype(low)
    bias_grad = jnp.sum(d_qkv[...].astype(full), 0, keepdims=True)
    vectors = jnp.concatenate([gain_one_grad, gain_two_grad, bias_grad], 1)
    part = vectors.shape[1] // 8
    for r in range(8):
        vector_in[0, r : r + 1] = vectors[:, r * part : (r + 1) * part]
    vector_send[0].start()
    sum_qkv.start_first()
    vector_send[0].wait_recv()
    vector_in[2] = vector_in[0] + vector_in[1]
    vector_send[1].start()

    gu_first[2].wait_recv()
    gu_second[0].wait_recv()
    total = gu_own[:, :units].astype(full) + gu_x[0].astype(full) + gu_ended[0].astype(full)
    gu_own[:, :units] = total.astype(low)
    gu_first[3].wait_recv()
    gu_second[1].wait_recv()
    total = gu_own[:, units:].astype(full) + gu_y[0].astype(full) + gu_ended[1].astype(full)
    gu_own[:, units:] = total.astype(low)
    for copy in gu_send:
        copy.start()
    keep_rows = here(rows_for(gu_own, 0, 0), gu_rows.at[0], 6)
    keep_rows.start()
    sum_out.start_second()
    vector_send[1].wait_recv()
    vector_in[4] = vector_in[2] + vector_in[3]
    vector_send[2].start()

    sum_qkv.start_second()
    sum_out.finish()
    chain_out.one()
    vector_send[2].wait_recv()
    vector_in[6] = vector_in[4] + vector_in[5]
    for copy in vector_send[3:]:
        copy.start()
    chain_out.add_one()
    chain_out.two()
    sum_qkv.finish()
    chain_qkv.one()
    chain_out.three()
    chain.last(working)
    layer[...] = (resid[...] + working[...]).astype(low)
    chain_qkv.add_one()
    chain_qkv.two()
    for copy in vector_send[3:]:
        copy.wait_recv()
    vector[...] = vector_in[6] + vector_in[7] + vector_in[8] + vector_in[9]
    chain_out.last(grad_out)
    chain_qkv.three()
    chain_qkv.last(grad_qkv)
    for copy in gu_send:
        copy.wait_recv()
    keep_rows.wait()
    for part in (chain_out, chain_qkv):
        part.one_sent()
        part.sent()
    chain.sent()
    sum_out.sent()
    sum_qkv.sent()
    for copy in gu_first + gu_second + gu_send + vector_send:
        copy.wait_send()
    for g in range(KV_HEADS):
        for copy in dkv_send[g]:
            copy.wait_send()


def back(
    columns, resid, gain_two, cotangent, attended, queries, paired, slots, slot_row, first_row,
    logsum, normed_one, tokens, gain_one, cosine, sine, w_out, w_qkv, gu_sum, branch,
):
    rows, width = tokens.shape
    n_s = paired.shape[0]
    group = n_s * rows
    kv_width = KV_HEADS * HEAD_DIM
    qkv_width = width + 2 * kv_width
    block = width // 8
    piece = block // n_s
    units = gu_sum.shape[2] // 2
    low, full = jnp.bfloat16, jnp.float32
    vmem = pl.BlockSpec(memory_space=pltpu.VMEM)
    hbm = pl.BlockSpec(memory_space=pl.ANY)
    shape = jax.ShapeDtypeStruct
    vectors = (2 * width + qkv_width) // 8
    return pl.pallas_call(
        back_kernel,
        in_specs=[hbm] + [vmem] * 15 + [hbm] * 4,
        out_specs=[vmem] * 5 + [hbm],
        out_shape=[
            shape((rows, width), low),
            shape((rows, width), low),
            shape((8, vectors), full),
            shape((piece, width), full),
            shape((piece, qkv_width), full),
            shape((n_s, piece, 2 * units), low),
        ],
        scratch_shapes=[
            pltpu.VMEM((width, width), low),
            pltpu.VMEM((width, qkv_width), low),
            pltpu.VMEM((block, 2 * units), low),
            pltpu.VMEM((block, units), low),
            pltpu.VMEM((block, units), low),
            pltpu.VMEM((2, block, units), low),
            pltpu.VMEM((2, block, units), low),
            pltpu.VMEM((2, block, units), low),
            pltpu.VMEM((group, width), low),
            pltpu.VMEM((rows, width), low),
            pltpu.VMEM((2, rows, width), low),
            pltpu.VMEM((2, rows, width), low),
            pltpu.VMEM((rows, width), full),
            pltpu.VMEM((group, rows), full),
            pltpu.VMEM((rows, width), low),
            pltpu.VMEM((rows, width), low),
            pltpu.VMEM((rows, qkv_width), low),
            pltpu.VMEM((rows, width), full),
            pltpu.VMEM((group, HEAD_DIM), full),
            pltpu.VMEM((group, HEAD_DIM), full),
            pltpu.VMEM((KV_HEADS, n_s, rows, 2 * HEAD_DIM), low),
            pltpu.VMEM((KV_HEADS, n_s, rows, 2 * HEAD_DIM), low),
            pltpu.VMEM((4, block, width), low),
            pltpu.VMEM((2, block, width // 2), low),
            pltpu.VMEM((2, block, width // 2), low),
            pltpu.VMEM((2, block, width // 2), low),
            pltpu.VMEM((4, block, qkv_width), low),
            pltpu.VMEM((2, block, qkv_width // 2), low),
            pltpu.VMEM((2, block, qkv_width // 2), low),
            pltpu.VMEM((2, block, qkv_width // 2), low),
            pltpu.VMEM((piece, width), low),
            pltpu.VMEM((2, piece, width), low),
            pltpu.VMEM((2, piece, width), low),
            pltpu.VMEM((piece, qkv_width), low),
            pltpu.VMEM((2, piece, qkv_width), low),
            pltpu.VMEM((2, piece, qkv_width), low),
            pltpu.VMEM((10, 8, vectors), full),
            pltpu.SemaphoreType.DMA((10,)),
            pltpu.SemaphoreType.DMA((68,)),
            pltpu.SemaphoreType.DMA((68,)),
        ],
        compiler_params=pltpu.CompilerParams(
            collective_id=2, has_side_effects=True, vmem_limit_bytes=63 * 2**20
        ),
        name="back",
    )(
        columns, resid, gain_two, cotangent, attended, queries, paired, slots, slot_row, first_row,
        logsum, normed_one, tokens, gain_one, cosine, sine, w_out, w_qkv, gu_sum, branch,
    )


def finish_kernel(
    layer, input_rows, grad_out, grad_qkv, grad_down, gu_rows,
    layer_out, input_grad, out_out, query_out, key_out, value_out, down_out, gate_out, up_out,
    layer_v, input_v, out_v, qkv_v, down_v, gu_v, gate_v, up_v, load, store,
):
    s = lax.axis_index("seq")
    n_s = gu_rows.shape[0]
    width = grad_out.shape[1]
    kv_width = KV_HEADS * HEAD_DIM
    unit_pad = grad_down.shape[0]
    unit = down_out.shape[0]
    units = gu_rows.shape[2] // 2
    moves = [
        (layer, layer_v, [(layer_v, layer_out)]),
        (input_rows, input_v, [(input_v, input_grad)]),
        (grad_down, down_v, [(down_v.at[:unit], down_out)]),
        (grad_out, out_v, [(out_v, out_out)]),
        (grad_qkv, qkv_v, [
            (qkv_v.at[:, :width], query_out),
            (qkv_v.at[:, width : width + kv_width], key_out),
            (qkv_v.at[:, width + kv_width :], value_out),
        ]),
    ]
    load_gu = pltpu.make_async_copy(gu_rows, gu_v, load.at[0])
    load_gu.start()
    loads, stores = [], []
    for i, (source, place, _) in enumerate(moves):
        loads.append(pltpu.make_async_copy(source, place, load.at[1 + i]))
        loads[-1].start()
    for copy, (_, _, parts) in zip(loads, moves):
        copy.wait()
        for source, target in parts:
            stores.append(pltpu.make_async_copy(source, target, store.at[len(stores)]))
            stores[-1].start()
    load_gu.wait()
    window = 512
    lanes = lax.broadcasted_iota(jnp.int32, (gu_rows.shape[1], 128), 1)
    for base, out, target_out in ((0, gate_v, gate_out), (units, up_v, up_out)):
        for f in range(units // unit_pad):
            for owner in range(n_s):
                source = base + f * unit_pad
                begin = min(source // 128 * 128, 2 * units - window)
                target = (f * n_s + owner) * unit
                first = target // 128 * 128
                slot = lax.rem(s + n_s - owner, n_s)
                value = gu_v[slot, :, begin : begin + window].astype(jnp.float32)
                turn = ((target - first) - (source - begin)) % window
                if turn:
                    value = pltpu.roll(value, turn, 1)
                for t in range(first, min(target + unit, out.shape[1]), 128):
                    part = value[:, t - first : t - first + 128]
                    if t < target:
                        part = jnp.where(lanes >= target - t, part, out[:, t : t + 128])
                    out[:, t : t + 128] = part
        stores.append(pltpu.make_async_copy(out, target_out, store.at[len(stores)]))
        stores[-1].start()
    for copy in stores:
        copy.wait()


def finish(layer, input_rows, grad_out, grad_qkv, grad_down, gu_rows, unit, hidden_width):
    piece, width = grad_out.shape
    kv_width = KV_HEADS * HEAD_DIM
    low, full = jnp.bfloat16, jnp.float32
    shape = jax.ShapeDtypeStruct
    hbm = pl.BlockSpec(memory_space=pl.ANY)
    wide = pltpu.VMEM((piece, hidden_width), full)
    return pl.pallas_call(
        finish_kernel,
        in_specs=[hbm] * 6,
        out_specs=[hbm] * 9,
        out_shape=[
            shape(layer.shape, low),
            shape(layer.shape, low),
            shape((piece, width), full),
            shape((piece, width), full),
            shape((piece, kv_width), full),
            shape((piece, kv_width), full),
            shape((unit, width), full),
            shape((piece, hidden_width), full),
            shape((piece, hidden_width), full),
        ],
        scratch_shapes=[
            pltpu.VMEM(value.shape, value.dtype)
            for value in (layer, input_rows, grad_out, grad_qkv, grad_down, gu_rows)
        ] + [wide, wide, pltpu.SemaphoreType.DMA((6,)), pltpu.SemaphoreType.DMA((9,))],
        compiler_params=pltpu.CompilerParams(vmem_limit_bytes=63 * 2**20),
        name="finish",
    )(layer, input_rows, grad_out, grad_qkv, grad_down, gu_rows)


def per_device(
    tokens, cotangent, lengths, balance, norm1_gain, w_query, b_query, w_key, b_key,
    w_value, b_value, w_out, norm2_gain, w_gate, w_up, w_down,
):
    seq_count = lax.axis_size("seq")
    fsdp_count = lax.axis_size("fsdp")
    seq_rank = lax.axis_index("seq")
    fsdp_rank = lax.axis_index("fsdp")
    rows_here, width = tokens.shape
    kv_width = KV_HEADS * HEAD_DIM
    hidden_width = w_gate.shape[1]
    unit = hidden_width // (fsdp_count * seq_count)
    (
        weight_gu, weight_down, upstream_all, normed_all, hidden, factor_gate, factor_up,
        weight_qkv, weight_out, queries, paired, slots, logsum, attended, resid, normed_one,
        gain_one, gain_two, slot_row, first_row, cosine, sine,
    ) = front(
        tokens, cotangent, lengths, balance, (norm1_gain, norm2_gain, b_query, b_key, b_value),
        (w_query, w_key, w_value, w_out, w_gate, w_up, w_down),
    )
    columns, grad_down, gu_sum, branch = ffn(
        normed_all, upstream_all, weight_gu, weight_down, hidden, factor_gate, factor_up
    )
    layer, input_rows, vectors, grad_out, grad_qkv, gu_rows = back(
        columns, resid, gain_two, cotangent, attended, queries, paired, slots, slot_row, first_row,
        logsum, normed_one, tokens, gain_one, cosine, sine, weight_out, weight_qkv, gu_sum, branch,
    )
    (
        layer_out, input_grad, grad_out, grad_query, grad_key, grad_value, grad_down, grad_gate,
        grad_up,
    ) = finish(layer, input_rows, grad_out, grad_qkv, grad_down, gu_rows, unit, hidden_width)
    vectors = vectors.reshape(-1)
    own = width // (fsdp_count * seq_count)
    first = (fsdp_rank * seq_count + seq_rank) * own

    def own_part(offset):
        return lax.dynamic_slice_in_dim(vectors, offset + first, own, 0)

    biases = 2 * width
    return (
        layer_out,
        input_grad,
        own_part(0),
        grad_query,
        own_part(biases),
        grad_key,
        vectors[biases + width : biases + width + kv_width],
        grad_value,
        vectors[biases + width + kv_width :],
        grad_out,
        own_part(width),
        grad_gate,
        grad_up,
        grad_down,
    )


def solution(mesh):
    both = P(("fsdp", "seq"), None)
    both_one = P(("fsdp", "seq"))
    placed = (
        both, both, P("fsdp", None), both_one, P("fsdp"), P("fsdp", None), P("fsdp"),
        P("fsdp", None), P("fsdp"), P("fsdp", None), P("fsdp"), P("fsdp", None), P("fsdp"),
        P("fsdp", None), P("fsdp", None), P("fsdp", None),
    )
    return jax.shard_map(
        per_device if mesh.shape["fsdp"] == 8 else plain_device,
        mesh=mesh,
        in_specs=placed,
        out_specs=(
            both, both, both_one, both, both_one, both, P(), both, P(), both, both_one,
            both, both, both,
        ),
        check_vma=False,
    )
```

```python
import jax
import jax.numpy as jnp
import numpy as np
from jax import lax
from jax.experimental import pallas as pl
from jax.experimental.pallas import tpu as pltpu
from jax.sharding import PartitionSpec as P

HEADS = 12
KV_HEADS = 2
HEAD_DIM = 128

MESH = pl.DeviceIdType.MESH

epsilon = 1e-06
rope_base = 1000000.0


def norm_piece(values, gain):
    return values * lax.rsqrt(jnp.mean(values * values, -1, keepdims=True) + epsilon) * gain


def rope_tables(position):
    half = HEAD_DIM // 2
    inverse = rope_base ** (-(jnp.arange(half, dtype=jnp.float32) * 2.0 / HEAD_DIM))
    angle = position.astype(jnp.float32)[:, None] * inverse[None, :]
    cosine = jnp.concatenate([jnp.cos(angle), jnp.cos(angle)], -1)
    sine = jnp.concatenate([jnp.sin(angle), jnp.sin(angle)], -1)
    return (cosine, sine)


def turn_half(values):
    half = values.shape[-1] // 2
    return jnp.concatenate([-values[..., half:], values[..., :half]], -1)


def rotate(values, cosine, sine):
    return values * cosine[:, None, :] + turn_half(values) * sine[:, None, :]


def rotate_back(grads, cosine, sine):
    return grads * cosine[:, None, :] - turn_half(grads * sine[:, None, :])


def segment_of(slots, starts):
    return (slots >= starts[1]).astype(jnp.int32) + (slots >= starts[2]).astype(jnp.int32)


def contract_rows(left, right):
    return lax.dot_general(
        left, right, (((0,), (0,)), ((), ())), preferred_element_type=jnp.float32
    )


def contract_columns(left, right):
    return lax.dot_general(
        left, right, (((1,), (1,)), ((), ())), preferred_element_type=jnp.float32
    )


def plain_device(
    tokens, cotangent, lengths, balance, norm1_gain, w_query, b_query, w_key, b_key,
    w_value, b_value, w_out, norm2_gain, w_gate, w_up, w_down,
):
    seq_count = lax.axis_size("seq")
    fsdp_count = lax.axis_size("fsdp")
    seq_rank = lax.axis_index("seq")
    rows_here, width = tokens.shape
    group = seq_count * rows_here
    kv_width = KV_HEADS * HEAD_DIM
    qkv_width = width + 2 * kv_width
    hidden_width = w_gate.shape[1]
    unit = hidden_width // (fsdp_count * seq_count)
    own_units = hidden_width // seq_count
    weight_rows = w_gate.shape[0]
    score_scale = HEAD_DIM ** (-0.5)
    repeat = HEADS // KV_HEADS

    slot = balance % group
    slots_all = lax.all_gather(slot, "seq", axis=0, tiled=True)
    seq_lengths = lengths[0]
    starts = jnp.cumsum(seq_lengths) - seq_lengths
    segment = segment_of(slot, starts)
    segments_all = segment_of(slots_all, starts)
    first_row = jnp.where(segment == 0, starts[0], jnp.where(segment == 1, starts[1], starts[2]))
    cosine, sine = rope_tables(slot - first_row)
    allowed = (segment[:, None] == segments_all[None, :]) & (slots_all[None, :] <= slot[:, None])

    small = jnp.concatenate([norm1_gain, norm2_gain, b_query, b_key, b_value], 0)[None]
    small = lax.all_gather(small, "fsdp", axis=0, tiled=True)
    piece = norm1_gain.shape[0]
    bias_piece = b_key.shape[0]
    gain_one = small[:, :piece].reshape(-1).astype(jnp.float32)
    gain_two = small[:, piece : 2 * piece].reshape(-1).astype(jnp.float32)
    bias_qkv = jnp.concatenate(
        [
            small[:, 2 * piece : 3 * piece].reshape(-1),
            small[:, 3 * piece : 3 * piece + bias_piece].reshape(-1),
            small[:, 3 * piece + bias_piece :].reshape(-1),
        ],
        0,
    ).astype(jnp.float32)
    weight_qkv = lax.all_gather(
        jnp.concatenate([w_query, w_key, w_value], 1), "fsdp", axis=0, tiled=True
    )
    weight_out = lax.all_gather(w_out, "fsdp", axis=0, tiled=True)
    upstream_all = lax.all_gather(cotangent, "seq", axis=0, tiled=True)

    def own_columns(weight):
        cut = weight.reshape(weight_rows, fsdp_count, seq_count, unit)
        return lax.dynamic_index_in_dim(cut, seq_rank, 2, False).reshape(weight_rows, own_units)

    weight_gu = lax.all_gather(
        jnp.concatenate([own_columns(w_gate), own_columns(w_up)], 1), "fsdp", axis=0, tiled=True
    )
    weight_down = lax.all_gather(
        lax.dynamic_slice_in_dim(w_down, seq_rank * unit, unit, 0), "fsdp", axis=0, tiled=True
    )

    inputs = tokens.astype(jnp.float32)
    normed_one = norm_piece(inputs, gain_one).astype(jnp.bfloat16)
    projected = jnp.dot(normed_one, weight_qkv, preferred_element_type=jnp.float32) + bias_qkv
    query_pre = projected[:, :width].reshape(rows_here, HEADS, HEAD_DIM)
    key_pre = projected[:, width : width + kv_width].reshape(rows_here, KV_HEADS, HEAD_DIM)
    value_pre = projected[:, width + kv_width :]
    queries = rotate(query_pre, cosine, sine).astype(jnp.bfloat16)
    keys = rotate(key_pre, cosine, sine).astype(jnp.bfloat16).reshape(rows_here, kv_width)
    values = value_pre.astype(jnp.bfloat16)
    paired = lax.all_gather(jnp.concatenate([keys, values], 1), "seq", axis=0, tiled=True)
    keys_all = paired[:, :kv_width].reshape(group, KV_HEADS, HEAD_DIM)
    values_all = paired[:, kv_width:].reshape(group, KV_HEADS, HEAD_DIM)
    grouped = queries.reshape(rows_here, KV_HEADS, repeat, HEAD_DIM)
    raw = (
        jnp.einsum("qgrd,kgd->grqk", grouped, keys_all, preferred_element_type=jnp.float32)
        * score_scale
    )
    scores = jnp.where(allowed, raw, -jnp.inf)
    expo = jnp.exp(scores - jnp.max(scores, -1, keepdims=True))
    probs = expo / jnp.sum(expo, -1, keepdims=True)
    probs_low = probs.astype(jnp.bfloat16)
    attended = jnp.einsum(
        "grqk,kgd->qgrd", probs_low, values_all, preferred_element_type=jnp.float32
    )
    attended = attended.astype(jnp.bfloat16).reshape(rows_here, width)
    resid = inputs + jnp.dot(attended, weight_out, preferred_element_type=jnp.float32)
    normed_two = norm_piece(resid, gain_two).astype(jnp.bfloat16)

    normed_all = lax.all_gather(normed_two, "seq", axis=0, tiled=True)
    both = jnp.dot(normed_all, weight_gu, preferred_element_type=jnp.float32)
    gate = both[:, :own_units]
    up = both[:, own_units:]
    sigma = jax.nn.sigmoid(gate)
    activated = gate * sigma
    hidden = (activated * up).astype(jnp.bfloat16)
    d_hidden = contract_columns(upstream_all, weight_down)
    d_gate = (d_hidden * up * sigma * (1.0 + gate * (1.0 - sigma))).astype(jnp.bfloat16)
    d_up = (d_hidden * activated).astype(jnp.bfloat16)
    d_both = jnp.concatenate([d_gate, d_up], 1)
    columns = lax.psum_scatter(
        contract_columns(d_both, weight_gu).astype(jnp.bfloat16),
        "seq", scatter_dimension=0, tiled=True,
    ).astype(jnp.float32)
    branch = lax.psum_scatter(
        jnp.dot(hidden, weight_down, preferred_element_type=jnp.float32).astype(jnp.bfloat16),
        "seq", scatter_dimension=0, tiled=True,
    ).astype(jnp.float32)
    layer_out = (resid + branch).astype(jnp.bfloat16)
    grad_down = lax.psum_scatter(
        contract_rows(hidden, upstream_all).astype(jnp.bfloat16),
        "fsdp", scatter_dimension=0, tiled=True,
    ).astype(jnp.float32)
    grad_pair = lax.psum_scatter(
        contract_rows(normed_all, d_both).astype(jnp.bfloat16),
        "fsdp", scatter_dimension=0, tiled=True,
    )
    grad_pair = lax.all_to_all(grad_pair, "seq", split_axis=0, concat_axis=0, tiled=True)
    grad_pair = grad_pair.reshape(seq_count, weight_rows // seq_count, 2, fsdp_count, unit)
    grad_pair = grad_pair.transpose(2, 1, 3, 0, 4).astype(jnp.float32)
    grad_pair = grad_pair.reshape(2, weight_rows // seq_count, hidden_width)

    _, pull_two = jax.vjp(norm_piece, resid, gain_two)
    d_resid_norm, grad_gain_two = pull_two(columns)
    d_resid = cotangent.astype(jnp.float32) + d_resid_norm
    d_branch = d_resid.astype(jnp.bfloat16)
    grad_out = contract_rows(attended, d_branch).astype(jnp.bfloat16)
    d_attended = contract_columns(d_branch, weight_out).astype(jnp.bfloat16)
    d_attended = d_attended.reshape(rows_here, KV_HEADS, repeat, HEAD_DIM)
    d_probs = jnp.einsum(
        "qgrd,kgd->grqk", d_attended, values_all, preferred_element_type=jnp.float32
    )
    delta = jnp.sum(probs * d_probs, -1, keepdims=True)
    d_score = (probs * (d_probs - delta)).astype(jnp.bfloat16)
    d_queries = (
        jnp.einsum("grqk,kgd->qgrd", d_score, keys_all, preferred_element_type=jnp.float32)
        * score_scale
    )
    d_keys = (
        jnp.einsum("grqk,qgrd->kgd", d_score, grouped, preferred_element_type=jnp.float32)
        * score_scale
    )
    d_values = jnp.einsum(
        "grqk,qgrd->kgd", probs_low, d_attended, preferred_element_type=jnp.float32
    )
    d_paired = jnp.concatenate([d_keys.reshape(group, kv_width), d_values.reshape(group, kv_width)], 1)
    d_paired = lax.psum_scatter(
        d_paired.astype(jnp.bfloat16), "seq", scatter_dimension=0, tiled=True
    ).astype(jnp.float32)
    d_query_pre = rotate_back(
        d_queries.reshape(rows_here, HEADS, HEAD_DIM), cosine, sine
    ).astype(jnp.bfloat16)
    d_key_pre = rotate_back(
        d_paired[:, :kv_width].reshape(rows_here, KV_HEADS, HEAD_DIM), cosine, sine
    ).astype(jnp.bfloat16)
    d_value_pre = d_paired[:, kv_width:].astype(jnp.bfloat16)
    d_qkv = jnp.concatenate(
        [
            d_query_pre.reshape(rows_here, width),
            d_key_pre.reshape(rows_here, kv_width),
            d_value_pre,
        ],
        1,
    )
    grad_qkv = contract_rows(normed_one, d_qkv).astype(jnp.bfloat16)
    grad_bias = jnp.sum(d_qkv.astype(jnp.float32), 0)
    d_normed_one = contract_columns(d_qkv, weight_qkv)
    _, pull_one = jax.vjp(norm_piece, inputs, gain_one)
    d_input_norm, grad_gain_one = pull_one(d_normed_one)
    input_grad = (d_resid + d_input_norm).astype(jnp.bfloat16)

    def summed(value):
        value = lax.psum_scatter(value, "fsdp", scatter_dimension=0, tiled=True)
        return lax.psum_scatter(value, "seq", scatter_dimension=0, tiled=True).astype(jnp.float32)

    grad_out = summed(grad_out)
    grad_qkv = summed(grad_qkv)
    vectors = lax.psum(
        jnp.concatenate([grad_gain_one, grad_gain_two, grad_bias], 0), ("fsdp", "seq")
    )
    own = width // (fsdp_count * seq_count)
    first = (lax.axis_index("fsdp") * seq_count + seq_rank) * own

    def own_part(offset):
        return lax.dynamic_slice_in_dim(vectors, offset + first, own, 0)

    biases = 2 * width
    return (
        layer_out,
        input_grad,
        own_part(0),
        grad_qkv[:, :width],
        own_part(biases),
        grad_qkv[:, width : width + kv_width],
        vectors[biases + width : biases + width + kv_width],
        grad_qkv[:, width + kv_width :],
        vectors[biases + width + kv_width :],
        grad_out,
        own_part(width),
        grad_pair[0],
        grad_pair[1],
        grad_down,
    )


SEQ = 4


class SumChain:
    def __init__(self, held, z_one, z_two, z_three, there, index):
        self.rank = lax.axis_index("seq")
        s = self.rank
        self.held, self.arrived = held, (z_one, z_two, z_three)
        self.up = [
            there(held(1), z_one, index, seq=s + 1),
            there(held(2), z_two.at[0], index + 2, seq=s + 1),
            there(held(3), z_three.at[0], index + 4, seq=s + 1),
        ]
        self.down = [
            there(held(3), z_one, index + 1, seq=s - 1),
            there(held(2), z_two.at[1], index + 3, seq=s - 1),
            there(held(1), z_three.at[1], index + 5, seq=s - 1),
        ]

    def add(self, j, arrived):
        ref = self.held(j)
        ref[...] = ref[...] + arrived[...]

    def one(self):
        pl.when(self.rank == 0)(self.up[0].start)
        pl.when(self.rank == 3)(self.down[0].start)

    def add_one(self):
        @pl.when(self.rank == 1)
        def _():
            self.up[0].wait_recv()
            self.add(2, self.arrived[0])

        @pl.when(self.rank == 2)
        def _():
            self.down[0].wait_recv()
            self.add(2, self.arrived[0])

    def two(self):
        pl.when(self.rank <= 1)(self.up[1].start)
        pl.when(self.rank >= 2)(self.down[1].start)

    def add_two(self):
        @pl.when((self.rank == 1) | (self.rank == 2))
        def _():
            self.up[1].wait_recv()
            self.add(3, self.arrived[1].at[0])
            self.down[1].wait_recv()
            self.add(1, self.arrived[1].at[1])

    def three(self):
        pl.when(self.rank <= 2)(self.up[2].start)
        pl.when(self.rank >= 1)(self.down[2].start)

    def last(self, out):
        out[...] = self.held(0)[...].astype(jnp.float32)

        @pl.when(self.rank >= 1)
        def _():
            self.up[2].wait_recv()
            out[...] += self.arrived[2][0].astype(jnp.float32)

        @pl.when(self.rank <= 2)
        def _():
            self.down[2].wait_recv()
            out[...] += self.arrived[2][1].astype(jnp.float32)

    def one_sent(self):
        pl.when(self.rank == 0)(self.up[0].wait_send)
        pl.when(self.rank == 3)(self.down[0].wait_send)

    def two_sent(self):
        pl.when(self.rank <= 1)(self.up[1].wait_send)
        pl.when(self.rank >= 2)(self.down[1].wait_send)

    def three_sent(self):
        pl.when(self.rank <= 2)(self.up[2].wait_send)
        pl.when(self.rank >= 1)(self.down[2].wait_send)


class SumPlane:
    def __init__(self, buffer, block, plane, arrived, by_x, by_y, ended, there, index):
        half = buffer.shape[1] // 2
        low, high = pl.ds(0, half), pl.ds(half, half)

        def part(k):
            return buffer.at[pl.ds(pl.multiple_of(plane[k] * block, 16), block)]

        self.parts = own, to_x, to_y, to_both = [part(k) for k in (0, 2, 4, 6)]
        self.arrived, self.by_x, self.by_y, self.ended, self.half = arrived, by_x, by_y, ended, half
        self.core = [
            there(part(2 * i + 1), arrived.at[i], index + i, fsdp=plane[1]) for i in range(4)
        ]
        self.first = [
            there(to_both.at[:, low], by_x.at[1], index + 5, fsdp=plane[2]),
            there(to_both.at[:, high], by_y.at[1], index + 7, fsdp=plane[4]),
            there(to_x.at[:, low], by_x.at[0], index + 4, fsdp=plane[2]),
            there(to_y.at[:, high], by_y.at[0], index + 6, fsdp=plane[4]),
        ]
        self.second = [
            there(to_y.at[:, low], ended.at[0], index + 8, fsdp=plane[4]),
            there(to_x.at[:, high], ended.at[1], index + 9, fsdp=plane[2]),
        ]

    def start_core(self):
        for copy in self.core:
            copy.start()

    def start_first(self):
        for i in (3, 1, 2, 0):
            self.core[i].wait_recv()
            part = self.parts[i]
            part[...] = part[...] + self.arrived[i]
        for copy in self.first:
            copy.start()

    def start_second(self):
        half = self.half
        _, to_x, to_y, _ = self.parts
        self.first[0].wait_recv()
        to_y[:, :half] = to_y[:, :half] + self.by_x[1]
        self.second[0].start()
        self.first[1].wait_recv()
        to_x[:, half:] = to_x[:, half:] + self.by_y[1]
        self.second[1].start()

    def finish(self):
        half = self.half
        own = self.parts[0]
        self.first[2].wait_recv()
        self.second[0].wait_recv()
        total = own[:, :half].astype(jnp.float32) + self.by_x[0].astype(jnp.float32)
        own[:, :half] = (total + self.ended[0].astype(jnp.float32)).astype(jnp.bfloat16)
        self.first[3].wait_recv()
        self.second[1].wait_recv()
        total = own[:, half:].astype(jnp.float32) + self.by_y[0].astype(jnp.float32)
        own[:, half:] = (total + self.ended[1].astype(jnp.float32)).astype(jnp.bfloat16)

    def sent(self):
        for copy in self.core + self.first + self.second:
            copy.wait_send()


def block_at(place):
    far = 2 * (lax.axis_index("seq") // 2)
    return (1 + far, 2, 3 - far, 0)[place]


def in_order(partial, rows):
    far = 2 * (lax.axis_index("seq") // 2)
    places = {0: 3, 1: far, 2: 1, 3: 2 - far}

    def held(j):
        return partial.at[pl.ds(pl.multiple_of(places[j] * rows, rows), rows)]

    return held


def front_kernel(
    lengths, tokens, cotangent, small, balance, inverse,
    w_query, w_key, w_value, w_out, w_gate, w_up, w_down,
    gu_all, down_all, upstream_all, normed_all, hidden, factor_gate, factor_up, qkv_out, out_out,
    queries, paired_out, slots_out, logsum, attended, resid, normed_one, gain_one, gain_two,
    slot_row, first_row, cosine, sine,
    q_w, kv_w, out_w, gate_v, up_v, gu, normed, kv, small_own, small_all, slots_all, bias,
    cotangent_v, down_raw, down_own, hidden_v, gate_part, up_part,
    local, ssem, rsem, zsend, zrecv,
):
    f = lax.axis_index("fsdp")
    s = lax.axis_index("seq")
    rows, width = tokens.shape
    n_f, n_s = 8, slots_all.shape[0]
    group = n_s * rows
    block = w_query.shape[0]
    unit_pad = down_own.shape[0]
    unit = w_gate.shape[1] // (n_f * n_s)
    units = n_f * unit_pad
    kv_width = KV_HEADS * HEAD_DIM
    qkv_width = width + 2 * kv_width
    scale = HEAD_DIM ** (-0.5)
    repeat = HEADS // KV_HEADS
    plane = [f ^ k for k in range(n_f)]

    entry = pltpu.get_barrier_semaphore()
    for k in range(1, n_f):
        pl.semaphore_signal(entry, inc=1, device_id={"fsdp": plane[k]}, device_id_type=MESH)
    for j in range(1, n_s):
        pl.semaphore_signal(
            entry, inc=1, device_id={"seq": lax.rem(s + j, n_s)}, device_id_type=MESH
        )

    def here(source, target, index):
        return pltpu.make_async_copy(source, target, local.at[index])

    def there(source, target, index, **device):
        return pltpu.make_async_remote_copy(
            src_ref=source, dst_ref=target, send_sem=ssem.at[index], recv_sem=rsem.at[index],
            device_id=device, device_id_type=MESH,
        )

    def own_rows(ref, owner, size, start=0, count=None):
        first = pl.multiple_of(owner * size + start, 16)
        return ref.at[pl.ds(first, size if count is None else count)]

    class Gather:
        def __init__(self, source, target, size, index):
            half = size // 2
            x, y, c = plane[2], plane[4], plane[1]
            self.own = here(source, own_rows(target, f, size), index // 8) if source is not None else None
            if source is None:
                source = own_rows(target, f, size)
            mine = own_rows(target, f, size)
            self.first = [
                there(source, mine, index, fsdp=x),
                there(source, mine, index + 1, fsdp=y),
                there(source, mine, index + 2, fsdp=c),
            ]
            from_x, from_y = own_rows(target, x, size), own_rows(target, y, size)
            part_x = own_rows(target, x, size, 0, half)
            part_y = own_rows(target, y, size, half, half)
            self.second = [
                there(part_x, part_x, index + 3, fsdp=y),
                there(part_y, part_y, index + 4, fsdp=x),
                there(from_x, from_x, index + 5, fsdp=c),
                there(from_y, from_y, index + 6, fsdp=c),
            ]
            diagonal = own_rows(target, plane[6], size)
            self.third = there(diagonal, diagonal, index + 7, fsdp=c)

        def start(self):
            if self.own is not None:
                self.own.start()
            for copy in self.first:
                copy.start()

        def forward(self):
            self.first[0].wait_recv()
            self.second[0].start()
            self.second[2].start()
            self.first[1].wait_recv()
            self.second[1].start()
            self.second[3].start()

        def last(self):
            self.second[0].wait_recv()
            self.second[1].wait_recv()
            self.third.start()

        def finish(self):
            if self.own is not None:
                self.own.wait()
            self.first[2].wait_recv()
            self.second[2].wait_recv()
            self.second[3].wait_recv()
            self.third.wait_recv()

        def sent(self):
            for copy in self.first + self.second + [self.third]:
                copy.wait_send()

    class Chain:
        def __init__(self, target, index, own=None):
            self.steps = []
            for step in range(1, n_s):
                up = own_rows(target, s - (step - 1), rows)
                down = own_rows(target, s + (step - 1), rows)
                source = own if own is not None and step == 1 else up
                i = index + 2 * (step - 1)
                self.steps.append((
                    pltpu.make_async_remote_copy(
                        src_ref=source, dst_ref=up, send_sem=zsend.at[i], recv_sem=zrecv.at[i],
                        device_id={"seq": s + 1}, device_id_type=MESH,
                    ),
                    pltpu.make_async_remote_copy(
                        src_ref=down if source is up else source, dst_ref=down, send_sem=zsend.at[i + 1], recv_sem=zrecv.at[i + 1],
                        device_id={"seq": s - 1}, device_id_type=MESH,
                    ),
                    (s >= step - 1) & (s < n_s - 1),
                    (s >= 1) & (s <= n_s - step),
                    s >= step,
                    s <= n_s - 1 - step,
                ))

        def send(self, step):
            up, down, can_up, can_down, _, _ = self.steps[step - 1]
            pl.when(can_up)(up.start)
            pl.when(can_down)(down.start)

        def receive(self, step):
            up, down, _, _, from_below, from_above = self.steps[step - 1]
            pl.when(from_below)(up.wait_recv)
            pl.when(from_above)(down.wait_recv)

        def sent(self):
            for up, down, can_up, can_down, _, _ in self.steps:
                pl.when(can_up)(up.wait_send)
                pl.when(can_down)(down.wait_send)

    own_block = pl.ds(pl.multiple_of(f * block, 16), block)
    pieces = [
        here(w_key, kv_w.at[own_block, pl.ds(0, kv_width)], 6),
        here(w_value, kv_w.at[own_block, pl.ds(kv_width, kv_width)], 7),
        here(w_query, q_w.at[own_block], 5),
        here(cotangent, cotangent_v, 8),
    ]
    load_gate = here(w_gate, gate_v, 9)
    load_up = here(w_up, up_v, 10)
    first_unit = pl.multiple_of(s * unit // 16 * 16, 16)
    load_down = here(w_down.at[pl.ds(first_unit, unit_pad)], down_raw, 15)
    for copy in pieces[:2]:
        copy.start()

    slot = (balance[...] & (group - 1)).astype(jnp.float32)
    second = lengths[0, 0].astype(jnp.float32)
    third = (lengths[0, 0] + lengths[0, 1]).astype(jnp.float32)
    first = jnp.where(slot >= third, third, jnp.where(slot >= second, second, 0.0))
    slot_row[...] = jnp.broadcast_to(slot, slot_row.shape)
    first_row[...] = jnp.broadcast_to(first, first_row.shape)
    slots_all[s] = jnp.broadcast_to(slot, (128, rows)).T
    lanes = lax.broadcasted_iota(jnp.int32, small.shape, 1)
    sorts = lax.broadcasted_iota(jnp.int32, small.shape, 0)
    small_own[...] = jnp.where(
        sorts < 3,
        pltpu.roll(small[...], lax.rem(f, 2) * block, 1),
        pltpu.roll(small[...], f * (kv_width // n_f), 1),
    )
    small_all[f] = small_own[...]

    gather_kv = Gather(None, kv_w, block, 0)
    gather_q = Gather(None, q_w, block, 8)
    gather_out = Gather(w_out, out_w, block, 16)
    gather_gu = Gather(None, gu, block, 24)
    gather_down = Gather(down_own, down_all, unit_pad, 32)
    chain_up = Chain(upstream_all, 0, cotangent_v)
    chain_normed = Chain(normed, 6)
    send_small = [
        there(small_own, small_all.at[f], 40 + k, fsdp=plane[k]) for k in range(1, n_f)
    ]
    send_slots = [
        there(slots_all.at[s], slots_all.at[s], 48 + j, seq=lax.rem(s + j, n_s))
        for j in range(1, n_s)
    ]
    send_kv = [
        there(kv.at[s], kv.at[s], 52 + j, seq=lax.rem(s + j, n_s)) for j in range(1, n_s)
    ]
    for copy in pieces[:2]:
        copy.wait()
    for copy in pieces[2:]:
        copy.start()
    pl.semaphore_wait(entry, n_f - 1 + n_s - 1)
    gather_kv.start()
    for copy in send_small + send_slots:
        copy.start()
    for copy in pieces[2:]:
        copy.wait()
    chain_up.send(1)
    load_gate.start()
    load_up.start()
    load_down.start()
    save_own = here(cotangent_v, own_rows(upstream_all, s, rows), 8)
    save_own.start()
    position = slots_all[s] - jnp.broadcast_to(first, (128, rows)).T
    angle = position * inverse[...]
    cosine[...] = jnp.cos(angle)
    sine[...] = jnp.where(
        lax.broadcasted_iota(jnp.int32, angle.shape, 1) < HEAD_DIM // 2, -1.0, 1.0
    ) * jnp.sin(angle)

    for copy in send_small + send_slots:
        copy.wait_recv()

    def joined(sort):
        return jnp.concatenate(
            [
                small_all[2 * i, sort : sort + 1] + small_all[2 * i + 1, sort : sort + 1]
                for i in range(n_f // 2)
            ],
            1,
        )

    gain_one[...] = joined(0)
    gain_two[...] = joined(1)
    bias_query = joined(2)
    bias_key = sum(small_all[i, 3:4, :kv_width] for i in range(n_f))
    bias_value = sum(small_all[i, 4:5, :kv_width] for i in range(n_f))

    inputs = tokens[...].astype(jnp.float32)
    root = lax.rsqrt(jnp.mean(inputs * inputs, -1, keepdims=True) + epsilon)
    normed_one[...] = (inputs * root * gain_one[...]).astype(jnp.bfloat16)
    gather_kv.forward()
    gather_q.start()
    gather_kv.last()
    gather_kv.finish()

    def turned(value):
        return value * cosine[...] + pltpu.roll(value, HEAD_DIM // 2, 1) * sine[...]

    rows_low = normed_one[...]
    pair = jnp.dot(rows_low, kv_w[:, :kv_width], preferred_element_type=jnp.float32)
    pair = pair + bias_key
    for g in range(KV_HEADS):
        columns = slice(g * HEAD_DIM, (g + 1) * HEAD_DIM)
        kv[s, :, columns] = turned(pair[:, columns]).astype(jnp.bfloat16)
    pair = jnp.dot(rows_low, kv_w[:, kv_width:], preferred_element_type=jnp.float32)
    kv[s, :, kv_width:] = (pair + bias_value).astype(jnp.bfloat16)
    for copy in send_kv:
        copy.start()
    save_kv_w = here(kv_w, qkv_out.at[:, pl.ds(width, 2 * kv_width)], 11)
    save_kv_w.start()

    load_gate.wait()
    load_up.wait()
    pick_units(gate_v, up_v, gu.at[own_block], w_gate.shape[1] // n_f, unit, unit_pad)
    gather_q.forward()
    gather_out.start()
    load_down.wait()
    raw = down_raw[...].astype(jnp.float32)
    shifted = jnp.concatenate([raw[8:], jnp.zeros((8, width), jnp.float32)], 0)
    raw = jnp.where(lax.rem(s * unit, 16) == 0, raw, shifted)
    inside = lax.broadcasted_iota(jnp.int32, raw.shape, 0) < unit
    down_own[...] = jnp.where(inside, raw, 0.0).astype(jnp.bfloat16)

    for j in range(n_s):
        keys_slot = slots_all[j]
        keys_slot = jnp.concatenate([keys_slot] * (rows // 128), 1)
        ok = (keys_slot <= slot) & (keys_slot >= first)
        bias[j * rows : (j + 1) * rows] = jnp.where(ok, 0.0, -1e30)

    gather_q.last()
    gather_q.finish()
    save_q_w = here(q_w, qkv_out.at[:, pl.ds(0, width)], 0)
    save_q_w.start()
    for g in range(HEADS // 2):
        columns = slice(g * 2 * HEAD_DIM, (g + 1) * 2 * HEAD_DIM)
        pair = jnp.dot(rows_low, q_w[:, columns], preferred_element_type=jnp.float32)
        pair = pair + bias_query[:, columns]
        for h in range(2):
            part = turned(pair[:, h * HEAD_DIM : (h + 1) * HEAD_DIM]).astype(jnp.bfloat16)
            queries[:, (2 * g + h) * HEAD_DIM : (2 * g + h + 1) * HEAD_DIM] = part

    gather_out.forward()
    chain_up.receive(1)
    for copy in send_kv:
        copy.wait_recv()
    chain_up.send(2)
    save_kv = here(kv, paired_out, 12)
    save_kv.start()
    slots_out[...] = slots_all[...]

    for g in range(KV_HEADS):
        keys = kv[:, :, g * HEAD_DIM : (g + 1) * HEAD_DIM].reshape(n_s * rows, HEAD_DIM)
        values = kv[:, :, kv_width + g * HEAD_DIM : kv_width + (g + 1) * HEAD_DIM]
        values = values.reshape(n_s * rows, HEAD_DIM)

        def head(i, carry, g=g, keys=keys, values=values):
            h = g * repeat + i
            columns = pl.ds(pl.multiple_of(h * HEAD_DIM, HEAD_DIM), HEAD_DIM)
            raw = lax.dot_general(
                keys, queries[:, columns], (((1,), (1,)), ((), ())),
                preferred_element_type=jnp.float32,
            )
            scores = raw * scale + bias[...]
            top = jnp.max(scores, 0, keepdims=True)
            expo = jnp.exp(scores - top)
            total = jnp.sum(expo, 0, keepdims=True)
            probs = (expo * (1.0 / total)).astype(jnp.bfloat16)
            mixed = lax.dot_general(
                values, probs, (((0,), (0,)), ((), ())), preferred_element_type=jnp.float32
            )
            attended[:, columns] = mixed.T.astype(jnp.bfloat16)
            logsum[pl.ds(pl.multiple_of(h * 8, 8), 8)] = jnp.broadcast_to(
                top + jnp.log(total), (8, rows)
            )
            return carry

        lax.fori_loop(0, repeat, head, 0)
        if g == 0:
            gather_out.last()
            gather_gu.start()

    gather_out.finish()
    save_out = here(out_w, out_out, 13)
    save_out.start()
    mixed = attended[...]
    for g in range(width // 256):
        columns = slice(g * 256, (g + 1) * 256)
        part = jnp.dot(mixed, out_w[:, columns], preferred_element_type=jnp.float32)
        resid[:, columns] = tokens[:, columns].astype(jnp.float32) + part
    value = resid[...]
    root = lax.rsqrt(jnp.mean(value * value, -1, keepdims=True) + epsilon)
    own_tokens = pl.ds(pl.multiple_of(s * rows, rows), rows)
    normed[own_tokens] = (value * root * gain_two[...]).astype(jnp.bfloat16)
    chain_normed.send(1)

    wide = hidden_v.shape[2]
    count = units // wide

    def saves(owner, t, slot):
        place = (
            pl.ds(pl.multiple_of(owner * rows, rows), rows),
            pl.ds(pl.multiple_of(t * wide, wide), wide),
        )
        return [
            here(part.at[slot], whole.at[place], 16 + 3 * slot + i)
            for i, (part, whole) in enumerate(
                ((hidden_v, hidden), (gate_part, factor_gate), (up_part, factor_up))
            )
        ]

    def feed(owner, done):
        def body(t, carry):
            slot = lax.rem(t + done, 2)
            mine = normed[pl.ds(pl.multiple_of(owner * rows, rows), rows)]
            gate_columns = pl.ds(pl.multiple_of(t * wide, wide), wide)
            up_columns = pl.ds(pl.multiple_of(units + t * wide, wide), wide)
            gate = jnp.dot(mine, gu[:, gate_columns], preferred_element_type=jnp.float32)
            up = jnp.dot(mine, gu[:, up_columns], preferred_element_type=jnp.float32)
            sigma = jax.nn.sigmoid(gate)
            activated = gate * sigma

            @pl.when(t + done >= 2)
            def _():
                for copy in saves(owner, t, slot):
                    copy.wait()

            hidden_v[slot] = (activated * up).astype(jnp.bfloat16)
            gate_part[slot] = (up * sigma * (1.0 + gate * (1.0 - sigma))).astype(jnp.bfloat16)
            up_part[slot] = activated.astype(jnp.bfloat16)
            for copy in saves(owner, t, slot):
                copy.start()
            return carry

        lax.fori_loop(0, count, body, 0)

    chain_up.receive(2)
    chain_normed.receive(1)
    chain_normed.send(2)
    gather_gu.forward()
    chain_normed.receive(2)
    chain_normed.send(3)
    gather_gu.last()
    gather_down.start()
    gather_gu.finish()
    save_gu = here(gu, gu_all, 22)
    save_gu.start()
    feed(s, 0)
    feed(s ^ 1, count)
    chain_normed.receive(3)
    chain_up.send(3)
    save_normed = here(normed, normed_all, 23)
    save_normed.start()
    feed(s ^ 2, 2 * count)
    gather_down.forward()
    feed(s ^ 3, 3 * count)
    gather_down.last()
    for t in (count - 2, count - 1):
        for copy in saves(s ^ 3, t, (t + 3 * count) % 2):
            copy.wait()
    chain_up.receive(3)
    gather_down.finish()
    for copy in (save_own, save_kv_w, save_q_w, save_kv, save_out, save_gu, save_normed):
        copy.wait()
    for part in (gather_kv, gather_q, gather_out, gather_gu, gather_down, chain_up, chain_normed):
        part.sent()
    for copy in send_small + send_slots + send_kv:
        copy.wait_send()


def pick_units(gate, up, out, stride, unit, padded):
    rank = lax.axis_index("seq")
    pieces = gate.shape[1] // stride
    half = out.shape[1] // 2
    window, tile = 512, 128
    rows = lax.broadcasted_iota(jnp.int32, (window, tile), 0)
    columns = lax.broadcasted_iota(jnp.int32, (window, tile), 1)
    for first in range(0, 2 * half, tile):
        source = gate if first < half else up
        local = first % half
        total = jnp.zeros((out.shape[0], tile), jnp.float32)
        for f in range(pieces):
            low = max(local, f * padded)
            high = min(local + tile, f * padded + unit)
            if low >= high:
                continue
            begin = f * stride + rank * unit
            base = jnp.minimum(begin // 128, (source.shape[1] - window) // 128) * 128
            base = pl.multiple_of(base, 128)
            wanted = columns + (local - f * padded + begin - base)
            inside = (columns >= low - local) & (columns < high - local)
            chosen = jnp.where((rows == wanted) & inside, 1.0, 0.0).astype(jnp.bfloat16)
            total += jnp.dot(
                source[:, pl.ds(base, window)], chosen, preferred_element_type=jnp.float32
            )
        out[:, first : first + tile] = total.astype(jnp.bfloat16)


def front(tokens, cotangent, lengths, balance, vectors, weights):
    rows, width = tokens.shape
    n_s = lax.axis_size("seq")
    w_query, w_key, w_value, w_out, w_gate, w_up, w_down = weights
    block = w_query.shape[0]
    unit_pad = -(-w_down.shape[0] // n_s // 16) * 16
    kv_width = KV_HEADS * HEAD_DIM
    qkv_width = width + 2 * kv_width
    units = 8 * unit_pad
    group = n_s * rows
    wide = 768
    low, full = jnp.bfloat16, jnp.float32
    small = sum(
        jnp.pad(v.astype(full)[None], ((i, 7 - i), (0, 2 * block - v.shape[0])))
        for i, v in enumerate(vectors)
    )
    half = HEAD_DIM // 2
    inverse = rope_base ** (-(np.arange(half, dtype=np.float32) * np.float32(2.0 / HEAD_DIM)))
    inverse = jnp.asarray(np.concatenate([inverse, inverse])[None], full)
    smem = pl.BlockSpec(memory_space=pltpu.SMEM)
    vmem = pl.BlockSpec(memory_space=pltpu.VMEM)
    hbm = pl.BlockSpec(memory_space=pl.ANY)
    shape = jax.ShapeDtypeStruct
    return pl.pallas_call(
        front_kernel,
        in_specs=[smem, vmem, hbm, vmem, vmem, vmem] + [hbm] * 7,
        out_specs=[hbm] * 9 + [vmem, hbm] + [vmem] * 11,
        out_shape=[
            shape((width, 2 * units), low),
            shape((units, width), low),
            shape((group, width), low),
            shape((group, width), low),
            shape((group, units), low),
            shape((group, units), low),
            shape((group, units), low),
            shape((width, qkv_width), low),
            shape((width, width), low),
            shape((rows, width), low),
            shape((n_s, rows, 2 * kv_width), low),
            shape((n_s, rows, 128), full),
            shape((8 * HEADS, rows), full),
            shape((rows, width), low),
            shape((rows, width), full),
            shape((rows, width), low),
            shape((1, width), full),
            shape((1, width), full),
            shape((8, rows), full),
            shape((8, rows), full),
            shape((rows, HEAD_DIM), full),
            shape((rows, HEAD_DIM), full),
        ],
        scratch_shapes=[
            pltpu.VMEM((width, width), low),
            pltpu.VMEM((width, 2 * kv_width), low),
            pltpu.VMEM((width, width), low),
            pltpu.VMEM(w_gate.shape, low),
            pltpu.VMEM(w_up.shape, low),
            pltpu.VMEM((width, 2 * units), low),
            pltpu.VMEM((group, width), low),
            pltpu.VMEM((n_s, rows, 2 * kv_width), low),
            pltpu.VMEM((8, 2 * block), full),
            pltpu.VMEM((8, 8, 2 * block), full),
            pltpu.VMEM((n_s, rows, 128), full),
            pltpu.VMEM((group, rows), full),
            pltpu.VMEM((rows, width), low),
            pltpu.VMEM((unit_pad, width), low),
            pltpu.VMEM((unit_pad, width), low),
            pltpu.VMEM((2, rows, wide), low),
            pltpu.VMEM((2, rows, wide), low),
            pltpu.VMEM((2, rows, wide), low),
            pltpu.SemaphoreType.DMA((24,)),
            pltpu.SemaphoreType.DMA((56,)),
            pltpu.SemaphoreType.DMA((56,)),
            pltpu.SemaphoreType.DMA((12,)),
            pltpu.SemaphoreType.DMA((12,)),
        ],
        compiler_params=pltpu.CompilerParams(
            collective_id=0, has_side_effects=True, vmem_limit_bytes=62 * 2**20
        ),
        name="front",
    )(
        lengths, tokens, cotangent, small, balance.reshape(1, rows), inverse,
        w_query, w_key, w_value, w_out, w_gate, w_up, w_down,
    )


def ffn_kernel(
    normed_all, upstream_all, w_gu, w_down, hidden_all, factor_gate, factor_up,
    columns, grad_down, gu_sum, branch, down_arrived, gu_arrived,
    normed, upstream, gu, down, hidden, d_both, partial, z_one, z_two, z_three,
    down_x, down_y, down_last, down_piece,
    load, ssem, rsem,
):
    f = lax.axis_index("fsdp")
    s = lax.axis_index("seq")
    n_s = SEQ
    group, width = normed.shape
    rows = group // n_s
    half_rows = group // 2
    units = down.shape[0]
    tile = 256
    tiles = units // tile
    wide = 768
    block = gu.shape[0] // 8
    unit = units // 8
    half = width // 2
    plane = [f ^ k for k in range(8)]
    full = jnp.float32

    entry = pltpu.get_barrier_semaphore()
    for k in (1, 2, 4):
        pl.semaphore_signal(entry, inc=1, device_id={"fsdp": plane[k]}, device_id_type=MESH)
    for j in (1, n_s - 1):
        pl.semaphore_signal(
            entry, inc=1, device_id={"seq": lax.rem(s + j, n_s)}, device_id_type=MESH
        )

    def here(source, target, index):
        return pltpu.make_async_copy(source, target, load.at[index])

    def there(source, target, index, **device):
        return pltpu.make_async_remote_copy(
            src_ref=source, dst_ref=target, send_sem=ssem.at[index], recv_sem=rsem.at[index],
            device_id=device, device_id_type=MESH,
        )

    def part(ref, owner, size):
        return ref.at[pl.ds(pl.multiple_of(owner * size, 16), size)]

    early, late = (0,), (1, 2, 3)

    def rows_of(p):
        return pl.ds(p * rows, rows)

    def row_loads(p):
        owner = lax.rem(s + n_s - block_at(p), n_s)
        mine = rows_of(p)
        return [
            here(part(upstream_all, owner, rows), upstream.at[mine], 5 * p),
            here(part(factor_gate, owner, rows), d_both.at[mine, pl.ds(0, units)], 5 * p + 1),
            here(part(factor_up, owner, rows), d_both.at[mine, pl.ds(units, units)], 5 * p + 2),
            here(part(hidden_all, owner, rows), hidden.at[mine], 5 * p + 3),
            here(part(normed_all, owner, rows), normed.at[mine], 5 * p + 4),
        ]

    def down_load(t):
        mine = pl.ds(pl.multiple_of(t * wide, wide), wide)
        return here(w_down.at[mine], down.at[mine], 20 + t)

    def gu_load(n):
        mine = pl.ds(pl.multiple_of(n * 512, 512), 512)
        return here(w_gu.at[mine], gu.at[mine], 23 + n)

    loads = [row_loads(p) for p in range(n_s)]
    order = [loads[0][0], down_load(0)]
    order += [loads[p][i] for i in (1, 2) for p in early]
    order += [down_load(t) for t in range(1, units // wide)]
    second = [gu_load(n) for n in range(width // 512)]
    second += [loads[p][i] for i in (0, 1, 2) for p in late]
    third = [loads[p][i] for i in (3, 4) for p in range(n_s)]
    for copy in order:
        copy.start()

    def forward(blocks, wait, following):
        for p in blocks:
            for copy in loads[p][:3]:
                copy.wait()
        for copy in following:
            copy.start()
        mine = pl.ds(blocks[0] * rows, len(blocks) * rows)

        def body(t, carry):
            if wait:
                down_load(t).wait()
            gate_columns = pl.ds(pl.multiple_of(t * wide, wide), wide)
            up_columns = pl.ds(pl.multiple_of(units + t * wide, wide), wide)
            d_hidden = lax.dot_general(
                upstream[mine], down[gate_columns], (((1,), (1,)), ((), ())),
                preferred_element_type=full,
            )
            value = d_hidden * d_both[mine, gate_columns].astype(full)
            d_both[mine, gate_columns] = value.astype(jnp.bfloat16)
            value = d_hidden * d_both[mine, up_columns].astype(full)
            d_both[mine, up_columns] = value.astype(jnp.bfloat16)
            return carry

        lax.fori_loop(0, units // wide, body, 0)

    def backward(blocks, wait):
        part_rows = pl.ds(blocks[0] * rows, len(blocks) * rows)

        def body(n, carry):
            if wait:
                gu_load(n).wait()
            out_columns = pl.ds(pl.multiple_of(n * 512, 512), 512)
            value = lax.dot_general(
                d_both[part_rows], gu[out_columns], (((1,), (1,)), ((), ())),
                preferred_element_type=full,
            )
            partial[part_rows, out_columns] = value.astype(jnp.bfloat16)
            return carry

        lax.fori_loop(0, width // 512, body, 0)

    chain = SumChain(in_order(partial, rows), z_one, z_two, z_three, there, 0)
    pieces = [(first, min(group, units - first)) for first in range(0, units, group)]
    forward((0,), True, second)
    backward((0,), True)
    pl.semaphore_wait(entry, 5)
    chain.one()
    forward((1,), False, third)
    backward((1,), False)
    forward((2, 3), False, ())
    backward((2, 3), False)
    chain.add_one()
    chain.two()

    for p in range(n_s):
        loads[p][3].wait()
        loads[p][4].wait()

    def down_body(t, carry):
        unit_rows = pl.ds(pl.multiple_of(t * tile, tile), tile)
        value = lax.dot_general(
            hidden[:, unit_rows], upstream[...], (((0,), (0,)), ((), ())),
            preferred_element_type=full,
        )
        down[unit_rows] = value.astype(jnp.bfloat16)
        return carry

    lax.fori_loop(0, tiles, down_body, 0)
    down_core = [
        there(part(down, plane[2 * i + 1], unit), down_arrived.at[i], 6 + i, fsdp=plane[1])
        for i in range(4)
    ]
    for i in (3, 1, 2, 0):
        down_core[i].start()

    again_in = [upstream] + [
        d_both.at[:count, i * width : (i + 1) * width] for i, (_, count) in enumerate(pieces[1:])
    ]
    again = [
        here(w_down.at[first : first + count], place, 36 + i)
        for i, ((first, count), place) in enumerate(zip(pieces, again_in))
    ]
    again[0].start()

    def gu_body(m, carry):
        in_columns = pl.ds(pl.multiple_of(m * tile, tile), tile)
        turned = normed[:, in_columns].T
        for first in range(0, 2 * units, units // 3):
            value = jnp.dot(turned, d_both[:, first : first + units // 3], preferred_element_type=full)
            gu[in_columns, first : first + units // 3] = value.astype(jnp.bfloat16)
        return carry

    lax.fori_loop(0, 2, gu_body, 0)

    class Arrivals:
        def __init__(self, ref, size, arrived, copies, turns, index):
            self.ref, self.size, self.copies = ref, size, copies
            self.pieces = {}
            for n, i in enumerate((3, 1, 2, 0)):
                self.pieces[i] = [
                    (here(arrived.at[i, :, columns], piece, index + 3 * (n % 2) + k), columns, piece)
                    for k, (columns, piece) in enumerate(turns[n % 2])
                ]

        def fetch(self, i):
            self.copies[i].wait_recv()
            for copy, _, _ in self.pieces[i]:
                copy.start()

        def add(self, i):
            target = part(self.ref, plane[2 * i], self.size)
            for copy, columns, piece in self.pieces[i]:
                copy.wait()
                target[:, columns] = target[:, columns] + piece[...]

    down_turns = [[(pl.ds(0, width), piece)] for piece in (down_piece.at[0], down_piece.at[1])]
    down_sum = Arrivals(down, unit, down_arrived, down_core, down_turns, 26)
    down_sum.fetch(3)
    for i, following in ((3, 1), (1, 2), (2, 0), (0, None)):
        if following is not None:
            down_sum.fetch(following)
        down_sum.add(i)
    to_x, to_y, to_both = [part(down, plane[k], unit) for k in (2, 4, 6)]
    low_half, high_half = pl.ds(0, half), pl.ds(half, half)
    down_first = [
        there(to_x.at[:, low_half], down_x.at[0], 10, fsdp=plane[2]),
        there(to_both.at[:, low_half], down_x.at[1], 11, fsdp=plane[2]),
        there(to_y.at[:, high_half], down_y.at[0], 12, fsdp=plane[4]),
        there(to_both.at[:, high_half], down_y.at[1], 13, fsdp=plane[4]),
    ]
    for copy in down_first:
        copy.start()
    chain.add_two()
    chain.three()
    lax.fori_loop(2, width // tile, gu_body, 0)
    gu_core = [
        there(part(gu, plane[2 * i + 1], block), gu_arrived.at[i], 16 + i, fsdp=plane[1])
        for i in range(4)
    ]
    for i in (3, 1, 2, 0):
        gu_core[i].start()

    for copy in again[1:]:
        copy.start()
    for copy in again:
        copy.wait()

    def branch_body(n, carry):
        out_columns = pl.ds(pl.multiple_of(n * wide, wide), wide)
        for m in range(2):
            mine = slice(m * half_rows, (m + 1) * half_rows)
            value = jnp.zeros((half_rows, wide), full)
            for i, (first, count) in enumerate(pieces):
                value += jnp.dot(
                    hidden[mine, first : first + count], again_in[i][:, out_columns],
                    preferred_element_type=full,
                )
            normed[mine, out_columns] = value.astype(jnp.bfloat16)
        return carry

    lax.fori_loop(0, width // wide, branch_body, 0)
    chain.last(columns)
    chain_branch = SumChain(in_order(normed, rows), z_one, z_two, z_three, there, 22)
    chain_branch.one()
    down_second = [
        there(to_y.at[:, low_half], down_last.at[0], 14, fsdp=plane[4]),
        there(to_x.at[:, high_half], down_last.at[1], 15, fsdp=plane[2]),
    ]
    down_first[1].wait_recv()
    to_y[:, :half] = to_y[:, :half] + down_x[1]
    down_second[0].start()
    down_first[3].wait_recv()
    to_x[:, half:] = to_x[:, half:] + down_y[1]
    down_second[1].start()
    gu_turns = [
        [(pl.ds(k * units, units), hidden.at[(2 * n + k) * block : (2 * n + k + 1) * block]) for k in range(2)]
        for n in range(2)
    ]
    gu_arrivals = Arrivals(gu, block, gu_arrived, gu_core, gu_turns, 26)
    store = [here(part(gu, plane[2 * i], block), gu_sum.at[i], 32 + i) for i in range(4)]
    gu_arrivals.fetch(3)
    for i, following in ((3, 1), (1, 2), (2, 0), (0, None)):
        if following is not None:
            gu_arrivals.fetch(following)
        gu_arrivals.add(i)
        store[i].start()
    down_first[0].wait_recv()
    down_first[2].wait_recv()
    own = part(down, f, unit)
    down_second[0].wait_recv()
    grad_down[:, :half] = (
        own[:, :half].astype(full) + down_x[0].astype(full) + down_last[0].astype(full)
    )
    down_second[1].wait_recv()
    grad_down[:, half:] = (
        own[:, half:].astype(full) + down_y[0].astype(full) + down_last[1].astype(full)
    )
    chain_branch.add_one()
    chain_branch.one_sent()
    store_branch = here(normed, branch, 39)
    store_branch.start()
    chain.one_sent()
    chain.two_sent()
    chain.three_sent()
    for copy in down_core + down_first + down_second + gu_core:
        copy.wait_send()
    for copy in store + [store_branch]:
        copy.wait()


def ffn(normed_all, upstream_all, w_gu, w_down, hidden, factor_gate, factor_up):
    group, width = normed_all.shape
    units = w_down.shape[0]
    rows = group // SEQ
    unit, block, half = units // 8, width // 8, width // 2
    low, full = jnp.bfloat16, jnp.float32
    vmem = pl.BlockSpec(memory_space=pltpu.VMEM)
    hbm = pl.BlockSpec(memory_space=pl.ANY)
    shape = jax.ShapeDtypeStruct
    return pl.pallas_call(
        ffn_kernel,
        in_specs=[hbm] * 7,
        out_specs=[vmem] * 2 + [hbm] * 4,
        out_shape=[
            shape((rows, width), full),
            shape((unit, width), full),
            shape((4, block, 2 * units), low),
            shape((group, width), low),
            shape((4, unit, width), low),
            shape((4, block, 2 * units), low),
        ],
        scratch_shapes=[
            pltpu.VMEM((group, width), low),
            pltpu.VMEM((group, width), low),
            pltpu.VMEM((width, 2 * units), low),
            pltpu.VMEM((units, width), low),
            pltpu.VMEM((group, units), low),
            pltpu.VMEM((group, 2 * units), low),
            pltpu.VMEM((group, width), low),
            pltpu.VMEM((rows, width), low),
            pltpu.VMEM((2, rows, width), low),
            pltpu.VMEM((2, rows, width), low),
            pltpu.VMEM((2, unit, half), low),
            pltpu.VMEM((2, unit, half), low),
            pltpu.VMEM((2, unit, half), low),
            pltpu.VMEM((2, unit, width), low),
            pltpu.SemaphoreType.DMA((40,)),
            pltpu.SemaphoreType.DMA((28,)),
            pltpu.SemaphoreType.DMA((28,)),
        ],
        compiler_params=pltpu.CompilerParams(
            collective_id=1, has_side_effects=True, vmem_limit_bytes=63 * 2**20
        ),
        name="ffn",
    )(normed_all, upstream_all, w_gu, w_down, hidden, factor_gate, factor_up)[:4]


def back_kernel(
    gain_two, slot_row, first_row, logsum, gain_one, cosine, sine, slots,
    resid_in, cotangent_in, attended_in, queries_in, paired_in, normed_in, tokens_in,
    columns, w_out, w_qkv, gu_sum, branch,
    layer, input_rows, vector, grad_out, grad_qkv, gu_rows,
    resid, cotangent, attended, queries, paired, normed_one, tokens,
    out_w, qkv, gu_own, gu_to_y, gu_to_x, gu_x, gu_y, gu_ended,
    branch_v, z_one, z_two, z_three, working, bias, d_branch, d_attended, d_qkv, d_resid,
    keys_grad, values_grad, dkv, dkv_in,
    out_arrived, out_x, out_y, out_ended, qkv_arrived, qkv_x, qkv_y, qkv_ended,
    out_in, qkv_one, qkv_two, qkv_three, vector_in,
    load, ssem, rsem,
):
    f = lax.axis_index("fsdp")
    s = lax.axis_index("seq")
    rows, width = tokens.shape
    n_s = paired.shape[0]
    kv_width = KV_HEADS * HEAD_DIM
    repeat = HEADS // KV_HEADS
    scale = HEAD_DIM ** (-0.5)
    block = width // 8
    piece = block // n_s
    units = gu_sum.shape[2] // 2
    tile = 256
    full, low = jnp.float32, jnp.bfloat16
    plane = [f ^ k for k in range(8)]

    entry = pltpu.get_barrier_semaphore()
    for k in (1, 2, 4):
        pl.semaphore_signal(entry, inc=1, device_id={"fsdp": plane[k]}, device_id_type=MESH)
    for j in range(1, n_s):
        pl.semaphore_signal(
            entry, inc=1, device_id={"seq": lax.rem(s + j, n_s)}, device_id_type=MESH
        )

    def here(source, target, index):
        return pltpu.make_async_copy(source, target, load.at[index])

    def there(source, target, index, **device):
        return pltpu.make_async_remote_copy(
            src_ref=source, dst_ref=target, send_sem=ssem.at[index], recv_sem=rsem.at[index],
            device_id=device, device_id_type=MESH,
        )

    low_units, high_units = pl.ds(0, units), pl.ds(units, units)
    load_branch = here(branch, branch_v, 0)
    load_out = here(w_out, out_w, 1)
    load_gu = [
        here(gu_sum.at[0], gu_own, 2),
        here(gu_sum.at[2, :, low_units], gu_to_y, 3),
        here(gu_sum.at[1, :, high_units], gu_to_x, 4),
    ]
    load_qkv = here(w_qkv, qkv, 5)
    load_columns = here(columns, working, 7)
    load_rows = [
        here(source, place, 10 + i)
        for i, (source, place) in enumerate((
            (resid_in, resid), (cotangent_in, cotangent), (attended_in, attended),
            (queries_in, queries), (paired_in, paired), (normed_in, normed_one),
            (tokens_in, tokens),
        ))
    ]
    for copy in [load_columns] + load_rows[:2] + [load_branch]:
        copy.start()

    gu_first = [
        there(gu_sum.at[3, :, low_units], gu_x.at[1], 0, fsdp=plane[2]),
        there(gu_sum.at[3, :, high_units], gu_y.at[1], 1, fsdp=plane[4]),
        there(gu_sum.at[1, :, low_units], gu_x.at[0], 2, fsdp=plane[2]),
        there(gu_sum.at[2, :, high_units], gu_y.at[0], 3, fsdp=plane[4]),
    ]
    gu_second = [
        there(gu_to_y, gu_ended.at[0], 4, fsdp=plane[4]),
        there(gu_to_x, gu_ended.at[1], 5, fsdp=plane[2]),
    ]

    def around(j):
        return {"seq": lax.rem(s + j, n_s)}

    def rows_for(ref, first, j):
        owner = lax.rem(s + j, n_s)
        return ref.at[pl.ds(pl.multiple_of(first + owner * piece, 16), piece)]

    gu_send = [there(rows_for(gu_own, 0, j), gu_rows.at[j], 5 + j, **around(j)) for j in range(1, n_s)]
    dkv_send = [
        [
            there(dkv.at[g, lax.rem(s + j, n_s)], dkv_in.at[g, j], 8 + 3 * g + j, **around(j))
            for j in range(1, n_s)
        ]
        for g in range(KV_HEADS)
    ]
    chain = SumChain(in_order(branch_v, rows), z_one, z_two, z_three, there, 16)
    sum_out = SumPlane(out_w, block, plane, out_arrived, out_x, out_y, out_ended, there, 24)
    sum_qkv = SumPlane(qkv, block, plane, qkv_arrived, qkv_x, qkv_y, qkv_ended, there, 36)

    def own_part(ref):
        return lambda j: rows_for(ref, f * block, n_s - j)

    out_send = [
        there(own_part(out_w)(n_s - j), out_in.at[j], 47 + j, **around(j)) for j in range(1, n_s)
    ]
    chain_qkv = SumChain(own_part(qkv), qkv_one, qkv_two, qkv_three, there, 54)
    vector_send = [
        there(vector_in.at[0], vector_in.at[1], 60, fsdp=plane[1]),
        there(vector_in.at[2], vector_in.at[3], 61, fsdp=plane[2]),
        there(vector_in.at[4], vector_in.at[5], 62, fsdp=plane[4]),
    ] + [there(vector_in.at[6], vector_in.at[6 + j], 62 + j, **around(j)) for j in range(1, n_s)]

    pl.semaphore_wait(entry, 3 + n_s - 1)
    for copy in gu_first:
        copy.start()
    load_branch.wait()
    chain.two()

    def norm_back(value, gain, grad):
        root = lax.rsqrt(jnp.mean(value * value, -1, keepdims=True) + epsilon)
        scaled = gain * grad
        inner = jnp.mean(scaled * value, -1, keepdims=True)
        gain_grad = jnp.sum(grad * (value * root), 0, keepdims=True)
        return root * scaled - value * (root * root * root * inner), gain_grad

    load_columns.wait()
    for copy in load_rows[:2]:
        copy.wait()
    for copy in [load_out] + load_rows[2:] + load_gu + [load_qkv]:
        copy.start()
    d_norm, gain_two_grad = norm_back(resid[...], gain_two[...], working[...])
    d_total = cotangent[...].astype(full) + d_norm
    d_branch[...] = d_total.astype(low)
    d_resid[...] = d_total
    for j in range(n_s):
        keys_slot = slots[j]
        keys_slot = jnp.concatenate([keys_slot] * (rows // 128), 1)
        ok = (keys_slot <= slot_row[0:1]) & (keys_slot >= first_row[0:1])
        bias[j * rows : (j + 1) * rows] = jnp.where(ok, 0.0, -1e30)
    load_out.wait()
    for copy in load_rows[2:]:
        copy.wait()
    for n in range(width // tile):
        value = lax.dot_general(
            d_branch[...], out_w[n * tile : (n + 1) * tile], (((1,), (1,)), ((), ())),
            preferred_element_type=full,
        )
        d_attended[:, n * tile : (n + 1) * tile] = value.astype(low)

    def turned_back(value):
        return value * cosine[...] + pltpu.roll(value * sine[...], HEAD_DIM // 2, 1)

    for g in range(KV_HEADS):
        keys = paired[:, :, g * HEAD_DIM : (g + 1) * HEAD_DIM].reshape(n_s * rows, HEAD_DIM)
        values = paired[:, :, kv_width + g * HEAD_DIM : kv_width + (g + 1) * HEAD_DIM]
        values = values.reshape(n_s * rows, HEAD_DIM)
        keys_grad[...] = jnp.zeros_like(keys_grad)
        values_grad[...] = jnp.zeros_like(values_grad)

        def head(i, carry, g=g, keys=keys, values=values):
            h = g * repeat + i
            head_columns = pl.ds(pl.multiple_of(h * HEAD_DIM, HEAD_DIM), HEAD_DIM)
            query = queries[:, head_columns]
            grad = d_attended[:, head_columns]
            raw = lax.dot_general(
                keys, query, (((1,), (1,)), ((), ())), preferred_element_type=full
            )
            logs = logsum[pl.ds(pl.multiple_of(h * 8, 8), 8)][0:1]
            probs = jnp.exp(raw * scale + bias[...] - logs)
            d_probs = lax.dot_general(
                values, grad, (((1,), (1,)), ((), ())), preferred_element_type=full
            )
            delta = jnp.sum(probs * d_probs, 0, keepdims=True)
            d_score = (probs * (d_probs - delta)).astype(low)
            turned = lax.dot_general(
                keys, d_score, (((0,), (0,)), ((), ())), preferred_element_type=full
            )
            d_qkv[:, head_columns] = turned_back((turned * scale).T).astype(low)
            keys_grad[...] += jnp.dot(d_score, query, preferred_element_type=full) * scale
            values_grad[...] += jnp.dot(probs.astype(low), grad, preferred_element_type=full)
            return carry

        lax.fori_loop(0, repeat, head, 0)
        dkv[g, :, :, :HEAD_DIM] = keys_grad[...].astype(low).reshape(n_s, rows, HEAD_DIM)
        dkv[g, :, :, HEAD_DIM:] = values_grad[...].astype(low).reshape(n_s, rows, HEAD_DIM)
        for copy in dkv_send[g]:
            copy.start()

    turned = attended[...].T
    for n in range(width // tile):
        n_columns = slice(n * tile, (n + 1) * tile)
        value = jnp.dot(turned, d_branch[:, n_columns], preferred_element_type=full)
        out_w[:, n_columns] = value.astype(low)
    sum_out.start_core()
    load_qkv.wait()

    def back_one(first, count, start):
        for n in range(width // tile):
            n_rows = slice(n * tile, (n + 1) * tile)
            value = lax.dot_general(
                d_qkv[:, first : first + count], qkv[n_rows, first : first + count],
                (((1,), (1,)), ((), ())), preferred_element_type=full,
            )
            working[:, n_rows] = value if start else working[:, n_rows] + value

    back_one(0, width, True)
    normed_turned = normed_one[...].T
    for n in range(width // tile):
        n_columns = slice(n * tile, (n + 1) * tile)
        value = jnp.dot(normed_turned, d_qkv[:, n_columns], preferred_element_type=full)
        qkv[:, n_columns] = value.astype(low)
    for copy in load_gu:
        copy.wait()
    gu_first[0].wait_recv()
    gu_to_y[...] = gu_to_y[...] + gu_x[1]
    gu_second[0].start()
    gu_first[1].wait_recv()
    gu_to_x[...] = gu_to_x[...] + gu_y[1]
    gu_second[1].start()

    for g in range(KV_HEADS):
        for copy in dkv_send[g]:
            copy.wait_recv()
        total = dkv[g, s].astype(full)
        for j in range(1, n_s):
            total = total + dkv_in[g, j].astype(full)
        key_columns = slice(width + g * HEAD_DIM, width + (g + 1) * HEAD_DIM)
        value_columns = slice(width + kv_width + g * HEAD_DIM, width + kv_width + (g + 1) * HEAD_DIM)
        d_qkv[:, key_columns] = turned_back(total[:, :HEAD_DIM]).astype(low)
        d_qkv[:, value_columns] = total[:, HEAD_DIM:].astype(low)
    back_one(width, 2 * kv_width, False)
    value = jnp.dot(normed_turned, d_qkv[:, width:], preferred_element_type=full)
    qkv[:, width:] = value.astype(low)
    sum_qkv.start_core()
    chain.add_two()
    chain.three()

    d_norm, gain_one_grad = norm_back(tokens[...].astype(full), gain_one[...], working[...])
    input_rows[...] = (d_resid[...] + d_norm).astype(low)
    bias_grad = jnp.sum(d_qkv[...].astype(full), 0, keepdims=True)
    vectors = jnp.concatenate([gain_one_grad, gain_two_grad, bias_grad], 1)
    part = vectors.shape[1] // 8
    for r in range(8):
        vector_in[0, r : r + 1] = vectors[:, r * part : (r + 1) * part]
    vector_send[0].start()
    sum_qkv.start_first()
    vector_send[0].wait_recv()
    vector_in[2] = vector_in[0] + vector_in[1]
    vector_send[1].start()
    sum_out.start_first()

    gu_first[2].wait_recv()
    gu_second[0].wait_recv()
    total = gu_own[:, :units].astype(full) + gu_x[0].astype(full) + gu_ended[0].astype(full)
    gu_own[:, :units] = total.astype(low)
    gu_first[3].wait_recv()
    gu_second[1].wait_recv()
    total = gu_own[:, units:].astype(full) + gu_y[0].astype(full) + gu_ended[1].astype(full)
    gu_own[:, units:] = total.astype(low)
    for copy in gu_send:
        copy.start()
    keep_rows = here(rows_for(gu_own, 0, 0), gu_rows.at[0], 6)
    keep_rows.start()
    vector_send[1].wait_recv()
    vector_in[4] = vector_in[2] + vector_in[3]
    vector_send[2].start()
    sum_qkv.start_second()
    sum_out.start_second()
    vector_send[2].wait_recv()
    vector_in[6] = vector_in[4] + vector_in[5]
    for copy in vector_send[3:]:
        copy.start()
    sum_qkv.finish()
    chain_qkv.one()
    chain.last(working)
    layer[...] = (resid[...] + working[...]).astype(low)
    chain_qkv.add_one()
    chain_qkv.two()
    sum_out.finish()
    for copy in out_send:
        copy.start()
    for copy in vector_send[3:]:
        copy.wait_recv()
    vector[...] = vector_in[6] + vector_in[7] + vector_in[8] + vector_in[9]
    chain_qkv.add_two()
    chain_qkv.three()
    chain_qkv.last(grad_qkv)
    total = own_part(out_w)(0)[...].astype(full)
    for copy in out_send:
        copy.wait_recv()
    for j in range(1, n_s):
        total = total + out_in[j].astype(full)
    grad_out[...] = total
    for copy in gu_send:
        copy.wait_recv()
    keep_rows.wait()
    chain_qkv.one_sent()
    chain_qkv.two_sent()
    chain_qkv.three_sent()
    chain.two_sent()
    chain.three_sent()
    sum_out.sent()
    sum_qkv.sent()
    for copy in gu_first + gu_second + gu_send + out_send + vector_send:
        copy.wait_send()
    for g in range(KV_HEADS):
        for copy in dkv_send[g]:
            copy.wait_send()


def back(
    columns, resid, gain_two, cotangent, attended, queries, paired, slots, slot_row, first_row,
    logsum, normed_one, tokens, gain_one, cosine, sine, w_out, w_qkv, gu_sum, branch,
):
    rows, width = tokens.shape
    n_s = paired.shape[0]
    group = n_s * rows
    kv_width = KV_HEADS * HEAD_DIM
    qkv_width = width + 2 * kv_width
    block = width // 8
    piece = block // n_s
    units = gu_sum.shape[2] // 2
    low, full = jnp.bfloat16, jnp.float32
    vmem = pl.BlockSpec(memory_space=pltpu.VMEM)
    hbm = pl.BlockSpec(memory_space=pl.ANY)
    shape = jax.ShapeDtypeStruct
    vectors = (2 * width + qkv_width) // 8
    return pl.pallas_call(
        back_kernel,
        in_specs=[vmem] * 8 + [hbm] * 12,
        out_specs=[vmem] * 5 + [hbm],
        out_shape=[
            shape((rows, width), low),
            shape((rows, width), low),
            shape((8, vectors), full),
            shape((piece, width), full),
            shape((piece, qkv_width), full),
            shape((n_s, piece, 2 * units), low),
        ],
        scratch_shapes=[
            pltpu.VMEM((rows, width), full),
            pltpu.VMEM((rows, width), low),
            pltpu.VMEM((rows, width), low),
            pltpu.VMEM((rows, width), low),
            pltpu.VMEM(paired.shape, low),
            pltpu.VMEM((rows, width), low),
            pltpu.VMEM((rows, width), low),
            pltpu.VMEM((width, width), low),
            pltpu.VMEM((width, qkv_width), low),
            pltpu.VMEM((block, 2 * units), low),
            pltpu.VMEM((block, units), low),
            pltpu.VMEM((block, units), low),
            pltpu.VMEM((2, block, units), low),
            pltpu.VMEM((2, block, units), low),
            pltpu.VMEM((2, block, units), low),
            pltpu.VMEM((group, width), low),
            pltpu.VMEM((rows, width), low),
            pltpu.VMEM((2, rows, width), low),
            pltpu.VMEM((2, rows, width), low),
            pltpu.VMEM((rows, width), full),
            pltpu.VMEM((group, rows), full),
            pltpu.VMEM((rows, width), low),
            pltpu.VMEM((rows, width), low),
            pltpu.VMEM((rows, qkv_width), low),
            pltpu.VMEM((rows, width), full),
            pltpu.VMEM((group, HEAD_DIM), full),
            pltpu.VMEM((group, HEAD_DIM), full),
            pltpu.VMEM((KV_HEADS, n_s, rows, 2 * HEAD_DIM), low),
            pltpu.VMEM((KV_HEADS, n_s, rows, 2 * HEAD_DIM), low),
            pltpu.VMEM((4, block, width), low),
            pltpu.VMEM((2, block, width // 2), low),
            pltpu.VMEM((2, block, width // 2), low),
            pltpu.VMEM((2, block, width // 2), low),
            pltpu.VMEM((4, block, qkv_width), low),
            pltpu.VMEM((2, block, qkv_width // 2), low),
            pltpu.VMEM((2, block, qkv_width // 2), low),
            pltpu.VMEM((2, block, qkv_width // 2), low),
            pltpu.VMEM((n_s, piece, width), low),
            pltpu.VMEM((piece, qkv_width), low),
            pltpu.VMEM((2, piece, qkv_width), low),
            pltpu.VMEM((2, piece, qkv_width), low),
            pltpu.VMEM((10, 8, vectors), full),
            pltpu.SemaphoreType.DMA((18,)),
            pltpu.SemaphoreType.DMA((68,)),
            pltpu.SemaphoreType.DMA((68,)),
        ],
        compiler_params=pltpu.CompilerParams(
            collective_id=2, has_side_effects=True, vmem_limit_bytes=63 * 2**20
        ),
        name="back",
    )(
        gain_two, slot_row, first_row, logsum, gain_one, cosine, sine, slots,
        resid, cotangent, attended, queries, paired, normed_one, tokens,
        columns, w_out, w_qkv, gu_sum, branch,
    )


def finish_kernel(
    layer, input_rows, grad_out, grad_qkv, grad_down, gu_rows,
    layer_out, input_grad, out_out, query_out, key_out, value_out, down_out, gate_out, up_out,
    layer_v, input_v, out_v, qkv_v, down_v, gu_v, gate_v, up_v, load, store,
):
    s = lax.axis_index("seq")
    n_s = gu_rows.shape[0]
    width = grad_out.shape[1]
    kv_width = KV_HEADS * HEAD_DIM
    unit_pad = grad_down.shape[0]
    unit = down_out.shape[0]
    units = gu_rows.shape[2] // 2
    moves = [
        (layer, layer_v, [(layer_v, layer_out)]),
        (input_rows, input_v, [(input_v, input_grad)]),
        (grad_down, down_v, [(down_v.at[:unit], down_out)]),
        (grad_out, out_v, [(out_v, out_out)]),
        (grad_qkv, qkv_v, [
            (qkv_v.at[:, :width], query_out),
            (qkv_v.at[:, width : width + kv_width], key_out),
            (qkv_v.at[:, width + kv_width :], value_out),
        ]),
    ]
    load_gu = pltpu.make_async_copy(gu_rows, gu_v, load.at[0])
    load_gu.start()
    loads, stores = [], []
    for i, (source, place, _) in enumerate(moves):
        loads.append(pltpu.make_async_copy(source, place, load.at[1 + i]))
        loads[-1].start()
    for copy, (_, _, parts) in zip(loads, moves):
        copy.wait()
        for source, target in parts:
            stores.append(pltpu.make_async_copy(source, target, store.at[len(stores)]))
            stores[-1].start()
    load_gu.wait()
    window = 512
    lanes = lax.broadcasted_iota(jnp.int32, (gu_rows.shape[1], 128), 1)
    for base, out, target_out in ((0, gate_v, gate_out), (units, up_v, up_out)):
        for f in range(units // unit_pad):
            for owner in range(n_s):
                source = base + f * unit_pad
                begin = min(source // 128 * 128, 2 * units - window)
                target = (f * n_s + owner) * unit
                first = target // 128 * 128
                slot = lax.rem(s + n_s - owner, n_s)
                value = gu_v[slot, :, begin : begin + window].astype(jnp.float32)
                turn = ((target - first) - (source - begin)) % window
                if turn:
                    value = pltpu.roll(value, turn, 1)
                for t in range(first, min(target + unit, out.shape[1]), 128):
                    part = value[:, t - first : t - first + 128]
                    if t < target:
                        part = jnp.where(lanes >= target - t, part, out[:, t : t + 128])
                    out[:, t : t + 128] = part
        stores.append(pltpu.make_async_copy(out, target_out, store.at[len(stores)]))
        stores[-1].start()
    for copy in stores:
        copy.wait()


def finish(layer, input_rows, grad_out, grad_qkv, grad_down, gu_rows, unit, hidden_width):
    piece, width = grad_out.shape
    kv_width = KV_HEADS * HEAD_DIM
    low, full = jnp.bfloat16, jnp.float32
    shape = jax.ShapeDtypeStruct
    hbm = pl.BlockSpec(memory_space=pl.ANY)
    wide = pltpu.VMEM((piece, hidden_width), full)
    return pl.pallas_call(
        finish_kernel,
        in_specs=[hbm] * 6,
        out_specs=[hbm] * 9,
        out_shape=[
            shape(layer.shape, low),
            shape(layer.shape, low),
            shape((piece, width), full),
            shape((piece, width), full),
            shape((piece, kv_width), full),
            shape((piece, kv_width), full),
            shape((unit, width), full),
            shape((piece, hidden_width), full),
            shape((piece, hidden_width), full),
        ],
        scratch_shapes=[
            pltpu.VMEM(value.shape, value.dtype)
            for value in (layer, input_rows, grad_out, grad_qkv, grad_down, gu_rows)
        ] + [wide, wide, pltpu.SemaphoreType.DMA((6,)), pltpu.SemaphoreType.DMA((9,))],
        compiler_params=pltpu.CompilerParams(vmem_limit_bytes=63 * 2**20),
        name="finish",
    )(layer, input_rows, grad_out, grad_qkv, grad_down, gu_rows)


def per_device(
    tokens, cotangent, lengths, balance, norm1_gain, w_query, b_query, w_key, b_key,
    w_value, b_value, w_out, norm2_gain, w_gate, w_up, w_down,
):
    seq_count = lax.axis_size("seq")
    fsdp_count = lax.axis_size("fsdp")
    seq_rank = lax.axis_index("seq")
    fsdp_rank = lax.axis_index("fsdp")
    rows_here, width = tokens.shape
    kv_width = KV_HEADS * HEAD_DIM
    hidden_width = w_gate.shape[1]
    unit = hidden_width // (fsdp_count * seq_count)
    (
        weight_gu, weight_down, upstream_all, normed_all, hidden, factor_gate, factor_up,
        weight_qkv, weight_out, queries, paired, slots, logsum, attended, resid, normed_one,
        gain_one, gain_two, slot_row, first_row, cosine, sine,
    ) = front(
        tokens, cotangent, lengths, balance, (norm1_gain, norm2_gain, b_query, b_key, b_value),
        (w_query, w_key, w_value, w_out, w_gate, w_up, w_down),
    )
    columns, grad_down, gu_sum, branch = ffn(
        normed_all, upstream_all, weight_gu, weight_down, hidden, factor_gate, factor_up
    )
    layer, input_rows, vectors, grad_out, grad_qkv, gu_rows = back(
        columns, resid, gain_two, cotangent, attended, queries, paired, slots, slot_row, first_row,
        logsum, normed_one, tokens, gain_one, cosine, sine, weight_out, weight_qkv, gu_sum, branch,
    )
    (
        layer_out, input_grad, grad_out, grad_query, grad_key, grad_value, grad_down, grad_gate,
        grad_up,
    ) = finish(layer, input_rows, grad_out, grad_qkv, grad_down, gu_rows, unit, hidden_width)
    vectors = vectors.reshape(-1)
    own = width // (fsdp_count * seq_count)
    first = (fsdp_rank * seq_count + seq_rank) * own

    def own_part(offset):
        return lax.dynamic_slice_in_dim(vectors, offset + first, own, 0)

    biases = 2 * width
    return (
        layer_out,
        input_grad,
        own_part(0),
        grad_query,
        own_part(biases),
        grad_key,
        vectors[biases + width : biases + width + kv_width],
        grad_value,
        vectors[biases + width + kv_width :],
        grad_out,
        own_part(width),
        grad_gate,
        grad_up,
        grad_down,
    )


def solution(mesh):
    both = P(("fsdp", "seq"), None)
    both_one = P(("fsdp", "seq"))
    placed = (
        both, both, P("fsdp", None), both_one, P("fsdp"), P("fsdp", None), P("fsdp"),
        P("fsdp", None), P("fsdp"), P("fsdp", None), P("fsdp"), P("fsdp", None), P("fsdp"),
        P("fsdp", None), P("fsdp", None), P("fsdp", None),
    )
    return jax.shard_map(
        per_device if mesh.shape["fsdp"] == 8 else plain_device,
        mesh=mesh,
        in_specs=placed,
        out_specs=(
            both, both, both_one, both, both_one, both, P(), both, P(), both, both_one,
            both, both, both,
        ),
        check_vma=False,
    )
```

```python
import jax
import jax.numpy as jnp
import numpy as np
from jax import lax
from jax.experimental import pallas as pl
from jax.experimental.pallas import tpu as pltpu
from jax.sharding import PartitionSpec as P

HEADS = 12
KV_HEADS = 2
HEAD_DIM = 128

MESH = pl.DeviceIdType.MESH

epsilon = 1e-06
rope_base = 1000000.0


def norm_piece(values, gain):
    return values * lax.rsqrt(jnp.mean(values * values, -1, keepdims=True) + epsilon) * gain


def rope_tables(position):
    half = HEAD_DIM // 2
    inverse = rope_base ** (-(jnp.arange(half, dtype=jnp.float32) * 2.0 / HEAD_DIM))
    angle = position.astype(jnp.float32)[:, None] * inverse[None, :]
    cosine = jnp.concatenate([jnp.cos(angle), jnp.cos(angle)], -1)
    sine = jnp.concatenate([jnp.sin(angle), jnp.sin(angle)], -1)
    return (cosine, sine)


def turn_half(values):
    half = values.shape[-1] // 2
    return jnp.concatenate([-values[..., half:], values[..., :half]], -1)


def rotate(values, cosine, sine):
    return values * cosine[:, None, :] + turn_half(values) * sine[:, None, :]


def rotate_back(grads, cosine, sine):
    return grads * cosine[:, None, :] - turn_half(grads * sine[:, None, :])


def segment_of(slots, starts):
    return (slots >= starts[1]).astype(jnp.int32) + (slots >= starts[2]).astype(jnp.int32)


def contract_rows(left, right):
    return lax.dot_general(
        left, right, (((0,), (0,)), ((), ())), preferred_element_type=jnp.float32
    )


def contract_columns(left, right):
    return lax.dot_general(
        left, right, (((1,), (1,)), ((), ())), preferred_element_type=jnp.float32
    )


def plain_device(
    tokens, cotangent, lengths, balance, norm1_gain, w_query, b_query, w_key, b_key,
    w_value, b_value, w_out, norm2_gain, w_gate, w_up, w_down,
):
    seq_count = lax.axis_size("seq")
    fsdp_count = lax.axis_size("fsdp")
    seq_rank = lax.axis_index("seq")
    rows_here, width = tokens.shape
    group = seq_count * rows_here
    kv_width = KV_HEADS * HEAD_DIM
    qkv_width = width + 2 * kv_width
    hidden_width = w_gate.shape[1]
    unit = hidden_width // (fsdp_count * seq_count)
    own_units = hidden_width // seq_count
    weight_rows = w_gate.shape[0]
    score_scale = HEAD_DIM ** (-0.5)
    repeat = HEADS // KV_HEADS

    slot = balance % group
    slots_all = lax.all_gather(slot, "seq", axis=0, tiled=True)
    seq_lengths = lengths[0]
    starts = jnp.cumsum(seq_lengths) - seq_lengths
    segment = segment_of(slot, starts)
    segments_all = segment_of(slots_all, starts)
    first_row = jnp.where(segment == 0, starts[0], jnp.where(segment == 1, starts[1], starts[2]))
    cosine, sine = rope_tables(slot - first_row)
    allowed = (segment[:, None] == segments_all[None, :]) & (slots_all[None, :] <= slot[:, None])

    small = jnp.concatenate([norm1_gain, norm2_gain, b_query, b_key, b_value], 0)[None]
    small = lax.all_gather(small, "fsdp", axis=0, tiled=True)
    piece = norm1_gain.shape[0]
    bias_piece = b_key.shape[0]
    gain_one = small[:, :piece].reshape(-1).astype(jnp.float32)
    gain_two = small[:, piece : 2 * piece].reshape(-1).astype(jnp.float32)
    bias_qkv = jnp.concatenate(
        [
            small[:, 2 * piece : 3 * piece].reshape(-1),
            small[:, 3 * piece : 3 * piece + bias_piece].reshape(-1),
            small[:, 3 * piece + bias_piece :].reshape(-1),
        ],
        0,
    ).astype(jnp.float32)
    weight_qkv = lax.all_gather(
        jnp.concatenate([w_query, w_key, w_value], 1), "fsdp", axis=0, tiled=True
    )
    weight_out = lax.all_gather(w_out, "fsdp", axis=0, tiled=True)
    upstream_all = lax.all_gather(cotangent, "seq", axis=0, tiled=True)

    def own_columns(weight):
        cut = weight.reshape(weight_rows, fsdp_count, seq_count, unit)
        return lax.dynamic_index_in_dim(cut, seq_rank, 2, False).reshape(weight_rows, own_units)

    weight_gu = lax.all_gather(
        jnp.concatenate([own_columns(w_gate), own_columns(w_up)], 1), "fsdp", axis=0, tiled=True
    )
    weight_down = lax.all_gather(
        lax.dynamic_slice_in_dim(w_down, seq_rank * unit, unit, 0), "fsdp", axis=0, tiled=True
    )

    inputs = tokens.astype(jnp.float32)
    normed_one = norm_piece(inputs, gain_one).astype(jnp.bfloat16)
    projected = jnp.dot(normed_one, weight_qkv, preferred_element_type=jnp.float32) + bias_qkv
    query_pre = projected[:, :width].reshape(rows_here, HEADS, HEAD_DIM)
    key_pre = projected[:, width : width + kv_width].reshape(rows_here, KV_HEADS, HEAD_DIM)
    value_pre = projected[:, width + kv_width :]
    queries = rotate(query_pre, cosine, sine).astype(jnp.bfloat16)
    keys = rotate(key_pre, cosine, sine).astype(jnp.bfloat16).reshape(rows_here, kv_width)
    values = value_pre.astype(jnp.bfloat16)
    paired = lax.all_gather(jnp.concatenate([keys, values], 1), "seq", axis=0, tiled=True)
    keys_all = paired[:, :kv_width].reshape(group, KV_HEADS, HEAD_DIM)
    values_all = paired[:, kv_width:].reshape(group, KV_HEADS, HEAD_DIM)
    grouped = queries.reshape(rows_here, KV_HEADS, repeat, HEAD_DIM)
    raw = (
        jnp.einsum("qgrd,kgd->grqk", grouped, keys_all, preferred_element_type=jnp.float32)
        * score_scale
    )
    scores = jnp.where(allowed, raw, -jnp.inf)
    expo = jnp.exp(scores - jnp.max(scores, -1, keepdims=True))
    probs = expo / jnp.sum(expo, -1, keepdims=True)
    probs_low = probs.astype(jnp.bfloat16)
    attended = jnp.einsum(
        "grqk,kgd->qgrd", probs_low, values_all, preferred_element_type=jnp.float32
    )
    attended = attended.astype(jnp.bfloat16).reshape(rows_here, width)
    resid = inputs + jnp.dot(attended, weight_out, preferred_element_type=jnp.float32)
    normed_two = norm_piece(resid, gain_two).astype(jnp.bfloat16)

    normed_all = lax.all_gather(normed_two, "seq", axis=0, tiled=True)
    both = jnp.dot(normed_all, weight_gu, preferred_element_type=jnp.float32)
    gate = both[:, :own_units]
    up = both[:, own_units:]
    sigma = jax.nn.sigmoid(gate)
    activated = gate * sigma
    hidden = (activated * up).astype(jnp.bfloat16)
    d_hidden = contract_columns(upstream_all, weight_down)
    d_gate = (d_hidden * up * sigma * (1.0 + gate * (1.0 - sigma))).astype(jnp.bfloat16)
    d_up = (d_hidden * activated).astype(jnp.bfloat16)
    d_both = jnp.concatenate([d_gate, d_up], 1)
    columns = lax.psum_scatter(
        contract_columns(d_both, weight_gu).astype(jnp.bfloat16),
        "seq", scatter_dimension=0, tiled=True,
    ).astype(jnp.float32)
    branch = lax.psum_scatter(
        jnp.dot(hidden, weight_down, preferred_element_type=jnp.float32).astype(jnp.bfloat16),
        "seq", scatter_dimension=0, tiled=True,
    ).astype(jnp.float32)
    layer_out = (resid + branch).astype(jnp.bfloat16)
    grad_down = lax.psum_scatter(
        contract_rows(hidden, upstream_all).astype(jnp.bfloat16),
        "fsdp", scatter_dimension=0, tiled=True,
    ).astype(jnp.float32)
    grad_pair = lax.psum_scatter(
        contract_rows(normed_all, d_both).astype(jnp.bfloat16),
        "fsdp", scatter_dimension=0, tiled=True,
    )
    grad_pair = lax.all_to_all(grad_pair, "seq", split_axis=0, concat_axis=0, tiled=True)
    grad_pair = grad_pair.reshape(seq_count, weight_rows // seq_count, 2, fsdp_count, unit)
    grad_pair = grad_pair.transpose(2, 1, 3, 0, 4).astype(jnp.float32)
    grad_pair = grad_pair.reshape(2, weight_rows // seq_count, hidden_width)

    _, pull_two = jax.vjp(norm_piece, resid, gain_two)
    d_resid_norm, grad_gain_two = pull_two(columns)
    d_resid = cotangent.astype(jnp.float32) + d_resid_norm
    d_branch = d_resid.astype(jnp.bfloat16)
    grad_out = contract_rows(attended, d_branch).astype(jnp.bfloat16)
    d_attended = contract_columns(d_branch, weight_out).astype(jnp.bfloat16)
    d_attended = d_attended.reshape(rows_here, KV_HEADS, repeat, HEAD_DIM)
    d_probs = jnp.einsum(
        "qgrd,kgd->grqk", d_attended, values_all, preferred_element_type=jnp.float32
    )
    delta = jnp.sum(probs * d_probs, -1, keepdims=True)
    d_score = (probs * (d_probs - delta)).astype(jnp.bfloat16)
    d_queries = (
        jnp.einsum("grqk,kgd->qgrd", d_score, keys_all, preferred_element_type=jnp.float32)
        * score_scale
    )
    d_keys = (
        jnp.einsum("grqk,qgrd->kgd", d_score, grouped, preferred_element_type=jnp.float32)
        * score_scale
    )
    d_values = jnp.einsum(
        "grqk,qgrd->kgd", probs_low, d_attended, preferred_element_type=jnp.float32
    )
    d_paired = jnp.concatenate([d_keys.reshape(group, kv_width), d_values.reshape(group, kv_width)], 1)
    d_paired = lax.psum_scatter(
        d_paired.astype(jnp.bfloat16), "seq", scatter_dimension=0, tiled=True
    ).astype(jnp.float32)
    d_query_pre = rotate_back(
        d_queries.reshape(rows_here, HEADS, HEAD_DIM), cosine, sine
    ).astype(jnp.bfloat16)
    d_key_pre = rotate_back(
        d_paired[:, :kv_width].reshape(rows_here, KV_HEADS, HEAD_DIM), cosine, sine
    ).astype(jnp.bfloat16)
    d_value_pre = d_paired[:, kv_width:].astype(jnp.bfloat16)
    d_qkv = jnp.concatenate(
        [
            d_query_pre.reshape(rows_here, width),
            d_key_pre.reshape(rows_here, kv_width),
            d_value_pre,
        ],
        1,
    )
    grad_qkv = contract_rows(normed_one, d_qkv).astype(jnp.bfloat16)
    grad_bias = jnp.sum(d_qkv.astype(jnp.float32), 0)
    d_normed_one = contract_columns(d_qkv, weight_qkv)
    _, pull_one = jax.vjp(norm_piece, inputs, gain_one)
    d_input_norm, grad_gain_one = pull_one(d_normed_one)
    input_grad = (d_resid + d_input_norm).astype(jnp.bfloat16)

    def summed(value):
        value = lax.psum_scatter(value, "fsdp", scatter_dimension=0, tiled=True)
        return lax.psum_scatter(value, "seq", scatter_dimension=0, tiled=True).astype(jnp.float32)

    grad_out = summed(grad_out)
    grad_qkv = summed(grad_qkv)
    vectors = lax.psum(
        jnp.concatenate([grad_gain_one, grad_gain_two, grad_bias], 0), ("fsdp", "seq")
    )
    own = width // (fsdp_count * seq_count)
    first = (lax.axis_index("fsdp") * seq_count + seq_rank) * own

    def own_part(offset):
        return lax.dynamic_slice_in_dim(vectors, offset + first, own, 0)

    biases = 2 * width
    return (
        layer_out,
        input_grad,
        own_part(0),
        grad_qkv[:, :width],
        own_part(biases),
        grad_qkv[:, width : width + kv_width],
        vectors[biases + width : biases + width + kv_width],
        grad_qkv[:, width + kv_width :],
        vectors[biases + width + kv_width :],
        grad_out,
        own_part(width),
        grad_pair[0],
        grad_pair[1],
        grad_down,
    )


SEQ = 4


class SumChain:
    def __init__(self, held, z_one, z_two, z_three, there, index):
        self.rank = lax.axis_index("seq")
        s = self.rank
        self.held, self.arrived = held, (z_one, z_two, z_three)
        self.up = [
            there(held(1), z_one, index, seq=s + 1),
            there(held(2), z_two.at[0], index + 2, seq=s + 1),
            there(held(3), z_three.at[0], index + 4, seq=s + 1),
        ]
        self.down = [
            there(held(3), z_one, index + 1, seq=s - 1),
            there(held(2), z_two.at[1], index + 3, seq=s - 1),
            there(held(1), z_three.at[1], index + 5, seq=s - 1),
        ]

    def add(self, j, arrived):
        ref = self.held(j)
        ref[...] = ref[...] + arrived[...]

    def one(self):
        pl.when(self.rank == 0)(self.up[0].start)
        pl.when(self.rank == 3)(self.down[0].start)

    def add_one(self):
        @pl.when(self.rank == 1)
        def _():
            self.up[0].wait_recv()
            self.add(2, self.arrived[0])

        @pl.when(self.rank == 2)
        def _():
            self.down[0].wait_recv()
            self.add(2, self.arrived[0])

    def two(self):
        pl.when(self.rank <= 1)(self.up[1].start)
        pl.when(self.rank >= 2)(self.down[1].start)

    def add_two(self):
        @pl.when((self.rank == 1) | (self.rank == 2))
        def _():
            self.up[1].wait_recv()
            self.add(3, self.arrived[1].at[0])
            self.down[1].wait_recv()
            self.add(1, self.arrived[1].at[1])

    def three(self):
        pl.when(self.rank <= 2)(self.up[2].start)
        pl.when(self.rank >= 1)(self.down[2].start)

    def last(self, out):
        out[...] = self.held(0)[...].astype(jnp.float32)

        @pl.when(self.rank >= 1)
        def _():
            self.up[2].wait_recv()
            out[...] += self.arrived[2][0].astype(jnp.float32)

        @pl.when(self.rank <= 2)
        def _():
            self.down[2].wait_recv()
            out[...] += self.arrived[2][1].astype(jnp.float32)

    def one_sent(self):
        pl.when(self.rank == 0)(self.up[0].wait_send)
        pl.when(self.rank == 3)(self.down[0].wait_send)

    def two_sent(self):
        pl.when(self.rank <= 1)(self.up[1].wait_send)
        pl.when(self.rank >= 2)(self.down[1].wait_send)

    def three_sent(self):
        pl.when(self.rank <= 2)(self.up[2].wait_send)
        pl.when(self.rank >= 1)(self.down[2].wait_send)


class SumPlane:
    def __init__(self, buffer, block, plane, arrived, by_x, by_y, ended, there, index):
        half = buffer.shape[1] // 2
        low, high = pl.ds(0, half), pl.ds(half, half)

        def part(k):
            return buffer.at[pl.ds(pl.multiple_of(plane[k] * block, 16), block)]

        self.parts = own, to_x, to_y, to_both = [part(k) for k in (0, 2, 4, 6)]
        self.arrived, self.by_x, self.by_y, self.ended, self.half = arrived, by_x, by_y, ended, half
        self.core = [
            there(part(2 * i + 1), arrived.at[i], index + i, fsdp=plane[1]) for i in range(4)
        ]
        self.first = [
            there(to_both.at[:, low], by_x.at[1], index + 5, fsdp=plane[2]),
            there(to_both.at[:, high], by_y.at[1], index + 7, fsdp=plane[4]),
            there(to_x.at[:, low], by_x.at[0], index + 4, fsdp=plane[2]),
            there(to_y.at[:, high], by_y.at[0], index + 6, fsdp=plane[4]),
        ]
        self.second = [
            there(to_y.at[:, low], ended.at[0], index + 8, fsdp=plane[4]),
            there(to_x.at[:, high], ended.at[1], index + 9, fsdp=plane[2]),
        ]

    def start_core(self):
        for copy in self.core:
            copy.start()

    def start_first(self):
        for i in (3, 1, 2, 0):
            self.core[i].wait_recv()
            part = self.parts[i]
            part[...] = part[...] + self.arrived[i]
        for copy in self.first:
            copy.start()

    def start_second(self):
        half = self.half
        _, to_x, to_y, _ = self.parts
        self.first[0].wait_recv()
        to_y[:, :half] = to_y[:, :half] + self.by_x[1]
        self.second[0].start()
        self.first[1].wait_recv()
        to_x[:, half:] = to_x[:, half:] + self.by_y[1]
        self.second[1].start()

    def finish(self):
        half = self.half
        own = self.parts[0]
        self.first[2].wait_recv()
        self.second[0].wait_recv()
        total = own[:, :half].astype(jnp.float32) + self.by_x[0].astype(jnp.float32)
        own[:, :half] = (total + self.ended[0].astype(jnp.float32)).astype(jnp.bfloat16)
        self.first[3].wait_recv()
        self.second[1].wait_recv()
        total = own[:, half:].astype(jnp.float32) + self.by_y[0].astype(jnp.float32)
        own[:, half:] = (total + self.ended[1].astype(jnp.float32)).astype(jnp.bfloat16)

    def sent(self):
        for copy in self.core + self.first + self.second:
            copy.wait_send()


def block_at(place):
    far = 2 * (lax.axis_index("seq") // 2)
    return (1 + far, 2, 3 - far, 0)[place]


def in_order(partial, rows):
    far = 2 * (lax.axis_index("seq") // 2)
    places = {0: 3, 1: far, 2: 1, 3: 2 - far}

    def held(j):
        return partial.at[pl.ds(pl.multiple_of(places[j] * rows, rows), rows)]

    return held


def front_kernel(
    lengths, tokens, cotangent, small, balance, inverse,
    w_query, w_key, w_value, w_out, w_gate, w_up, w_down,
    gu_all, down_all, upstream_all, normed_all, hidden, factor_gate, factor_up, qkv_out, out_out,
    queries, paired_out, slots_out, logsum, attended, resid, normed_one, gain_one, gain_two,
    slot_row, first_row, cosine, sine,
    q_w, kv_w, out_w, gate_v, up_v, gu, normed, kv, small_own, small_all, slots_all, bias,
    cotangent_v, down_raw, down_own, hidden_v, gate_part, up_part,
    local, ssem, rsem, zsend, zrecv,
):
    f = lax.axis_index("fsdp")
    s = lax.axis_index("seq")
    rows, width = tokens.shape
    n_f, n_s = 8, slots_all.shape[0]
    group = n_s * rows
    block = w_query.shape[0]
    unit_pad = down_own.shape[0]
    unit = w_gate.shape[1] // (n_f * n_s)
    units = n_f * unit_pad
    kv_width = KV_HEADS * HEAD_DIM
    qkv_width = width + 2 * kv_width
    scale = HEAD_DIM ** (-0.5)
    repeat = HEADS // KV_HEADS
    plane = [f ^ k for k in range(n_f)]

    entry = pltpu.get_barrier_semaphore()
    for k in range(1, n_f):
        pl.semaphore_signal(entry, inc=1, device_id={"fsdp": plane[k]}, device_id_type=MESH)
    for j in range(1, n_s):
        pl.semaphore_signal(
            entry, inc=1, device_id={"seq": lax.rem(s + j, n_s)}, device_id_type=MESH
        )

    def here(source, target, index):
        return pltpu.make_async_copy(source, target, local.at[index])

    def there(source, target, index, **device):
        return pltpu.make_async_remote_copy(
            src_ref=source, dst_ref=target, send_sem=ssem.at[index], recv_sem=rsem.at[index],
            device_id=device, device_id_type=MESH,
        )

    def own_rows(ref, owner, size, start=0, count=None):
        first = pl.multiple_of(owner * size + start, 16)
        return ref.at[pl.ds(first, size if count is None else count)]

    class Gather:
        def __init__(self, source, target, size, index):
            half = size // 2
            x, y, c = plane[2], plane[4], plane[1]
            self.own = here(source, own_rows(target, f, size), index // 8) if source is not None else None
            if source is None:
                source = own_rows(target, f, size)
            mine = own_rows(target, f, size)
            self.first = [
                there(source, mine, index, fsdp=x),
                there(source, mine, index + 1, fsdp=y),
                there(source, mine, index + 2, fsdp=c),
            ]
            from_x, from_y = own_rows(target, x, size), own_rows(target, y, size)
            part_x = own_rows(target, x, size, 0, half)
            part_y = own_rows(target, y, size, half, half)
            self.second = [
                there(part_x, part_x, index + 3, fsdp=y),
                there(part_y, part_y, index + 4, fsdp=x),
                there(from_x, from_x, index + 5, fsdp=c),
                there(from_y, from_y, index + 6, fsdp=c),
            ]
            diagonal = own_rows(target, plane[6], size)
            self.third = there(diagonal, diagonal, index + 7, fsdp=c)

        def start(self):
            if self.own is not None:
                self.own.start()
            for copy in self.first:
                copy.start()

        def forward(self):
            self.first[0].wait_recv()
            self.second[0].start()
            self.second[2].start()
            self.first[1].wait_recv()
            self.second[1].start()
            self.second[3].start()

        def last(self):
            self.second[0].wait_recv()
            self.second[1].wait_recv()
            self.third.start()

        def finish(self):
            if self.own is not None:
                self.own.wait()
            self.first[2].wait_recv()
            self.second[2].wait_recv()
            self.second[3].wait_recv()
            self.third.wait_recv()

        def sent(self):
            for copy in self.first + self.second + [self.third]:
                copy.wait_send()

    class Chain:
        def __init__(self, target, index, own=None):
            self.steps = []
            for step in range(1, n_s):
                up = own_rows(target, s - (step - 1), rows)
                down = own_rows(target, s + (step - 1), rows)
                source = own if own is not None and step == 1 else up
                i = index + 2 * (step - 1)
                self.steps.append((
                    pltpu.make_async_remote_copy(
                        src_ref=source, dst_ref=up, send_sem=zsend.at[i], recv_sem=zrecv.at[i],
                        device_id={"seq": s + 1}, device_id_type=MESH,
                    ),
                    pltpu.make_async_remote_copy(
                        src_ref=down if source is up else source, dst_ref=down, send_sem=zsend.at[i + 1], recv_sem=zrecv.at[i + 1],
                        device_id={"seq": s - 1}, device_id_type=MESH,
                    ),
                    (s >= step - 1) & (s < n_s - 1),
                    (s >= 1) & (s <= n_s - step),
                    s >= step,
                    s <= n_s - 1 - step,
                ))

        def send(self, step):
            up, down, can_up, can_down, _, _ = self.steps[step - 1]
            pl.when(can_up)(up.start)
            pl.when(can_down)(down.start)

        def receive(self, step):
            up, down, _, _, from_below, from_above = self.steps[step - 1]
            pl.when(from_below)(up.wait_recv)
            pl.when(from_above)(down.wait_recv)

        def sent(self):
            for up, down, can_up, can_down, _, _ in self.steps:
                pl.when(can_up)(up.wait_send)
                pl.when(can_down)(down.wait_send)

    own_block = pl.ds(pl.multiple_of(f * block, 16), block)
    pieces = [
        here(w_key, kv_w.at[own_block, pl.ds(0, kv_width)], 6),
        here(w_value, kv_w.at[own_block, pl.ds(kv_width, kv_width)], 7),
        here(w_query, q_w.at[own_block], 5),
        here(cotangent, cotangent_v, 8),
    ]
    load_gate = here(w_gate, gate_v, 9)
    load_up = here(w_up, up_v, 10)
    first_unit = pl.multiple_of(s * unit // 16 * 16, 16)
    load_down = here(w_down.at[pl.ds(first_unit, unit_pad)], down_raw, 15)
    for copy in pieces[:2]:
        copy.start()

    slot = (balance[...] & (group - 1)).astype(jnp.float32)
    second = lengths[0, 0].astype(jnp.float32)
    third = (lengths[0, 0] + lengths[0, 1]).astype(jnp.float32)
    first = jnp.where(slot >= third, third, jnp.where(slot >= second, second, 0.0))
    slot_row[...] = jnp.broadcast_to(slot, slot_row.shape)
    first_row[...] = jnp.broadcast_to(first, first_row.shape)
    slots_all[s] = jnp.broadcast_to(slot, (128, rows)).T
    lanes = lax.broadcasted_iota(jnp.int32, small.shape, 1)
    sorts = lax.broadcasted_iota(jnp.int32, small.shape, 0)
    small_own[...] = jnp.where(
        sorts < 3,
        pltpu.roll(small[...], lax.rem(f, 2) * block, 1),
        pltpu.roll(small[...], f * (kv_width // n_f), 1),
    )
    small_all[f] = small_own[...]

    gather_kv = Gather(None, kv_w, block, 0)
    gather_q = Gather(None, q_w, block, 8)
    gather_out = Gather(w_out, out_w, block, 16)
    gather_gu = Gather(None, gu, block, 24)
    gather_down = Gather(down_own, down_all, unit_pad, 32)
    chain_up = Chain(upstream_all, 0, cotangent_v)
    chain_normed = Chain(normed, 6)
    send_small = [
        there(small_own, small_all.at[f], 40 + k, fsdp=plane[k]) for k in range(1, n_f)
    ]
    send_slots = [
        there(slots_all.at[s], slots_all.at[s], 48 + j, seq=lax.rem(s + j, n_s))
        for j in range(1, n_s)
    ]
    send_kv = [
        there(kv.at[s], kv.at[s], 52 + j, seq=lax.rem(s + j, n_s)) for j in range(1, n_s)
    ]
    for copy in pieces[:2]:
        copy.wait()
    for copy in pieces[2:]:
        copy.start()
    pl.semaphore_wait(entry, n_f - 1 + n_s - 1)
    gather_kv.start()
    for copy in send_small + send_slots:
        copy.start()
    for copy in pieces[2:]:
        copy.wait()
    chain_up.send(1)
    load_gate.start()
    load_up.start()
    load_down.start()
    save_own = here(cotangent_v, own_rows(upstream_all, s, rows), 8)
    save_own.start()
    position = slots_all[s] - jnp.broadcast_to(first, (128, rows)).T
    angle = position * inverse[...]
    cosine[...] = jnp.cos(angle)
    sine[...] = jnp.where(
        lax.broadcasted_iota(jnp.int32, angle.shape, 1) < HEAD_DIM // 2, -1.0, 1.0
    ) * jnp.sin(angle)

    for copy in send_small + send_slots:
        copy.wait_recv()

    def joined(sort):
        return jnp.concatenate(
            [
                small_all[2 * i, sort : sort + 1] + small_all[2 * i + 1, sort : sort + 1]
                for i in range(n_f // 2)
            ],
            1,
        )

    gain_one[...] = joined(0)
    gain_two[...] = joined(1)
    bias_query = joined(2)
    bias_key = sum(small_all[i, 3:4, :kv_width] for i in range(n_f))
    bias_value = sum(small_all[i, 4:5, :kv_width] for i in range(n_f))

    inputs = tokens[...].astype(jnp.float32)
    root = lax.rsqrt(jnp.mean(inputs * inputs, -1, keepdims=True) + epsilon)
    normed_one[...] = (inputs * root * gain_one[...]).astype(jnp.bfloat16)
    gather_kv.forward()
    gather_q.start()
    gather_kv.last()
    gather_kv.finish()

    def turned(value):
        return value * cosine[...] + pltpu.roll(value, HEAD_DIM // 2, 1) * sine[...]

    rows_low = normed_one[...]
    pair = jnp.dot(rows_low, kv_w[:, :kv_width], preferred_element_type=jnp.float32)
    pair = pair + bias_key
    for g in range(KV_HEADS):
        columns = slice(g * HEAD_DIM, (g + 1) * HEAD_DIM)
        kv[s, :, columns] = turned(pair[:, columns]).astype(jnp.bfloat16)
    pair = jnp.dot(rows_low, kv_w[:, kv_width:], preferred_element_type=jnp.float32)
    kv[s, :, kv_width:] = (pair + bias_value).astype(jnp.bfloat16)
    for copy in send_kv:
        copy.start()
    save_kv_w = here(kv_w, qkv_out.at[:, pl.ds(width, 2 * kv_width)], 11)
    save_kv_w.start()

    load_gate.wait()
    load_up.wait()
    pick_units(gate_v, up_v, gu.at[own_block], w_gate.shape[1] // n_f, unit, unit_pad)
    gather_q.forward()
    gather_out.start()
    load_down.wait()
    raw = down_raw[...].astype(jnp.float32)
    shifted = jnp.concatenate([raw[8:], jnp.zeros((8, width), jnp.float32)], 0)
    raw = jnp.where(lax.rem(s * unit, 16) == 0, raw, shifted)
    inside = lax.broadcasted_iota(jnp.int32, raw.shape, 0) < unit
    down_own[...] = jnp.where(inside, raw, 0.0).astype(jnp.bfloat16)

    for j in range(n_s):
        keys_slot = slots_all[j]
        keys_slot = jnp.concatenate([keys_slot] * (rows // 128), 1)
        ok = (keys_slot <= slot) & (keys_slot >= first)
        bias[j * rows : (j + 1) * rows] = jnp.where(ok, 0.0, -1e30)

    gather_q.last()
    gather_q.finish()
    save_q_w = here(q_w, qkv_out.at[:, pl.ds(0, width)], 0)
    save_q_w.start()
    for g in range(HEADS // 2):
        columns = slice(g * 2 * HEAD_DIM, (g + 1) * 2 * HEAD_DIM)
        pair = jnp.dot(rows_low, q_w[:, columns], preferred_element_type=jnp.float32)
        pair = pair + bias_query[:, columns]
        for h in range(2):
            part = turned(pair[:, h * HEAD_DIM : (h + 1) * HEAD_DIM]).astype(jnp.bfloat16)
            queries[:, (2 * g + h) * HEAD_DIM : (2 * g + h + 1) * HEAD_DIM] = part

    gather_out.forward()
    gather_gu.start()
    chain_up.receive(1)
    for copy in send_kv:
        copy.wait_recv()
    chain_up.send(2)
    save_kv = here(kv, paired_out, 12)
    save_kv.start()
    slots_out[...] = slots_all[...]

    for g in range(KV_HEADS):
        keys = kv[:, :, g * HEAD_DIM : (g + 1) * HEAD_DIM].reshape(n_s * rows, HEAD_DIM)
        values = kv[:, :, kv_width + g * HEAD_DIM : kv_width + (g + 1) * HEAD_DIM]
        values = values.reshape(n_s * rows, HEAD_DIM)

        def head(i, carry, g=g, keys=keys, values=values):
            h = g * repeat + i
            columns = pl.ds(pl.multiple_of(h * HEAD_DIM, HEAD_DIM), HEAD_DIM)
            raw = lax.dot_general(
                keys, queries[:, columns], (((1,), (1,)), ((), ())),
                preferred_element_type=jnp.float32,
            )
            scores = raw * scale + bias[...]
            top = jnp.max(scores, 0, keepdims=True)
            expo = jnp.exp(scores - top)
            total = jnp.sum(expo, 0, keepdims=True)
            probs = (expo * (1.0 / total)).astype(jnp.bfloat16)
            mixed = lax.dot_general(
                values, probs, (((0,), (0,)), ((), ())), preferred_element_type=jnp.float32
            )
            attended[:, columns] = mixed.T.astype(jnp.bfloat16)
            logsum[pl.ds(pl.multiple_of(h * 8, 8), 8)] = jnp.broadcast_to(
                top + jnp.log(total), (8, rows)
            )
            return carry

        lax.fori_loop(0, repeat, head, 0)
        if g == 0:
            gather_out.last()

    gather_out.finish()
    save_out = here(out_w, out_out, 13)
    save_out.start()
    mixed = attended[...]
    for g in range(width // 256):
        columns = slice(g * 256, (g + 1) * 256)
        part = jnp.dot(mixed, out_w[:, columns], preferred_element_type=jnp.float32)
        resid[:, columns] = tokens[:, columns].astype(jnp.float32) + part
    value = resid[...]
    root = lax.rsqrt(jnp.mean(value * value, -1, keepdims=True) + epsilon)
    own_tokens = pl.ds(pl.multiple_of(s * rows, rows), rows)
    normed[own_tokens] = (value * root * gain_two[...]).astype(jnp.bfloat16)
    chain_normed.send(1)

    wide = hidden_v.shape[2]
    count = units // wide

    def saves(owner, t, slot):
        place = (
            pl.ds(pl.multiple_of(owner * rows, rows), rows),
            pl.ds(pl.multiple_of(t * wide, wide), wide),
        )
        return [
            here(part.at[slot], whole.at[place], 16 + 3 * slot + i)
            for i, (part, whole) in enumerate(
                ((hidden_v, hidden), (gate_part, factor_gate), (up_part, factor_up))
            )
        ]

    def feed(owner, done):
        def body(t, carry):
            slot = lax.rem(t + done, 2)
            mine = normed[pl.ds(pl.multiple_of(owner * rows, rows), rows)]
            gate_columns = pl.ds(pl.multiple_of(t * wide, wide), wide)
            up_columns = pl.ds(pl.multiple_of(units + t * wide, wide), wide)
            gate = jnp.dot(mine, gu[:, gate_columns], preferred_element_type=jnp.float32)
            up = jnp.dot(mine, gu[:, up_columns], preferred_element_type=jnp.float32)
            sigma = jax.nn.sigmoid(gate)
            activated = gate * sigma

            @pl.when(t + done >= 2)
            def _():
                for copy in saves(owner, t, slot):
                    copy.wait()

            hidden_v[slot] = (activated * up).astype(jnp.bfloat16)
            gate_part[slot] = (up * sigma * (1.0 + gate * (1.0 - sigma))).astype(jnp.bfloat16)
            up_part[slot] = activated.astype(jnp.bfloat16)
            for copy in saves(owner, t, slot):
                copy.start()
            return carry

        lax.fori_loop(0, count, body, 0)

    chain_up.receive(2)
    chain_normed.receive(1)
    chain_normed.send(2)
    gather_gu.forward()
    chain_normed.receive(2)
    chain_normed.send(3)
    gather_gu.last()
    gather_down.start()
    gather_gu.finish()
    save_gu = here(gu, gu_all, 22)
    save_gu.start()
    feed(s, 0)
    feed(s ^ 1, count)
    chain_normed.receive(3)
    chain_up.send(3)
    save_normed = here(normed, normed_all, 23)
    save_normed.start()
    gather_down.forward()
    feed(s ^ 2, 2 * count)
    feed(s ^ 3, 3 * count)
    gather_down.last()
    for t in (count - 2, count - 1):
        for copy in saves(s ^ 3, t, (t + 3 * count) % 2):
            copy.wait()
    chain_up.receive(3)
    gather_down.finish()
    for copy in (save_own, save_kv_w, save_q_w, save_kv, save_out, save_gu, save_normed):
        copy.wait()
    for part in (gather_kv, gather_q, gather_out, gather_gu, gather_down, chain_up, chain_normed):
        part.sent()
    for copy in send_small + send_slots + send_kv:
        copy.wait_send()


def pick_units(gate, up, out, stride, unit, padded):
    rank = lax.axis_index("seq")
    pieces = gate.shape[1] // stride
    half = out.shape[1] // 2
    window, tile = 512, 128
    rows = lax.broadcasted_iota(jnp.int32, (window, tile), 0)
    columns = lax.broadcasted_iota(jnp.int32, (window, tile), 1)
    for first in range(0, 2 * half, tile):
        source = gate if first < half else up
        local = first % half
        total = jnp.zeros((out.shape[0], tile), jnp.float32)
        for f in range(pieces):
            low = max(local, f * padded)
            high = min(local + tile, f * padded + unit)
            if low >= high:
                continue
            begin = f * stride + rank * unit
            base = jnp.minimum(begin // 128, (source.shape[1] - window) // 128) * 128
            base = pl.multiple_of(base, 128)
            wanted = columns + (local - f * padded + begin - base)
            inside = (columns >= low - local) & (columns < high - local)
            chosen = jnp.where((rows == wanted) & inside, 1.0, 0.0).astype(jnp.bfloat16)
            total += jnp.dot(
                source[:, pl.ds(base, window)], chosen, preferred_element_type=jnp.float32
            )
        out[:, first : first + tile] = total.astype(jnp.bfloat16)


def front(tokens, cotangent, lengths, balance, vectors, weights):
    rows, width = tokens.shape
    n_s = lax.axis_size("seq")
    w_query, w_key, w_value, w_out, w_gate, w_up, w_down = weights
    block = w_query.shape[0]
    unit_pad = -(-w_down.shape[0] // n_s // 16) * 16
    kv_width = KV_HEADS * HEAD_DIM
    qkv_width = width + 2 * kv_width
    units = 8 * unit_pad
    group = n_s * rows
    wide = 768
    low, full = jnp.bfloat16, jnp.float32
    small = sum(
        jnp.pad(v.astype(full)[None], ((i, 7 - i), (0, 2 * block - v.shape[0])))
        for i, v in enumerate(vectors)
    )
    half = HEAD_DIM // 2
    inverse = rope_base ** (-(np.arange(half, dtype=np.float32) * np.float32(2.0 / HEAD_DIM)))
    inverse = jnp.asarray(np.concatenate([inverse, inverse])[None], full)
    smem = pl.BlockSpec(memory_space=pltpu.SMEM)
    vmem = pl.BlockSpec(memory_space=pltpu.VMEM)
    hbm = pl.BlockSpec(memory_space=pl.ANY)
    shape = jax.ShapeDtypeStruct
    return pl.pallas_call(
        front_kernel,
        in_specs=[smem, vmem, hbm, vmem, vmem, vmem] + [hbm] * 7,
        out_specs=[hbm] * 9 + [vmem, hbm] + [vmem] * 11,
        out_shape=[
            shape((width, 2 * units), low),
            shape((units, width), low),
            shape((group, width), low),
            shape((group, width), low),
            shape((group, units), low),
            shape((group, units), low),
            shape((group, units), low),
            shape((width, qkv_width), low),
            shape((width, width), low),
            shape((rows, width), low),
            shape((n_s, rows, 2 * kv_width), low),
            shape((n_s, rows, 128), full),
            shape((8 * HEADS, rows), full),
            shape((rows, width), low),
            shape((rows, width), full),
            shape((rows, width), low),
            shape((1, width), full),
            shape((1, width), full),
            shape((8, rows), full),
            shape((8, rows), full),
            shape((rows, HEAD_DIM), full),
            shape((rows, HEAD_DIM), full),
        ],
        scratch_shapes=[
            pltpu.VMEM((width, width), low),
            pltpu.VMEM((width, 2 * kv_width), low),
            pltpu.VMEM((width, width), low),
            pltpu.VMEM(w_gate.shape, low),
            pltpu.VMEM(w_up.shape, low),
            pltpu.VMEM((width, 2 * units), low),
            pltpu.VMEM((group, width), low),
            pltpu.VMEM((n_s, rows, 2 * kv_width), low),
            pltpu.VMEM((8, 2 * block), full),
            pltpu.VMEM((8, 8, 2 * block), full),
            pltpu.VMEM((n_s, rows, 128), full),
            pltpu.VMEM((group, rows), full),
            pltpu.VMEM((rows, width), low),
            pltpu.VMEM((unit_pad, width), low),
            pltpu.VMEM((unit_pad, width), low),
            pltpu.VMEM((2, rows, wide), low),
            pltpu.VMEM((2, rows, wide), low),
            pltpu.VMEM((2, rows, wide), low),
            pltpu.SemaphoreType.DMA((24,)),
            pltpu.SemaphoreType.DMA((56,)),
            pltpu.SemaphoreType.DMA((56,)),
            pltpu.SemaphoreType.DMA((12,)),
            pltpu.SemaphoreType.DMA((12,)),
        ],
        compiler_params=pltpu.CompilerParams(
            collective_id=0, has_side_effects=True, vmem_limit_bytes=62 * 2**20
        ),
        name="front",
    )(
        lengths, tokens, cotangent, small, balance.reshape(1, rows), inverse,
        w_query, w_key, w_value, w_out, w_gate, w_up, w_down,
    )


def ffn_kernel(
    normed_all, upstream_all, w_gu, w_down, hidden_all, factor_gate, factor_up,
    columns, grad_down, gu_sum, branch, down_arrived, gu_arrived,
    normed, upstream, gu, down, hidden, d_both, partial, z_one, z_two, z_three,
    down_x, down_y, down_last, down_piece,
    load, ssem, rsem,
):
    f = lax.axis_index("fsdp")
    s = lax.axis_index("seq")
    n_s = SEQ
    group, width = normed.shape
    rows = group // n_s
    half_rows = group // 2
    units = down.shape[0]
    tile = 256
    tiles = units // tile
    wide = 768
    block = gu.shape[0] // 8
    unit = units // 8
    half = width // 2
    plane = [f ^ k for k in range(8)]
    full = jnp.float32

    entry = pltpu.get_barrier_semaphore()
    for k in (1, 2, 4):
        pl.semaphore_signal(entry, inc=1, device_id={"fsdp": plane[k]}, device_id_type=MESH)
    for j in (1, n_s - 1):
        pl.semaphore_signal(
            entry, inc=1, device_id={"seq": lax.rem(s + j, n_s)}, device_id_type=MESH
        )

    def here(source, target, index):
        return pltpu.make_async_copy(source, target, load.at[index])

    def there(source, target, index, **device):
        return pltpu.make_async_remote_copy(
            src_ref=source, dst_ref=target, send_sem=ssem.at[index], recv_sem=rsem.at[index],
            device_id=device, device_id_type=MESH,
        )

    def part(ref, owner, size):
        return ref.at[pl.ds(pl.multiple_of(owner * size, 16), size)]

    early, late = (0,), (1, 2, 3)

    def rows_of(p):
        return pl.ds(p * rows, rows)

    def row_loads(p):
        owner = lax.rem(s + n_s - block_at(p), n_s)
        mine = rows_of(p)
        return [
            here(part(upstream_all, owner, rows), upstream.at[mine], 5 * p),
            here(part(factor_gate, owner, rows), d_both.at[mine, pl.ds(0, units)], 5 * p + 1),
            here(part(factor_up, owner, rows), d_both.at[mine, pl.ds(units, units)], 5 * p + 2),
            here(part(hidden_all, owner, rows), hidden.at[mine], 5 * p + 3),
            here(part(normed_all, owner, rows), normed.at[mine], 5 * p + 4),
        ]

    def down_load(t):
        mine = pl.ds(pl.multiple_of(t * wide, wide), wide)
        return here(w_down.at[mine], down.at[mine], 20 + t)

    def gu_load(n):
        mine = pl.ds(pl.multiple_of(n * 512, 512), 512)
        return here(w_gu.at[mine], gu.at[mine], 23 + n)

    loads = [row_loads(p) for p in range(n_s)]
    order = [loads[0][0], down_load(0)]
    order += [loads[p][i] for i in (1, 2) for p in early]
    order += [down_load(t) for t in range(1, units // wide)]
    second = [gu_load(n) for n in range(width // 512)]
    second += [loads[p][i] for i in (0, 1, 2) for p in late]
    third = [loads[p][i] for i in (3, 4) for p in range(n_s)]
    for copy in order:
        copy.start()

    def forward(blocks, wait, following):
        for p in blocks:
            for copy in loads[p][:3]:
                copy.wait()
        for copy in following:
            copy.start()
        mine = pl.ds(blocks[0] * rows, len(blocks) * rows)

        def body(t, carry):
            if wait:
                down_load(t).wait()
            gate_columns = pl.ds(pl.multiple_of(t * wide, wide), wide)
            up_columns = pl.ds(pl.multiple_of(units + t * wide, wide), wide)
            d_hidden = lax.dot_general(
                upstream[mine], down[gate_columns], (((1,), (1,)), ((), ())),
                preferred_element_type=full,
            )
            value = d_hidden * d_both[mine, gate_columns].astype(full)
            d_both[mine, gate_columns] = value.astype(jnp.bfloat16)
            value = d_hidden * d_both[mine, up_columns].astype(full)
            d_both[mine, up_columns] = value.astype(jnp.bfloat16)
            return carry

        lax.fori_loop(0, units // wide, body, 0)

    def backward(blocks, wait):
        part_rows = pl.ds(blocks[0] * rows, len(blocks) * rows)

        def body(n, carry):
            if wait:
                gu_load(n).wait()
            out_columns = pl.ds(pl.multiple_of(n * 512, 512), 512)
            value = lax.dot_general(
                d_both[part_rows], gu[out_columns], (((1,), (1,)), ((), ())),
                preferred_element_type=full,
            )
            partial[part_rows, out_columns] = value.astype(jnp.bfloat16)
            return carry

        lax.fori_loop(0, width // 512, body, 0)

    chain = SumChain(in_order(partial, rows), z_one, z_two, z_three, there, 0)
    pieces = [(first, min(group, units - first)) for first in range(0, units, group)]
    forward((0,), True, second)
    backward((0,), True)
    pl.semaphore_wait(entry, 5)
    chain.one()
    forward((1,), False, third)
    backward((1,), False)
    forward((2, 3), False, ())
    backward((2, 3), False)
    chain.add_one()
    chain.two()

    for p in range(n_s):
        loads[p][3].wait()
        loads[p][4].wait()

    def down_body(t, carry):
        unit_rows = pl.ds(pl.multiple_of(t * tile, tile), tile)
        value = lax.dot_general(
            hidden[:, unit_rows], upstream[...], (((0,), (0,)), ((), ())),
            preferred_element_type=full,
        )
        down[unit_rows] = value.astype(jnp.bfloat16)
        return carry

    lax.fori_loop(0, tiles, down_body, 0)
    down_core = [
        there(part(down, plane[2 * i + 1], unit), down_arrived.at[i], 6 + i, fsdp=plane[1])
        for i in range(4)
    ]
    for i in (3, 1, 2, 0):
        down_core[i].start()

    again_in = [upstream] + [
        d_both.at[:count, i * width : (i + 1) * width] for i, (_, count) in enumerate(pieces[1:])
    ]
    again = [
        here(w_down.at[first : first + count], place, 36 + i)
        for i, ((first, count), place) in enumerate(zip(pieces, again_in))
    ]
    again[0].start()

    def gu_body(m, carry):
        in_columns = pl.ds(pl.multiple_of(m * tile, tile), tile)
        turned = normed[:, in_columns].T
        for first in range(0, 2 * units, units // 3):
            value = jnp.dot(turned, d_both[:, first : first + units // 3], preferred_element_type=full)
            gu[in_columns, first : first + units // 3] = value.astype(jnp.bfloat16)
        return carry

    lax.fori_loop(0, 2, gu_body, 0)
    chain.add_two()
    chain.three()

    class Arrivals:
        def __init__(self, ref, size, arrived, copies, turns, index):
            self.ref, self.size, self.copies = ref, size, copies
            self.pieces = {}
            for n, i in enumerate((3, 1, 2, 0)):
                self.pieces[i] = [
                    (here(arrived.at[i, :, columns], piece, index + 3 * (n % 2) + k), columns, piece)
                    for k, (columns, piece) in enumerate(turns[n % 2])
                ]

        def fetch(self, i):
            self.copies[i].wait_recv()
            for copy, _, _ in self.pieces[i]:
                copy.start()

        def add(self, i):
            target = part(self.ref, plane[2 * i], self.size)
            for copy, columns, piece in self.pieces[i]:
                copy.wait()
                target[:, columns] = target[:, columns] + piece[...]

    down_turns = [[(pl.ds(0, width), piece)] for piece in (down_piece.at[0], down_piece.at[1])]
    down_sum = Arrivals(down, unit, down_arrived, down_core, down_turns, 26)
    down_sum.fetch(3)
    for i, following in ((3, 1), (1, 2), (2, 0), (0, None)):
        if following is not None:
            down_sum.fetch(following)
        down_sum.add(i)
    to_x, to_y, to_both = [part(down, plane[k], unit) for k in (2, 4, 6)]
    low_half, high_half = pl.ds(0, half), pl.ds(half, half)
    down_first = [
        there(to_x.at[:, low_half], down_x.at[0], 10, fsdp=plane[2]),
        there(to_both.at[:, low_half], down_x.at[1], 11, fsdp=plane[2]),
        there(to_y.at[:, high_half], down_y.at[0], 12, fsdp=plane[4]),
        there(to_both.at[:, high_half], down_y.at[1], 13, fsdp=plane[4]),
    ]
    for copy in down_first:
        copy.start()
    lax.fori_loop(2, width // tile, gu_body, 0)
    gu_core = [
        there(part(gu, plane[2 * i + 1], block), gu_arrived.at[i], 16 + i, fsdp=plane[1])
        for i in range(4)
    ]
    for i in (3, 1, 2, 0):
        gu_core[i].start()

    for copy in again[1:]:
        copy.start()
    for copy in again:
        copy.wait()

    def branch_body(n, carry):
        out_columns = pl.ds(pl.multiple_of(n * wide, wide), wide)
        for m in range(2):
            mine = slice(m * half_rows, (m + 1) * half_rows)
            value = jnp.zeros((half_rows, wide), full)
            for i, (first, count) in enumerate(pieces):
                value += jnp.dot(
                    hidden[mine, first : first + count], again_in[i][:, out_columns],
                    preferred_element_type=full,
                )
            normed[mine, out_columns] = value.astype(jnp.bfloat16)
        return carry

    lax.fori_loop(0, width // wide, branch_body, 0)
    chain.last(columns)
    chain_branch = SumChain(in_order(normed, rows), z_one, z_two, z_three, there, 22)
    chain_branch.one()
    down_second = [
        there(to_y.at[:, low_half], down_last.at[0], 14, fsdp=plane[4]),
        there(to_x.at[:, high_half], down_last.at[1], 15, fsdp=plane[2]),
    ]
    down_first[1].wait_recv()
    to_y[:, :half] = to_y[:, :half] + down_x[1]
    down_second[0].start()
    down_first[3].wait_recv()
    to_x[:, half:] = to_x[:, half:] + down_y[1]
    down_second[1].start()
    gu_turns = [
        [(pl.ds(k * units, units), hidden.at[(2 * n + k) * block : (2 * n + k + 1) * block]) for k in range(2)]
        for n in range(2)
    ]
    gu_arrivals = Arrivals(gu, block, gu_arrived, gu_core, gu_turns, 26)
    store = [here(part(gu, plane[2 * i], block), gu_sum.at[i], 32 + i) for i in range(4)]
    gu_arrivals.fetch(3)
    for i, following in ((3, 1), (1, 2), (2, 0), (0, None)):
        if following is not None:
            gu_arrivals.fetch(following)
        gu_arrivals.add(i)
        store[i].start()
    down_first[0].wait_recv()
    down_first[2].wait_recv()
    own = part(down, f, unit)
    down_second[0].wait_recv()
    grad_down[:, :half] = (
        own[:, :half].astype(full) + down_x[0].astype(full) + down_last[0].astype(full)
    )
    down_second[1].wait_recv()
    grad_down[:, half:] = (
        own[:, half:].astype(full) + down_y[0].astype(full) + down_last[1].astype(full)
    )
    chain_branch.add_one()
    chain_branch.one_sent()
    store_branch = here(normed, branch, 39)
    store_branch.start()
    chain.one_sent()
    chain.two_sent()
    chain.three_sent()
    for copy in down_core + down_first + down_second + gu_core:
        copy.wait_send()
    for copy in store + [store_branch]:
        copy.wait()


def ffn(normed_all, upstream_all, w_gu, w_down, hidden, factor_gate, factor_up):
    group, width = normed_all.shape
    units = w_down.shape[0]
    rows = group // SEQ
    unit, block, half = units // 8, width // 8, width // 2
    low, full = jnp.bfloat16, jnp.float32
    vmem = pl.BlockSpec(memory_space=pltpu.VMEM)
    hbm = pl.BlockSpec(memory_space=pl.ANY)
    shape = jax.ShapeDtypeStruct
    return pl.pallas_call(
        ffn_kernel,
        in_specs=[hbm] * 7,
        out_specs=[vmem] * 2 + [hbm] * 4,
        out_shape=[
            shape((rows, width), full),
            shape((unit, width), full),
            shape((4, block, 2 * units), low),
            shape((group, width), low),
            shape((4, unit, width), low),
            shape((4, block, 2 * units), low),
        ],
        scratch_shapes=[
            pltpu.VMEM((group, width), low),
            pltpu.VMEM((group, width), low),
            pltpu.VMEM((width, 2 * units), low),
            pltpu.VMEM((units, width), low),
            pltpu.VMEM((group, units), low),
            pltpu.VMEM((group, 2 * units), low),
            pltpu.VMEM((group, width), low),
            pltpu.VMEM((rows, width), low),
            pltpu.VMEM((2, rows, width), low),
            pltpu.VMEM((2, rows, width), low),
            pltpu.VMEM((2, unit, half), low),
            pltpu.VMEM((2, unit, half), low),
            pltpu.VMEM((2, unit, half), low),
            pltpu.VMEM((2, unit, width), low),
            pltpu.SemaphoreType.DMA((40,)),
            pltpu.SemaphoreType.DMA((28,)),
            pltpu.SemaphoreType.DMA((28,)),
        ],
        compiler_params=pltpu.CompilerParams(
            collective_id=1, has_side_effects=True, vmem_limit_bytes=63 * 2**20
        ),
        name="ffn",
    )(normed_all, upstream_all, w_gu, w_down, hidden, factor_gate, factor_up)[:4]


def back_kernel(
    gain_two, slot_row, first_row, logsum, gain_one, cosine, sine, slots,
    resid_in, cotangent_in, attended_in, queries_in, paired_in, normed_in, tokens_in,
    columns, w_out, w_qkv, gu_sum, branch,
    layer, input_rows, vector, grad_out, grad_qkv, gu_rows,
    resid, cotangent, attended, queries, paired, normed_one, tokens,
    out_w, qkv, gu_own, gu_to_y, gu_to_x, gu_x, gu_y, gu_ended,
    branch_v, z_one, z_two, z_three, working, bias, d_branch, d_attended, d_qkv, d_resid,
    keys_grad, values_grad, dkv, dkv_in,
    out_arrived, out_x, out_y, out_ended, qkv_arrived, qkv_x, qkv_y, qkv_ended,
    out_in, qkv_one, qkv_two, qkv_three, vector_in,
    load, ssem, rsem,
):
    f = lax.axis_index("fsdp")
    s = lax.axis_index("seq")
    rows, width = tokens.shape
    n_s = paired.shape[0]
    kv_width = KV_HEADS * HEAD_DIM
    repeat = HEADS // KV_HEADS
    scale = HEAD_DIM ** (-0.5)
    block = width // 8
    piece = block // n_s
    units = gu_sum.shape[2] // 2
    tile = 256
    full, low = jnp.float32, jnp.bfloat16
    plane = [f ^ k for k in range(8)]

    entry = pltpu.get_barrier_semaphore()
    for k in (1, 2, 4):
        pl.semaphore_signal(entry, inc=1, device_id={"fsdp": plane[k]}, device_id_type=MESH)
    for j in range(1, n_s):
        pl.semaphore_signal(
            entry, inc=1, device_id={"seq": lax.rem(s + j, n_s)}, device_id_type=MESH
        )

    def here(source, target, index):
        return pltpu.make_async_copy(source, target, load.at[index])

    def there(source, target, index, **device):
        return pltpu.make_async_remote_copy(
            src_ref=source, dst_ref=target, send_sem=ssem.at[index], recv_sem=rsem.at[index],
            device_id=device, device_id_type=MESH,
        )

    low_units, high_units = pl.ds(0, units), pl.ds(units, units)
    load_branch = here(branch, branch_v, 0)
    load_out = here(w_out, out_w, 1)
    load_gu = [
        here(gu_sum.at[0], gu_own, 2),
        here(gu_sum.at[2, :, low_units], gu_to_y, 3),
        here(gu_sum.at[1, :, high_units], gu_to_x, 4),
    ]
    load_qkv = here(w_qkv, qkv, 5)
    load_columns = here(columns, working, 7)
    load_rows = [
        here(source, place, 10 + i)
        for i, (source, place) in enumerate((
            (resid_in, resid), (cotangent_in, cotangent), (attended_in, attended),
            (queries_in, queries), (paired_in, paired), (normed_in, normed_one),
            (tokens_in, tokens),
        ))
    ]
    for copy in [load_columns] + load_rows[:2] + [load_branch]:
        copy.start()

    gu_first = [
        there(gu_sum.at[3, :, low_units], gu_x.at[1], 0, fsdp=plane[2]),
        there(gu_sum.at[3, :, high_units], gu_y.at[1], 1, fsdp=plane[4]),
        there(gu_sum.at[1, :, low_units], gu_x.at[0], 2, fsdp=plane[2]),
        there(gu_sum.at[2, :, high_units], gu_y.at[0], 3, fsdp=plane[4]),
    ]
    gu_second = [
        there(gu_to_y, gu_ended.at[0], 4, fsdp=plane[4]),
        there(gu_to_x, gu_ended.at[1], 5, fsdp=plane[2]),
    ]

    def around(j):
        return {"seq": lax.rem(s + j, n_s)}

    def rows_for(ref, first, j):
        owner = lax.rem(s + j, n_s)
        return ref.at[pl.ds(pl.multiple_of(first + owner * piece, 16), piece)]

    gu_send = [there(rows_for(gu_own, 0, j), gu_rows.at[j], 5 + j, **around(j)) for j in range(1, n_s)]
    dkv_send = [
        [
            there(dkv.at[g, lax.rem(s + j, n_s)], dkv_in.at[g, j], 8 + 3 * g + j, **around(j))
            for j in range(1, n_s)
        ]
        for g in range(KV_HEADS)
    ]
    chain = SumChain(in_order(branch_v, rows), z_one, z_two, z_three, there, 16)
    sum_out = SumPlane(out_w, block, plane, out_arrived, out_x, out_y, out_ended, there, 24)
    sum_qkv = SumPlane(qkv, block, plane, qkv_arrived, qkv_x, qkv_y, qkv_ended, there, 36)

    def own_part(ref):
        return lambda j: rows_for(ref, f * block, n_s - j)

    out_send = [
        there(own_part(out_w)(n_s - j), out_in.at[j], 47 + j, **around(j)) for j in range(1, n_s)
    ]
    chain_qkv = SumChain(own_part(qkv), qkv_one, qkv_two, qkv_three, there, 54)
    vector_send = [
        there(vector_in.at[0], vector_in.at[1], 60, fsdp=plane[1]),
        there(vector_in.at[2], vector_in.at[3], 61, fsdp=plane[2]),
        there(vector_in.at[4], vector_in.at[5], 62, fsdp=plane[4]),
    ] + [there(vector_in.at[6], vector_in.at[6 + j], 62 + j, **around(j)) for j in range(1, n_s)]

    pl.semaphore_wait(entry, 3 + n_s - 1)
    for copy in gu_first:
        copy.start()
    load_branch.wait()
    chain.two()

    def norm_back(value, gain, grad):
        root = lax.rsqrt(jnp.mean(value * value, -1, keepdims=True) + epsilon)
        scaled = gain * grad
        inner = jnp.mean(scaled * value, -1, keepdims=True)
        gain_grad = jnp.sum(grad * (value * root), 0, keepdims=True)
        return root * scaled - value * (root * root * root * inner), gain_grad

    load_columns.wait()
    for copy in load_rows[:2]:
        copy.wait()
    for copy in [load_out] + load_rows[2:] + load_gu + [load_qkv]:
        copy.start()
    d_norm, gain_two_grad = norm_back(resid[...], gain_two[...], working[...])
    d_total = cotangent[...].astype(full) + d_norm
    d_branch[...] = d_total.astype(low)
    d_resid[...] = d_total
    for j in range(n_s):
        keys_slot = slots[j]
        keys_slot = jnp.concatenate([keys_slot] * (rows // 128), 1)
        ok = (keys_slot <= slot_row[0:1]) & (keys_slot >= first_row[0:1])
        bias[j * rows : (j + 1) * rows] = jnp.where(ok, 0.0, -1e30)
    load_out.wait()
    for copy in load_rows[2:]:
        copy.wait()
    for n in range(width // tile):
        value = lax.dot_general(
            d_branch[...], out_w[n * tile : (n + 1) * tile], (((1,), (1,)), ((), ())),
            preferred_element_type=full,
        )
        d_attended[:, n * tile : (n + 1) * tile] = value.astype(low)

    def turned_back(value):
        return value * cosine[...] + pltpu.roll(value * sine[...], HEAD_DIM // 2, 1)

    for g in range(KV_HEADS):
        keys = paired[:, :, g * HEAD_DIM : (g + 1) * HEAD_DIM].reshape(n_s * rows, HEAD_DIM)
        values = paired[:, :, kv_width + g * HEAD_DIM : kv_width + (g + 1) * HEAD_DIM]
        values = values.reshape(n_s * rows, HEAD_DIM)
        keys_grad[...] = jnp.zeros_like(keys_grad)
        values_grad[...] = jnp.zeros_like(values_grad)

        def head(i, carry, g=g, keys=keys, values=values):
            h = g * repeat + i
            head_columns = pl.ds(pl.multiple_of(h * HEAD_DIM, HEAD_DIM), HEAD_DIM)
            query = queries[:, head_columns]
            grad = d_attended[:, head_columns]
            raw = lax.dot_general(
                keys, query, (((1,), (1,)), ((), ())), preferred_element_type=full
            )
            logs = logsum[pl.ds(pl.multiple_of(h * 8, 8), 8)][0:1]
            probs = jnp.exp(raw * scale + bias[...] - logs)
            d_probs = lax.dot_general(
                values, grad, (((1,), (1,)), ((), ())), preferred_element_type=full
            )
            delta = jnp.sum(probs * d_probs, 0, keepdims=True)
            d_score = (probs * (d_probs - delta)).astype(low)
            turned = lax.dot_general(
                keys, d_score, (((0,), (0,)), ((), ())), preferred_element_type=full
            )
            d_qkv[:, head_columns] = turned_back((turned * scale).T).astype(low)
            keys_grad[...] += jnp.dot(d_score, query, preferred_element_type=full) * scale
            values_grad[...] += jnp.dot(probs.astype(low), grad, preferred_element_type=full)
            return carry

        lax.fori_loop(0, repeat, head, 0)
        dkv[g, :, :, :HEAD_DIM] = keys_grad[...].astype(low).reshape(n_s, rows, HEAD_DIM)
        dkv[g, :, :, HEAD_DIM:] = values_grad[...].astype(low).reshape(n_s, rows, HEAD_DIM)
        for copy in dkv_send[g]:
            copy.start()

    turned = attended[...].T
    for n in range(width // tile):
        n_columns = slice(n * tile, (n + 1) * tile)
        value = jnp.dot(turned, d_branch[:, n_columns], preferred_element_type=full)
        out_w[:, n_columns] = value.astype(low)
    sum_out.start_core()
    load_qkv.wait()

    def back_one(first, count, start):
        for n in range(width // tile):
            n_rows = slice(n * tile, (n + 1) * tile)
            value = lax.dot_general(
                d_qkv[:, first : first + count], qkv[n_rows, first : first + count],
                (((1,), (1,)), ((), ())), preferred_element_type=full,
            )
            working[:, n_rows] = value if start else working[:, n_rows] + value

    back_one(0, width, True)
    normed_turned = normed_one[...].T
    for n in range(width // tile):
        n_columns = slice(n * tile, (n + 1) * tile)
        value = jnp.dot(normed_turned, d_qkv[:, n_columns], preferred_element_type=full)
        qkv[:, n_columns] = value.astype(low)
    for copy in load_gu:
        copy.wait()
    gu_first[0].wait_recv()
    gu_to_y[...] = gu_to_y[...] + gu_x[1]
    gu_second[0].start()
    gu_first[1].wait_recv()
    gu_to_x[...] = gu_to_x[...] + gu_y[1]
    gu_second[1].start()

    for g in range(KV_HEADS):
        for copy in dkv_send[g]:
            copy.wait_recv()
        total = dkv[g, s].astype(full)
        for j in range(1, n_s):
            total = total + dkv_in[g, j].astype(full)
        key_columns = slice(width + g * HEAD_DIM, width + (g + 1) * HEAD_DIM)
        value_columns = slice(width + kv_width + g * HEAD_DIM, width + kv_width + (g + 1) * HEAD_DIM)
        d_qkv[:, key_columns] = turned_back(total[:, :HEAD_DIM]).astype(low)
        d_qkv[:, value_columns] = total[:, HEAD_DIM:].astype(low)
    back_one(width, 2 * kv_width, False)
    value = jnp.dot(normed_turned, d_qkv[:, width:], preferred_element_type=full)
    qkv[:, width:] = value.astype(low)
    sum_qkv.start_core()
    chain.add_two()
    chain.three()

    d_norm, gain_one_grad = norm_back(tokens[...].astype(full), gain_one[...], working[...])
    input_rows[...] = (d_resid[...] + d_norm).astype(low)
    bias_grad = jnp.sum(d_qkv[...].astype(full), 0, keepdims=True)
    vectors = jnp.concatenate([gain_one_grad, gain_two_grad, bias_grad], 1)
    part = vectors.shape[1] // 8
    for r in range(8):
        vector_in[0, r : r + 1] = vectors[:, r * part : (r + 1) * part]
    vector_send[0].start()
    sum_qkv.start_first()
    vector_send[0].wait_recv()
    vector_in[2] = vector_in[0] + vector_in[1]
    vector_send[1].start()
    gu_first[2].wait_recv()
    gu_second[0].wait_recv()
    total = gu_own[:, :units].astype(full) + gu_x[0].astype(full) + gu_ended[0].astype(full)
    gu_own[:, :units] = total.astype(low)
    gu_first[3].wait_recv()
    gu_second[1].wait_recv()
    total = gu_own[:, units:].astype(full) + gu_y[0].astype(full) + gu_ended[1].astype(full)
    gu_own[:, units:] = total.astype(low)
    for copy in gu_send:
        copy.start()
    keep_rows = here(rows_for(gu_own, 0, 0), gu_rows.at[0], 6)
    keep_rows.start()
    sum_out.start_first()

    vector_send[1].wait_recv()
    vector_in[4] = vector_in[2] + vector_in[3]
    vector_send[2].start()
    sum_qkv.start_second()
    sum_out.start_second()
    vector_send[2].wait_recv()
    vector_in[6] = vector_in[4] + vector_in[5]
    for copy in vector_send[3:]:
        copy.start()
    sum_qkv.finish()
    chain_qkv.one()
    chain.last(working)
    layer[...] = (resid[...] + working[...]).astype(low)
    chain_qkv.add_one()
    chain_qkv.two()
    sum_out.finish()
    for copy in out_send:
        copy.start()
    for copy in vector_send[3:]:
        copy.wait_recv()
    vector[...] = vector_in[6] + vector_in[7] + vector_in[8] + vector_in[9]
    chain_qkv.add_two()
    chain_qkv.three()
    chain_qkv.last(grad_qkv)
    total = own_part(out_w)(0)[...].astype(full)
    for copy in out_send:
        copy.wait_recv()
    for j in range(1, n_s):
        total = total + out_in[j].astype(full)
    grad_out[...] = total
    for copy in gu_send:
        copy.wait_recv()
    keep_rows.wait()
    chain_qkv.one_sent()
    chain_qkv.two_sent()
    chain_qkv.three_sent()
    chain.two_sent()
    chain.three_sent()
    sum_out.sent()
    sum_qkv.sent()
    for copy in gu_first + gu_second + gu_send + out_send + vector_send:
        copy.wait_send()
    for g in range(KV_HEADS):
        for copy in dkv_send[g]:
            copy.wait_send()


def back(
    columns, resid, gain_two, cotangent, attended, queries, paired, slots, slot_row, first_row,
    logsum, normed_one, tokens, gain_one, cosine, sine, w_out, w_qkv, gu_sum, branch,
):
    rows, width = tokens.shape
    n_s = paired.shape[0]
    group = n_s * rows
    kv_width = KV_HEADS * HEAD_DIM
    qkv_width = width + 2 * kv_width
    block = width // 8
    piece = block // n_s
    units = gu_sum.shape[2] // 2
    low, full = jnp.bfloat16, jnp.float32
    vmem = pl.BlockSpec(memory_space=pltpu.VMEM)
    hbm = pl.BlockSpec(memory_space=pl.ANY)
    shape = jax.ShapeDtypeStruct
    vectors = (2 * width + qkv_width) // 8
    return pl.pallas_call(
        back_kernel,
        in_specs=[vmem] * 8 + [hbm] * 12,
        out_specs=[vmem] * 5 + [hbm],
        out_shape=[
            shape((rows, width), low),
            shape((rows, width), low),
            shape((8, vectors), full),
            shape((piece, width), full),
            shape((piece, qkv_width), full),
            shape((n_s, piece, 2 * units), low),
        ],
        scratch_shapes=[
            pltpu.VMEM((rows, width), full),
            pltpu.VMEM((rows, width), low),
            pltpu.VMEM((rows, width), low),
            pltpu.VMEM((rows, width), low),
            pltpu.VMEM(paired.shape, low),
            pltpu.VMEM((rows, width), low),
            pltpu.VMEM((rows, width), low),
            pltpu.VMEM((width, width), low),
            pltpu.VMEM((width, qkv_width), low),
            pltpu.VMEM((block, 2 * units), low),
            pltpu.VMEM((block, units), low),
            pltpu.VMEM((block, units), low),
            pltpu.VMEM((2, block, units), low),
            pltpu.VMEM((2, block, units), low),
            pltpu.VMEM((2, block, units), low),
            pltpu.VMEM((group, width), low),
            pltpu.VMEM((rows, width), low),
            pltpu.VMEM((2, rows, width), low),
            pltpu.VMEM((2, rows, width), low),
            pltpu.VMEM((rows, width), full),
            pltpu.VMEM((group, rows), full),
            pltpu.VMEM((rows, width), low),
            pltpu.VMEM((rows, width), low),
            pltpu.VMEM((rows, qkv_width), low),
            pltpu.VMEM((rows, width), full),
            pltpu.VMEM((group, HEAD_DIM), full),
            pltpu.VMEM((group, HEAD_DIM), full),
            pltpu.VMEM((KV_HEADS, n_s, rows, 2 * HEAD_DIM), low),
            pltpu.VMEM((KV_HEADS, n_s, rows, 2 * HEAD_DIM), low),
            pltpu.VMEM((4, block, width), low),
            pltpu.VMEM((2, block, width // 2), low),
            pltpu.VMEM((2, block, width // 2), low),
            pltpu.VMEM((2, block, width // 2), low),
            pltpu.VMEM((4, block, qkv_width), low),
            pltpu.VMEM((2, block, qkv_width // 2), low),
            pltpu.VMEM((2, block, qkv_width // 2), low),
            pltpu.VMEM((2, block, qkv_width // 2), low),
            pltpu.VMEM((n_s, piece, width), low),
            pltpu.VMEM((piece, qkv_width), low),
            pltpu.VMEM((2, piece, qkv_width), low),
            pltpu.VMEM((2, piece, qkv_width), low),
            pltpu.VMEM((10, 8, vectors), full),
            pltpu.SemaphoreType.DMA((18,)),
            pltpu.SemaphoreType.DMA((68,)),
            pltpu.SemaphoreType.DMA((68,)),
        ],
        compiler_params=pltpu.CompilerParams(
            collective_id=2, has_side_effects=True, vmem_limit_bytes=63 * 2**20
        ),
        name="back",
    )(
        gain_two, slot_row, first_row, logsum, gain_one, cosine, sine, slots,
        resid, cotangent, attended, queries, paired, normed_one, tokens,
        columns, w_out, w_qkv, gu_sum, branch,
    )


def finish_kernel(
    layer, input_rows, grad_out, grad_qkv, grad_down, gu_rows,
    layer_out, input_grad, out_out, query_out, key_out, value_out, down_out, gate_out, up_out,
    layer_v, input_v, out_v, qkv_v, down_v, gu_v, gate_v, up_v, load, store,
):
    s = lax.axis_index("seq")
    n_s = gu_rows.shape[0]
    width = grad_out.shape[1]
    kv_width = KV_HEADS * HEAD_DIM
    unit_pad = grad_down.shape[0]
    unit = down_out.shape[0]
    units = gu_rows.shape[2] // 2
    moves = [
        (layer, layer_v, [(layer_v, layer_out)]),
        (input_rows, input_v, [(input_v, input_grad)]),
        (grad_down, down_v, [(down_v.at[:unit], down_out)]),
        (grad_out, out_v, [(out_v, out_out)]),
        (grad_qkv, qkv_v, [
            (qkv_v.at[:, :width], query_out),
            (qkv_v.at[:, width : width + kv_width], key_out),
            (qkv_v.at[:, width + kv_width :], value_out),
        ]),
    ]
    load_gu = pltpu.make_async_copy(gu_rows, gu_v, load.at[0])
    load_gu.start()
    loads, stores = [], []
    for i, (source, place, _) in enumerate(moves):
        loads.append(pltpu.make_async_copy(source, place, load.at[1 + i]))
        loads[-1].start()
    for copy, (_, _, parts) in zip(loads, moves):
        copy.wait()
        for source, target in parts:
            stores.append(pltpu.make_async_copy(source, target, store.at[len(stores)]))
            stores[-1].start()
    load_gu.wait()
    window = 512
    lanes = lax.broadcasted_iota(jnp.int32, (gu_rows.shape[1], 128), 1)
    for base, out, target_out in ((0, gate_v, gate_out), (units, up_v, up_out)):
        for f in range(units // unit_pad):
            for owner in range(n_s):
                source = base + f * unit_pad
                begin = min(source // 128 * 128, 2 * units - window)
                target = (f * n_s + owner) * unit
                first = target // 128 * 128
                slot = lax.rem(s + n_s - owner, n_s)
                value = gu_v[slot, :, begin : begin + window].astype(jnp.float32)
                turn = ((target - first) - (source - begin)) % window
                if turn:
                    value = pltpu.roll(value, turn, 1)
                for t in range(first, min(target + unit, out.shape[1]), 128):
                    part = value[:, t - first : t - first + 128]
                    if t < target:
                        part = jnp.where(lanes >= target - t, part, out[:, t : t + 128])
                    out[:, t : t + 128] = part
        stores.append(pltpu.make_async_copy(out, target_out, store.at[len(stores)]))
        stores[-1].start()
    for copy in stores:
        copy.wait()


def finish(layer, input_rows, grad_out, grad_qkv, grad_down, gu_rows, unit, hidden_width):
    piece, width = grad_out.shape
    kv_width = KV_HEADS * HEAD_DIM
    low, full = jnp.bfloat16, jnp.float32
    shape = jax.ShapeDtypeStruct
    hbm = pl.BlockSpec(memory_space=pl.ANY)
    wide = pltpu.VMEM((piece, hidden_width), full)
    return pl.pallas_call(
        finish_kernel,
        in_specs=[hbm] * 6,
        out_specs=[hbm] * 9,
        out_shape=[
            shape(layer.shape, low),
            shape(layer.shape, low),
            shape((piece, width), full),
            shape((piece, width), full),
            shape((piece, kv_width), full),
            shape((piece, kv_width), full),
            shape((unit, width), full),
            shape((piece, hidden_width), full),
            shape((piece, hidden_width), full),
        ],
        scratch_shapes=[
            pltpu.VMEM(value.shape, value.dtype)
            for value in (layer, input_rows, grad_out, grad_qkv, grad_down, gu_rows)
        ] + [wide, wide, pltpu.SemaphoreType.DMA((6,)), pltpu.SemaphoreType.DMA((9,))],
        compiler_params=pltpu.CompilerParams(vmem_limit_bytes=63 * 2**20),
        name="finish",
    )(layer, input_rows, grad_out, grad_qkv, grad_down, gu_rows)


def per_device(
    tokens, cotangent, lengths, balance, norm1_gain, w_query, b_query, w_key, b_key,
    w_value, b_value, w_out, norm2_gain, w_gate, w_up, w_down,
):
    seq_count = lax.axis_size("seq")
    fsdp_count = lax.axis_size("fsdp")
    seq_rank = lax.axis_index("seq")
    fsdp_rank = lax.axis_index("fsdp")
    rows_here, width = tokens.shape
    kv_width = KV_HEADS * HEAD_DIM
    hidden_width = w_gate.shape[1]
    unit = hidden_width // (fsdp_count * seq_count)
    (
        weight_gu, weight_down, upstream_all, normed_all, hidden, factor_gate, factor_up,
        weight_qkv, weight_out, queries, paired, slots, logsum, attended, resid, normed_one,
        gain_one, gain_two, slot_row, first_row, cosine, sine,
    ) = front(
        tokens, cotangent, lengths, balance, (norm1_gain, norm2_gain, b_query, b_key, b_value),
        (w_query, w_key, w_value, w_out, w_gate, w_up, w_down),
    )
    columns, grad_down, gu_sum, branch = ffn(
        normed_all, upstream_all, weight_gu, weight_down, hidden, factor_gate, factor_up
    )
    layer, input_rows, vectors, grad_out, grad_qkv, gu_rows = back(
        columns, resid, gain_two, cotangent, attended, queries, paired, slots, slot_row, first_row,
        logsum, normed_one, tokens, gain_one, cosine, sine, weight_out, weight_qkv, gu_sum, branch,
    )
    (
        layer_out, input_grad, grad_out, grad_query, grad_key, grad_value, grad_down, grad_gate,
        grad_up,
    ) = finish(layer, input_rows, grad_out, grad_qkv, grad_down, gu_rows, unit, hidden_width)
    vectors = vectors.reshape(-1)
    own = width // (fsdp_count * seq_count)
    first = (fsdp_rank * seq_count + seq_rank) * own

    def own_part(offset):
        return lax.dynamic_slice_in_dim(vectors, offset + first, own, 0)

    biases = 2 * width
    return (
        layer_out,
        input_grad,
        own_part(0),
        grad_query,
        own_part(biases),
        grad_key,
        vectors[biases + width : biases + width + kv_width],
        grad_value,
        vectors[biases + width + kv_width :],
        grad_out,
        own_part(width),
        grad_gate,
        grad_up,
        grad_down,
    )


def solution(mesh):
    both = P(("fsdp", "seq"), None)
    both_one = P(("fsdp", "seq"))
    placed = (
        both, both, P("fsdp", None), both_one, P("fsdp"), P("fsdp", None), P("fsdp"),
        P("fsdp", None), P("fsdp"), P("fsdp", None), P("fsdp"), P("fsdp", None), P("fsdp"),
        P("fsdp", None), P("fsdp", None), P("fsdp", None),
    )
    return jax.shard_map(
        per_device if mesh.shape["fsdp"] == 8 else plain_device,
        mesh=mesh,
        in_specs=placed,
        out_specs=(
            both, both, both_one, both, both_one, both, P(), both, P(), both, both_one,
            both, both, both,
        ),
        check_vma=False,
    )
```

```python
import jax
import jax.numpy as jnp
import numpy as np
from jax import lax
from jax.experimental import pallas as pl
from jax.experimental.pallas import tpu as pltpu
from jax.sharding import PartitionSpec as P

HEADS = 12
KV_HEADS = 2
HEAD_DIM = 128

MESH = pl.DeviceIdType.MESH

epsilon = 1e-06
rope_base = 1000000.0


def norm_piece(values, gain):
    return values * lax.rsqrt(jnp.mean(values * values, -1, keepdims=True) + epsilon) * gain


def rope_tables(position):
    half = HEAD_DIM // 2
    inverse = rope_base ** (-(jnp.arange(half, dtype=jnp.float32) * 2.0 / HEAD_DIM))
    angle = position.astype(jnp.float32)[:, None] * inverse[None, :]
    cosine = jnp.concatenate([jnp.cos(angle), jnp.cos(angle)], -1)
    sine = jnp.concatenate([jnp.sin(angle), jnp.sin(angle)], -1)
    return (cosine, sine)


def turn_half(values):
    half = values.shape[-1] // 2
    return jnp.concatenate([-values[..., half:], values[..., :half]], -1)


def rotate(values, cosine, sine):
    return values * cosine[:, None, :] + turn_half(values) * sine[:, None, :]


def rotate_back(grads, cosine, sine):
    return grads * cosine[:, None, :] - turn_half(grads * sine[:, None, :])


def segment_of(slots, starts):
    return (slots >= starts[1]).astype(jnp.int32) + (slots >= starts[2]).astype(jnp.int32)


def contract_rows(left, right):
    return lax.dot_general(
        left, right, (((0,), (0,)), ((), ())), preferred_element_type=jnp.float32
    )


def contract_columns(left, right):
    return lax.dot_general(
        left, right, (((1,), (1,)), ((), ())), preferred_element_type=jnp.float32
    )


def plain_device(
    tokens, cotangent, lengths, balance, norm1_gain, w_query, b_query, w_key, b_key,
    w_value, b_value, w_out, norm2_gain, w_gate, w_up, w_down,
):
    seq_count = lax.axis_size("seq")
    fsdp_count = lax.axis_size("fsdp")
    seq_rank = lax.axis_index("seq")
    rows_here, width = tokens.shape
    group = seq_count * rows_here
    kv_width = KV_HEADS * HEAD_DIM
    qkv_width = width + 2 * kv_width
    hidden_width = w_gate.shape[1]
    unit = hidden_width // (fsdp_count * seq_count)
    own_units = hidden_width // seq_count
    weight_rows = w_gate.shape[0]
    score_scale = HEAD_DIM ** (-0.5)
    repeat = HEADS // KV_HEADS

    slot = balance % group
    slots_all = lax.all_gather(slot, "seq", axis=0, tiled=True)
    seq_lengths = lengths[0]
    starts = jnp.cumsum(seq_lengths) - seq_lengths
    segment = segment_of(slot, starts)
    segments_all = segment_of(slots_all, starts)
    first_row = jnp.where(segment == 0, starts[0], jnp.where(segment == 1, starts[1], starts[2]))
    cosine, sine = rope_tables(slot - first_row)
    allowed = (segment[:, None] == segments_all[None, :]) & (slots_all[None, :] <= slot[:, None])

    small = jnp.concatenate([norm1_gain, norm2_gain, b_query, b_key, b_value], 0)[None]
    small = lax.all_gather(small, "fsdp", axis=0, tiled=True)
    piece = norm1_gain.shape[0]
    bias_piece = b_key.shape[0]
    gain_one = small[:, :piece].reshape(-1).astype(jnp.float32)
    gain_two = small[:, piece : 2 * piece].reshape(-1).astype(jnp.float32)
    bias_qkv = jnp.concatenate(
        [
            small[:, 2 * piece : 3 * piece].reshape(-1),
            small[:, 3 * piece : 3 * piece + bias_piece].reshape(-1),
            small[:, 3 * piece + bias_piece :].reshape(-1),
        ],
        0,
    ).astype(jnp.float32)
    weight_qkv = lax.all_gather(
        jnp.concatenate([w_query, w_key, w_value], 1), "fsdp", axis=0, tiled=True
    )
    weight_out = lax.all_gather(w_out, "fsdp", axis=0, tiled=True)
    upstream_all = lax.all_gather(cotangent, "seq", axis=0, tiled=True)

    def own_columns(weight):
        cut = weight.reshape(weight_rows, fsdp_count, seq_count, unit)
        return lax.dynamic_index_in_dim(cut, seq_rank, 2, False).reshape(weight_rows, own_units)

    weight_gu = lax.all_gather(
        jnp.concatenate([own_columns(w_gate), own_columns(w_up)], 1), "fsdp", axis=0, tiled=True
    )
    weight_down = lax.all_gather(
        lax.dynamic_slice_in_dim(w_down, seq_rank * unit, unit, 0), "fsdp", axis=0, tiled=True
    )

    inputs = tokens.astype(jnp.float32)
    normed_one = norm_piece(inputs, gain_one).astype(jnp.bfloat16)
    projected = jnp.dot(normed_one, weight_qkv, preferred_element_type=jnp.float32) + bias_qkv
    query_pre = projected[:, :width].reshape(rows_here, HEADS, HEAD_DIM)
    key_pre = projected[:, width : width + kv_width].reshape(rows_here, KV_HEADS, HEAD_DIM)
    value_pre = projected[:, width + kv_width :]
    queries = rotate(query_pre, cosine, sine).astype(jnp.bfloat16)
    keys = rotate(key_pre, cosine, sine).astype(jnp.bfloat16).reshape(rows_here, kv_width)
    values = value_pre.astype(jnp.bfloat16)
    paired = lax.all_gather(jnp.concatenate([keys, values], 1), "seq", axis=0, tiled=True)
    keys_all = paired[:, :kv_width].reshape(group, KV_HEADS, HEAD_DIM)
    values_all = paired[:, kv_width:].reshape(group, KV_HEADS, HEAD_DIM)
    grouped = queries.reshape(rows_here, KV_HEADS, repeat, HEAD_DIM)
    raw = (
        jnp.einsum("qgrd,kgd->grqk", grouped, keys_all, preferred_element_type=jnp.float32)
        * score_scale
    )
    scores = jnp.where(allowed, raw, -jnp.inf)
    expo = jnp.exp(scores - jnp.max(scores, -1, keepdims=True))
    probs = expo / jnp.sum(expo, -1, keepdims=True)
    probs_low = probs.astype(jnp.bfloat16)
    attended = jnp.einsum(
        "grqk,kgd->qgrd", probs_low, values_all, preferred_element_type=jnp.float32
    )
    attended = attended.astype(jnp.bfloat16).reshape(rows_here, width)
    resid = inputs + jnp.dot(attended, weight_out, preferred_element_type=jnp.float32)
    normed_two = norm_piece(resid, gain_two).astype(jnp.bfloat16)

    normed_all = lax.all_gather(normed_two, "seq", axis=0, tiled=True)
    both = jnp.dot(normed_all, weight_gu, preferred_element_type=jnp.float32)
    gate = both[:, :own_units]
    up = both[:, own_units:]
    sigma = jax.nn.sigmoid(gate)
    activated = gate * sigma
    hidden = (activated * up).astype(jnp.bfloat16)
    d_hidden = contract_columns(upstream_all, weight_down)
    d_gate = (d_hidden * up * sigma * (1.0 + gate * (1.0 - sigma))).astype(jnp.bfloat16)
    d_up = (d_hidden * activated).astype(jnp.bfloat16)
    d_both = jnp.concatenate([d_gate, d_up], 1)
    columns = lax.psum_scatter(
        contract_columns(d_both, weight_gu).astype(jnp.bfloat16),
        "seq", scatter_dimension=0, tiled=True,
    ).astype(jnp.float32)
    branch = lax.psum_scatter(
        jnp.dot(hidden, weight_down, preferred_element_type=jnp.float32).astype(jnp.bfloat16),
        "seq", scatter_dimension=0, tiled=True,
    ).astype(jnp.float32)
    layer_out = (resid + branch).astype(jnp.bfloat16)
    grad_down = lax.psum_scatter(
        contract_rows(hidden, upstream_all).astype(jnp.bfloat16),
        "fsdp", scatter_dimension=0, tiled=True,
    ).astype(jnp.float32)
    grad_pair = lax.psum_scatter(
        contract_rows(normed_all, d_both).astype(jnp.bfloat16),
        "fsdp", scatter_dimension=0, tiled=True,
    )
    grad_pair = lax.all_to_all(grad_pair, "seq", split_axis=0, concat_axis=0, tiled=True)
    grad_pair = grad_pair.reshape(seq_count, weight_rows // seq_count, 2, fsdp_count, unit)
    grad_pair = grad_pair.transpose(2, 1, 3, 0, 4).astype(jnp.float32)
    grad_pair = grad_pair.reshape(2, weight_rows // seq_count, hidden_width)

    _, pull_two = jax.vjp(norm_piece, resid, gain_two)
    d_resid_norm, grad_gain_two = pull_two(columns)
    d_resid = cotangent.astype(jnp.float32) + d_resid_norm
    d_branch = d_resid.astype(jnp.bfloat16)
    grad_out = contract_rows(attended, d_branch).astype(jnp.bfloat16)
    d_attended = contract_columns(d_branch, weight_out).astype(jnp.bfloat16)
    d_attended = d_attended.reshape(rows_here, KV_HEADS, repeat, HEAD_DIM)
    d_probs = jnp.einsum(
        "qgrd,kgd->grqk", d_attended, values_all, preferred_element_type=jnp.float32
    )
    delta = jnp.sum(probs * d_probs, -1, keepdims=True)
    d_score = (probs * (d_probs - delta)).astype(jnp.bfloat16)
    d_queries = (
        jnp.einsum("grqk,kgd->qgrd", d_score, keys_all, preferred_element_type=jnp.float32)
        * score_scale
    )
    d_keys = (
        jnp.einsum("grqk,qgrd->kgd", d_score, grouped, preferred_element_type=jnp.float32)
        * score_scale
    )
    d_values = jnp.einsum(
        "grqk,qgrd->kgd", probs_low, d_attended, preferred_element_type=jnp.float32
    )
    d_paired = jnp.concatenate([d_keys.reshape(group, kv_width), d_values.reshape(group, kv_width)], 1)
    d_paired = lax.psum_scatter(
        d_paired.astype(jnp.bfloat16), "seq", scatter_dimension=0, tiled=True
    ).astype(jnp.float32)
    d_query_pre = rotate_back(
        d_queries.reshape(rows_here, HEADS, HEAD_DIM), cosine, sine
    ).astype(jnp.bfloat16)
    d_key_pre = rotate_back(
        d_paired[:, :kv_width].reshape(rows_here, KV_HEADS, HEAD_DIM), cosine, sine
    ).astype(jnp.bfloat16)
    d_value_pre = d_paired[:, kv_width:].astype(jnp.bfloat16)
    d_qkv = jnp.concatenate(
        [
            d_query_pre.reshape(rows_here, width),
            d_key_pre.reshape(rows_here, kv_width),
            d_value_pre,
        ],
        1,
    )
    grad_qkv = contract_rows(normed_one, d_qkv).astype(jnp.bfloat16)
    grad_bias = jnp.sum(d_qkv.astype(jnp.float32), 0)
    d_normed_one = contract_columns(d_qkv, weight_qkv)
    _, pull_one = jax.vjp(norm_piece, inputs, gain_one)
    d_input_norm, grad_gain_one = pull_one(d_normed_one)
    input_grad = (d_resid + d_input_norm).astype(jnp.bfloat16)

    def summed(value):
        value = lax.psum_scatter(value, "fsdp", scatter_dimension=0, tiled=True)
        return lax.psum_scatter(value, "seq", scatter_dimension=0, tiled=True).astype(jnp.float32)

    grad_out = summed(grad_out)
    grad_qkv = summed(grad_qkv)
    vectors = lax.psum(
        jnp.concatenate([grad_gain_one, grad_gain_two, grad_bias], 0), ("fsdp", "seq")
    )
    own = width // (fsdp_count * seq_count)
    first = (lax.axis_index("fsdp") * seq_count + seq_rank) * own

    def own_part(offset):
        return lax.dynamic_slice_in_dim(vectors, offset + first, own, 0)

    biases = 2 * width
    return (
        layer_out,
        input_grad,
        own_part(0),
        grad_qkv[:, :width],
        own_part(biases),
        grad_qkv[:, width : width + kv_width],
        vectors[biases + width : biases + width + kv_width],
        grad_qkv[:, width + kv_width :],
        vectors[biases + width + kv_width :],
        grad_out,
        own_part(width),
        grad_pair[0],
        grad_pair[1],
        grad_down,
    )


SEQ = 4


class SumChain:
    def __init__(self, held, z_one, z_two, z_three, there, index):
        self.rank = lax.axis_index("seq")
        s = self.rank
        self.held, self.arrived = held, (z_one, z_two, z_three)
        self.up = [
            there(held(1), z_one, index, seq=s + 1),
            there(held(2), z_two.at[0], index + 2, seq=s + 1),
            there(held(3), z_three.at[0], index + 4, seq=s + 1),
        ]
        self.down = [
            there(held(3), z_one, index + 1, seq=s - 1),
            there(held(2), z_two.at[1], index + 3, seq=s - 1),
            there(held(1), z_three.at[1], index + 5, seq=s - 1),
        ]

    def add(self, j, arrived):
        ref = self.held(j)
        ref[...] = ref[...] + arrived[...]

    def one(self):
        pl.when(self.rank == 0)(self.up[0].start)
        pl.when(self.rank == 3)(self.down[0].start)

    def add_one(self):
        @pl.when(self.rank == 1)
        def _():
            self.up[0].wait_recv()
            self.add(2, self.arrived[0])

        @pl.when(self.rank == 2)
        def _():
            self.down[0].wait_recv()
            self.add(2, self.arrived[0])

    def two(self):
        pl.when(self.rank <= 1)(self.up[1].start)
        pl.when(self.rank >= 2)(self.down[1].start)

    def add_two(self):
        @pl.when((self.rank == 1) | (self.rank == 2))
        def _():
            self.up[1].wait_recv()
            self.add(3, self.arrived[1].at[0])
            self.down[1].wait_recv()
            self.add(1, self.arrived[1].at[1])

    def three(self):
        pl.when(self.rank <= 2)(self.up[2].start)
        pl.when(self.rank >= 1)(self.down[2].start)

    def last(self, out):
        out[...] = self.held(0)[...].astype(jnp.float32)

        @pl.when(self.rank >= 1)
        def _():
            self.up[2].wait_recv()
            out[...] += self.arrived[2][0].astype(jnp.float32)

        @pl.when(self.rank <= 2)
        def _():
            self.down[2].wait_recv()
            out[...] += self.arrived[2][1].astype(jnp.float32)

    def one_sent(self):
        pl.when(self.rank == 0)(self.up[0].wait_send)
        pl.when(self.rank == 3)(self.down[0].wait_send)

    def two_sent(self):
        pl.when(self.rank <= 1)(self.up[1].wait_send)
        pl.when(self.rank >= 2)(self.down[1].wait_send)

    def three_sent(self):
        pl.when(self.rank <= 2)(self.up[2].wait_send)
        pl.when(self.rank >= 1)(self.down[2].wait_send)


class SumPlane:
    def __init__(self, buffer, block, plane, arrived, by_x, by_y, ended, there, index):
        half = buffer.shape[1] // 2
        low, high = pl.ds(0, half), pl.ds(half, half)

        def part(k):
            return buffer.at[pl.ds(pl.multiple_of(plane[k] * block, 16), block)]

        self.parts = own, to_x, to_y, to_both = [part(k) for k in (0, 2, 4, 6)]
        self.arrived, self.by_x, self.by_y, self.ended, self.half = arrived, by_x, by_y, ended, half
        self.core = [
            there(part(2 * i + 1), arrived.at[i], index + i, fsdp=plane[1]) for i in range(4)
        ]
        self.first = [
            there(to_both.at[:, low], by_x.at[1], index + 5, fsdp=plane[2]),
            there(to_both.at[:, high], by_y.at[1], index + 7, fsdp=plane[4]),
            there(to_x.at[:, low], by_x.at[0], index + 4, fsdp=plane[2]),
            there(to_y.at[:, high], by_y.at[0], index + 6, fsdp=plane[4]),
        ]
        self.second = [
            there(to_y.at[:, low], ended.at[0], index + 8, fsdp=plane[4]),
            there(to_x.at[:, high], ended.at[1], index + 9, fsdp=plane[2]),
        ]

    def start_core(self):
        for copy in self.core:
            copy.start()

    def start_first(self):
        for i in (3, 1, 2, 0):
            self.core[i].wait_recv()
            part = self.parts[i]
            part[...] = part[...] + self.arrived[i]
        for copy in self.first:
            copy.start()

    def start_second(self):
        half = self.half
        _, to_x, to_y, _ = self.parts
        self.first[0].wait_recv()
        to_y[:, :half] = to_y[:, :half] + self.by_x[1]
        self.second[0].start()
        self.first[1].wait_recv()
        to_x[:, half:] = to_x[:, half:] + self.by_y[1]
        self.second[1].start()

    def finish(self):
        half = self.half
        own = self.parts[0]
        self.first[2].wait_recv()
        self.second[0].wait_recv()
        total = own[:, :half].astype(jnp.float32) + self.by_x[0].astype(jnp.float32)
        own[:, :half] = (total + self.ended[0].astype(jnp.float32)).astype(jnp.bfloat16)
        self.first[3].wait_recv()
        self.second[1].wait_recv()
        total = own[:, half:].astype(jnp.float32) + self.by_y[0].astype(jnp.float32)
        own[:, half:] = (total + self.ended[1].astype(jnp.float32)).astype(jnp.bfloat16)

    def sent(self):
        for copy in self.core + self.first + self.second:
            copy.wait_send()


def block_at(place):
    far = 2 * (lax.axis_index("seq") // 2)
    return (1 + far, 2, 3 - far, 0)[place]


def in_order(partial, rows):
    far = 2 * (lax.axis_index("seq") // 2)
    places = {0: 3, 1: far, 2: 1, 3: 2 - far}

    def held(j):
        return partial.at[pl.ds(pl.multiple_of(places[j] * rows, rows), rows)]

    return held


def front_kernel(
    lengths, tokens, cotangent, small, balance, inverse,
    w_query, w_key, w_value, w_out, w_gate, w_up, w_down,
    gu_all, down_all, upstream_all, normed_all, hidden, factor_gate, factor_up, qkv_out, out_out,
    queries, paired_out, slots_out, logsum, attended, resid, normed_one, gain_one, gain_two,
    slot_row, first_row, cosine, sine,
    q_w, kv_w, out_w, gate_v, up_v, gu, normed, kv, small_own, small_all, slots_all, bias,
    cotangent_v, down_raw, down_own, hidden_v, gate_part, up_part,
    local, ssem, rsem, zsend, zrecv,
):
    f = lax.axis_index("fsdp")
    s = lax.axis_index("seq")
    rows, width = tokens.shape
    n_f, n_s = 8, slots_all.shape[0]
    group = n_s * rows
    block = w_query.shape[0]
    unit_pad = down_own.shape[0]
    unit = w_gate.shape[1] // (n_f * n_s)
    units = n_f * unit_pad
    kv_width = KV_HEADS * HEAD_DIM
    qkv_width = width + 2 * kv_width
    scale = HEAD_DIM ** (-0.5)
    repeat = HEADS // KV_HEADS
    plane = [f ^ k for k in range(n_f)]

    entry = pltpu.get_barrier_semaphore()
    for k in range(1, n_f):
        pl.semaphore_signal(entry, inc=1, device_id={"fsdp": plane[k]}, device_id_type=MESH)
    for j in range(1, n_s):
        pl.semaphore_signal(
            entry, inc=1, device_id={"seq": lax.rem(s + j, n_s)}, device_id_type=MESH
        )

    def here(source, target, index):
        return pltpu.make_async_copy(source, target, local.at[index])

    def there(source, target, index, **device):
        return pltpu.make_async_remote_copy(
            src_ref=source, dst_ref=target, send_sem=ssem.at[index], recv_sem=rsem.at[index],
            device_id=device, device_id_type=MESH,
        )

    def own_rows(ref, owner, size, start=0, count=None):
        first = pl.multiple_of(owner * size + start, 16)
        return ref.at[pl.ds(first, size if count is None else count)]

    class Gather:
        def __init__(self, source, target, size, index):
            half = size // 2
            x, y, c = plane[2], plane[4], plane[1]
            self.own = here(source, own_rows(target, f, size), index // 8) if source is not None else None
            if source is None:
                source = own_rows(target, f, size)
            mine = own_rows(target, f, size)
            self.first = [
                there(source, mine, index, fsdp=x),
                there(source, mine, index + 1, fsdp=y),
                there(source, mine, index + 2, fsdp=c),
            ]
            from_x, from_y = own_rows(target, x, size), own_rows(target, y, size)
            part_x = own_rows(target, x, size, 0, half)
            part_y = own_rows(target, y, size, half, half)
            self.second = [
                there(part_x, part_x, index + 3, fsdp=y),
                there(part_y, part_y, index + 4, fsdp=x),
                there(from_x, from_x, index + 5, fsdp=c),
                there(from_y, from_y, index + 6, fsdp=c),
            ]
            diagonal = own_rows(target, plane[6], size)
            self.third = there(diagonal, diagonal, index + 7, fsdp=c)

        def start(self):
            if self.own is not None:
                self.own.start()
            for copy in self.first:
                copy.start()

        def forward(self):
            self.first[0].wait_recv()
            self.second[0].start()
            self.second[2].start()
            self.first[1].wait_recv()
            self.second[1].start()
            self.second[3].start()

        def last(self):
            self.second[0].wait_recv()
            self.second[1].wait_recv()
            self.third.start()

        def finish(self):
            if self.own is not None:
                self.own.wait()
            self.first[2].wait_recv()
            self.second[2].wait_recv()
            self.second[3].wait_recv()
            self.third.wait_recv()

        def sent(self):
            for copy in self.first + self.second + [self.third]:
                copy.wait_send()

    class Chain:
        def __init__(self, target, index, own=None):
            self.steps = []
            for step in range(1, n_s):
                up = own_rows(target, s - (step - 1), rows)
                down = own_rows(target, s + (step - 1), rows)
                source = own if own is not None and step == 1 else up
                i = index + 2 * (step - 1)
                self.steps.append((
                    pltpu.make_async_remote_copy(
                        src_ref=source, dst_ref=up, send_sem=zsend.at[i], recv_sem=zrecv.at[i],
                        device_id={"seq": s + 1}, device_id_type=MESH,
                    ),
                    pltpu.make_async_remote_copy(
                        src_ref=down if source is up else source, dst_ref=down, send_sem=zsend.at[i + 1], recv_sem=zrecv.at[i + 1],
                        device_id={"seq": s - 1}, device_id_type=MESH,
                    ),
                    (s >= step - 1) & (s < n_s - 1),
                    (s >= 1) & (s <= n_s - step),
                    s >= step,
                    s <= n_s - 1 - step,
                ))

        def send(self, step):
            up, down, can_up, can_down, _, _ = self.steps[step - 1]
            pl.when(can_up)(up.start)
            pl.when(can_down)(down.start)

        def receive(self, step):
            up, down, _, _, from_below, from_above = self.steps[step - 1]
            pl.when(from_below)(up.wait_recv)
            pl.when(from_above)(down.wait_recv)

        def sent(self):
            for up, down, can_up, can_down, _, _ in self.steps:
                pl.when(can_up)(up.wait_send)
                pl.when(can_down)(down.wait_send)

    own_block = pl.ds(pl.multiple_of(f * block, 16), block)
    pieces = [
        here(w_key, kv_w.at[own_block, pl.ds(0, kv_width)], 6),
        here(w_value, kv_w.at[own_block, pl.ds(kv_width, kv_width)], 7),
        here(w_query, q_w.at[own_block], 5),
        here(cotangent, cotangent_v, 8),
    ]
    load_gate = here(w_gate, gate_v, 9)
    load_up = here(w_up, up_v, 10)
    first_unit = pl.multiple_of(s * unit // 16 * 16, 16)
    load_down = here(w_down.at[pl.ds(first_unit, unit_pad)], down_raw, 15)
    for copy in pieces[:2]:
        copy.start()

    slot = (balance[...] & (group - 1)).astype(jnp.float32)
    second = lengths[0, 0].astype(jnp.float32)
    third = (lengths[0, 0] + lengths[0, 1]).astype(jnp.float32)
    first = jnp.where(slot >= third, third, jnp.where(slot >= second, second, 0.0))
    slot_row[...] = jnp.broadcast_to(slot, slot_row.shape)
    first_row[...] = jnp.broadcast_to(first, first_row.shape)
    slots_all[s] = jnp.broadcast_to(slot, (128, rows)).T
    lanes = lax.broadcasted_iota(jnp.int32, small.shape, 1)
    sorts = lax.broadcasted_iota(jnp.int32, small.shape, 0)
    small_own[...] = jnp.where(
        sorts < 3,
        pltpu.roll(small[...], lax.rem(f, 2) * block, 1),
        pltpu.roll(small[...], f * (kv_width // n_f), 1),
    )
    small_all[f] = small_own[...]

    gather_kv = Gather(None, kv_w, block, 0)
    gather_q = Gather(None, q_w, block, 8)
    gather_out = Gather(w_out, out_w, block, 16)
    gather_gu = Gather(None, gu, block, 24)
    gather_down = Gather(down_own, down_all, unit_pad, 32)
    chain_up = Chain(upstream_all, 0, cotangent_v)
    chain_normed = Chain(normed, 6)
    send_small = [
        there(small_own, small_all.at[f], 40 + k, fsdp=plane[k]) for k in range(1, n_f)
    ]
    send_slots = [
        there(slots_all.at[s], slots_all.at[s], 48 + j, seq=lax.rem(s + j, n_s))
        for j in range(1, n_s)
    ]
    send_kv = [
        there(kv.at[s], kv.at[s], 52 + j, seq=lax.rem(s + j, n_s)) for j in range(1, n_s)
    ]
    for copy in pieces[:2]:
        copy.wait()
    for copy in pieces[2:]:
        copy.start()
    pl.semaphore_wait(entry, n_f - 1 + n_s - 1)
    gather_kv.start()
    for copy in send_small + send_slots:
        copy.start()
    for copy in pieces[2:]:
        copy.wait()
    chain_up.send(1)
    load_gate.start()
    load_up.start()
    load_down.start()
    save_own = here(cotangent_v, own_rows(upstream_all, s, rows), 8)
    save_own.start()
    position = slots_all[s] - jnp.broadcast_to(first, (128, rows)).T
    angle = position * inverse[...]
    cosine[...] = jnp.cos(angle)
    sine[...] = jnp.where(
        lax.broadcasted_iota(jnp.int32, angle.shape, 1) < HEAD_DIM // 2, -1.0, 1.0
    ) * jnp.sin(angle)

    for copy in send_small + send_slots:
        copy.wait_recv()

    def joined(sort):
        return jnp.concatenate(
            [
                small_all[2 * i, sort : sort + 1] + small_all[2 * i + 1, sort : sort + 1]
                for i in range(n_f // 2)
            ],
            1,
        )

    gain_one[...] = joined(0)
    gain_two[...] = joined(1)
    bias_query = joined(2)
    bias_key = sum(small_all[i, 3:4, :kv_width] for i in range(n_f))
    bias_value = sum(small_all[i, 4:5, :kv_width] for i in range(n_f))

    inputs = tokens[...].astype(jnp.float32)
    root = lax.rsqrt(jnp.mean(inputs * inputs, -1, keepdims=True) + epsilon)
    normed_one[...] = (inputs * root * gain_one[...]).astype(jnp.bfloat16)
    gather_kv.forward()
    gather_q.start()
    gather_kv.last()
    gather_kv.finish()

    def turned(value):
        return value * cosine[...] + pltpu.roll(value, HEAD_DIM // 2, 1) * sine[...]

    rows_low = normed_one[...]
    pair = jnp.dot(rows_low, kv_w[:, :kv_width], preferred_element_type=jnp.float32)
    pair = pair + bias_key
    for g in range(KV_HEADS):
        columns = slice(g * HEAD_DIM, (g + 1) * HEAD_DIM)
        kv[s, :, columns] = turned(pair[:, columns]).astype(jnp.bfloat16)
    pair = jnp.dot(rows_low, kv_w[:, kv_width:], preferred_element_type=jnp.float32)
    kv[s, :, kv_width:] = (pair + bias_value).astype(jnp.bfloat16)
    for copy in send_kv:
        copy.start()
    save_kv_w = here(kv_w, qkv_out.at[:, pl.ds(width, 2 * kv_width)], 11)
    save_kv_w.start()

    load_gate.wait()
    load_up.wait()
    pick_units(gate_v, up_v, gu.at[own_block], w_gate.shape[1] // n_f, unit, unit_pad)
    gather_q.forward()
    gather_out.start()
    load_down.wait()
    raw = down_raw[...].astype(jnp.float32)
    shifted = jnp.concatenate([raw[8:], jnp.zeros((8, width), jnp.float32)], 0)
    raw = jnp.where(lax.rem(s * unit, 16) == 0, raw, shifted)
    inside = lax.broadcasted_iota(jnp.int32, raw.shape, 0) < unit
    down_own[...] = jnp.where(inside, raw, 0.0).astype(jnp.bfloat16)

    for j in range(n_s):
        keys_slot = slots_all[j]
        keys_slot = jnp.concatenate([keys_slot] * (rows // 128), 1)
        ok = (keys_slot <= slot) & (keys_slot >= first)
        bias[j * rows : (j + 1) * rows] = jnp.where(ok, 0.0, -1e30)

    gather_q.last()
    gather_q.finish()
    save_q_w = here(q_w, qkv_out.at[:, pl.ds(0, width)], 0)
    save_q_w.start()
    for g in range(HEADS // 2):
        columns = slice(g * 2 * HEAD_DIM, (g + 1) * 2 * HEAD_DIM)
        pair = jnp.dot(rows_low, q_w[:, columns], preferred_element_type=jnp.float32)
        pair = pair + bias_query[:, columns]
        for h in range(2):
            part = turned(pair[:, h * HEAD_DIM : (h + 1) * HEAD_DIM]).astype(jnp.bfloat16)
            queries[:, (2 * g + h) * HEAD_DIM : (2 * g + h + 1) * HEAD_DIM] = part

    gather_out.forward()
    gather_gu.start()
    chain_up.receive(1)
    for copy in send_kv:
        copy.wait_recv()
    chain_up.send(2)
    save_kv = here(kv, paired_out, 12)
    save_kv.start()
    slots_out[...] = slots_all[...]

    for g in range(KV_HEADS):
        keys = kv[:, :, g * HEAD_DIM : (g + 1) * HEAD_DIM].reshape(n_s * rows, HEAD_DIM)
        values = kv[:, :, kv_width + g * HEAD_DIM : kv_width + (g + 1) * HEAD_DIM]
        values = values.reshape(n_s * rows, HEAD_DIM)

        def head(i, carry, g=g, keys=keys, values=values):
            h = g * repeat + i
            columns = pl.ds(pl.multiple_of(h * HEAD_DIM, HEAD_DIM), HEAD_DIM)
            raw = lax.dot_general(
                keys, queries[:, columns], (((1,), (1,)), ((), ())),
                preferred_element_type=jnp.float32,
            )
            scores = raw * scale + bias[...]
            top = jnp.max(scores, 0, keepdims=True)
            expo = jnp.exp(scores - top)
            total = jnp.sum(expo, 0, keepdims=True)
            probs = (expo * (1.0 / total)).astype(jnp.bfloat16)
            mixed = lax.dot_general(
                values, probs, (((0,), (0,)), ((), ())), preferred_element_type=jnp.float32
            )
            attended[:, columns] = mixed.T.astype(jnp.bfloat16)
            logsum[pl.ds(pl.multiple_of(h * 8, 8), 8)] = jnp.broadcast_to(
                top + jnp.log(total), (8, rows)
            )
            return carry

        lax.fori_loop(0, repeat, head, 0)
        if g == 0:
            gather_out.last()

    gather_out.finish()
    save_out = here(out_w, out_out, 13)
    save_out.start()
    mixed = attended[...]
    for g in range(width // 256):
        columns = slice(g * 256, (g + 1) * 256)
        part = jnp.dot(mixed, out_w[:, columns], preferred_element_type=jnp.float32)
        resid[:, columns] = tokens[:, columns].astype(jnp.float32) + part
    value = resid[...]
    root = lax.rsqrt(jnp.mean(value * value, -1, keepdims=True) + epsilon)
    own_tokens = pl.ds(pl.multiple_of(s * rows, rows), rows)
    normed[own_tokens] = (value * root * gain_two[...]).astype(jnp.bfloat16)
    chain_normed.send(1)

    wide = hidden_v.shape[2]
    count = units // wide

    def saves(owner, t, slot):
        place = (
            pl.ds(pl.multiple_of(owner * rows, rows), rows),
            pl.ds(pl.multiple_of(t * wide, wide), wide),
        )
        return [
            here(part.at[slot], whole.at[place], 16 + 3 * slot + i)
            for i, (part, whole) in enumerate(
                ((hidden_v, hidden), (gate_part, factor_gate), (up_part, factor_up))
            )
        ]

    def feed(owner, done):
        def body(t, carry):
            slot = lax.rem(t + done, 2)
            mine = normed[pl.ds(pl.multiple_of(owner * rows, rows), rows)]
            gate_columns = pl.ds(pl.multiple_of(t * wide, wide), wide)
            up_columns = pl.ds(pl.multiple_of(units + t * wide, wide), wide)
            gate = jnp.dot(mine, gu[:, gate_columns], preferred_element_type=jnp.float32)
            up = jnp.dot(mine, gu[:, up_columns], preferred_element_type=jnp.float32)
            sigma = jax.nn.sigmoid(gate)
            activated = gate * sigma

            @pl.when(t + done >= 2)
            def _():
                for copy in saves(owner, t, slot):
                    copy.wait()

            hidden_v[slot] = (activated * up).astype(jnp.bfloat16)
            gate_part[slot] = (up * sigma * (1.0 + gate * (1.0 - sigma))).astype(jnp.bfloat16)
            up_part[slot] = activated.astype(jnp.bfloat16)
            for copy in saves(owner, t, slot):
                copy.start()
            return carry

        lax.fori_loop(0, count, body, 0)

    chain_up.receive(2)
    chain_normed.receive(1)
    chain_normed.send(2)
    gather_gu.forward()
    chain_normed.receive(2)
    chain_normed.send(3)
    gather_gu.last()
    gather_down.start()
    gather_gu.finish()
    save_gu = here(gu, gu_all, 22)
    save_gu.start()
    feed(s, 0)
    feed(s ^ 1, count)
    chain_normed.receive(3)
    chain_up.send(3)
    save_normed = here(normed, normed_all, 23)
    save_normed.start()
    gather_down.forward()
    feed(s ^ 2, 2 * count)
    feed(s ^ 3, 3 * count)
    gather_down.last()
    for t in (count - 2, count - 1):
        for copy in saves(s ^ 3, t, (t + 3 * count) % 2):
            copy.wait()
    chain_up.receive(3)
    gather_down.finish()
    for copy in (save_own, save_kv_w, save_q_w, save_kv, save_out, save_gu, save_normed):
        copy.wait()
    for part in (gather_kv, gather_q, gather_out, gather_gu, gather_down, chain_up, chain_normed):
        part.sent()
    for copy in send_small + send_slots + send_kv:
        copy.wait_send()


def pick_units(gate, up, out, stride, unit, padded):
    rank = lax.axis_index("seq")
    pieces = gate.shape[1] // stride
    half = out.shape[1] // 2
    window, tile = 512, 128
    rows = lax.broadcasted_iota(jnp.int32, (window, tile), 0)
    columns = lax.broadcasted_iota(jnp.int32, (window, tile), 1)
    for first in range(0, 2 * half, tile):
        source = gate if first < half else up
        local = first % half
        total = jnp.zeros((out.shape[0], tile), jnp.float32)
        for f in range(pieces):
            low = max(local, f * padded)
            high = min(local + tile, f * padded + unit)
            if low >= high:
                continue
            begin = f * stride + rank * unit
            base = jnp.minimum(begin // 128, (source.shape[1] - window) // 128) * 128
            base = pl.multiple_of(base, 128)
            wanted = columns + (local - f * padded + begin - base)
            inside = (columns >= low - local) & (columns < high - local)
            chosen = jnp.where((rows == wanted) & inside, 1.0, 0.0).astype(jnp.bfloat16)
            total += jnp.dot(
                source[:, pl.ds(base, window)], chosen, preferred_element_type=jnp.float32
            )
        out[:, first : first + tile] = total.astype(jnp.bfloat16)


def front(tokens, cotangent, lengths, balance, vectors, weights):
    rows, width = tokens.shape
    n_s = lax.axis_size("seq")
    w_query, w_key, w_value, w_out, w_gate, w_up, w_down = weights
    block = w_query.shape[0]
    unit_pad = -(-w_down.shape[0] // n_s // 16) * 16
    kv_width = KV_HEADS * HEAD_DIM
    qkv_width = width + 2 * kv_width
    units = 8 * unit_pad
    group = n_s * rows
    wide = 768
    low, full = jnp.bfloat16, jnp.float32
    small = sum(
        jnp.pad(v.astype(full)[None], ((i, 7 - i), (0, 2 * block - v.shape[0])))
        for i, v in enumerate(vectors)
    )
    half = HEAD_DIM // 2
    inverse = rope_base ** (-(np.arange(half, dtype=np.float32) * np.float32(2.0 / HEAD_DIM)))
    inverse = jnp.asarray(np.concatenate([inverse, inverse])[None], full)
    smem = pl.BlockSpec(memory_space=pltpu.SMEM)
    vmem = pl.BlockSpec(memory_space=pltpu.VMEM)
    hbm = pl.BlockSpec(memory_space=pl.ANY)
    shape = jax.ShapeDtypeStruct
    return pl.pallas_call(
        front_kernel,
        in_specs=[smem, vmem, hbm, vmem, vmem, vmem] + [hbm] * 7,
        out_specs=[hbm] * 9 + [vmem, hbm] + [vmem] * 11,
        out_shape=[
            shape((width, 2 * units), low),
            shape((units, width), low),
            shape((group, width), low),
            shape((group, width), low),
            shape((group, units), low),
            shape((group, units), low),
            shape((group, units), low),
            shape((width, qkv_width), low),
            shape((width, width), low),
            shape((rows, width), low),
            shape((n_s, rows, 2 * kv_width), low),
            shape((n_s, rows, 128), full),
            shape((8 * HEADS, rows), full),
            shape((rows, width), low),
            shape((rows, width), full),
            shape((rows, width), low),
            shape((1, width), full),
            shape((1, width), full),
            shape((8, rows), full),
            shape((8, rows), full),
            shape((rows, HEAD_DIM), full),
            shape((rows, HEAD_DIM), full),
        ],
        scratch_shapes=[
            pltpu.VMEM((width, width), low),
            pltpu.VMEM((width, 2 * kv_width), low),
            pltpu.VMEM((width, width), low),
            pltpu.VMEM(w_gate.shape, low),
            pltpu.VMEM(w_up.shape, low),
            pltpu.VMEM((width, 2 * units), low),
            pltpu.VMEM((group, width), low),
            pltpu.VMEM((n_s, rows, 2 * kv_width), low),
            pltpu.VMEM((8, 2 * block), full),
            pltpu.VMEM((8, 8, 2 * block), full),
            pltpu.VMEM((n_s, rows, 128), full),
            pltpu.VMEM((group, rows), full),
            pltpu.VMEM((rows, width), low),
            pltpu.VMEM((unit_pad, width), low),
            pltpu.VMEM((unit_pad, width), low),
            pltpu.VMEM((2, rows, wide), low),
            pltpu.VMEM((2, rows, wide), low),
            pltpu.VMEM((2, rows, wide), low),
            pltpu.SemaphoreType.DMA((24,)),
            pltpu.SemaphoreType.DMA((56,)),
            pltpu.SemaphoreType.DMA((56,)),
            pltpu.SemaphoreType.DMA((12,)),
            pltpu.SemaphoreType.DMA((12,)),
        ],
        compiler_params=pltpu.CompilerParams(
            collective_id=0, has_side_effects=True, vmem_limit_bytes=62 * 2**20
        ),
        name="front",
    )(
        lengths, tokens, cotangent, small, balance.reshape(1, rows), inverse,
        w_query, w_key, w_value, w_out, w_gate, w_up, w_down,
    )


def ffn_kernel(
    normed_all, upstream_all, w_gu, w_down, hidden_all, factor_gate, factor_up,
    columns, grad_down, gu_sum, branch, down_arrived, gu_arrived,
    normed, upstream, gu, down, hidden, d_both, partial, z_one, z_two, z_three,
    down_x, down_y, down_last, down_piece,
    load, ssem, rsem,
):
    f = lax.axis_index("fsdp")
    s = lax.axis_index("seq")
    n_s = SEQ
    group, width = normed.shape
    rows = group // n_s
    half_rows = group // 2
    units = down.shape[0]
    tile = 256
    tiles = units // tile
    wide = 768
    block = gu.shape[0] // 8
    unit = units // 8
    half = width // 2
    plane = [f ^ k for k in range(8)]
    full = jnp.float32

    entry = pltpu.get_barrier_semaphore()
    for k in (1, 2, 4):
        pl.semaphore_signal(entry, inc=1, device_id={"fsdp": plane[k]}, device_id_type=MESH)
    for j in (1, n_s - 1):
        pl.semaphore_signal(
            entry, inc=1, device_id={"seq": lax.rem(s + j, n_s)}, device_id_type=MESH
        )

    def here(source, target, index):
        return pltpu.make_async_copy(source, target, load.at[index])

    def there(source, target, index, **device):
        return pltpu.make_async_remote_copy(
            src_ref=source, dst_ref=target, send_sem=ssem.at[index], recv_sem=rsem.at[index],
            device_id=device, device_id_type=MESH,
        )

    def part(ref, owner, size):
        return ref.at[pl.ds(pl.multiple_of(owner * size, 16), size)]

    early, late = (0,), (1, 2, 3)

    def rows_of(p):
        return pl.ds(p * rows, rows)

    def row_loads(p):
        owner = lax.rem(s + n_s - block_at(p), n_s)
        mine = rows_of(p)
        return [
            here(part(upstream_all, owner, rows), upstream.at[mine], 5 * p),
            here(part(factor_gate, owner, rows), d_both.at[mine, pl.ds(0, units)], 5 * p + 1),
            here(part(factor_up, owner, rows), d_both.at[mine, pl.ds(units, units)], 5 * p + 2),
            here(part(hidden_all, owner, rows), hidden.at[mine], 5 * p + 3),
            here(part(normed_all, owner, rows), normed.at[mine], 5 * p + 4),
        ]

    def down_load(t):
        mine = pl.ds(pl.multiple_of(t * wide, wide), wide)
        return here(w_down.at[mine], down.at[mine], 20 + t)

    def gu_load(n):
        mine = pl.ds(pl.multiple_of(n * 512, 512), 512)
        return here(w_gu.at[mine], gu.at[mine], 23 + n)

    loads = [row_loads(p) for p in range(n_s)]
    order = [loads[0][0], down_load(0)]
    order += [loads[p][i] for i in (1, 2) for p in early]
    order += [down_load(t) for t in range(1, units // wide)]
    second = [gu_load(n) for n in range(width // 512)]
    second += [loads[p][i] for i in (0, 1, 2) for p in late]
    third = [loads[p][i] for i in (3, 4) for p in range(n_s)]
    for copy in order:
        copy.start()

    def forward(blocks, wait, following):
        for p in blocks:
            for copy in loads[p][:3]:
                copy.wait()
        for copy in following:
            copy.start()
        mine = pl.ds(blocks[0] * rows, len(blocks) * rows)

        def body(t, carry):
            if wait:
                down_load(t).wait()
            gate_columns = pl.ds(pl.multiple_of(t * wide, wide), wide)
            up_columns = pl.ds(pl.multiple_of(units + t * wide, wide), wide)
            d_hidden = lax.dot_general(
                upstream[mine], down[gate_columns], (((1,), (1,)), ((), ())),
                preferred_element_type=full,
            )
            value = d_hidden * d_both[mine, gate_columns].astype(full)
            d_both[mine, gate_columns] = value.astype(jnp.bfloat16)
            value = d_hidden * d_both[mine, up_columns].astype(full)
            d_both[mine, up_columns] = value.astype(jnp.bfloat16)
            return carry

        lax.fori_loop(0, units // wide, body, 0)

    def backward(blocks, wait):
        part_rows = pl.ds(blocks[0] * rows, len(blocks) * rows)

        def body(n, carry):
            if wait:
                gu_load(n).wait()
            out_columns = pl.ds(pl.multiple_of(n * 512, 512), 512)
            value = lax.dot_general(
                d_both[part_rows], gu[out_columns], (((1,), (1,)), ((), ())),
                preferred_element_type=full,
            )
            partial[part_rows, out_columns] = value.astype(jnp.bfloat16)
            return carry

        lax.fori_loop(0, width // 512, body, 0)

    chain = SumChain(in_order(partial, rows), z_one, z_two, z_three, there, 0)
    pieces = [(first, min(group, units - first)) for first in range(0, units, group)]
    forward((0,), True, second)
    backward((0,), True)
    pl.semaphore_wait(entry, 5)
    chain.one()
    forward((1,), False, third)
    backward((1,), False)
    forward((2, 3), False, ())
    backward((2, 3), False)
    chain.add_one()
    chain.two()

    for p in range(n_s):
        loads[p][3].wait()
        loads[p][4].wait()

    def down_body(t, carry):
        unit_rows = pl.ds(pl.multiple_of(t * tile, tile), tile)
        value = lax.dot_general(
            hidden[:, unit_rows], upstream[...], (((0,), (0,)), ((), ())),
            preferred_element_type=full,
        )
        down[unit_rows] = value.astype(jnp.bfloat16)
        return carry

    lax.fori_loop(0, tiles, down_body, 0)
    down_core = [
        there(part(down, plane[2 * i + 1], unit), down_arrived.at[i], 6 + i, fsdp=plane[1])
        for i in range(4)
    ]
    for i in (3, 1, 2, 0):
        down_core[i].start()

    again_in = [upstream] + [
        d_both.at[:count, i * width : (i + 1) * width] for i, (_, count) in enumerate(pieces[1:])
    ]
    again = [
        here(w_down.at[first : first + count], place, 36 + i)
        for i, ((first, count), place) in enumerate(zip(pieces, again_in))
    ]
    again[0].start()

    def gu_body(m, carry):
        in_columns = pl.ds(pl.multiple_of(m * tile, tile), tile)
        turned = normed[:, in_columns].T
        for first in range(0, 2 * units, units // 3):
            value = jnp.dot(turned, d_both[:, first : first + units // 3], preferred_element_type=full)
            gu[in_columns, first : first + units // 3] = value.astype(jnp.bfloat16)
        return carry

    lax.fori_loop(0, 2, gu_body, 0)
    chain.add_two()
    chain.three()

    class Arrivals:
        def __init__(self, ref, size, arrived, copies, turns, index):
            self.ref, self.size, self.copies = ref, size, copies
            self.pieces = {}
            for n, i in enumerate((3, 1, 2, 0)):
                self.pieces[i] = [
                    (here(arrived.at[i, :, columns], piece, index + 3 * (n % 2) + k), columns, piece)
                    for k, (columns, piece) in enumerate(turns[n % 2])
                ]

        def fetch(self, i):
            self.copies[i].wait_recv()
            for copy, _, _ in self.pieces[i]:
                copy.start()

        def add(self, i):
            target = part(self.ref, plane[2 * i], self.size)
            for copy, columns, piece in self.pieces[i]:
                copy.wait()
                target[:, columns] = target[:, columns] + piece[...]

    down_turns = [[(pl.ds(0, width), piece)] for piece in (down_piece.at[0], down_piece.at[1])]
    down_sum = Arrivals(down, unit, down_arrived, down_core, down_turns, 26)
    down_sum.fetch(3)
    for i, following in ((3, 1), (1, 2), (2, 0), (0, None)):
        if following is not None:
            down_sum.fetch(following)
        down_sum.add(i)
    to_x, to_y, to_both = [part(down, plane[k], unit) for k in (2, 4, 6)]
    low_half, high_half = pl.ds(0, half), pl.ds(half, half)
    down_first = [
        there(to_x.at[:, low_half], down_x.at[0], 10, fsdp=plane[2]),
        there(to_both.at[:, low_half], down_x.at[1], 11, fsdp=plane[2]),
        there(to_y.at[:, high_half], down_y.at[0], 12, fsdp=plane[4]),
        there(to_both.at[:, high_half], down_y.at[1], 13, fsdp=plane[4]),
    ]
    for copy in down_first:
        copy.start()
    lax.fori_loop(2, width // tile, gu_body, 0)
    gu_core = [
        there(part(gu, plane[2 * i + 1], block), gu_arrived.at[i], 16 + i, fsdp=plane[1])
        for i in range(4)
    ]
    for i in (3, 1, 2, 0):
        gu_core[i].start()

    for copy in again[1:]:
        copy.start()
    for copy in again:
        copy.wait()

    def branch_body(n, carry):
        out_columns = pl.ds(pl.multiple_of(n * wide, wide), wide)
        for m in range(2):
            mine = slice(m * half_rows, (m + 1) * half_rows)
            value = jnp.zeros((half_rows, wide), full)
            for i, (first, count) in enumerate(pieces):
                value += jnp.dot(
                    hidden[mine, first : first + count], again_in[i][:, out_columns],
                    preferred_element_type=full,
                )
            normed[mine, out_columns] = value.astype(jnp.bfloat16)
        return carry

    lax.fori_loop(0, width // wide, branch_body, 0)
    chain.last(columns)
    chain_branch = SumChain(in_order(normed, rows), z_one, z_two, z_three, there, 22)
    chain_branch.one()
    down_second = [
        there(to_y.at[:, low_half], down_last.at[0], 14, fsdp=plane[4]),
        there(to_x.at[:, high_half], down_last.at[1], 15, fsdp=plane[2]),
    ]
    down_first[1].wait_recv()
    to_y[:, :half] = to_y[:, :half] + down_x[1]
    down_second[0].start()
    down_first[3].wait_recv()
    to_x[:, half:] = to_x[:, half:] + down_y[1]
    down_second[1].start()
    gu_turns = [
        [(pl.ds(k * units, units), hidden.at[(2 * n + k) * block : (2 * n + k + 1) * block]) for k in range(2)]
        for n in range(2)
    ]
    gu_arrivals = Arrivals(gu, block, gu_arrived, gu_core, gu_turns, 26)
    store = [here(part(gu, plane[2 * i], block), gu_sum.at[i], 32 + i) for i in range(4)]
    gu_arrivals.fetch(3)
    for i, following in ((3, 1), (1, 2), (2, 0), (0, None)):
        if following is not None:
            gu_arrivals.fetch(following)
        gu_arrivals.add(i)
        store[i].start()
    down_first[0].wait_recv()
    down_first[2].wait_recv()
    own = part(down, f, unit)
    down_second[0].wait_recv()
    grad_down[:, :half] = (
        own[:, :half].astype(full) + down_x[0].astype(full) + down_last[0].astype(full)
    )
    down_second[1].wait_recv()
    grad_down[:, half:] = (
        own[:, half:].astype(full) + down_y[0].astype(full) + down_last[1].astype(full)
    )
    chain_branch.add_one()
    chain_branch.one_sent()
    store_branch = here(normed, branch, 39)
    store_branch.start()
    chain.one_sent()
    chain.two_sent()
    chain.three_sent()
    for copy in down_core + down_first + down_second + gu_core:
        copy.wait_send()
    for copy in store + [store_branch]:
        copy.wait()


def ffn(normed_all, upstream_all, w_gu, w_down, hidden, factor_gate, factor_up):
    group, width = normed_all.shape
    units = w_down.shape[0]
    rows = group // SEQ
    unit, block, half = units // 8, width // 8, width // 2
    low, full = jnp.bfloat16, jnp.float32
    vmem = pl.BlockSpec(memory_space=pltpu.VMEM)
    hbm = pl.BlockSpec(memory_space=pl.ANY)
    shape = jax.ShapeDtypeStruct
    return pl.pallas_call(
        ffn_kernel,
        in_specs=[hbm] * 7,
        out_specs=[vmem] * 2 + [hbm] * 4,
        out_shape=[
            shape((rows, width), full),
            shape((unit, width), full),
            shape((4, block, 2 * units), low),
            shape((group, width), low),
            shape((4, unit, width), low),
            shape((4, block, 2 * units), low),
        ],
        scratch_shapes=[
            pltpu.VMEM((group, width), low),
            pltpu.VMEM((group, width), low),
            pltpu.VMEM((width, 2 * units), low),
            pltpu.VMEM((units, width), low),
            pltpu.VMEM((group, units), low),
            pltpu.VMEM((group, 2 * units), low),
            pltpu.VMEM((group, width), low),
            pltpu.VMEM((rows, width), low),
            pltpu.VMEM((2, rows, width), low),
            pltpu.VMEM((2, rows, width), low),
            pltpu.VMEM((2, unit, half), low),
            pltpu.VMEM((2, unit, half), low),
            pltpu.VMEM((2, unit, half), low),
            pltpu.VMEM((2, unit, width), low),
            pltpu.SemaphoreType.DMA((40,)),
            pltpu.SemaphoreType.DMA((28,)),
            pltpu.SemaphoreType.DMA((28,)),
        ],
        compiler_params=pltpu.CompilerParams(
            collective_id=1, has_side_effects=True, vmem_limit_bytes=63 * 2**20
        ),
        name="ffn",
    )(normed_all, upstream_all, w_gu, w_down, hidden, factor_gate, factor_up)[:4]


def back_kernel(
    gain_two, slot_row, first_row, logsum, gain_one, cosine, sine, slots,
    resid_in, cotangent_in, attended_in, queries_in, paired_in, normed_in, tokens_in,
    columns, w_out, w_qkv, gu_sum, branch,
    layer, input_rows, vector, grad_out, grad_qkv, gu_rows,
    resid, cotangent, attended, queries, paired, normed_one, tokens,
    out_w, qkv, gu_own, gu_to_y, gu_to_x, gu_x, gu_y, gu_ended,
    branch_v, z_one, z_two, z_three, working, bias, d_branch, d_attended, d_qkv, d_resid,
    keys_grad, values_grad, dkv, dkv_in,
    out_arrived, out_x, out_y, out_ended, qkv_arrived, qkv_x, qkv_y, qkv_ended,
    out_one, out_two, out_three, qkv_one, qkv_two, qkv_three, vector_in,
    load, ssem, rsem,
):
    f = lax.axis_index("fsdp")
    s = lax.axis_index("seq")
    rows, width = tokens.shape
    n_s = paired.shape[0]
    kv_width = KV_HEADS * HEAD_DIM
    repeat = HEADS // KV_HEADS
    scale = HEAD_DIM ** (-0.5)
    block = width // 8
    piece = block // n_s
    units = gu_sum.shape[2] // 2
    tile = 256
    full, low = jnp.float32, jnp.bfloat16
    plane = [f ^ k for k in range(8)]

    entry = pltpu.get_barrier_semaphore()
    for k in (1, 2, 4):
        pl.semaphore_signal(entry, inc=1, device_id={"fsdp": plane[k]}, device_id_type=MESH)
    for j in range(1, n_s):
        pl.semaphore_signal(
            entry, inc=1, device_id={"seq": lax.rem(s + j, n_s)}, device_id_type=MESH
        )

    def here(source, target, index):
        return pltpu.make_async_copy(source, target, load.at[index])

    def there(source, target, index, **device):
        return pltpu.make_async_remote_copy(
            src_ref=source, dst_ref=target, send_sem=ssem.at[index], recv_sem=rsem.at[index],
            device_id=device, device_id_type=MESH,
        )

    low_units, high_units = pl.ds(0, units), pl.ds(units, units)
    load_branch = here(branch, branch_v, 0)
    load_out = here(w_out, out_w, 1)
    load_gu = [
        here(gu_sum.at[0], gu_own, 2),
        here(gu_sum.at[2, :, low_units], gu_to_y, 3),
        here(gu_sum.at[1, :, high_units], gu_to_x, 4),
    ]
    load_qkv = here(w_qkv, qkv, 5)
    load_columns = here(columns, working, 7)
    load_rows = [
        here(source, place, 10 + i)
        for i, (source, place) in enumerate((
            (resid_in, resid), (cotangent_in, cotangent), (attended_in, attended),
            (queries_in, queries), (paired_in, paired), (normed_in, normed_one),
            (tokens_in, tokens),
        ))
    ]
    for copy in [load_columns] + load_rows[:2] + [load_branch]:
        copy.start()

    gu_first = [
        there(gu_sum.at[3, :, low_units], gu_x.at[1], 0, fsdp=plane[2]),
        there(gu_sum.at[3, :, high_units], gu_y.at[1], 1, fsdp=plane[4]),
        there(gu_sum.at[1, :, low_units], gu_x.at[0], 2, fsdp=plane[2]),
        there(gu_sum.at[2, :, high_units], gu_y.at[0], 3, fsdp=plane[4]),
    ]
    gu_second = [
        there(gu_to_y, gu_ended.at[0], 4, fsdp=plane[4]),
        there(gu_to_x, gu_ended.at[1], 5, fsdp=plane[2]),
    ]

    def around(j):
        return {"seq": lax.rem(s + j, n_s)}

    def rows_for(ref, first, j):
        owner = lax.rem(s + j, n_s)
        return ref.at[pl.ds(pl.multiple_of(first + owner * piece, 16), piece)]

    gu_send = [there(rows_for(gu_own, 0, j), gu_rows.at[j], 5 + j, **around(j)) for j in range(1, n_s)]
    dkv_send = [
        [
            there(dkv.at[g, lax.rem(s + j, n_s)], dkv_in.at[g, j], 8 + 3 * g + j, **around(j))
            for j in range(1, n_s)
        ]
        for g in range(KV_HEADS)
    ]
    chain = SumChain(in_order(branch_v, rows), z_one, z_two, z_three, there, 16)
    sum_out = SumPlane(out_w, block, plane, out_arrived, out_x, out_y, out_ended, there, 24)
    sum_qkv = SumPlane(qkv, block, plane, qkv_arrived, qkv_x, qkv_y, qkv_ended, there, 36)

    def own_part(ref):
        return lambda j: rows_for(ref, f * block, n_s - j)

    chain_out = SumChain(own_part(out_w), out_one, out_two, out_three, there, 48)
    chain_qkv = SumChain(own_part(qkv), qkv_one, qkv_two, qkv_three, there, 54)
    vector_send = [
        there(vector_in.at[0], vector_in.at[1], 60, fsdp=plane[1]),
        there(vector_in.at[2], vector_in.at[3], 61, fsdp=plane[2]),
        there(vector_in.at[4], vector_in.at[5], 62, fsdp=plane[4]),
    ] + [there(vector_in.at[6], vector_in.at[6 + j], 62 + j, **around(j)) for j in range(1, n_s)]

    pl.semaphore_wait(entry, 3 + n_s - 1)
    for copy in gu_first:
        copy.start()
    load_branch.wait()
    chain.two()

    def norm_back(value, gain, grad):
        root = lax.rsqrt(jnp.mean(value * value, -1, keepdims=True) + epsilon)
        scaled = gain * grad
        inner = jnp.mean(scaled * value, -1, keepdims=True)
        gain_grad = jnp.sum(grad * (value * root), 0, keepdims=True)
        return root * scaled - value * (root * root * root * inner), gain_grad

    load_columns.wait()
    for copy in load_rows[:2]:
        copy.wait()
    for copy in [load_out] + load_rows[2:] + load_gu + [load_qkv]:
        copy.start()
    d_norm, gain_two_grad = norm_back(resid[...], gain_two[...], working[...])
    d_total = cotangent[...].astype(full) + d_norm
    d_branch[...] = d_total.astype(low)
    d_resid[...] = d_total
    for j in range(n_s):
        keys_slot = slots[j]
        keys_slot = jnp.concatenate([keys_slot] * (rows // 128), 1)
        ok = (keys_slot <= slot_row[0:1]) & (keys_slot >= first_row[0:1])
        bias[j * rows : (j + 1) * rows] = jnp.where(ok, 0.0, -1e30)
    load_out.wait()
    for copy in load_rows[2:]:
        copy.wait()
    for n in range(width // tile):
        value = lax.dot_general(
            d_branch[...], out_w[n * tile : (n + 1) * tile], (((1,), (1,)), ((), ())),
            preferred_element_type=full,
        )
        d_attended[:, n * tile : (n + 1) * tile] = value.astype(low)

    def turned_back(value):
        return value * cosine[...] + pltpu.roll(value * sine[...], HEAD_DIM // 2, 1)

    for g in range(KV_HEADS):
        keys = paired[:, :, g * HEAD_DIM : (g + 1) * HEAD_DIM].reshape(n_s * rows, HEAD_DIM)
        values = paired[:, :, kv_width + g * HEAD_DIM : kv_width + (g + 1) * HEAD_DIM]
        values = values.reshape(n_s * rows, HEAD_DIM)
        keys_grad[...] = jnp.zeros_like(keys_grad)
        values_grad[...] = jnp.zeros_like(values_grad)

        def head(i, carry, g=g, keys=keys, values=values):
            h = g * repeat + i
            head_columns = pl.ds(pl.multiple_of(h * HEAD_DIM, HEAD_DIM), HEAD_DIM)
            query = queries[:, head_columns]
            grad = d_attended[:, head_columns]
            raw = lax.dot_general(
                keys, query, (((1,), (1,)), ((), ())), preferred_element_type=full
            )
            logs = logsum[pl.ds(pl.multiple_of(h * 8, 8), 8)][0:1]
            probs = jnp.exp(raw * scale + bias[...] - logs)
            d_probs = lax.dot_general(
                values, grad, (((1,), (1,)), ((), ())), preferred_element_type=full
            )
            delta = jnp.sum(probs * d_probs, 0, keepdims=True)
            d_score = (probs * (d_probs - delta)).astype(low)
            turned = lax.dot_general(
                keys, d_score, (((0,), (0,)), ((), ())), preferred_element_type=full
            )
            d_qkv[:, head_columns] = turned_back((turned * scale).T).astype(low)
            keys_grad[...] += jnp.dot(d_score, query, preferred_element_type=full) * scale
            values_grad[...] += jnp.dot(probs.astype(low), grad, preferred_element_type=full)
            return carry

        lax.fori_loop(0, repeat, head, 0)
        dkv[g, :, :, :HEAD_DIM] = keys_grad[...].astype(low).reshape(n_s, rows, HEAD_DIM)
        dkv[g, :, :, HEAD_DIM:] = values_grad[...].astype(low).reshape(n_s, rows, HEAD_DIM)
        for copy in dkv_send[g]:
            copy.start()

    turned = attended[...].T
    for n in range(width // tile):
        n_columns = slice(n * tile, (n + 1) * tile)
        value = jnp.dot(turned, d_branch[:, n_columns], preferred_element_type=full)
        out_w[:, n_columns] = value.astype(low)
    sum_out.start_core()
    load_qkv.wait()

    def back_one(first, count, start):
        for n in range(width // tile):
            n_rows = slice(n * tile, (n + 1) * tile)
            value = lax.dot_general(
                d_qkv[:, first : first + count], qkv[n_rows, first : first + count],
                (((1,), (1,)), ((), ())), preferred_element_type=full,
            )
            working[:, n_rows] = value if start else working[:, n_rows] + value

    back_one(0, width, True)
    normed_turned = normed_one[...].T
    for n in range(width // tile):
        n_columns = slice(n * tile, (n + 1) * tile)
        value = jnp.dot(normed_turned, d_qkv[:, n_columns], preferred_element_type=full)
        qkv[:, n_columns] = value.astype(low)
    for copy in load_gu:
        copy.wait()
    gu_first[0].wait_recv()
    gu_to_y[...] = gu_to_y[...] + gu_x[1]
    gu_second[0].start()
    gu_first[1].wait_recv()
    gu_to_x[...] = gu_to_x[...] + gu_y[1]
    gu_second[1].start()

    for g in range(KV_HEADS):
        for copy in dkv_send[g]:
            copy.wait_recv()
        total = dkv[g, s].astype(full)
        for j in range(1, n_s):
            total = total + dkv_in[g, j].astype(full)
        key_columns = slice(width + g * HEAD_DIM, width + (g + 1) * HEAD_DIM)
        value_columns = slice(width + kv_width + g * HEAD_DIM, width + kv_width + (g + 1) * HEAD_DIM)
        d_qkv[:, key_columns] = turned_back(total[:, :HEAD_DIM]).astype(low)
        d_qkv[:, value_columns] = total[:, HEAD_DIM:].astype(low)
    back_one(width, 2 * kv_width, False)
    value = jnp.dot(normed_turned, d_qkv[:, width:], preferred_element_type=full)
    qkv[:, width:] = value.astype(low)
    sum_qkv.start_core()
    chain.add_two()
    chain.three()

    d_norm, gain_one_grad = norm_back(tokens[...].astype(full), gain_one[...], working[...])
    input_rows[...] = (d_resid[...] + d_norm).astype(low)
    bias_grad = jnp.sum(d_qkv[...].astype(full), 0, keepdims=True)
    vectors = jnp.concatenate([gain_one_grad, gain_two_grad, bias_grad], 1)
    part = vectors.shape[1] // 8
    for r in range(8):
        vector_in[0, r : r + 1] = vectors[:, r * part : (r + 1) * part]
    vector_send[0].start()
    sum_qkv.start_first()
    vector_send[0].wait_recv()
    vector_in[2] = vector_in[0] + vector_in[1]
    vector_send[1].start()
    gu_first[2].wait_recv()
    gu_second[0].wait_recv()
    total = gu_own[:, :units].astype(full) + gu_x[0].astype(full) + gu_ended[0].astype(full)
    gu_own[:, :units] = total.astype(low)
    gu_first[3].wait_recv()
    gu_second[1].wait_recv()
    total = gu_own[:, units:].astype(full) + gu_y[0].astype(full) + gu_ended[1].astype(full)
    gu_own[:, units:] = total.astype(low)
    for copy in gu_send:
        copy.start()
    keep_rows = here(rows_for(gu_own, 0, 0), gu_rows.at[0], 6)
    keep_rows.start()
    sum_out.start_first()

    vector_send[1].wait_recv()
    vector_in[4] = vector_in[2] + vector_in[3]
    vector_send[2].start()
    sum_qkv.start_second()
    sum_out.start_second()
    vector_send[2].wait_recv()
    vector_in[6] = vector_in[4] + vector_in[5]
    for copy in vector_send[3:]:
        copy.start()
    sum_qkv.finish()
    chain_qkv.one()
    chain.last(working)
    layer[...] = (resid[...] + working[...]).astype(low)
    chain_qkv.add_one()
    chain_qkv.two()
    sum_out.finish()
    chain_out.one()
    for copy in vector_send[3:]:
        copy.wait_recv()
    vector[...] = vector_in[6] + vector_in[7] + vector_in[8] + vector_in[9]
    chain_qkv.add_two()
    chain_qkv.three()
    chain_out.add_one()
    chain_out.two()
    chain_qkv.last(grad_qkv)
    chain_out.add_two()
    chain_out.three()
    chain_out.last(grad_out)
    for copy in gu_send:
        copy.wait_recv()
    keep_rows.wait()
    for part in (chain_qkv, chain_out):
        part.one_sent()
        part.two_sent()
        part.three_sent()
    chain.two_sent()
    chain.three_sent()
    sum_out.sent()
    sum_qkv.sent()
    for copy in gu_first + gu_second + gu_send + vector_send:
        copy.wait_send()
    for g in range(KV_HEADS):
        for copy in dkv_send[g]:
            copy.wait_send()


def back(
    columns, resid, gain_two, cotangent, attended, queries, paired, slots, slot_row, first_row,
    logsum, normed_one, tokens, gain_one, cosine, sine, w_out, w_qkv, gu_sum, branch,
):
    rows, width = tokens.shape
    n_s = paired.shape[0]
    group = n_s * rows
    kv_width = KV_HEADS * HEAD_DIM
    qkv_width = width + 2 * kv_width
    block = width // 8
    piece = block // n_s
    units = gu_sum.shape[2] // 2
    low, full = jnp.bfloat16, jnp.float32
    vmem = pl.BlockSpec(memory_space=pltpu.VMEM)
    hbm = pl.BlockSpec(memory_space=pl.ANY)
    shape = jax.ShapeDtypeStruct
    vectors = (2 * width + qkv_width) // 8
    return pl.pallas_call(
        back_kernel,
        in_specs=[vmem] * 8 + [hbm] * 12,
        out_specs=[vmem] * 5 + [hbm],
        out_shape=[
            shape((rows, width), low),
            shape((rows, width), low),
            shape((8, vectors), full),
            shape((piece, width), full),
            shape((piece, qkv_width), full),
            shape((n_s, piece, 2 * units), low),
        ],
        scratch_shapes=[
            pltpu.VMEM((rows, width), full),
            pltpu.VMEM((rows, width), low),
            pltpu.VMEM((rows, width), low),
            pltpu.VMEM((rows, width), low),
            pltpu.VMEM(paired.shape, low),
            pltpu.VMEM((rows, width), low),
            pltpu.VMEM((rows, width), low),
            pltpu.VMEM((width, width), low),
            pltpu.VMEM((width, qkv_width), low),
            pltpu.VMEM((block, 2 * units), low),
            pltpu.VMEM((block, units), low),
            pltpu.VMEM((block, units), low),
            pltpu.VMEM((2, block, units), low),
            pltpu.VMEM((2, block, units), low),
            pltpu.VMEM((2, block, units), low),
            pltpu.VMEM((group, width), low),
            pltpu.VMEM((rows, width), low),
            pltpu.VMEM((2, rows, width), low),
            pltpu.VMEM((2, rows, width), low),
            pltpu.VMEM((rows, width), full),
            pltpu.VMEM((group, rows), full),
            pltpu.VMEM((rows, width), low),
            pltpu.VMEM((rows, width), low),
            pltpu.VMEM((rows, qkv_width), low),
            pltpu.VMEM((rows, width), full),
            pltpu.VMEM((group, HEAD_DIM), full),
            pltpu.VMEM((group, HEAD_DIM), full),
            pltpu.VMEM((KV_HEADS, n_s, rows, 2 * HEAD_DIM), low),
            pltpu.VMEM((KV_HEADS, n_s, rows, 2 * HEAD_DIM), low),
            pltpu.VMEM((4, block, width), low),
            pltpu.VMEM((2, block, width // 2), low),
            pltpu.VMEM((2, block, width // 2), low),
            pltpu.VMEM((2, block, width // 2), low),
            pltpu.VMEM((4, block, qkv_width), low),
            pltpu.VMEM((2, block, qkv_width // 2), low),
            pltpu.VMEM((2, block, qkv_width // 2), low),
            pltpu.VMEM((2, block, qkv_width // 2), low),
            pltpu.VMEM((piece, width), low),
            pltpu.VMEM((2, piece, width), low),
            pltpu.VMEM((2, piece, width), low),
            pltpu.VMEM((piece, qkv_width), low),
            pltpu.VMEM((2, piece, qkv_width), low),
            pltpu.VMEM((2, piece, qkv_width), low),
            pltpu.VMEM((10, 8, vectors), full),
            pltpu.SemaphoreType.DMA((18,)),
            pltpu.SemaphoreType.DMA((68,)),
            pltpu.SemaphoreType.DMA((68,)),
        ],
        compiler_params=pltpu.CompilerParams(
            collective_id=2, has_side_effects=True, vmem_limit_bytes=63 * 2**20
        ),
        name="back",
    )(
        gain_two, slot_row, first_row, logsum, gain_one, cosine, sine, slots,
        resid, cotangent, attended, queries, paired, normed_one, tokens,
        columns, w_out, w_qkv, gu_sum, branch,
    )


def finish_kernel(
    layer, input_rows, grad_out, grad_qkv, grad_down, gu_rows,
    layer_out, input_grad, out_out, query_out, key_out, value_out, down_out, gate_out, up_out,
    layer_v, input_v, out_v, qkv_v, down_v, gu_v, gate_v, up_v, load, store,
):
    s = lax.axis_index("seq")
    n_s = gu_rows.shape[0]
    width = grad_out.shape[1]
    kv_width = KV_HEADS * HEAD_DIM
    unit_pad = grad_down.shape[0]
    unit = down_out.shape[0]
    units = gu_rows.shape[2] // 2
    moves = [
        (layer, layer_v, [(layer_v, layer_out)]),
        (input_rows, input_v, [(input_v, input_grad)]),
        (grad_down, down_v, [(down_v.at[:unit], down_out)]),
        (grad_out, out_v, [(out_v, out_out)]),
        (grad_qkv, qkv_v, [
            (qkv_v.at[:, :width], query_out),
            (qkv_v.at[:, width : width + kv_width], key_out),
            (qkv_v.at[:, width + kv_width :], value_out),
        ]),
    ]
    load_gu = pltpu.make_async_copy(gu_rows, gu_v, load.at[0])
    load_gu.start()
    loads, stores = [], []
    for i, (source, place, _) in enumerate(moves):
        loads.append(pltpu.make_async_copy(source, place, load.at[1 + i]))
        loads[-1].start()
    for copy, (_, _, parts) in zip(loads, moves):
        copy.wait()
        for source, target in parts:
            stores.append(pltpu.make_async_copy(source, target, store.at[len(stores)]))
            stores[-1].start()
    load_gu.wait()
    window = 512
    lanes = lax.broadcasted_iota(jnp.int32, (gu_rows.shape[1], 128), 1)
    for base, out, target_out in ((0, gate_v, gate_out), (units, up_v, up_out)):
        for f in range(units // unit_pad):
            for owner in range(n_s):
                source = base + f * unit_pad
                begin = min(source // 128 * 128, 2 * units - window)
                target = (f * n_s + owner) * unit
                first = target // 128 * 128
                slot = lax.rem(s + n_s - owner, n_s)
                value = gu_v[slot, :, begin : begin + window].astype(jnp.float32)
                turn = ((target - first) - (source - begin)) % window
                if turn:
                    value = pltpu.roll(value, turn, 1)
                for t in range(first, min(target + unit, out.shape[1]), 128):
                    part = value[:, t - first : t - first + 128]
                    if t < target:
                        part = jnp.where(lanes >= target - t, part, out[:, t : t + 128])
                    out[:, t : t + 128] = part
        stores.append(pltpu.make_async_copy(out, target_out, store.at[len(stores)]))
        stores[-1].start()
    for copy in stores:
        copy.wait()


def finish(layer, input_rows, grad_out, grad_qkv, grad_down, gu_rows, unit, hidden_width):
    piece, width = grad_out.shape
    kv_width = KV_HEADS * HEAD_DIM
    low, full = jnp.bfloat16, jnp.float32
    shape = jax.ShapeDtypeStruct
    hbm = pl.BlockSpec(memory_space=pl.ANY)
    wide = pltpu.VMEM((piece, hidden_width), full)
    return pl.pallas_call(
        finish_kernel,
        in_specs=[hbm] * 6,
        out_specs=[hbm] * 9,
        out_shape=[
            shape(layer.shape, low),
            shape(layer.shape, low),
            shape((piece, width), full),
            shape((piece, width), full),
            shape((piece, kv_width), full),
            shape((piece, kv_width), full),
            shape((unit, width), full),
            shape((piece, hidden_width), full),
            shape((piece, hidden_width), full),
        ],
        scratch_shapes=[
            pltpu.VMEM(value.shape, value.dtype)
            for value in (layer, input_rows, grad_out, grad_qkv, grad_down, gu_rows)
        ] + [wide, wide, pltpu.SemaphoreType.DMA((6,)), pltpu.SemaphoreType.DMA((9,))],
        compiler_params=pltpu.CompilerParams(vmem_limit_bytes=63 * 2**20),
        name="finish",
    )(layer, input_rows, grad_out, grad_qkv, grad_down, gu_rows)


def per_device(
    tokens, cotangent, lengths, balance, norm1_gain, w_query, b_query, w_key, b_key,
    w_value, b_value, w_out, norm2_gain, w_gate, w_up, w_down,
):
    seq_count = lax.axis_size("seq")
    fsdp_count = lax.axis_size("fsdp")
    seq_rank = lax.axis_index("seq")
    fsdp_rank = lax.axis_index("fsdp")
    rows_here, width = tokens.shape
    kv_width = KV_HEADS * HEAD_DIM
    hidden_width = w_gate.shape[1]
    unit = hidden_width // (fsdp_count * seq_count)
    (
        weight_gu, weight_down, upstream_all, normed_all, hidden, factor_gate, factor_up,
        weight_qkv, weight_out, queries, paired, slots, logsum, attended, resid, normed_one,
        gain_one, gain_two, slot_row, first_row, cosine, sine,
    ) = front(
        tokens, cotangent, lengths, balance, (norm1_gain, norm2_gain, b_query, b_key, b_value),
        (w_query, w_key, w_value, w_out, w_gate, w_up, w_down),
    )
    columns, grad_down, gu_sum, branch = ffn(
        normed_all, upstream_all, weight_gu, weight_down, hidden, factor_gate, factor_up
    )
    layer, input_rows, vectors, grad_out, grad_qkv, gu_rows = back(
        columns, resid, gain_two, cotangent, attended, queries, paired, slots, slot_row, first_row,
        logsum, normed_one, tokens, gain_one, cosine, sine, weight_out, weight_qkv, gu_sum, branch,
    )
    (
        layer_out, input_grad, grad_out, grad_query, grad_key, grad_value, grad_down, grad_gate,
        grad_up,
    ) = finish(layer, input_rows, grad_out, grad_qkv, grad_down, gu_rows, unit, hidden_width)
    vectors = vectors.reshape(-1)
    own = width // (fsdp_count * seq_count)
    first = (fsdp_rank * seq_count + seq_rank) * own

    def own_part(offset):
        return lax.dynamic_slice_in_dim(vectors, offset + first, own, 0)

    biases = 2 * width
    return (
        layer_out,
        input_grad,
        own_part(0),
        grad_query,
        own_part(biases),
        grad_key,
        vectors[biases + width : biases + width + kv_width],
        grad_value,
        vectors[biases + width + kv_width :],
        grad_out,
        own_part(width),
        grad_gate,
        grad_up,
        grad_down,
    )


def solution(mesh):
    both = P(("fsdp", "seq"), None)
    both_one = P(("fsdp", "seq"))
    placed = (
        both, both, P("fsdp", None), both_one, P("fsdp"), P("fsdp", None), P("fsdp"),
        P("fsdp", None), P("fsdp"), P("fsdp", None), P("fsdp"), P("fsdp", None), P("fsdp"),
        P("fsdp", None), P("fsdp", None), P("fsdp", None),
    )
    return jax.shard_map(
        per_device if mesh.shape["fsdp"] == 8 else plain_device,
        mesh=mesh,
        in_specs=placed,
        out_specs=(
            both, both, both_one, both, both_one, both, P(), both, P(), both, both_one,
            both, both, both,
        ),
        check_vma=False,
    )
```
